32 devices in a mesh: dp: 8 (over z, core), seq: 4 (over y, x).
Axes of the slice: x: 2, y: 2, z: 4, core: 2. Of those that a mesh axis runs over, the one named last changes fastest.
Arguments:
- tokens: bfloat16 [8, 2048, 2048], P('dp', 'seq'), may hold values from -60 to 60
- cotangent: bfloat16 [8, 2048, 2048], P('dp', 'seq'), may hold values from -6 to 6
- lengths: int32 [8], P('dp'), may hold values from 1537 to 2048, as said below
- key_mask: int32 [8, 2048], P('dp', 'seq'), may hold values 0 or 1
- attn_gain: bfloat16 [2048], P(('dp', 'seq')), may hold values from 0.5 to 1.5
- attn_shift: bfloat16 [2048], P(('dp', 'seq')), may hold values from -4 to 4
- qkv_weight: bfloat16 [2048, 6144], P(('dp', 'seq')), may hold values from -0.125 to 0.125
- qv_bias: bfloat16 [4096], P(('dp', 'seq')), may hold values from -4 to 4
- proj_weight: bfloat16 [2048, 2048], P(('dp', 'seq')), may hold values from -1.5 to 1.5
- proj_bias: bfloat16 [2048], P(('dp', 'seq')), may hold values from -4 to 4
- mlp_gain: bfloat16 [2048], P(('dp', 'seq')), may hold values from 0.5 to 1.5
- mlp_shift: bfloat16 [2048], P(('dp', 'seq')), may hold values from -4 to 4
- fc_weight: bfloat16 [2048, 8192], P(('dp', 'seq')), may hold values from -0.125 to 0.125
- fc_bias: bfloat16 [8192], P(('dp', 'seq')), may hold values from -4 to 4
- down_weight: bfloat16 [8192, 2048], P(('dp', 'seq')), may hold values from -0.0625 to 0.0625
- down_bias: bfloat16 [2048], P(('dp', 'seq')), may hold values from -4 to 4
Outputs:
- block_out: bfloat16 [8, 2048, 2048], P('dp', 'seq')
- tokens_grad: float32 [8, 2048, 2048], P('dp', 'seq')
- attn_gain_grad: float32 [2048], P(('dp', 'seq'))
- attn_shift_grad: float32 [2048], P(('dp', 'seq'))
- qkv_weight_grad: float32 [2048, 6144], P(('dp', 'seq'))
- qv_bias_grad: float32 [4096], P(('dp', 'seq'))
- proj_weight_grad: float32 [2048, 2048], P(('dp', 'seq'))
- proj_bias_grad: float32 [2048], P(('dp', 'seq'))
- mlp_gain_grad: float32 [2048], P(('dp', 'seq'))
- mlp_shift_grad: float32 [2048], P(('dp', 'seq'))
- fc_weight_grad: float32 [2048, 8192], P(('dp', 'seq'))
- fc_bias_grad: float32 [8192], P(('dp', 'seq'))
- down_weight_grad: float32 [8192, 2048], P(('dp', 'seq'))
- down_bias_grad: float32 [2048], P(('dp', 'seq'))
The draws below stay inside these ranges and needn't reach their ends.
Inputs may be any that keep to these rules, and one draw needn't show every extreme that they name: `lengths`: in every draw some sequence has length 2048.
All inputs are finite; a program needn't handle non-finite values. No bound on the sum of `key_mask` on one device may be relied on, other than what follows from the above.
Results may differ from the reference program's by a relative error of at most 0.0094.
Values may be sent and summed in bfloat16 or wider, within the bound.
A program may use at most 448 MiB of HBM per device.

```python
import math
import jax
import jax.numpy as jnp
from jax import lax

D = 2048
HEADS = 16
HEAD_DIM = 128
FF = 8192
LEN = 2048
PIECE = 512
SEQUENCES = 8


def draw_tokens(key, part):
    key = jax.random.fold_in(key, 11)
    key_base, key_rows, key_cols = jax.random.split(key, 3)
    row_scale = jnp.exp(jax.random.uniform(key_rows, (SEQUENCES, LEN, 1), jnp.float32, 0.0, math.log(10.0)))
    col_scale = jnp.exp(jax.random.uniform(key_cols, (1, 1, D), jnp.float32, 0.0, math.log(10.0)))
    base = jax.random.normal(key_base, (SEQUENCES, LEN, D), jnp.float32)
    base = jnp.clip(base, -4.0, 4.0)
    return (0.15 * base * row_scale * col_scale).astype(jnp.bfloat16)


def draw_lengths(key, part):
    key = jax.random.fold_in(key, 23)
    key_draw, key_full = jax.random.split(key)
    lowest = LEN - PIECE + 1
    drawn = jax.random.randint(key_draw, (SEQUENCES,), lowest, LEN + 1)
    chosen = jax.random.randint(key_full, (), 0, SEQUENCES)
    return jnp.where(jnp.arange(SEQUENCES) == chosen, LEN, drawn).astype(jnp.int32)


def set_ends(values, rng, low, top_value):
    shape = values.shape
    spot = [jax.random.randint(jax.random.fold_in(rng, axis), (), 0, shape[axis]) for axis in range(len(shape))]
    values = values.at[tuple(spot)].set(low)
    longest = shape.index(max(shape))
    spot[longest] = (spot[longest] + 1) % shape[longest]
    return values.at[tuple(spot)].set(top_value)


def block_levels(key, dims, shards, low, largest):
    level = 1.0
    for axis_at, parts in shards:
        draws = jax.random.uniform(jax.random.fold_in(jax.random.fold_in(key, 6), axis_at), (parts,), jnp.float32, low / len(shards), largest / len(shards))
        level = level * jnp.repeat(jnp.exp(draws), dims[axis_at] // parts).reshape((-1,) + (1,) * (len(dims) - 1 - axis_at))
    return level


def gaussian(stream_key, dims, width, most, cuts=(), held_as=jnp.bfloat16):
    entries = width * jax.random.normal(stream_key, dims, jnp.float32)
    if cuts:
        entries = entries * block_levels(stream_key, dims, cuts, -0.22, 0.18)
    return jnp.clip(entries, -most, most).astype(held_as)


def setup_inputs(seed: int = 0) -> dict:
    arg_keys = jax.random.split(jax.random.key(seed), 17)
    tokens = draw_tokens(jax.random.fold_in(arg_keys[16], 71), 0)
    cotangent = gaussian(arg_keys[1], (SEQUENCES, LEN, D), 1.0, 6.0, ((0, 8), (1, 4)))
    lengths = draw_lengths(jax.random.fold_in(arg_keys[16], 71), 0)
    key_mask = set_ends((jax.random.randint(arg_keys[3], (SEQUENCES, LEN), 0, 8) < 7).astype(jnp.int32), jax.random.fold_in(arg_keys[3], 1), 0, 1)
    attn_gain = jnp.clip(1.0 + 0.1 * jax.random.normal(arg_keys[4], (D,), jnp.float32), 0.5, 1.5).astype(jnp.bfloat16)
    attn_shift = gaussian(arg_keys[5], (D,), 0.3, 4.0, ((0, 32),))
    qkv_weight = gaussian(arg_keys[6], (D, 3 * D), D ** -0.5, 0.125, ((0, 32),))
    qv_bias = gaussian(arg_keys[7], (2 * D,), 0.3, 4.0, ((0, 32),))
    proj_weight = gaussian(arg_keys[8], (D, D), (max(D // 128, 1)) ** -0.5, 1.5, ((0, 32),))
    proj_bias = gaussian(arg_keys[9], (D,), 0.3, 4.0, ((0, 32),))
    mlp_gain = jnp.clip(1.0 + 0.1 * jax.random.normal(arg_keys[10], (D,), jnp.float32), 0.5, 1.5).astype(jnp.bfloat16)
    mlp_shift = gaussian(arg_keys[11], (D,), 0.3, 4.0, ((0, 32),))
    fc_weight = gaussian(arg_keys[12], (D, FF), D ** -0.5, 0.125, ((0, 32),))
    fc_bias = gaussian(arg_keys[13], (FF,), 0.3, 4.0, ((0, 32),))
    down_weight = gaussian(arg_keys[14], (FF, D), FF ** -0.5, 0.0625, ((0, 32),))
    down_bias = gaussian(arg_keys[15], (D,), 0.3, 4.0, ((0, 32),))
    return dict(tokens=tokens, cotangent=cotangent, lengths=lengths, key_mask=key_mask, attn_gain=attn_gain, attn_shift=attn_shift, qkv_weight=qkv_weight, qv_bias=qv_bias, proj_weight=proj_weight, proj_bias=proj_bias, mlp_gain=mlp_gain, mlp_shift=mlp_shift, fc_weight=fc_weight, fc_bias=fc_bias, down_weight=down_weight, down_bias=down_bias)


@jax.custom_vjp
def low(v):
    return lax.optimization_barrier(v.astype(jnp.bfloat16)).astype(jnp.float32)

@jax.custom_vjp
def low_back(v):
    return v

def low_keep(v):
    return (low(v), None)

def low_pass(kept, grad):
    return (grad,)

def back_keep(v):
    return (v, None)

def back_low(kept, grad):
    return (low(grad),)
low.defvjp(low_keep, low_pass)
low_back.defvjp(back_keep, back_low)
HIGH = lax.Precision.HIGHEST
EPS = 1e-05
NEG = -1e+30

def layer_norm(values, gain, shift):
    average = lax.optimization_barrier(jnp.mean(values, axis=-1, keepdims=True))
    centred = values - average
    spread = lax.optimization_barrier(jnp.mean(centred * centred, axis=-1, keepdims=True))
    return centred * lax.rsqrt(spread + EPS) * gain + shift

def head_attention(query_head, key_head, value_head, allowed):
    factor = HEAD_DIM ** (-0.5)
    scores = low_back(jnp.dot(query_head, key_head.T, precision=HIGH) * factor)
    scores = jnp.where(allowed == 1, scores, NEG)
    highest = lax.optimization_barrier(jnp.max(scores, axis=-1, keepdims=True))
    exp_scores = jnp.exp(scores - highest)
    chances = low(exp_scores / lax.optimization_barrier(jnp.sum(exp_scores, axis=-1, keepdims=True)))
    return jnp.dot(chances, value_head, precision=HIGH)

def sequence_forward(sequence, key_ok, params):
    attn_gain, attn_shift, qkv_weight, qv_bias, proj_weight, proj_bias, mlp_gain, mlp_shift, fc_weight, fc_bias, down_weight, down_bias = params
    position = jnp.arange(LEN)
    allowed = ((position[None, :] <= position[:, None]) & (key_ok[None, :] | (position[None, :] == position[:, None]))).astype(jnp.int32)
    normed_one = low(layer_norm(sequence, attn_gain, attn_shift))
    qkv_shift = jnp.concatenate([qv_bias[:D], jnp.zeros((D,), sequence.dtype), qv_bias[D:]])
    projected = low(low_back(jnp.dot(normed_one, qkv_weight, precision=HIGH) + qkv_shift))
    query_heads = projected[:, :D].reshape(LEN, HEADS, HEAD_DIM).transpose(1, 0, 2)
    key_heads = projected[:, D:2 * D].reshape(LEN, HEADS, HEAD_DIM).transpose(1, 0, 2)
    value_heads = projected[:, 2 * D:].reshape(LEN, HEADS, HEAD_DIM).transpose(1, 0, 2)
    checked = jax.checkpoint(head_attention)

    def per_head(operands):
        return checked(operands[0], operands[1], operands[2], allowed)
    head_out = lax.map(per_head, (query_heads, key_heads, value_heads))
    attended = low(low_back(head_out.transpose(1, 0, 2).reshape(LEN, D)))
    middle = sequence + low_back(jnp.dot(attended, proj_weight, precision=HIGH) + proj_bias)
    normed_two = low(layer_norm(middle, mlp_gain, mlp_shift))
    hidden = low_back(jnp.dot(normed_two, fc_weight, precision=HIGH) + fc_bias)
    active = low(jax.nn.gelu(hidden, approximate=True))
    return middle + low_back(jnp.dot(active, down_weight, precision=HIGH) + down_bias)

def reference(tokens, cotangent, lengths, key_mask, attn_gain, attn_shift, qkv_weight, qv_bias, proj_weight, proj_bias, mlp_gain, mlp_shift, fc_weight, fc_bias, down_weight, down_bias):
    params = tuple((item.astype(jnp.float32) for item in (attn_gain, attn_shift, qkv_weight, qv_bias, proj_weight, proj_bias, mlp_gain, mlp_shift, fc_weight, fc_bias, down_weight, down_bias)))
    position = jnp.arange(LEN)

    def per_sequence(totals, element):
        sequence, upstream, length, flags = element
        key_ok = (flags == 1) & (position < length)

        def forward_fn(inputs, weights):
            return sequence_forward(inputs, key_ok, weights)
        result, pullback = jax.vjp(forward_fn, sequence.astype(jnp.float32), params)
        gradients = pullback(upstream.astype(jnp.float32))
        totals = jax.tree.map(jnp.add, totals, gradients[1])
        return (totals, (result.astype(jnp.bfloat16), gradients[0]))
    initial = tuple((jnp.zeros_like(item) for item in params))
    totals, (block_out, tokens_grad) = lax.scan(per_sequence, initial, (tokens, cotangent, lengths, key_mask))
    return (block_out, tokens_grad, totals[0], totals[1], totals[2], totals[3], totals[4], totals[5], totals[6], totals[7], totals[8], totals[9], totals[10], totals[11])
```

```python
import functools
import math

import jax
import jax.numpy as jnp
from jax import lax
from jax.experimental import pallas as pl
from jax.experimental.pallas import tpu as pltpu
from jax.sharding import PartitionSpec as P

HEADS = 16
HEAD_DIM = 128
EPS = 1e-05
NEG = -1e30
FACTOR = HEAD_DIM ** (-0.5)
LOG2E = math.log2(math.e)
F32 = jnp.float32
BF16 = jnp.bfloat16
BOTH = ("dp", "seq")


def nn(left, right):
    return lax.dot_general(left, right, (((1,), (0,)), ((), ())), preferred_element_type=F32)


def nt(left, right):
    return lax.dot_general(left, right, (((1,), (1,)), ((), ())), preferred_element_type=F32)


def tn(left, right):
    return lax.dot_general(left, right, (((0,), (0,)), ((), ())), preferred_element_type=F32)


def scores_of(key_ref, bias_ref, query, rel, piece, diagonal):
    rows = pl.ds(pl.multiple_of(rel * piece, piece), piece)
    scores = nt(key_ref[rows, :], query) * (FACTOR * LOG2E)
    key_bias = bias_ref[rows, :]
    if not diagonal:
        return scores + key_bias
    key_at = lax.broadcasted_iota(jnp.int32, scores.shape, 0)
    query_at = lax.broadcasted_iota(jnp.int32, scores.shape, 1)
    allowed = ((key_at < query_at) & (key_bias > -1.0)) | (key_at == query_at)
    return jnp.where(allowed, scores, NEG)


def forward_kernel(rank_ref, query_ref, key_ref, value_ref, bias_ref, out_ref, lse_ref, score_ref, value_t):
    piece = query_ref.shape[0]
    rank = rank_ref[0]
    step = pl.program_id(1)
    true = lax.bitwise_xor(step, rank)

    @pl.when(step == 0)
    def _():
        value_t[...] = value_ref[...].astype(F32).T.astype(BF16)

    query = query_ref[...]

    def first(at, top):
        scores = scores_of(key_ref, bias_ref, query, lax.bitwise_xor(at, rank), piece, False)
        score_ref[pl.ds(pl.multiple_of(at * piece, piece), piece), :] = scores
        return jnp.maximum(top, jnp.max(scores, axis=0, keepdims=True))

    last = scores_of(key_ref, bias_ref, query, step, piece, True)
    top = lax.fori_loop(0, true, first, jnp.max(last, axis=0, keepdims=True))

    def weigh(scores, rel):
        weights = jnp.exp2(scores - top)
        columns = pl.ds(pl.multiple_of(rel * piece, piece), piece)
        return jnp.sum(weights, axis=0, keepdims=True), nn(value_t[:, columns], weights.astype(BF16))

    def second(at, carry):
        total, out = carry
        more, part = weigh(
            score_ref[pl.ds(pl.multiple_of(at * piece, piece), piece), :], lax.bitwise_xor(at, rank)
        )
        return total + more, out + part

    total, out = lax.fori_loop(0, true, second, weigh(last, step))
    out_ref[...] = (out / total).T.astype(BF16)
    lse_ref[0] = top + jnp.log2(total)


def attend(rank, qkv, key_bias, piece):
    length, heads = qkv.shape[0], qkv.shape[1] // (3 * HEAD_DIM)
    grid_spec = pltpu.PrefetchScalarGridSpec(
        num_scalar_prefetch=1,
        grid=(heads, length // piece),
        in_specs=[
            pl.BlockSpec((piece, HEAD_DIM), lambda h, i, r: (i, 3 * h)),
            pl.BlockSpec((length, HEAD_DIM), lambda h, i, r: (0, 3 * h + 1)),
            pl.BlockSpec((length, HEAD_DIM), lambda h, i, r: (0, 3 * h + 2)),
            pl.BlockSpec((length, 1), lambda h, i, r: (0, 0)),
        ],
        out_specs=[
            pl.BlockSpec((piece, HEAD_DIM), lambda h, i, r: (i, h)),
            pl.BlockSpec((1, 1, piece), lambda h, i, r: (h, 0, i)),
        ],
        scratch_shapes=[pltpu.VMEM((length, piece), F32), pltpu.VMEM((HEAD_DIM, length), BF16)],
    )
    flops = 4 * heads * length * length * HEAD_DIM
    return pl.pallas_call(
        forward_kernel,
        grid_spec=grid_spec,
        out_shape=(
            jax.ShapeDtypeStruct((length, heads * HEAD_DIM), BF16),
            jax.ShapeDtypeStruct((heads, 1, length), F32),
        ),
        compiler_params=pltpu.CompilerParams(
            dimension_semantics=("arbitrary", "arbitrary"), vmem_limit_bytes=48 * 2**20
        ),
        cost_estimate=pl.CostEstimate(
            flops=flops, bytes_accessed=qkv.size * 3, transcendentals=heads * length * length // 2
        ),
    )(rank, qkv, qkv, qkv, key_bias)


def backward_kernel(
    rank_ref, query_ref, grad_ref, lse_ref, key_ref, value_ref, bias_ref, out_ref,
    prob_ref, chance_ref, key_t, key_sum, value_sum,
):
    piece = query_ref.shape[0]
    rank = rank_ref[0]
    step = pl.program_id(1)
    true = lax.bitwise_xor(step, rank)

    @pl.when(step == 0)
    def _():
        key_t[...] = key_ref[...].astype(F32).T.astype(BF16)
        key_sum[...] = jnp.zeros_like(key_sum)
        value_sum[...] = jnp.zeros_like(value_sum)

    query, grad, lse = query_ref[...], grad_ref[...], lse_ref[0]

    def rows_of(block):
        return pl.ds(pl.multiple_of(block * piece, piece), piece)

    def measure(scores, rel):
        rows = rows_of(rel)
        probs = jnp.exp2(scores - lse)
        grad_chances = nt(value_ref[rows, :], grad)
        value_sum[rows, :] += nn(probs.astype(BF16), grad)
        prob_ref[rows, :] = probs
        chance_ref[rows, :] = grad_chances
        return jnp.sum(probs * grad_chances, axis=0, keepdims=True)

    def first(at, weighted):
        rel = lax.bitwise_xor(at, rank)
        scores = scores_of(key_ref, bias_ref, query, rel, piece, False)
        return weighted + measure(scores, rel)

    last = scores_of(key_ref, bias_ref, query, step, piece, True)
    weighted = lax.fori_loop(0, true, first, measure(last, step))

    def second(at, total):
        rel = lax.bitwise_xor(at, rank)
        rows = rows_of(rel)
        grad_scores = (prob_ref[rows, :] * (chance_ref[rows, :] - weighted)).astype(BF16)
        key_sum[rows, :] += nn(grad_scores, query)
        return total + nn(key_t[:, rows], grad_scores)

    total = lax.fori_loop(0, true + 1, second, jnp.zeros((HEAD_DIM, piece), F32))
    out_ref[rows_of(step), 0:HEAD_DIM] = (total * FACTOR).T.astype(BF16)

    @pl.when(step == pl.num_programs(1) - 1)
    def _():
        out_ref[:, HEAD_DIM : 2 * HEAD_DIM] = (key_sum[...] * FACTOR).astype(BF16)
        out_ref[:, 2 * HEAD_DIM :] = value_sum[...].astype(BF16)


def attend_backward(rank, qkv, grad_attended, lse, key_bias, piece):
    length, heads = qkv.shape[0], qkv.shape[1] // (3 * HEAD_DIM)
    grid_spec = pltpu.PrefetchScalarGridSpec(
        num_scalar_prefetch=1,
        grid=(heads, length // piece),
        in_specs=[
            pl.BlockSpec((piece, HEAD_DIM), lambda h, i, r: (i, 3 * h)),
            pl.BlockSpec((piece, HEAD_DIM), lambda h, i, r: (i, h)),
            pl.BlockSpec((1, 1, piece), lambda h, i, r: (h, 0, i)),
            pl.BlockSpec((length, HEAD_DIM), lambda h, i, r: (0, 3 * h + 1)),
            pl.BlockSpec((length, HEAD_DIM), lambda h, i, r: (0, 3 * h + 2)),
            pl.BlockSpec((length, 1), lambda h, i, r: (0, 0)),
        ],
        out_specs=pl.BlockSpec((length, 3 * HEAD_DIM), lambda h, i, r: (0, h)),
        scratch_shapes=[
            pltpu.VMEM((length, piece), F32),
            pltpu.VMEM((length, piece), F32),
            pltpu.VMEM((HEAD_DIM, length), BF16),
            pltpu.VMEM((length, HEAD_DIM), F32),
            pltpu.VMEM((length, HEAD_DIM), F32),
        ],
    )
    flops = 10 * heads * length * length * HEAD_DIM
    return pl.pallas_call(
        backward_kernel,
        grid_spec=grid_spec,
        out_shape=jax.ShapeDtypeStruct(qkv.shape, BF16),
        compiler_params=pltpu.CompilerParams(
            dimension_semantics=("arbitrary", "arbitrary"), vmem_limit_bytes=48 * 2**20
        ),
        cost_estimate=pl.CostEstimate(
            flops=flops, bytes_accessed=qkv.size * 6, transcendentals=heads * length * length // 2
        ),
    )(rank, qkv, grad_attended, lse, qkv, qkv, key_bias)


def shift(value, axis, distance):
    count = lax.axis_size(axis)
    return lax.ppermute(value, axis, [(i, i ^ distance) for i in range(count)])


def gather_blocks(value, axis="seq"):
    return [value] + [shift(value, axis, k) for k in range(1, lax.axis_size(axis))]


def scatter_blocks(blocks, axis="seq"):
    return [blocks[0]] + [shift(blocks[k], axis, k) for k in range(1, lax.axis_size(axis))]


def by_rank(blocks, rank):
    bit = 1
    while bit < len(blocks):
        odd = (rank & bit) != 0
        blocks = [jnp.where(odd, blocks[k ^ bit], blocks[k]) for k in range(len(blocks))]
        bit *= 2
    return blocks


def pick(pieces, at):
    return lax.dynamic_index_in_dim(pieces, at, axis=0, keepdims=False)


def exchange(pieces, rank):
    sent = [pick(pieces, rank ^ k) for k in range(pieces.shape[0])]
    return by_rank(scatter_blocks(sent), rank)


def small_scatter(pieces, dp_rank, seq_rank):
    total = 0.0
    sent = [lax.dynamic_index_in_dim(pieces, seq_rank ^ k, axis=1, keepdims=False) for k in range(pieces.shape[1])]
    for part in scatter_blocks(sent):
        total = total + part
    sent = [pick(total, dp_rank ^ k) for k in range(pieces.shape[0])]
    total = 0.0
    for part in scatter_blocks(sent, "dp"):
        total = total + part
    return total


def swap_pairs(dp_count, seq_count, sub):
    pairs = []
    for d in range(dp_count):
        for s in range(seq_count):
            source = ((d // sub) * sub + s % sub) * seq_count + (s // sub) * sub + d % sub
            pairs.append((source, d * seq_count + s))
    return pairs


def norm_parts(values):
    average = jnp.mean(values, axis=-1, keepdims=True)
    centred = values - average
    scale = lax.rsqrt(jnp.mean(centred * centred, axis=-1, keepdims=True) + EPS)
    return centred * scale, scale


def norm_backward(normed, scale, gain, upstream):
    weighted = upstream * gain
    return scale * (
        weighted
        - jnp.mean(weighted, axis=-1, keepdims=True)
        - normed * jnp.mean(weighted * normed, axis=-1, keepdims=True)
    )


def add_up(parts):
    total = parts[0].astype(F32)
    for part in parts[1:]:
        total = total + part.astype(F32)
    return total


def shards(
    tokens,
    cotangent,
    lengths,
    key_mask,
    attn_gain,
    attn_shift,
    qkv_weight,
    qv_bias,
    proj_weight,
    proj_bias,
    mlp_gain,
    mlp_shift,
    fc_weight,
    fc_bias,
    down_weight,
    down_bias,
):
    _, piece, width = tokens.shape
    dp_count, seq_count = lax.axis_size("dp"), lax.axis_size("seq")
    dp_rank, seq_rank = lax.axis_index("dp"), lax.axis_index("seq")
    length = piece * seq_count
    own_heads = HEADS // seq_count
    rows = qkv_weight.shape[0]
    sub = HEAD_DIM // proj_weight.shape[0]
    high = seq_count // sub
    block = down_weight.shape[0]
    rank = jnp.reshape(seq_rank, (1,)).astype(jnp.int32)
    swap = swap_pairs(dp_count, seq_count, sub)

    qkv_pieces = (
        qkv_weight.reshape(rows, 3, own_heads, sub, high, HEAD_DIM)
        .transpose(4, 3, 0, 2, 1, 5)
        .reshape(seq_count, rows, own_heads * 3 * HEAD_DIM)
    )
    qkv_rows = jnp.concatenate(exchange(qkv_pieces, seq_rank), axis=0)
    qkv_full = lax.all_gather(qkv_rows, "dp", axis=0, tiled=True)
    tokens_own = tokens[0]
    token_blocks = gather_blocks(tokens_own)
    proj_full = lax.all_gather(lax.ppermute(proj_weight, BOTH, swap), "dp", axis=0, tiled=True)
    down_full = lax.all_gather(down_weight, "dp", axis=0, tiled=True)
    fc_pieces = (
        fc_weight.reshape(rows, dp_count, seq_count, block)
        .transpose(2, 0, 1, 3)
        .reshape(seq_count, rows, dp_count * block)
    )
    fc_rows = jnp.concatenate(exchange(fc_pieces, seq_rank), axis=0)
    fc_full = lax.all_gather(fc_rows, "dp", axis=0, tiled=True)

    small = (attn_gain, attn_shift, qv_bias, proj_bias, mlp_gain, mlp_shift, fc_bias, down_bias)
    sizes = [item.shape[0] for item in small]
    packed = jnp.concatenate(small)
    packed = jnp.stack(by_rank(gather_blocks(packed), seq_rank))
    packed = jnp.stack(by_rank(gather_blocks(packed, "dp"), dp_rank)).astype(F32)
    parts, start = [], 0
    for size in sizes:
        parts.append(packed[:, :, start : start + size])
        start += size
    whole = [part.reshape(-1) for part in parts]
    gain_one, shift_one, qv_full, proj_shift, gain_two, shift_two, _, down_shift = whole
    fc_shift = lax.dynamic_index_in_dim(parts[6], seq_rank, axis=1, keepdims=False).reshape(-1)
    rank_low, rank_high = seq_rank % sub, seq_rank // sub
    qv_heads = qv_full.reshape(2, own_heads, sub, high, HEAD_DIM)
    qv_own = lax.dynamic_index_in_dim(
        lax.dynamic_index_in_dim(qv_heads, rank_low, axis=2, keepdims=False), rank_high, axis=2, keepdims=False
    )
    qkv_shift = jnp.stack([qv_own[0], jnp.zeros_like(qv_own[0]), qv_own[1]], axis=1).reshape(-1)

    positions = seq_rank * piece + jnp.arange(piece, dtype=jnp.int32)
    own_flags = ((key_mask[0] == 1) & (positions < lengths[0])).astype(BF16)
    flags = jnp.concatenate(gather_blocks(own_flags))
    key_bias = jnp.where(flags > 0, 0.0, NEG).astype(F32)[:, None]

    own = tokens_own.astype(F32)
    cot_own, token_blocks[-1] = lax.optimization_barrier((cotangent[0], token_blocks[-1]))
    cot_blocks = gather_blocks(cot_own)
    token_all = jnp.concatenate(token_blocks, axis=0).astype(F32)
    normed_one = (norm_parts(token_all)[0] * gain_one + shift_one).astype(BF16)
    qkv = (nn(normed_one, qkv_full) + qkv_shift).astype(BF16)
    attended, lse = attend(rank, qkv, key_bias, piece)
    proj_terms = [
        nn(attended[k * piece : (k + 1) * piece], proj_full).astype(BF16) for k in range(seq_count)
    ]
    middle = own + (add_up(scatter_blocks(proj_terms)) + proj_shift)
    unit_two, scale_two = norm_parts(middle)
    normed_two = (unit_two * gain_two + shift_two).astype(BF16)

    normed_two_all = jnp.concatenate(gather_blocks(normed_two), axis=0)
    cot_all = jnp.concatenate(cot_blocks, axis=0)
    grad_active = nt(cot_all, down_full)
    hidden = nn(normed_two_all, fc_full) + fc_shift
    active, gelu_pull = jax.vjp(lambda h: jax.nn.gelu(h, approximate=True), hidden)
    active = active.astype(BF16)
    grad_hidden = gelu_pull(grad_active)[0].astype(BF16)
    grad_two_terms = [
        nt(grad_hidden[k * piece : (k + 1) * piece], fc_full).astype(BF16) for k in range(seq_count)
    ]
    upstream_two = add_up(scatter_blocks(grad_two_terms))
    cot_f32 = cotangent[0].astype(F32)
    grad_middle = cot_f32 + norm_backward(unit_two, scale_two, gain_two, upstream_two)
    grad_mid_low = grad_middle.astype(BF16)
    grad_mid_blocks = gather_blocks(grad_mid_low)

    grad_down = tn(active, cot_all).astype(BF16)
    grad_down = lax.psum_scatter(grad_down, "dp", scatter_dimension=0, tiled=True).astype(F32)
    grad_fc = tn(normed_two_all, grad_hidden).astype(BF16)
    grad_fc = lax.psum_scatter(grad_fc, "dp", scatter_dimension=0, tiled=True)
    grad_fc = exchange(grad_fc.reshape(seq_count, rows, dp_count * block), seq_rank)
    grad_fc = jnp.stack([item.reshape(rows, dp_count, block) for item in grad_fc], axis=2)
    grad_fc = grad_fc.reshape(fc_weight.shape).astype(F32)
    down_terms = [
        nn(active[k * piece : (k + 1) * piece], down_full).astype(BF16) for k in range(seq_count)
    ]
    block_out = (middle + (add_up(scatter_blocks(down_terms)) + down_shift)).astype(BF16)

    grad_mid_all = jnp.concatenate(grad_mid_blocks, axis=0)
    grad_proj = tn(attended, grad_mid_all).astype(BF16)
    grad_proj = lax.psum_scatter(grad_proj, "dp", scatter_dimension=0, tiled=True)
    grad_proj = lax.ppermute(grad_proj, BOTH, swap).astype(F32)
    grad_attended = nt(grad_mid_all, proj_full).astype(BF16)
    grad_qkv = attend_backward(rank, qkv, grad_attended, lse, key_bias, piece)
    grad_qkv_weight = tn(normed_one, grad_qkv).astype(BF16)
    grad_qkv_weight = lax.psum_scatter(grad_qkv_weight, "dp", scatter_dimension=0, tiled=True)
    grad_qkv_weight = exchange(grad_qkv_weight.reshape(seq_count, rows, -1), seq_rank)
    grad_qkv_weight = (
        jnp.stack(grad_qkv_weight)
        .reshape(high, sub, rows, own_heads, 3, HEAD_DIM)
        .transpose(2, 4, 3, 1, 0, 5)
        .reshape(qkv_weight.shape)
        .astype(F32)
    )
    grad_one_terms = [
        nt(grad_qkv[k * piece : (k + 1) * piece], qkv_full).astype(BF16) for k in range(seq_count)
    ]
    upstream_one = add_up(scatter_blocks(grad_one_terms))
    unit_one, scale_one = norm_parts(own)
    tokens_grad = grad_middle + norm_backward(unit_one, scale_one, gain_one, upstream_one)

    def spread(vector):
        return vector.reshape(dp_count, seq_count, -1)

    def at_rank(vector):
        here = (jnp.arange(seq_count) == seq_rank).astype(F32)
        return vector.reshape(dp_count, 1, -1) * here[None, :, None]

    early = (
        spread(jnp.sum(grad_mid_low.astype(F32), axis=0)),
        spread(jnp.sum(upstream_two * unit_two, axis=0)),
        spread(jnp.sum(upstream_two, axis=0)),
        spread(jnp.sum(cot_f32, axis=0)),
        at_rank(jnp.sum(grad_hidden.astype(F32), axis=0)),
    )
    early = small_scatter(jnp.concatenate(early, axis=2), dp_rank, seq_rank)
    column_sums = jnp.sum(grad_qkv.astype(F32), axis=0).reshape(own_heads, 3, HEAD_DIM)
    qv_sums = jnp.stack([column_sums[:, 0], column_sums[:, 2]])[:, :, None, None, :]
    here = (jnp.arange(sub) == rank_low)[:, None] & (jnp.arange(high) == rank_high)[None, :]
    qv_sums = qv_sums * here.astype(F32)[None, None, :, :, None]
    late = (
        spread(jnp.sum(upstream_one * unit_one, axis=0)),
        spread(jnp.sum(upstream_one, axis=0)),
        spread(qv_sums),
    )
    late = small_scatter(jnp.concatenate(late, axis=2), dp_rank, seq_rank)
    share = attn_gain.shape[0]
    return (
        block_out[None],
        tokens_grad[None],
        late[:share],
        late[share : 2 * share],
        grad_qkv_weight,
        late[2 * share :],
        grad_proj,
        early[:share],
        early[share : 2 * share],
        early[2 * share : 3 * share],
        grad_fc,
        early[4 * share :],
        grad_down,
        early[3 * share : 4 * share],
    )


def solution(mesh):
    in_specs = (
        P("dp", "seq", None),
        P("dp", "seq", None),
        P("dp"),
        P("dp", "seq"),
        P(BOTH),
        P(BOTH),
        P(BOTH, None),
        P(BOTH),
        P(BOTH, None),
        P(BOTH),
        P(BOTH),
        P(BOTH),
        P(BOTH, None),
        P(BOTH),
        P(BOTH, None),
        P(BOTH),
    )
    out_specs = (
        P("dp", "seq", None),
        P("dp", "seq", None),
        P(BOTH),
        P(BOTH),
        P(BOTH, None),
        P(BOTH),
        P(BOTH, None),
        P(BOTH),
        P(BOTH),
        P(BOTH),
        P(BOTH, None),
        P(BOTH),
        P(BOTH, None),
        P(BOTH),
    )
    return jax.shard_map(shards, mesh=mesh, in_specs=in_specs, out_specs=out_specs, check_vma=False)
```

```python
import functools
import math

import jax
import jax.numpy as jnp
from jax import lax
from jax.experimental import pallas as pl
from jax.experimental.pallas import tpu as pltpu
from jax.sharding import PartitionSpec as P

HEADS = 16
HEAD_DIM = 128
EPS = 1e-05
NEG = -1e30
FACTOR = HEAD_DIM ** (-0.5)
LOG2E = math.log2(math.e)
F32 = jnp.float32
BF16 = jnp.bfloat16
BOTH = ("dp", "seq")


def nn(left, right):
    return lax.dot_general(left, right, (((1,), (0,)), ((), ())), preferred_element_type=F32)


def nt(left, right):
    return lax.dot_general(left, right, (((1,), (1,)), ((), ())), preferred_element_type=F32)


def tn(left, right):
    return lax.dot_general(left, right, (((0,), (0,)), ((), ())), preferred_element_type=F32)


def params(limit_mib=56):
    return pltpu.CompilerParams(dimension_semantics=("arbitrary",), vmem_limit_bytes=limit_mib * 2**20)


def cost(flops, moved, exps=0):
    return pl.CostEstimate(flops=int(flops), bytes_accessed=int(moved), transcendentals=int(exps))


def call_on_block(kernel, grid, inputs, fresh, shared, previous, scratch, estimate, rank=None):
    arrays = [item for item, _ in inputs]
    specs = [spec for _, spec in inputs]
    aliases = {}
    lead = 0 if rank is None else 1
    if previous is not None:
        for at, item in enumerate(previous):
            aliases[lead + len(arrays)] = len(fresh) + at
            arrays.append(item)
            specs.append(pl.BlockSpec(memory_space=pl.ANY))
    count = len(inputs)
    skipped = 0 if previous is None else len(previous)

    def body(*refs):
        refs = list(refs)
        kernel(*refs[: lead + count], *refs[lead + count + skipped :])

    out_specs = [spec for _, spec in fresh] + [spec for _, spec in shared]
    out_shape = [shape for shape, _ in fresh] + [shape for shape, _ in shared]
    if rank is None:
        results = pl.pallas_call(
            body, grid=grid, in_specs=specs, out_specs=out_specs, out_shape=out_shape, scratch_shapes=scratch,
            input_output_aliases=aliases, compiler_params=params(), cost_estimate=estimate,
        )(*arrays)
    else:
        results = pl.pallas_call(
            body,
            grid_spec=pltpu.PrefetchScalarGridSpec(
                num_scalar_prefetch=1, grid=grid, in_specs=specs, out_specs=out_specs, scratch_shapes=scratch
            ),
            out_shape=out_shape, input_output_aliases=aliases, compiler_params=params(), cost_estimate=estimate,
        )(rank, *arrays)
    return results[: len(fresh)], results[len(fresh) :]


def norm_parts(values):
    average = jnp.mean(values, axis=-1, keepdims=True)
    centred = values - average
    scale = lax.rsqrt(jnp.mean(centred * centred, axis=-1, keepdims=True) + EPS)
    return centred * scale, scale


def norm_backward(normed, scale, gain, upstream):
    weighted = upstream * gain
    return scale * (
        weighted
        - jnp.mean(weighted, axis=-1, keepdims=True)
        - normed * jnp.mean(weighted * normed, axis=-1, keepdims=True)
    )


def project_kernel(x, gain, shift_, wq, wk, wv, bias, normed, q, k, v, k_t, v_t):
    columns = wq.shape[1]
    rows = (norm_parts(x[...].astype(F32))[0] * gain[...] + shift_[...]).astype(BF16)
    normed[...] = rows
    q[...] = (nn(rows, wq[...]) + bias[:, :columns]).astype(BF16)
    keys = nn(rows, wk[...])
    k[...] = keys.astype(BF16)
    k_t[...] = keys.T.astype(BF16)
    values = nn(rows, wv[...]) + bias[:, columns:]
    v[...] = values.astype(BF16)
    v_t[...] = values.T.astype(BF16)


def project(at, x, gain, shift_, weights, bias, count, previous):
    piece, width = x.shape
    columns = weights[0].shape[1]
    tile = min(256, piece)
    steps = piece // tile
    whole = lambda shape: pl.BlockSpec(shape, lambda i: (0, 0))
    rows = lambda n: pl.BlockSpec((tile, n), lambda i: (at * steps + i, 0))
    turned = pl.BlockSpec((columns, tile), lambda i: (0, at * steps + i))
    length = piece * count
    inputs = [
        (x, pl.BlockSpec((tile, width), lambda i: (i, 0))),
        (gain, whole((1, width))),
        (shift_, whole((1, width))),
        *[(item, whole((width, columns))) for item in weights],
        (bias, whole((1, 2 * columns))),
    ]
    shape = lambda *dims: jax.ShapeDtypeStruct(dims, BF16)
    shared = [(shape(length, width), rows(width))] + [(shape(length, columns), rows(columns))] * 3
    shared += [(shape(columns, length), turned)] * 2
    return call_on_block(
        project_kernel, (steps,), inputs, [], shared, previous, [],
        cost(6 * piece * width * columns, 4 * piece * width + 6 * width * columns + 10 * piece * columns),
    )[1]


def rows_of(block, piece):
    return pl.ds(pl.multiple_of(block * piece, piece), piece)


def scores_of(key_ref, bias_ref, query, rel, piece, diagonal):
    rows = rows_of(rel, piece)
    scores = nt(key_ref[rows, :], query) * (FACTOR * LOG2E)
    key_bias = bias_ref[rows, :]
    if not diagonal:
        return scores + key_bias
    key_at = lax.broadcasted_iota(jnp.int32, scores.shape, 0)
    query_at = lax.broadcasted_iota(jnp.int32, scores.shape, 1)
    allowed = ((key_at < query_at) & (key_bias > -1.0)) | (key_at == query_at)
    return jnp.where(allowed, scores, NEG)


def attend_kernel(at, rank_ref, query_ref, key_ref, value_t, bias_ref, proj_ref, part_ref, attended, lse_ref, score_ref, sum_ref):
    piece = query_ref.shape[0]
    rank = rank_ref[0]
    head = pl.program_id(0)
    true = lax.bitwise_xor(at, rank)
    query = query_ref[...]

    def first(block, top):
        scores = scores_of(key_ref, bias_ref, query, lax.bitwise_xor(block, rank), piece, False)
        score_ref[rows_of(block, piece), :] = scores
        return jnp.maximum(top, jnp.max(scores, axis=0, keepdims=True))

    last = scores_of(key_ref, bias_ref, query, at, piece, True)
    top = lax.fori_loop(0, true, first, jnp.max(last, axis=0, keepdims=True))

    def weigh(scores, rel):
        weights = jnp.exp2(scores - top)
        return jnp.sum(weights, axis=0, keepdims=True), nn(value_t[:, rows_of(rel, piece)], weights.astype(BF16))

    def second(block, carry):
        total, out = carry
        more, part = weigh(score_ref[rows_of(block, piece), :], lax.bitwise_xor(block, rank))
        return total + more, out + part

    total, out = lax.fori_loop(0, true, second, weigh(last, at))
    result = (out / total).T.astype(BF16)
    attended[...] = result
    lse_ref[0] = top + jnp.log2(total)
    term = nn(result, proj_ref[...])

    @pl.when(head == 0)
    def _():
        sum_ref[...] = term

    @pl.when(head > 0)
    def _():
        sum_ref[...] += term

    @pl.when(head == pl.num_programs(0) - 1)
    def _():
        part_ref[...] = sum_ref[...].astype(BF16)


def attend(at, rank, q, k, v_t, key_bias, proj, piece, previous):
    length, columns = q.shape
    heads, width = columns // HEAD_DIM, proj.shape[1]
    inputs = [
        (q, pl.BlockSpec((piece, HEAD_DIM), lambda h, r: (at, h))),
        (k, pl.BlockSpec((length, HEAD_DIM), lambda h, r: (0, h))),
        (v_t, pl.BlockSpec((HEAD_DIM, length), lambda h, r: (h, 0))),
        (key_bias, pl.BlockSpec((length, 1), lambda h, r: (0, 0))),
        (proj, pl.BlockSpec((HEAD_DIM, width), lambda h, r: (h, 0))),
    ]
    fresh = [(jax.ShapeDtypeStruct((piece, width), BF16), pl.BlockSpec((piece, width), lambda h, r: (0, 0)))]
    shared = [
        (jax.ShapeDtypeStruct((length, columns), BF16), pl.BlockSpec((piece, HEAD_DIM), lambda h, r: (at, h))),
        (jax.ShapeDtypeStruct((heads, 1, length), F32), pl.BlockSpec((1, 1, piece), lambda h, r: (h, 0, at))),
    ]
    scratch = [pltpu.VMEM((length, piece), F32), pltpu.VMEM((piece, width), F32)]
    (part,), shared = call_on_block(
        functools.partial(attend_kernel, at), (heads,), inputs, fresh, shared, previous, scratch,
        cost(
            2 * length * piece * columns * 1.3 + 2 * piece * columns * width, 6 * length * columns + 2 * width * columns,
            heads * length * piece * 0.6,
        ), rank,
    )
    return part, shared


def feed_kernel(normed, cot, fc, bias, down, part, active_out, hidden_out, normed_out, cot_out, sum_ref):
    step = pl.program_id(0)
    weights = fc[...]
    hidden = nn(normed[...], weights) + bias[...]
    grad_active = nt(cot[...], down[...])
    inner = math.sqrt(2 / math.pi) * (hidden + 0.044715 * (hidden * hidden * hidden))
    bent = jnp.tanh(inner)
    half = 0.5 * (1.0 + bent)
    active_out[...] = (hidden * half).astype(BF16)
    slope = half + (0.5 * hidden) * (1.0 - bent * bent) * (
        math.sqrt(2 / math.pi) * (1.0 + (3 * 0.044715) * (hidden * hidden))
    )
    grad_hidden = (grad_active * slope).astype(BF16)
    hidden_out[...] = grad_hidden
    term = nt(grad_hidden, weights)

    @pl.when(step == 0)
    def _():
        sum_ref[...] = term
        normed_out[...] = normed[...]
        cot_out[...] = cot[...]

    @pl.when(step > 0)
    def _():
        sum_ref[...] += term

    @pl.when(step == pl.num_programs(0) - 1)
    def _():
        part[...] = sum_ref[...].astype(BF16)


def feed(at, normed, cot, fc, bias, down, count, previous):
    piece, width = normed.shape
    inner = fc.shape[1]
    tile = min(512, inner)
    length = piece * count
    rows = pl.BlockSpec((piece, width), lambda j: (0, 0))
    inputs = [
        (normed, rows),
        (cot, rows),
        (fc, pl.BlockSpec((width, tile), lambda j: (0, j))),
        (bias, pl.BlockSpec((1, tile), lambda j: (0, j))),
        (down, pl.BlockSpec((tile, width), lambda j: (j, 0))),
    ]
    shape = lambda n: jax.ShapeDtypeStruct((length, n), BF16)
    columns = pl.BlockSpec((piece, tile), lambda j: (at, j))
    here = pl.BlockSpec((piece, width), lambda j: (at, 0))
    fresh = [(jax.ShapeDtypeStruct((piece, width), BF16), rows)]
    shared = [(shape(inner), columns), (shape(inner), columns), (shape(width), here), (shape(width), here)]
    (part,), shared = call_on_block(
        feed_kernel, (inner // tile,), inputs, fresh, shared, previous, [pltpu.VMEM((piece, width), F32)],
        cost(6 * piece * width * inner, 4 * width * inner + 10 * piece * width + 4 * piece * inner, piece * inner),
    )
    return part, shared


def retreat_kernel(
    at, first_call, last_call, rank_ref, low_ref, proj_ref, query_ref, lse_ref, key_ref, value_ref, key_t, bias_ref, *rest
):
    rest = list(rest)
    key_in, value_in = (None, None) if first_call else (rest.pop(0), rest.pop(0))
    key_out, value_out, query_out, low_out, prob_ref, chance_ref, key_sum, value_sum = rest
    piece = query_ref.shape[0]
    rank = rank_ref[0]
    true = lax.bitwise_xor(at, rank)

    @pl.when(pl.program_id(0) == 0)
    def _():
        low_out[...] = low_ref[...]

    if first_call:
        key_sum[...] = jnp.zeros_like(key_sum)
        value_sum[...] = jnp.zeros_like(value_sum)
    else:
        key_sum[...] = key_in[...]
        value_sum[...] = value_in[...]
    query, lse = query_ref[...], lse_ref[0]
    grad = nt(low_ref[...], proj_ref[...]).astype(BF16)

    def measure(scores, rel):
        rows = rows_of(rel, piece)
        probs = jnp.exp2(scores - lse)
        grad_chances = nt(value_ref[rows, :], grad)
        value_sum[rows, :] += nn(probs.astype(BF16), grad)
        prob_ref[rows, :] = probs
        chance_ref[rows, :] = grad_chances
        return jnp.sum(probs * grad_chances, axis=0, keepdims=True)

    def first(block, weighted):
        rel = lax.bitwise_xor(block, rank)
        return weighted + measure(scores_of(key_ref, bias_ref, query, rel, piece, False), rel)

    last = scores_of(key_ref, bias_ref, query, at, piece, True)
    weighted = lax.fori_loop(0, true, first, measure(last, at))

    def second(block, total):
        rows = rows_of(lax.bitwise_xor(block, rank), piece)
        grad_scores = (prob_ref[rows, :] * (chance_ref[rows, :] - weighted)).astype(BF16)
        key_sum[rows, :] += nn(grad_scores, query)
        return total + nn(key_t[:, rows], grad_scores)

    total = lax.fori_loop(0, true + 1, second, jnp.zeros((HEAD_DIM, piece), F32))
    query_out[...] = (total * FACTOR).T.astype(BF16)
    if last_call:
        key_out[...] = (key_sum[...] * FACTOR).astype(BF16)
        value_out[...] = value_sum[...].astype(BF16)
    else:
        key_out[...] = key_sum[...]
        value_out[...] = value_sum[...]


def retreat(at, rank, low, proj, q, lse, k, v, k_t, key_bias, sums, previous, last_call):
    length, columns = q.shape
    piece, width = low.shape
    heads = columns // HEAD_DIM
    tall = pl.BlockSpec((length, HEAD_DIM), lambda h, r: (0, h))
    part = pl.BlockSpec((piece, HEAD_DIM), lambda h, r: (at, h))
    inputs = [
        (low, pl.BlockSpec((piece, width), lambda h, r: (0, 0))),
        (proj, pl.BlockSpec((HEAD_DIM, width), lambda h, r: (h, 0))),
        (q, part),
        (lse, pl.BlockSpec((1, 1, piece), lambda h, r: (h, 0, at))),
        (k, tall),
        (v, tall),
        (k_t, pl.BlockSpec((HEAD_DIM, length), lambda h, r: (h, 0))),
        (key_bias, pl.BlockSpec((length, 1), lambda h, r: (0, 0))),
    ]
    if sums is not None:
        inputs += [(item, tall) for item in sums]
    kind = BF16 if last_call else F32
    fresh = [(jax.ShapeDtypeStruct((length, columns), kind), tall)] * 2
    shared = [
        (jax.ShapeDtypeStruct((length, columns), BF16), part),
        (jax.ShapeDtypeStruct((length, width), BF16), pl.BlockSpec((piece, width), lambda h, r: (at, 0))),
    ]
    scratch = [pltpu.VMEM((length, piece), F32)] * 2 + [pltpu.VMEM((length, HEAD_DIM), F32)] * 2
    return call_on_block(
        functools.partial(retreat_kernel, at, sums is None, last_call), (heads,), inputs, fresh, shared, previous,
        scratch,
        cost(
            5 * 1.3 * length * piece * columns + 2 * piece * columns * width, 20 * length * columns,
            heads * length * piece * 0.6,
        ), rank,
    )


def back_kernel(dq, dk, dv, wq, wk, wv, out):
    out[...] = (nt(dq[...], wq[...]) + nt(dk[...], wk[...]) + nt(dv[...], wv[...])).astype(BF16)


def back(at, grads, weights, piece):
    columns, width = grads[0].shape[1], weights[0].shape[0]
    tile = min(512, width)
    return pl.pallas_call(
        back_kernel,
        grid=(width // tile,),
        in_specs=[pl.BlockSpec((piece, columns), lambda j: (at, 0))] * 3
        + [pl.BlockSpec((tile, columns), lambda j: (j, 0))] * 3,
        out_specs=pl.BlockSpec((piece, tile), lambda j: (0, j)),
        out_shape=jax.ShapeDtypeStruct((piece, width), BF16),
        compiler_params=params(),
        cost_estimate=cost(6 * piece * width * columns, 6 * width * columns + 6 * piece * columns + 2 * piece * width),
    )(*grads, *weights)


def part_specs(parts, tile, steps, width):
    arrays, specs = [], []
    for part in parts:
        if isinstance(part, tuple):
            middle = steps // 2
            arrays += list(part)
            specs.append(pl.BlockSpec((tile, width), lambda i: (jnp.minimum(i, middle - 1), 0)))
            specs.append(pl.BlockSpec((tile, width), lambda i: (jnp.maximum(i - middle, 0), 0)))
        else:
            arrays.append(part)
            specs.append(pl.BlockSpec((tile, width), lambda i: (i, 0)))
    return arrays, specs


def add_parts(kinds, refs):
    total = None
    upper = pl.program_id(0) < pl.num_programs(0) // 2
    for kind in kinds:
        if kind:
            high, low = refs.pop(0)[...], refs.pop(0)[...]
            term = jnp.where(upper, high.astype(F32), low.astype(F32))
        else:
            term = refs.pop(0)[...].astype(F32)
        total = term if total is None else total + term
    return total


def rowwise(kernel, parts, rows, vectors, outputs, sums):
    count, width = rows[0].shape
    tile = min(128, count // 2)
    steps = count // tile
    arrays, specs = part_specs(parts, tile, steps, width)
    kinds = [isinstance(part, tuple) for part in parts]
    specs += [pl.BlockSpec((tile, width), lambda i: (i, 0))] * len(rows)
    specs += [pl.BlockSpec((1, width), lambda i: (0, 0))] * len(vectors)

    def body(*refs):
        refs = list(refs)
        total = add_parts(kinds, refs)
        tiles = [refs.pop(0)[...] for _ in rows]
        given = [refs.pop(0)[...] for _ in vectors]
        results = kernel(total, tiles, given)
        for result, _ in zip(results, outputs):
            refs.pop(0)[...] = result
        for result in results[len(outputs) :]:
            ref = refs.pop(0)
            column = jnp.sum(result, axis=0, keepdims=True)

            @pl.when(pl.program_id(0) == 0)
            def _():
                ref[...] = column

            @pl.when(pl.program_id(0) > 0)
            def _():
                ref[...] += column

    return pl.pallas_call(
        body,
        grid=(steps,),
        in_specs=specs,
        out_specs=[pl.BlockSpec((tile, width), lambda i: (i, 0))] * len(outputs)
        + [pl.BlockSpec((1, width), lambda i: (0, 0))] * sums,
        out_shape=[jax.ShapeDtypeStruct((count, width), kind) for kind in outputs]
        + [jax.ShapeDtypeStruct((1, width), F32)] * sums,
        compiler_params=params(),
        cost_estimate=cost(20 * count * width, count * width * (2 * len(arrays) + 4 * len(rows) + 4 * len(outputs))),
    )(*arrays, *rows, *vectors)


def middle_kernel(total, rows, vectors):
    (tokens,), (bias, gain, shift_) = rows, vectors
    middle = tokens.astype(F32) + (total + bias)
    return middle, (norm_parts(middle)[0] * gain + shift_).astype(BF16)


def out_kernel(total, rows, vectors):
    return (((rows[0] + (total + vectors[0])).astype(BF16)),)


def middle_back_kernel(total, rows, vectors):
    (middle, cot), (gain,) = rows, vectors
    normed, scale = norm_parts(middle)
    cot = cot.astype(F32)
    grad = cot + norm_backward(normed, scale, gain, total)
    low = grad.astype(BF16)
    return grad, low, total * normed, total, low.astype(F32), cot


def tokens_back_kernel(total, rows, vectors):
    (tokens, grad_middle), (gain,) = rows, vectors
    normed, scale = norm_parts(tokens.astype(F32))
    return grad_middle + norm_backward(normed, scale, gain, total), total * normed, total


def lay_out(rank, blocks, width, places):
    rows = blocks[0][0].shape[0]
    count, each = len(blocks), len(blocks[0])
    unit = places[1]

    def body(rank_ref, *refs):
        out = refs[-1]
        for k in range(count):
            source = lax.bitwise_xor(k, rank_ref[0])
            for array, column, target in places[0](source):
                out[:, pl.ds(pl.multiple_of(target * unit, unit), unit)] = refs[k * each + array][
                    :, column * unit : (column + 1) * unit
                ].astype(F32)

    arrays = [item for block in blocks for item in block]
    return pl.pallas_call(
        body,
        grid_spec=pltpu.PrefetchScalarGridSpec(
            num_scalar_prefetch=1,
            grid=(1,),
            in_specs=[pl.BlockSpec(item.shape, lambda i, r: (0, 0)) for item in arrays],
            out_specs=pl.BlockSpec((rows, width), lambda i, r: (0, 0)),
        ),
        out_shape=jax.ShapeDtypeStruct((rows, width), F32),
        compiler_params=params(),
        cost_estimate=cost(rows * width, 6 * rows * width),
    )(rank, *arrays)


def after(value, *others):
    return lax.optimization_barrier((value, *others))[0]


def shift(value, axis, distance):
    count = lax.axis_size(axis)
    return lax.ppermute(value, axis, [(i, i ^ distance) for i in range(count)])


def gather_blocks(value, axis="seq"):
    return [value] + [shift(value, axis, k) for k in range(1, lax.axis_size(axis))]


def scatter_blocks(blocks, axis="seq"):
    return [blocks[0]] + [shift(blocks[k], axis, k) for k in range(1, lax.axis_size(axis))]


def gather_plane(value):
    if lax.axis_size("seq") != 4:
        return gather_blocks(value)
    half = value.shape[0] // 2
    one, two = shift(value, "seq", 1), shift(value, "seq", 2)
    three = jnp.concatenate([shift(one[:half], "seq", 2), shift(two[half:], "seq", 1)], axis=0)
    return [value, one, two, three]


def scatter_plane(blocks):
    if lax.axis_size("seq") != 4:
        return scatter_blocks(blocks)
    half = blocks[0].shape[0] // 2
    up, low = shift(blocks[3][:half], "seq", 1), shift(blocks[3][half:], "seq", 2)
    one = shift(blocks[1][:half], "seq", 1)
    two = shift(blocks[2][half:], "seq", 2)
    one_low = (blocks[1][half:].astype(F32) + low.astype(F32)).astype(BF16)
    two_up = (blocks[2][:half].astype(F32) + up.astype(F32)).astype(BF16)
    return [blocks[0], (one, shift(one_low, "seq", 1)), (shift(two_up, "seq", 2), two)]


def by_rank(blocks, rank):
    bit = 1
    while bit < len(blocks):
        odd = (rank & bit) != 0
        blocks = [jnp.where(odd, blocks[k ^ bit], blocks[k]) for k in range(len(blocks))]
        bit *= 2
    return blocks


def pick(pieces, at):
    return lax.dynamic_index_in_dim(pieces, at, axis=0, keepdims=False)


def exchange(pieces, rank):
    return scatter_blocks([pick(pieces, rank ^ k) for k in range(pieces.shape[0])])


def small_scatter(pieces, dp_rank, seq_rank):
    total = 0.0
    sent = [lax.dynamic_index_in_dim(pieces, seq_rank ^ k, axis=1, keepdims=False) for k in range(pieces.shape[1])]
    for part in scatter_blocks(sent):
        total = total + part
    sent = [pick(total, dp_rank ^ k) for k in range(pieces.shape[0])]
    total = 0.0
    for part in scatter_blocks(sent, "dp"):
        total = total + part
    return total


def swap_pairs(dp_count, seq_count, sub):
    pairs = []
    for d in range(dp_count):
        for s in range(seq_count):
            source = ((d // sub) * sub + s % sub) * seq_count + (s // sub) * sub + d % sub
            pairs.append((source, d * seq_count + s))
    return pairs


def gather_dp(value):
    return lax.all_gather(value, "dp", axis=0, tiled=True)


def scatter_dp(value):
    return lax.psum_scatter(value, "dp", scatter_dimension=0, tiled=True)


def shards(
    tokens,
    cotangent,
    lengths,
    key_mask,
    attn_gain,
    attn_shift,
    qkv_weight,
    qv_bias,
    proj_weight,
    proj_bias,
    mlp_gain,
    mlp_shift,
    fc_weight,
    fc_bias,
    down_weight,
    down_bias,
):
    _, piece, width = tokens.shape
    dp_count, seq_count = lax.axis_size("dp"), lax.axis_size("seq")
    dp_rank, seq_rank = lax.axis_index("dp"), lax.axis_index("seq")
    own_heads = HEADS // seq_count
    own_width = own_heads * HEAD_DIM
    rows = qkv_weight.shape[0]
    sub = HEAD_DIM // proj_weight.shape[0]
    high = seq_count // sub
    block = down_weight.shape[0]
    rank = jnp.reshape(seq_rank, (1,)).astype(jnp.int32)
    swap = swap_pairs(dp_count, seq_count, sub)
    order = list(range(seq_count - 1, -1, -1))
    if seq_count == 4:
        order = [3, 1, 2, 0]

    qkv_pieces = (
        qkv_weight.reshape(rows, 3, own_heads, sub, high, HEAD_DIM)
        .transpose(4, 3, 0, 1, 2, 5)
        .reshape(seq_count, rows, 3 * own_width)
    )
    qkv_rows = jnp.concatenate(by_rank(exchange(qkv_pieces, seq_rank), seq_rank), axis=0)
    weights = [gather_dp(qkv_rows[:, i * own_width : (i + 1) * own_width]) for i in range(3)]
    tokens_own = after(tokens[0], qkv_pieces)
    token_blocks = gather_plane(tokens_own)

    small = (attn_gain, attn_shift, qv_bias, proj_bias, mlp_gain, mlp_shift, fc_bias, down_bias)
    sizes = [item.shape[0] for item in small]
    positions = seq_rank * piece + jnp.arange(piece, dtype=jnp.int32)
    own_flags = ((key_mask[0] == 1) & (positions < lengths[0])).astype(BF16)
    packed = after(jnp.concatenate(small + (own_flags,)), qkv_rows)
    blocks = gather_blocks(packed)
    flags = jnp.concatenate([item[-piece:] for item in blocks])
    key_bias = jnp.where(flags > 0, 0.0, NEG).astype(F32)[:, None]
    packed = jnp.stack(by_rank([item[:-piece] for item in blocks], seq_rank))
    packed = jnp.stack(by_rank(gather_blocks(packed, "dp"), dp_rank)).astype(F32)
    parts, start = [], 0
    for size in sizes:
        parts.append(packed[:, :, start : start + size])
        start += size
    whole = [part.reshape(1, -1) for part in parts]
    gain_one, shift_one, qv_full, proj_shift, gain_two, shift_two, _, down_shift = whole
    fc_shift = lax.dynamic_index_in_dim(parts[6], seq_rank, axis=1, keepdims=False).reshape(1, -1)
    rank_low, rank_high = seq_rank % sub, seq_rank // sub
    qv_heads = qv_full.reshape(2, own_heads, sub, high, HEAD_DIM)
    qv_own = lax.dynamic_index_in_dim(
        lax.dynamic_index_in_dim(qv_heads, rank_low, axis=2, keepdims=False), rank_high, axis=2, keepdims=False
    )
    qv_own = qv_own.reshape(1, -1)

    proj_full = gather_dp(lax.ppermute(after(proj_weight, qkv_rows), BOTH, swap))
    fc_pieces = (
        after(fc_weight, qkv_rows)
        .reshape(rows, dp_count, seq_count, block)
        .transpose(2, 0, 1, 3)
        .reshape(seq_count, rows, dp_count * block)
    )
    fc_rows = jnp.concatenate(by_rank(exchange(fc_pieces, seq_rank), seq_rank), axis=0)
    fc_full = gather_dp(fc_rows)
    down_full = gather_dp(after(down_weight, fc_rows))

    cot_blocks = gather_plane(after(cotangent[0], token_blocks[-1]))
    shared = None
    for k in range(seq_count):
        shared = project(k, token_blocks[k], gain_one, shift_one, weights, qv_own, seq_count, shared)
    normed_one, q, keys, values, keys_t, values_t = shared
    proj_terms, shared = [None] * seq_count, None
    for k in order:
        proj_terms[k], shared = attend(k, rank, q, keys, values_t, key_bias, proj_full, piece, shared)
    attended, lse = shared
    middle, normed_two = rowwise(
        middle_kernel, scatter_plane(proj_terms), [tokens_own], [proj_shift, gain_two, shift_two], [F32, BF16], 0
    )

    normed_blocks = gather_plane(normed_two)
    grad_terms, shared = [], None
    for k in range(seq_count):
        term, shared = feed(k, normed_blocks[k], cot_blocks[k], fc_full, fc_shift, down_full, seq_count, shared)
        grad_terms.append(term)
    active, grad_hidden, normed_all, cot_all = shared
    grad_down = tn(active, cot_all).astype(BF16)
    grad_fc = tn(normed_all, grad_hidden).astype(BF16)
    received = scatter_plane(grad_terms)
    received[0] = after(received[0], grad_down, grad_fc)
    grad_middle, grad_mid_low, *sums_two = rowwise(
        middle_back_kernel, received, [middle, cotangent[0]], [gain_two], [F32, BF16], 4
    )
    low_blocks = gather_plane(grad_mid_low)
    grad_down = scatter_dp(grad_down)
    grad_fc = scatter_dp(grad_fc)
    down_terms = [
        nn(active[k * piece : (k + 1) * piece], down_full).astype(BF16) for k in range(seq_count)
    ]
    low_blocks[1], *down_terms = lax.optimization_barrier((low_blocks[1], *down_terms))
    down_terms, _ = lax.optimization_barrier((down_terms, low_blocks[-1]))

    sums, shared = None, None
    for k in range(seq_count):
        sums, shared = retreat(
            k, rank, low_blocks[k], proj_full, q, lse, keys, values, keys_t, key_bias, sums, shared, k == seq_count - 1
        )
    grad_q, low_all = shared
    grads = [grad_q, sums[0], sums[1]]
    grad_qkv = [scatter_dp(tn(normed_one, item).astype(BF16)) for item in grads]
    back_terms = [None] * seq_count
    for k in order:
        back_terms[k] = back(k, grads, weights, piece)
    tokens_grad, *sums_one = rowwise(
        tokens_back_kernel, scatter_plane(back_terms), [tokens_own, grad_middle], [gain_one], [F32], 2
    )
    (block_out,) = rowwise(out_kernel, scatter_plane(down_terms), [middle], [down_shift], [BF16], 0)
    grad_proj = scatter_dp(tn(attended, low_all).astype(BF16))
    grad_proj = lax.ppermute(grad_proj, BOTH, swap).astype(F32)

    blocks = exchange(grad_fc.reshape(seq_count, rows, dp_count * block), seq_rank)
    if block % 128 == 0:
        fc_places = lambda s: [(0, d, d * seq_count + s) for d in range(dp_count)]
        grad_fc = lay_out(rank, [[item] for item in blocks], fc_weight.shape[1], (fc_places, block))
    else:
        blocks = [item.reshape(rows, dp_count, block) for item in by_rank(blocks, seq_rank)]
        grad_fc = jnp.stack(blocks, axis=2).reshape(fc_weight.shape).astype(F32)
    blocks = list(zip(*[exchange(item.reshape(seq_count, rows, own_width), seq_rank) for item in grad_qkv]))
    qkv_places = lambda s: [
        (part, head, part * HEADS + (head * sub + s % sub) * high + s // sub)
        for part in range(3)
        for head in range(own_heads)
    ]
    grad_qkv_weight = lay_out(rank, blocks, qkv_weight.shape[1], (qkv_places, HEAD_DIM))

    def spread(vector):
        return vector.reshape(dp_count, seq_count, -1)

    here = (jnp.arange(seq_count) == seq_rank).astype(F32)
    hidden_sums = jnp.sum(grad_hidden.astype(F32), axis=0).reshape(dp_count, 1, -1) * here[None, :, None]
    early = jnp.concatenate([spread(item) for item in sums_two] + [hidden_sums], axis=2)
    early = small_scatter(early, dp_rank, seq_rank)
    qv_sums = jnp.stack([jnp.sum(item.astype(F32), axis=0) for item in (grads[0], grads[2])])
    here = (jnp.arange(sub) == rank_low)[:, None] & (jnp.arange(high) == rank_high)[None, :]
    qv_sums = qv_sums.reshape(2, own_heads, 1, 1, HEAD_DIM) * here.astype(F32)[None, None, :, :, None]
    late = jnp.concatenate([spread(item) for item in sums_one] + [spread(qv_sums)], axis=2)
    late = small_scatter(late, dp_rank, seq_rank)
    share = attn_gain.shape[0]
    return (
        block_out[None],
        tokens_grad[None],
        late[:share],
        late[share : 2 * share],
        grad_qkv_weight,
        late[2 * share :],
        grad_proj,
        early[2 * share : 3 * share],
        early[:share],
        early[share : 2 * share],
        grad_fc,
        early[4 * share :],
        grad_down.astype(F32),
        early[3 * share : 4 * share],
    )


def solution(mesh):
    in_specs = (
        P("dp", "seq", None),
        P("dp", "seq", None),
        P("dp"),
        P("dp", "seq"),
        P(BOTH),
        P(BOTH),
        P(BOTH, None),
        P(BOTH),
        P(BOTH, None),
        P(BOTH),
        P(BOTH),
        P(BOTH),
        P(BOTH, None),
        P(BOTH),
        P(BOTH, None),
        P(BOTH),
    )
    out_specs = (
        P("dp", "seq", None),
        P("dp", "seq", None),
        P(BOTH),
        P(BOTH),
        P(BOTH, None),
        P(BOTH),
        P(BOTH, None),
        P(BOTH),
        P(BOTH),
        P(BOTH),
        P(BOTH, None),
        P(BOTH),
        P(BOTH, None),
        P(BOTH),
    )
    return jax.shard_map(shards, mesh=mesh, in_specs=in_specs, out_specs=out_specs, check_vma=False)
```

```python
import functools
import math

import jax
import jax.numpy as jnp
from jax import lax
from jax.experimental import pallas as pl
from jax.experimental.pallas import tpu as pltpu
from jax.sharding import PartitionSpec as P

HEADS = 16
HEAD_DIM = 128
EPS = 1e-05
NEG = -1e30
FACTOR = HEAD_DIM ** (-0.5)
LOG2E = math.log2(math.e)
F32 = jnp.float32
BF16 = jnp.bfloat16
BOTH = ("dp", "seq")
MESH = pl.DeviceIdType.MESH


def nn(left, right):
    return lax.dot_general(left, right, (((1,), (0,)), ((), ())), preferred_element_type=F32)


def nt(left, right):
    return lax.dot_general(left, right, (((1,), (1,)), ((), ())), preferred_element_type=F32)


def tn(left, right):
    return lax.dot_general(left, right, (((0,), (0,)), ((), ())), preferred_element_type=F32)


def params(limit_mib=56):
    return pltpu.CompilerParams(dimension_semantics=("arbitrary",), vmem_limit_bytes=limit_mib * 2**20)


def cost(flops, moved, exps=0):
    return pl.CostEstimate(flops=int(flops), bytes_accessed=int(moved), transcendentals=int(exps))


def call_on_block(kernel, grid, inputs, fresh, shared, previous, scratch, estimate, rank=None):
    arrays = [item for item, _ in inputs]
    specs = [spec for _, spec in inputs]
    aliases = {}
    lead = 0 if rank is None else 1
    if previous is not None:
        for at, item in enumerate(previous):
            aliases[lead + len(arrays)] = len(fresh) + at
            arrays.append(item)
            specs.append(pl.BlockSpec(memory_space=pl.ANY))
    count = len(inputs)
    skipped = 0 if previous is None else len(previous)

    def body(*refs):
        refs = list(refs)
        kernel(*refs[: lead + count], *refs[lead + count + skipped :])

    out_specs = [spec for _, spec in fresh] + [spec for _, spec in shared]
    out_shape = [shape for shape, _ in fresh] + [shape for shape, _ in shared]
    if rank is None:
        results = pl.pallas_call(
            body, grid=grid, in_specs=specs, out_specs=out_specs, out_shape=out_shape, scratch_shapes=scratch,
            input_output_aliases=aliases, compiler_params=params(), cost_estimate=estimate,
        )(*arrays)
    else:
        results = pl.pallas_call(
            body,
            grid_spec=pltpu.PrefetchScalarGridSpec(
                num_scalar_prefetch=1, grid=grid, in_specs=specs, out_specs=out_specs, scratch_shapes=scratch
            ),
            out_shape=out_shape, input_output_aliases=aliases, compiler_params=params(), cost_estimate=estimate,
        )(rank, *arrays)
    return results[: len(fresh)], results[len(fresh) :]


def norm_parts(values):
    average = jnp.mean(values, axis=-1, keepdims=True)
    centred = values - average
    scale = lax.rsqrt(jnp.mean(centred * centred, axis=-1, keepdims=True) + EPS)
    return centred * scale, scale


def norm_backward(normed, scale, gain, upstream):
    weighted = upstream * gain
    return scale * (
        weighted
        - jnp.mean(weighted, axis=-1, keepdims=True)
        - normed * jnp.mean(weighted * normed, axis=-1, keepdims=True)
    )


def project_kernel(x, gain, shift_, wq, wk, wv, bias, normed, q, k, v, k_t, v_t):
    columns = wq.shape[1]
    rows = (norm_parts(x[...].astype(F32))[0] * gain[...] + shift_[...]).astype(BF16)
    normed[...] = rows
    q[...] = (nn(rows, wq[...]) + bias[:, :columns]).astype(BF16)
    keys = nn(rows, wk[...])
    k[...] = keys.astype(BF16)
    k_t[...] = keys.T.astype(BF16)
    values = nn(rows, wv[...]) + bias[:, columns:]
    v[...] = values.astype(BF16)
    v_t[...] = values.T.astype(BF16)


def project(at, x, first, gain, shift_, weights, bias, piece, count, previous):
    width = x.shape[1]
    columns = weights[0].shape[1]
    tile = min(256, piece)
    steps = piece // tile
    whole = lambda shape: pl.BlockSpec(shape, lambda i: (0, 0))
    rows = lambda n: pl.BlockSpec((tile, n), lambda i: (at * steps + i, 0))
    turned = pl.BlockSpec((columns, tile), lambda i: (0, at * steps + i))
    length = piece * count
    inputs = [
        (x, pl.BlockSpec((tile, width), lambda i: (first * steps + i, 0))),
        (gain, whole((1, width))),
        (shift_, whole((1, width))),
        *[(item, whole((width, columns))) for item in weights],
        (bias, whole((1, 2 * columns))),
    ]
    shape = lambda *dims: jax.ShapeDtypeStruct(dims, BF16)
    shared = [(shape(length, width), rows(width))] + [(shape(length, columns), rows(columns))] * 3
    shared += [(shape(columns, length), turned)] * 2
    return call_on_block(
        project_kernel, (steps,), inputs, [], shared, previous, [],
        cost(6 * piece * width * columns, 4 * piece * width + 6 * width * columns + 10 * piece * columns),
    )[1]


def rows_of(block, piece):
    return pl.ds(pl.multiple_of(block * piece, piece), piece)


def scores_of(key_ref, bias_ref, query, rel, piece, diagonal):
    rows = rows_of(rel, piece)
    scores = nt(key_ref[rows, :], query) * (FACTOR * LOG2E)
    key_bias = bias_ref[rows, :]
    if not diagonal:
        return scores + key_bias
    key_at = lax.broadcasted_iota(jnp.int32, scores.shape, 0)
    query_at = lax.broadcasted_iota(jnp.int32, scores.shape, 1)
    allowed = ((key_at < query_at) & (key_bias > -1.0)) | (key_at == query_at)
    return jnp.where(allowed, scores, NEG)


def attend_kernel(at, rank_ref, query_ref, key_ref, value_t, bias_ref, proj_ref, part_ref, attended, lse_ref, score_ref, sum_ref):
    piece = query_ref.shape[0]
    rank = rank_ref[0]
    head = pl.program_id(0)
    true = lax.bitwise_xor(at, rank)
    query = query_ref[...]

    def first(block, top):
        scores = scores_of(key_ref, bias_ref, query, lax.bitwise_xor(block, rank), piece, False)
        score_ref[rows_of(block, piece), :] = scores
        return jnp.maximum(top, jnp.max(scores, axis=0, keepdims=True))

    last = scores_of(key_ref, bias_ref, query, at, piece, True)
    top = lax.fori_loop(0, true, first, jnp.max(last, axis=0, keepdims=True))

    def weigh(scores, rel):
        weights = jnp.exp2(scores - top)
        return jnp.sum(weights, axis=0, keepdims=True), nn(value_t[:, rows_of(rel, piece)], weights.astype(BF16))

    def second(block, carry):
        total, out = carry
        more, part = weigh(score_ref[rows_of(block, piece), :], lax.bitwise_xor(block, rank))
        return total + more, out + part

    total, out = lax.fori_loop(0, true, second, weigh(last, at))
    result = (out / total).T.astype(BF16)
    attended[...] = result
    lse_ref[0] = top + jnp.log2(total)
    term = nn(result, proj_ref[...])

    @pl.when(head == 0)
    def _():
        sum_ref[...] = term

    @pl.when(head > 0)
    def _():
        sum_ref[...] += term

    @pl.when(head == pl.num_programs(0) - 1)
    def _():
        part_ref[...] = sum_ref[...].astype(BF16)


def attend(at, rank, q, k, v_t, key_bias, proj, piece, previous):
    length, columns = q.shape
    heads, width = columns // HEAD_DIM, proj.shape[1]
    inputs = [
        (q, pl.BlockSpec((piece, HEAD_DIM), lambda h, r: (at, h))),
        (k, pl.BlockSpec((length, HEAD_DIM), lambda h, r: (0, h))),
        (v_t, pl.BlockSpec((HEAD_DIM, length), lambda h, r: (h, 0))),
        (key_bias, pl.BlockSpec((length, 1), lambda h, r: (0, 0))),
        (proj, pl.BlockSpec((HEAD_DIM, width), lambda h, r: (h, 0))),
    ]
    fresh = [(jax.ShapeDtypeStruct((piece, width), BF16), pl.BlockSpec((piece, width), lambda h, r: (0, 0)))]
    shared = [
        (jax.ShapeDtypeStruct((length, columns), BF16), pl.BlockSpec((piece, HEAD_DIM), lambda h, r: (at, h))),
        (jax.ShapeDtypeStruct((heads, 1, length), F32), pl.BlockSpec((1, 1, piece), lambda h, r: (h, 0, at))),
    ]
    scratch = [pltpu.VMEM((length, piece), F32), pltpu.VMEM((piece, width), F32)]
    (part,), shared = call_on_block(
        functools.partial(attend_kernel, at), (heads,), inputs, fresh, shared, previous, scratch,
        cost(
            2 * length * piece * columns * 1.3 + 2 * piece * columns * width, 6 * length * columns + 2 * width * columns,
            heads * length * piece * 0.6,
        ), rank,
    )
    return part, shared


def feed_kernel(normed, cot, fc, bias, down, part, active_out, hidden_out, normed_out, cot_out, sum_ref):
    step = pl.program_id(0)
    weights = fc[...]
    hidden = nn(normed[...], weights) + bias[...]
    grad_active = nt(cot[...], down[...])
    inner = math.sqrt(2 / math.pi) * (hidden + 0.044715 * (hidden * hidden * hidden))
    bent = jnp.tanh(inner)
    half = 0.5 * (1.0 + bent)
    active_out[...] = (hidden * half).astype(BF16)
    slope = half + (0.5 * hidden) * (1.0 - bent * bent) * (
        math.sqrt(2 / math.pi) * (1.0 + (3 * 0.044715) * (hidden * hidden))
    )
    grad_hidden = (grad_active * slope).astype(BF16)
    hidden_out[...] = grad_hidden
    term = nt(grad_hidden, weights)

    @pl.when(step == 0)
    def _():
        sum_ref[...] = term
        normed_out[...] = normed[...]
        cot_out[...] = cot[...]

    @pl.when(step > 0)
    def _():
        sum_ref[...] += term

    @pl.when(step == pl.num_programs(0) - 1)
    def _():
        part[...] = sum_ref[...].astype(BF16)


def feed(at, normed, cot, fc, bias, down, count, previous):
    piece, width = normed.shape
    inner = fc.shape[1]
    tile = min(512, inner)
    length = piece * count
    rows = pl.BlockSpec((piece, width), lambda j: (0, 0))
    inputs = [
        (normed, rows),
        (cot, rows),
        (fc, pl.BlockSpec((width, tile), lambda j: (0, j))),
        (bias, pl.BlockSpec((1, tile), lambda j: (0, j))),
        (down, pl.BlockSpec((tile, width), lambda j: (j, 0))),
    ]
    shape = lambda n: jax.ShapeDtypeStruct((length, n), BF16)
    columns = pl.BlockSpec((piece, tile), lambda j: (at, j))
    here = pl.BlockSpec((piece, width), lambda j: (at, 0))
    fresh = [(jax.ShapeDtypeStruct((piece, width), BF16), rows)]
    shared = [(shape(inner), columns), (shape(inner), columns), (shape(width), here), (shape(width), here)]
    (part,), shared = call_on_block(
        feed_kernel, (inner // tile,), inputs, fresh, shared, previous, [pltpu.VMEM((piece, width), F32)],
        cost(6 * piece * width * inner, 4 * width * inner + 10 * piece * width + 4 * piece * inner, piece * inner),
    )
    return part, shared


def retreat_kernel(
    at, first_call, last_call, rank_ref, low_ref, proj_ref, query_ref, lse_ref, key_ref, value_ref, key_t, bias_ref, *rest
):
    rest = list(rest)
    key_in, value_in = (None, None) if first_call else (rest.pop(0), rest.pop(0))
    key_out, value_out, query_out, low_out, prob_ref, chance_ref, key_sum, value_sum = rest
    piece = query_ref.shape[0]
    rank = rank_ref[0]
    true = lax.bitwise_xor(at, rank)

    @pl.when(pl.program_id(0) == 0)
    def _():
        low_out[...] = low_ref[...]

    if first_call:
        key_sum[...] = jnp.zeros_like(key_sum)
        value_sum[...] = jnp.zeros_like(value_sum)
    else:
        key_sum[...] = key_in[...]
        value_sum[...] = value_in[...]
    query, lse = query_ref[...], lse_ref[0]
    grad = nt(low_ref[...], proj_ref[...]).astype(BF16)

    def measure(scores, rel):
        rows = rows_of(rel, piece)
        probs = jnp.exp2(scores - lse)
        grad_chances = nt(value_ref[rows, :], grad)
        value_sum[rows, :] += nn(probs.astype(BF16), grad)
        prob_ref[rows, :] = probs
        chance_ref[rows, :] = grad_chances
        return jnp.sum(probs * grad_chances, axis=0, keepdims=True)

    def first(block, weighted):
        rel = lax.bitwise_xor(block, rank)
        return weighted + measure(scores_of(key_ref, bias_ref, query, rel, piece, False), rel)

    last = scores_of(key_ref, bias_ref, query, at, piece, True)
    weighted = lax.fori_loop(0, true, first, measure(last, at))

    def second(block, total):
        rows = rows_of(lax.bitwise_xor(block, rank), piece)
        grad_scores = (prob_ref[rows, :] * (chance_ref[rows, :] - weighted)).astype(BF16)
        key_sum[rows, :] += nn(grad_scores, query)
        return total + nn(key_t[:, rows], grad_scores)

    total = lax.fori_loop(0, true + 1, second, jnp.zeros((HEAD_DIM, piece), F32))
    query_out[...] = (total * FACTOR).T.astype(BF16)
    if last_call:
        key_out[...] = (key_sum[...] * FACTOR).astype(BF16)
        value_out[...] = value_sum[...].astype(BF16)
    else:
        key_out[...] = key_sum[...]
        value_out[...] = value_sum[...]


def retreat(at, rank, low, proj, q, lse, k, v, k_t, key_bias, sums, previous, last_call):
    length, columns = q.shape
    piece, width = low.shape
    heads = columns // HEAD_DIM
    tall = pl.BlockSpec((length, HEAD_DIM), lambda h, r: (0, h))
    part = pl.BlockSpec((piece, HEAD_DIM), lambda h, r: (at, h))
    inputs = [
        (low, pl.BlockSpec((piece, width), lambda h, r: (0, 0))),
        (proj, pl.BlockSpec((HEAD_DIM, width), lambda h, r: (h, 0))),
        (q, part),
        (lse, pl.BlockSpec((1, 1, piece), lambda h, r: (h, 0, at))),
        (k, tall),
        (v, tall),
        (k_t, pl.BlockSpec((HEAD_DIM, length), lambda h, r: (h, 0))),
        (key_bias, pl.BlockSpec((length, 1), lambda h, r: (0, 0))),
    ]
    if sums is not None:
        inputs += [(item, tall) for item in sums]
    kind = BF16 if last_call else F32
    fresh = [(jax.ShapeDtypeStruct((length, columns), kind), tall)] * 2
    shared = [
        (jax.ShapeDtypeStruct((length, columns), BF16), part),
        (jax.ShapeDtypeStruct((length, width), BF16), pl.BlockSpec((piece, width), lambda h, r: (at, 0))),
    ]
    scratch = [pltpu.VMEM((length, piece), F32)] * 2 + [pltpu.VMEM((length, HEAD_DIM), F32)] * 2
    return call_on_block(
        functools.partial(retreat_kernel, at, sums is None, last_call), (heads,), inputs, fresh, shared, previous,
        scratch,
        cost(
            5 * 1.3 * length * piece * columns + 2 * piece * columns * width, 20 * length * columns,
            heads * length * piece * 0.6,
        ), rank,
    )


def back_kernel(dq, dk, dv, wq, wk, wv, out):
    out[...] = (nt(dq[...], wq[...]) + nt(dk[...], wk[...]) + nt(dv[...], wv[...])).astype(BF16)


def back(at, grads, weights, piece):
    columns, width = grads[0].shape[1], weights[0].shape[0]
    tile = min(512, width)
    return pl.pallas_call(
        back_kernel,
        grid=(width // tile,),
        in_specs=[pl.BlockSpec((piece, columns), lambda j: (at, 0))] * 3
        + [pl.BlockSpec((tile, columns), lambda j: (j, 0))] * 3,
        out_specs=pl.BlockSpec((piece, tile), lambda j: (0, j)),
        out_shape=jax.ShapeDtypeStruct((piece, width), BF16),
        compiler_params=params(),
        cost_estimate=cost(6 * piece * width * columns, 6 * width * columns + 6 * piece * columns + 2 * piece * width),
    )(*grads, *weights)


def part_specs(parts, tile, steps, width):
    arrays, specs = [], []
    for part in parts:
        if isinstance(part, tuple):
            middle = steps // 2
            arrays += list(part)
            specs.append(pl.BlockSpec((tile, width), lambda i: (jnp.minimum(i, middle - 1), 0)))
            specs.append(pl.BlockSpec((tile, width), lambda i: (jnp.maximum(i - middle, 0), 0)))
        else:
            arrays.append(part)
            specs.append(pl.BlockSpec((tile, width), lambda i: (i, 0)))
    return arrays, specs


def add_parts(kinds, refs):
    total = None
    upper = pl.program_id(0) < pl.num_programs(0) // 2
    for kind in kinds:
        if kind:
            high, low = refs.pop(0)[...], refs.pop(0)[...]
            term = jnp.where(upper, high.astype(F32), low.astype(F32))
        else:
            term = refs.pop(0)[...].astype(F32)
        total = term if total is None else total + term
    return total


def rowwise(kernel, parts, rows, vectors, outputs, sums):
    count, width = rows[0].shape
    tile = min(128, count // 2)
    steps = count // tile
    arrays, specs = part_specs(parts, tile, steps, width)
    kinds = [isinstance(part, tuple) for part in parts]
    specs += [pl.BlockSpec((tile, width), lambda i: (i, 0))] * len(rows)
    specs += [pl.BlockSpec((1, width), lambda i: (0, 0))] * len(vectors)

    def body(*refs):
        refs = list(refs)
        total = add_parts(kinds, refs)
        tiles = [refs.pop(0)[...] for _ in rows]
        given = [refs.pop(0)[...] for _ in vectors]
        results = kernel(total, tiles, given)
        for result, _ in zip(results, outputs):
            refs.pop(0)[...] = result
        for result in results[len(outputs) :]:
            ref = refs.pop(0)
            column = jnp.sum(result, axis=0, keepdims=True)

            @pl.when(pl.program_id(0) == 0)
            def _():
                ref[...] = column

            @pl.when(pl.program_id(0) > 0)
            def _():
                ref[...] += column

    return pl.pallas_call(
        body,
        grid=(steps,),
        in_specs=specs,
        out_specs=[pl.BlockSpec((tile, width), lambda i: (i, 0))] * len(outputs)
        + [pl.BlockSpec((1, width), lambda i: (0, 0))] * sums,
        out_shape=[jax.ShapeDtypeStruct((count, width), kind) for kind in outputs]
        + [jax.ShapeDtypeStruct((1, width), F32)] * sums,
        compiler_params=params(),
        cost_estimate=cost(20 * count * width, count * width * (2 * len(arrays) + 4 * len(rows) + 4 * len(outputs))),
    )(*arrays, *rows, *vectors)


def middle_kernel(total, rows, vectors):
    (tokens,), (bias, gain, shift_) = rows, vectors
    middle = tokens.astype(F32) + (total + bias)
    return middle, (norm_parts(middle)[0] * gain + shift_).astype(BF16)


def out_kernel(total, rows, vectors):
    return (((rows[0] + (total + vectors[0])).astype(BF16)),)


def middle_back_kernel(total, rows, vectors):
    (middle, cot), (gain,) = rows, vectors
    normed, scale = norm_parts(middle)
    cot = cot.astype(F32)
    grad = cot + norm_backward(normed, scale, gain, total)
    low = grad.astype(BF16)
    return grad, low, total * normed, total, low.astype(F32), cot


def tokens_back_kernel(total, rows, vectors):
    (tokens, grad_middle), (gain,) = rows, vectors
    normed, scale = norm_parts(tokens.astype(F32))
    return grad_middle + norm_backward(normed, scale, gain, total), total * normed, total


def lay_out(rank, blocks, width, places):
    rows = blocks[0][0].shape[0]
    count, each = len(blocks), len(blocks[0])
    unit = places[1]

    def body(rank_ref, *refs):
        out = refs[-1]
        for k in range(count):
            source = lax.bitwise_xor(k, rank_ref[0])
            for array, column, target in places[0](source):
                out[:, pl.ds(pl.multiple_of(target * unit, unit), unit)] = refs[k * each + array][
                    :, column * unit : (column + 1) * unit
                ].astype(F32)

    arrays = [item for block in blocks for item in block]
    return pl.pallas_call(
        body,
        grid_spec=pltpu.PrefetchScalarGridSpec(
            num_scalar_prefetch=1,
            grid=(1,),
            in_specs=[pl.BlockSpec(item.shape, lambda i, r: (0, 0)) for item in arrays],
            out_specs=pl.BlockSpec((rows, width), lambda i, r: (0, 0)),
        ),
        out_shape=jax.ShapeDtypeStruct((rows, width), F32),
        compiler_params=params(),
        cost_estimate=cost(rows * width, 6 * rows * width),
    )(rank, *arrays)


def neighbours():
    rank = lax.axis_index("seq")
    return rank + 1 - 2 * lax.rem(rank, 2), rank + 2 - 4 * lax.rem(lax.div(rank, 2), 2)


def remote(source, target, send, receive, axis, device):
    return pltpu.make_async_remote_copy(
        src_ref=source, dst_ref=target, send_sem=send, recv_sem=receive, device_id={axis: device}, device_id_type=MESH
    )


def greet(axis, device):
    pl.semaphore_signal(pltpu.get_barrier_semaphore(), inc=1, device_id={axis: device}, device_id_type=MESH)


def opening_kernel(
    tokens, cot, down, fc_pieces, token_all, cot_all, down_full, fc_rows,
    local, send, receive, right_send, right_receive, left_send, left_receive, mate_send, mate_receive,
):
    piece = tokens.shape[0]
    half = piece // 2
    rows = down.shape[0]
    fine = fc_pieces.shape[1]
    me, place = lax.axis_index("seq"), lax.axis_index("dp")
    one, two = neighbours()
    three = 3 - me
    stages = lax.axis_size("dp") // 2
    level, core = lax.div(place, 2), lax.rem(place, 2)
    mate = place + 1 - 2 * core
    above, below = level < stages - 1, level > 0

    for device in (one, two, three):
        greet("seq", device)
    greet("dp", mate)
    pl.when(above)(lambda: greet("dp", place + 2))
    pl.when(below)(lambda: greet("dp", place - 2))
    pl.semaphore_wait(pltpu.get_barrier_semaphore(), 4 + above.astype(jnp.int32) + below.astype(jnp.int32))

    def block(ref, at, start=0, size=piece):
        return ref.at[pl.ds(at * piece + start, size)]

    def pair(source, target, at):
        return (
            remote(source, block(target, 1), send.at[at], receive.at[at], "seq", one),
            remote(source, block(target, 2), send.at[at + 1], receive.at[at + 1], "seq", two),
        )

    token_one, token_two = pair(tokens, token_all, 0)
    token_three = (
        remote(block(token_all, 1, 0, half), block(token_all, 3, 0, half), send.at[2], receive.at[2], "seq", two),
        remote(block(token_all, 2, half, half), block(token_all, 3, half, half), send.at[3], receive.at[3], "seq", one),
    )
    cot_one, cot_two = pair(cot, cot_all, 4)
    mine = fc_rows.at[pl.ds(me * fine, fine)]
    pieces = [
        remote(fc_pieces.at[device], mine, send.at[6 + i], receive.at[6 + i], "seq", device)
        for i, device in enumerate((one, two, three))
    ]
    shard = lambda ref, at: ref.at[pl.ds((2 * at + core) * rows, rows)]
    kept = [
        pltpu.make_async_copy(tokens, block(token_all, 0), local.at[0]),
        pltpu.make_async_copy(cot, block(cot_all, 0), local.at[1]),
        pltpu.make_async_copy(down, shard(down_full, level), local.at[2]),
        pltpu.make_async_copy(fc_pieces.at[me], mine, local.at[3]),
    ]

    def right(step):
        at = level - (step - 1)
        source = down if step == 1 else shard(down_full, at)
        return remote(source, shard(down_full, at), right_send.at[step - 1], right_receive.at[step - 1], "dp", place + 2)

    def left(step):
        at = level + (step - 1)
        source = down if step == 1 else shard(down_full, at)
        return remote(source, shard(down_full, at), left_send.at[step - 1], left_receive.at[step - 1], "dp", place - 2)

    def across(index, at):
        return remote(shard(down_full, at), shard(down_full, at), mate_send.at[index], mate_receive.at[index], "dp", mate)

    right_sends = lambda step: above & (level >= step - 1)
    left_sends = lambda step: below & (level <= stages - step)
    right_gets = lambda step: level >= step
    left_gets = lambda step: level + step <= stages - 1

    def relay(step):
        pl.when(right_sends(step))(lambda: right(step).start())
        pl.when(left_sends(step))(lambda: left(step).start())

    def take(step):
        @pl.when(right_gets(step))
        def _():
            remote(down, shard(down_full, level - step), right_send.at[step - 1], right_receive.at[step - 1], "dp", mate).wait_recv()
            across(step, level - step).start()

        @pl.when(left_gets(step))
        def _():
            remote(down, shard(down_full, level + step), left_send.at[step - 1], left_receive.at[step - 1], "dp", mate).wait_recv()
            across(stages - 1 + step, level + step).start()

    token_one.start()
    token_two.start()
    relay(1)
    for copy in pieces + kept:
        copy.start()
    remote(down, shard(down_full, level), mate_send.at[0], mate_receive.at[0], "dp", mate).start()
    take(1)
    relay(2)
    token_one.wait_recv()
    token_two.wait_recv()
    for copy in token_three:
        copy.start()
    take(2)
    relay(3)
    for copy in token_three:
        copy.wait_recv()
    cot_one.start()
    cot_two.start()
    take(3)
    for copy in kept:
        copy.wait()
    for copy in pieces:
        copy.wait()
    token_one.wait_send()
    token_two.wait_send()
    for copy in token_three:
        copy.wait_send()
    for step in range(1, stages):
        pl.when(right_sends(step))(lambda step=step: right(step).wait_send())
        pl.when(left_sends(step))(lambda step=step: left(step).wait_send())

        @pl.when(right_gets(step))
        def _(step=step):
            across(step, level - step).wait()

        @pl.when(left_gets(step))
        def _(step=step):
            across(stages - 1 + step, level + step).wait()

    remote(down, shard(down_full, level), mate_send.at[0], mate_receive.at[0], "dp", mate).wait()
    cot_one.wait()
    cot_two.wait()


def opening(tokens, cot, down, fc_pieces, seq_count, dp_count):
    piece, width = tokens.shape
    steps = dp_count // 2 - 1
    anywhere = pl.BlockSpec(memory_space=pl.ANY)
    shape = lambda rows, columns: jax.ShapeDtypeStruct((rows, columns), BF16)
    dma = pltpu.SemaphoreType.DMA
    return pl.pallas_call(
        opening_kernel,
        in_specs=[anywhere] * 4,
        out_specs=[anywhere] * 4,
        out_shape=[
            shape(piece * seq_count, width),
            shape(piece * seq_count, width),
            shape(down.shape[0] * dp_count, width),
            shape(seq_count * fc_pieces.shape[1], fc_pieces.shape[2]),
        ],
        scratch_shapes=[
            dma((4,)), dma((9,)), dma((9,)), dma((steps,)), dma((steps,)), dma((steps,)), dma((steps,)),
            dma((2 * steps + 1,)), dma((2 * steps + 1,)),
        ],
        compiler_params=pltpu.CompilerParams(collective_id=0, has_side_effects=True),
        cost_estimate=cost(0, 10 * piece * seq_count * width),
    )(tokens, cot, down, fc_pieces)


def plane_kernel(
    normed, cot_in, fc, bias, down, middle, gain,
    grad_middle, low, sums, active, hidden_grad, normed_all, cot_all, terms,
    normed_buf, cot_buf, sum_ref, joined, passed, arrived, load, local, send, receive,
):
    piece, width = normed.shape
    half = piece // 2
    inner = fc.shape[1]
    tile = min(512, inner)
    last = inner // tile - 1
    one, two = neighbours()
    for device in (one, two):
        greet("seq", device)
    pl.semaphore_wait(pltpu.get_barrier_semaphore(), 2)

    up, lower = pl.ds(0, half), pl.ds(half, half)
    rows = lambda k, start=0, size=piece: pl.ds(k * piece + start, size)

    def copy(index, source, target, device):
        return remote(source, target, send.at[index], receive.at[index], "seq", device)

    normed_one = copy(0, normed, normed_buf.at[1], one)
    normed_two = copy(1, normed, normed_buf.at[2], two)
    normed_three = (
        copy(2, normed_buf.at[1, up], normed_buf.at[3, up], two),
        copy(3, normed_buf.at[2, lower], normed_buf.at[3, lower], one),
    )
    cot_three = (
        copy(4, cot_buf.at[1, up], cot_buf.at[3, up], two),
        copy(5, cot_buf.at[2, lower], cot_buf.at[3, lower], one),
    )
    across = (copy(6, cot_buf.at[0, up], passed.at[0], one), copy(7, cot_buf.at[0, lower], passed.at[1], two))
    plain_one = copy(8, cot_buf.at[1, up], arrived.at[0, up], one)
    plain_two = copy(9, cot_buf.at[2, lower], arrived.at[1, lower], two)
    joined_one = copy(10, joined.at[0], arrived.at[0, lower], one)
    joined_two = copy(11, joined.at[1], arrived.at[1, up], two)

    loads = [pltpu.make_async_copy(cot_in.at[rows(k)], cot_buf.at[k], load.at[k]) for k in range(3)]
    own = pltpu.make_async_copy(normed, normed_buf.at[0], load.at[3])
    keeps = [pltpu.make_async_copy(normed_buf.at[k], normed_all.at[rows(k)], local.at[k]) for k in range(4)]
    keep_cot = pltpu.make_async_copy(cot_buf.at[3], cot_all.at[rows(3)], local.at[4])

    normed_one.start()
    normed_two.start()
    own.start()
    for item in loads:
        item.start()

    def feed_body(fc_tile, down_tile, active_tile, hidden_tile):
        k, j = pl.program_id(0), pl.program_id(1)

        @pl.when((k == 0) & (j == 0))
        def _():
            own.wait()
            loads[0].wait()
            keeps[0].start()

        @pl.when((k == 1) & (j == 0))
        def _():
            normed_one.wait_recv()
            normed_two.wait_recv()
            for item in normed_three:
                item.start()
            loads[1].wait()
            loads[2].wait()
            for item in cot_three:
                item.start()
            keeps[1].start()
            keeps[2].start()

        @pl.when((k == 3) & (j == 0))
        def _():
            for item in normed_three + cot_three:
                item.wait_recv()
            keeps[3].start()
            keep_cot.start()

        weights = fc_tile[...]
        hidden = nn(normed_buf[k], weights) + bias[:, pl.ds(pl.multiple_of(j * tile, tile), tile)]
        grad_active = nt(cot_buf[k], down_tile[...])
        square = hidden * hidden
        bent = jnp.tanh(math.sqrt(2 / math.pi) * (hidden + 0.044715 * (square * hidden)))
        share = 0.5 * (1.0 + bent)
        active_tile[...] = (hidden * share).astype(BF16)
        slope = share + (0.5 * hidden) * (1.0 - bent * bent) * (
            math.sqrt(2 / math.pi) * (1.0 + (3 * 0.044715) * square)
        )
        grad_hidden = (grad_active * slope).astype(BF16)
        hidden_tile[...] = grad_hidden
        term = nt(grad_hidden, weights)

        @pl.when(j == 0)
        def _():
            sum_ref[...] = term

        @pl.when(j > 0)
        def _():
            sum_ref[...] += term

        @pl.when((j == last) & (k == 0))
        def _():
            arrived[2] = sum_ref[...].astype(BF16)

        @pl.when((j == last) & (k == 1))
        def _():
            cot_three[0].wait_send()
            cot_buf[1] = sum_ref[...].astype(BF16)
            plain_one.start()

        @pl.when((j == last) & (k == 2))
        def _():
            cot_three[1].wait_send()
            cot_buf[2] = sum_ref[...].astype(BF16)
            plain_two.start()

        @pl.when((j == last) & (k == 3))
        def _():
            cot_buf[0] = sum_ref[...].astype(BF16)
            for item in across:
                item.start()

    pltpu.emit_pipeline(
        feed_body,
        grid=(4, inner // tile),
        in_specs=[
            pl.BlockSpec((width, tile), lambda k, j: (0, j)),
            pl.BlockSpec((tile, width), lambda k, j: (j, 0)),
        ],
        out_specs=[pl.BlockSpec((piece, tile), lambda k, j: (k, j))] * 2,
    )(fc, down, active, hidden_grad)

    narrow = min(512, width)

    def down_body(active_rows, down_columns, out):
        out[...] = nn(active_rows[...], down_columns[...]).astype(BF16)

    def multiply_down(start):
        pltpu.emit_pipeline(
            down_body,
            grid=(2, width // narrow),
            in_specs=[
                pl.BlockSpec((piece, inner), lambda k, j: (start + k, 0)),
                pl.BlockSpec((inner, narrow), lambda k, j: (0, j)),
            ],
            out_specs=[pl.BlockSpec((piece, narrow), lambda k, j: (start + k, j))],
        )(active, down, terms)

    multiply_down(0)
    for item in across:
        item.wait_recv()
    joined[0] = (cot_buf[1, half:].astype(F32) + passed[1].astype(F32)).astype(BF16)
    joined[1] = (cot_buf[2, :half].astype(F32) + passed[0].astype(F32)).astype(BF16)
    joined_one.start()
    joined_two.start()
    multiply_down(2)
    for item in (plain_one, plain_two, joined_one, joined_two):
        item.wait_recv()

    part = min(128, piece)

    def norm_body(middle_tile, cot_tile, grad_tile, low_tile):
        i = pl.program_id(0)
        here = pl.ds(pl.multiple_of(i * part, part), part)
        upstream = (
            arrived[2, here, :].astype(F32) + arrived[0, here, :].astype(F32) + arrived[1, here, :].astype(F32)
        )
        values = middle_tile[...]
        unit, scale = norm_parts(values)
        cot = cot_tile[...].astype(F32)
        grad = cot + norm_backward(unit, scale, gain[...], upstream)
        rounded = grad.astype(BF16)
        grad_tile[...] = grad
        low_tile[...] = rounded
        for at, item in enumerate((upstream * unit, upstream, rounded.astype(F32), cot)):
            column = jnp.sum(item, axis=0, keepdims=True)

            @pl.when(i == 0)
            def _():
                sums[at : at + 1, :] = column

            @pl.when(i > 0)
            def _():
                sums[at : at + 1, :] += column

    line = pl.BlockSpec((part, width), lambda i: (i, 0))
    pltpu.emit_pipeline(norm_body, grid=(piece // part,), in_specs=[line] * 2, out_specs=[line] * 2)(
        middle, cot_in, grad_middle, low
    )
    for item in keeps + [keep_cot]:
        item.wait()
    for item in (normed_one, normed_two, *normed_three, *across, plain_one, plain_two, joined_one, joined_two):
        item.wait_send()


def feed_plane(normed, cot_all, fc, bias, down, middle, gain):
    piece, width = normed.shape
    length, inner = cot_all.shape[0], fc.shape[1]
    half = piece // 2
    anywhere = pl.BlockSpec(memory_space=pl.ANY)
    inside = pl.BlockSpec(memory_space=pltpu.VMEM)
    shape = lambda rows, columns, kind=BF16: jax.ShapeDtypeStruct((rows, columns), kind)
    dma = pltpu.SemaphoreType.DMA
    return pl.pallas_call(
        plane_kernel,
        in_specs=[anywhere, anywhere, anywhere, inside, anywhere, anywhere, inside],
        out_specs=[anywhere, anywhere, inside] + [anywhere] * 5,
        out_shape=[
            shape(piece, width, F32), shape(piece, width), shape(4, width, F32), shape(length, inner),
            shape(length, inner), shape(length, width), shape(length, width), shape(length, width),
        ],
        scratch_shapes=[
            pltpu.VMEM((4, piece, width), BF16),
            pltpu.VMEM((4, piece, width), BF16),
            pltpu.VMEM((piece, width), F32),
            pltpu.VMEM((2, half, width), BF16),
            pltpu.VMEM((2, half, width), BF16),
            pltpu.VMEM((3, piece, width), BF16),
            dma((4,)), dma((5,)), dma((12,)), dma((12,)),
        ],
        input_output_aliases={1: 6},
        compiler_params=pltpu.CompilerParams(collective_id=1, has_side_effects=True, vmem_limit_bytes=60 * 2**20),
        cost_estimate=cost(8 * length * width * inner, 10 * length * width),
    )(normed, cot_all, fc, bias, down, middle, gain)


def after(value, *others):
    return lax.optimization_barrier((value, *others))[0]


def shift(value, axis, distance):
    count = lax.axis_size(axis)
    return lax.ppermute(value, axis, [(i, i ^ distance) for i in range(count)])


def gather_blocks(value, axis="seq"):
    return [value] + [shift(value, axis, k) for k in range(1, lax.axis_size(axis))]


def scatter_blocks(blocks, axis="seq"):
    return [blocks[0]] + [shift(blocks[k], axis, k) for k in range(1, lax.axis_size(axis))]


def gather_plane(value):
    if lax.axis_size("seq") != 4:
        return gather_blocks(value)
    half = value.shape[0] // 2
    one, two = shift(value, "seq", 1), shift(value, "seq", 2)
    three = jnp.concatenate([shift(one[:half], "seq", 2), shift(two[half:], "seq", 1)], axis=0)
    return [value, one, two, three]


def scatter_plane(blocks):
    if lax.axis_size("seq") != 4:
        return scatter_blocks(blocks)
    half = blocks[0].shape[0] // 2
    up, low = shift(blocks[3][:half], "seq", 1), shift(blocks[3][half:], "seq", 2)
    one = shift(blocks[1][:half], "seq", 1)
    two = shift(blocks[2][half:], "seq", 2)
    one_low = (blocks[1][half:].astype(F32) + low.astype(F32)).astype(BF16)
    two_up = (blocks[2][:half].astype(F32) + up.astype(F32)).astype(BF16)
    return [blocks[0], (one, shift(one_low, "seq", 1)), (shift(two_up, "seq", 2), two)]


def by_rank(blocks, rank):
    bit = 1
    while bit < len(blocks):
        odd = (rank & bit) != 0
        blocks = [jnp.where(odd, blocks[k ^ bit], blocks[k]) for k in range(len(blocks))]
        bit *= 2
    return blocks


def pick(pieces, at):
    return lax.dynamic_index_in_dim(pieces, at, axis=0, keepdims=False)


def exchange(pieces, rank):
    return scatter_blocks([pick(pieces, rank ^ k) for k in range(pieces.shape[0])])


def small_scatter(pieces, dp_rank, seq_rank):
    total = 0.0
    sent = [lax.dynamic_index_in_dim(pieces, seq_rank ^ k, axis=1, keepdims=False) for k in range(pieces.shape[1])]
    for part in scatter_blocks(sent):
        total = total + part
    sent = [pick(total, dp_rank ^ k) for k in range(pieces.shape[0])]
    total = 0.0
    for part in scatter_blocks(sent, "dp"):
        total = total + part
    return total


def swap_pairs(dp_count, seq_count, sub):
    pairs = []
    for d in range(dp_count):
        for s in range(seq_count):
            source = ((d // sub) * sub + s % sub) * seq_count + (s // sub) * sub + d % sub
            pairs.append((source, d * seq_count + s))
    return pairs


def gather_dp(value):
    return lax.all_gather(value, "dp", axis=0, tiled=True)


def scatter_dp(value):
    return lax.psum_scatter(value, "dp", scatter_dimension=0, tiled=True)


def shards(
    tokens,
    cotangent,
    lengths,
    key_mask,
    attn_gain,
    attn_shift,
    qkv_weight,
    qv_bias,
    proj_weight,
    proj_bias,
    mlp_gain,
    mlp_shift,
    fc_weight,
    fc_bias,
    down_weight,
    down_bias,
):
    _, piece, width = tokens.shape
    dp_count, seq_count = lax.axis_size("dp"), lax.axis_size("seq")
    dp_rank, seq_rank = lax.axis_index("dp"), lax.axis_index("seq")
    own_heads = HEADS // seq_count
    own_width = own_heads * HEAD_DIM
    rows = qkv_weight.shape[0]
    sub = HEAD_DIM // proj_weight.shape[0]
    high = seq_count // sub
    block = down_weight.shape[0]
    rank = jnp.reshape(seq_rank, (1,)).astype(jnp.int32)
    swap = swap_pairs(dp_count, seq_count, sub)
    order = list(range(seq_count - 1, -1, -1))
    if seq_count == 4:
        order = [3, 1, 2, 0]

    in_plane = seq_count == 4 and dp_count == 8
    qkv_pieces = (
        qkv_weight.reshape(rows, 3, own_heads, sub, high, HEAD_DIM)
        .transpose(4, 3, 0, 1, 2, 5)
        .reshape(seq_count, rows, 3 * own_width)
    )
    qkv_rows = jnp.concatenate(by_rank(exchange(qkv_pieces, seq_rank), seq_rank), axis=0)
    weights = [gather_dp(qkv_rows[:, i * own_width : (i + 1) * own_width]) for i in range(3)]
    tokens_own, cot_own = tokens[0], cotangent[0]

    small = (attn_gain, attn_shift, qv_bias, proj_bias, mlp_gain, mlp_shift, fc_bias, down_bias)
    sizes = [item.shape[0] for item in small]
    positions = seq_rank * piece + jnp.arange(piece, dtype=jnp.int32)
    own_flags = ((key_mask[0] == 1) & (positions < lengths[0])).astype(BF16)
    packed = jnp.concatenate(small + (own_flags,))
    blocks = gather_blocks(packed)
    flags = jnp.concatenate([item[-piece:] for item in blocks])
    key_bias = jnp.where(flags > 0, 0.0, NEG).astype(F32)[:, None]
    packed = jnp.stack(by_rank([item[:-piece] for item in blocks], seq_rank))
    packed = jnp.stack(by_rank(gather_blocks(packed, "dp"), dp_rank)).astype(F32)
    parts, start = [], 0
    for size in sizes:
        parts.append(packed[:, :, start : start + size])
        start += size
    whole = [part.reshape(1, -1) for part in parts]
    gain_one, shift_one, qv_full, proj_shift, gain_two, shift_two, _, down_shift = whole
    fc_shift = lax.dynamic_index_in_dim(parts[6], seq_rank, axis=1, keepdims=False).reshape(1, -1)
    rank_low, rank_high = seq_rank % sub, seq_rank // sub
    qv_heads = qv_full.reshape(2, own_heads, sub, high, HEAD_DIM)
    qv_own = lax.dynamic_index_in_dim(
        lax.dynamic_index_in_dim(qv_heads, rank_low, axis=2, keepdims=False), rank_high, axis=2, keepdims=False
    )
    qv_own = qv_own.reshape(1, -1)

    proj_full = gather_dp(lax.ppermute(proj_weight, BOTH, swap))
    fc_pieces = (
        fc_weight.reshape(rows, dp_count, seq_count, block)
        .transpose(2, 0, 1, 3)
        .reshape(seq_count, rows, dp_count * block)
    )
    shared = None
    if in_plane:
        token_all, cot_all, down_full, fc_rows = opening(
            after(tokens_own, qkv_rows, packed), cot_own, down_weight, fc_pieces, seq_count, dp_count
        )
        for k in range(seq_count):
            shared = project(k, token_all, k, gain_one, shift_one, weights, qv_own, piece, seq_count, shared)
    else:
        token_blocks = gather_blocks(tokens_own)
        cot_blocks = gather_blocks(after(cot_own, token_blocks[-1]))
        down_full = gather_dp(down_weight)
        fc_rows = jnp.concatenate(by_rank(exchange(fc_pieces, seq_rank), seq_rank), axis=0)
        for k in range(seq_count):
            shared = project(k, token_blocks[k], 0, gain_one, shift_one, weights, qv_own, piece, seq_count, shared)
    fc_full = gather_dp(fc_rows)
    normed_one, q, keys, values, keys_t, values_t = shared
    proj_terms, shared = [None] * seq_count, None
    for k in order:
        proj_terms[k], shared = attend(k, rank, q, keys, values_t, key_bias, proj_full, piece, shared)
    attended, lse = shared
    middle, normed_two = rowwise(
        middle_kernel, scatter_plane(proj_terms), [tokens_own], [proj_shift, gain_two, shift_two], [F32, BF16], 0
    )

    if in_plane:
        grad_middle, grad_mid_low, sums_two, active, grad_hidden, normed_all, cot_all, down_terms = feed_plane(
            normed_two, cot_all, fc_full, fc_shift, down_full, middle, gain_two
        )
        sums_two = [sums_two[i] for i in range(4)]
        down_terms = [down_terms[k * piece : (k + 1) * piece] for k in range(seq_count)]
    else:
        normed_blocks = gather_blocks(normed_two)
        grad_terms, shared = [], None
        for k in range(seq_count):
            term, shared = feed(k, normed_blocks[k], cot_blocks[k], fc_full, fc_shift, down_full, seq_count, shared)
            grad_terms.append(term)
        active, grad_hidden, normed_all, cot_all = shared
        grad_middle, grad_mid_low, *sums_two = rowwise(
            middle_back_kernel, scatter_blocks(grad_terms), [middle, cot_own], [gain_two], [F32, BF16], 4
        )
        down_terms = [
            nn(active[k * piece : (k + 1) * piece], down_full).astype(BF16) for k in range(seq_count)
        ]
    low_blocks = gather_plane(grad_mid_low)
    grad_down = tn(active, cot_all).astype(BF16)
    grad_fc = tn(normed_all, grad_hidden).astype(BF16)
    low_blocks[1] = after(low_blocks[1], grad_down, grad_fc)
    grad_down = scatter_dp(grad_down)
    grad_fc = scatter_dp(grad_fc)
    down_terms, _ = lax.optimization_barrier((down_terms, low_blocks[-1]))
    block_out = rowwise(out_kernel, scatter_plane(down_terms), [middle], [down_shift], [BF16], 0)[0]

    sums, shared = None, None
    for k in range(seq_count):
        sums, shared = retreat(
            k, rank, low_blocks[k], proj_full, q, lse, keys, values, keys_t, key_bias, sums, shared, k == seq_count - 1
        )
    grad_q, low_all = shared
    grads = [grad_q, sums[0], sums[1]]
    normed_one = after(normed_one, grad_down)
    grad_qkv = [scatter_dp(tn(normed_one, item).astype(BF16)) for item in grads]
    back_terms = [None] * seq_count
    for k in order:
        back_terms[k] = back(k, grads, weights, piece)
    tokens_grad, *sums_one = rowwise(
        tokens_back_kernel, scatter_plane(back_terms), [tokens_own, grad_middle], [gain_one], [F32], 2
    )
    grad_proj = scatter_dp(tn(attended, low_all).astype(BF16))
    grad_proj = lax.ppermute(grad_proj, BOTH, swap).astype(F32)

    blocks = exchange(grad_fc.reshape(seq_count, rows, dp_count * block), seq_rank)
    if block % 128 == 0:
        fc_places = lambda s: [(0, d, d * seq_count + s) for d in range(dp_count)]
        grad_fc = lay_out(rank, [[item] for item in blocks], fc_weight.shape[1], (fc_places, block))
    else:
        blocks = [item.reshape(rows, dp_count, block) for item in by_rank(blocks, seq_rank)]
        grad_fc = jnp.stack(blocks, axis=2).reshape(fc_weight.shape).astype(F32)
    blocks = list(zip(*[exchange(item.reshape(seq_count, rows, own_width), seq_rank) for item in grad_qkv]))
    qkv_places = lambda s: [
        (part, head, part * HEADS + (head * sub + s % sub) * high + s // sub)
        for part in range(3)
        for head in range(own_heads)
    ]
    grad_qkv_weight = lay_out(rank, blocks, qkv_weight.shape[1], (qkv_places, HEAD_DIM))

    def spread(vector):
        return vector.reshape(dp_count, seq_count, -1)

    here = (jnp.arange(seq_count) == seq_rank).astype(F32)
    hidden_sums = jnp.sum(grad_hidden.astype(F32), axis=0).reshape(dp_count, 1, -1) * here[None, :, None]
    early = jnp.concatenate([spread(item) for item in sums_two] + [hidden_sums], axis=2)
    early = small_scatter(early, dp_rank, seq_rank)
    qv_sums = jnp.stack([jnp.sum(item.astype(F32), axis=0) for item in (grads[0], grads[2])])
    here = (jnp.arange(sub) == rank_low)[:, None] & (jnp.arange(high) == rank_high)[None, :]
    qv_sums = qv_sums.reshape(2, own_heads, 1, 1, HEAD_DIM) * here.astype(F32)[None, None, :, :, None]
    late = jnp.concatenate([spread(item) for item in sums_one] + [spread(qv_sums)], axis=2)
    late = small_scatter(late, dp_rank, seq_rank)
    share = attn_gain.shape[0]
    return (
        block_out[None],
        tokens_grad[None],
        late[:share],
        late[share : 2 * share],
        grad_qkv_weight,
        late[2 * share :],
        grad_proj,
        early[2 * share : 3 * share],
        early[:share],
        early[share : 2 * share],
        grad_fc,
        early[4 * share :],
        grad_down.astype(F32),
        early[3 * share : 4 * share],
    )


def solution(mesh):
    in_specs = (
        P("dp", "seq", None),
        P("dp", "seq", None),
        P("dp"),
        P("dp", "seq"),
        P(BOTH),
        P(BOTH),
        P(BOTH, None),
        P(BOTH),
        P(BOTH, None),
        P(BOTH),
        P(BOTH),
        P(BOTH),
        P(BOTH, None),
        P(BOTH),
        P(BOTH, None),
        P(BOTH),
    )
    out_specs = (
        P("dp", "seq", None),
        P("dp", "seq", None),
        P(BOTH),
        P(BOTH),
        P(BOTH, None),
        P(BOTH),
        P(BOTH, None),
        P(BOTH),
        P(BOTH),
        P(BOTH),
        P(BOTH, None),
        P(BOTH),
        P(BOTH, None),
        P(BOTH),
    )
    return jax.shard_map(shards, mesh=mesh, in_specs=in_specs, out_specs=out_specs, check_vma=False)
```

```python
import functools
import math

import jax
import jax.numpy as jnp
from jax import lax
from jax.experimental import pallas as pl
from jax.experimental.pallas import tpu as pltpu
from jax.sharding import PartitionSpec as P

HEADS = 16
HEAD_DIM = 128
EPS = 1e-05
NEG = -1e30
FACTOR = HEAD_DIM ** (-0.5)
LOG2E = math.log2(math.e)
F32 = jnp.float32
BF16 = jnp.bfloat16
BOTH = ("dp", "seq")
MESH = pl.DeviceIdType.MESH


def nn(left, right):
    return lax.dot_general(left, right, (((1,), (0,)), ((), ())), preferred_element_type=F32)


def nt(left, right):
    return lax.dot_general(left, right, (((1,), (1,)), ((), ())), preferred_element_type=F32)


def tn(left, right):
    return lax.dot_general(left, right, (((0,), (0,)), ((), ())), preferred_element_type=F32)


def params(limit_mib=56):
    return pltpu.CompilerParams(dimension_semantics=("arbitrary",), vmem_limit_bytes=limit_mib * 2**20)


def cost(flops, moved, exps=0):
    return pl.CostEstimate(flops=int(flops), bytes_accessed=int(moved), transcendentals=int(exps))


def call_on_block(kernel, grid, inputs, fresh, shared, previous, scratch, estimate, rank=None):
    arrays = [item for item, _ in inputs]
    specs = [spec for _, spec in inputs]
    aliases = {}
    lead = 0 if rank is None else 1
    if previous is not None:
        for at, item in enumerate(previous):
            aliases[lead + len(arrays)] = len(fresh) + at
            arrays.append(item)
            specs.append(pl.BlockSpec(memory_space=pl.ANY))
    count = len(inputs)
    skipped = 0 if previous is None else len(previous)

    def body(*refs):
        refs = list(refs)
        kernel(*refs[: lead + count], *refs[lead + count + skipped :])

    out_specs = [spec for _, spec in fresh] + [spec for _, spec in shared]
    out_shape = [shape for shape, _ in fresh] + [shape for shape, _ in shared]
    if rank is None:
        results = pl.pallas_call(
            body, grid=grid, in_specs=specs, out_specs=out_specs, out_shape=out_shape, scratch_shapes=scratch,
            input_output_aliases=aliases, compiler_params=params(), cost_estimate=estimate,
        )(*arrays)
    else:
        results = pl.pallas_call(
            body,
            grid_spec=pltpu.PrefetchScalarGridSpec(
                num_scalar_prefetch=1, grid=grid, in_specs=specs, out_specs=out_specs, scratch_shapes=scratch
            ),
            out_shape=out_shape, input_output_aliases=aliases, compiler_params=params(), cost_estimate=estimate,
        )(rank, *arrays)
    return results[: len(fresh)], results[len(fresh) :]


def norm_parts(values):
    average = jnp.mean(values, axis=-1, keepdims=True)
    centred = values - average
    scale = lax.rsqrt(jnp.mean(centred * centred, axis=-1, keepdims=True) + EPS)
    return centred * scale, scale


def norm_backward(normed, scale, gain, upstream):
    weighted = upstream * gain
    return scale * (
        weighted
        - jnp.mean(weighted, axis=-1, keepdims=True)
        - normed * jnp.mean(weighted * normed, axis=-1, keepdims=True)
    )


def project_kernel(x, gain, shift_, wq, wk, wv, bias, normed, q, k, v, k_t, v_t):
    columns = wq.shape[1]
    rows = (norm_parts(x[...].astype(F32))[0] * gain[...] + shift_[...]).astype(BF16)
    normed[...] = rows
    q[...] = (nn(rows, wq[...]) + bias[:, :columns]).astype(BF16)
    keys = nn(rows, wk[...])
    k[...] = keys.astype(BF16)
    k_t[...] = keys.T.astype(BF16)
    values = nn(rows, wv[...]) + bias[:, columns:]
    v[...] = values.astype(BF16)
    v_t[...] = values.T.astype(BF16)


def project(at, x, first, rows_here, gain, shift_, weight, bias, count, previous):
    width, columns = x.shape[1], weight.shape[1] // 3
    tile = min(256, rows_here)
    steps = rows_here // tile
    whole = lambda shape: pl.BlockSpec(shape, lambda i: (0, 0))
    rows = lambda n: pl.BlockSpec((tile, n), lambda i: (at * steps + i, 0))
    turned = pl.BlockSpec((columns, tile), lambda i: (0, at * steps + i))
    inputs = [
        (x, pl.BlockSpec((tile, width), lambda i: (first * steps + i, 0))),
        (gain, whole((1, width))),
        (shift_, whole((1, width))),
        *[(weight, pl.BlockSpec((width, columns), lambda i, part=part: (0, part))) for part in range(3)],
        (bias, whole((1, 2 * columns))),
    ]
    shape = lambda *dims: jax.ShapeDtypeStruct(dims, BF16)
    shared = [(shape(count, width), rows(width))] + [(shape(count, columns), rows(columns))] * 3
    shared += [(shape(columns, count), turned)] * 2
    return call_on_block(
        project_kernel, (steps,), inputs, [], shared, previous, [],
        cost(6 * rows_here * width * columns, 4 * rows_here * width + 6 * width * columns + 10 * rows_here * columns),
    )[1]


def rows_of(block, piece):
    return pl.ds(pl.multiple_of(block * piece, piece), piece)


def scores_of(key_ref, bias_ref, query, rel, piece, diagonal):
    rows = rows_of(rel, piece)
    scores = nt(key_ref[rows, :], query) * (FACTOR * LOG2E)
    key_bias = bias_ref[rows, :]
    if not diagonal:
        return scores + key_bias
    key_at = lax.broadcasted_iota(jnp.int32, scores.shape, 0)
    query_at = lax.broadcasted_iota(jnp.int32, scores.shape, 1)
    allowed = ((key_at < query_at) & (key_bias > -1.0)) | (key_at == query_at)
    return jnp.where(allowed, scores, NEG)


def attend_kernel(at, rank_ref, query_ref, key_ref, value_t, bias_ref, proj_ref, part_ref, attended, lse_ref, score_ref, sum_ref):
    piece = query_ref.shape[0]
    rank = rank_ref[0]
    head = pl.program_id(0)
    true = lax.bitwise_xor(at, rank)
    query = query_ref[...]

    def first(block, top):
        scores = scores_of(key_ref, bias_ref, query, lax.bitwise_xor(block, rank), piece, False)
        score_ref[rows_of(block, piece), :] = scores
        return jnp.maximum(top, jnp.max(scores, axis=0, keepdims=True))

    last = scores_of(key_ref, bias_ref, query, at, piece, True)
    top = lax.fori_loop(0, true, first, jnp.max(last, axis=0, keepdims=True))

    def weigh(scores, rel):
        weights = jnp.exp2(scores - top)
        return jnp.sum(weights, axis=0, keepdims=True), nn(value_t[:, rows_of(rel, piece)], weights.astype(BF16))

    def second(block, carry):
        total, out = carry
        more, part = weigh(score_ref[rows_of(block, piece), :], lax.bitwise_xor(block, rank))
        return total + more, out + part

    total, out = lax.fori_loop(0, true, second, weigh(last, at))
    result = (out / total).T.astype(BF16)
    attended[...] = result
    lse_ref[0] = top + jnp.log2(total)
    term = nn(result, proj_ref[...])

    @pl.when(head == 0)
    def _():
        sum_ref[...] = term

    @pl.when(head > 0)
    def _():
        sum_ref[...] += term

    @pl.when(head == pl.num_programs(0) - 1)
    def _():
        part_ref[...] = sum_ref[...].astype(BF16)


def attend(at, rank, q, k, v_t, key_bias, proj, piece, previous):
    length, columns = q.shape
    heads, width = columns // HEAD_DIM, proj.shape[1]
    inputs = [
        (q, pl.BlockSpec((piece, HEAD_DIM), lambda h, r: (at, h))),
        (k, pl.BlockSpec((length, HEAD_DIM), lambda h, r: (0, h))),
        (v_t, pl.BlockSpec((HEAD_DIM, length), lambda h, r: (h, 0))),
        (key_bias, pl.BlockSpec((length, 1), lambda h, r: (0, 0))),
        (proj, pl.BlockSpec((HEAD_DIM, width), lambda h, r: (h, 0))),
    ]
    fresh = [(jax.ShapeDtypeStruct((piece, width), BF16), pl.BlockSpec((piece, width), lambda h, r: (0, 0)))]
    shared = [
        (jax.ShapeDtypeStruct((length, columns), BF16), pl.BlockSpec((piece, HEAD_DIM), lambda h, r: (at, h))),
        (jax.ShapeDtypeStruct((heads, 1, length), F32), pl.BlockSpec((1, 1, piece), lambda h, r: (h, 0, at))),
    ]
    scratch = [pltpu.VMEM((length, piece), F32), pltpu.VMEM((piece, width), F32)]
    (part,), shared = call_on_block(
        functools.partial(attend_kernel, at), (heads,), inputs, fresh, shared, previous, scratch,
        cost(
            2 * length * piece * columns * 1.3 + 2 * piece * columns * width, 6 * length * columns + 2 * width * columns,
            heads * length * piece * 0.6,
        ), rank,
    )
    return part, shared


def feed_kernel(normed, cot, fc, bias, down, part, active_out, hidden_out, normed_out, cot_out, sum_ref):
    step = pl.program_id(0)
    weights = fc[...]
    hidden = nn(normed[...], weights) + bias[...]
    grad_active = nt(cot[...], down[...])
    inner = math.sqrt(2 / math.pi) * (hidden + 0.044715 * (hidden * hidden * hidden))
    bent = jnp.tanh(inner)
    half = 0.5 * (1.0 + bent)
    active_out[...] = (hidden * half).astype(BF16)
    slope = half + (0.5 * hidden) * (1.0 - bent * bent) * (
        math.sqrt(2 / math.pi) * (1.0 + (3 * 0.044715) * (hidden * hidden))
    )
    grad_hidden = (grad_active * slope).astype(BF16)
    hidden_out[...] = grad_hidden
    term = nt(grad_hidden, weights)

    @pl.when(step == 0)
    def _():
        sum_ref[...] = term
        normed_out[...] = normed[...]
        cot_out[...] = cot[...]

    @pl.when(step > 0)
    def _():
        sum_ref[...] += term

    @pl.when(step == pl.num_programs(0) - 1)
    def _():
        part[...] = sum_ref[...].astype(BF16)


def feed(at, normed, cot, fc, bias, down, count, previous):
    piece, width = normed.shape
    inner = fc.shape[1]
    tile = min(512, inner)
    length = piece * count
    rows = pl.BlockSpec((piece, width), lambda j: (0, 0))
    inputs = [
        (normed, rows),
        (cot, rows),
        (fc, pl.BlockSpec((width, tile), lambda j: (0, j))),
        (bias, pl.BlockSpec((1, tile), lambda j: (0, j))),
        (down, pl.BlockSpec((tile, width), lambda j: (j, 0))),
    ]
    shape = lambda n: jax.ShapeDtypeStruct((length, n), BF16)
    columns = pl.BlockSpec((piece, tile), lambda j: (at, j))
    here = pl.BlockSpec((piece, width), lambda j: (at, 0))
    fresh = [(jax.ShapeDtypeStruct((piece, width), BF16), rows)]
    shared = [(shape(inner), columns), (shape(inner), columns), (shape(width), here), (shape(width), here)]
    (part,), shared = call_on_block(
        feed_kernel, (inner // tile,), inputs, fresh, shared, previous, [pltpu.VMEM((piece, width), F32)],
        cost(6 * piece * width * inner, 4 * width * inner + 10 * piece * width + 4 * piece * inner, piece * inner),
    )
    return part, shared


def retreat_kernel(
    at, first_call, last_call, rank_ref, low_ref, proj_ref, query_ref, lse_ref, key_ref, value_ref, key_t, bias_ref, *rest
):
    rest = list(rest)
    key_in, value_in = (None, None) if first_call else (rest.pop(0), rest.pop(0))
    key_out, value_out, query_out, low_out, prob_ref, chance_ref, key_sum, value_sum = rest
    piece = query_ref.shape[0]
    rank = rank_ref[0]
    true = lax.bitwise_xor(at, rank)

    @pl.when(pl.program_id(0) == 0)
    def _():
        low_out[...] = low_ref[...]

    if first_call:
        key_sum[...] = jnp.zeros_like(key_sum)
        value_sum[...] = jnp.zeros_like(value_sum)
    else:
        key_sum[...] = key_in[...]
        value_sum[...] = value_in[...]
    query, lse = query_ref[...], lse_ref[0]
    grad = nt(low_ref[...], proj_ref[...]).astype(BF16)

    def measure(scores, rel):
        rows = rows_of(rel, piece)
        probs = jnp.exp2(scores - lse)
        grad_chances = nt(value_ref[rows, :], grad)
        value_sum[rows, :] += nn(probs.astype(BF16), grad)
        prob_ref[rows, :] = probs
        chance_ref[rows, :] = grad_chances
        return jnp.sum(probs * grad_chances, axis=0, keepdims=True)

    def first(block, weighted):
        rel = lax.bitwise_xor(block, rank)
        return weighted + measure(scores_of(key_ref, bias_ref, query, rel, piece, False), rel)

    last = scores_of(key_ref, bias_ref, query, at, piece, True)
    weighted = lax.fori_loop(0, true, first, measure(last, at))

    def second(block, total):
        rows = rows_of(lax.bitwise_xor(block, rank), piece)
        grad_scores = (prob_ref[rows, :] * (chance_ref[rows, :] - weighted)).astype(BF16)
        key_sum[rows, :] += nn(grad_scores, query)
        return total + nn(key_t[:, rows], grad_scores)

    total = lax.fori_loop(0, true + 1, second, jnp.zeros((HEAD_DIM, piece), F32))
    query_out[...] = (total * FACTOR).T.astype(BF16)
    if last_call:
        key_out[...] = (key_sum[...] * FACTOR).astype(BF16)
        value_out[...] = value_sum[...].astype(BF16)
    else:
        key_out[...] = key_sum[...]
        value_out[...] = value_sum[...]


def retreat(at, rank, low, proj, q, lse, k, v, k_t, key_bias, sums, previous, last_call):
    length, columns = q.shape
    piece, width = low.shape
    heads = columns // HEAD_DIM
    tall = pl.BlockSpec((length, HEAD_DIM), lambda h, r: (0, h))
    part = pl.BlockSpec((piece, HEAD_DIM), lambda h, r: (at, h))
    inputs = [
        (low, pl.BlockSpec((piece, width), lambda h, r: (0, 0))),
        (proj, pl.BlockSpec((HEAD_DIM, width), lambda h, r: (h, 0))),
        (q, part),
        (lse, pl.BlockSpec((1, 1, piece), lambda h, r: (h, 0, at))),
        (k, tall),
        (v, tall),
        (k_t, pl.BlockSpec((HEAD_DIM, length), lambda h, r: (h, 0))),
        (key_bias, pl.BlockSpec((length, 1), lambda h, r: (0, 0))),
    ]
    if sums is not None:
        inputs += [(item, tall) for item in sums]
    kind = BF16 if last_call else F32
    fresh = [(jax.ShapeDtypeStruct((length, columns), kind), tall)] * 2
    shared = [
        (jax.ShapeDtypeStruct((length, columns), BF16), part),
        (jax.ShapeDtypeStruct((length, width), BF16), pl.BlockSpec((piece, width), lambda h, r: (at, 0))),
    ]
    scratch = [pltpu.VMEM((length, piece), F32)] * 2 + [pltpu.VMEM((length, HEAD_DIM), F32)] * 2
    return call_on_block(
        functools.partial(retreat_kernel, at, sums is None, last_call), (heads,), inputs, fresh, shared, previous,
        scratch,
        cost(
            5 * 1.3 * length * piece * columns + 2 * piece * columns * width, 20 * length * columns,
            heads * length * piece * 0.6,
        ), rank,
    )


def back_kernel(grads, weight, out):
    out[...] = nt(grads[...], weight[...]).astype(BF16)


def back(at, grads, weight, piece):
    columns, width = grads.shape[1], weight.shape[0]
    tile = min(512, width)
    return pl.pallas_call(
        back_kernel,
        grid=(width // tile,),
        in_specs=[
            pl.BlockSpec((piece, columns), lambda j: (at, 0)),
            pl.BlockSpec((tile, columns), lambda j: (j, 0)),
        ],
        out_specs=pl.BlockSpec((piece, tile), lambda j: (0, j)),
        out_shape=jax.ShapeDtypeStruct((piece, width), BF16),
        compiler_params=params(),
        cost_estimate=cost(2 * piece * width * columns, 2 * width * columns + 2 * piece * (columns + width)),
    )(grads, weight)


def part_specs(parts, tile, steps, width):
    arrays, specs = [], []
    for part in parts:
        if isinstance(part, tuple):
            middle = steps // 2
            arrays += list(part)
            specs.append(pl.BlockSpec((tile, width), lambda i: (jnp.minimum(i, middle - 1), 0)))
            specs.append(pl.BlockSpec((tile, width), lambda i: (jnp.maximum(i - middle, 0), 0)))
        else:
            arrays.append(part)
            specs.append(pl.BlockSpec((tile, width), lambda i: (i, 0)))
    return arrays, specs


def add_parts(kinds, refs):
    total = None
    upper = pl.program_id(0) < pl.num_programs(0) // 2
    for kind in kinds:
        if kind:
            high, low = refs.pop(0)[...], refs.pop(0)[...]
            term = jnp.where(upper, high.astype(F32), low.astype(F32))
        else:
            term = refs.pop(0)[...].astype(F32)
        total = term if total is None else total + term
    return total


def rowwise(kernel, parts, rows, vectors, outputs, sums):
    count, width = rows[0].shape
    tile = min(128, count // 2)
    steps = count // tile
    arrays, specs = part_specs(parts, tile, steps, width)
    kinds = [isinstance(part, tuple) for part in parts]
    specs += [pl.BlockSpec((tile, width), lambda i: (i, 0))] * len(rows)
    specs += [pl.BlockSpec((1, width), lambda i: (0, 0))] * len(vectors)

    def body(*refs):
        refs = list(refs)
        total = add_parts(kinds, refs)
        tiles = [refs.pop(0)[...] for _ in rows]
        given = [refs.pop(0)[...] for _ in vectors]
        results = kernel(total, tiles, given)
        for result, _ in zip(results, outputs):
            refs.pop(0)[...] = result
        for result in results[len(outputs) :]:
            ref = refs.pop(0)
            column = jnp.sum(result, axis=0, keepdims=True)

            @pl.when(pl.program_id(0) == 0)
            def _():
                ref[...] = column

            @pl.when(pl.program_id(0) > 0)
            def _():
                ref[...] += column

    return pl.pallas_call(
        body,
        grid=(steps,),
        in_specs=specs,
        out_specs=[pl.BlockSpec((tile, width), lambda i: (i, 0))] * len(outputs)
        + [pl.BlockSpec((1, width), lambda i: (0, 0))] * sums,
        out_shape=[jax.ShapeDtypeStruct((count, width), kind) for kind in outputs]
        + [jax.ShapeDtypeStruct((1, width), F32)] * sums,
        compiler_params=params(),
        cost_estimate=cost(20 * count * width, count * width * (2 * len(arrays) + 4 * len(rows) + 4 * len(outputs))),
    )(*arrays, *rows, *vectors)


def middle_kernel(total, rows, vectors):
    (tokens,), (bias, gain, shift_) = rows, vectors
    middle = tokens.astype(F32) + (total + bias)
    return middle, (norm_parts(middle)[0] * gain + shift_).astype(BF16)


def out_kernel(total, rows, vectors):
    return (((rows[0] + (total + vectors[0])).astype(BF16)),)


def middle_back_kernel(total, rows, vectors):
    (middle, cot), (gain,) = rows, vectors
    normed, scale = norm_parts(middle)
    cot = cot.astype(F32)
    grad = cot + norm_backward(normed, scale, gain, total)
    low = grad.astype(BF16)
    return grad, low, total * normed, total, low.astype(F32), cot


def tokens_back_kernel(total, rows, vectors):
    (tokens, grad_middle), (gain,) = rows, vectors
    normed, scale = norm_parts(tokens.astype(F32))
    return grad_middle + norm_backward(normed, scale, gain, total), total * normed, total


def lay_out(rank, blocks, width, places):
    rows = blocks[0][0].shape[0]
    count, each = len(blocks), len(blocks[0])
    unit = places[1]

    def body(rank_ref, *refs):
        out = refs[-1]
        for k in range(count):
            source = lax.bitwise_xor(k, rank_ref[0])
            for array, column, target in places[0](source):
                out[:, pl.ds(pl.multiple_of(target * unit, unit), unit)] = refs[k * each + array][
                    :, column * unit : (column + 1) * unit
                ].astype(F32)

    arrays = [item for block in blocks for item in block]
    return pl.pallas_call(
        body,
        grid_spec=pltpu.PrefetchScalarGridSpec(
            num_scalar_prefetch=1,
            grid=(1,),
            in_specs=[pl.BlockSpec(item.shape, lambda i, r: (0, 0)) for item in arrays],
            out_specs=pl.BlockSpec((rows, width), lambda i, r: (0, 0)),
        ),
        out_shape=jax.ShapeDtypeStruct((rows, width), F32),
        compiler_params=params(),
        cost_estimate=cost(rows * width, 6 * rows * width),
    )(rank, *arrays)


def neighbours():
    rank = lax.axis_index("seq")
    return rank + 1 - 2 * lax.rem(rank, 2), rank + 2 - 4 * lax.rem(lax.div(rank, 2), 2)


def remote(source, target, send, receive, axis, device):
    return pltpu.make_async_remote_copy(
        src_ref=source, dst_ref=target, send_sem=send, recv_sem=receive, device_id={axis: device}, device_id_type=MESH
    )


def greet(axis, device):
    pl.semaphore_signal(pltpu.get_barrier_semaphore(), inc=1, device_id={axis: device}, device_id_type=MESH)


def opening_kernel(
    tokens, qkv_pieces, fc_pieces, small, token_all, qkv_full, fc_rows, small_full,
    qkv_rows, small_rows, local, send, receive, up_send, up_receive, down_send, down_receive, mate_send, mate_receive,
):
    piece = tokens.shape[0]
    half = piece // 2
    me, place = lax.axis_index("seq"), lax.axis_index("dp")
    one, two = neighbours()
    three = 3 - me
    stages = lax.axis_size("dp") // 2
    level, core = lax.div(place, 2), lax.rem(place, 2)
    mate = place + 1 - 2 * core
    above, below = level < stages - 1, level > 0

    for device in (one, two, three):
        greet("seq", device)
    greet("dp", mate)
    pl.when(above)(lambda: greet("dp", place + 2))
    pl.when(below)(lambda: greet("dp", place - 2))
    pl.semaphore_wait(pltpu.get_barrier_semaphore(), 4 + above.astype(jnp.int32) + below.astype(jnp.int32))

    def block(ref, at, start=0, size=piece):
        return ref.at[pl.ds(at * piece + start, size)]

    def spread(pieces, target, at):
        rows = target.shape[0] // 4
        mine = target.at[pl.ds(me * rows, rows)]
        source = lambda device: pieces if pieces is small else pieces.at[device]
        copies = [
            remote(source(device), mine, send.at[at + i], receive.at[at + i], "seq", device)
            for i, device in enumerate((one, two, three))
        ]
        return copies, source(me), mine

    qkv_copies, qkv_own, qkv_mine = spread(qkv_pieces, qkv_rows, 0)
    small_copies, small_own, small_mine = spread(small, small_rows, 3)
    fc_copies, fc_own, fc_mine = spread(fc_pieces, fc_rows, 6)
    token_one = remote(tokens, block(token_all, 1), send.at[9], receive.at[9], "seq", one)
    token_two = remote(tokens, block(token_all, 2), send.at[10], receive.at[10], "seq", two)
    token_three = (
        remote(block(token_all, 1, 0, half), block(token_all, 3, 0, half), send.at[11], receive.at[11], "seq", two),
        remote(block(token_all, 2, half, half), block(token_all, 3, half, half), send.at[12], receive.at[12], "seq", one),
    )
    first_kept = [pltpu.make_async_copy(qkv_own, qkv_mine, local.at[0]), pltpu.make_async_copy(small_own, small_mine, local.at[1])]
    later_kept = [pltpu.make_async_copy(fc_own, fc_mine, local.at[2]), pltpu.make_async_copy(tokens, block(token_all, 0), local.at[3])]

    chains = ((qkv_rows, qkv_full), (small_rows, small_full))

    def shard(array, at):
        rows = chains[array][0].shape[0]
        return chains[array][1].at[pl.ds((2 * at + core) * rows, rows)]

    def rising(array, step, device):
        at = level - (step - 1)
        source = chains[array][0] if step == 1 else shard(array, at)
        return remote(source, shard(array, at), up_send.at[array, step - 1], up_receive.at[array, step - 1], "dp", device)

    def falling(array, step, device):
        at = level + (step - 1)
        source = chains[array][0] if step == 1 else shard(array, at)
        return remote(source, shard(array, at), down_send.at[array, step - 1], down_receive.at[array, step - 1], "dp", device)

    def across(array, index, at):
        source = chains[array][0] if index == 0 else shard(array, at)
        return remote(source, shard(array, at), mate_send.at[array, index], mate_receive.at[array, index], "dp", mate)

    rises = lambda step: above & (level >= step - 1)
    falls = lambda step: below & (level <= stages - step)
    from_below = lambda step: level >= step
    from_above = lambda step: level + step <= stages - 1

    def relay(step):
        @pl.when(rises(step))
        def _():
            for array in (1, 0):
                rising(array, step, place + 2).start()

        @pl.when(falls(step))
        def _():
            for array in (1, 0):
                falling(array, step, place - 2).start()

    def take(step):
        @pl.when(from_below(step))
        def _():
            for array in (1, 0):
                got = shard(array, level - step)
                remote(got, got, up_send.at[array, step - 1], up_receive.at[array, step - 1], "dp", mate).wait_recv()
                across(array, step, level - step).start()

        @pl.when(from_above(step))
        def _():
            for array in (1, 0):
                got = shard(array, level + step)
                remote(got, got, down_send.at[array, step - 1], down_receive.at[array, step - 1], "dp", mate).wait_recv()
                across(array, stages - 1 + step, level + step).start()

    for copy in qkv_copies + small_copies + first_kept:
        copy.start()
    token_one.start()
    token_two.start()
    for copy in qkv_copies + small_copies:
        copy.wait_recv()
    for copy in first_kept:
        copy.wait()
    relay(1)
    own_full = [pltpu.make_async_copy(chains[array][0], shard(array, level), local.at[4 + array]) for array in range(2)]
    for array in range(2):
        across(array, 0, level).start()
        own_full[array].start()
    for copy in fc_copies + later_kept:
        copy.start()
    take(1)
    relay(2)
    take(2)
    relay(3)
    token_one.wait_recv()
    token_two.wait_recv()
    for copy in token_three:
        copy.start()
    take(3)
    for copy in later_kept + own_full:
        copy.wait()
    for copy in fc_copies:
        copy.wait_recv()
    for copy in qkv_copies + small_copies + fc_copies:
        copy.wait_send()
    token_one.wait_send()
    token_two.wait_send()
    for step in range(1, stages):

        @pl.when(rises(step))
        def _(step=step):
            for array in range(2):
                rising(array, step, place + 2).wait_send()

        @pl.when(falls(step))
        def _(step=step):
            for array in range(2):
                falling(array, step, place - 2).wait_send()

        @pl.when(from_below(step))
        def _(step=step):
            for array in range(2):
                across(array, step, level - step).wait()

        @pl.when(from_above(step))
        def _(step=step):
            for array in range(2):
                across(array, stages - 1 + step, level + step).wait()

    for array in range(2):
        across(array, 0, level).wait()
    for copy in token_three:
        copy.wait()


def opening(tokens, qkv_pieces, fc_pieces, small, dp_count):
    piece, width = tokens.shape
    steps = dp_count // 2 - 1
    anywhere = pl.BlockSpec(memory_space=pl.ANY)
    shape = lambda rows, columns: jax.ShapeDtypeStruct((rows, columns), BF16)
    dma = pltpu.SemaphoreType.DMA
    inside = pl.BlockSpec(memory_space=pltpu.VMEM)
    rows, columns = 4 * qkv_pieces.shape[1], qkv_pieces.shape[2]
    fine = 4 * small.shape[0]
    return pl.pallas_call(
        opening_kernel,
        in_specs=[inside] * 4,
        out_specs=[anywhere] * 4,
        out_shape=[
            shape(4 * piece, width),
            shape(rows * dp_count, columns),
            shape(4 * fc_pieces.shape[1], fc_pieces.shape[2]),
            shape(fine * dp_count, small.shape[1]),
        ],
        scratch_shapes=[
            pltpu.VMEM((rows, columns), BF16), pltpu.VMEM((fine, small.shape[1]), BF16),
            dma((6,)), dma((13,)), dma((13,)), dma((2, steps)), dma((2, steps)), dma((2, steps)), dma((2, steps)),
            dma((2, 2 * steps + 1)), dma((2, 2 * steps + 1)),
        ],
        compiler_params=pltpu.CompilerParams(collective_id=0, has_side_effects=True, vmem_limit_bytes=32 * 2**20),
        cost_estimate=cost(0, 10 * 4 * piece * width),
    )(tokens, qkv_pieces, fc_pieces, small)


def flip(first, second):
    low = lax.rem(first + second, 2)
    high = lax.rem(lax.div(first, 2) + lax.div(second, 2), 2)
    return 2 * high + low


def attend_plane_kernel(
    q, k, v_t, tokens, cot_one, cot_two, key_bias, proj, vectors,
    middle, normed, attended, lse, cot_three,
    score_ref, joint, terms, passed, joined, arrived, send, receive,
):
    piece, width = tokens.shape
    half = piece // 2
    heads = q.shape[1] // HEAD_DIM
    rank = lax.axis_index("seq")
    one, two = neighbours()
    for device in (one, two):
        greet("seq", device)
    pl.semaphore_wait(pltpu.get_barrier_semaphore(), 2)
    up, lower = pl.ds(0, half), pl.ds(half, half)

    def copy(index, source, target, device):
        return remote(source, target, send.at[index], receive.at[index], "seq", device)

    cot_copies = (copy(0, cot_one.at[up], cot_three.at[up], two), copy(1, cot_two.at[lower], cot_three.at[lower], one))
    across = (copy(2, terms.at[3, up], passed.at[0], one), copy(3, terms.at[3, lower], passed.at[1], two))
    plain_one = copy(4, terms.at[1, up], arrived.at[0, up], one)
    plain_two = copy(5, terms.at[2, lower], arrived.at[1, lower], two)
    joined_one = copy(6, joined.at[0], arrived.at[0, lower], one)
    joined_two = copy(7, joined.at[1], arrived.at[1, up], two)
    for item in cot_copies:
        item.start()

    def body(query_ref, key_ref, value_t, attended_tile, lse_tile):
        group, head = pl.program_id(0), pl.program_id(1)
        at = 3 - group
        true = flip(at, rank)
        query = query_ref[...]

        def first(block, top):
            scores = scores_of(key_ref, key_bias, query, flip(block, rank), piece, False)
            score_ref[rows_of(block, piece), :] = scores
            return jnp.maximum(top, jnp.max(scores, axis=0, keepdims=True))

        last = scores_of(key_ref, key_bias, query, at, piece, True)
        top = lax.fori_loop(0, true, first, jnp.max(last, axis=0, keepdims=True))

        def weigh(scores, rel):
            weights = jnp.exp2(scores - top)
            return jnp.sum(weights, axis=0, keepdims=True), nn(value_t[:, rows_of(rel, piece)], weights.astype(BF16))

        def second(block, carry):
            total, out = carry
            more, part = weigh(score_ref[rows_of(block, piece), :], flip(block, rank))
            return total + more, out + part

        total, out = lax.fori_loop(0, true, second, weigh(last, at))
        result = (out / total).T.astype(BF16)
        attended_tile[...] = result
        lse_tile[0] = top + jnp.log2(total)
        joint[:, pl.ds(pl.multiple_of(head * HEAD_DIM, HEAD_DIM), HEAD_DIM)] = result

        @pl.when(head == heads - 1)
        def _():
            terms[at] = nn(joint[...], proj[...]).astype(BF16)

        @pl.when((head == heads - 1) & (group == 0))
        def _():
            for item in across:
                item.start()

        @pl.when((head == heads - 1) & (group == 1))
        def _():
            plain_two.start()

        @pl.when((head == heads - 1) & (group == 2))
        def _():
            plain_one.start()
            for item in across:
                item.wait_recv()
            joined[0] = (terms[1, half:].astype(F32) + passed[1].astype(F32)).astype(BF16)
            joined[1] = (terms[2, :half].astype(F32) + passed[0].astype(F32)).astype(BF16)
            joined_one.start()
            joined_two.start()

    length = q.shape[0]
    pltpu.emit_pipeline(
        body,
        grid=(4, heads),
        in_specs=[
            pl.BlockSpec((piece, HEAD_DIM), lambda g, h: (3 - g, h)),
            pl.BlockSpec((length, HEAD_DIM), lambda g, h: (0, h)),
            pl.BlockSpec((HEAD_DIM, length), lambda g, h: (h, 0)),
        ],
        out_specs=[
            pl.BlockSpec((piece, HEAD_DIM), lambda g, h: (3 - g, h)),
            pl.BlockSpec((1, 1, piece), lambda g, h: (h, 0, 3 - g)),
        ],
    )(q, k, v_t, attended, lse)

    for item in (plain_one, plain_two, joined_one, joined_two):
        item.wait_recv()
    part = min(128, piece)

    def norm_body(token_tile, middle_tile, normed_tile):
        here = pl.ds(pl.multiple_of(pl.program_id(0) * part, part), part)
        total = terms[0, here, :].astype(F32) + arrived[0, here, :].astype(F32) + arrived[1, here, :].astype(F32)
        values = token_tile[...].astype(F32) + (total + vectors[0:1, :])
        middle_tile[...] = values
        normed_tile[...] = (norm_parts(values)[0] * vectors[1:2, :] + vectors[2:3, :]).astype(BF16)

    line = pl.BlockSpec((part, width), lambda i: (i, 0))
    pltpu.emit_pipeline(norm_body, grid=(piece // part,), in_specs=[line], out_specs=[line] * 2)(tokens, middle, normed)
    for item in cot_copies:
        item.wait()
    for item in (*across, plain_one, plain_two, joined_one, joined_two):
        item.wait_send()


def attend_plane(q, k, v_t, tokens, cots, key_bias, proj, vectors):
    piece, width = tokens.shape
    length, columns = q.shape
    heads, half = columns // HEAD_DIM, piece // 2
    anywhere = pl.BlockSpec(memory_space=pl.ANY)
    inside = pl.BlockSpec(memory_space=pltpu.VMEM)
    shape = lambda *dims: jax.ShapeDtypeStruct(dims, BF16)
    dma = pltpu.SemaphoreType.DMA
    return pl.pallas_call(
        attend_plane_kernel,
        in_specs=[anywhere] * 6 + [inside] * 3,
        out_specs=[anywhere] * 5,
        out_shape=[
            jax.ShapeDtypeStruct((piece, width), F32), shape(piece, width), shape(length, columns),
            jax.ShapeDtypeStruct((heads, 1, length), F32), shape(piece, width),
        ],
        scratch_shapes=[
            pltpu.VMEM((length, piece), F32),
            pltpu.VMEM((piece, columns), BF16),
            pltpu.VMEM((4, piece, width), BF16),
            pltpu.VMEM((2, half, width), BF16),
            pltpu.VMEM((2, half, width), BF16),
            pltpu.VMEM((2, piece, width), BF16),
            dma((8,)), dma((8,)),
        ],
        compiler_params=pltpu.CompilerParams(collective_id=2, has_side_effects=True, vmem_limit_bytes=56 * 2**20),
        cost_estimate=cost(3 * length * length * columns + 2 * length * columns * width, 10 * length * width, heads * length * length // 2),
    )(q, k, v_t, tokens, *cots, key_bias, proj, vectors)


def sum_rows(ref, at, columns, value, first):
    total = jnp.sum(value, axis=0, keepdims=True)

    @pl.when(first)
    def _():
        ref[at : at + 1, columns] = total

    @pl.when(jnp.logical_not(first))
    def _():
        ref[at : at + 1, columns] += total


def plane_kernel(
    normed, cot_own, cot_one, cot_two, cot_three, fc, bias, down, middle, gain,
    grad_middle, low_all, sums, hidden_sums, active, hidden_grad, normed_all, cot_all, terms, grad_down, grad_fc,
    normed_buf, cot_buf, sum_ref, joined, passed, arrived, load, local, send, receive,
):
    piece, width = normed.shape
    half = piece // 2
    inner = fc.shape[1]
    length = normed_all.shape[0]
    tile = min(512, inner)
    last = inner // tile - 1
    one, two = neighbours()
    for device in (one, two):
        greet("seq", device)
    pl.semaphore_wait(pltpu.get_barrier_semaphore(), 2)

    up, lower = pl.ds(0, half), pl.ds(half, half)
    rows = lambda k, start=0, size=piece: pl.ds(k * piece + start, size)

    def copy(index, source, target, device):
        return remote(source, target, send.at[index], receive.at[index], "seq", device)

    normed_one = copy(0, normed, normed_buf.at[1], one)
    normed_two = copy(1, normed, normed_buf.at[2], two)
    normed_three = (
        copy(2, normed_buf.at[1, up], normed_buf.at[3, up], two),
        copy(3, normed_buf.at[2, lower], normed_buf.at[3, lower], one),
    )
    across = (copy(4, cot_buf.at[3, up], passed.at[0], one), copy(5, cot_buf.at[3, lower], passed.at[1], two))
    plain_one = copy(6, cot_buf.at[1, up], arrived.at[0, up], one)
    plain_two = copy(7, cot_buf.at[2, lower], arrived.at[1, lower], two)
    joined_one = copy(8, joined.at[0], arrived.at[0, lower], one)
    joined_two = copy(9, joined.at[1], arrived.at[1, up], two)
    low_one = copy(10, low_all.at[rows(0)], low_all.at[rows(1)], one)
    low_two = copy(11, low_all.at[rows(0)], low_all.at[rows(2)], two)
    low_three = (
        copy(12, low_all.at[rows(1, 0, half)], low_all.at[rows(3, 0, half)], two),
        copy(13, low_all.at[rows(2, half, half)], low_all.at[rows(3, half, half)], one),
    )

    loads = [
        pltpu.make_async_copy(source, cot_buf.at[k], load.at[k])
        for k, source in enumerate((cot_own, cot_one, cot_two, cot_three))
    ]
    own = pltpu.make_async_copy(normed, normed_buf.at[0], load.at[4])
    keeps = [pltpu.make_async_copy(normed_buf.at[k], normed_all.at[rows(k)], local.at[k]) for k in range(4)]
    keeps_cot = [pltpu.make_async_copy(cot_buf.at[k], cot_all.at[rows(k)], local.at[4 + k]) for k in range(4)]

    normed_one.start()
    normed_two.start()
    own.start()
    for item in loads:
        item.start()

    def feed_body(fc_tile, down_tile, active_tile, hidden_tile):
        k, j = pl.program_id(0), pl.program_id(1)

        @pl.when((k == 0) & (j == 0))
        def _():
            own.wait()
            keeps[0].start()
            for item in loads:
                item.wait()
            for item in keeps_cot:
                item.start()

        @pl.when((k == 1) & (j == 0))
        def _():
            normed_one.wait_recv()
            normed_two.wait_recv()
            for item in normed_three:
                item.start()
            keeps[1].start()
            keeps[2].start()

        @pl.when((k == 3) & (j == 0))
        def _():
            for item in normed_three:
                item.wait_recv()
            keeps[3].start()

        weights = fc_tile[...]
        columns = pl.ds(pl.multiple_of(j * tile, tile), tile)
        hidden = nn(normed_buf[k], weights) + bias[:, columns]
        grad_active = nt(cot_buf[k], down_tile[...])
        square = hidden * hidden
        bent = jnp.tanh(math.sqrt(2 / math.pi) * (hidden + 0.044715 * (square * hidden)))
        share = 0.5 * (1.0 + bent)
        active_tile[...] = (hidden * share).astype(BF16)
        slope = share + (0.5 * hidden) * (1.0 - bent * bent) * (
            math.sqrt(2 / math.pi) * (1.0 + (3 * 0.044715) * square)
        )
        grad_hidden = (grad_active * slope).astype(BF16)
        hidden_tile[...] = grad_hidden
        sum_rows(hidden_sums, 0, columns, grad_hidden.astype(F32), k == 0)
        term = nt(grad_hidden, weights)

        @pl.when(j == 0)
        def _():
            sum_ref[...] = term

        @pl.when(j > 0)
        def _():
            sum_ref[...] += term

        @pl.when((j == last) & (k == 0))
        def _():
            for item in keeps_cot:
                item.wait()
            arrived[2] = sum_ref[...].astype(BF16)

        @pl.when((j == last) & (k == 1))
        def _():
            cot_buf[1] = sum_ref[...].astype(BF16)
            plain_one.start()

        @pl.when((j == last) & (k == 2))
        def _():
            cot_buf[2] = sum_ref[...].astype(BF16)
            plain_two.start()

        @pl.when((j == last) & (k == 3))
        def _():
            cot_buf[3] = sum_ref[...].astype(BF16)
            for item in across:
                item.start()

    pltpu.emit_pipeline(
        feed_body,
        grid=(4, inner // tile),
        in_specs=[
            pl.BlockSpec((width, tile), lambda k, j: (0, j)),
            pl.BlockSpec((tile, width), lambda k, j: (j, 0)),
        ],
        out_specs=[pl.BlockSpec((piece, tile), lambda k, j: (k, j))] * 2,
    )(fc, down, active, hidden_grad)

    narrow = min(512, width)

    def down_body(active_rows, down_columns, out):
        out[...] = nn(active_rows[...], down_columns[...]).astype(BF16)

    def multiply_down(start):
        pltpu.emit_pipeline(
            down_body,
            grid=(2, width // narrow),
            in_specs=[
                pl.BlockSpec((piece, inner), lambda k, j: (start + k, 0)),
                pl.BlockSpec((inner, narrow), lambda k, j: (0, j)),
            ],
            out_specs=[pl.BlockSpec((piece, narrow), lambda k, j: (start + k, j))],
        )(active, down, terms)

    multiply_down(0)
    for item in across:
        item.wait_recv()
    joined[0] = (cot_buf[1, half:].astype(F32) + passed[1].astype(F32)).astype(BF16)
    joined[1] = (cot_buf[2, :half].astype(F32) + passed[0].astype(F32)).astype(BF16)
    joined_one.start()
    joined_two.start()
    for item in keeps:
        item.wait()
    multiply_down(2)
    for item in (plain_one, plain_two, joined_one, joined_two):
        item.wait_recv()

    part = min(128, piece)

    def norm_body(middle_tile, cot_tile, grad_tile, low_tile):
        i = pl.program_id(0)
        here = pl.ds(pl.multiple_of(i * part, part), part)
        upstream = (
            arrived[2, here, :].astype(F32) + arrived[0, here, :].astype(F32) + arrived[1, here, :].astype(F32)
        )
        unit, scale = norm_parts(middle_tile[...])
        cot = cot_tile[...].astype(F32)
        grad = cot + norm_backward(unit, scale, gain[...], upstream)
        rounded = grad.astype(BF16)
        grad_tile[...] = grad
        low_tile[...] = rounded
        for at, item in enumerate((upstream * unit, upstream, rounded.astype(F32), cot)):
            sum_rows(sums, at, slice(None), item, i == 0)

    line = pl.BlockSpec((part, width), lambda i: (i, 0))
    pltpu.emit_pipeline(norm_body, grid=(piece // part,), in_specs=[line] * 2, out_specs=[line] * 2)(
        middle, cot_own, grad_middle, low_all
    )
    low_one.start()
    low_two.start()

    wide, tall = min(1024, width), min(1024, inner)

    def outer_body(left, right, out):
        out[...] = tn(left[...], right[...]).astype(BF16)

    def outer(left, right, out, shape):
        pltpu.emit_pipeline(
            outer_body,
            grid=(out.shape[0] // shape[0], out.shape[1] // shape[1]),
            in_specs=[
                pl.BlockSpec((length, shape[0]), lambda i, j: (0, i)),
                pl.BlockSpec((length, shape[1]), lambda i, j: (0, j)),
            ],
            out_specs=[pl.BlockSpec(shape, lambda i, j: (i, j))],
        )(left, right, out)

    outer(active, cot_all, grad_down, (tall, wide))
    low_one.wait_recv()
    low_two.wait_recv()
    for item in low_three:
        item.start()
    outer(normed_all, hidden_grad, grad_fc, (wide, tall))
    for item in low_three:
        item.wait()
    for item in (
        normed_one, normed_two, *normed_three, *across, plain_one, plain_two, joined_one, joined_two, low_one, low_two
    ):
        item.wait_send()


def feed_plane(normed, cots, fc, bias, down, middle, gain):
    piece, width = normed.shape
    inner = fc.shape[1]
    length, half = 4 * piece, piece // 2
    anywhere = pl.BlockSpec(memory_space=pl.ANY)
    inside = pl.BlockSpec(memory_space=pltpu.VMEM)
    shape = lambda rows, columns, kind=BF16: jax.ShapeDtypeStruct((rows, columns), kind)
    dma = pltpu.SemaphoreType.DMA
    return pl.pallas_call(
        plane_kernel,
        in_specs=[anywhere] * 6 + [inside, anywhere, anywhere, inside],
        out_specs=[anywhere, anywhere, inside, inside] + [anywhere] * 7,
        out_shape=[
            shape(piece, width, F32), shape(length, width), shape(4, width, F32), shape(1, inner, F32),
            shape(length, inner), shape(length, inner), shape(length, width), shape(length, width),
            shape(length, width), shape(inner, width), shape(width, inner),
        ],
        scratch_shapes=[
            pltpu.VMEM((4, piece, width), BF16),
            pltpu.VMEM((4, piece, width), BF16),
            pltpu.VMEM((piece, width), F32),
            pltpu.VMEM((2, half, width), BF16),
            pltpu.VMEM((2, half, width), BF16),
            pltpu.VMEM((3, piece, width), BF16),
            dma((5,)), dma((8,)), dma((14,)), dma((14,)),
        ],
        compiler_params=pltpu.CompilerParams(collective_id=1, has_side_effects=True, vmem_limit_bytes=60 * 2**20),
        cost_estimate=cost(12 * length * width * inner, 10 * length * width),
    )(normed, *cots, fc, bias, down, middle, gain)


def retreat_plane_kernel(
    low_all, q, k, v, k_t, lse, terms, middle, key_bias, proj, down_shift,
    grads, column_sums, block_out,
    prob_ref, chance_ref, grad_ref, key_sum, value_sum, rounded, own, passed, joined, arrived,
    load, local, send, receive,
):
    piece, width = middle.shape
    half = piece // 2
    length, columns = q.shape
    heads = columns // HEAD_DIM
    rank = lax.axis_index("seq")
    one, two = neighbours()
    for device in (one, two):
        greet("seq", device)
    pl.semaphore_wait(pltpu.get_barrier_semaphore(), 2)
    up, lower = pl.ds(0, half), pl.ds(half, half)
    rows = lambda at, start=0, size=piece: pl.ds(at * piece + start, size)

    def copy(index, source, target, device):
        return remote(source, target, send.at[index], receive.at[index], "seq", device)

    across = (
        copy(0, terms.at[rows(3, 0, half)], passed.at[0], one),
        copy(1, terms.at[rows(3, half, half)], passed.at[1], two),
    )
    plain_one = copy(2, terms.at[rows(1, 0, half)], arrived.at[0, up], one)
    plain_two = copy(3, terms.at[rows(2, half, half)], arrived.at[1, lower], two)
    joined_one = copy(4, joined.at[0], arrived.at[0, lower], one)
    joined_two = copy(5, joined.at[1], arrived.at[1, up], two)
    loads = (
        pltpu.make_async_copy(terms.at[rows(1, half, half)], own.at[0], load.at[0]),
        pltpu.make_async_copy(terms.at[rows(2, 0, half)], own.at[1], load.at[1]),
    )
    for item in (*across, plain_one, plain_two, *loads):
        item.start()
    key_sum[...] = jnp.zeros_like(key_sum)
    value_sum[...] = jnp.zeros_like(value_sum)

    def body(low_ref, query_ref, key_ref, value_ref, key_t, lse_ref, query_out):
        at, head = pl.program_id(0), pl.program_id(1)
        true = flip(at, rank)
        here = pl.ds(pl.multiple_of(head * HEAD_DIM, HEAD_DIM), HEAD_DIM)

        @pl.when(head == 0)
        def _():
            grad_ref[...] = nt(low_ref[...], proj[...]).astype(BF16)

        @pl.when((at == 1) & (head == 2))
        def _():
            for item in (*across,):
                item.wait_recv()
            for item in loads:
                item.wait()
            joined[0] = (own[0].astype(F32) + passed[1].astype(F32)).astype(BF16)
            joined[1] = (own[1].astype(F32) + passed[0].astype(F32)).astype(BF16)
            joined_one.start()
            joined_two.start()

        query, grad, base = query_ref[...], grad_ref[:, here], lse_ref[0]

        def measure(scores, rel):
            block = rows_of(rel, piece)
            probs = jnp.exp2(scores - base)
            grad_chances = nt(value_ref[block, :], grad)
            value_sum[block, here] += nn(probs.astype(BF16), grad)
            prob_ref[block, :] = probs
            chance_ref[block, :] = grad_chances
            return jnp.sum(probs * grad_chances, axis=0, keepdims=True)

        def first(block, weighted):
            rel = flip(block, rank)
            return weighted + measure(scores_of(key_ref, key_bias, query, rel, piece, False), rel)

        last = scores_of(key_ref, key_bias, query, at, piece, True)
        weighted = lax.fori_loop(0, true, first, measure(last, at))

        def second(block, total):
            block = rows_of(flip(block, rank), piece)
            grad_scores = (prob_ref[block, :] * (chance_ref[block, :] - weighted)).astype(BF16)
            key_sum[block, here] += nn(grad_scores, query)
            return total + nn(key_t[:, block], grad_scores)

        total = lax.fori_loop(0, true + 1, second, jnp.zeros((HEAD_DIM, piece), F32))
        result = (total * FACTOR).T.astype(BF16)
        query_out[...] = result
        sum_rows(column_sums, 0, here, result.astype(F32), at == 0)

    pltpu.emit_pipeline(
        body,
        grid=(4, heads),
        in_specs=[
            pl.BlockSpec((piece, width), lambda g, h: (g, 0)),
            pl.BlockSpec((piece, HEAD_DIM), lambda g, h: (g, h)),
            pl.BlockSpec((length, HEAD_DIM), lambda g, h: (0, h)),
            pl.BlockSpec((length, HEAD_DIM), lambda g, h: (0, h)),
            pl.BlockSpec((HEAD_DIM, length), lambda g, h: (h, 0)),
            pl.BlockSpec((1, 1, piece), lambda g, h: (h, 0, g)),
        ],
        out_specs=[pl.BlockSpec((piece, HEAD_DIM), lambda g, h: (g, h))],
    )(low_all, q, k, v, k_t, lse, grads)

    rounded[:, :columns] = (key_sum[...] * FACTOR).astype(BF16)
    values = value_sum[...].astype(BF16)
    rounded[:, columns:] = values
    column_sums[1:2, :] = jnp.sum(values.astype(F32), axis=0, keepdims=True)
    keep = pltpu.make_async_copy(rounded, grads.at[:, pl.ds(columns, 2 * columns)], local.at[0])
    keep.start()
    for item in (plain_one, plain_two, joined_one, joined_two):
        item.wait_recv()
    part = min(128, piece)

    def out_body(middle_tile, term_tile, out):
        here = pl.ds(pl.multiple_of(pl.program_id(0) * part, part), part)
        total = term_tile[...].astype(F32) + arrived[0, here, :].astype(F32) + arrived[1, here, :].astype(F32)
        out[...] = (middle_tile[...] + (total + down_shift[...])).astype(BF16)

    line = pl.BlockSpec((part, width), lambda i: (i, 0))
    pltpu.emit_pipeline(out_body, grid=(piece // part,), in_specs=[line] * 2, out_specs=[line])(middle, terms, block_out)
    keep.wait()
    for item in (*across, plain_one, plain_two, joined_one, joined_two):
        item.wait_send()


def retreat_plane(low_all, q, k, v, k_t, lse, terms, middle, key_bias, proj, down_shift):
    piece, width = middle.shape
    length, columns = q.shape
    half = piece // 2
    anywhere = pl.BlockSpec(memory_space=pl.ANY)
    inside = pl.BlockSpec(memory_space=pltpu.VMEM)
    dma = pltpu.SemaphoreType.DMA
    return pl.pallas_call(
        retreat_plane_kernel,
        in_specs=[anywhere] * 8 + [inside] * 3,
        out_specs=[anywhere, inside, anywhere],
        out_shape=[
            jax.ShapeDtypeStruct((length, 3 * columns), BF16),
            jax.ShapeDtypeStruct((2, columns), F32),
            jax.ShapeDtypeStruct((piece, width), BF16),
        ],
        scratch_shapes=[
            pltpu.VMEM((length, piece), F32),
            pltpu.VMEM((length, piece), F32),
            pltpu.VMEM((piece, columns), BF16),
            pltpu.VMEM((length, columns), F32),
            pltpu.VMEM((length, columns), F32),
            pltpu.VMEM((length, 2 * columns), BF16),
            pltpu.VMEM((2, half, width), BF16),
            pltpu.VMEM((2, half, width), BF16),
            pltpu.VMEM((2, half, width), BF16),
            pltpu.VMEM((2, piece, width), BF16),
            dma((2,)), dma((1,)), dma((6,)), dma((6,)),
        ],
        compiler_params=pltpu.CompilerParams(collective_id=3, has_side_effects=True, vmem_limit_bytes=60 * 2**20),
        cost_estimate=cost(8 * length * length * columns + 2 * length * columns * width, 10 * length * width),
    )(low_all, q, k, v, k_t, lse, terms, middle, key_bias, proj, down_shift)


def closing_kernel(
    grads, weight, tokens, grad_middle, gain, tokens_grad, sums,
    terms, passed, joined, arrived, send, receive,
):
    piece, width = tokens.shape
    half = piece // 2
    one, two = neighbours()
    for device in (one, two):
        greet("seq", device)
    pl.semaphore_wait(pltpu.get_barrier_semaphore(), 2)
    up, lower = pl.ds(0, half), pl.ds(half, half)

    def copy(index, source, target, device):
        return remote(source, target, send.at[index], receive.at[index], "seq", device)

    across = (copy(0, terms.at[3, up], passed.at[0], one), copy(1, terms.at[3, lower], passed.at[1], two))
    plain_one = copy(2, terms.at[1, up], arrived.at[0, up], one)
    plain_two = copy(3, terms.at[2, lower], arrived.at[1, lower], two)
    joined_one = copy(4, joined.at[0], arrived.at[0, lower], one)
    joined_two = copy(5, joined.at[1], arrived.at[1, up], two)

    @pl.loop(0, 4)
    def _(step):
        at = 3 - step
        terms[at] = nt(grads[pl.ds(pl.multiple_of(at * piece, piece), piece), :], weight[...]).astype(BF16)

        @pl.when(step == 0)
        def _():
            for item in across:
                item.start()

        @pl.when(step == 1)
        def _():
            plain_two.start()

        @pl.when(step == 2)
        def _():
            plain_one.start()

    for item in across:
        item.wait_recv()
    joined[0] = (terms[1, half:].astype(F32) + passed[1].astype(F32)).astype(BF16)
    joined[1] = (terms[2, :half].astype(F32) + passed[0].astype(F32)).astype(BF16)
    joined_one.start()
    joined_two.start()
    for item in (plain_one, plain_two, joined_one, joined_two):
        item.wait_recv()
    part = min(128, piece)

    def norm_body(token_tile, middle_tile, out):
        i = pl.program_id(0)
        here = pl.ds(pl.multiple_of(i * part, part), part)
        upstream = terms[0, here, :].astype(F32) + arrived[0, here, :].astype(F32) + arrived[1, here, :].astype(F32)
        unit, scale = norm_parts(token_tile[...].astype(F32))
        out[...] = middle_tile[...] + norm_backward(unit, scale, gain[...], upstream)
        for at, item in enumerate((upstream * unit, upstream)):
            sum_rows(sums, at, slice(None), item, i == 0)

    line = pl.BlockSpec((part, width), lambda i: (i, 0))
    pltpu.emit_pipeline(norm_body, grid=(piece // part,), in_specs=[line] * 2, out_specs=[line])(
        tokens, grad_middle, tokens_grad
    )
    for item in (*across, plain_one, plain_two, joined_one, joined_two):
        item.wait_send()


def closing(grads, weight, tokens, grad_middle, gain):
    piece, width = tokens.shape
    half = piece // 2
    anywhere = pl.BlockSpec(memory_space=pl.ANY)
    inside = pl.BlockSpec(memory_space=pltpu.VMEM)
    dma = pltpu.SemaphoreType.DMA
    return pl.pallas_call(
        closing_kernel,
        in_specs=[inside, inside, anywhere, anywhere, inside],
        out_specs=[anywhere, inside],
        out_shape=[jax.ShapeDtypeStruct((piece, width), F32), jax.ShapeDtypeStruct((2, width), F32)],
        scratch_shapes=[
            pltpu.VMEM((4, piece, width), BF16),
            pltpu.VMEM((2, half, width), BF16),
            pltpu.VMEM((2, half, width), BF16),
            pltpu.VMEM((2, piece, width), BF16),
            dma((6,)), dma((6,)),
        ],
        compiler_params=pltpu.CompilerParams(collective_id=4, has_side_effects=True, vmem_limit_bytes=60 * 2**20),
        cost_estimate=cost(8 * piece * width * grads.shape[1], 10 * piece * width),
    )(grads, weight, tokens, grad_middle, gain)


def after(value, *others):
    return lax.optimization_barrier((value, *others))[0]


def shift(value, axis, distance):
    count = lax.axis_size(axis)
    return lax.ppermute(value, axis, [(i, i ^ distance) for i in range(count)])


def gather_blocks(value, axis="seq"):
    return [value] + [shift(value, axis, k) for k in range(1, lax.axis_size(axis))]


def scatter_blocks(blocks, axis="seq"):
    return [blocks[0]] + [shift(blocks[k], axis, k) for k in range(1, lax.axis_size(axis))]


def gather_plane(value):
    if lax.axis_size("seq") != 4:
        return gather_blocks(value)
    half = value.shape[0] // 2
    one, two = shift(value, "seq", 1), shift(value, "seq", 2)
    three = jnp.concatenate([shift(one[:half], "seq", 2), shift(two[half:], "seq", 1)], axis=0)
    return [value, one, two, three]


def scatter_plane(blocks):
    if lax.axis_size("seq") != 4:
        return scatter_blocks(blocks)
    half = blocks[0].shape[0] // 2
    up, low = shift(blocks[3][:half], "seq", 1), shift(blocks[3][half:], "seq", 2)
    one = shift(blocks[1][:half], "seq", 1)
    two = shift(blocks[2][half:], "seq", 2)
    one_low = (blocks[1][half:].astype(F32) + low.astype(F32)).astype(BF16)
    two_up = (blocks[2][:half].astype(F32) + up.astype(F32)).astype(BF16)
    return [blocks[0], (one, shift(one_low, "seq", 1)), (shift(two_up, "seq", 2), two)]


def by_rank(blocks, rank):
    bit = 1
    while bit < len(blocks):
        odd = (rank & bit) != 0
        blocks = [jnp.where(odd, blocks[k ^ bit], blocks[k]) for k in range(len(blocks))]
        bit *= 2
    return blocks


def pick(pieces, at):
    return lax.dynamic_index_in_dim(pieces, at, axis=0, keepdims=False)


def exchange(pieces, rank):
    return scatter_blocks([pick(pieces, rank ^ k) for k in range(pieces.shape[0])])


def small_scatter(pieces, dp_rank, seq_rank):
    total = 0.0
    sent = [lax.dynamic_index_in_dim(pieces, seq_rank ^ k, axis=1, keepdims=False) for k in range(pieces.shape[1])]
    for part in scatter_blocks(sent):
        total = total + part
    sent = [pick(total, dp_rank ^ k) for k in range(pieces.shape[0])]
    total = 0.0
    for part in scatter_blocks(sent, "dp"):
        total = total + part
    return total


def swap_pairs(dp_count, seq_count, sub):
    pairs = []
    for d in range(dp_count):
        for s in range(seq_count):
            source = ((d // sub) * sub + s % sub) * seq_count + (s // sub) * sub + d % sub
            pairs.append((source, d * seq_count + s))
    return pairs


def gather_dp(value):
    return lax.all_gather(value, "dp", axis=0, tiled=True)


def scatter_dp(value):
    return lax.psum_scatter(value, "dp", scatter_dimension=0, tiled=True)


def shards(
    tokens,
    cotangent,
    lengths,
    key_mask,
    attn_gain,
    attn_shift,
    qkv_weight,
    qv_bias,
    proj_weight,
    proj_bias,
    mlp_gain,
    mlp_shift,
    fc_weight,
    fc_bias,
    down_weight,
    down_bias,
):
    _, piece, width = tokens.shape
    dp_count, seq_count = lax.axis_size("dp"), lax.axis_size("seq")
    dp_rank, seq_rank = lax.axis_index("dp"), lax.axis_index("seq")
    own_heads = HEADS // seq_count
    own_width = own_heads * HEAD_DIM
    rows = qkv_weight.shape[0]
    sub = HEAD_DIM // proj_weight.shape[0]
    high = seq_count // sub
    block = down_weight.shape[0]
    rank = jnp.reshape(seq_rank, (1,)).astype(jnp.int32)
    swap = swap_pairs(dp_count, seq_count, sub)
    order = list(range(seq_count - 1, -1, -1))
    if seq_count == 4:
        order = [3, 1, 2, 0]

    in_plane = seq_count == 4 and dp_count == 8
    qkv_pieces = (
        qkv_weight.reshape(rows, 3, own_heads, sub, high, HEAD_DIM)
        .transpose(4, 3, 0, 1, 2, 5)
        .reshape(seq_count, rows, 3 * own_width)
    )
    tokens_own, cot_own = tokens[0], cotangent[0]

    small = (attn_gain, attn_shift, qv_bias, proj_bias, mlp_gain, mlp_shift, fc_bias, down_bias)
    sizes = [item.shape[0] for item in small]
    positions = seq_rank * piece + jnp.arange(piece, dtype=jnp.int32)
    own_flags = ((key_mask[0] == 1) & (positions < lengths[0])).astype(BF16)
    packed = jnp.concatenate(small + (own_flags,))
    fc_pieces = (
        fc_weight.reshape(rows, dp_count, seq_count, block)
        .transpose(2, 0, 1, 3)
        .reshape(seq_count, rows, dp_count * block)
    )
    if in_plane:
        room = -(-packed.shape[0] // 2048) * 2048
        small_rows = jnp.pad(packed, (0, room - packed.shape[0])).reshape(room // 128, 128)
        token_all, qkv_full, fc_rows, small_full = opening(
            tokens_own, qkv_pieces, fc_pieces, small_rows, dp_count
        )
        packed = small_full.reshape(dp_count, seq_count, room)
        flags = lax.dynamic_index_in_dim(packed, dp_rank, axis=0, keepdims=False)
        flags = jnp.concatenate(by_rank([flags[s, sum(sizes) : sum(sizes) + piece] for s in range(seq_count)], seq_rank))
        packed = packed[:, :, : sum(sizes)].astype(F32)
    else:
        qkv_full = gather_dp(jnp.concatenate(by_rank(exchange(qkv_pieces, seq_rank), seq_rank), axis=0))
        blocks = gather_blocks(packed)
        flags = jnp.concatenate([item[-piece:] for item in blocks])
        packed = jnp.stack(by_rank([item[:-piece] for item in blocks], seq_rank))
        packed = jnp.stack(by_rank(gather_blocks(packed, "dp"), dp_rank)).astype(F32)
        fc_rows = jnp.concatenate(by_rank(exchange(fc_pieces, seq_rank), seq_rank), axis=0)
    key_bias = jnp.where(flags > 0, 0.0, NEG).astype(F32)[:, None]
    parts, start = [], 0
    for size in sizes:
        parts.append(packed[:, :, start : start + size])
        start += size
    whole = [part.reshape(1, -1) for part in parts]
    gain_one, shift_one, qv_full, proj_shift, gain_two, shift_two, _, down_shift = whole
    fc_shift = lax.dynamic_index_in_dim(parts[6], seq_rank, axis=1, keepdims=False).reshape(1, -1)
    rank_low, rank_high = seq_rank % sub, seq_rank // sub
    qv_heads = qv_full.reshape(2, own_heads, sub, high, HEAD_DIM)
    qv_own = lax.dynamic_index_in_dim(
        lax.dynamic_index_in_dim(qv_heads, rank_low, axis=2, keepdims=False), rank_high, axis=2, keepdims=False
    )
    qv_own = qv_own.reshape(1, -1)

    length = piece * seq_count
    proj_full = gather_dp(lax.ppermute(proj_weight, BOTH, swap))
    down_full = gather_dp(after(down_weight, fc_rows) if in_plane else down_weight)
    fc_full = gather_dp(fc_rows)
    shared = None
    if in_plane:
        cot_own, token_all = lax.optimization_barrier((cot_own, token_all))
        cots = (shift(cot_own, "seq", 1), shift(cot_own, "seq", 2))
        shared = project(0, token_all, 0, length, gain_one, shift_one, qkv_full, qv_own, length, None)
    else:
        token_blocks = gather_blocks(tokens_own)
        cot_blocks = gather_blocks(after(cot_own, token_blocks[-1]))
        for k in range(seq_count):
            shared = project(k, token_blocks[k], 0, piece, gain_one, shift_one, qkv_full, qv_own, length, shared)
    normed_one, q, keys, values, keys_t, values_t = shared
    if in_plane:
        middle, normed_two, attended, lse, cot_three = attend_plane(
            q, keys, values_t, tokens_own, cots, key_bias, proj_full,
            jnp.concatenate([proj_shift, gain_two, shift_two], axis=0),
        )
    else:
        proj_terms, shared = [None] * seq_count, None
        for k in order:
            proj_terms[k], shared = attend(k, rank, q, keys, values_t, key_bias, proj_full, piece, shared)
        attended, lse = shared
        middle, normed_two = rowwise(
            middle_kernel, scatter_blocks(proj_terms), [tokens_own], [proj_shift, gain_two, shift_two], [F32, BF16], 0
        )

    if in_plane:
        grad_middle, low_all, sums_two, hidden_sums, _, _, _, _, down_terms, grad_down, grad_fc = feed_plane(
            normed_two, (cot_own, *cots, cot_three), fc_full, fc_shift, down_full, middle, gain_two
        )
        sums_two = [sums_two[i] for i in range(4)]
        grad_down, grad_fc = scatter_dp(grad_down), scatter_dp(grad_fc)
        grads, qv_sums, block_out = retreat_plane(
            low_all, q, keys, values, keys_t, lse, down_terms, middle, key_bias, proj_full, down_shift
        )
    else:
        normed_blocks = gather_blocks(normed_two)
        grad_terms, shared = [], None
        for k in range(seq_count):
            term, shared = feed(k, normed_blocks[k], cot_blocks[k], fc_full, fc_shift, down_full, seq_count, shared)
            grad_terms.append(term)
        active, grad_hidden, normed_all, cot_all = shared
        grad_middle, grad_mid_low, *sums_two = rowwise(
            middle_back_kernel, scatter_blocks(grad_terms), [middle, cot_own], [gain_two], [F32, BF16], 4
        )
        down_terms = [
            nn(active[k * piece : (k + 1) * piece], down_full).astype(BF16) for k in range(seq_count)
        ]
        low_blocks = gather_blocks(grad_mid_low)
        grad_down = scatter_dp(tn(active, cot_all).astype(BF16))
        grad_fc = scatter_dp(tn(normed_all, grad_hidden).astype(BF16))
        hidden_sums = jnp.sum(grad_hidden.astype(F32), axis=0)
        block_out = rowwise(out_kernel, scatter_blocks(down_terms), [middle], [down_shift], [BF16], 0)[0]
        sums, shared = None, None
        for k in range(seq_count):
            sums, shared = retreat(
                k, rank, low_blocks[k], proj_full, q, lse, keys, values, keys_t, key_bias, sums, shared,
                k == seq_count - 1,
            )
        grad_q, low_all = shared
        grads = jnp.concatenate([grad_q, sums[0], sums[1]], axis=1)
        qv_sums = jnp.stack([jnp.sum(item.astype(F32), axis=0) for item in (grad_q, sums[1])])
    grad_qkv = scatter_dp(tn(normed_one, grads).astype(BF16))
    grad_proj = scatter_dp(tn(attended, low_all).astype(BF16))
    grad_proj = lax.ppermute(grad_proj, BOTH, swap).astype(F32)
    if in_plane:
        tokens_grad, sums_one = closing(grads, qkv_full, tokens_own, grad_middle, gain_one)
        sums_one = [sums_one[i] for i in range(2)]
    else:
        back_terms = [None] * seq_count
        for k in order:
            back_terms[k] = back(k, grads, qkv_full, piece)
        tokens_grad, *sums_one = rowwise(
            tokens_back_kernel, scatter_blocks(back_terms), [tokens_own, grad_middle], [gain_one], [F32], 2
        )

    blocks = exchange(grad_fc.reshape(seq_count, rows, dp_count * block), seq_rank)
    if block % 128 == 0:
        fc_places = lambda s: [(0, d, d * seq_count + s) for d in range(dp_count)]
        grad_fc = lay_out(rank, [[item] for item in blocks], fc_weight.shape[1], (fc_places, block))
    else:
        blocks = [item.reshape(rows, dp_count, block) for item in by_rank(blocks, seq_rank)]
        grad_fc = jnp.stack(blocks, axis=2).reshape(fc_weight.shape).astype(F32)
    blocks = [[item] for item in exchange(grad_qkv.reshape(seq_count, rows, 3 * own_width), seq_rank)]
    qkv_places = lambda s: [
        (0, part * own_heads + head, part * HEADS + (head * sub + s % sub) * high + s // sub)
        for part in range(3)
        for head in range(own_heads)
    ]
    grad_qkv_weight = lay_out(rank, blocks, qkv_weight.shape[1], (qkv_places, HEAD_DIM))

    def spread(vector):
        return vector.reshape(dp_count, seq_count, -1)

    here = (jnp.arange(seq_count) == seq_rank).astype(F32)
    hidden_sums = hidden_sums.reshape(dp_count, 1, -1) * here[None, :, None]
    early = jnp.concatenate([spread(item) for item in sums_two] + [hidden_sums], axis=2)
    early = small_scatter(early, dp_rank, seq_rank)
    here = (jnp.arange(sub) == rank_low)[:, None] & (jnp.arange(high) == rank_high)[None, :]
    qv_sums = qv_sums.reshape(2, own_heads, 1, 1, HEAD_DIM) * here.astype(F32)[None, None, :, :, None]
    late = jnp.concatenate([spread(item) for item in sums_one] + [spread(qv_sums)], axis=2)
    late = small_scatter(late, dp_rank, seq_rank)
    share = attn_gain.shape[0]
    return (
        block_out[None],
        tokens_grad[None],
        late[:share],
        late[share : 2 * share],
        grad_qkv_weight,
        late[2 * share :],
        grad_proj,
        early[2 * share : 3 * share],
        early[:share],
        early[share : 2 * share],
        grad_fc,
        early[4 * share :],
        grad_down.astype(F32),
        early[3 * share : 4 * share],
    )


def solution(mesh):
    in_specs = (
        P("dp", "seq", None),
        P("dp", "seq", None),
        P("dp"),
        P("dp", "seq"),
        P(BOTH),
        P(BOTH),
        P(BOTH, None),
        P(BOTH),
        P(BOTH, None),
        P(BOTH),
        P(BOTH),
        P(BOTH),
        P(BOTH, None),
        P(BOTH),
        P(BOTH, None),
        P(BOTH),
    )
    out_specs = (
        P("dp", "seq", None),
        P("dp", "seq", None),
        P(BOTH),
        P(BOTH),
        P(BOTH, None),
        P(BOTH),
        P(BOTH, None),
        P(BOTH),
        P(BOTH),
        P(BOTH),
        P(BOTH, None),
        P(BOTH),
        P(BOTH, None),
        P(BOTH),
    )
    return jax.shard_map(shards, mesh=mesh, in_specs=in_specs, out_specs=out_specs, check_vma=False)
```

```python
import functools
import math

import jax
import jax.numpy as jnp
from jax import lax
from jax.experimental import pallas as pl
from jax.experimental.pallas import tpu as pltpu
from jax.sharding import PartitionSpec as P

HEADS = 16
HEAD_DIM = 128
EPS = 1e-05
NEG = -1e30
FACTOR = HEAD_DIM ** (-0.5)
LOG2E = math.log2(math.e)
F32 = jnp.float32
BF16 = jnp.bfloat16
BOTH = ("dp", "seq")
MESH = pl.DeviceIdType.MESH


def nn(left, right):
    return lax.dot_general(left, right, (((1,), (0,)), ((), ())), preferred_element_type=F32)


def nt(left, right):
    return lax.dot_general(left, right, (((1,), (1,)), ((), ())), preferred_element_type=F32)


def tn(left, right):
    return lax.dot_general(left, right, (((0,), (0,)), ((), ())), preferred_element_type=F32)


def params(limit_mib=56):
    return pltpu.CompilerParams(dimension_semantics=("arbitrary",), vmem_limit_bytes=limit_mib * 2**20)


def cost(flops, moved, exps=0):
    return pl.CostEstimate(flops=int(flops), bytes_accessed=int(moved), transcendentals=int(exps))


def call_on_block(kernel, grid, inputs, fresh, shared, previous, scratch, estimate, rank=None):
    arrays = [item for item, _ in inputs]
    specs = [spec for _, spec in inputs]
    aliases = {}
    lead = 0 if rank is None else 1
    if previous is not None:
        for at, item in enumerate(previous):
            aliases[lead + len(arrays)] = len(fresh) + at
            arrays.append(item)
            specs.append(pl.BlockSpec(memory_space=pl.ANY))
    count = len(inputs)
    skipped = 0 if previous is None else len(previous)

    def body(*refs):
        refs = list(refs)
        kernel(*refs[: lead + count], *refs[lead + count + skipped :])

    out_specs = [spec for _, spec in fresh] + [spec for _, spec in shared]
    out_shape = [shape for shape, _ in fresh] + [shape for shape, _ in shared]
    if rank is None:
        results = pl.pallas_call(
            body, grid=grid, in_specs=specs, out_specs=out_specs, out_shape=out_shape, scratch_shapes=scratch,
            input_output_aliases=aliases, compiler_params=params(), cost_estimate=estimate,
        )(*arrays)
    else:
        results = pl.pallas_call(
            body,
            grid_spec=pltpu.PrefetchScalarGridSpec(
                num_scalar_prefetch=1, grid=grid, in_specs=specs, out_specs=out_specs, scratch_shapes=scratch
            ),
            out_shape=out_shape, input_output_aliases=aliases, compiler_params=params(), cost_estimate=estimate,
        )(rank, *arrays)
    return results[: len(fresh)], results[len(fresh) :]


def norm_parts(values):
    average = jnp.mean(values, axis=-1, keepdims=True)
    centred = values - average
    scale = lax.rsqrt(jnp.mean(centred * centred, axis=-1, keepdims=True) + EPS)
    return centred * scale, scale


def norm_backward(normed, scale, gain, upstream):
    weighted = upstream * gain
    return scale * (
        weighted
        - jnp.mean(weighted, axis=-1, keepdims=True)
        - normed * jnp.mean(weighted * normed, axis=-1, keepdims=True)
    )


def project_kernel(x, gain, shift_, wq, wk, wv, bias, normed, q, k, v, k_t, v_t):
    columns = wq.shape[1]
    rows = (norm_parts(x[...].astype(F32))[0] * gain[...] + shift_[...]).astype(BF16)
    normed[...] = rows
    q[...] = (nn(rows, wq[...]) + bias[:, :columns]).astype(BF16)
    keys = nn(rows, wk[...])
    k[...] = keys.astype(BF16)
    k_t[...] = keys.T.astype(BF16)
    values = nn(rows, wv[...]) + bias[:, columns:]
    v[...] = values.astype(BF16)
    v_t[...] = values.T.astype(BF16)


def project(at, x, first, rows_here, gain, shift_, weight, bias, count, previous):
    width, columns = x.shape[1], weight.shape[1] // 3
    tile = min(256, rows_here)
    steps = rows_here // tile
    whole = lambda shape: pl.BlockSpec(shape, lambda i: (0, 0))
    rows = lambda n: pl.BlockSpec((tile, n), lambda i: (at * steps + i, 0))
    turned = pl.BlockSpec((columns, tile), lambda i: (0, at * steps + i))
    inputs = [
        (x, pl.BlockSpec((tile, width), lambda i: (first * steps + i, 0))),
        (gain, whole((1, width))),
        (shift_, whole((1, width))),
        *[(weight, pl.BlockSpec((width, columns), lambda i, part=part: (0, part))) for part in range(3)],
        (bias, whole((1, 2 * columns))),
    ]
    shape = lambda *dims: jax.ShapeDtypeStruct(dims, BF16)
    shared = [(shape(count, width), rows(width))] + [(shape(count, columns), rows(columns))] * 3
    shared += [(shape(columns, count), turned)] * 2
    return call_on_block(
        project_kernel, (steps,), inputs, [], shared, previous, [],
        cost(6 * rows_here * width * columns, 4 * rows_here * width + 6 * width * columns + 10 * rows_here * columns),
    )[1]


def rows_of(block, piece):
    return pl.ds(pl.multiple_of(block * piece, piece), piece)


def scores_of(key_ref, bias_ref, query, rel, piece, diagonal):
    rows = rows_of(rel, piece)
    scores = nt(key_ref[rows, :], query) * (FACTOR * LOG2E)
    key_bias = bias_ref[rows, :]
    if not diagonal:
        return scores + key_bias
    key_at = lax.broadcasted_iota(jnp.int32, scores.shape, 0)
    query_at = lax.broadcasted_iota(jnp.int32, scores.shape, 1)
    allowed = ((key_at < query_at) & (key_bias > -1.0)) | (key_at == query_at)
    return jnp.where(allowed, scores, NEG)


def attend_kernel(at, rank_ref, query_ref, key_ref, value_t, bias_ref, proj_ref, part_ref, attended, lse_ref, score_ref, sum_ref):
    piece = query_ref.shape[0]
    rank = rank_ref[0]
    head = pl.program_id(0)
    true = lax.bitwise_xor(at, rank)
    query = query_ref[...]

    def first(block, top):
        scores = scores_of(key_ref, bias_ref, query, lax.bitwise_xor(block, rank), piece, False)
        score_ref[rows_of(block, piece), :] = scores
        return jnp.maximum(top, jnp.max(scores, axis=0, keepdims=True))

    last = scores_of(key_ref, bias_ref, query, at, piece, True)
    top = lax.fori_loop(0, true, first, jnp.max(last, axis=0, keepdims=True))

    def weigh(scores, rel):
        weights = jnp.exp2(scores - top)
        return jnp.sum(weights, axis=0, keepdims=True), nn(value_t[:, rows_of(rel, piece)], weights.astype(BF16))

    def second(block, carry):
        total, out = carry
        more, part = weigh(score_ref[rows_of(block, piece), :], lax.bitwise_xor(block, rank))
        return total + more, out + part

    total, out = lax.fori_loop(0, true, second, weigh(last, at))
    result = (out / total).T.astype(BF16)
    attended[...] = result
    lse_ref[0] = top + jnp.log2(total)
    term = nn(result, proj_ref[...])

    @pl.when(head == 0)
    def _():
        sum_ref[...] = term

    @pl.when(head > 0)
    def _():
        sum_ref[...] += term

    @pl.when(head == pl.num_programs(0) - 1)
    def _():
        part_ref[...] = sum_ref[...].astype(BF16)


def attend(at, rank, q, k, v_t, key_bias, proj, piece, previous):
    length, columns = q.shape
    heads, width = columns // HEAD_DIM, proj.shape[1]
    inputs = [
        (q, pl.BlockSpec((piece, HEAD_DIM), lambda h, r: (at, h))),
        (k, pl.BlockSpec((length, HEAD_DIM), lambda h, r: (0, h))),
        (v_t, pl.BlockSpec((HEAD_DIM, length), lambda h, r: (h, 0))),
        (key_bias, pl.BlockSpec((length, 1), lambda h, r: (0, 0))),
        (proj, pl.BlockSpec((HEAD_DIM, width), lambda h, r: (h, 0))),
    ]
    fresh = [(jax.ShapeDtypeStruct((piece, width), BF16), pl.BlockSpec((piece, width), lambda h, r: (0, 0)))]
    shared = [
        (jax.ShapeDtypeStruct((length, columns), BF16), pl.BlockSpec((piece, HEAD_DIM), lambda h, r: (at, h))),
        (jax.ShapeDtypeStruct((heads, 1, length), F32), pl.BlockSpec((1, 1, piece), lambda h, r: (h, 0, at))),
    ]
    scratch = [pltpu.VMEM((length, piece), F32), pltpu.VMEM((piece, width), F32)]
    (part,), shared = call_on_block(
        functools.partial(attend_kernel, at), (heads,), inputs, fresh, shared, previous, scratch,
        cost(
            2 * length * piece * columns * 1.3 + 2 * piece * columns * width, 6 * length * columns + 2 * width * columns,
            heads * length * piece * 0.6,
        ), rank,
    )
    return part, shared


def feed_kernel(normed, cot, fc, bias, down, part, active_out, hidden_out, normed_out, cot_out, sum_ref):
    step = pl.program_id(0)
    weights = fc[...]
    hidden = nn(normed[...], weights) + bias[...]
    grad_active = nt(cot[...], down[...])
    inner = math.sqrt(2 / math.pi) * (hidden + 0.044715 * (hidden * hidden * hidden))
    bent = jnp.tanh(inner)
    half = 0.5 * (1.0 + bent)
    active_out[...] = (hidden * half).astype(BF16)
    slope = half + (0.5 * hidden) * (1.0 - bent * bent) * (
        math.sqrt(2 / math.pi) * (1.0 + (3 * 0.044715) * (hidden * hidden))
    )
    grad_hidden = (grad_active * slope).astype(BF16)
    hidden_out[...] = grad_hidden
    term = nt(grad_hidden, weights)

    @pl.when(step == 0)
    def _():
        sum_ref[...] = term
        normed_out[...] = normed[...]
        cot_out[...] = cot[...]

    @pl.when(step > 0)
    def _():
        sum_ref[...] += term

    @pl.when(step == pl.num_programs(0) - 1)
    def _():
        part[...] = sum_ref[...].astype(BF16)


def feed(at, normed, cot, fc, bias, down, count, previous):
    piece, width = normed.shape
    inner = fc.shape[1]
    tile = min(512, inner)
    length = piece * count
    rows = pl.BlockSpec((piece, width), lambda j: (0, 0))
    inputs = [
        (normed, rows),
        (cot, rows),
        (fc, pl.BlockSpec((width, tile), lambda j: (0, j))),
        (bias, pl.BlockSpec((1, tile), lambda j: (0, j))),
        (down, pl.BlockSpec((tile, width), lambda j: (j, 0))),
    ]
    shape = lambda n: jax.ShapeDtypeStruct((length, n), BF16)
    columns = pl.BlockSpec((piece, tile), lambda j: (at, j))
    here = pl.BlockSpec((piece, width), lambda j: (at, 0))
    fresh = [(jax.ShapeDtypeStruct((piece, width), BF16), rows)]
    shared = [(shape(inner), columns), (shape(inner), columns), (shape(width), here), (shape(width), here)]
    (part,), shared = call_on_block(
        feed_kernel, (inner // tile,), inputs, fresh, shared, previous, [pltpu.VMEM((piece, width), F32)],
        cost(6 * piece * width * inner, 4 * width * inner + 10 * piece * width + 4 * piece * inner, piece * inner),
    )
    return part, shared


def retreat_kernel(
    at, first_call, last_call, rank_ref, low_ref, proj_ref, query_ref, lse_ref, key_ref, value_ref, key_t, bias_ref, *rest
):
    rest = list(rest)
    key_in, value_in = (None, None) if first_call else (rest.pop(0), rest.pop(0))
    key_out, value_out, query_out, low_out, prob_ref, chance_ref, key_sum, value_sum = rest
    piece = query_ref.shape[0]
    rank = rank_ref[0]
    true = lax.bitwise_xor(at, rank)

    @pl.when(pl.program_id(0) == 0)
    def _():
        low_out[...] = low_ref[...]

    if first_call:
        key_sum[...] = jnp.zeros_like(key_sum)
        value_sum[...] = jnp.zeros_like(value_sum)
    else:
        key_sum[...] = key_in[...]
        value_sum[...] = value_in[...]
    query, lse = query_ref[...], lse_ref[0]
    grad = nt(low_ref[...], proj_ref[...]).astype(BF16)

    def measure(scores, rel):
        rows = rows_of(rel, piece)
        probs = jnp.exp2(scores - lse)
        grad_chances = nt(value_ref[rows, :], grad)
        value_sum[rows, :] += nn(probs.astype(BF16), grad)
        prob_ref[rows, :] = probs
        chance_ref[rows, :] = grad_chances
        return jnp.sum(probs * grad_chances, axis=0, keepdims=True)

    def first(block, weighted):
        rel = lax.bitwise_xor(block, rank)
        return weighted + measure(scores_of(key_ref, bias_ref, query, rel, piece, False), rel)

    last = scores_of(key_ref, bias_ref, query, at, piece, True)
    weighted = lax.fori_loop(0, true, first, measure(last, at))

    def second(block, total):
        rows = rows_of(lax.bitwise_xor(block, rank), piece)
        grad_scores = (prob_ref[rows, :] * (chance_ref[rows, :] - weighted)).astype(BF16)
        key_sum[rows, :] += nn(grad_scores, query)
        return total + nn(key_t[:, rows], grad_scores)

    total = lax.fori_loop(0, true + 1, second, jnp.zeros((HEAD_DIM, piece), F32))
    query_out[...] = (total * FACTOR).T.astype(BF16)
    if last_call:
        key_out[...] = (key_sum[...] * FACTOR).astype(BF16)
        value_out[...] = value_sum[...].astype(BF16)
    else:
        key_out[...] = key_sum[...]
        value_out[...] = value_sum[...]


def retreat(at, rank, low, proj, q, lse, k, v, k_t, key_bias, sums, previous, last_call):
    length, columns = q.shape
    piece, width = low.shape
    heads = columns // HEAD_DIM
    tall = pl.BlockSpec((length, HEAD_DIM), lambda h, r: (0, h))
    part = pl.BlockSpec((piece, HEAD_DIM), lambda h, r: (at, h))
    inputs = [
        (low, pl.BlockSpec((piece, width), lambda h, r: (0, 0))),
        (proj, pl.BlockSpec((HEAD_DIM, width), lambda h, r: (h, 0))),
        (q, part),
        (lse, pl.BlockSpec((1, 1, piece), lambda h, r: (h, 0, at))),
        (k, tall),
        (v, tall),
        (k_t, pl.BlockSpec((HEAD_DIM, length), lambda h, r: (h, 0))),
        (key_bias, pl.BlockSpec((length, 1), lambda h, r: (0, 0))),
    ]
    if sums is not None:
        inputs += [(item, tall) for item in sums]
    kind = BF16 if last_call else F32
    fresh = [(jax.ShapeDtypeStruct((length, columns), kind), tall)] * 2
    shared = [
        (jax.ShapeDtypeStruct((length, columns), BF16), part),
        (jax.ShapeDtypeStruct((length, width), BF16), pl.BlockSpec((piece, width), lambda h, r: (at, 0))),
    ]
    scratch = [pltpu.VMEM((length, piece), F32)] * 2 + [pltpu.VMEM((length, HEAD_DIM), F32)] * 2
    return call_on_block(
        functools.partial(retreat_kernel, at, sums is None, last_call), (heads,), inputs, fresh, shared, previous,
        scratch,
        cost(
            5 * 1.3 * length * piece * columns + 2 * piece * columns * width, 20 * length * columns,
            heads * length * piece * 0.6,
        ), rank,
    )


def back_kernel(grads, weight, out):
    out[...] = nt(grads[...], weight[...]).astype(BF16)


def back(at, grads, weight, piece):
    columns, width = grads.shape[1], weight.shape[0]
    tile = min(512, width)
    return pl.pallas_call(
        back_kernel,
        grid=(width // tile,),
        in_specs=[
            pl.BlockSpec((piece, columns), lambda j: (at, 0)),
            pl.BlockSpec((tile, columns), lambda j: (j, 0)),
        ],
        out_specs=pl.BlockSpec((piece, tile), lambda j: (0, j)),
        out_shape=jax.ShapeDtypeStruct((piece, width), BF16),
        compiler_params=params(),
        cost_estimate=cost(2 * piece * width * columns, 2 * width * columns + 2 * piece * (columns + width)),
    )(grads, weight)


def part_specs(parts, tile, steps, width):
    arrays, specs = [], []
    for part in parts:
        if isinstance(part, tuple):
            middle = steps // 2
            arrays += list(part)
            specs.append(pl.BlockSpec((tile, width), lambda i: (jnp.minimum(i, middle - 1), 0)))
            specs.append(pl.BlockSpec((tile, width), lambda i: (jnp.maximum(i - middle, 0), 0)))
        else:
            arrays.append(part)
            specs.append(pl.BlockSpec((tile, width), lambda i: (i, 0)))
    return arrays, specs


def add_parts(kinds, refs):
    total = None
    upper = pl.program_id(0) < pl.num_programs(0) // 2
    for kind in kinds:
        if kind:
            high, low = refs.pop(0)[...], refs.pop(0)[...]
            term = jnp.where(upper, high.astype(F32), low.astype(F32))
        else:
            term = refs.pop(0)[...].astype(F32)
        total = term if total is None else total + term
    return total


def rowwise(kernel, parts, rows, vectors, outputs, sums):
    count, width = rows[0].shape
    tile = min(128, count // 2)
    steps = count // tile
    arrays, specs = part_specs(parts, tile, steps, width)
    kinds = [isinstance(part, tuple) for part in parts]
    specs += [pl.BlockSpec((tile, width), lambda i: (i, 0))] * len(rows)
    specs += [pl.BlockSpec((1, width), lambda i: (0, 0))] * len(vectors)

    def body(*refs):
        refs = list(refs)
        total = add_parts(kinds, refs)
        tiles = [refs.pop(0)[...] for _ in rows]
        given = [refs.pop(0)[...] for _ in vectors]
        results = kernel(total, tiles, given)
        for result, _ in zip(results, outputs):
            refs.pop(0)[...] = result
        for result in results[len(outputs) :]:
            ref = refs.pop(0)
            column = jnp.sum(result, axis=0, keepdims=True)

            @pl.when(pl.program_id(0) == 0)
            def _():
                ref[...] = column

            @pl.when(pl.program_id(0) > 0)
            def _():
                ref[...] += column

    return pl.pallas_call(
        body,
        grid=(steps,),
        in_specs=specs,
        out_specs=[pl.BlockSpec((tile, width), lambda i: (i, 0))] * len(outputs)
        + [pl.BlockSpec((1, width), lambda i: (0, 0))] * sums,
        out_shape=[jax.ShapeDtypeStruct((count, width), kind) for kind in outputs]
        + [jax.ShapeDtypeStruct((1, width), F32)] * sums,
        compiler_params=params(),
        cost_estimate=cost(20 * count * width, count * width * (2 * len(arrays) + 4 * len(rows) + 4 * len(outputs))),
    )(*arrays, *rows, *vectors)


def middle_kernel(total, rows, vectors):
    (tokens,), (bias, gain, shift_) = rows, vectors
    middle = tokens.astype(F32) + (total + bias)
    return middle, (norm_parts(middle)[0] * gain + shift_).astype(BF16)


def out_kernel(total, rows, vectors):
    return (((rows[0] + (total + vectors[0])).astype(BF16)),)


def middle_back_kernel(total, rows, vectors):
    (middle, cot), (gain,) = rows, vectors
    normed, scale = norm_parts(middle)
    cot = cot.astype(F32)
    grad = cot + norm_backward(normed, scale, gain, total)
    low = grad.astype(BF16)
    return grad, low, total * normed, total, low.astype(F32), cot


def tokens_back_kernel(total, rows, vectors):
    (tokens, grad_middle), (gain,) = rows, vectors
    normed, scale = norm_parts(tokens.astype(F32))
    return grad_middle + norm_backward(normed, scale, gain, total), total * normed, total


def lay_out(rank, blocks, width, places):
    rows = blocks[0][0].shape[0]
    count, each = len(blocks), len(blocks[0])
    unit = places[1]

    def body(rank_ref, *refs):
        out = refs[-1]
        for k in range(count):
            source = lax.bitwise_xor(k, rank_ref[0])
            for array, column, target in places[0](source):
                out[:, pl.ds(pl.multiple_of(target * unit, unit), unit)] = refs[k * each + array][
                    :, column * unit : (column + 1) * unit
                ].astype(F32)

    arrays = [item for block in blocks for item in block]
    return pl.pallas_call(
        body,
        grid_spec=pltpu.PrefetchScalarGridSpec(
            num_scalar_prefetch=1,
            grid=(1,),
            in_specs=[pl.BlockSpec(item.shape, lambda i, r: (0, 0)) for item in arrays],
            out_specs=pl.BlockSpec((rows, width), lambda i, r: (0, 0)),
        ),
        out_shape=jax.ShapeDtypeStruct((rows, width), F32),
        compiler_params=params(),
        cost_estimate=cost(rows * width, 6 * rows * width),
    )(rank, *arrays)


def neighbours():
    rank = lax.axis_index("seq")
    return rank + 1 - 2 * lax.rem(rank, 2), rank + 2 - 4 * lax.rem(lax.div(rank, 2), 2)


def remote(source, target, send, receive, axis, device):
    return pltpu.make_async_remote_copy(
        src_ref=source, dst_ref=target, send_sem=send, recv_sem=receive, device_id={axis: device}, device_id_type=MESH
    )


def greet(axis, device):
    pl.semaphore_signal(pltpu.get_barrier_semaphore(), inc=1, device_id={axis: device}, device_id_type=MESH)


def opening_kernel(
    tokens, qkv_pieces, fc_pieces, small, token_all, qkv_full, fc_rows, small_full,
    qkv_rows, small_rows, local, send, receive, up_send, up_receive, down_send, down_receive, mate_send, mate_receive,
):
    piece = tokens.shape[0]
    half = piece // 2
    me, place = lax.axis_index("seq"), lax.axis_index("dp")
    one, two = neighbours()
    three = 3 - me
    stages = lax.axis_size("dp") // 2
    level, core = lax.div(place, 2), lax.rem(place, 2)
    mate = place + 1 - 2 * core
    above, below = level < stages - 1, level > 0

    for device in (one, two, three):
        greet("seq", device)
    greet("dp", mate)
    pl.when(above)(lambda: greet("dp", place + 2))
    pl.when(below)(lambda: greet("dp", place - 2))
    pl.semaphore_wait(pltpu.get_barrier_semaphore(), 4 + above.astype(jnp.int32) + below.astype(jnp.int32))

    def block(ref, at, start=0, size=piece):
        return ref.at[pl.ds(at * piece + start, size)]

    def spread(pieces, target, at):
        rows = target.shape[0] // 4
        mine = target.at[pl.ds(me * rows, rows)]
        source = lambda device: pieces if pieces is small else pieces.at[device]
        copies = [
            remote(source(device), mine, send.at[at + i], receive.at[at + i], "seq", device)
            for i, device in enumerate((one, two, three))
        ]
        return copies, source(me), mine

    qkv_copies, qkv_own, qkv_mine = spread(qkv_pieces, qkv_rows, 0)
    small_copies, small_own, small_mine = spread(small, small_rows, 3)
    fc_copies, fc_own, fc_mine = spread(fc_pieces, fc_rows, 6)
    token_one = remote(tokens, block(token_all, 1), send.at[9], receive.at[9], "seq", one)
    token_two = remote(tokens, block(token_all, 2), send.at[10], receive.at[10], "seq", two)
    token_three = (
        remote(block(token_all, 1, 0, half), block(token_all, 3, 0, half), send.at[11], receive.at[11], "seq", two),
        remote(block(token_all, 2, half, half), block(token_all, 3, half, half), send.at[12], receive.at[12], "seq", one),
    )
    first_kept = [pltpu.make_async_copy(qkv_own, qkv_mine, local.at[0]), pltpu.make_async_copy(small_own, small_mine, local.at[1])]
    later_kept = [pltpu.make_async_copy(fc_own, fc_mine, local.at[2]), pltpu.make_async_copy(tokens, block(token_all, 0), local.at[3])]

    chains = ((qkv_rows, qkv_full), (small_rows, small_full))

    def shard(array, at):
        rows = chains[array][0].shape[0]
        return chains[array][1].at[pl.ds((2 * at + core) * rows, rows)]

    def rising(array, step, device):
        at = level - (step - 1)
        source = chains[array][0] if step == 1 else shard(array, at)
        return remote(source, shard(array, at), up_send.at[array, step - 1], up_receive.at[array, step - 1], "dp", device)

    def falling(array, step, device):
        at = level + (step - 1)
        source = chains[array][0] if step == 1 else shard(array, at)
        return remote(source, shard(array, at), down_send.at[array, step - 1], down_receive.at[array, step - 1], "dp", device)

    def across(array, index, at):
        source = chains[array][0] if index == 0 else shard(array, at)
        return remote(source, shard(array, at), mate_send.at[array, index], mate_receive.at[array, index], "dp", mate)

    rises = lambda step: above & (level >= step - 1)
    falls = lambda step: below & (level <= stages - step)
    from_below = lambda step: level >= step
    from_above = lambda step: level + step <= stages - 1

    def relay(step):
        @pl.when(rises(step))
        def _():
            for array in (1, 0):
                rising(array, step, place + 2).start()

        @pl.when(falls(step))
        def _():
            for array in (1, 0):
                falling(array, step, place - 2).start()

    def take(step):
        @pl.when(from_below(step))
        def _():
            for array in (1, 0):
                got = shard(array, level - step)
                remote(got, got, up_send.at[array, step - 1], up_receive.at[array, step - 1], "dp", mate).wait_recv()
                across(array, step, level - step).start()

        @pl.when(from_above(step))
        def _():
            for array in (1, 0):
                got = shard(array, level + step)
                remote(got, got, down_send.at[array, step - 1], down_receive.at[array, step - 1], "dp", mate).wait_recv()
                across(array, stages - 1 + step, level + step).start()

    for copy in qkv_copies + small_copies + first_kept:
        copy.start()
    token_one.start()
    token_two.start()
    for copy in qkv_copies + small_copies:
        copy.wait_recv()
    for copy in first_kept:
        copy.wait()
    relay(1)
    own_full = [pltpu.make_async_copy(chains[array][0], shard(array, level), local.at[4 + array]) for array in range(2)]
    for array in range(2):
        across(array, 0, level).start()
        own_full[array].start()
    for copy in fc_copies + later_kept:
        copy.start()
    take(1)
    relay(2)
    take(2)
    relay(3)
    token_one.wait_recv()
    token_two.wait_recv()
    for copy in token_three:
        copy.start()
    take(3)
    for copy in later_kept + own_full:
        copy.wait()
    for copy in fc_copies:
        copy.wait_recv()
    for copy in qkv_copies + small_copies + fc_copies:
        copy.wait_send()
    token_one.wait_send()
    token_two.wait_send()
    for step in range(1, stages):

        @pl.when(rises(step))
        def _(step=step):
            for array in range(2):
                rising(array, step, place + 2).wait_send()

        @pl.when(falls(step))
        def _(step=step):
            for array in range(2):
                falling(array, step, place - 2).wait_send()

        @pl.when(from_below(step))
        def _(step=step):
            for array in range(2):
                across(array, step, level - step).wait()

        @pl.when(from_above(step))
        def _(step=step):
            for array in range(2):
                across(array, stages - 1 + step, level + step).wait()

    for array in range(2):
        across(array, 0, level).wait()
    for copy in token_three:
        copy.wait()


def opening(tokens, qkv_pieces, fc_pieces, small, dp_count):
    piece, width = tokens.shape
    steps = dp_count // 2 - 1
    anywhere = pl.BlockSpec(memory_space=pl.ANY)
    shape = lambda rows, columns: jax.ShapeDtypeStruct((rows, columns), BF16)
    dma = pltpu.SemaphoreType.DMA
    inside = pl.BlockSpec(memory_space=pltpu.VMEM)
    rows, columns = 4 * qkv_pieces.shape[1], qkv_pieces.shape[2]
    fine = 4 * small.shape[0]
    return pl.pallas_call(
        opening_kernel,
        in_specs=[inside] * 4,
        out_specs=[anywhere] * 4,
        out_shape=[
            shape(4 * piece, width),
            shape(rows * dp_count, columns),
            shape(4 * fc_pieces.shape[1], fc_pieces.shape[2]),
            shape(fine * dp_count, small.shape[1]),
        ],
        scratch_shapes=[
            pltpu.VMEM((rows, columns), BF16), pltpu.VMEM((fine, small.shape[1]), BF16),
            dma((6,)), dma((13,)), dma((13,)), dma((2, steps)), dma((2, steps)), dma((2, steps)), dma((2, steps)),
            dma((2, 2 * steps + 1)), dma((2, 2 * steps + 1)),
        ],
        compiler_params=pltpu.CompilerParams(collective_id=0, has_side_effects=True, vmem_limit_bytes=32 * 2**20),
        cost_estimate=cost(0, 10 * 4 * piece * width),
    )(tokens, qkv_pieces, fc_pieces, small)


def flip(first, second):
    low = lax.rem(first + second, 2)
    high = lax.rem(lax.div(first, 2) + lax.div(second, 2), 2)
    return 2 * high + low


def attend_plane_kernel(
    q, k, v_t, tokens, cot_one, cot_two, key_bias, proj, vectors,
    middle, normed, attended, lse, cot_three,
    score_ref, joint, terms, passed, joined, arrived, send, receive,
):
    piece, width = tokens.shape
    half = piece // 2
    heads = q.shape[1] // HEAD_DIM
    rank = lax.axis_index("seq")
    one, two = neighbours()
    for device in (one, two):
        greet("seq", device)
    pl.semaphore_wait(pltpu.get_barrier_semaphore(), 2)
    up, lower = pl.ds(0, half), pl.ds(half, half)

    def copy(index, source, target, device):
        return remote(source, target, send.at[index], receive.at[index], "seq", device)

    cot_copies = (copy(0, cot_one.at[up], cot_three.at[up], two), copy(1, cot_two.at[lower], cot_three.at[lower], one))
    across = (copy(2, terms.at[3, up], passed.at[0], one), copy(3, terms.at[3, lower], passed.at[1], two))
    plain_one = copy(4, terms.at[1, up], arrived.at[0, up], one)
    plain_two = copy(5, terms.at[2, lower], arrived.at[1, lower], two)
    joined_one = copy(6, joined.at[0], arrived.at[0, lower], one)
    joined_two = copy(7, joined.at[1], arrived.at[1, up], two)
    for item in cot_copies:
        item.start()

    def body(query_ref, key_ref, value_t, attended_tile, lse_tile):
        group, head = pl.program_id(0), pl.program_id(1)
        at = 3 - group
        true = flip(at, rank)
        query = query_ref[...]

        def first(block, top):
            scores = scores_of(key_ref, key_bias, query, flip(block, rank), piece, False)
            score_ref[rows_of(block, piece), :] = scores
            return jnp.maximum(top, jnp.max(scores, axis=0, keepdims=True))

        last = scores_of(key_ref, key_bias, query, at, piece, True)
        top = lax.fori_loop(0, true, first, jnp.max(last, axis=0, keepdims=True))

        def weigh(scores, rel):
            weights = jnp.exp2(scores - top)
            return jnp.sum(weights, axis=0, keepdims=True), nn(value_t[:, rows_of(rel, piece)], weights.astype(BF16))

        def second(block, carry):
            total, out = carry
            more, part = weigh(score_ref[rows_of(block, piece), :], flip(block, rank))
            return total + more, out + part

        total, out = lax.fori_loop(0, true, second, weigh(last, at))
        result = (out / total).T.astype(BF16)
        attended_tile[...] = result
        lse_tile[0] = top + jnp.log2(total)
        joint[:, pl.ds(pl.multiple_of(head * HEAD_DIM, HEAD_DIM), HEAD_DIM)] = result

        @pl.when(head == heads - 1)
        def _():
            terms[at] = nn(joint[...], proj[...]).astype(BF16)

        @pl.when((head == heads - 1) & (group == 0))
        def _():
            for item in across:
                item.start()

        @pl.when((head == heads - 1) & (group == 1))
        def _():
            plain_two.start()

        @pl.when((head == heads - 1) & (group == 2))
        def _():
            plain_one.start()
            for item in across:
                item.wait_recv()
            joined[0] = (terms[1, half:].astype(F32) + passed[1].astype(F32)).astype(BF16)
            joined[1] = (terms[2, :half].astype(F32) + passed[0].astype(F32)).astype(BF16)
            joined_one.start()
            joined_two.start()

    length = q.shape[0]
    pltpu.emit_pipeline(
        body,
        grid=(4, heads),
        in_specs=[
            pl.BlockSpec((piece, HEAD_DIM), lambda g, h: (3 - g, h)),
            pl.BlockSpec((length, HEAD_DIM), lambda g, h: (0, h)),
            pl.BlockSpec((HEAD_DIM, length), lambda g, h: (h, 0)),
        ],
        out_specs=[
            pl.BlockSpec((piece, HEAD_DIM), lambda g, h: (3 - g, h)),
            pl.BlockSpec((1, 1, piece), lambda g, h: (h, 0, 3 - g)),
        ],
    )(q, k, v_t, attended, lse)

    for item in (plain_one, plain_two, joined_one, joined_two):
        item.wait_recv()
    part = min(128, piece)

    def norm_body(token_tile, middle_tile, normed_tile):
        here = pl.ds(pl.multiple_of(pl.program_id(0) * part, part), part)
        total = terms[0, here, :].astype(F32) + arrived[0, here, :].astype(F32) + arrived[1, here, :].astype(F32)
        values = token_tile[...].astype(F32) + (total + vectors[0:1, :])
        middle_tile[...] = values
        normed_tile[...] = (norm_parts(values)[0] * vectors[1:2, :] + vectors[2:3, :]).astype(BF16)

    line = pl.BlockSpec((part, width), lambda i: (i, 0))
    pltpu.emit_pipeline(norm_body, grid=(piece // part,), in_specs=[line], out_specs=[line] * 2)(tokens, middle, normed)
    for item in cot_copies:
        item.wait()
    for item in (*across, plain_one, plain_two, joined_one, joined_two):
        item.wait_send()


def attend_plane(q, k, v_t, tokens, cots, key_bias, proj, vectors):
    piece, width = tokens.shape
    length, columns = q.shape
    heads, half = columns // HEAD_DIM, piece // 2
    anywhere = pl.BlockSpec(memory_space=pl.ANY)
    inside = pl.BlockSpec(memory_space=pltpu.VMEM)
    shape = lambda *dims: jax.ShapeDtypeStruct(dims, BF16)
    dma = pltpu.SemaphoreType.DMA
    return pl.pallas_call(
        attend_plane_kernel,
        in_specs=[anywhere] * 6 + [inside] * 3,
        out_specs=[anywhere] * 5,
        out_shape=[
            jax.ShapeDtypeStruct((piece, width), F32), shape(piece, width), shape(length, columns),
            jax.ShapeDtypeStruct((heads, 1, length), F32), shape(piece, width),
        ],
        scratch_shapes=[
            pltpu.VMEM((length, piece), F32),
            pltpu.VMEM((piece, columns), BF16),
            pltpu.VMEM((4, piece, width), BF16),
            pltpu.VMEM((2, half, width), BF16),
            pltpu.VMEM((2, half, width), BF16),
            pltpu.VMEM((2, piece, width), BF16),
            dma((8,)), dma((8,)),
        ],
        compiler_params=pltpu.CompilerParams(collective_id=2, has_side_effects=True, vmem_limit_bytes=56 * 2**20),
        cost_estimate=cost(3 * length * length * columns + 2 * length * columns * width, 10 * length * width, heads * length * length // 2),
    )(q, k, v_t, tokens, *cots, key_bias, proj, vectors)


def sum_rows(ref, at, columns, value, first):
    total = jnp.sum(value, axis=0, keepdims=True)

    @pl.when(first)
    def _():
        ref[at : at + 1, columns] = total

    @pl.when(jnp.logical_not(first))
    def _():
        ref[at : at + 1, columns] += total


class LevelScatter:
    def __init__(self, source, mate_in, summed, got, send, receive):
        self.source, self.mate_in, self.summed, self.got = source, mate_in, summed, got
        self.send, self.receive = send, receive
        self.rows = mate_in.shape[0] // 4
        self.place = lax.axis_index("dp")
        self.level, self.core = lax.div(self.place, 2), lax.rem(self.place, 2)
        self.mate = self.place + 1 - 2 * self.core

    def greet(self):
        greet("dp", self.mate)
        count = jnp.int32(1)
        for step in (1, 2):
            up, down = self.level + step <= 3, self.level >= step
            pl.when(up)(lambda step=step: greet("dp", self.place + 2 * step))
            pl.when(down)(lambda step=step: greet("dp", self.place - 2 * step))
            count = count + up.astype(jnp.int32) + down.astype(jnp.int32)
        return count

    def block(self, ref, at):
        return ref.at[pl.ds(at * self.rows, self.rows)]

    def swaps(self):
        return [
            remote(
                self.block(self.source, 2 * at + 1 - self.core), self.block(self.mate_in, at),
                self.send.at[at], self.receive.at[at], "dp", self.mate,
            )
            for at in range(4)
        ]

    def start(self):
        for item in self.swaps():
            item.start()

    def add(self, first, second, out, grid, first_at, second_at, out_at):
        def body(left, right, total):
            total[...] = (left[...].astype(F32) + right[...].astype(F32)).astype(total.dtype)

        spec = lambda at: pl.BlockSpec((self.rows, first.shape[1]), lambda i: (at(i), 0))
        pltpu.emit_pipeline(
            body, grid=(grid,), in_specs=[spec(first_at), spec(second_at)], out_specs=[spec(out_at)]
        )(first, second, out)

    def hop(self, at, slot, index, steps):
        return remote(
            self.block(self.summed, at), self.block(self.got, slot), self.send.at[4 + index], self.receive.at[4 + slot],
            "dp", self.place + 2 * steps,
        )

    def hops(self):
        level = self.level
        return [
            (level == 0, self.hop(3, 3, 0, 1)),
            (level == 3, self.hop(0, 3, 0, -1)),
            (level == 0, self.hop(2, 2, 1, 2)),
            (level == 3, self.hop(1, 2, 1, -2)),
            (level <= 2, self.hop(lax.rem(level + 1, 4), 0, 2, 1)),
            (level >= 1, self.hop(lax.rem(level + 3, 4), 1, 3, -1)),
        ]

    def passes(self):
        return [(self.level == 1, self.hop(3, 2, 1, 2)), (self.level == 2, self.hop(0, 2, 1, -2))]

    def spread(self):
        for item in self.swaps():
            item.wait_recv()
        self.add(
            self.source, self.mate_in, self.summed, 4, lambda i: 2 * i + self.core, lambda i: i, lambda i: i
        )
        for condition, copy in self.hops():
            pl.when(condition)(lambda copy=copy: copy.start())

    def arrive(self, slot):
        here = self.block(self.got, slot)
        remote(here, here, self.send.at[0], self.receive.at[4 + slot], "dp", self.mate).wait_recv()

    def pass_on(self):
        for level, at in ((1, 3), (2, 0)):

            @pl.when(self.level == level)
            def _(at=at):
                self.arrive(3)
                self.add(self.summed, self.got, self.summed, 1, lambda i: at, lambda i: 3, lambda i: at)

        for condition, copy in self.passes():
            pl.when(condition)(lambda copy=copy: copy.start())

    def finish(self, out):
        level = self.level
        pl.when(level >= 1)(lambda: self.arrive(0))
        pl.when(level <= 2)(lambda: self.arrive(1))
        self.arrive(2)
        rows = min(64, self.rows)

        def body(own, mate, below, above, far, total):
            value = own[...].astype(F32) + mate[...].astype(F32) + far[...].astype(F32)
            below_term, above_term = below[...].astype(F32), above[...].astype(F32)
            value = value + jnp.where(level >= 1, below_term, 0.0) + jnp.where(level <= 2, above_term, 0.0)
            total[...] = value.astype(total.dtype)

        steps = self.rows // rows
        spec = lambda at: pl.BlockSpec((rows, out.shape[1]), lambda i: (at * steps + i, 0))
        pltpu.emit_pipeline(
            body,
            grid=(steps,),
            in_specs=[spec(self.place), spec(level), spec(0), spec(1), spec(2)],
            out_specs=[spec(0)],
        )(self.source, self.mate_in, self.got, self.got, self.got, out)

    def close(self):
        for item in self.swaps():
            item.wait_send()
        for condition, copy in self.hops() + self.passes():
            pl.when(condition)(lambda copy=copy: copy.wait_send())


def plane_kernel(
    normed, cot_own, cot_one, cot_two, cot_three, fc, bias, down, middle, gain,
    grad_middle, low_all, sums, hidden_sums, active, hidden_grad, normed_all, cot_all, terms, grad_down, grad_fc,
    mate_in, summed, got, down_share,
    normed_buf, cot_buf, sum_ref, joined, passed, arrived, load, local, send, receive, level_send, level_receive,
):
    piece, width = normed.shape
    half = piece // 2
    inner = fc.shape[1]
    length = normed_all.shape[0]
    tile = min(512, inner)
    last = inner // tile - 1
    one, two = neighbours()
    scatter = LevelScatter(grad_down, mate_in, summed, got, level_send, level_receive)
    for device in (one, two):
        greet("seq", device)
    pl.semaphore_wait(pltpu.get_barrier_semaphore(), 2 + scatter.greet())

    up, lower = pl.ds(0, half), pl.ds(half, half)
    rows = lambda k, start=0, size=piece: pl.ds(k * piece + start, size)

    def copy(index, source, target, device):
        return remote(source, target, send.at[index], receive.at[index], "seq", device)

    normed_one = copy(0, normed, normed_buf.at[1], one)
    normed_two = copy(1, normed, normed_buf.at[2], two)
    normed_three = (
        copy(2, normed_buf.at[1, up], normed_buf.at[3, up], two),
        copy(3, normed_buf.at[2, lower], normed_buf.at[3, lower], one),
    )
    across = (copy(4, cot_buf.at[3, up], passed.at[0], one), copy(5, cot_buf.at[3, lower], passed.at[1], two))
    plain_one = copy(6, cot_buf.at[1, up], arrived.at[0, up], one)
    plain_two = copy(7, cot_buf.at[2, lower], arrived.at[1, lower], two)
    joined_one = copy(8, joined.at[0], arrived.at[0, lower], one)
    joined_two = copy(9, joined.at[1], arrived.at[1, up], two)
    low_one = copy(10, low_all.at[rows(0)], low_all.at[rows(1)], one)
    low_two = copy(11, low_all.at[rows(0)], low_all.at[rows(2)], two)
    low_three = (
        copy(12, low_all.at[rows(1, 0, half)], low_all.at[rows(3, 0, half)], two),
        copy(13, low_all.at[rows(2, half, half)], low_all.at[rows(3, half, half)], one),
    )

    loads = [
        pltpu.make_async_copy(source, cot_buf.at[k], load.at[k])
        for k, source in enumerate((cot_own, cot_one, cot_two, cot_three))
    ]
    own = pltpu.make_async_copy(normed, normed_buf.at[0], load.at[4])
    keeps = [pltpu.make_async_copy(normed_buf.at[k], normed_all.at[rows(k)], local.at[k]) for k in range(4)]
    keeps_cot = [pltpu.make_async_copy(cot_buf.at[k], cot_all.at[rows(k)], local.at[4 + k]) for k in range(4)]

    normed_one.start()
    normed_two.start()
    own.start()
    for item in loads:
        item.start()

    def feed_body(fc_tile, down_tile, active_tile, hidden_tile):
        k, j = pl.program_id(0), pl.program_id(1)

        @pl.when((k == 0) & (j == 0))
        def _():
            own.wait()
            keeps[0].start()
            for item in loads:
                item.wait()
            for item in keeps_cot:
                item.start()

        @pl.when((k == 1) & (j == 0))
        def _():
            normed_one.wait_recv()
            normed_two.wait_recv()
            for item in normed_three:
                item.start()
            keeps[1].start()
            keeps[2].start()

        @pl.when((k == 3) & (j == 0))
        def _():
            for item in normed_three:
                item.wait_recv()
            keeps[3].start()

        weights = fc_tile[...]
        columns = pl.ds(pl.multiple_of(j * tile, tile), tile)
        hidden = nn(normed_buf[k], weights) + bias[:, columns]
        grad_active = nt(cot_buf[k], down_tile[...])
        square = hidden * hidden
        bent = jnp.tanh(math.sqrt(2 / math.pi) * (hidden + 0.044715 * (square * hidden)))
        share = 0.5 * (1.0 + bent)
        active_tile[...] = (hidden * share).astype(BF16)
        slope = share + (0.5 * hidden) * (1.0 - bent * bent) * (
            math.sqrt(2 / math.pi) * (1.0 + (3 * 0.044715) * square)
        )
        grad_hidden = (grad_active * slope).astype(BF16)
        hidden_tile[...] = grad_hidden
        sum_rows(hidden_sums, 0, columns, grad_hidden.astype(F32), k == 0)
        term = nt(grad_hidden, weights)

        @pl.when(j == 0)
        def _():
            sum_ref[...] = term

        @pl.when(j > 0)
        def _():
            sum_ref[...] += term

        @pl.when((j == last) & (k == 0))
        def _():
            for item in keeps_cot:
                item.wait()
            arrived[2] = sum_ref[...].astype(BF16)

        @pl.when((j == last) & (k == 1))
        def _():
            cot_buf[1] = sum_ref[...].astype(BF16)
            plain_one.start()

        @pl.when((j == last) & (k == 2))
        def _():
            cot_buf[2] = sum_ref[...].astype(BF16)
            plain_two.start()

        @pl.when((j == last) & (k == 3))
        def _():
            cot_buf[3] = sum_ref[...].astype(BF16)
            for item in across:
                item.start()

    pltpu.emit_pipeline(
        feed_body,
        grid=(4, inner // tile),
        in_specs=[
            pl.BlockSpec((width, tile), lambda k, j: (0, j)),
            pl.BlockSpec((tile, width), lambda k, j: (j, 0)),
        ],
        out_specs=[pl.BlockSpec((piece, tile), lambda k, j: (k, j))] * 2,
    )(fc, down, active, hidden_grad)

    narrow = min(512, width)

    def down_body(active_rows, down_columns, out):
        out[...] = nn(active_rows[...], down_columns[...]).astype(BF16)

    def multiply_down(start):
        pltpu.emit_pipeline(
            down_body,
            grid=(2, width // narrow),
            in_specs=[
                pl.BlockSpec((piece, inner), lambda k, j: (start + k, 0)),
                pl.BlockSpec((inner, narrow), lambda k, j: (0, j)),
            ],
            out_specs=[pl.BlockSpec((piece, narrow), lambda k, j: (start + k, j))],
        )(active, down, terms)

    wide, tall = min(1024, width), min(1024, inner)

    def outer_body(left, right, out):
        out[...] = tn(left[...], right[...]).astype(BF16)

    def outer(left, right, out, shape):
        pltpu.emit_pipeline(
            outer_body,
            grid=(out.shape[0] // shape[0], out.shape[1] // shape[1]),
            in_specs=[
                pl.BlockSpec((length, shape[0]), lambda i, j: (0, i)),
                pl.BlockSpec((length, shape[1]), lambda i, j: (0, j)),
            ],
            out_specs=[pl.BlockSpec(shape, lambda i, j: (i, j))],
        )(left, right, out)

    outer(active, cot_all, grad_down, (tall, wide))
    scatter.start()
    for item in across:
        item.wait_recv()
    joined[0] = (cot_buf[1, half:].astype(F32) + passed[1].astype(F32)).astype(BF16)
    joined[1] = (cot_buf[2, :half].astype(F32) + passed[0].astype(F32)).astype(BF16)
    joined_one.start()
    joined_two.start()
    for item in keeps:
        item.wait()
    multiply_down(0)
    scatter.spread()
    for item in (plain_one, plain_two, joined_one, joined_two):
        item.wait_recv()

    part = min(128, piece)

    def norm_body(middle_tile, cot_tile, grad_tile, low_tile):
        i = pl.program_id(0)
        here = pl.ds(pl.multiple_of(i * part, part), part)
        upstream = (
            arrived[2, here, :].astype(F32) + arrived[0, here, :].astype(F32) + arrived[1, here, :].astype(F32)
        )
        unit, scale = norm_parts(middle_tile[...])
        cot = cot_tile[...].astype(F32)
        grad = cot + norm_backward(unit, scale, gain[...], upstream)
        rounded = grad.astype(BF16)
        grad_tile[...] = grad
        low_tile[...] = rounded
        for at, item in enumerate((upstream * unit, upstream, rounded.astype(F32), cot)):
            sum_rows(sums, at, slice(None), item, i == 0)

    line = pl.BlockSpec((part, width), lambda i: (i, 0))
    pltpu.emit_pipeline(norm_body, grid=(piece // part,), in_specs=[line] * 2, out_specs=[line] * 2)(
        middle, cot_own, grad_middle, low_all
    )
    low_one.start()
    low_two.start()

    multiply_down(2)
    scatter.pass_on()
    outer(normed_all, hidden_grad, grad_fc, (wide, tall))
    low_one.wait_recv()
    low_two.wait_recv()
    for item in low_three:
        item.start()
    scatter.finish(down_share)
    scatter.close()
    for item in low_three:
        item.wait()
    for item in (
        normed_one, normed_two, *normed_three, *across, plain_one, plain_two, joined_one, joined_two, low_one, low_two
    ):
        item.wait_send()


def feed_plane(normed, cots, fc, bias, down, middle, gain):
    piece, width = normed.shape
    inner = fc.shape[1]
    length, half = 4 * piece, piece // 2
    anywhere = pl.BlockSpec(memory_space=pl.ANY)
    inside = pl.BlockSpec(memory_space=pltpu.VMEM)
    shape = lambda rows, columns, kind=BF16: jax.ShapeDtypeStruct((rows, columns), kind)
    dma = pltpu.SemaphoreType.DMA
    return pl.pallas_call(
        plane_kernel,
        in_specs=[anywhere] * 6 + [inside, anywhere, anywhere, inside],
        out_specs=[anywhere, anywhere, inside, inside] + [anywhere] * 11,
        out_shape=[
            shape(piece, width, F32), shape(length, width), shape(4, width, F32), shape(1, inner, F32),
            shape(length, inner), shape(length, inner), shape(length, width), shape(length, width),
            shape(length, width), shape(inner, width), shape(width, inner),
            shape(inner // 2, width), shape(inner // 2, width), shape(inner // 2, width), shape(inner // 8, width, F32),
        ],
        scratch_shapes=[
            pltpu.VMEM((4, piece, width), BF16),
            pltpu.VMEM((4, piece, width), BF16),
            pltpu.VMEM((piece, width), F32),
            pltpu.VMEM((2, half, width), BF16),
            pltpu.VMEM((2, half, width), BF16),
            pltpu.VMEM((3, piece, width), BF16),
            dma((5,)), dma((8,)), dma((14,)), dma((14,)), dma((8,)), dma((8,)),
        ],
        compiler_params=pltpu.CompilerParams(collective_id=1, has_side_effects=True, vmem_limit_bytes=60 * 2**20),
        cost_estimate=cost(12 * length * width * inner, 10 * length * width),
    )(normed, *cots, fc, bias, down, middle, gain)


def retreat_plane_kernel(
    low_all, q, k, v, k_t, lse, terms, middle, key_bias, proj, down_shift,
    grads, column_sums, block_out,
    prob_ref, chance_ref, grad_ref, key_sum, value_sum, rounded, own, passed, joined, arrived,
    load, local, send, receive,
):
    piece, width = middle.shape
    half = piece // 2
    length, columns = q.shape
    heads = columns // HEAD_DIM
    rank = lax.axis_index("seq")
    one, two = neighbours()
    for device in (one, two):
        greet("seq", device)
    pl.semaphore_wait(pltpu.get_barrier_semaphore(), 2)
    up, lower = pl.ds(0, half), pl.ds(half, half)
    rows = lambda at, start=0, size=piece: pl.ds(at * piece + start, size)

    def copy(index, source, target, device):
        return remote(source, target, send.at[index], receive.at[index], "seq", device)

    across = (
        copy(0, terms.at[rows(3, 0, half)], passed.at[0], one),
        copy(1, terms.at[rows(3, half, half)], passed.at[1], two),
    )
    plain_one = copy(2, terms.at[rows(1, 0, half)], arrived.at[0, up], one)
    plain_two = copy(3, terms.at[rows(2, half, half)], arrived.at[1, lower], two)
    joined_one = copy(4, joined.at[0], arrived.at[0, lower], one)
    joined_two = copy(5, joined.at[1], arrived.at[1, up], two)
    loads = (
        pltpu.make_async_copy(terms.at[rows(1, half, half)], own.at[0], load.at[0]),
        pltpu.make_async_copy(terms.at[rows(2, 0, half)], own.at[1], load.at[1]),
    )
    for item in (*across, plain_one, plain_two, *loads):
        item.start()
    key_sum[...] = jnp.zeros_like(key_sum)
    value_sum[...] = jnp.zeros_like(value_sum)

    def body(low_ref, query_ref, key_ref, value_ref, key_t, lse_ref, query_out):
        at, head = pl.program_id(0), pl.program_id(1)
        true = flip(at, rank)
        here = pl.ds(pl.multiple_of(head * HEAD_DIM, HEAD_DIM), HEAD_DIM)

        @pl.when(head == 0)
        def _():
            grad_ref[...] = nt(low_ref[...], proj[...]).astype(BF16)

        @pl.when((at == 1) & (head == 2))
        def _():
            for item in (*across,):
                item.wait_recv()
            for item in loads:
                item.wait()
            joined[0] = (own[0].astype(F32) + passed[1].astype(F32)).astype(BF16)
            joined[1] = (own[1].astype(F32) + passed[0].astype(F32)).astype(BF16)
            joined_one.start()
            joined_two.start()

        query, grad, base = query_ref[...], grad_ref[:, here], lse_ref[0]

        def measure(scores, rel):
            block = rows_of(rel, piece)
            probs = jnp.exp2(scores - base)
            grad_chances = nt(value_ref[block, :], grad)
            value_sum[block, here] += nn(probs.astype(BF16), grad)
            prob_ref[block, :] = probs
            chance_ref[block, :] = grad_chances
            return jnp.sum(probs * grad_chances, axis=0, keepdims=True)

        def first(block, weighted):
            rel = flip(block, rank)
            return weighted + measure(scores_of(key_ref, key_bias, query, rel, piece, False), rel)

        last = scores_of(key_ref, key_bias, query, at, piece, True)
        weighted = lax.fori_loop(0, true, first, measure(last, at))

        def second(block, total):
            block = rows_of(flip(block, rank), piece)
            grad_scores = (prob_ref[block, :] * (chance_ref[block, :] - weighted)).astype(BF16)
            key_sum[block, here] += nn(grad_scores, query)
            return total + nn(key_t[:, block], grad_scores)

        total = lax.fori_loop(0, true + 1, second, jnp.zeros((HEAD_DIM, piece), F32))
        result = (total * FACTOR).T.astype(BF16)
        query_out[...] = result
        sum_rows(column_sums, 0, here, result.astype(F32), at == 0)

    pltpu.emit_pipeline(
        body,
        grid=(4, heads),
        in_specs=[
            pl.BlockSpec((piece, width), lambda g, h: (g, 0)),
            pl.BlockSpec((piece, HEAD_DIM), lambda g, h: (g, h)),
            pl.BlockSpec((length, HEAD_DIM), lambda g, h: (0, h)),
            pl.BlockSpec((length, HEAD_DIM), lambda g, h: (0, h)),
            pl.BlockSpec((HEAD_DIM, length), lambda g, h: (h, 0)),
            pl.BlockSpec((1, 1, piece), lambda g, h: (h, 0, g)),
        ],
        out_specs=[pl.BlockSpec((piece, HEAD_DIM), lambda g, h: (g, h))],
    )(low_all, q, k, v, k_t, lse, grads)

    rounded[:, :columns] = (key_sum[...] * FACTOR).astype(BF16)
    values = value_sum[...].astype(BF16)
    rounded[:, columns:] = values
    column_sums[1:2, :] = jnp.sum(values.astype(F32), axis=0, keepdims=True)
    keep = pltpu.make_async_copy(rounded, grads.at[:, pl.ds(columns, 2 * columns)], local.at[0])
    keep.start()
    for item in (plain_one, plain_two, joined_one, joined_two):
        item.wait_recv()
    part = min(128, piece)

    def out_body(middle_tile, term_tile, out):
        here = pl.ds(pl.multiple_of(pl.program_id(0) * part, part), part)
        total = term_tile[...].astype(F32) + arrived[0, here, :].astype(F32) + arrived[1, here, :].astype(F32)
        out[...] = (middle_tile[...] + (total + down_shift[...])).astype(BF16)

    line = pl.BlockSpec((part, width), lambda i: (i, 0))
    pltpu.emit_pipeline(out_body, grid=(piece // part,), in_specs=[line] * 2, out_specs=[line])(middle, terms, block_out)
    keep.wait()
    for item in (*across, plain_one, plain_two, joined_one, joined_two):
        item.wait_send()


def retreat_plane(low_all, q, k, v, k_t, lse, terms, middle, key_bias, proj, down_shift):
    piece, width = middle.shape
    length, columns = q.shape
    half = piece // 2
    anywhere = pl.BlockSpec(memory_space=pl.ANY)
    inside = pl.BlockSpec(memory_space=pltpu.VMEM)
    dma = pltpu.SemaphoreType.DMA
    return pl.pallas_call(
        retreat_plane_kernel,
        in_specs=[anywhere] * 8 + [inside] * 3,
        out_specs=[anywhere, inside, anywhere],
        out_shape=[
            jax.ShapeDtypeStruct((length, 3 * columns), BF16),
            jax.ShapeDtypeStruct((2, columns), F32),
            jax.ShapeDtypeStruct((piece, width), BF16),
        ],
        scratch_shapes=[
            pltpu.VMEM((length, piece), F32),
            pltpu.VMEM((length, piece), F32),
            pltpu.VMEM((piece, columns), BF16),
            pltpu.VMEM((length, columns), F32),
            pltpu.VMEM((length, columns), F32),
            pltpu.VMEM((length, 2 * columns), BF16),
            pltpu.VMEM((2, half, width), BF16),
            pltpu.VMEM((2, half, width), BF16),
            pltpu.VMEM((2, half, width), BF16),
            pltpu.VMEM((2, piece, width), BF16),
            dma((2,)), dma((1,)), dma((6,)), dma((6,)),
        ],
        compiler_params=pltpu.CompilerParams(collective_id=3, has_side_effects=True, vmem_limit_bytes=60 * 2**20),
        cost_estimate=cost(8 * length * length * columns + 2 * length * columns * width, 10 * length * width),
    )(low_all, q, k, v, k_t, lse, terms, middle, key_bias, proj, down_shift)


def closing_kernel(
    grads, weight, tokens, grad_middle, gain, tokens_grad, sums,
    terms, passed, joined, arrived, send, receive,
):
    piece, width = tokens.shape
    half = piece // 2
    one, two = neighbours()
    for device in (one, two):
        greet("seq", device)
    pl.semaphore_wait(pltpu.get_barrier_semaphore(), 2)
    up, lower = pl.ds(0, half), pl.ds(half, half)

    def copy(index, source, target, device):
        return remote(source, target, send.at[index], receive.at[index], "seq", device)

    across = (copy(0, terms.at[3, up], passed.at[0], one), copy(1, terms.at[3, lower], passed.at[1], two))
    plain_one = copy(2, terms.at[1, up], arrived.at[0, up], one)
    plain_two = copy(3, terms.at[2, lower], arrived.at[1, lower], two)
    joined_one = copy(4, joined.at[0], arrived.at[0, lower], one)
    joined_two = copy(5, joined.at[1], arrived.at[1, up], two)

    @pl.loop(0, 4)
    def _(step):
        at = 3 - step
        terms[at] = nt(grads[pl.ds(pl.multiple_of(at * piece, piece), piece), :], weight[...]).astype(BF16)

        @pl.when(step == 0)
        def _():
            for item in across:
                item.start()

        @pl.when(step == 1)
        def _():
            plain_two.start()

        @pl.when(step == 2)
        def _():
            plain_one.start()

    for item in across:
        item.wait_recv()
    joined[0] = (terms[1, half:].astype(F32) + passed[1].astype(F32)).astype(BF16)
    joined[1] = (terms[2, :half].astype(F32) + passed[0].astype(F32)).astype(BF16)
    joined_one.start()
    joined_two.start()
    for item in (plain_one, plain_two, joined_one, joined_two):
        item.wait_recv()
    part = min(128, piece)

    def norm_body(token_tile, middle_tile, out):
        i = pl.program_id(0)
        here = pl.ds(pl.multiple_of(i * part, part), part)
        upstream = terms[0, here, :].astype(F32) + arrived[0, here, :].astype(F32) + arrived[1, here, :].astype(F32)
        unit, scale = norm_parts(token_tile[...].astype(F32))
        out[...] = middle_tile[...] + norm_backward(unit, scale, gain[...], upstream)
        for at, item in enumerate((upstream * unit, upstream)):
            sum_rows(sums, at, slice(None), item, i == 0)

    line = pl.BlockSpec((part, width), lambda i: (i, 0))
    pltpu.emit_pipeline(norm_body, grid=(piece // part,), in_specs=[line] * 2, out_specs=[line])(
        tokens, grad_middle, tokens_grad
    )
    for item in (*across, plain_one, plain_two, joined_one, joined_two):
        item.wait_send()


def closing(grads, weight, tokens, grad_middle, gain):
    piece, width = tokens.shape
    half = piece // 2
    anywhere = pl.BlockSpec(memory_space=pl.ANY)
    inside = pl.BlockSpec(memory_space=pltpu.VMEM)
    dma = pltpu.SemaphoreType.DMA
    return pl.pallas_call(
        closing_kernel,
        in_specs=[inside, inside, anywhere, anywhere, inside],
        out_specs=[anywhere, inside],
        out_shape=[jax.ShapeDtypeStruct((piece, width), F32), jax.ShapeDtypeStruct((2, width), F32)],
        scratch_shapes=[
            pltpu.VMEM((4, piece, width), BF16),
            pltpu.VMEM((2, half, width), BF16),
            pltpu.VMEM((2, half, width), BF16),
            pltpu.VMEM((2, piece, width), BF16),
            dma((6,)), dma((6,)),
        ],
        compiler_params=pltpu.CompilerParams(collective_id=4, has_side_effects=True, vmem_limit_bytes=60 * 2**20),
        cost_estimate=cost(8 * piece * width * grads.shape[1], 10 * piece * width),
    )(grads, weight, tokens, grad_middle, gain)


def after(value, *others):
    return lax.optimization_barrier((value, *others))[0]


def shift(value, axis, distance):
    count = lax.axis_size(axis)
    return lax.ppermute(value, axis, [(i, i ^ distance) for i in range(count)])


def gather_blocks(value, axis="seq"):
    return [value] + [shift(value, axis, k) for k in range(1, lax.axis_size(axis))]


def scatter_blocks(blocks, axis="seq"):
    return [blocks[0]] + [shift(blocks[k], axis, k) for k in range(1, lax.axis_size(axis))]


def gather_plane(value):
    if lax.axis_size("seq") != 4:
        return gather_blocks(value)
    half = value.shape[0] // 2
    one, two = shift(value, "seq", 1), shift(value, "seq", 2)
    three = jnp.concatenate([shift(one[:half], "seq", 2), shift(two[half:], "seq", 1)], axis=0)
    return [value, one, two, three]


def scatter_plane(blocks):
    if lax.axis_size("seq") != 4:
        return scatter_blocks(blocks)
    half = blocks[0].shape[0] // 2
    up, low = shift(blocks[3][:half], "seq", 1), shift(blocks[3][half:], "seq", 2)
    one = shift(blocks[1][:half], "seq", 1)
    two = shift(blocks[2][half:], "seq", 2)
    one_low = (blocks[1][half:].astype(F32) + low.astype(F32)).astype(BF16)
    two_up = (blocks[2][:half].astype(F32) + up.astype(F32)).astype(BF16)
    return [blocks[0], (one, shift(one_low, "seq", 1)), (shift(two_up, "seq", 2), two)]


def by_rank(blocks, rank):
    bit = 1
    while bit < len(blocks):
        odd = (rank & bit) != 0
        blocks = [jnp.where(odd, blocks[k ^ bit], blocks[k]) for k in range(len(blocks))]
        bit *= 2
    return blocks


def pick(pieces, at):
    return lax.dynamic_index_in_dim(pieces, at, axis=0, keepdims=False)


def exchange(pieces, rank):
    return scatter_blocks([pick(pieces, rank ^ k) for k in range(pieces.shape[0])])


def small_scatter(pieces, dp_rank, seq_rank):
    total = 0.0
    sent = [lax.dynamic_index_in_dim(pieces, seq_rank ^ k, axis=1, keepdims=False) for k in range(pieces.shape[1])]
    for part in scatter_blocks(sent):
        total = total + part
    sent = [pick(total, dp_rank ^ k) for k in range(pieces.shape[0])]
    total = 0.0
    for part in scatter_blocks(sent, "dp"):
        total = total + part
    return total


def swap_pairs(dp_count, seq_count, sub):
    pairs = []
    for d in range(dp_count):
        for s in range(seq_count):
            source = ((d // sub) * sub + s % sub) * seq_count + (s // sub) * sub + d % sub
            pairs.append((source, d * seq_count + s))
    return pairs


def gather_dp(value):
    return lax.all_gather(value, "dp", axis=0, tiled=True)


def scatter_dp(value):
    return lax.psum_scatter(value, "dp", scatter_dimension=0, tiled=True)


def shards(
    tokens,
    cotangent,
    lengths,
    key_mask,
    attn_gain,
    attn_shift,
    qkv_weight,
    qv_bias,
    proj_weight,
    proj_bias,
    mlp_gain,
    mlp_shift,
    fc_weight,
    fc_bias,
    down_weight,
    down_bias,
):
    _, piece, width = tokens.shape
    dp_count, seq_count = lax.axis_size("dp"), lax.axis_size("seq")
    dp_rank, seq_rank = lax.axis_index("dp"), lax.axis_index("seq")
    own_heads = HEADS // seq_count
    own_width = own_heads * HEAD_DIM
    rows = qkv_weight.shape[0]
    sub = HEAD_DIM // proj_weight.shape[0]
    high = seq_count // sub
    block = down_weight.shape[0]
    rank = jnp.reshape(seq_rank, (1,)).astype(jnp.int32)
    swap = swap_pairs(dp_count, seq_count, sub)
    order = list(range(seq_count - 1, -1, -1))
    if seq_count == 4:
        order = [3, 1, 2, 0]

    in_plane = seq_count == 4 and dp_count == 8
    qkv_pieces = (
        qkv_weight.reshape(rows, 3, own_heads, sub, high, HEAD_DIM)
        .transpose(4, 3, 0, 1, 2, 5)
        .reshape(seq_count, rows, 3 * own_width)
    )
    tokens_own, cot_own = tokens[0], cotangent[0]

    small = (attn_gain, attn_shift, qv_bias, proj_bias, mlp_gain, mlp_shift, fc_bias, down_bias)
    sizes = [item.shape[0] for item in small]
    positions = seq_rank * piece + jnp.arange(piece, dtype=jnp.int32)
    own_flags = ((key_mask[0] == 1) & (positions < lengths[0])).astype(BF16)
    packed = jnp.concatenate(small + (own_flags,))
    fc_pieces = (
        fc_weight.reshape(rows, dp_count, seq_count, block)
        .transpose(2, 0, 1, 3)
        .reshape(seq_count, rows, dp_count * block)
    )
    if in_plane:
        room = -(-packed.shape[0] // 2048) * 2048
        small_rows = jnp.pad(packed, (0, room - packed.shape[0])).reshape(room // 128, 128)
        token_all, qkv_full, fc_rows, small_full = opening(
            tokens_own, qkv_pieces, fc_pieces, small_rows, dp_count
        )
        packed = small_full.reshape(dp_count, seq_count, room)
        flags = lax.dynamic_index_in_dim(packed, dp_rank, axis=0, keepdims=False)
        flags = jnp.concatenate(by_rank([flags[s, sum(sizes) : sum(sizes) + piece] for s in range(seq_count)], seq_rank))
        packed = packed[:, :, : sum(sizes)].astype(F32)
    else:
        qkv_full = gather_dp(jnp.concatenate(by_rank(exchange(qkv_pieces, seq_rank), seq_rank), axis=0))
        blocks = gather_blocks(packed)
        flags = jnp.concatenate([item[-piece:] for item in blocks])
        packed = jnp.stack(by_rank([item[:-piece] for item in blocks], seq_rank))
        packed = jnp.stack(by_rank(gather_blocks(packed, "dp"), dp_rank)).astype(F32)
        fc_rows = jnp.concatenate(by_rank(exchange(fc_pieces, seq_rank), seq_rank), axis=0)
    key_bias = jnp.where(flags > 0, 0.0, NEG).astype(F32)[:, None]
    parts, start = [], 0
    for size in sizes:
        parts.append(packed[:, :, start : start + size])
        start += size
    whole = [part.reshape(1, -1) for part in parts]
    gain_one, shift_one, qv_full, proj_shift, gain_two, shift_two, _, down_shift = whole
    fc_shift = lax.dynamic_index_in_dim(parts[6], seq_rank, axis=1, keepdims=False).reshape(1, -1)
    rank_low, rank_high = seq_rank % sub, seq_rank // sub
    qv_heads = qv_full.reshape(2, own_heads, sub, high, HEAD_DIM)
    qv_own = lax.dynamic_index_in_dim(
        lax.dynamic_index_in_dim(qv_heads, rank_low, axis=2, keepdims=False), rank_high, axis=2, keepdims=False
    )
    qv_own = qv_own.reshape(1, -1)

    length = piece * seq_count
    proj_full = gather_dp(lax.ppermute(proj_weight, BOTH, swap))
    down_full = gather_dp(after(down_weight, fc_rows) if in_plane else down_weight)
    fc_full = gather_dp(fc_rows)
    shared = None
    if in_plane:
        cot_own, token_all = lax.optimization_barrier((cot_own, token_all))
        cots = (shift(cot_own, "seq", 1), shift(cot_own, "seq", 2))
        shared = project(0, token_all, 0, length, gain_one, shift_one, qkv_full, qv_own, length, None)
    else:
        token_blocks = gather_blocks(tokens_own)
        cot_blocks = gather_blocks(after(cot_own, token_blocks[-1]))
        for k in range(seq_count):
            shared = project(k, token_blocks[k], 0, piece, gain_one, shift_one, qkv_full, qv_own, length, shared)
    normed_one, q, keys, values, keys_t, values_t = shared
    if in_plane:
        middle, normed_two, attended, lse, cot_three = attend_plane(
            q, keys, values_t, tokens_own, cots, key_bias, proj_full,
            jnp.concatenate([proj_shift, gain_two, shift_two], axis=0),
        )
    else:
        proj_terms, shared = [None] * seq_count, None
        for k in order:
            proj_terms[k], shared = attend(k, rank, q, keys, values_t, key_bias, proj_full, piece, shared)
        attended, lse = shared
        middle, normed_two = rowwise(
            middle_kernel, scatter_blocks(proj_terms), [tokens_own], [proj_shift, gain_two, shift_two], [F32, BF16], 0
        )

    if in_plane:
        results = feed_plane(normed_two, (cot_own, *cots, cot_three), fc_full, fc_shift, down_full, middle, gain_two)
        grad_middle, low_all, sums_two, hidden_sums, down_terms, grad_fc, grad_down = [
            results[i] for i in (0, 1, 2, 3, 8, 10, 14)
        ]
        sums_two = [sums_two[i] for i in range(4)]
        grad_fc = scatter_dp(grad_fc)
        grads, qv_sums, block_out = retreat_plane(
            low_all, q, keys, values, keys_t, lse, down_terms, middle, key_bias, proj_full, down_shift
        )
    else:
        normed_blocks = gather_blocks(normed_two)
        grad_terms, shared = [], None
        for k in range(seq_count):
            term, shared = feed(k, normed_blocks[k], cot_blocks[k], fc_full, fc_shift, down_full, seq_count, shared)
            grad_terms.append(term)
        active, grad_hidden, normed_all, cot_all = shared
        grad_middle, grad_mid_low, *sums_two = rowwise(
            middle_back_kernel, scatter_blocks(grad_terms), [middle, cot_own], [gain_two], [F32, BF16], 4
        )
        down_terms = [
            nn(active[k * piece : (k + 1) * piece], down_full).astype(BF16) for k in range(seq_count)
        ]
        low_blocks = gather_blocks(grad_mid_low)
        grad_down = scatter_dp(tn(active, cot_all).astype(BF16))
        grad_fc = scatter_dp(tn(normed_all, grad_hidden).astype(BF16))
        hidden_sums = jnp.sum(grad_hidden.astype(F32), axis=0)
        block_out = rowwise(out_kernel, scatter_blocks(down_terms), [middle], [down_shift], [BF16], 0)[0]
        sums, shared = None, None
        for k in range(seq_count):
            sums, shared = retreat(
                k, rank, low_blocks[k], proj_full, q, lse, keys, values, keys_t, key_bias, sums, shared,
                k == seq_count - 1,
            )
        grad_q, low_all = shared
        grads = jnp.concatenate([grad_q, sums[0], sums[1]], axis=1)
        qv_sums = jnp.stack([jnp.sum(item.astype(F32), axis=0) for item in (grad_q, sums[1])])
    grad_proj = tn(attended, low_all).astype(BF16)
    if in_plane:
        normed_one = after(normed_one, grad_fc, grad_proj)
    grad_qkv = scatter_dp(tn(normed_one, grads).astype(BF16))
    grad_proj = scatter_dp(grad_proj)
    grad_proj = lax.ppermute(grad_proj, BOTH, swap).astype(F32)
    if in_plane:
        tokens_grad, sums_one = closing(grads, qkv_full, tokens_own, grad_middle, gain_one)
        sums_one = [sums_one[i] for i in range(2)]
    else:
        back_terms = [None] * seq_count
        for k in order:
            back_terms[k] = back(k, grads, qkv_full, piece)
        tokens_grad, *sums_one = rowwise(
            tokens_back_kernel, scatter_blocks(back_terms), [tokens_own, grad_middle], [gain_one], [F32], 2
        )

    blocks = exchange(grad_fc.reshape(seq_count, rows, dp_count * block), seq_rank)
    if block % 128 == 0:
        fc_places = lambda s: [(0, d, d * seq_count + s) for d in range(dp_count)]
        grad_fc = lay_out(rank, [[item] for item in blocks], fc_weight.shape[1], (fc_places, block))
    else:
        blocks = [item.reshape(rows, dp_count, block) for item in by_rank(blocks, seq_rank)]
        grad_fc = jnp.stack(blocks, axis=2).reshape(fc_weight.shape).astype(F32)
    blocks = [[item] for item in exchange(grad_qkv.reshape(seq_count, rows, 3 * own_width), seq_rank)]
    qkv_places = lambda s: [
        (0, part * own_heads + head, part * HEADS + (head * sub + s % sub) * high + s // sub)
        for part in range(3)
        for head in range(own_heads)
    ]
    grad_qkv_weight = lay_out(rank, blocks, qkv_weight.shape[1], (qkv_places, HEAD_DIM))

    def spread(vector):
        return vector.reshape(dp_count, seq_count, -1)

    here = (jnp.arange(seq_count) == seq_rank).astype(F32)
    hidden_sums = hidden_sums.reshape(dp_count, 1, -1) * here[None, :, None]
    early = jnp.concatenate([spread(item) for item in sums_two] + [hidden_sums], axis=2)
    early = small_scatter(early, dp_rank, seq_rank)
    here = (jnp.arange(sub) == rank_low)[:, None] & (jnp.arange(high) == rank_high)[None, :]
    qv_sums = qv_sums.reshape(2, own_heads, 1, 1, HEAD_DIM) * here.astype(F32)[None, None, :, :, None]
    late = jnp.concatenate([spread(item) for item in sums_one] + [spread(qv_sums)], axis=2)
    late = small_scatter(late, dp_rank, seq_rank)
    share = attn_gain.shape[0]
    return (
        block_out[None],
        tokens_grad[None],
        late[:share],
        late[share : 2 * share],
        grad_qkv_weight,
        late[2 * share :],
        grad_proj,
        early[2 * share : 3 * share],
        early[:share],
        early[share : 2 * share],
        grad_fc,
        early[4 * share :],
        grad_down.astype(F32),
        early[3 * share : 4 * share],
    )


def solution(mesh):
    in_specs = (
        P("dp", "seq", None),
        P("dp", "seq", None),
        P("dp"),
        P("dp", "seq"),
        P(BOTH),
        P(BOTH),
        P(BOTH, None),
        P(BOTH),
        P(BOTH, None),
        P(BOTH),
        P(BOTH),
        P(BOTH),
        P(BOTH, None),
        P(BOTH),
        P(BOTH, None),
        P(BOTH),
    )
    out_specs = (
        P("dp", "seq", None),
        P("dp", "seq", None),
        P(BOTH),
        P(BOTH),
        P(BOTH, None),
        P(BOTH),
        P(BOTH, None),
        P(BOTH),
        P(BOTH),
        P(BOTH),
        P(BOTH, None),
        P(BOTH),
        P(BOTH, None),
        P(BOTH),
    )
    return jax.shard_map(shards, mesh=mesh, in_specs=in_specs, out_specs=out_specs, check_vma=False)
```

```python
import functools
import math

import jax
import jax.numpy as jnp
from jax import lax
from jax.experimental import pallas as pl
from jax.experimental.pallas import tpu as pltpu
from jax.sharding import PartitionSpec as P

HEADS = 16
HEAD_DIM = 128
EPS = 1e-05
NEG = -1e30
FACTOR = HEAD_DIM ** (-0.5)
LOG2E = math.log2(math.e)
F32 = jnp.float32
BF16 = jnp.bfloat16
BOTH = ("dp", "seq")
MESH = pl.DeviceIdType.MESH


def nn(left, right):
    return lax.dot_general(left, right, (((1,), (0,)), ((), ())), preferred_element_type=F32)


def nt(left, right):
    return lax.dot_general(left, right, (((1,), (1,)), ((), ())), preferred_element_type=F32)


def tn(left, right):
    return lax.dot_general(left, right, (((0,), (0,)), ((), ())), preferred_element_type=F32)


def params(limit_mib=56):
    return pltpu.CompilerParams(dimension_semantics=("arbitrary",), vmem_limit_bytes=limit_mib * 2**20)


def cost(flops, moved, exps=0):
    return pl.CostEstimate(flops=int(flops), bytes_accessed=int(moved), transcendentals=int(exps))


def call_on_block(kernel, grid, inputs, fresh, shared, previous, scratch, estimate, rank=None):
    arrays = [item for item, _ in inputs]
    specs = [spec for _, spec in inputs]
    aliases = {}
    lead = 0 if rank is None else 1
    if previous is not None:
        for at, item in enumerate(previous):
            aliases[lead + len(arrays)] = len(fresh) + at
            arrays.append(item)
            specs.append(pl.BlockSpec(memory_space=pl.ANY))
    count = len(inputs)
    skipped = 0 if previous is None else len(previous)

    def body(*refs):
        refs = list(refs)
        kernel(*refs[: lead + count], *refs[lead + count + skipped :])

    out_specs = [spec for _, spec in fresh] + [spec for _, spec in shared]
    out_shape = [shape for shape, _ in fresh] + [shape for shape, _ in shared]
    if rank is None:
        results = pl.pallas_call(
            body, grid=grid, in_specs=specs, out_specs=out_specs, out_shape=out_shape, scratch_shapes=scratch,
            input_output_aliases=aliases, compiler_params=params(), cost_estimate=estimate,
        )(*arrays)
    else:
        results = pl.pallas_call(
            body,
            grid_spec=pltpu.PrefetchScalarGridSpec(
                num_scalar_prefetch=1, grid=grid, in_specs=specs, out_specs=out_specs, scratch_shapes=scratch
            ),
            out_shape=out_shape, input_output_aliases=aliases, compiler_params=params(), cost_estimate=estimate,
        )(rank, *arrays)
    return results[: len(fresh)], results[len(fresh) :]


def norm_parts(values):
    average = jnp.mean(values, axis=-1, keepdims=True)
    centred = values - average
    scale = lax.rsqrt(jnp.mean(centred * centred, axis=-1, keepdims=True) + EPS)
    return centred * scale, scale


def norm_backward(normed, scale, gain, upstream):
    weighted = upstream * gain
    return scale * (
        weighted
        - jnp.mean(weighted, axis=-1, keepdims=True)
        - normed * jnp.mean(weighted * normed, axis=-1, keepdims=True)
    )


def project_kernel(x, gain, shift_, wq, wk, wv, bias, normed, q, k, v, k_t, v_t):
    columns = wq.shape[1]
    rows = (norm_parts(x[...].astype(F32))[0] * gain[...] + shift_[...]).astype(BF16)
    normed[...] = rows
    q[...] = (nn(rows, wq[...]) + bias[:, :columns]).astype(BF16)
    keys = nn(rows, wk[...])
    k[...] = keys.astype(BF16)
    k_t[...] = keys.T.astype(BF16)
    values = nn(rows, wv[...]) + bias[:, columns:]
    v[...] = values.astype(BF16)
    v_t[...] = values.T.astype(BF16)


def project(at, x, first, rows_here, gain, shift_, weight, bias, count, previous):
    width, columns = x.shape[1], weight.shape[1] // 3
    tile = min(256, rows_here)
    steps = rows_here // tile
    whole = lambda shape: pl.BlockSpec(shape, lambda i: (0, 0))
    rows = lambda n: pl.BlockSpec((tile, n), lambda i: (at * steps + i, 0))
    turned = pl.BlockSpec((columns, tile), lambda i: (0, at * steps + i))
    inputs = [
        (x, pl.BlockSpec((tile, width), lambda i: (first * steps + i, 0))),
        (gain, whole((1, width))),
        (shift_, whole((1, width))),
        *[(weight, pl.BlockSpec((width, columns), lambda i, part=part: (0, part))) for part in range(3)],
        (bias, whole((1, 2 * columns))),
    ]
    shape = lambda *dims: jax.ShapeDtypeStruct(dims, BF16)
    shared = [(shape(count, width), rows(width))] + [(shape(count, columns), rows(columns))] * 3
    shared += [(shape(columns, count), turned)] * 2
    return call_on_block(
        project_kernel, (steps,), inputs, [], shared, previous, [],
        cost(6 * rows_here * width * columns, 4 * rows_here * width + 6 * width * columns + 10 * rows_here * columns),
    )[1]


def rows_of(block, piece):
    return pl.ds(pl.multiple_of(block * piece, piece), piece)


def scores_of(key_ref, bias_ref, query, rel, piece, diagonal):
    rows = rows_of(rel, piece)
    scores = nt(key_ref[rows, :], query) * (FACTOR * LOG2E)
    key_bias = bias_ref[rows, :]
    if not diagonal:
        return scores + key_bias
    key_at = lax.broadcasted_iota(jnp.int32, scores.shape, 0)
    query_at = lax.broadcasted_iota(jnp.int32, scores.shape, 1)
    allowed = ((key_at < query_at) & (key_bias > -1.0)) | (key_at == query_at)
    return jnp.where(allowed, scores, NEG)


def attend_kernel(at, rank_ref, query_ref, key_ref, value_t, bias_ref, proj_ref, part_ref, attended, lse_ref, score_ref, sum_ref):
    piece = query_ref.shape[0]
    rank = rank_ref[0]
    head = pl.program_id(0)
    true = lax.bitwise_xor(at, rank)
    query = query_ref[...]

    def first(block, top):
        scores = scores_of(key_ref, bias_ref, query, lax.bitwise_xor(block, rank), piece, False)
        score_ref[rows_of(block, piece), :] = scores
        return jnp.maximum(top, jnp.max(scores, axis=0, keepdims=True))

    last = scores_of(key_ref, bias_ref, query, at, piece, True)
    top = lax.fori_loop(0, true, first, jnp.max(last, axis=0, keepdims=True))

    def weigh(scores, rel):
        weights = jnp.exp2(scores - top)
        return jnp.sum(weights, axis=0, keepdims=True), nn(value_t[:, rows_of(rel, piece)], weights.astype(BF16))

    def second(block, carry):
        total, out = carry
        more, part = weigh(score_ref[rows_of(block, piece), :], lax.bitwise_xor(block, rank))
        return total + more, out + part

    total, out = lax.fori_loop(0, true, second, weigh(last, at))
    result = (out / total).T.astype(BF16)
    attended[...] = result
    lse_ref[0] = top + jnp.log2(total)
    term = nn(result, proj_ref[...])

    @pl.when(head == 0)
    def _():
        sum_ref[...] = term

    @pl.when(head > 0)
    def _():
        sum_ref[...] += term

    @pl.when(head == pl.num_programs(0) - 1)
    def _():
        part_ref[...] = sum_ref[...].astype(BF16)


def attend(at, rank, q, k, v_t, key_bias, proj, piece, previous):
    length, columns = q.shape
    heads, width = columns // HEAD_DIM, proj.shape[1]
    inputs = [
        (q, pl.BlockSpec((piece, HEAD_DIM), lambda h, r: (at, h))),
        (k, pl.BlockSpec((length, HEAD_DIM), lambda h, r: (0, h))),
        (v_t, pl.BlockSpec((HEAD_DIM, length), lambda h, r: (h, 0))),
        (key_bias, pl.BlockSpec((length, 1), lambda h, r: (0, 0))),
        (proj, pl.BlockSpec((HEAD_DIM, width), lambda h, r: (h, 0))),
    ]
    fresh = [(jax.ShapeDtypeStruct((piece, width), BF16), pl.BlockSpec((piece, width), lambda h, r: (0, 0)))]
    shared = [
        (jax.ShapeDtypeStruct((length, columns), BF16), pl.BlockSpec((piece, HEAD_DIM), lambda h, r: (at, h))),
        (jax.ShapeDtypeStruct((heads, 1, length), F32), pl.BlockSpec((1, 1, piece), lambda h, r: (h, 0, at))),
    ]
    scratch = [pltpu.VMEM((length, piece), F32), pltpu.VMEM((piece, width), F32)]
    (part,), shared = call_on_block(
        functools.partial(attend_kernel, at), (heads,), inputs, fresh, shared, previous, scratch,
        cost(
            2 * length * piece * columns * 1.3 + 2 * piece * columns * width, 6 * length * columns + 2 * width * columns,
            heads * length * piece * 0.6,
        ), rank,
    )
    return part, shared


def feed_kernel(normed, cot, fc, bias, down, part, active_out, hidden_out, normed_out, cot_out, sum_ref):
    step = pl.program_id(0)
    weights = fc[...]
    hidden = nn(normed[...], weights) + bias[...]
    grad_active = nt(cot[...], down[...])
    inner = math.sqrt(2 / math.pi) * (hidden + 0.044715 * (hidden * hidden * hidden))
    bent = jnp.tanh(inner)
    half = 0.5 * (1.0 + bent)
    active_out[...] = (hidden * half).astype(BF16)
    slope = half + (0.5 * hidden) * (1.0 - bent * bent) * (
        math.sqrt(2 / math.pi) * (1.0 + (3 * 0.044715) * (hidden * hidden))
    )
    grad_hidden = (grad_active * slope).astype(BF16)
    hidden_out[...] = grad_hidden
    term = nt(grad_hidden, weights)

    @pl.when(step == 0)
    def _():
        sum_ref[...] = term
        normed_out[...] = normed[...]
        cot_out[...] = cot[...]

    @pl.when(step > 0)
    def _():
        sum_ref[...] += term

    @pl.when(step == pl.num_programs(0) - 1)
    def _():
        part[...] = sum_ref[...].astype(BF16)


def feed(at, normed, cot, fc, bias, down, count, previous):
    piece, width = normed.shape
    inner = fc.shape[1]
    tile = min(512, inner)
    length = piece * count
    rows = pl.BlockSpec((piece, width), lambda j: (0, 0))
    inputs = [
        (normed, rows),
        (cot, rows),
        (fc, pl.BlockSpec((width, tile), lambda j: (0, j))),
        (bias, pl.BlockSpec((1, tile), lambda j: (0, j))),
        (down, pl.BlockSpec((tile, width), lambda j: (j, 0))),
    ]
    shape = lambda n: jax.ShapeDtypeStruct((length, n), BF16)
    columns = pl.BlockSpec((piece, tile), lambda j: (at, j))
    here = pl.BlockSpec((piece, width), lambda j: (at, 0))
    fresh = [(jax.ShapeDtypeStruct((piece, width), BF16), rows)]
    shared = [(shape(inner), columns), (shape(inner), columns), (shape(width), here), (shape(width), here)]
    (part,), shared = call_on_block(
        feed_kernel, (inner // tile,), inputs, fresh, shared, previous, [pltpu.VMEM((piece, width), F32)],
        cost(6 * piece * width * inner, 4 * width * inner + 10 * piece * width + 4 * piece * inner, piece * inner),
    )
    return part, shared


def retreat_kernel(
    at, first_call, last_call, rank_ref, low_ref, proj_ref, query_ref, lse_ref, key_ref, value_ref, key_t, bias_ref, *rest
):
    rest = list(rest)
    key_in, value_in = (None, None) if first_call else (rest.pop(0), rest.pop(0))
    key_out, value_out, query_out, low_out, prob_ref, chance_ref, key_sum, value_sum = rest
    piece = query_ref.shape[0]
    rank = rank_ref[0]
    true = lax.bitwise_xor(at, rank)

    @pl.when(pl.program_id(0) == 0)
    def _():
        low_out[...] = low_ref[...]

    if first_call:
        key_sum[...] = jnp.zeros_like(key_sum)
        value_sum[...] = jnp.zeros_like(value_sum)
    else:
        key_sum[...] = key_in[...]
        value_sum[...] = value_in[...]
    query, lse = query_ref[...], lse_ref[0]
    grad = nt(low_ref[...], proj_ref[...]).astype(BF16)

    def measure(scores, rel):
        rows = rows_of(rel, piece)
        probs = jnp.exp2(scores - lse)
        grad_chances = nt(value_ref[rows, :], grad)
        value_sum[rows, :] += nn(probs.astype(BF16), grad)
        prob_ref[rows, :] = probs
        chance_ref[rows, :] = grad_chances
        return jnp.sum(probs * grad_chances, axis=0, keepdims=True)

    def first(block, weighted):
        rel = lax.bitwise_xor(block, rank)
        return weighted + measure(scores_of(key_ref, bias_ref, query, rel, piece, False), rel)

    last = scores_of(key_ref, bias_ref, query, at, piece, True)
    weighted = lax.fori_loop(0, true, first, measure(last, at))

    def second(block, total):
        rows = rows_of(lax.bitwise_xor(block, rank), piece)
        grad_scores = (prob_ref[rows, :] * (chance_ref[rows, :] - weighted)).astype(BF16)
        key_sum[rows, :] += nn(grad_scores, query)
        return total + nn(key_t[:, rows], grad_scores)

    total = lax.fori_loop(0, true + 1, second, jnp.zeros((HEAD_DIM, piece), F32))
    query_out[...] = (total * FACTOR).T.astype(BF16)
    if last_call:
        key_out[...] = (key_sum[...] * FACTOR).astype(BF16)
        value_out[...] = value_sum[...].astype(BF16)
    else:
        key_out[...] = key_sum[...]
        value_out[...] = value_sum[...]


def retreat(at, rank, low, proj, q, lse, k, v, k_t, key_bias, sums, previous, last_call):
    length, columns = q.shape
    piece, width = low.shape
    heads = columns // HEAD_DIM
    tall = pl.BlockSpec((length, HEAD_DIM), lambda h, r: (0, h))
    part = pl.BlockSpec((piece, HEAD_DIM), lambda h, r: (at, h))
    inputs = [
        (low, pl.BlockSpec((piece, width), lambda h, r: (0, 0))),
        (proj, pl.BlockSpec((HEAD_DIM, width), lambda h, r: (h, 0))),
        (q, part),
        (lse, pl.BlockSpec((1, 1, piece), lambda h, r: (h, 0, at))),
        (k, tall),
        (v, tall),
        (k_t, pl.BlockSpec((HEAD_DIM, length), lambda h, r: (h, 0))),
        (key_bias, pl.BlockSpec((length, 1), lambda h, r: (0, 0))),
    ]
    if sums is not None:
        inputs += [(item, tall) for item in sums]
    kind = BF16 if last_call else F32
    fresh = [(jax.ShapeDtypeStruct((length, columns), kind), tall)] * 2
    shared = [
        (jax.ShapeDtypeStruct((length, columns), BF16), part),
        (jax.ShapeDtypeStruct((length, width), BF16), pl.BlockSpec((piece, width), lambda h, r: (at, 0))),
    ]
    scratch = [pltpu.VMEM((length, piece), F32)] * 2 + [pltpu.VMEM((length, HEAD_DIM), F32)] * 2
    return call_on_block(
        functools.partial(retreat_kernel, at, sums is None, last_call), (heads,), inputs, fresh, shared, previous,
        scratch,
        cost(
            5 * 1.3 * length * piece * columns + 2 * piece * columns * width, 20 * length * columns,
            heads * length * piece * 0.6,
        ), rank,
    )


def back_kernel(grads, weight, out):
    out[...] = nt(grads[...], weight[...]).astype(BF16)


def back(at, grads, weight, piece):
    columns, width = grads.shape[1], weight.shape[0]
    tile = min(512, width)
    return pl.pallas_call(
        back_kernel,
        grid=(width // tile,),
        in_specs=[
            pl.BlockSpec((piece, columns), lambda j: (at, 0)),
            pl.BlockSpec((tile, columns), lambda j: (j, 0)),
        ],
        out_specs=pl.BlockSpec((piece, tile), lambda j: (0, j)),
        out_shape=jax.ShapeDtypeStruct((piece, width), BF16),
        compiler_params=params(),
        cost_estimate=cost(2 * piece * width * columns, 2 * width * columns + 2 * piece * (columns + width)),
    )(grads, weight)


def part_specs(parts, tile, steps, width):
    arrays, specs = [], []
    for part in parts:
        if isinstance(part, tuple):
            middle = steps // 2
            arrays += list(part)
            specs.append(pl.BlockSpec((tile, width), lambda i: (jnp.minimum(i, middle - 1), 0)))
            specs.append(pl.BlockSpec((tile, width), lambda i: (jnp.maximum(i - middle, 0), 0)))
        else:
            arrays.append(part)
            specs.append(pl.BlockSpec((tile, width), lambda i: (i, 0)))
    return arrays, specs


def add_parts(kinds, refs):
    total = None
    upper = pl.program_id(0) < pl.num_programs(0) // 2
    for kind in kinds:
        if kind:
            high, low = refs.pop(0)[...], refs.pop(0)[...]
            term = jnp.where(upper, high.astype(F32), low.astype(F32))
        else:
            term = refs.pop(0)[...].astype(F32)
        total = term if total is None else total + term
    return total


def rowwise(kernel, parts, rows, vectors, outputs, sums):
    count, width = rows[0].shape
    tile = min(128, count // 2)
    steps = count // tile
    arrays, specs = part_specs(parts, tile, steps, width)
    kinds = [isinstance(part, tuple) for part in parts]
    specs += [pl.BlockSpec((tile, width), lambda i: (i, 0))] * len(rows)
    specs += [pl.BlockSpec((1, width), lambda i: (0, 0))] * len(vectors)

    def body(*refs):
        refs = list(refs)
        total = add_parts(kinds, refs)
        tiles = [refs.pop(0)[...] for _ in rows]
        given = [refs.pop(0)[...] for _ in vectors]
        results = kernel(total, tiles, given)
        for result, _ in zip(results, outputs):
            refs.pop(0)[...] = result
        for result in results[len(outputs) :]:
            ref = refs.pop(0)
            column = jnp.sum(result, axis=0, keepdims=True)

            @pl.when(pl.program_id(0) == 0)
            def _():
                ref[...] = column

            @pl.when(pl.program_id(0) > 0)
            def _():
                ref[...] += column

    return pl.pallas_call(
        body,
        grid=(steps,),
        in_specs=specs,
        out_specs=[pl.BlockSpec((tile, width), lambda i: (i, 0))] * len(outputs)
        + [pl.BlockSpec((1, width), lambda i: (0, 0))] * sums,
        out_shape=[jax.ShapeDtypeStruct((count, width), kind) for kind in outputs]
        + [jax.ShapeDtypeStruct((1, width), F32)] * sums,
        compiler_params=params(),
        cost_estimate=cost(20 * count * width, count * width * (2 * len(arrays) + 4 * len(rows) + 4 * len(outputs))),
    )(*arrays, *rows, *vectors)


def middle_kernel(total, rows, vectors):
    (tokens,), (bias, gain, shift_) = rows, vectors
    middle = tokens.astype(F32) + (total + bias)
    return middle, (norm_parts(middle)[0] * gain + shift_).astype(BF16)


def out_kernel(total, rows, vectors):
    return (((rows[0] + (total + vectors[0])).astype(BF16)),)


def middle_back_kernel(total, rows, vectors):
    (middle, cot), (gain,) = rows, vectors
    normed, scale = norm_parts(middle)
    cot = cot.astype(F32)
    grad = cot + norm_backward(normed, scale, gain, total)
    low = grad.astype(BF16)
    return grad, low, total * normed, total, low.astype(F32), cot


def tokens_back_kernel(total, rows, vectors):
    (tokens, grad_middle), (gain,) = rows, vectors
    normed, scale = norm_parts(tokens.astype(F32))
    return grad_middle + norm_backward(normed, scale, gain, total), total * normed, total


def lay_out(rank, blocks, width, places):
    rows = blocks[0][0].shape[0]
    count, each = len(blocks), len(blocks[0])
    unit = places[1]

    def body(rank_ref, *refs):
        out = refs[-1]
        for k in range(count):
            source = lax.bitwise_xor(k, rank_ref[0])
            for array, column, target in places[0](source):
                out[:, pl.ds(pl.multiple_of(target * unit, unit), unit)] = refs[k * each + array][
                    :, column * unit : (column + 1) * unit
                ].astype(F32)

    arrays = [item for block in blocks for item in block]
    return pl.pallas_call(
        body,
        grid_spec=pltpu.PrefetchScalarGridSpec(
            num_scalar_prefetch=1,
            grid=(1,),
            in_specs=[pl.BlockSpec(item.shape, lambda i, r: (0, 0)) for item in arrays],
            out_specs=pl.BlockSpec((rows, width), lambda i, r: (0, 0)),
        ),
        out_shape=jax.ShapeDtypeStruct((rows, width), F32),
        compiler_params=params(),
        cost_estimate=cost(rows * width, 6 * rows * width),
    )(rank, *arrays)


def neighbours():
    rank = lax.axis_index("seq")
    return rank + 1 - 2 * lax.rem(rank, 2), rank + 2 - 4 * lax.rem(lax.div(rank, 2), 2)


def remote(source, target, send, receive, axis, device):
    return pltpu.make_async_remote_copy(
        src_ref=source, dst_ref=target, send_sem=send, recv_sem=receive, device_id={axis: device}, device_id_type=MESH
    )


def greet(axis, device):
    pl.semaphore_signal(pltpu.get_barrier_semaphore(), inc=1, device_id={axis: device}, device_id_type=MESH)


def opening_kernel(
    tokens, qkv_pieces, fc_pieces, small, token_all, qkv_full, fc_rows, small_full,
    qkv_rows, small_rows, local, send, receive, up_send, up_receive, down_send, down_receive, mate_send, mate_receive,
):
    piece = tokens.shape[0]
    half = piece // 2
    me, place = lax.axis_index("seq"), lax.axis_index("dp")
    one, two = neighbours()
    three = 3 - me
    stages = lax.axis_size("dp") // 2
    level, core = lax.div(place, 2), lax.rem(place, 2)
    mate = place + 1 - 2 * core
    above, below = level < stages - 1, level > 0

    for device in (one, two, three):
        greet("seq", device)
    greet("dp", mate)
    pl.when(above)(lambda: greet("dp", place + 2))
    pl.when(below)(lambda: greet("dp", place - 2))
    pl.semaphore_wait(pltpu.get_barrier_semaphore(), 4 + above.astype(jnp.int32) + below.astype(jnp.int32))

    def block(ref, at, start=0, size=piece):
        return ref.at[pl.ds(at * piece + start, size)]

    def spread(pieces, target, at):
        rows = target.shape[0] // 4
        mine = target.at[pl.ds(me * rows, rows)]
        source = lambda device: pieces if pieces is small else pieces.at[device]
        copies = [
            remote(source(device), mine, send.at[at + i], receive.at[at + i], "seq", device)
            for i, device in enumerate((one, two, three))
        ]
        return copies, source(me), mine

    qkv_copies, qkv_own, qkv_mine = spread(qkv_pieces, qkv_rows, 0)
    small_copies, small_own, small_mine = spread(small, small_rows, 3)
    fc_copies, fc_own, fc_mine = spread(fc_pieces, fc_rows, 6)
    token_one = remote(tokens, block(token_all, 1), send.at[9], receive.at[9], "seq", one)
    token_two = remote(tokens, block(token_all, 2), send.at[10], receive.at[10], "seq", two)
    token_three = (
        remote(block(token_all, 1, 0, half), block(token_all, 3, 0, half), send.at[11], receive.at[11], "seq", two),
        remote(block(token_all, 2, half, half), block(token_all, 3, half, half), send.at[12], receive.at[12], "seq", one),
    )
    first_kept = [pltpu.make_async_copy(qkv_own, qkv_mine, local.at[0]), pltpu.make_async_copy(small_own, small_mine, local.at[1])]
    later_kept = [pltpu.make_async_copy(fc_own, fc_mine, local.at[2]), pltpu.make_async_copy(tokens, block(token_all, 0), local.at[3])]

    chains = ((qkv_rows, qkv_full), (small_rows, small_full))

    def shard(array, at):
        rows = chains[array][0].shape[0]
        return chains[array][1].at[pl.ds((2 * at + core) * rows, rows)]

    def rising(array, step, device):
        at = level - (step - 1)
        source = chains[array][0] if step == 1 else shard(array, at)
        return remote(source, shard(array, at), up_send.at[array, step - 1], up_receive.at[array, step - 1], "dp", device)

    def falling(array, step, device):
        at = level + (step - 1)
        source = chains[array][0] if step == 1 else shard(array, at)
        return remote(source, shard(array, at), down_send.at[array, step - 1], down_receive.at[array, step - 1], "dp", device)

    def across(array, index, at):
        source = chains[array][0] if index == 0 else shard(array, at)
        return remote(source, shard(array, at), mate_send.at[array, index], mate_receive.at[array, index], "dp", mate)

    rises = lambda step: above & (level >= step - 1)
    falls = lambda step: below & (level <= stages - step)
    from_below = lambda step: level >= step
    from_above = lambda step: level + step <= stages - 1

    def relay(step):
        @pl.when(rises(step))
        def _():
            for array in (1, 0):
                rising(array, step, place + 2).start()

        @pl.when(falls(step))
        def _():
            for array in (1, 0):
                falling(array, step, place - 2).start()

    def take(step):
        @pl.when(from_below(step))
        def _():
            for array in (1, 0):
                got = shard(array, level - step)
                remote(got, got, up_send.at[array, step - 1], up_receive.at[array, step - 1], "dp", mate).wait_recv()
                across(array, step, level - step).start()

        @pl.when(from_above(step))
        def _():
            for array in (1, 0):
                got = shard(array, level + step)
                remote(got, got, down_send.at[array, step - 1], down_receive.at[array, step - 1], "dp", mate).wait_recv()
                across(array, stages - 1 + step, level + step).start()

    for copy in qkv_copies + small_copies + first_kept:
        copy.start()
    token_one.start()
    token_two.start()
    for copy in qkv_copies + small_copies:
        copy.wait_recv()
    for copy in first_kept:
        copy.wait()
    relay(1)
    own_full = [pltpu.make_async_copy(chains[array][0], shard(array, level), local.at[4 + array]) for array in range(2)]
    for array in range(2):
        across(array, 0, level).start()
        own_full[array].start()
    for copy in fc_copies + later_kept:
        copy.start()
    take(1)
    relay(2)
    take(2)
    relay(3)
    token_one.wait_recv()
    token_two.wait_recv()
    for copy in token_three:
        copy.start()
    take(3)
    for copy in later_kept + own_full:
        copy.wait()
    for copy in fc_copies:
        copy.wait_recv()
    for copy in qkv_copies + small_copies + fc_copies:
        copy.wait_send()
    token_one.wait_send()
    token_two.wait_send()
    for step in range(1, stages):

        @pl.when(rises(step))
        def _(step=step):
            for array in range(2):
                rising(array, step, place + 2).wait_send()

        @pl.when(falls(step))
        def _(step=step):
            for array in range(2):
                falling(array, step, place - 2).wait_send()

        @pl.when(from_below(step))
        def _(step=step):
            for array in range(2):
                across(array, step, level - step).wait()

        @pl.when(from_above(step))
        def _(step=step):
            for array in range(2):
                across(array, stages - 1 + step, level + step).wait()

    for array in range(2):
        across(array, 0, level).wait()
    for copy in token_three:
        copy.wait()


def opening(tokens, qkv_pieces, fc_pieces, small, dp_count):
    piece, width = tokens.shape
    steps = dp_count // 2 - 1
    anywhere = pl.BlockSpec(memory_space=pl.ANY)
    shape = lambda rows, columns: jax.ShapeDtypeStruct((rows, columns), BF16)
    dma = pltpu.SemaphoreType.DMA
    inside = pl.BlockSpec(memory_space=pltpu.VMEM)
    rows, columns = 4 * qkv_pieces.shape[1], qkv_pieces.shape[2]
    fine = 4 * small.shape[0]
    return pl.pallas_call(
        opening_kernel,
        in_specs=[inside] * 4,
        out_specs=[anywhere] * 4,
        out_shape=[
            shape(4 * piece, width),
            shape(rows * dp_count, columns),
            shape(4 * fc_pieces.shape[1], fc_pieces.shape[2]),
            shape(fine * dp_count, small.shape[1]),
        ],
        scratch_shapes=[
            pltpu.VMEM((rows, columns), BF16), pltpu.VMEM((fine, small.shape[1]), BF16),
            dma((6,)), dma((13,)), dma((13,)), dma((2, steps)), dma((2, steps)), dma((2, steps)), dma((2, steps)),
            dma((2, 2 * steps + 1)), dma((2, 2 * steps + 1)),
        ],
        compiler_params=pltpu.CompilerParams(collective_id=0, has_side_effects=True, vmem_limit_bytes=32 * 2**20),
        cost_estimate=cost(0, 10 * 4 * piece * width),
    )(tokens, qkv_pieces, fc_pieces, small)


def flip(first, second):
    low = lax.rem(first + second, 2)
    high = lax.rem(lax.div(first, 2) + lax.div(second, 2), 2)
    return 2 * high + low


def attend_plane_kernel(
    q, k, v_t, tokens, cot_one, cot_two, key_bias, proj, vectors,
    middle, normed, attended, lse, cot_three,
    score_ref, joint, terms, passed, joined, arrived, send, receive,
):
    piece, width = tokens.shape
    half = piece // 2
    heads = q.shape[1] // HEAD_DIM
    rank = lax.axis_index("seq")
    one, two = neighbours()
    for device in (one, two):
        greet("seq", device)
    pl.semaphore_wait(pltpu.get_barrier_semaphore(), 2)
    up, lower = pl.ds(0, half), pl.ds(half, half)

    def copy(index, source, target, device):
        return remote(source, target, send.at[index], receive.at[index], "seq", device)

    cot_copies = (copy(0, cot_one.at[up], cot_three.at[up], two), copy(1, cot_two.at[lower], cot_three.at[lower], one))
    across = (copy(2, terms.at[3, up], passed.at[0], one), copy(3, terms.at[3, lower], passed.at[1], two))
    plain_one = copy(4, terms.at[1, up], arrived.at[0, up], one)
    plain_two = copy(5, terms.at[2, lower], arrived.at[1, lower], two)
    joined_one = copy(6, joined.at[0], arrived.at[0, lower], one)
    joined_two = copy(7, joined.at[1], arrived.at[1, up], two)
    for item in cot_copies:
        item.start()

    def body(query_ref, key_ref, value_t, attended_tile, lse_tile):
        group, head = pl.program_id(0), pl.program_id(1)
        at = 3 - group
        true = flip(at, rank)
        query = query_ref[...]

        def first(block, top):
            scores = scores_of(key_ref, key_bias, query, flip(block, rank), piece, False)
            score_ref[rows_of(block, piece), :] = scores
            return jnp.maximum(top, jnp.max(scores, axis=0, keepdims=True))

        last = scores_of(key_ref, key_bias, query, at, piece, True)
        top = lax.fori_loop(0, true, first, jnp.max(last, axis=0, keepdims=True))

        def weigh(scores, rel):
            weights = jnp.exp2(scores - top)
            return jnp.sum(weights, axis=0, keepdims=True), nn(value_t[:, rows_of(rel, piece)], weights.astype(BF16))

        def second(block, carry):
            total, out = carry
            more, part = weigh(score_ref[rows_of(block, piece), :], flip(block, rank))
            return total + more, out + part

        total, out = lax.fori_loop(0, true, second, weigh(last, at))
        result = (out / total).T.astype(BF16)
        attended_tile[...] = result
        lse_tile[0] = top + jnp.log2(total)
        joint[:, pl.ds(pl.multiple_of(head * HEAD_DIM, HEAD_DIM), HEAD_DIM)] = result

        @pl.when(head == heads - 1)
        def _():
            terms[at] = nn(joint[...], proj[...]).astype(BF16)

        @pl.when((head == heads - 1) & (group == 0))
        def _():
            for item in across:
                item.start()

        @pl.when((head == heads - 1) & (group == 1))
        def _():
            plain_two.start()

        @pl.when((head == heads - 1) & (group == 2))
        def _():
            plain_one.start()
            for item in across:
                item.wait_recv()
            joined[0] = (terms[1, half:].astype(F32) + passed[1].astype(F32)).astype(BF16)
            joined[1] = (terms[2, :half].astype(F32) + passed[0].astype(F32)).astype(BF16)
            joined_one.start()
            joined_two.start()

    length = q.shape[0]
    pltpu.emit_pipeline(
        body,
        grid=(4, heads),
        in_specs=[
            pl.BlockSpec((piece, HEAD_DIM), lambda g, h: (3 - g, h)),
            pl.BlockSpec((length, HEAD_DIM), lambda g, h: (0, h)),
            pl.BlockSpec((HEAD_DIM, length), lambda g, h: (h, 0)),
        ],
        out_specs=[
            pl.BlockSpec((piece, HEAD_DIM), lambda g, h: (3 - g, h)),
            pl.BlockSpec((1, 1, piece), lambda g, h: (h, 0, 3 - g)),
        ],
    )(q, k, v_t, attended, lse)

    for item in (plain_one, plain_two, joined_one, joined_two):
        item.wait_recv()
    part = min(128, piece)

    def norm_body(token_tile, middle_tile, normed_tile):
        here = pl.ds(pl.multiple_of(pl.program_id(0) * part, part), part)
        total = terms[0, here, :].astype(F32) + arrived[0, here, :].astype(F32) + arrived[1, here, :].astype(F32)
        values = token_tile[...].astype(F32) + (total + vectors[0:1, :])
        middle_tile[...] = values
        normed_tile[...] = (norm_parts(values)[0] * vectors[1:2, :] + vectors[2:3, :]).astype(BF16)

    line = pl.BlockSpec((part, width), lambda i: (i, 0))
    pltpu.emit_pipeline(norm_body, grid=(piece // part,), in_specs=[line], out_specs=[line] * 2)(tokens, middle, normed)
    for item in cot_copies:
        item.wait()
    for item in (*across, plain_one, plain_two, joined_one, joined_two):
        item.wait_send()


def attend_plane(q, k, v_t, tokens, cots, key_bias, proj, vectors):
    piece, width = tokens.shape
    length, columns = q.shape
    heads, half = columns // HEAD_DIM, piece // 2
    anywhere = pl.BlockSpec(memory_space=pl.ANY)
    inside = pl.BlockSpec(memory_space=pltpu.VMEM)
    shape = lambda *dims: jax.ShapeDtypeStruct(dims, BF16)
    dma = pltpu.SemaphoreType.DMA
    return pl.pallas_call(
        attend_plane_kernel,
        in_specs=[anywhere] * 6 + [inside] * 3,
        out_specs=[anywhere] * 5,
        out_shape=[
            jax.ShapeDtypeStruct((piece, width), F32), shape(piece, width), shape(length, columns),
            jax.ShapeDtypeStruct((heads, 1, length), F32), shape(piece, width),
        ],
        scratch_shapes=[
            pltpu.VMEM((length, piece), F32),
            pltpu.VMEM((piece, columns), BF16),
            pltpu.VMEM((4, piece, width), BF16),
            pltpu.VMEM((2, half, width), BF16),
            pltpu.VMEM((2, half, width), BF16),
            pltpu.VMEM((2, piece, width), BF16),
            dma((8,)), dma((8,)),
        ],
        compiler_params=pltpu.CompilerParams(collective_id=2, has_side_effects=True, vmem_limit_bytes=56 * 2**20),
        cost_estimate=cost(3 * length * length * columns + 2 * length * columns * width, 10 * length * width, heads * length * length // 2),
    )(q, k, v_t, tokens, *cots, key_bias, proj, vectors)


def sum_rows(ref, at, columns, value, first):
    total = jnp.sum(value, axis=0, keepdims=True)

    @pl.when(first)
    def _():
        ref[at : at + 1, columns] = total

    @pl.when(jnp.logical_not(first))
    def _():
        ref[at : at + 1, columns] += total


class LevelScatter:
    def __init__(self, source, mate_in, summed, got, send, receive):
        self.source, self.mate_in, self.summed, self.got = source, mate_in, summed, got
        self.send, self.receive = send, receive
        self.rows = mate_in.shape[0] // 4
        self.place = lax.axis_index("dp")
        self.level, self.core = lax.div(self.place, 2), lax.rem(self.place, 2)
        self.mate = self.place + 1 - 2 * self.core

    def greet(self):
        greet("dp", self.mate)
        count = jnp.int32(1)
        for step in (1, 2):
            up, down = self.level + step <= 3, self.level >= step
            pl.when(up)(lambda step=step: greet("dp", self.place + 2 * step))
            pl.when(down)(lambda step=step: greet("dp", self.place - 2 * step))
            count = count + up.astype(jnp.int32) + down.astype(jnp.int32)
        return count

    def block(self, ref, at):
        return ref.at[pl.ds(at * self.rows, self.rows)]

    def swaps(self):
        return [
            remote(
                self.block(self.source, 2 * at + 1 - self.core), self.block(self.mate_in, at),
                self.send.at[at], self.receive.at[at], "dp", self.mate,
            )
            for at in range(4)
        ]

    def start(self):
        for item in self.swaps():
            item.start()

    def add(self, first, second, out, grid, first_at, second_at, out_at):
        def body(left, right, total):
            total[...] = (left[...].astype(F32) + right[...].astype(F32)).astype(total.dtype)

        spec = lambda at: pl.BlockSpec((self.rows, first.shape[1]), lambda i: (at(i), 0))
        pltpu.emit_pipeline(
            body, grid=(grid,), in_specs=[spec(first_at), spec(second_at)], out_specs=[spec(out_at)]
        )(first, second, out)

    def hop(self, at, slot, index, steps):
        return remote(
            self.block(self.summed, at), self.block(self.got, slot), self.send.at[4 + index], self.receive.at[4 + slot],
            "dp", self.place + 2 * steps,
        )

    def hops(self):
        level = self.level
        return [
            (level == 0, self.hop(3, 3, 0, 1)),
            (level == 3, self.hop(0, 3, 0, -1)),
            (level == 0, self.hop(2, 2, 1, 2)),
            (level == 3, self.hop(1, 2, 1, -2)),
            (level <= 2, self.hop(lax.rem(level + 1, 4), 0, 2, 1)),
            (level >= 1, self.hop(lax.rem(level + 3, 4), 1, 3, -1)),
        ]

    def passes(self):
        return [(self.level == 1, self.hop(3, 2, 1, 2)), (self.level == 2, self.hop(0, 2, 1, -2))]

    def spread(self):
        for item in self.swaps():
            item.wait_recv()
        self.add(
            self.source, self.mate_in, self.summed, 4, lambda i: 2 * i + self.core, lambda i: i, lambda i: i
        )
        for condition, copy in self.hops():
            pl.when(condition)(lambda copy=copy: copy.start())

    def arrive(self, slot):
        here = self.block(self.got, slot)
        remote(here, here, self.send.at[0], self.receive.at[4 + slot], "dp", self.mate).wait_recv()

    def pass_on(self):
        for level, at in ((1, 3), (2, 0)):

            @pl.when(self.level == level)
            def _(at=at):
                self.arrive(3)
                self.add(self.summed, self.got, self.summed, 1, lambda i: at, lambda i: 3, lambda i: at)

        for condition, copy in self.passes():
            pl.when(condition)(lambda copy=copy: copy.start())

    def finish(self, out):
        level = self.level
        pl.when(level >= 1)(lambda: self.arrive(0))
        pl.when(level <= 2)(lambda: self.arrive(1))
        self.arrive(2)
        rows = min(64, self.rows)

        def body(own, mate, below, above, far, total):
            value = own[...].astype(F32) + mate[...].astype(F32) + far[...].astype(F32)
            below_term, above_term = below[...].astype(F32), above[...].astype(F32)
            value = value + jnp.where(level >= 1, below_term, 0.0) + jnp.where(level <= 2, above_term, 0.0)
            total[...] = value.astype(total.dtype)

        steps = self.rows // rows
        spec = lambda at: pl.BlockSpec((rows, out.shape[1]), lambda i: (at * steps + i, 0))
        pltpu.emit_pipeline(
            body,
            grid=(steps,),
            in_specs=[spec(self.place), spec(level), spec(0), spec(1), spec(2)],
            out_specs=[spec(0)],
        )(self.source, self.mate_in, self.got, self.got, self.got, out)

    def close(self):
        for item in self.swaps():
            item.wait_send()
        for condition, copy in self.hops() + self.passes():
            pl.when(condition)(lambda copy=copy: copy.wait_send())


def plane_kernel(
    normed, cot_own, cot_one, cot_two, cot_three, fc, bias, down, middle, gain,
    grad_middle, low_all, sums, hidden_sums, active, hidden_grad, normed_all, cot_all, terms, grad_down, grad_fc,
    mate_in, summed, got, down_share,
    normed_buf, cot_buf, sum_ref, joined, passed, arrived, load, local, send, receive, level_send, level_receive,
):
    piece, width = normed.shape
    half = piece // 2
    inner = fc.shape[1]
    length = normed_all.shape[0]
    tile = min(512, inner)
    last = inner // tile - 1
    one, two = neighbours()
    scatter = LevelScatter(grad_down, mate_in, summed, got, level_send, level_receive)
    for device in (one, two):
        greet("seq", device)
    pl.semaphore_wait(pltpu.get_barrier_semaphore(), 2 + scatter.greet())

    up, lower = pl.ds(0, half), pl.ds(half, half)
    rows = lambda k, start=0, size=piece: pl.ds(k * piece + start, size)

    def copy(index, source, target, device):
        return remote(source, target, send.at[index], receive.at[index], "seq", device)

    normed_one = copy(0, normed, normed_buf.at[1], one)
    normed_two = copy(1, normed, normed_buf.at[2], two)
    normed_three = (
        copy(2, normed_buf.at[1, up], normed_buf.at[3, up], two),
        copy(3, normed_buf.at[2, lower], normed_buf.at[3, lower], one),
    )
    across = (copy(4, cot_buf.at[3, up], passed.at[0], one), copy(5, cot_buf.at[3, lower], passed.at[1], two))
    plain_one = copy(6, cot_buf.at[1, up], arrived.at[0, up], one)
    plain_two = copy(7, cot_buf.at[2, lower], arrived.at[1, lower], two)
    joined_one = copy(8, joined.at[0], arrived.at[0, lower], one)
    joined_two = copy(9, joined.at[1], arrived.at[1, up], two)
    low_one = copy(10, low_all.at[rows(0)], low_all.at[rows(1)], one)
    low_two = copy(11, low_all.at[rows(0)], low_all.at[rows(2)], two)
    low_three = (
        copy(12, low_all.at[rows(1, 0, half)], low_all.at[rows(3, 0, half)], two),
        copy(13, low_all.at[rows(2, half, half)], low_all.at[rows(3, half, half)], one),
    )

    loads = [
        pltpu.make_async_copy(source, cot_buf.at[k], load.at[k])
        for k, source in enumerate((cot_own, cot_one, cot_two, cot_three))
    ]
    own = pltpu.make_async_copy(normed, normed_buf.at[0], load.at[4])
    keeps = [pltpu.make_async_copy(normed_buf.at[k], normed_all.at[rows(k)], local.at[k]) for k in range(4)]
    keeps_cot = [pltpu.make_async_copy(cot_buf.at[k], cot_all.at[rows(k)], local.at[4 + k]) for k in range(4)]

    normed_one.start()
    normed_two.start()
    own.start()
    for item in loads:
        item.start()

    def feed_body(fc_tile, down_tile, active_tile, hidden_tile):
        k, j = pl.program_id(0), pl.program_id(1)

        @pl.when((k == 0) & (j == 0))
        def _():
            own.wait()
            keeps[0].start()
            for item in loads:
                item.wait()
            for item in keeps_cot:
                item.start()

        @pl.when((k == 1) & (j == 0))
        def _():
            normed_one.wait_recv()
            normed_two.wait_recv()
            for item in normed_three:
                item.start()
            keeps[1].start()
            keeps[2].start()

        @pl.when((k == 3) & (j == 0))
        def _():
            for item in normed_three:
                item.wait_recv()
            keeps[3].start()

        weights = fc_tile[...]
        columns = pl.ds(pl.multiple_of(j * tile, tile), tile)
        hidden = nn(normed_buf[k], weights) + bias[:, columns]
        grad_active = nt(cot_buf[k], down_tile[...])
        square = hidden * hidden
        bent = jnp.tanh(math.sqrt(2 / math.pi) * (hidden + 0.044715 * (square * hidden)))
        share = 0.5 * (1.0 + bent)
        active_tile[...] = (hidden * share).astype(BF16)
        slope = share + (0.5 * hidden) * (1.0 - bent * bent) * (
            math.sqrt(2 / math.pi) * (1.0 + (3 * 0.044715) * square)
        )
        grad_hidden = (grad_active * slope).astype(BF16)
        hidden_tile[...] = grad_hidden
        sum_rows(hidden_sums, 0, columns, grad_hidden.astype(F32), k == 0)
        term = nt(grad_hidden, weights)

        @pl.when(j == 0)
        def _():
            sum_ref[...] = term

        @pl.when(j > 0)
        def _():
            sum_ref[...] += term

        @pl.when((j == last) & (k == 0))
        def _():
            for item in keeps_cot:
                item.wait()
            arrived[2] = sum_ref[...].astype(BF16)

        @pl.when((j == last) & (k == 1))
        def _():
            cot_buf[1] = sum_ref[...].astype(BF16)
            plain_one.start()

        @pl.when((j == last) & (k == 2))
        def _():
            cot_buf[2] = sum_ref[...].astype(BF16)
            plain_two.start()

        @pl.when((j == last) & (k == 3))
        def _():
            cot_buf[3] = sum_ref[...].astype(BF16)
            for item in across:
                item.start()

    pltpu.emit_pipeline(
        feed_body,
        grid=(4, inner // tile),
        in_specs=[
            pl.BlockSpec((width, tile), lambda k, j: (0, j)),
            pl.BlockSpec((tile, width), lambda k, j: (j, 0)),
        ],
        out_specs=[pl.BlockSpec((piece, tile), lambda k, j: (k, j))] * 2,
    )(fc, down, active, hidden_grad)

    narrow = min(512, width)

    def down_body(active_rows, down_columns, out):
        out[...] = nn(active_rows[...], down_columns[...]).astype(BF16)

    def multiply_down(start):
        pltpu.emit_pipeline(
            down_body,
            grid=(2, width // narrow),
            in_specs=[
                pl.BlockSpec((piece, inner), lambda k, j: (start + k, 0)),
                pl.BlockSpec((inner, narrow), lambda k, j: (0, j)),
            ],
            out_specs=[pl.BlockSpec((piece, narrow), lambda k, j: (start + k, j))],
        )(active, down, terms)

    wide, tall = min(1024, width), min(1024, inner)

    def outer_body(left, right, out):
        out[...] = tn(left[...], right[...]).astype(BF16)

    def outer(left, right, out, shape):
        pltpu.emit_pipeline(
            outer_body,
            grid=(out.shape[0] // shape[0], out.shape[1] // shape[1]),
            in_specs=[
                pl.BlockSpec((length, shape[0]), lambda i, j: (0, i)),
                pl.BlockSpec((length, shape[1]), lambda i, j: (0, j)),
            ],
            out_specs=[pl.BlockSpec(shape, lambda i, j: (i, j))],
        )(left, right, out)

    outer(active, cot_all, grad_down, (tall, wide))
    scatter.start()
    for item in across:
        item.wait_recv()
    joined[0] = (cot_buf[1, half:].astype(F32) + passed[1].astype(F32)).astype(BF16)
    joined[1] = (cot_buf[2, :half].astype(F32) + passed[0].astype(F32)).astype(BF16)
    joined_one.start()
    joined_two.start()
    for item in keeps:
        item.wait()
    multiply_down(0)
    scatter.spread()
    for item in (plain_one, plain_two, joined_one, joined_two):
        item.wait_recv()

    part = min(128, piece)

    def norm_body(middle_tile, cot_tile, grad_tile, low_tile):
        i = pl.program_id(0)
        here = pl.ds(pl.multiple_of(i * part, part), part)
        upstream = (
            arrived[2, here, :].astype(F32) + arrived[0, here, :].astype(F32) + arrived[1, here, :].astype(F32)
        )
        unit, scale = norm_parts(middle_tile[...])
        cot = cot_tile[...].astype(F32)
        grad = cot + norm_backward(unit, scale, gain[...], upstream)
        rounded = grad.astype(BF16)
        grad_tile[...] = grad
        low_tile[...] = rounded
        for at, item in enumerate((upstream * unit, upstream, rounded.astype(F32), cot)):
            sum_rows(sums, at, slice(None), item, i == 0)

    line = pl.BlockSpec((part, width), lambda i: (i, 0))
    pltpu.emit_pipeline(norm_body, grid=(piece // part,), in_specs=[line] * 2, out_specs=[line] * 2)(
        middle, cot_own, grad_middle, low_all
    )
    low_one.start()
    low_two.start()

    multiply_down(2)
    scatter.pass_on()
    outer(normed_all, hidden_grad, grad_fc, (wide, tall))
    low_one.wait_recv()
    low_two.wait_recv()
    for item in low_three:
        item.start()
    scatter.finish(down_share)
    scatter.close()
    for item in low_three:
        item.wait()
    for item in (
        normed_one, normed_two, *normed_three, *across, plain_one, plain_two, joined_one, joined_two, low_one, low_two
    ):
        item.wait_send()


def feed_plane(normed, cots, fc, bias, down, middle, gain):
    piece, width = normed.shape
    inner = fc.shape[1]
    length, half = 4 * piece, piece // 2
    anywhere = pl.BlockSpec(memory_space=pl.ANY)
    inside = pl.BlockSpec(memory_space=pltpu.VMEM)
    shape = lambda rows, columns, kind=BF16: jax.ShapeDtypeStruct((rows, columns), kind)
    dma = pltpu.SemaphoreType.DMA
    return pl.pallas_call(
        plane_kernel,
        in_specs=[anywhere] * 6 + [inside, anywhere, anywhere, inside],
        out_specs=[anywhere, anywhere, inside, inside] + [anywhere] * 11,
        out_shape=[
            shape(piece, width, F32), shape(length, width), shape(4, width, F32), shape(1, inner, F32),
            shape(length, inner), shape(length, inner), shape(length, width), shape(length, width),
            shape(length, width), shape(inner, width), shape(width, inner),
            shape(inner // 2, width), shape(inner // 2, width), shape(inner // 2, width), shape(inner // 8, width, F32),
        ],
        scratch_shapes=[
            pltpu.VMEM((4, piece, width), BF16),
            pltpu.VMEM((4, piece, width), BF16),
            pltpu.VMEM((piece, width), F32),
            pltpu.VMEM((2, half, width), BF16),
            pltpu.VMEM((2, half, width), BF16),
            pltpu.VMEM((3, piece, width), BF16),
            dma((5,)), dma((8,)), dma((14,)), dma((14,)), dma((8,)), dma((8,)),
        ],
        compiler_params=pltpu.CompilerParams(collective_id=1, has_side_effects=True, vmem_limit_bytes=60 * 2**20),
        cost_estimate=cost(12 * length * width * inner, 10 * length * width),
    )(normed, *cots, fc, bias, down, middle, gain)


def retreat_plane_kernel(
    low_all, q, k, v, k_t, lse, terms, middle, key_bias, proj, down_shift,
    grads, column_sums, block_out,
    prob_ref, chance_ref, grad_ref, key_sum, value_sum, rounded, own, passed, joined, arrived,
    load, local, send, receive,
):
    piece, width = middle.shape
    half = piece // 2
    length, columns = q.shape
    heads = columns // HEAD_DIM
    rank = lax.axis_index("seq")
    one, two = neighbours()
    for device in (one, two):
        greet("seq", device)
    pl.semaphore_wait(pltpu.get_barrier_semaphore(), 2)
    up, lower = pl.ds(0, half), pl.ds(half, half)
    rows = lambda at, start=0, size=piece: pl.ds(at * piece + start, size)

    def copy(index, source, target, device):
        return remote(source, target, send.at[index], receive.at[index], "seq", device)

    across = (
        copy(0, terms.at[rows(3, 0, half)], passed.at[0], one),
        copy(1, terms.at[rows(3, half, half)], passed.at[1], two),
    )
    plain_one = copy(2, terms.at[rows(1, 0, half)], arrived.at[0, up], one)
    plain_two = copy(3, terms.at[rows(2, half, half)], arrived.at[1, lower], two)
    joined_one = copy(4, joined.at[0], arrived.at[0, lower], one)
    joined_two = copy(5, joined.at[1], arrived.at[1, up], two)
    loads = (
        pltpu.make_async_copy(terms.at[rows(1, half, half)], own.at[0], load.at[0]),
        pltpu.make_async_copy(terms.at[rows(2, 0, half)], own.at[1], load.at[1]),
    )
    for item in (*across, plain_one, plain_two, *loads):
        item.start()
    key_sum[...] = jnp.zeros_like(key_sum)
    value_sum[...] = jnp.zeros_like(value_sum)

    def body(low_ref, query_ref, key_ref, value_ref, key_t, lse_ref, query_out):
        at, head = pl.program_id(0), pl.program_id(1)
        true = flip(at, rank)
        here = pl.ds(pl.multiple_of(head * HEAD_DIM, HEAD_DIM), HEAD_DIM)

        @pl.when(head == 0)
        def _():
            grad_ref[...] = nt(low_ref[...], proj[...]).astype(BF16)

        @pl.when((at == 1) & (head == 2))
        def _():
            for item in (*across,):
                item.wait_recv()
            for item in loads:
                item.wait()
            joined[0] = (own[0].astype(F32) + passed[1].astype(F32)).astype(BF16)
            joined[1] = (own[1].astype(F32) + passed[0].astype(F32)).astype(BF16)
            joined_one.start()
            joined_two.start()

        query, grad, base = query_ref[...], grad_ref[:, here], lse_ref[0]

        def measure(scores, rel):
            block = rows_of(rel, piece)
            probs = jnp.exp2(scores - base)
            grad_chances = nt(value_ref[block, :], grad)
            value_sum[block, here] += nn(probs.astype(BF16), grad)
            prob_ref[block, :] = probs
            chance_ref[block, :] = grad_chances
            return jnp.sum(probs * grad_chances, axis=0, keepdims=True)

        def first(block, weighted):
            rel = flip(block, rank)
            return weighted + measure(scores_of(key_ref, key_bias, query, rel, piece, False), rel)

        last = scores_of(key_ref, key_bias, query, at, piece, True)
        weighted = lax.fori_loop(0, true, first, measure(last, at))

        def second(block, total):
            block = rows_of(flip(block, rank), piece)
            grad_scores = (prob_ref[block, :] * (chance_ref[block, :] - weighted)).astype(BF16)
            key_sum[block, here] += nn(grad_scores, query)
            return total + nn(key_t[:, block], grad_scores)

        total = lax.fori_loop(0, true + 1, second, jnp.zeros((HEAD_DIM, piece), F32))
        result = (total * FACTOR).T.astype(BF16)
        query_out[...] = result
        sum_rows(column_sums, 0, here, result.astype(F32), at == 0)

    pltpu.emit_pipeline(
        body,
        grid=(4, heads),
        in_specs=[
            pl.BlockSpec((piece, width), lambda g, h: (g, 0)),
            pl.BlockSpec((piece, HEAD_DIM), lambda g, h: (g, h)),
            pl.BlockSpec((length, HEAD_DIM), lambda g, h: (0, h)),
            pl.BlockSpec((length, HEAD_DIM), lambda g, h: (0, h)),
            pl.BlockSpec((HEAD_DIM, length), lambda g, h: (h, 0)),
            pl.BlockSpec((1, 1, piece), lambda g, h: (h, 0, g)),
        ],
        out_specs=[pl.BlockSpec((piece, HEAD_DIM), lambda g, h: (g, h))],
    )(low_all, q, k, v, k_t, lse, grads)

    rounded[:, :columns] = (key_sum[...] * FACTOR).astype(BF16)
    values = value_sum[...].astype(BF16)
    rounded[:, columns:] = values
    column_sums[1:2, :] = jnp.sum(values.astype(F32), axis=0, keepdims=True)
    keep = pltpu.make_async_copy(rounded, grads.at[:, pl.ds(columns, 2 * columns)], local.at[0])
    keep.start()
    for item in (plain_one, plain_two, joined_one, joined_two):
        item.wait_recv()
    part = min(128, piece)

    def out_body(middle_tile, term_tile, out):
        here = pl.ds(pl.multiple_of(pl.program_id(0) * part, part), part)
        total = term_tile[...].astype(F32) + arrived[0, here, :].astype(F32) + arrived[1, here, :].astype(F32)
        out[...] = (middle_tile[...] + (total + down_shift[...])).astype(BF16)

    line = pl.BlockSpec((part, width), lambda i: (i, 0))
    pltpu.emit_pipeline(out_body, grid=(piece // part,), in_specs=[line] * 2, out_specs=[line])(middle, terms, block_out)
    keep.wait()
    for item in (*across, plain_one, plain_two, joined_one, joined_two):
        item.wait_send()


def retreat_plane(low_all, q, k, v, k_t, lse, terms, middle, key_bias, proj, down_shift):
    piece, width = middle.shape
    length, columns = q.shape
    half = piece // 2
    anywhere = pl.BlockSpec(memory_space=pl.ANY)
    inside = pl.BlockSpec(memory_space=pltpu.VMEM)
    dma = pltpu.SemaphoreType.DMA
    return pl.pallas_call(
        retreat_plane_kernel,
        in_specs=[anywhere] * 8 + [inside] * 3,
        out_specs=[anywhere, inside, anywhere],
        out_shape=[
            jax.ShapeDtypeStruct((length, 3 * columns), BF16),
            jax.ShapeDtypeStruct((2, columns), F32),
            jax.ShapeDtypeStruct((piece, width), BF16),
        ],
        scratch_shapes=[
            pltpu.VMEM((length, piece), F32),
            pltpu.VMEM((length, piece), F32),
            pltpu.VMEM((piece, columns), BF16),
            pltpu.VMEM((length, columns), F32),
            pltpu.VMEM((length, columns), F32),
            pltpu.VMEM((length, 2 * columns), BF16),
            pltpu.VMEM((2, half, width), BF16),
            pltpu.VMEM((2, half, width), BF16),
            pltpu.VMEM((2, half, width), BF16),
            pltpu.VMEM((2, piece, width), BF16),
            dma((2,)), dma((1,)), dma((6,)), dma((6,)),
        ],
        compiler_params=pltpu.CompilerParams(collective_id=3, has_side_effects=True, vmem_limit_bytes=60 * 2**20),
        cost_estimate=cost(8 * length * length * columns + 2 * length * columns * width, 10 * length * width),
    )(low_all, q, k, v, k_t, lse, terms, middle, key_bias, proj, down_shift)


def closing_kernel(
    grads, weight, normed_one, tokens, grad_middle, gain, sums_two, hidden_sums, qv_sums, fc_share,
    tokens_grad, qkv_out, fc_out, small_out, grad_qkv, mate_in, summed, got, qkv_share,
    terms, passed, joined, arrived, qkv_in, fc_in, mine, small_in, small_rows, small_got,
    send, receive, level_send, level_receive, small_send, small_receive, load,
):
    piece, width = tokens.shape
    half = piece // 2
    columns = grads.shape[1]
    heads = columns // (3 * HEAD_DIM)
    me, place = lax.axis_index("seq"), lax.axis_index("dp")
    one, two = neighbours()
    three = 3 - me
    plane = (one, two, three)
    others = [lax.rem(place + i, 8) for i in range(1, 8)]
    for device in plane:
        greet("seq", device)
    for device in others:
        greet("dp", device)
    pl.semaphore_wait(pltpu.get_barrier_semaphore(), 10)
    scatter = LevelScatter(grad_qkv, mate_in, summed, got, level_send, level_receive)
    up, lower = pl.ds(0, half), pl.ds(half, half)

    def copy(index, source, target, device):
        return remote(source, target, send.at[index], receive.at[index], "seq", device)

    across = (copy(0, terms.at[3, up], passed.at[0], one), copy(1, terms.at[3, lower], passed.at[1], two))
    plain_one = copy(2, terms.at[1, up], arrived.at[0, up], one)
    plain_two = copy(3, terms.at[2, lower], arrived.at[1, lower], two)
    joined_one = copy(4, joined.at[0], arrived.at[0, lower], one)
    joined_two = copy(5, joined.at[1], arrived.at[1, up], two)
    fine = qkv_in.shape[1]
    rows_for = lambda ref, device: ref.at[pl.ds(device * fine, fine)]
    fc_copies = [copy(6 + i, rows_for(fc_share, device), fc_in.at[i], device) for i, device in enumerate(plane)]
    qkv_copies = [copy(9 + i, rows_for(qkv_share, device), qkv_in.at[i], device) for i, device in enumerate(plane)]
    small_copies = [copy(12 + i, mine, small_in.at[i], device) for i, device in enumerate(plane)]
    fc_own = pltpu.make_async_copy(rows_for(fc_share, me), fc_in.at[3], load.at[0])
    qkv_own = pltpu.make_async_copy(rows_for(qkv_share, me), qkv_in.at[3], load.at[1])
    row_copies = [
        remote(small_rows.at[device], small_got.at[i], small_send.at[i], small_receive.at[i], "dp", device)
        for i, device in enumerate(others)
    ]

    def back_term(at):
        terms[at] = nt(grads[at * piece : (at + 1) * piece, :], weight[...]).astype(BF16)

    back_term(3)
    for item in across:
        item.start()
    tile = min(512, width)

    def outer_body(left, out):
        out[...] = tn(left[...], grads[...]).astype(BF16)

    pltpu.emit_pipeline(
        outer_body,
        grid=(width // tile,),
        in_specs=[pl.BlockSpec((normed_one.shape[0], tile), lambda i: (0, i))],
        out_specs=[pl.BlockSpec((tile, columns), lambda i: (i, 0))],
    )(normed_one, grad_qkv)
    scatter.start()
    fc_own.start()
    back_term(2)
    plain_two.start()
    back_term(1)
    plain_one.start()
    for item in across:
        item.wait_recv()
    joined[0] = (terms[1, half:].astype(F32) + passed[1].astype(F32)).astype(BF16)
    joined[1] = (terms[2, :half].astype(F32) + passed[0].astype(F32)).astype(BF16)
    joined_one.start()
    joined_two.start()
    scatter.spread()
    back_term(0)
    for item in fc_copies:
        item.start()
    mine[...] = jnp.zeros_like(mine)
    mine[2:6, :] = sums_two[...]
    for head in range(heads):
        at = (head * 2 + lax.rem(me, 2)) * 2 + lax.div(me, 2)
        here = pl.ds(pl.multiple_of(at * HEAD_DIM, HEAD_DIM), HEAD_DIM)
        for part in range(2):
            mine[6 + part : 7 + part, here] = qv_sums[part : part + 1, head * HEAD_DIM : (head + 1) * HEAD_DIM]
    scatter.pass_on()
    for item in (plain_one, plain_two, joined_one, joined_two):
        item.wait_recv()
    part = min(128, piece)

    def norm_body(token_tile, middle_tile, out):
        i = pl.program_id(0)
        here = pl.ds(pl.multiple_of(i * part, part), part)
        upstream = terms[0, here, :].astype(F32) + arrived[0, here, :].astype(F32) + arrived[1, here, :].astype(F32)
        unit, scale = norm_parts(token_tile[...].astype(F32))
        out[...] = middle_tile[...] + norm_backward(unit, scale, gain[...], upstream)
        for at, item in enumerate((upstream * unit, upstream)):
            sum_rows(mine, at, slice(None), item, i == 0)

    line = pl.BlockSpec((part, width), lambda i: (i, 0))
    pltpu.emit_pipeline(norm_body, grid=(piece // part,), in_specs=[line] * 2, out_specs=[line])(
        tokens, grad_middle, tokens_grad
    )
    for item in small_copies:
        item.start()
    scatter.finish(qkv_share)
    for item in qkv_copies:
        item.start()
    qkv_own.start()
    for item in small_copies:
        item.wait_recv()
    mine_total = mine[...] + small_in[0] + small_in[1] + small_in[2]
    small_rows[...] = jnp.zeros_like(small_rows)
    share, wide = width // 8, 2 * width // 8
    for d in range(8):
        small_rows[d, 0:6, 0:share] = mine_total[0:6, d * share : (d + 1) * share]
        row, at = 6 + d // 4, (d % 4) * wide
        small_rows[d, 6:7, :] = mine_total[row : row + 1, at : at + wide]
        inner = hidden_sums.shape[1] // 8
        small_rows[d, 7:8, 0:inner] = hidden_sums[:, d * inner : (d + 1) * inner]
    for item in row_copies:
        item.start()
    sources = (*plane, me)
    fc_own.wait()
    for item in fc_copies:
        item.wait_recv()
    block = fc_in.shape[2] // 8
    for i, source in enumerate(sources):
        for d in range(8):
            target = pl.ds(pl.multiple_of((d * 4 + source) * block, block), block)
            fc_out[:, target] = fc_in[i, :, d * block : (d + 1) * block].astype(F32)
    qkv_own.wait()
    for item in qkv_copies:
        item.wait_recv()
    for i, source in enumerate(sources):
        for part in range(3):
            for head in range(heads):
                at = part * HEADS + (head * 2 + lax.rem(source, 2)) * 2 + lax.div(source, 2)
                target = pl.ds(pl.multiple_of(at * HEAD_DIM, HEAD_DIM), HEAD_DIM)
                start = (part * heads + head) * HEAD_DIM
                qkv_out[:, target] = qkv_in[i, :, start : start + HEAD_DIM].astype(F32)
    for item in row_copies:
        item.wait_recv()
    total = small_rows[place]
    for i in range(7):
        total = total + small_got[i]
    small_out[...] = total
    for item in (*across, plain_one, plain_two, joined_one, joined_two, *fc_copies, *qkv_copies, *small_copies, *row_copies):
        item.wait_send()
    scatter.close()


def closing(grads, weight, normed_one, tokens, grad_middle, gain, sums_two, hidden_sums, qv_sums, fc_share):
    piece, width = tokens.shape
    columns, half = grads.shape[1], piece // 2
    fine = fc_share.shape[0] // 4
    wide = 2 * width // 8
    anywhere = pl.BlockSpec(memory_space=pl.ANY)
    inside = pl.BlockSpec(memory_space=pltpu.VMEM)
    shape = lambda rows, columns, kind=BF16: jax.ShapeDtypeStruct((rows, columns), kind)
    dma = pltpu.SemaphoreType.DMA
    return pl.pallas_call(
        closing_kernel,
        in_specs=[inside, inside, anywhere, anywhere, anywhere, inside, inside, inside, inside, anywhere],
        out_specs=[anywhere, inside, inside, inside] + [anywhere] * 5,
        out_shape=[
            shape(piece, width, F32), shape(fine, 4 * columns, F32), shape(fine, 4 * fc_share.shape[1], F32),
            shape(8, wide, F32), shape(width, columns), shape(width // 2, columns), shape(width // 2, columns),
            shape(width // 2, columns), shape(width // 8, columns),
        ],
        scratch_shapes=[
            pltpu.VMEM((4, piece, width), BF16),
            pltpu.VMEM((2, half, width), BF16),
            pltpu.VMEM((2, half, width), BF16),
            pltpu.VMEM((2, piece, width), BF16),
            pltpu.VMEM((4, fine, columns), BF16),
            pltpu.VMEM((4, fine, fc_share.shape[1]), BF16),
            pltpu.VMEM((8, width), F32),
            pltpu.VMEM((3, 8, width), F32),
            pltpu.VMEM((8, 8, wide), F32),
            pltpu.VMEM((7, 8, wide), F32),
            dma((15,)), dma((15,)), dma((8,)), dma((8,)), dma((7,)), dma((7,)), dma((2,)),
        ],
        compiler_params=pltpu.CompilerParams(collective_id=4, has_side_effects=True, vmem_limit_bytes=60 * 2**20),
        cost_estimate=cost(16 * piece * width * columns, 10 * piece * width),
    )(grads, weight, normed_one, tokens, grad_middle, gain, sums_two, hidden_sums, qv_sums, fc_share)


def after(value, *others):
    return lax.optimization_barrier((value, *others))[0]


def shift(value, axis, distance):
    count = lax.axis_size(axis)
    return lax.ppermute(value, axis, [(i, i ^ distance) for i in range(count)])


def gather_blocks(value, axis="seq"):
    return [value] + [shift(value, axis, k) for k in range(1, lax.axis_size(axis))]


def scatter_blocks(blocks, axis="seq"):
    return [blocks[0]] + [shift(blocks[k], axis, k) for k in range(1, lax.axis_size(axis))]


def gather_plane(value):
    if lax.axis_size("seq") != 4:
        return gather_blocks(value)
    half = value.shape[0] // 2
    one, two = shift(value, "seq", 1), shift(value, "seq", 2)
    three = jnp.concatenate([shift(one[:half], "seq", 2), shift(two[half:], "seq", 1)], axis=0)
    return [value, one, two, three]


def scatter_plane(blocks):
    if lax.axis_size("seq") != 4:
        return scatter_blocks(blocks)
    half = blocks[0].shape[0] // 2
    up, low = shift(blocks[3][:half], "seq", 1), shift(blocks[3][half:], "seq", 2)
    one = shift(blocks[1][:half], "seq", 1)
    two = shift(blocks[2][half:], "seq", 2)
    one_low = (blocks[1][half:].astype(F32) + low.astype(F32)).astype(BF16)
    two_up = (blocks[2][:half].astype(F32) + up.astype(F32)).astype(BF16)
    return [blocks[0], (one, shift(one_low, "seq", 1)), (shift(two_up, "seq", 2), two)]


def by_rank(blocks, rank):
    bit = 1
    while bit < len(blocks):
        odd = (rank & bit) != 0
        blocks = [jnp.where(odd, blocks[k ^ bit], blocks[k]) for k in range(len(blocks))]
        bit *= 2
    return blocks


def pick(pieces, at):
    return lax.dynamic_index_in_dim(pieces, at, axis=0, keepdims=False)


def exchange(pieces, rank):
    return scatter_blocks([pick(pieces, rank ^ k) for k in range(pieces.shape[0])])


def small_scatter(pieces, dp_rank, seq_rank):
    total = 0.0
    sent = [lax.dynamic_index_in_dim(pieces, seq_rank ^ k, axis=1, keepdims=False) for k in range(pieces.shape[1])]
    for part in scatter_blocks(sent):
        total = total + part
    sent = [pick(total, dp_rank ^ k) for k in range(pieces.shape[0])]
    total = 0.0
    for part in scatter_blocks(sent, "dp"):
        total = total + part
    return total


def swap_pairs(dp_count, seq_count, sub):
    pairs = []
    for d in range(dp_count):
        for s in range(seq_count):
            source = ((d // sub) * sub + s % sub) * seq_count + (s // sub) * sub + d % sub
            pairs.append((source, d * seq_count + s))
    return pairs


def gather_dp(value):
    return lax.all_gather(value, "dp", axis=0, tiled=True)


def scatter_dp(value):
    return lax.psum_scatter(value, "dp", scatter_dimension=0, tiled=True)


def shards(
    tokens,
    cotangent,
    lengths,
    key_mask,
    attn_gain,
    attn_shift,
    qkv_weight,
    qv_bias,
    proj_weight,
    proj_bias,
    mlp_gain,
    mlp_shift,
    fc_weight,
    fc_bias,
    down_weight,
    down_bias,
):
    _, piece, width = tokens.shape
    dp_count, seq_count = lax.axis_size("dp"), lax.axis_size("seq")
    dp_rank, seq_rank = lax.axis_index("dp"), lax.axis_index("seq")
    own_heads = HEADS // seq_count
    own_width = own_heads * HEAD_DIM
    rows = qkv_weight.shape[0]
    sub = HEAD_DIM // proj_weight.shape[0]
    high = seq_count // sub
    block = down_weight.shape[0]
    rank = jnp.reshape(seq_rank, (1,)).astype(jnp.int32)
    swap = swap_pairs(dp_count, seq_count, sub)
    order = list(range(seq_count - 1, -1, -1))
    if seq_count == 4:
        order = [3, 1, 2, 0]

    in_plane = seq_count == 4 and dp_count == 8
    qkv_pieces = (
        qkv_weight.reshape(rows, 3, own_heads, sub, high, HEAD_DIM)
        .transpose(4, 3, 0, 1, 2, 5)
        .reshape(seq_count, rows, 3 * own_width)
    )
    tokens_own, cot_own = tokens[0], cotangent[0]

    small = (attn_gain, attn_shift, qv_bias, proj_bias, mlp_gain, mlp_shift, fc_bias, down_bias)
    sizes = [item.shape[0] for item in small]
    positions = seq_rank * piece + jnp.arange(piece, dtype=jnp.int32)
    own_flags = ((key_mask[0] == 1) & (positions < lengths[0])).astype(BF16)
    packed = jnp.concatenate(small + (own_flags,))
    fc_pieces = (
        fc_weight.reshape(rows, dp_count, seq_count, block)
        .transpose(2, 0, 1, 3)
        .reshape(seq_count, rows, dp_count * block)
    )
    if in_plane:
        room = -(-packed.shape[0] // 2048) * 2048
        small_rows = jnp.pad(packed, (0, room - packed.shape[0])).reshape(room // 128, 128)
        token_all, qkv_full, fc_rows, small_full = opening(
            tokens_own, qkv_pieces, fc_pieces, small_rows, dp_count
        )
        packed = small_full.reshape(dp_count, seq_count, room)
        flags = lax.dynamic_index_in_dim(packed, dp_rank, axis=0, keepdims=False)
        flags = jnp.concatenate(by_rank([flags[s, sum(sizes) : sum(sizes) + piece] for s in range(seq_count)], seq_rank))
        packed = packed[:, :, : sum(sizes)].astype(F32)
    else:
        qkv_full = gather_dp(jnp.concatenate(by_rank(exchange(qkv_pieces, seq_rank), seq_rank), axis=0))
        blocks = gather_blocks(packed)
        flags = jnp.concatenate([item[-piece:] for item in blocks])
        packed = jnp.stack(by_rank([item[:-piece] for item in blocks], seq_rank))
        packed = jnp.stack(by_rank(gather_blocks(packed, "dp"), dp_rank)).astype(F32)
        fc_rows = jnp.concatenate(by_rank(exchange(fc_pieces, seq_rank), seq_rank), axis=0)
    key_bias = jnp.where(flags > 0, 0.0, NEG).astype(F32)[:, None]
    parts, start = [], 0
    for size in sizes:
        parts.append(packed[:, :, start : start + size])
        start += size
    whole = [part.reshape(1, -1) for part in parts]
    gain_one, shift_one, qv_full, proj_shift, gain_two, shift_two, _, down_shift = whole
    fc_shift = lax.dynamic_index_in_dim(parts[6], seq_rank, axis=1, keepdims=False).reshape(1, -1)
    rank_low, rank_high = seq_rank % sub, seq_rank // sub
    qv_heads = qv_full.reshape(2, own_heads, sub, high, HEAD_DIM)
    qv_own = lax.dynamic_index_in_dim(
        lax.dynamic_index_in_dim(qv_heads, rank_low, axis=2, keepdims=False), rank_high, axis=2, keepdims=False
    )
    qv_own = qv_own.reshape(1, -1)

    length = piece * seq_count
    proj_full = gather_dp(lax.ppermute(proj_weight, BOTH, swap))
    down_full = gather_dp(after(down_weight, fc_rows) if in_plane else down_weight)
    fc_full = gather_dp(fc_rows)
    shared = None
    if in_plane:
        cot_own, token_all = lax.optimization_barrier((cot_own, token_all))
        cots = (shift(cot_own, "seq", 1), shift(cot_own, "seq", 2))
        shared = project(0, token_all, 0, length, gain_one, shift_one, qkv_full, qv_own, length, None)
    else:
        token_blocks = gather_blocks(tokens_own)
        cot_blocks = gather_blocks(after(cot_own, token_blocks[-1]))
        for k in range(seq_count):
            shared = project(k, token_blocks[k], 0, piece, gain_one, shift_one, qkv_full, qv_own, length, shared)
    normed_one, q, keys, values, keys_t, values_t = shared
    if in_plane:
        middle, normed_two, attended, lse, cot_three = attend_plane(
            q, keys, values_t, tokens_own, cots, key_bias, proj_full,
            jnp.concatenate([proj_shift, gain_two, shift_two], axis=0),
        )
    else:
        proj_terms, shared = [None] * seq_count, None
        for k in order:
            proj_terms[k], shared = attend(k, rank, q, keys, values_t, key_bias, proj_full, piece, shared)
        attended, lse = shared
        middle, normed_two = rowwise(
            middle_kernel, scatter_blocks(proj_terms), [tokens_own], [proj_shift, gain_two, shift_two], [F32, BF16], 0
        )

    if in_plane:
        results = feed_plane(normed_two, (cot_own, *cots, cot_three), fc_full, fc_shift, down_full, middle, gain_two)
        grad_middle, low_all, sums_two, hidden_sums, down_terms, grad_fc, grad_down = [
            results[i] for i in (0, 1, 2, 3, 8, 10, 14)
        ]
        grad_fc = scatter_dp(grad_fc)
        grads, qv_sums, block_out = retreat_plane(
            low_all, q, keys, values, keys_t, lse, down_terms, middle, key_bias, proj_full, down_shift
        )
    else:
        normed_blocks = gather_blocks(normed_two)
        grad_terms, shared = [], None
        for k in range(seq_count):
            term, shared = feed(k, normed_blocks[k], cot_blocks[k], fc_full, fc_shift, down_full, seq_count, shared)
            grad_terms.append(term)
        active, grad_hidden, normed_all, cot_all = shared
        grad_middle, grad_mid_low, *sums_two = rowwise(
            middle_back_kernel, scatter_blocks(grad_terms), [middle, cot_own], [gain_two], [F32, BF16], 4
        )
        down_terms = [
            nn(active[k * piece : (k + 1) * piece], down_full).astype(BF16) for k in range(seq_count)
        ]
        low_blocks = gather_blocks(grad_mid_low)
        grad_down = scatter_dp(tn(active, cot_all).astype(BF16))
        grad_fc = scatter_dp(tn(normed_all, grad_hidden).astype(BF16))
        hidden_sums = jnp.sum(grad_hidden.astype(F32), axis=0)
        block_out = rowwise(out_kernel, scatter_blocks(down_terms), [middle], [down_shift], [BF16], 0)[0]
        sums, shared = None, None
        for k in range(seq_count):
            sums, shared = retreat(
                k, rank, low_blocks[k], proj_full, q, lse, keys, values, keys_t, key_bias, sums, shared,
                k == seq_count - 1,
            )
        grad_q, low_all = shared
        grads = jnp.concatenate([grad_q, sums[0], sums[1]], axis=1)
        qv_sums = jnp.stack([jnp.sum(item.astype(F32), axis=0) for item in (grad_q, sums[1])])
    grad_proj = tn(attended, low_all).astype(BF16)
    grad_proj = scatter_dp(after(grad_proj, grad_fc) if in_plane else grad_proj)
    grad_proj = lax.ppermute(grad_proj, BOTH, swap).astype(F32)
    share = attn_gain.shape[0]
    if in_plane:
        tokens_grad, grad_qkv_weight, grad_fc, smalls = closing(
            grads, qkv_full, normed_one, tokens_own, grad_middle, gain_one, sums_two, hidden_sums, qv_sums, grad_fc
        )[:4]
        own = lambda row, size: lax.dynamic_slice_in_dim(smalls[row], seq_rank * size, size)
        late = jnp.concatenate([own(0, share), own(1, share), own(6, 2 * share)])
        early = jnp.concatenate([own(row, share) for row in range(2, 6)] + [smalls[7, :block]])
    else:
        back_terms = [None] * seq_count
        for k in order:
            back_terms[k] = back(k, grads, qkv_full, piece)
        tokens_grad, *sums_one = rowwise(
            tokens_back_kernel, scatter_blocks(back_terms), [tokens_own, grad_middle], [gain_one], [F32], 2
        )

        blocks = exchange(grad_fc.reshape(seq_count, rows, dp_count * block), seq_rank)
        if block % 128 == 0:
            fc_places = lambda s: [(0, d, d * seq_count + s) for d in range(dp_count)]
            grad_fc = lay_out(rank, [[item] for item in blocks], fc_weight.shape[1], (fc_places, block))
        else:
            blocks = [item.reshape(rows, dp_count, block) for item in by_rank(blocks, seq_rank)]
            grad_fc = jnp.stack(blocks, axis=2).reshape(fc_weight.shape).astype(F32)
        grad_qkv = scatter_dp(tn(normed_one, grads).astype(BF16))
        blocks = [[item] for item in exchange(grad_qkv.reshape(seq_count, rows, 3 * own_width), seq_rank)]
        qkv_places = lambda s: [
            (0, part * own_heads + head, part * HEADS + (head * sub + s % sub) * high + s // sub)
            for part in range(3)
            for head in range(own_heads)
        ]
        grad_qkv_weight = lay_out(rank, blocks, qkv_weight.shape[1], (qkv_places, HEAD_DIM))

        def spread(vector):
            return vector.reshape(dp_count, seq_count, -1)

        here = (jnp.arange(seq_count) == seq_rank).astype(F32)
        hidden_sums = hidden_sums.reshape(dp_count, 1, -1) * here[None, :, None]
        early = jnp.concatenate([spread(item) for item in sums_two] + [hidden_sums], axis=2)
        early = small_scatter(early, dp_rank, seq_rank)
        here = (jnp.arange(sub) == rank_low)[:, None] & (jnp.arange(high) == rank_high)[None, :]
        qv_sums = qv_sums.reshape(2, own_heads, 1, 1, HEAD_DIM) * here.astype(F32)[None, None, :, :, None]
        late = jnp.concatenate([spread(item) for item in sums_one] + [spread(qv_sums)], axis=2)
        late = small_scatter(late, dp_rank, seq_rank)
    return (
        block_out[None],
        tokens_grad[None],
        late[:share],
        late[share : 2 * share],
        grad_qkv_weight,
        late[2 * share :],
        grad_proj,
        early[2 * share : 3 * share],
        early[:share],
        early[share : 2 * share],
        grad_fc,
        early[4 * share :],
        grad_down.astype(F32),
        early[3 * share : 4 * share],
    )


def solution(mesh):
    in_specs = (
        P("dp", "seq", None),
        P("dp", "seq", None),
        P("dp"),
        P("dp", "seq"),
        P(BOTH),
        P(BOTH),
        P(BOTH, None),
        P(BOTH),
        P(BOTH, None),
        P(BOTH),
        P(BOTH),
        P(BOTH),
        P(BOTH, None),
        P(BOTH),
        P(BOTH, None),
        P(BOTH),
    )
    out_specs = (
        P("dp", "seq", None),
        P("dp", "seq", None),
        P(BOTH),
        P(BOTH),
        P(BOTH, None),
        P(BOTH),
        P(BOTH, None),
        P(BOTH),
        P(BOTH),
        P(BOTH),
        P(BOTH, None),
        P(BOTH),
        P(BOTH, None),
        P(BOTH),
    )
    return jax.shard_map(shards, mesh=mesh, in_specs=in_specs, out_specs=out_specs, check_vma=False)
```

```python
import functools
import math

import jax
import jax.numpy as jnp
from jax import lax
from jax.experimental import pallas as pl
from jax.experimental.pallas import tpu as pltpu
from jax.sharding import PartitionSpec as P

HEADS = 16
HEAD_DIM = 128
EPS = 1e-05
NEG = -1e30
FACTOR = HEAD_DIM ** (-0.5)
LOG2E = math.log2(math.e)
F32 = jnp.float32
BF16 = jnp.bfloat16
BOTH = ("dp", "seq")
MESH = pl.DeviceIdType.MESH


def nn(left, right):
    return lax.dot_general(left, right, (((1,), (0,)), ((), ())), preferred_element_type=F32)


def nt(left, right):
    return lax.dot_general(left, right, (((1,), (1,)), ((), ())), preferred_element_type=F32)


def tn(left, right):
    return lax.dot_general(left, right, (((0,), (0,)), ((), ())), preferred_element_type=F32)


def params(limit_mib=56):
    return pltpu.CompilerParams(dimension_semantics=("arbitrary",), vmem_limit_bytes=limit_mib * 2**20)


def cost(flops, moved, exps=0):
    return pl.CostEstimate(flops=int(flops), bytes_accessed=int(moved), transcendentals=int(exps))


def call_on_block(kernel, grid, inputs, fresh, shared, previous, scratch, estimate, rank=None, limit_mib=62):
    arrays = [item for item, _ in inputs]
    specs = [spec for _, spec in inputs]
    aliases = {}
    lead = 0 if rank is None else 1
    if previous is not None:
        for at, item in enumerate(previous):
            aliases[lead + len(arrays)] = len(fresh) + at
            arrays.append(item)
            specs.append(pl.BlockSpec(memory_space=pl.ANY))
    count = len(inputs)
    skipped = 0 if previous is None else len(previous)

    def body(*refs):
        refs = list(refs)
        kernel(*refs[: lead + count], *refs[lead + count + skipped :])

    out_specs = [spec for _, spec in fresh] + [spec for _, spec in shared]
    out_shape = [shape for shape, _ in fresh] + [shape for shape, _ in shared]
    if rank is None:
        results = pl.pallas_call(
            body, grid=grid, in_specs=specs, out_specs=out_specs, out_shape=out_shape, scratch_shapes=scratch,
            input_output_aliases=aliases, compiler_params=params(limit_mib), cost_estimate=estimate,
        )(*arrays)
    else:
        results = pl.pallas_call(
            body,
            grid_spec=pltpu.PrefetchScalarGridSpec(
                num_scalar_prefetch=1, grid=grid, in_specs=specs, out_specs=out_specs, scratch_shapes=scratch
            ),
            out_shape=out_shape, input_output_aliases=aliases, compiler_params=params(limit_mib), cost_estimate=estimate,
        )(rank, *arrays)
    return results[: len(fresh)], results[len(fresh) :]


def norm_parts(values):
    average = jnp.mean(values, axis=-1, keepdims=True)
    centred = values - average
    scale = lax.rsqrt(jnp.mean(centred * centred, axis=-1, keepdims=True) + EPS)
    return centred * scale, scale


def norm_backward(normed, scale, gain, upstream):
    weighted = upstream * gain
    return scale * (
        weighted
        - jnp.mean(weighted, axis=-1, keepdims=True)
        - normed * jnp.mean(weighted * normed, axis=-1, keepdims=True)
    )


def project_kernel(x, vectors, wq, wk, wv, normed, q, k, v, k_t, v_t):
    columns = wq.shape[1]
    rows = (norm_parts(x[...].astype(F32))[0] * vectors[0:1, :] + vectors[1:2, :]).astype(BF16)
    normed[...] = rows
    q[...] = (nn(rows, wq[...]) + vectors[7:8, :columns]).astype(BF16)
    keys = nn(rows, wk[...])
    k[...] = keys.astype(BF16)
    k_t[...] = keys.T.astype(BF16)
    values = nn(rows, wv[...]) + vectors[7:8, columns : 2 * columns]
    v[...] = values.astype(BF16)
    v_t[...] = values.T.astype(BF16)


def project(at, x, first, rows_here, vectors, weight, count, previous):
    width, columns = x.shape[1], weight.shape[1] // 3
    tile = min(256, rows_here)
    steps = rows_here // tile
    whole = lambda shape: pl.BlockSpec(shape, lambda i: (0, 0))
    rows = lambda n: pl.BlockSpec((tile, n), lambda i: (at * steps + i, 0))
    turned = pl.BlockSpec((columns, tile), lambda i: (0, at * steps + i))
    inputs = [
        (x, pl.BlockSpec((tile, width), lambda i: (first * steps + i, 0))),
        (vectors, whole(vectors.shape)),
        *[(weight, pl.BlockSpec((width, columns), lambda i, part=part: (0, part))) for part in range(3)],
    ]
    shape = lambda *dims: jax.ShapeDtypeStruct(dims, BF16)
    shared = [(shape(count, width), rows(width))] + [(shape(count, columns), rows(columns))] * 3
    shared += [(shape(columns, count), turned)] * 2
    return call_on_block(
        project_kernel, (steps,), inputs, [], shared, previous, [],
        cost(6 * rows_here * width * columns, 4 * rows_here * width + 6 * width * columns + 10 * rows_here * columns),
    )[1]


def rows_of(block, piece):
    return pl.ds(pl.multiple_of(block * piece, piece), piece)


def scores_of(key_ref, bias_ref, query, rel, piece, diagonal):
    rows = rows_of(rel, piece)
    scores = nt(key_ref[rows, :], query) * (FACTOR * LOG2E)
    key_bias = bias_ref[rows, :]
    if not diagonal:
        return scores + key_bias
    key_at = lax.broadcasted_iota(jnp.int32, scores.shape, 0)
    query_at = lax.broadcasted_iota(jnp.int32, scores.shape, 1)
    allowed = ((key_at < query_at) & (key_bias > -1.0)) | (key_at == query_at)
    return jnp.where(allowed, scores, NEG)


def attend_kernel(at, rank_ref, query_ref, key_ref, value_t, bias_ref, proj_ref, part_ref, attended, lse_ref, score_ref, sum_ref):
    piece = query_ref.shape[0]
    rank = rank_ref[0]
    head = pl.program_id(0)
    true = lax.bitwise_xor(at, rank)
    query = query_ref[...]

    def first(block, top):
        scores = scores_of(key_ref, bias_ref, query, lax.bitwise_xor(block, rank), piece, False)
        score_ref[rows_of(block, piece), :] = scores
        return jnp.maximum(top, jnp.max(scores, axis=0, keepdims=True))

    last = scores_of(key_ref, bias_ref, query, at, piece, True)
    top = lax.fori_loop(0, true, first, jnp.max(last, axis=0, keepdims=True))

    def weigh(scores, rel):
        weights = jnp.exp2(scores - top)
        return jnp.sum(weights, axis=0, keepdims=True), nn(value_t[:, rows_of(rel, piece)], weights.astype(BF16))

    def second(block, carry):
        total, out = carry
        more, part = weigh(score_ref[rows_of(block, piece), :], lax.bitwise_xor(block, rank))
        return total + more, out + part

    total, out = lax.fori_loop(0, true, second, weigh(last, at))
    result = (out / total).T.astype(BF16)
    attended[...] = result
    lse_ref[0] = top + jnp.log2(total)
    term = nn(result, proj_ref[...])

    @pl.when(head == 0)
    def _():
        sum_ref[...] = term

    @pl.when(head > 0)
    def _():
        sum_ref[...] += term

    @pl.when(head == pl.num_programs(0) - 1)
    def _():
        part_ref[...] = sum_ref[...].astype(BF16)


def attend(at, rank, q, k, v_t, key_bias, proj, piece, previous):
    length, columns = q.shape
    heads, width = columns // HEAD_DIM, proj.shape[1]
    inputs = [
        (q, pl.BlockSpec((piece, HEAD_DIM), lambda h, r: (at, h))),
        (k, pl.BlockSpec((length, HEAD_DIM), lambda h, r: (0, h))),
        (v_t, pl.BlockSpec((HEAD_DIM, length), lambda h, r: (h, 0))),
        (key_bias, pl.BlockSpec((length, 1), lambda h, r: (0, 0))),
        (proj, pl.BlockSpec((HEAD_DIM, width), lambda h, r: (h, 0))),
    ]
    fresh = [(jax.ShapeDtypeStruct((piece, width), BF16), pl.BlockSpec((piece, width), lambda h, r: (0, 0)))]
    shared = [
        (jax.ShapeDtypeStruct((length, columns), BF16), pl.BlockSpec((piece, HEAD_DIM), lambda h, r: (at, h))),
        (jax.ShapeDtypeStruct((heads, 1, length), F32), pl.BlockSpec((1, 1, piece), lambda h, r: (h, 0, at))),
    ]
    scratch = [pltpu.VMEM((length, piece), F32), pltpu.VMEM((piece, width), F32)]
    (part,), shared = call_on_block(
        functools.partial(attend_kernel, at), (heads,), inputs, fresh, shared, previous, scratch,
        cost(
            2 * length * piece * columns * 1.3 + 2 * piece * columns * width, 6 * length * columns + 2 * width * columns,
            heads * length * piece * 0.6,
        ), rank,
    )
    return part, shared


def feed_kernel(normed, cot, fc, bias, down, part, active_out, hidden_out, normed_out, cot_out, sum_ref):
    step = pl.program_id(0)
    weights = fc[...]
    hidden = nn(normed[...], weights) + bias[...]
    grad_active = nt(cot[...], down[...])
    inner = math.sqrt(2 / math.pi) * (hidden + 0.044715 * (hidden * hidden * hidden))
    bent = jnp.tanh(inner)
    half = 0.5 * (1.0 + bent)
    active_out[...] = (hidden * half).astype(BF16)
    slope = half + (0.5 * hidden) * (1.0 - bent * bent) * (
        math.sqrt(2 / math.pi) * (1.0 + (3 * 0.044715) * (hidden * hidden))
    )
    grad_hidden = (grad_active * slope).astype(BF16)
    hidden_out[...] = grad_hidden
    term = nt(grad_hidden, weights)

    @pl.when(step == 0)
    def _():
        sum_ref[...] = term
        normed_out[...] = normed[...]
        cot_out[...] = cot[...]

    @pl.when(step > 0)
    def _():
        sum_ref[...] += term

    @pl.when(step == pl.num_programs(0) - 1)
    def _():
        part[...] = sum_ref[...].astype(BF16)


def feed(at, normed, cot, fc, bias, down, count, previous):
    piece, width = normed.shape
    inner = fc.shape[1]
    tile = min(512, inner)
    length = piece * count
    rows = pl.BlockSpec((piece, width), lambda j: (0, 0))
    inputs = [
        (normed, rows),
        (cot, rows),
        (fc, pl.BlockSpec((width, tile), lambda j: (0, j))),
        (bias, pl.BlockSpec((1, tile), lambda j: (0, j))),
        (down, pl.BlockSpec((tile, width), lambda j: (j, 0))),
    ]
    shape = lambda n: jax.ShapeDtypeStruct((length, n), BF16)
    columns = pl.BlockSpec((piece, tile), lambda j: (at, j))
    here = pl.BlockSpec((piece, width), lambda j: (at, 0))
    fresh = [(jax.ShapeDtypeStruct((piece, width), BF16), rows)]
    shared = [(shape(inner), columns), (shape(inner), columns), (shape(width), here), (shape(width), here)]
    (part,), shared = call_on_block(
        feed_kernel, (inner // tile,), inputs, fresh, shared, previous, [pltpu.VMEM((piece, width), F32)],
        cost(6 * piece * width * inner, 4 * width * inner + 10 * piece * width + 4 * piece * inner, piece * inner),
    )
    return part, shared


def retreat_kernel(
    at, first_call, last_call, rank_ref, low_ref, proj_ref, query_ref, lse_ref, key_ref, value_ref, key_t, bias_ref, *rest
):
    rest = list(rest)
    key_in, value_in = (None, None) if first_call else (rest.pop(0), rest.pop(0))
    key_out, value_out, query_out, low_out, prob_ref, chance_ref, key_sum, value_sum = rest
    piece = query_ref.shape[0]
    rank = rank_ref[0]
    true = lax.bitwise_xor(at, rank)

    @pl.when(pl.program_id(0) == 0)
    def _():
        low_out[...] = low_ref[...]

    if first_call:
        key_sum[...] = jnp.zeros_like(key_sum)
        value_sum[...] = jnp.zeros_like(value_sum)
    else:
        key_sum[...] = key_in[...]
        value_sum[...] = value_in[...]
    query, lse = query_ref[...], lse_ref[0]
    grad = nt(low_ref[...], proj_ref[...]).astype(BF16)

    def measure(scores, rel):
        rows = rows_of(rel, piece)
        probs = jnp.exp2(scores - lse)
        grad_chances = nt(value_ref[rows, :], grad)
        value_sum[rows, :] += nn(probs.astype(BF16), grad)
        prob_ref[rows, :] = probs
        chance_ref[rows, :] = grad_chances
        return jnp.sum(probs * grad_chances, axis=0, keepdims=True)

    def first(block, weighted):
        rel = lax.bitwise_xor(block, rank)
        return weighted + measure(scores_of(key_ref, bias_ref, query, rel, piece, False), rel)

    last = scores_of(key_ref, bias_ref, query, at, piece, True)
    weighted = lax.fori_loop(0, true, first, measure(last, at))

    def second(block, total):
        rows = rows_of(lax.bitwise_xor(block, rank), piece)
        grad_scores = (prob_ref[rows, :] * (chance_ref[rows, :] - weighted)).astype(BF16)
        key_sum[rows, :] += nn(grad_scores, query)
        return total + nn(key_t[:, rows], grad_scores)

    total = lax.fori_loop(0, true + 1, second, jnp.zeros((HEAD_DIM, piece), F32))
    query_out[...] = (total * FACTOR).T.astype(BF16)
    if last_call:
        key_out[...] = (key_sum[...] * FACTOR).astype(BF16)
        value_out[...] = value_sum[...].astype(BF16)
    else:
        key_out[...] = key_sum[...]
        value_out[...] = value_sum[...]


def retreat(at, rank, low, proj, q, lse, k, v, k_t, key_bias, sums, previous, last_call):
    length, columns = q.shape
    piece, width = low.shape
    heads = columns // HEAD_DIM
    tall = pl.BlockSpec((length, HEAD_DIM), lambda h, r: (0, h))
    part = pl.BlockSpec((piece, HEAD_DIM), lambda h, r: (at, h))
    inputs = [
        (low, pl.BlockSpec((piece, width), lambda h, r: (0, 0))),
        (proj, pl.BlockSpec((HEAD_DIM, width), lambda h, r: (h, 0))),
        (q, part),
        (lse, pl.BlockSpec((1, 1, piece), lambda h, r: (h, 0, at))),
        (k, tall),
        (v, tall),
        (k_t, pl.BlockSpec((HEAD_DIM, length), lambda h, r: (h, 0))),
        (key_bias, pl.BlockSpec((length, 1), lambda h, r: (0, 0))),
    ]
    if sums is not None:
        inputs += [(item, tall) for item in sums]
    kind = BF16 if last_call else F32
    fresh = [(jax.ShapeDtypeStruct((length, columns), kind), tall)] * 2
    shared = [
        (jax.ShapeDtypeStruct((length, columns), BF16), part),
        (jax.ShapeDtypeStruct((length, width), BF16), pl.BlockSpec((piece, width), lambda h, r: (at, 0))),
    ]
    scratch = [pltpu.VMEM((length, piece), F32)] * 2 + [pltpu.VMEM((length, HEAD_DIM), F32)] * 2
    return call_on_block(
        functools.partial(retreat_kernel, at, sums is None, last_call), (heads,), inputs, fresh, shared, previous,
        scratch,
        cost(
            5 * 1.3 * length * piece * columns + 2 * piece * columns * width, 20 * length * columns,
            heads * length * piece * 0.6,
        ), rank,
    )


def back_kernel(grads, weight, out):
    out[...] = nt(grads[...], weight[...]).astype(BF16)


def back(at, grads, weight, piece):
    columns, width = grads.shape[1], weight.shape[0]
    tile = min(512, width)
    return pl.pallas_call(
        back_kernel,
        grid=(width // tile,),
        in_specs=[
            pl.BlockSpec((piece, columns), lambda j: (at, 0)),
            pl.BlockSpec((tile, columns), lambda j: (j, 0)),
        ],
        out_specs=pl.BlockSpec((piece, tile), lambda j: (0, j)),
        out_shape=jax.ShapeDtypeStruct((piece, width), BF16),
        compiler_params=params(),
        cost_estimate=cost(2 * piece * width * columns, 2 * width * columns + 2 * piece * (columns + width)),
    )(grads, weight)


def part_specs(parts, tile, steps, width):
    arrays, specs = [], []
    for part in parts:
        if isinstance(part, tuple):
            middle = steps // 2
            arrays += list(part)
            specs.append(pl.BlockSpec((tile, width), lambda i: (jnp.minimum(i, middle - 1), 0)))
            specs.append(pl.BlockSpec((tile, width), lambda i: (jnp.maximum(i - middle, 0), 0)))
        else:
            arrays.append(part)
            specs.append(pl.BlockSpec((tile, width), lambda i: (i, 0)))
    return arrays, specs


def add_parts(kinds, refs):
    total = None
    upper = pl.program_id(0) < pl.num_programs(0) // 2
    for kind in kinds:
        if kind:
            high, low = refs.pop(0)[...], refs.pop(0)[...]
            term = jnp.where(upper, high.astype(F32), low.astype(F32))
        else:
            term = refs.pop(0)[...].astype(F32)
        total = term if total is None else total + term
    return total


def rowwise(kernel, parts, rows, vectors, outputs, sums):
    count, width = rows[0].shape
    tile = min(128, count // 2)
    steps = count // tile
    arrays, specs = part_specs(parts, tile, steps, width)
    kinds = [isinstance(part, tuple) for part in parts]
    specs += [pl.BlockSpec((tile, width), lambda i: (i, 0))] * len(rows)
    specs += [pl.BlockSpec((1, width), lambda i: (0, 0))] * len(vectors)

    def body(*refs):
        refs = list(refs)
        total = add_parts(kinds, refs)
        tiles = [refs.pop(0)[...] for _ in rows]
        given = [refs.pop(0)[...] for _ in vectors]
        results = kernel(total, tiles, given)
        for result, _ in zip(results, outputs):
            refs.pop(0)[...] = result
        for result in results[len(outputs) :]:
            ref = refs.pop(0)
            column = jnp.sum(result, axis=0, keepdims=True)

            @pl.when(pl.program_id(0) == 0)
            def _():
                ref[...] = column

            @pl.when(pl.program_id(0) > 0)
            def _():
                ref[...] += column

    return pl.pallas_call(
        body,
        grid=(steps,),
        in_specs=specs,
        out_specs=[pl.BlockSpec((tile, width), lambda i: (i, 0))] * len(outputs)
        + [pl.BlockSpec((1, width), lambda i: (0, 0))] * sums,
        out_shape=[jax.ShapeDtypeStruct((count, width), kind) for kind in outputs]
        + [jax.ShapeDtypeStruct((1, width), F32)] * sums,
        compiler_params=params(),
        cost_estimate=cost(20 * count * width, count * width * (2 * len(arrays) + 4 * len(rows) + 4 * len(outputs))),
    )(*arrays, *rows, *vectors)


def middle_kernel(total, rows, vectors):
    (tokens,), (bias, gain, shift_) = rows, vectors
    middle = tokens.astype(F32) + (total + bias)
    return middle, (norm_parts(middle)[0] * gain + shift_).astype(BF16)


def out_kernel(total, rows, vectors):
    return (((rows[0] + (total + vectors[0])).astype(BF16)),)


def middle_back_kernel(total, rows, vectors):
    (middle, cot), (gain,) = rows, vectors
    normed, scale = norm_parts(middle)
    cot = cot.astype(F32)
    grad = cot + norm_backward(normed, scale, gain, total)
    low = grad.astype(BF16)
    return grad, low, total * normed, total, low.astype(F32), cot


def tokens_back_kernel(total, rows, vectors):
    (tokens, grad_middle), (gain,) = rows, vectors
    normed, scale = norm_parts(tokens.astype(F32))
    return grad_middle + norm_backward(normed, scale, gain, total), total * normed, total


def lay_out(rank, blocks, width, places):
    rows = blocks[0][0].shape[0]
    count, each = len(blocks), len(blocks[0])
    unit = places[1]

    def body(rank_ref, *refs):
        out = refs[-1]
        for k in range(count):
            source = lax.bitwise_xor(k, rank_ref[0])
            for array, column, target in places[0](source):
                out[:, pl.ds(pl.multiple_of(target * unit, unit), unit)] = refs[k * each + array][
                    :, column * unit : (column + 1) * unit
                ].astype(F32)

    arrays = [item for block in blocks for item in block]
    return pl.pallas_call(
        body,
        grid_spec=pltpu.PrefetchScalarGridSpec(
            num_scalar_prefetch=1,
            grid=(1,),
            in_specs=[pl.BlockSpec(item.shape, lambda i, r: (0, 0)) for item in arrays],
            out_specs=pl.BlockSpec((rows, width), lambda i, r: (0, 0)),
        ),
        out_shape=jax.ShapeDtypeStruct((rows, width), F32),
        compiler_params=params(),
        cost_estimate=cost(rows * width, 6 * rows * width),
    )(rank, *arrays)


def neighbours():
    rank = lax.axis_index("seq")
    return rank + 1 - 2 * lax.rem(rank, 2), rank + 2 - 4 * lax.rem(lax.div(rank, 2), 2)


def remote(source, target, send, receive, axis, device):
    return pltpu.make_async_remote_copy(
        src_ref=source, dst_ref=target, send_sem=send, recv_sem=receive, device_id={axis: device}, device_id_type=MESH
    )


def greet(axis, device):
    pl.semaphore_signal(pltpu.get_barrier_semaphore(), inc=1, device_id={axis: device}, device_id_type=MESH)


def flip(first, second):
    low = lax.rem(first + second, 2)
    high = lax.rem(lax.div(first, 2) + lax.div(second, 2), 2)
    return 2 * high + low


class LevelScatter:
    def __init__(self, source, mate_in, summed, got, send, receive):
        self.source, self.mate_in, self.summed, self.got = source, mate_in, summed, got
        self.send, self.receive = send, receive
        self.rows = mate_in.shape[0] // 4
        self.place = lax.axis_index("dp")
        self.level, self.core = lax.div(self.place, 2), lax.rem(self.place, 2)
        self.mate = self.place + 1 - 2 * self.core

    def greet(self):
        greet("dp", self.mate)
        count = jnp.int32(1)
        for step in (1, 2):
            up, down = self.level + step <= 3, self.level >= step
            pl.when(up)(lambda step=step: greet("dp", self.place + 2 * step))
            pl.when(down)(lambda step=step: greet("dp", self.place - 2 * step))
            count = count + up.astype(jnp.int32) + down.astype(jnp.int32)
        return count

    def block(self, ref, at):
        return ref.at[pl.ds(at * self.rows, self.rows)]

    def swaps(self):
        return [
            remote(
                self.block(self.source, 2 * at + 1 - self.core), self.block(self.mate_in, at),
                self.send.at[at], self.receive.at[at], "dp", self.mate,
            )
            for at in range(4)
        ]

    def start(self):
        for item in self.swaps():
            item.start()

    def add(self, first, second, out, grid, first_at, second_at, out_at):
        def body(left, right, total):
            total[...] = (left[...].astype(F32) + right[...].astype(F32)).astype(total.dtype)

        spec = lambda at: pl.BlockSpec((self.rows, first.shape[1]), lambda i: (at(i), 0))
        pltpu.emit_pipeline(
            body, grid=(grid,), in_specs=[spec(first_at), spec(second_at)], out_specs=[spec(out_at)]
        )(first, second, out)

    def hop(self, at, slot, index, steps):
        return remote(
            self.block(self.summed, at), self.block(self.got, slot), self.send.at[4 + index], self.receive.at[4 + slot],
            "dp", self.place + 2 * steps,
        )

    def hops(self):
        level = self.level
        return [
            (level == 0, self.hop(3, 3, 0, 1)),
            (level == 3, self.hop(0, 3, 0, -1)),
            (level == 0, self.hop(2, 2, 1, 2)),
            (level == 3, self.hop(1, 2, 1, -2)),
            (level <= 2, self.hop(lax.rem(level + 1, 4), 0, 2, 1)),
            (level >= 1, self.hop(lax.rem(level + 3, 4), 1, 3, -1)),
        ]

    def passes(self):
        return [(self.level == 1, self.hop(3, 2, 1, 2)), (self.level == 2, self.hop(0, 2, 1, -2))]

    def spread(self):
        for item in self.swaps():
            item.wait_recv()
        self.add(
            self.source, self.mate_in, self.summed, 4, lambda i: 2 * i + self.core, lambda i: i, lambda i: i
        )
        for condition, copy in self.hops():
            pl.when(condition)(lambda copy=copy: copy.start())

    def arrive(self, slot):
        here = self.block(self.got, slot)
        remote(here, here, self.send.at[0], self.receive.at[4 + slot], "dp", self.mate).wait_recv()

    def pass_on(self):
        for level, at in ((1, 3), (2, 0)):

            @pl.when(self.level == level)
            def _(at=at):
                self.arrive(3)
                self.add(self.summed, self.got, self.summed, 1, lambda i: at, lambda i: 3, lambda i: at)

        for condition, copy in self.passes():
            pl.when(condition)(lambda copy=copy: copy.start())

    def finish(self, out):
        level = self.level
        pl.when(level >= 1)(lambda: self.arrive(0))
        pl.when(level <= 2)(lambda: self.arrive(1))
        self.arrive(2)
        rows = min(64, self.rows)

        def body(own, mate, below, above, far, total):
            value = own[...].astype(F32) + mate[...].astype(F32) + far[...].astype(F32)
            below_term, above_term = below[...].astype(F32), above[...].astype(F32)
            value = value + jnp.where(level >= 1, below_term, 0.0) + jnp.where(level <= 2, above_term, 0.0)
            total[...] = value.astype(total.dtype)

        steps = self.rows // rows
        spec = lambda at: pl.BlockSpec((rows, out.shape[1]), lambda i: (at * steps + i, 0))
        pltpu.emit_pipeline(
            body,
            grid=(steps,),
            in_specs=[spec(self.place), spec(level), spec(0), spec(1), spec(2)],
            out_specs=[spec(0)],
        )(self.source, self.mate_in, self.got, self.got, self.got, out)

    def close(self):
        for item in self.swaps():
            item.wait_send()
        for condition, copy in self.hops() + self.passes():
            pl.when(condition)(lambda copy=copy: copy.wait_send())


class NearScatter(LevelScatter):
    def part(self, ref, at):
        return ref[pl.ds(pl.multiple_of(at * self.rows, self.rows), self.rows), :].astype(F32)

    def spread(self):
        for item in self.swaps():
            item.wait_recv()
        for at in range(4):
            total = self.part(self.source, 2 * at + self.core) + self.part(self.mate_in, at)
            self.summed[at * self.rows : (at + 1) * self.rows, :] = total.astype(BF16)
        for condition, copy in self.hops():
            pl.when(condition)(lambda copy=copy: copy.start())

    def pass_on(self):
        for level, at in ((1, 3), (2, 0)):

            @pl.when(self.level == level)
            def _(at=at):
                self.arrive(3)
                total = self.part(self.summed, at) + self.part(self.got, 3)
                self.summed[at * self.rows : (at + 1) * self.rows, :] = total.astype(BF16)

        for condition, copy in self.passes():
            pl.when(condition)(lambda copy=copy: copy.start())

    def finish(self, out):
        level = self.level
        pl.when(level >= 1)(lambda: self.arrive(0))
        pl.when(level <= 2)(lambda: self.arrive(1))
        self.arrive(2)
        value = self.part(self.source, self.place) + self.part(self.mate_in, level) + self.part(self.got, 2)
        value = value + jnp.where(level >= 1, self.part(self.got, 0), 0.0)
        value = value + jnp.where(level <= 2, self.part(self.got, 1), 0.0)
        out[...] = value.astype(BF16)


class LevelGather:
    def __init__(self, own, full, send, receive, mate_send, mate_receive):
        self.own, self.full, self.send, self.receive = own, full, send, receive
        self.mate_send, self.mate_receive = mate_send, mate_receive
        self.rows = own.shape[0]
        self.place = lax.axis_index("dp")
        self.level, self.core = lax.div(self.place, 2), lax.rem(self.place, 2)
        self.mate = self.place + 1 - 2 * self.core

    greet = LevelScatter.greet

    def shard(self, level):
        return self.full.at[pl.ds((2 * level + self.core) * self.rows, self.rows)]

    def hop(self, index, steps, slot):
        return remote(
            self.own, self.shard(self.level), self.send.at[index], self.receive.at[slot], "dp", self.place + 2 * steps
        )

    def near(self):
        return [(self.level <= 2, self.hop(0, 1, 0)), (self.level >= 1, self.hop(1, -1, 1))]

    def second(self):
        inner = (self.level == 1) | (self.level == 2)
        lower, upper = self.shard(self.level - 1), self.shard(self.level + 1)
        return [
            (inner, remote(lower, lower, self.send.at[2], self.receive.at[2], "dp", self.place + 2)),
            (inner, remote(upper, upper, self.send.at[3], self.receive.at[2], "dp", self.place - 2)),
        ]

    def passes(self):
        first, last = self.shard(0), self.shard(3)
        return [
            (self.level == 2, remote(first, first, self.send.at[4], self.receive.at[3], "dp", self.place + 2)),
            (self.level == 1, remote(last, last, self.send.at[4], self.receive.at[3], "dp", self.place - 2)),
        ]

    def across(self, index, level):
        here = self.own if index == 4 else self.shard(level)
        return remote(here, self.shard(level), self.mate_send.at[index], self.mate_receive.at[index], "dp", self.mate)

    def arrivals(self, slots):
        level = self.level
        two_away = level + 2 - 4 * lax.div(level, 2)
        every = [
            (level >= 1, 0, level - 1),
            (level <= 2, 1, level + 1),
            (level >= 0, 2, two_away),
            ((level == 0) | (level == 3), 3, 3 - level),
        ]
        return [item for item in every if item[1] in slots]

    def start(self, hops):
        for condition, copy in hops:
            pl.when(condition)(lambda copy=copy: copy.start())

    def take(self, slots):
        for condition, slot, level in self.arrivals(slots):

            @pl.when(condition)
            def _(slot=slot, level=level):
                here = self.shard(level)
                remote(here, here, self.send.at[0], self.receive.at[slot], "dp", self.mate).wait_recv()
                self.across(slot, level).start()

    def finish(self, slots, hops):
        for condition, slot, level in self.arrivals(slots):
            pl.when(condition)(lambda slot=slot, level=level: self.across(slot, level).wait())
        for condition, copy in hops:
            pl.when(condition)(lambda copy=copy: copy.wait_send())


def opening_kernel(
    tokens, cot, qkv_weight, fc_weight, small, down, proj,
    token_all, qkv_full, fc_rows, cot_one, cot_two, down_full, proj_full, vectors, key_bias,
    qkv_pieces, fc_pieces, token_buf, qkv_rows, small_rows, small_full, proj_rows, square, local, send, receive, up_send, up_receive, down_send, down_receive, mate_send, mate_receive,
    level_send, level_receive, level_mate_send, level_mate_receive,
):
    piece = tokens.shape[0]
    half = piece // 2
    gather = LevelGather(down, down_full, level_send, level_receive, level_mate_send, level_mate_receive)
    me, place = lax.axis_index("seq"), lax.axis_index("dp")
    one, two = neighbours()
    three = 3 - me
    stages = lax.axis_size("dp") // 2
    level, core = lax.div(place, 2), lax.rem(place, 2)
    mate = place + 1 - 2 * core
    above, below = level < stages - 1, level > 0

    for device in (one, two, three):
        greet("seq", device)
    greet("dp", mate)
    pl.when(above)(lambda: greet("dp", place + 2))
    pl.when(below)(lambda: greet("dp", place - 2))
    swaps = core != lax.rem(me, 2)
    partner = {"dp": mate, "seq": one}

    @pl.when(swaps)
    def _():
        pl.semaphore_signal(pltpu.get_barrier_semaphore(), inc=1, device_id=partner, device_id_type=MESH)

    heads = qkv_pieces.shape[2] // (3 * HEAD_DIM)
    for rank in range(4):
        for part in range(3):
            for head in range(heads):
                source = (part * HEADS + (head * 2 + rank % 2) * 2 + rank // 2) * HEAD_DIM
                target = (part * heads + head) * HEAD_DIM
                qkv_pieces[rank, :, target : target + HEAD_DIM] = qkv_weight[:, source : source + HEAD_DIM]
    count = 4 + above.astype(jnp.int32) + below.astype(jnp.int32) + swaps.astype(jnp.int32)
    pl.semaphore_wait(pltpu.get_barrier_semaphore(), count)

    def block(ref, at, start=0, size=piece):
        return ref.at[pl.ds(at * piece + start, size)]

    def spread(pieces, target, at):
        rows = target.shape[0] // 4
        mine = target.at[pl.ds(me * rows, rows)]
        source = lambda device: pieces if pieces is small else pieces.at[device]
        copies = [
            remote(source(device), mine, send.at[at + i], receive.at[at + i], "seq", device)
            for i, device in enumerate((one, two, three))
        ]
        return copies, source(me), mine

    qkv_copies, qkv_own, qkv_mine = spread(qkv_pieces, qkv_rows, 0)
    small_copies, small_own, small_mine = spread(small, small_rows, 3)
    fc_copies, fc_own, fc_mine = spread(fc_pieces, fc_rows, 6)
    token_one = remote(tokens, block(token_all, 1), send.at[9], receive.at[9], "seq", one)
    token_two = remote(tokens, block(token_all, 2), send.at[10], receive.at[10], "seq", two)
    token_three = (
        remote(block(token_all, 1, 0, half), block(token_all, 3, 0, half), send.at[11], receive.at[11], "seq", two),
        remote(block(token_all, 2, half, half), block(token_all, 3, half, half), send.at[12], receive.at[12], "seq", one),
    )
    first_kept = [pltpu.make_async_copy(qkv_own, qkv_mine, local.at[0]), pltpu.make_async_copy(small_own, small_mine, local.at[1])]
    later_kept = [
        pltpu.make_async_copy(fc_own, fc_mine, local.at[2]),
        pltpu.make_async_copy(token_buf, block(token_all, 0), local.at[3]),
    ]
    token_load = pltpu.make_async_copy(tokens, token_buf, local.at[4])
    cot_copies = (
        remote(cot.at[pl.ds(0, half)], cot_one, send.at[13], receive.at[13], "seq", one),
        remote(cot.at[pl.ds(0, half)], cot_two, send.at[14], receive.at[14], "seq", two),
    )

    proj_copy = pltpu.make_async_remote_copy(
        src_ref=proj, dst_ref=proj_rows, send_sem=send.at[15], recv_sem=receive.at[15], device_id=partner,
        device_id_type=MESH,
    )
    chains = ((qkv_rows, qkv_full), (small_rows, small_full), (proj_rows, proj_full))

    def shard(array, at):
        rows = chains[array][0].shape[0]
        return chains[array][1].at[pl.ds((2 * at + core) * rows, rows)]

    def rising(array, step, device):
        at = level - (step - 1)
        source = chains[array][0] if step == 1 else shard(array, at)
        return remote(source, shard(array, at), up_send.at[array, step - 1], up_receive.at[array, step - 1], "dp", device)

    def falling(array, step, device):
        at = level + (step - 1)
        source = chains[array][0] if step == 1 else shard(array, at)
        return remote(source, shard(array, at), down_send.at[array, step - 1], down_receive.at[array, step - 1], "dp", device)

    def across(array, index, at):
        source = chains[array][0] if index == 0 else shard(array, at)
        return remote(source, shard(array, at), mate_send.at[array, index], mate_receive.at[array, index], "dp", mate)

    rises = lambda step: above & (level >= step - 1)
    falls = lambda step: below & (level <= stages - step)
    from_below = lambda step: level >= step
    from_above = lambda step: level + step <= stages - 1

    def relay(step):
        @pl.when(rises(step))
        def _():
            for array in (1, 0, 2):
                rising(array, step, place + 2).start()

        @pl.when(falls(step))
        def _():
            for array in (1, 0, 2):
                falling(array, step, place - 2).start()

    def take(step):
        @pl.when(from_below(step))
        def _():
            for array in (1, 0, 2):
                got = shard(array, level - step)
                remote(got, got, up_send.at[array, step - 1], up_receive.at[array, step - 1], "dp", mate).wait_recv()
                across(array, step, level - step).start()

        @pl.when(from_above(step))
        def _():
            for array in (1, 0, 2):
                got = shard(array, level + step)
                remote(got, got, down_send.at[array, step - 1], down_receive.at[array, step - 1], "dp", mate).wait_recv()
                across(array, stages - 1 + step, level + step).start()

    for copy in qkv_copies + small_copies + first_kept:
        copy.start()
    pl.when(swaps)(proj_copy.start)

    @pl.when(jnp.logical_not(swaps))
    def _():
        proj_rows[...] = proj[...]

    token_one.start()
    token_two.start()
    gather.start(gather.near())
    gather.across(4, level).start()
    down_kept = pltpu.make_async_copy(down, gather.shard(level), local.at[8])
    down_kept.start()
    token_load.start()
    inner = fc_pieces.shape[2] // 8
    for rank in range(4):
        for d in range(8):
            source = (d * 4 + rank) * inner
            fc_pieces[rank, :, d * inner : (d + 1) * inner] = fc_weight[:, source : source + inner]
    token_load.wait()
    for copy in qkv_copies + small_copies:
        copy.wait_recv()
    pl.when(swaps)(proj_copy.wait_recv)
    for copy in first_kept:
        copy.wait()
    relay(1)
    own_full = [pltpu.make_async_copy(chains[array][0], shard(array, level), local.at[5 + array]) for array in range(3)]
    for array in range(3):
        across(array, 0, level).start()
        own_full[array].start()
    for copy in fc_copies + later_kept:
        copy.start()
    take(1)
    relay(2)
    take(2)
    relay(3)
    gather.take((0, 1))
    token_one.wait_recv()
    token_two.wait_recv()
    for copy in token_three:
        copy.start()
    for copy in cot_copies:
        copy.start()
    take(3)
    for copy in later_kept + own_full:
        copy.wait()
    for copy in fc_copies:
        copy.wait_recv()
    for copy in qkv_copies + small_copies + fc_copies:
        copy.wait_send()
    token_one.wait_send()
    token_two.wait_send()
    for step in range(1, stages):

        @pl.when(rises(step))
        def _(step=step):
            for array in range(3):
                rising(array, step, place + 2).wait_send()

        @pl.when(falls(step))
        def _(step=step):
            for array in range(3):
                falling(array, step, place - 2).wait_send()

        @pl.when(from_below(step))
        def _(step=step):
            for array in range(3):
                across(array, step, level - step).wait()

        @pl.when(from_above(step))
        def _(step=step):
            for array in range(3):
                across(array, stages - 1 + step, level + step).wait()

    for array in range(3):
        across(array, 0, level).wait()
    for copy in token_three:
        copy.wait()
    down_kept.wait()
    pl.when(swaps)(proj_copy.wait_send)
    tile = lambda d, s: small_full[pl.ds(pl.multiple_of((d * 4 + s) * 16, 16), 16), :].astype(F32)
    vectors[...] = jnp.zeros_like(vectors)
    for d in range(8):
        for pair in range(2):
            both = tile(d, 2 * pair) + tile(d, 2 * pair + 1)
            vectors[0:6, (2 * d + pair) * 128 : (2 * d + pair + 1) * 128] = both[0:6]
        own = tile(d, me)
        for i in range(2):
            vectors[6:7, (2 * d + i) * 128 : (2 * d + i + 1) * 128] = own[7 + i : 8 + i]
        bias = tile(d, 2 * lax.rem(me, 2) + lax.div(me, 2))
        vectors[7:8, d * HEAD_DIM : (d + 1) * HEAD_DIM] = bias[6:7]
    square[...] = jnp.zeros_like(square)
    for i in range(4):
        square[4 * i : 4 * i + 4, :] = tile(place, flip(me, i))[9:13]
    turned = square[...].T
    lane = lax.broadcasted_iota(jnp.int32, turned.shape, 1)
    for i in range(16):
        flag = jnp.sum(jnp.where(lane == i, turned, 0.0), axis=1, keepdims=True)
        key_bias[i * 128 : (i + 1) * 128, :] = jnp.where(flag > 0, 0.0, NEG)
    for copy in cot_copies:
        copy.wait()
    gather.finish((0, 1), gather.near())
    gather.across(4, level).wait()


def opening(tokens, cot, qkv_weight, fc_weight, small, down, proj, dp_count):
    piece, width = tokens.shape
    steps = dp_count // 2 - 1
    anywhere = pl.BlockSpec(memory_space=pltpu.HBM)
    shape = lambda rows, columns: jax.ShapeDtypeStruct((rows, columns), BF16)
    dma = pltpu.SemaphoreType.DMA
    inside = pl.BlockSpec(memory_space=pltpu.VMEM)
    own_rows, columns, inner = qkv_weight.shape[0], qkv_weight.shape[1] // 4, fc_weight.shape[1] // 4
    rows, fine = 4 * own_rows, 4 * small.shape[0]
    return pl.pallas_call(
        opening_kernel,
        in_specs=[anywhere] * 2 + [inside] * 5,
        out_specs=[anywhere] * 7 + [inside] * 2,
        out_shape=[
            shape(4 * piece, width),
            shape(rows * dp_count, columns),
            shape(rows, inner),
            shape(piece // 2, width),
            shape(piece // 2, width),
            shape(down.shape[0] * dp_count, width),
            shape(proj.shape[0] * dp_count, width),
            jax.ShapeDtypeStruct((8, width), F32),
            jax.ShapeDtypeStruct((4 * piece, 1), F32),
        ],
        scratch_shapes=[
            pltpu.VMEM((4, own_rows, columns), BF16), pltpu.VMEM((4, own_rows, inner), BF16),
            pltpu.VMEM((piece, width), BF16),
            pltpu.VMEM((rows, columns), BF16), pltpu.VMEM((fine, 128), BF16), pltpu.VMEM((fine * dp_count, 128), BF16),
            pltpu.VMEM(proj.shape, BF16), pltpu.VMEM((128, 128), F32),
            dma((9,)), dma((16,)), dma((16,)), dma((3, steps)), dma((3, steps)), dma((3, steps)), dma((3, steps)),
            dma((3, 2 * steps + 1)), dma((3, 2 * steps + 1)), dma((5,)), dma((4,)), dma((5,)), dma((5,)),
        ],
        compiler_params=pltpu.CompilerParams(collective_id=0, has_side_effects=True, vmem_limit_bytes=62 * 2**20),
        cost_estimate=cost(0, 10 * 4 * piece * width),
    )(tokens, cot, qkv_weight, fc_weight, small, down, proj)


def attend_plane_kernel(
    tokens, cot, token_all, weight, cot_one, down, down_in, key_bias, proj, vectors,
    middle, normed, attended, lse, cot_three, down_full, normed_one, q, k, v, k_t, v_t, one_low, two_low,
    score_ref, joint, terms, passed, joined, arrived, send, receive,
    level_send, level_receive, mate_send, mate_receive,
):
    piece, width = tokens.shape
    half = piece // 2
    length, columns = q.shape
    heads = columns // HEAD_DIM
    rank = lax.axis_index("seq")
    one, two = neighbours()
    gather = LevelGather(down, down_full, level_send, level_receive, mate_send, mate_receive)
    for device in (one, two):
        greet("seq", device)
    pl.semaphore_wait(pltpu.get_barrier_semaphore(), 2 + gather.greet())
    up, lower = pl.ds(0, half), pl.ds(half, half)
    gather.start(gather.second())

    def copy(index, source, target, device):
        return remote(source, target, send.at[index], receive.at[index], "seq", device)

    cot_copies = (copy(0, cot_one, cot_three.at[up], two), copy(1, two_low, cot_three.at[lower], one))
    low_copies = (copy(8, cot.at[lower], one_low, one), copy(9, cot.at[lower], two_low, two))
    across = (copy(2, terms.at[3, up], passed.at[0], one), copy(3, terms.at[3, lower], passed.at[1], two))
    plain_one = copy(4, terms.at[1, up], arrived.at[0, up], one)
    plain_two = copy(5, terms.at[2, lower], arrived.at[1, lower], two)
    joined_one = copy(6, joined.at[0], arrived.at[0, lower], one)
    joined_two = copy(7, joined.at[1], arrived.at[1, up], two)
    for item in low_copies:
        item.start()
    cot_copies[0].start()
    tile = min(256, piece)
    rows = lambda n: pl.BlockSpec((tile, n), lambda i: (i, 0))
    turned = pl.BlockSpec((columns, tile), lambda i: (0, i))
    pltpu.emit_pipeline(
        lambda x, wq, wk, wv, *out: project_kernel(x, vectors, wq, wk, wv, *out),
        grid=(length // tile,),
        in_specs=[rows(width)] + [pl.BlockSpec((width, columns), lambda i, part=part: (0, part)) for part in range(3)],
        out_specs=[rows(width), rows(columns), rows(columns), rows(columns), turned, turned],
    )(token_all, weight, weight, weight, normed_one, q, k, v, k_t, v_t)
    for item in low_copies:
        item.wait_recv()
    cot_copies[1].start()

    def body(query_ref, key_ref, value_t, attended_tile, lse_tile):
        group, head = pl.program_id(0), pl.program_id(1)
        at = 3 - group
        true = flip(at, rank)
        query = query_ref[...]

        def first(block, top):
            scores = scores_of(key_ref, key_bias, query, flip(block, rank), piece, False)
            score_ref[rows_of(block, piece), :] = scores
            return jnp.maximum(top, jnp.max(scores, axis=0, keepdims=True))

        last = scores_of(key_ref, key_bias, query, at, piece, True)
        top = lax.fori_loop(0, true, first, jnp.max(last, axis=0, keepdims=True))

        def weigh(scores, rel):
            weights = jnp.exp2(scores - top)
            return jnp.sum(weights, axis=0, keepdims=True), nn(value_t[:, rows_of(rel, piece)], weights.astype(BF16))

        def second(block, carry):
            total, out = carry
            more, part = weigh(score_ref[rows_of(block, piece), :], flip(block, rank))
            return total + more, out + part

        total, out = lax.fori_loop(0, true, second, weigh(last, at))
        result = (out / total).T.astype(BF16)
        attended_tile[...] = result
        lse_tile[0] = top + jnp.log2(total)
        joint[:, pl.ds(pl.multiple_of(head * HEAD_DIM, HEAD_DIM), HEAD_DIM)] = result

        @pl.when(head == heads - 1)
        def _():
            terms[at] = nn(joint[...], proj[...]).astype(BF16)

        @pl.when((head == heads - 1) & (group == 0))
        def _():
            for item in across:
                item.start()

        @pl.when((head == heads - 1) & (group == 1))
        def _():
            plain_two.start()

        @pl.when((head == 0) & (group == 3))
        def _():
            gather.take((2,))
            gather.start(gather.passes())

        @pl.when((head == heads - 1) & (group == 2))
        def _():
            plain_one.start()
            for item in across:
                item.wait_recv()
            joined[0] = (terms[1, half:].astype(F32) + passed[1].astype(F32)).astype(BF16)
            joined[1] = (terms[2, :half].astype(F32) + passed[0].astype(F32)).astype(BF16)
            joined_one.start()
            joined_two.start()

    pltpu.emit_pipeline(
        body,
        grid=(4, heads),
        in_specs=[
            pl.BlockSpec((piece, HEAD_DIM), lambda g, h: (3 - g, h)),
            pl.BlockSpec((length, HEAD_DIM), lambda g, h: (0, h)),
            pl.BlockSpec((HEAD_DIM, length), lambda g, h: (h, 0)),
        ],
        out_specs=[
            pl.BlockSpec((piece, HEAD_DIM), lambda g, h: (3 - g, h)),
            pl.BlockSpec((1, 1, piece), lambda g, h: (h, 0, 3 - g)),
        ],
    )(q, k, v_t, attended, lse)

    for item in (plain_one, plain_two, joined_one, joined_two):
        item.wait_recv()
    part = min(128, piece)

    def norm_body(token_tile, middle_tile, normed_tile):
        here = pl.ds(pl.multiple_of(pl.program_id(0) * part, part), part)
        total = terms[0, here, :].astype(F32) + arrived[0, here, :].astype(F32) + arrived[1, here, :].astype(F32)
        values = token_tile[...].astype(F32) + (total + vectors[2:3, :])
        middle_tile[...] = values
        normed_tile[...] = (norm_parts(values)[0] * vectors[3:4, :] + vectors[4:5, :]).astype(BF16)

    line = pl.BlockSpec((part, width), lambda i: (i, 0))
    pltpu.emit_pipeline(norm_body, grid=(piece // part,), in_specs=[line], out_specs=[line] * 2)(tokens, middle, normed)
    gather.take((3,))
    gather.finish((2, 3), gather.second() + gather.passes())
    for item in cot_copies:
        item.wait()
    for item in low_copies:
        item.wait_send()
    for item in (*across, plain_one, plain_two, joined_one, joined_two):
        item.wait_send()


def attend_plane(tokens, cot, token_all, weight, cot_one, down, down_in, key_bias, proj, vectors):
    piece, width = tokens.shape
    length, columns = token_all.shape[0], proj.shape[0]
    heads, half = columns // HEAD_DIM, piece // 2
    anywhere = pl.BlockSpec(memory_space=pltpu.HBM)
    inside = pl.BlockSpec(memory_space=pltpu.VMEM)
    shape = lambda *dims: jax.ShapeDtypeStruct(dims, BF16)
    dma = pltpu.SemaphoreType.DMA
    return pl.pallas_call(
        attend_plane_kernel,
        in_specs=[anywhere] * 7 + [inside] * 3,
        out_specs=[anywhere] * 14,
        input_output_aliases={6: 5},
        out_shape=[
            jax.ShapeDtypeStruct((piece, width), F32), shape(piece, width), shape(length, columns),
            jax.ShapeDtypeStruct((heads, 1, length), F32), shape(piece, width), shape(*down_in.shape),
            shape(length, width), *[shape(length, columns)] * 3, *[shape(columns, length)] * 2,
            *[shape(half, width)] * 2,
        ],
        scratch_shapes=[
            pltpu.VMEM((length, piece), F32),
            pltpu.VMEM((piece, columns), BF16),
            pltpu.VMEM((4, piece, width), BF16),
            pltpu.VMEM((2, half, width), BF16),
            pltpu.VMEM((2, half, width), BF16),
            pltpu.VMEM((2, piece, width), BF16),
            dma((10,)), dma((10,)), dma((5,)), dma((4,)), dma((5,)), dma((5,)),
        ],
        compiler_params=pltpu.CompilerParams(collective_id=2, has_side_effects=True, vmem_limit_bytes=62 * 2**20),
        cost_estimate=cost(3 * length * length * columns + 2 * length * columns * width, 10 * length * width, heads * length * length // 2),
    )(tokens, cot, token_all, weight, cot_one, down, down_in, key_bias, proj, vectors)


def sum_rows(ref, at, columns, value, first):
    total = jnp.sum(value, axis=0, keepdims=True)

    @pl.when(first)
    def _():
        ref[at : at + 1, columns] = total

    @pl.when(jnp.logical_not(first))
    def _():
        ref[at : at + 1, columns] += total


def plane_kernel(
    normed, cot_own, one_up, one_low, two_up, two_low, cot_three, fc, down, middle, vectors,
    grad_middle, low_all, sums, hidden_sums, active, hidden_grad, normed_all, cot_all, terms, grad_down, grad_fc,
    mate_in, summed, got, down_share,
    normed_buf, cot_buf, sum_ref, joined, passed, arrived, load, local, send, receive, level_send, level_receive,
):
    piece, width = normed.shape
    half = piece // 2
    inner = fc.shape[1]
    length = normed_all.shape[0]
    tile = min(512, inner)
    last = inner // tile - 1
    one, two = neighbours()
    scatter = LevelScatter(grad_down, mate_in, summed, got, level_send, level_receive)
    for device in (one, two):
        greet("seq", device)
    pl.semaphore_wait(pltpu.get_barrier_semaphore(), 2 + scatter.greet())

    rows = lambda k, start=0, size=piece: pl.ds(k * piece + start, size)
    first, second = pl.ds(0, half), pl.ds(half, half)

    def copy(index, source, target, device):
        return remote(source, target, send.at[index], receive.at[index], "seq", device)

    normed_first = (copy(0, normed.at[first], normed_buf.at[2], one), copy(1, normed.at[second], normed_buf.at[5], two))
    normed_across = (copy(2, normed_buf.at[2], normed_buf.at[6], two), copy(3, normed_buf.at[5], normed_buf.at[7], one))
    normed_last = (copy(4, normed.at[second], normed_buf.at[3], one), copy(5, normed.at[first], normed_buf.at[4], two))
    across = (copy(6, cot_buf.at[6], passed.at[0], one), copy(7, cot_buf.at[7], passed.at[1], two))
    plain = (copy(8, cot_buf.at[2], arrived.at[0, 0], one), copy(9, cot_buf.at[5], arrived.at[1, 1], two))
    both = (copy(10, joined.at[0], arrived.at[0, 1], one), copy(11, joined.at[1], arrived.at[1, 0], two))
    low_near = (
        copy(12, low_all.at[rows(0)], low_all.at[rows(1)], one),
        copy(13, low_all.at[rows(0)], low_all.at[rows(2)], two),
    )
    low_three = (
        copy(14, low_all.at[rows(1, 0, half)], low_all.at[rows(3, 0, half)], two),
        copy(15, low_all.at[rows(2, half, half)], low_all.at[rows(3, half, half)], one),
    )

    sources = (
        cot_own.at[first], cot_own.at[second], one_up, one_low, two_up, two_low, cot_three.at[first], cot_three.at[second]
    )
    loads = [pltpu.make_async_copy(source, cot_buf.at[i], load.at[i]) for i, source in enumerate(sources)]
    own = [
        pltpu.make_async_copy(normed.at[part], normed_buf.at[i], load.at[8 + i]) for i, part in enumerate((first, second))
    ]
    keep_to = lambda target, i: target.at[pl.ds(i * half, half)]
    keeps = [pltpu.make_async_copy(normed_buf.at[i], keep_to(normed_all, i), local.at[i]) for i in range(8)]
    keeps_cot = [pltpu.make_async_copy(cot_buf.at[i], keep_to(cot_all, i), local.at[8 + i]) for i in range(8)]

    def start(*items):
        for item in items:
            item.start()

    def received(*items):
        for item in items:
            item.wait_recv()

    start(*normed_first, *own, *loads)

    place_of = lambda step: step + 2 * lax.div(step, 3) - 7 * lax.div(step, 6)

    def feed_body(fc_tile, down_tile, active_tile, hidden_tile):
        step, j = pl.program_id(0), pl.program_id(1)
        at = place_of(step)

        @pl.when((step == 0) & (j == 0))
        def _():
            for item in own:
                item.wait()
            start(*keeps[:2])
            for item in loads:
                item.wait()
            start(*keeps_cot)

        @pl.when((step == 2) & (j == 0))
        def _():
            received(*normed_first)
            start(*normed_across, keeps[2], keeps[5])

        @pl.when((step == 4) & (j == 0))
        def _():
            received(*normed_across)
            start(*normed_last, *keeps[6:])

        @pl.when((step == 6) & (j == 0))
        def _():
            received(*normed_last)
            start(*keeps[3:5])

        @pl.when((step == 7) & (j == 0))
        def _():
            start(*plain)

        weights = fc_tile[...]
        columns = pl.ds(pl.multiple_of(j * tile, tile), tile)
        hidden = nn(normed_buf[at], weights) + vectors[6:7, columns]
        grad_active = nt(cot_buf[at], down_tile[...])
        square = hidden * hidden
        bent = jnp.tanh(math.sqrt(2 / math.pi) * (hidden + 0.044715 * (square * hidden)))
        share = 0.5 * (1.0 + bent)
        active_tile[...] = (hidden * share).astype(BF16)
        slope = share + (0.5 * hidden) * (1.0 - bent * bent) * (
            math.sqrt(2 / math.pi) * (1.0 + (3 * 0.044715) * square)
        )
        grad_hidden = (grad_active * slope).astype(BF16)
        hidden_tile[...] = grad_hidden
        sum_rows(hidden_sums, 0, columns, grad_hidden.astype(F32), step == 0)
        term = nt(grad_hidden, weights)

        @pl.when(j == 0)
        def _():
            sum_ref[...] = term

        @pl.when(j > 0)
        def _():
            sum_ref[...] += term

        @pl.when((j == last) & (step == 0))
        def _():
            for item in keeps_cot:
                item.wait()

        @pl.when(j == last)
        def _():
            cot_buf[at] = sum_ref[...].astype(BF16)

        @pl.when((j == last) & (step == 5))
        def _():
            start(*across)

    pltpu.emit_pipeline(
        feed_body,
        grid=(8, inner // tile),
        in_specs=[
            pl.BlockSpec((width, tile), lambda s, j: (0, j)),
            pl.BlockSpec((tile, width), lambda s, j: (j, 0)),
        ],
        out_specs=[pl.BlockSpec((half, tile), lambda s, j: (place_of(s), j))] * 2,
    )(fc, down, active, hidden_grad)

    received(*across)
    joined[0] = (cot_buf[3].astype(F32) + passed[1].astype(F32)).astype(BF16)
    joined[1] = (cot_buf[4].astype(F32) + passed[0].astype(F32)).astype(BF16)
    start(*both)
    for item in keeps:
        item.wait()

    narrow = min(512, width)

    def down_body(active_rows, down_columns, out):
        out[...] = nn(active_rows[...], down_columns[...]).astype(BF16)

    def multiply_down(start):
        pltpu.emit_pipeline(
            down_body,
            grid=(2, width // narrow),
            in_specs=[
                pl.BlockSpec((piece, inner), lambda k, j: (start + k, 0)),
                pl.BlockSpec((inner, narrow), lambda k, j: (0, j)),
            ],
            out_specs=[pl.BlockSpec((piece, narrow), lambda k, j: (start + k, j))],
        )(active, down, terms)

    wide, tall = min(1024, width), min(1024, inner)

    def outer_body(left, right, out):
        out[...] = tn(left[...], right[...]).astype(BF16)

    def outer(left, right, out, shape):
        pltpu.emit_pipeline(
            outer_body,
            grid=(out.shape[0] // shape[0], out.shape[1] // shape[1]),
            in_specs=[
                pl.BlockSpec((length, shape[0]), lambda i, j: (0, i)),
                pl.BlockSpec((length, shape[1]), lambda i, j: (0, j)),
            ],
            out_specs=[pl.BlockSpec(shape, lambda i, j: (i, j))],
        )(left, right, out)

    outer(active, cot_all, grad_down, (tall, wide))
    scatter.start()
    multiply_down(0)
    scatter.spread()
    received(*plain, *both)
    part = min(128, half)
    steps = half // part

    def norm_body(middle_tile, cot_tile, grad_tile, low_tile):
        i = pl.program_id(0)
        at = lax.div(i, steps)
        here = pl.ds(pl.multiple_of(lax.rem(i, steps) * part, part), part)
        upstream = (
            cot_buf[at, here, :].astype(F32) + arrived[0, at, here, :].astype(F32) + arrived[1, at, here, :].astype(F32)
        )
        unit, scale = norm_parts(middle_tile[...])
        cot = cot_tile[...].astype(F32)
        grad = cot + norm_backward(unit, scale, vectors[3:4, :], upstream)
        rounded = grad.astype(BF16)
        grad_tile[...] = grad
        low_tile[...] = rounded
        for at, item in enumerate((upstream * unit, upstream, rounded.astype(F32), cot)):
            sum_rows(sums, at, slice(None), item, i == 0)

    line = pl.BlockSpec((part, width), lambda i: (i, 0))
    pltpu.emit_pipeline(norm_body, grid=(piece // part,), in_specs=[line] * 2, out_specs=[line] * 2)(
        middle, cot_own, grad_middle, low_all
    )
    start(*low_near)
    multiply_down(2)
    scatter.pass_on()
    outer(normed_all, hidden_grad, grad_fc, (wide, tall))
    received(*low_near)
    start(*low_three)
    scatter.finish(down_share)
    scatter.close()
    received(*low_three)
    for item in (*normed_first, *normed_across, *normed_last, *across, *plain, *both, *low_near, *low_three):
        item.wait_send()


def feed_plane(normed, cots, fc, down, middle, vectors):
    piece, width = normed.shape
    inner = fc.shape[1]
    length, half = 4 * piece, piece // 2
    anywhere = pl.BlockSpec(memory_space=pltpu.HBM)
    inside = pl.BlockSpec(memory_space=pltpu.VMEM)
    shape = lambda rows, columns, kind=BF16: jax.ShapeDtypeStruct((rows, columns), kind)
    dma = pltpu.SemaphoreType.DMA
    return pl.pallas_call(
        plane_kernel,
        in_specs=[anywhere] * 10 + [inside],
        out_specs=[anywhere, anywhere, inside, inside] + [anywhere] * 11,
        out_shape=[
            shape(piece, width, F32), shape(length, width), shape(4, width, F32), shape(1, inner, F32),
            shape(length, inner), shape(length, inner), shape(length, width), shape(length, width),
            shape(length, width), shape(inner, width), shape(width, inner),
            shape(inner // 2, width), shape(inner // 2, width), shape(inner // 2, width), shape(inner // 8, width, F32),
        ],
        scratch_shapes=[
            pltpu.VMEM((8, half, width), BF16),
            pltpu.VMEM((8, half, width), BF16),
            pltpu.VMEM((half, width), F32),
            pltpu.VMEM((2, half, width), BF16),
            pltpu.VMEM((2, half, width), BF16),
            pltpu.VMEM((2, 2, half, width), BF16),
            dma((10,)), dma((16,)), dma((16,)), dma((16,)), dma((8,)), dma((8,)),
        ],
        compiler_params=pltpu.CompilerParams(collective_id=1, has_side_effects=True, vmem_limit_bytes=60 * 2**20),
        cost_estimate=cost(12 * length * width * inner, 10 * length * width),
    )(normed, *cots, fc, down, middle, vectors)


def retreat_plane_kernel(
    low_all, q, k, v, k_t, lse, terms, middle, key_bias, proj, vectors,
    grads, column_sums, block_out,
    prob_ref, chance_ref, grad_ref, key_sum, value_sum, rounded, own, passed, joined, arrived,
    load, local, send, receive,
):
    piece, width = middle.shape
    half = piece // 2
    length, columns = q.shape
    heads = columns // HEAD_DIM
    rank = lax.axis_index("seq")
    one, two = neighbours()
    for device in (one, two):
        greet("seq", device)
    pl.semaphore_wait(pltpu.get_barrier_semaphore(), 2)
    up, lower = pl.ds(0, half), pl.ds(half, half)
    rows = lambda at, start=0, size=piece: pl.ds(at * piece + start, size)

    def copy(index, source, target, device):
        return remote(source, target, send.at[index], receive.at[index], "seq", device)

    across = (
        copy(0, terms.at[rows(3, 0, half)], passed.at[0], one),
        copy(1, terms.at[rows(3, half, half)], passed.at[1], two),
    )
    plain_one = copy(2, terms.at[rows(1, 0, half)], arrived.at[0, up], one)
    plain_two = copy(3, terms.at[rows(2, half, half)], arrived.at[1, lower], two)
    joined_one = copy(4, joined.at[0], arrived.at[0, lower], one)
    joined_two = copy(5, joined.at[1], arrived.at[1, up], two)
    loads = (
        pltpu.make_async_copy(terms.at[rows(1, half, half)], own.at[0], load.at[0]),
        pltpu.make_async_copy(terms.at[rows(2, 0, half)], own.at[1], load.at[1]),
    )
    for item in (*across, plain_one, plain_two, *loads):
        item.start()
    key_sum[...] = jnp.zeros_like(key_sum)
    value_sum[...] = jnp.zeros_like(value_sum)

    def body(low_ref, query_ref, key_ref, value_ref, key_t, lse_ref, query_out):
        at, head = pl.program_id(0), pl.program_id(1)
        true = flip(at, rank)
        here = pl.ds(pl.multiple_of(head * HEAD_DIM, HEAD_DIM), HEAD_DIM)

        @pl.when(head == 0)
        def _():
            grad_ref[...] = nt(low_ref[...], proj[...]).astype(BF16)

        @pl.when((at == 1) & (head == 2))
        def _():
            for item in (*across,):
                item.wait_recv()
            for item in loads:
                item.wait()
            joined[0] = (own[0].astype(F32) + passed[1].astype(F32)).astype(BF16)
            joined[1] = (own[1].astype(F32) + passed[0].astype(F32)).astype(BF16)
            joined_one.start()
            joined_two.start()

        query, grad, base = query_ref[...], grad_ref[:, here], lse_ref[0]

        def measure(scores, rel):
            block = rows_of(rel, piece)
            probs = jnp.exp2(scores - base)
            grad_chances = nt(value_ref[block, :], grad)
            value_sum[block, here] += nn(probs.astype(BF16), grad)
            prob_ref[block, :] = probs
            chance_ref[block, :] = grad_chances
            return jnp.sum(probs * grad_chances, axis=0, keepdims=True)

        def first(block, weighted):
            rel = flip(block, rank)
            return weighted + measure(scores_of(key_ref, key_bias, query, rel, piece, False), rel)

        last = scores_of(key_ref, key_bias, query, at, piece, True)
        weighted = lax.fori_loop(0, true, first, measure(last, at))

        def second(block, total):
            block = rows_of(flip(block, rank), piece)
            grad_scores = (prob_ref[block, :] * (chance_ref[block, :] - weighted)).astype(BF16)
            key_sum[block, here] += nn(grad_scores, query)
            return total + nn(key_t[:, block], grad_scores)

        total = lax.fori_loop(0, true + 1, second, jnp.zeros((HEAD_DIM, piece), F32))
        result = (total * FACTOR).T.astype(BF16)
        query_out[...] = result
        sum_rows(column_sums, 0, here, result.astype(F32), at == 0)

    pltpu.emit_pipeline(
        body,
        grid=(4, heads),
        in_specs=[
            pl.BlockSpec((piece, width), lambda g, h: (g, 0)),
            pl.BlockSpec((piece, HEAD_DIM), lambda g, h: (g, h)),
            pl.BlockSpec((length, HEAD_DIM), lambda g, h: (0, h)),
            pl.BlockSpec((length, HEAD_DIM), lambda g, h: (0, h)),
            pl.BlockSpec((HEAD_DIM, length), lambda g, h: (h, 0)),
            pl.BlockSpec((1, 1, piece), lambda g, h: (h, 0, g)),
        ],
        out_specs=[pl.BlockSpec((piece, HEAD_DIM), lambda g, h: (g, h))],
    )(low_all, q, k, v, k_t, lse, grads)

    rounded[:, :columns] = (key_sum[...] * FACTOR).astype(BF16)
    values = value_sum[...].astype(BF16)
    rounded[:, columns:] = values
    column_sums[1:2, :] = jnp.sum(values.astype(F32), axis=0, keepdims=True)
    keep = pltpu.make_async_copy(rounded, grads.at[:, pl.ds(columns, 2 * columns)], local.at[0])
    keep.start()
    for item in (plain_one, plain_two, joined_one, joined_two):
        item.wait_recv()
    part = min(128, piece)

    def out_body(middle_tile, term_tile, out):
        here = pl.ds(pl.multiple_of(pl.program_id(0) * part, part), part)
        total = term_tile[...].astype(F32) + arrived[0, here, :].astype(F32) + arrived[1, here, :].astype(F32)
        out[...] = (middle_tile[...] + (total + vectors[5:6, :])).astype(BF16)

    line = pl.BlockSpec((part, width), lambda i: (i, 0))
    pltpu.emit_pipeline(out_body, grid=(piece // part,), in_specs=[line] * 2, out_specs=[line])(middle, terms, block_out)
    keep.wait()
    for item in (*across, plain_one, plain_two, joined_one, joined_two):
        item.wait_send()


def retreat_plane(low_all, q, k, v, k_t, lse, terms, middle, key_bias, proj, vectors):
    piece, width = middle.shape
    length, columns = q.shape
    half = piece // 2
    anywhere = pl.BlockSpec(memory_space=pltpu.HBM)
    inside = pl.BlockSpec(memory_space=pltpu.VMEM)
    dma = pltpu.SemaphoreType.DMA
    return pl.pallas_call(
        retreat_plane_kernel,
        in_specs=[anywhere] * 8 + [inside] * 3,
        out_specs=[anywhere, inside, anywhere],
        out_shape=[
            jax.ShapeDtypeStruct((length, 3 * columns), BF16),
            jax.ShapeDtypeStruct((2, columns), F32),
            jax.ShapeDtypeStruct((piece, width), BF16),
        ],
        scratch_shapes=[
            pltpu.VMEM((length, piece), F32),
            pltpu.VMEM((length, piece), F32),
            pltpu.VMEM((piece, columns), BF16),
            pltpu.VMEM((length, columns), F32),
            pltpu.VMEM((length, columns), F32),
            pltpu.VMEM((length, 2 * columns), BF16),
            pltpu.VMEM((2, half, width), BF16),
            pltpu.VMEM((2, half, width), BF16),
            pltpu.VMEM((2, half, width), BF16),
            pltpu.VMEM((2, piece, width), BF16),
            dma((2,)), dma((1,)), dma((6,)), dma((6,)),
        ],
        compiler_params=pltpu.CompilerParams(collective_id=3, has_side_effects=True, vmem_limit_bytes=60 * 2**20),
        cost_estimate=cost(8 * length * length * columns + 2 * length * columns * width, 10 * length * width),
    )(low_all, q, k, v, k_t, lse, terms, middle, key_bias, proj, vectors)


def closing_kernel(
    grads, weight, normed_one, tokens, grad_middle, vectors, sums_two, hidden_sums, qv_sums, fc_share,
    tokens_grad, qkv_out, fc_out, small_out,
    terms, passed, joined, arrived, qkv_in, fc_in, mine, small_in, small_rows, small_got,
    grad_qkv, mate_in, summed, got, qkv_share,
    send, receive, level_send, level_receive, small_send, small_receive, load,
):
    pieces = [[ref.at[i] for ref in (grad_qkv, mate_in, summed, got, qkv_share)] for i in range(2)]
    piece, width = tokens.shape
    half = piece // 2
    columns = grads.shape[1]
    heads = columns // (3 * HEAD_DIM)
    me, place = lax.axis_index("seq"), lax.axis_index("dp")
    one, two = neighbours()
    three = 3 - me
    plane = (one, two, three)
    others = [lax.rem(place + i, 8) for i in range(1, 8)]
    for device in plane:
        greet("seq", device)
    for device in others:
        greet("dp", device)
    pl.semaphore_wait(pltpu.get_barrier_semaphore(), 10)
    scatters = [
        NearScatter(*refs[:4], level_send.at[i], level_receive.at[i]) for i, refs in enumerate(pieces)
    ]
    shares = [refs[4] for refs in pieces]
    up, lower = pl.ds(0, half), pl.ds(half, half)

    def copy(index, source, target, device):
        return remote(source, target, send.at[index], receive.at[index], "seq", device)

    across = (copy(0, terms.at[3, up], passed.at[0], one), copy(1, terms.at[3, lower], passed.at[1], two))
    plain_one = copy(2, terms.at[1, up], arrived.at[0, up], one)
    plain_two = copy(3, terms.at[2, lower], arrived.at[1, lower], two)
    joined_one = copy(4, joined.at[0], arrived.at[0, lower], one)
    joined_two = copy(5, joined.at[1], arrived.at[1, up], two)
    fine = qkv_in.shape[2]
    rows_for = lambda ref, device: ref.at[pl.ds(device * fine, fine)]
    fc_copies = [copy(6 + i, rows_for(fc_share, device), fc_in.at[i], device) for i, device in enumerate(plane)]
    qkv_copies = [
        [copy(15 + 3 * part + i, rows_for(share, device), qkv_in.at[part, i], device) for i, device in enumerate(plane)]
        for part, share in enumerate(shares)
    ]
    small_copies = [copy(9 + i, mine, small_in.at[i], device) for i, device in enumerate(plane)]
    fc_own = pltpu.make_async_copy(rows_for(fc_share, me), fc_in.at[3], load.at[0])
    qkv_own = [
        pltpu.make_async_copy(rows_for(share, me), qkv_in.at[part, 3], load.at[1 + part])
        for part, share in enumerate(shares)
    ]
    row_copies = [
        remote(small_rows.at[device], small_got.at[i], small_send.at[i], small_receive.at[i], "dp", device)
        for i, device in enumerate(others)
    ]

    def back_term(at):
        for start in range(0, width, width // 2):
            columns_here = slice(start, start + width // 2)
            term = nt(grads[at * piece : (at + 1) * piece, :], weight[columns_here, :])
            terms[at, :, columns_here] = term.astype(BF16)

    tile = min(512, width)
    narrow = columns // 2

    def outer(part):
        def body(left):
            here = pl.ds(pl.multiple_of(pl.program_id(0) * tile, tile), tile)
            grad_qkv[part, here, :] = tn(left[...], grads[:, part * narrow : (part + 1) * narrow]).astype(BF16)

        pltpu.emit_pipeline(
            body,
            grid=(width // tile,),
            in_specs=[pl.BlockSpec((normed_one.shape[0], tile), lambda i: (0, i))],
        )(normed_one)

    back_term(3)
    for item in across:
        item.start()
    back_term(1)
    plain_one.start()
    outer(0)
    scatters[0].start()
    back_term(2)
    plain_two.start()
    scatters[0].spread()
    outer(1)
    scatters[1].start()
    for item in across:
        item.wait_recv()
    joined[0] = (terms[1, half:].astype(F32) + passed[1].astype(F32)).astype(BF16)
    joined[1] = (terms[2, :half].astype(F32) + passed[0].astype(F32)).astype(BF16)
    joined_one.start()
    joined_two.start()
    scatters[1].spread()
    scatters[0].pass_on()
    fc_own.start()
    back_term(0)
    mine[...] = jnp.zeros_like(mine)
    mine[2:6, :] = sums_two[...]
    for head in range(heads):
        at = (head * 2 + lax.rem(me, 2)) * 2 + lax.div(me, 2)
        here = pl.ds(pl.multiple_of(at * HEAD_DIM, HEAD_DIM), HEAD_DIM)
        for part in range(2):
            mine[6 + part : 7 + part, here] = qv_sums[part : part + 1, head * HEAD_DIM : (head + 1) * HEAD_DIM]
    scatters[1].pass_on()

    scatters[0].finish(shares[0])
    for item in (plain_one, plain_two, joined_one, joined_two):
        item.wait_recv()
    for item in fc_copies:
        item.start()
    part = min(128, piece)

    def norm_body(token_tile, middle_tile, out):
        i = pl.program_id(0)
        here = pl.ds(pl.multiple_of(i * part, part), part)
        upstream = terms[0, here, :].astype(F32) + arrived[0, here, :].astype(F32) + arrived[1, here, :].astype(F32)
        unit, scale = norm_parts(token_tile[...].astype(F32))
        out[...] = middle_tile[...] + norm_backward(unit, scale, vectors[0:1, :], upstream)
        for at, item in enumerate((upstream * unit, upstream)):
            sum_rows(mine, at, slice(None), item, i == 0)

    line = pl.BlockSpec((part, width), lambda i: (i, 0))
    pltpu.emit_pipeline(norm_body, grid=(piece // part,), in_specs=[line] * 2, out_specs=[line])(
        tokens, grad_middle, tokens_grad
    )
    for item in small_copies:
        item.start()
    scatters[1].finish(shares[1])
    for part in range(2):
        for item in qkv_copies[part]:
            item.start()
        qkv_own[part].start()
    for item in small_copies:
        item.wait_recv()
    mine_total = mine[...] + small_in[0] + small_in[1] + small_in[2]
    small_rows[...] = jnp.zeros_like(small_rows)
    share, wide = width // 8, 2 * width // 8
    for d in range(8):
        small_rows[d, 0:6, 0:share] = mine_total[0:6, d * share : (d + 1) * share]
        row, at = 6 + d // 4, (d % 4) * wide
        small_rows[d, 6:7, :] = mine_total[row : row + 1, at : at + wide]
        inner = hidden_sums.shape[1] // 8
        small_rows[d, 7:8, 0:inner] = hidden_sums[:, d * inner : (d + 1) * inner]
    for item in row_copies:
        item.start()
    sources = (*plane, me)
    fc_own.wait()
    for item in fc_copies:
        item.wait_recv()
    block = fc_in.shape[2] // 8
    for i, source in enumerate(sources):
        for d in range(8):
            target = pl.ds(pl.multiple_of((d * 4 + source) * block, block), block)
            fc_out[:, target] = fc_in[i, :, d * block : (d + 1) * block].astype(F32)
    for part in range(2):
        qkv_own[part].wait()
        for item in qkv_copies[part]:
            item.wait_recv()
    for i, source in enumerate(sources):
        for part in range(3):
            for head in range(heads):
                at = part * HEADS + (head * 2 + lax.rem(source, 2)) * 2 + lax.div(source, 2)
                target = pl.ds(pl.multiple_of(at * HEAD_DIM, HEAD_DIM), HEAD_DIM)
                start = (part * heads + head) * HEAD_DIM
                which, start = start // narrow, start % narrow
                qkv_out[:, target] = qkv_in[which, i, :, start : start + HEAD_DIM].astype(F32)
    for item in row_copies:
        item.wait_recv()
    total = small_rows[place]
    for i in range(7):
        total = total + small_got[i]
    small_out[...] = total
    for item in (*across, plain_one, plain_two, joined_one, joined_two, *fc_copies, *small_copies, *row_copies):
        item.wait_send()
    for part in range(2):
        scatters[part].close()
        for item in qkv_copies[part]:
            item.wait_send()


def closing(grads, weight, normed_one, tokens, grad_middle, vectors, sums_two, hidden_sums, qv_sums, fc_share):
    piece, width = tokens.shape
    columns, half = grads.shape[1], piece // 2
    fine = fc_share.shape[0] // 4
    wide = 2 * width // 8
    anywhere = pl.BlockSpec(memory_space=pltpu.HBM)
    inside = pl.BlockSpec(memory_space=pltpu.VMEM)
    shape = lambda rows, columns, kind=BF16: jax.ShapeDtypeStruct((rows, columns), kind)
    dma = pltpu.SemaphoreType.DMA
    return pl.pallas_call(
        closing_kernel,
        in_specs=[inside, inside, anywhere, anywhere, anywhere, inside, inside, inside, inside, anywhere],
        out_specs=[anywhere, inside, inside, inside],
        out_shape=[
            shape(piece, width, F32), shape(fine, 4 * columns, F32), shape(fine, 4 * fc_share.shape[1], F32),
            shape(8, wide, F32),
        ],
        scratch_shapes=[
            pltpu.VMEM((4, piece, width), BF16),
            pltpu.VMEM((2, half, width), BF16),
            pltpu.VMEM((2, half, width), BF16),
            pltpu.VMEM((2, piece, width), BF16),
            pltpu.VMEM((2, 4, fine, columns // 2), BF16),
            pltpu.VMEM((4, fine, fc_share.shape[1]), BF16),
            pltpu.VMEM((8, width), F32),
            pltpu.VMEM((3, 8, width), F32),
            pltpu.VMEM((8, 8, wide), F32),
            pltpu.VMEM((7, 8, wide), F32),
            *[
                pltpu.VMEM((2, count, columns // 2), BF16)
                for count in (width, width // 2, width // 2, width // 2, width // 8)
            ],
            dma((21,)), dma((21,)), dma((2, 8)), dma((2, 8)), dma((7,)), dma((7,)), dma((3,)),
        ],
        compiler_params=pltpu.CompilerParams(collective_id=4, has_side_effects=True, vmem_limit_bytes=60 * 2**20),
        cost_estimate=cost(16 * piece * width * columns, 10 * piece * width),
    )(grads, weight, normed_one, tokens, grad_middle, vectors, sums_two, hidden_sums, qv_sums, fc_share)


def after(value, *others):
    return lax.optimization_barrier((value, *others))[0]


def shift(value, axis, distance):
    count = lax.axis_size(axis)
    return lax.ppermute(value, axis, [(i, i ^ distance) for i in range(count)])


def gather_blocks(value, axis="seq"):
    return [value] + [shift(value, axis, k) for k in range(1, lax.axis_size(axis))]


def scatter_blocks(blocks, axis="seq"):
    return [blocks[0]] + [shift(blocks[k], axis, k) for k in range(1, lax.axis_size(axis))]


def gather_plane(value):
    if lax.axis_size("seq") != 4:
        return gather_blocks(value)
    half = value.shape[0] // 2
    one, two = shift(value, "seq", 1), shift(value, "seq", 2)
    three = jnp.concatenate([shift(one[:half], "seq", 2), shift(two[half:], "seq", 1)], axis=0)
    return [value, one, two, three]


def scatter_plane(blocks):
    if lax.axis_size("seq") != 4:
        return scatter_blocks(blocks)
    half = blocks[0].shape[0] // 2
    up, low = shift(blocks[3][:half], "seq", 1), shift(blocks[3][half:], "seq", 2)
    one = shift(blocks[1][:half], "seq", 1)
    two = shift(blocks[2][half:], "seq", 2)
    one_low = (blocks[1][half:].astype(F32) + low.astype(F32)).astype(BF16)
    two_up = (blocks[2][:half].astype(F32) + up.astype(F32)).astype(BF16)
    return [blocks[0], (one, shift(one_low, "seq", 1)), (shift(two_up, "seq", 2), two)]


def by_rank(blocks, rank):
    bit = 1
    while bit < len(blocks):
        odd = (rank & bit) != 0
        blocks = [jnp.where(odd, blocks[k ^ bit], blocks[k]) for k in range(len(blocks))]
        bit *= 2
    return blocks


def pick(pieces, at):
    return lax.dynamic_index_in_dim(pieces, at, axis=0, keepdims=False)


def exchange(pieces, rank):
    return scatter_blocks([pick(pieces, rank ^ k) for k in range(pieces.shape[0])])


def small_scatter(pieces, dp_rank, seq_rank):
    total = 0.0
    sent = [lax.dynamic_index_in_dim(pieces, seq_rank ^ k, axis=1, keepdims=False) for k in range(pieces.shape[1])]
    for part in scatter_blocks(sent):
        total = total + part
    sent = [pick(total, dp_rank ^ k) for k in range(pieces.shape[0])]
    total = 0.0
    for part in scatter_blocks(sent, "dp"):
        total = total + part
    return total


def swap_pairs(dp_count, seq_count, sub):
    pairs = []
    for d in range(dp_count):
        for s in range(seq_count):
            source = ((d // sub) * sub + s % sub) * seq_count + (s // sub) * sub + d % sub
            pairs.append((source, d * seq_count + s))
    return pairs


def gather_dp(value):
    return lax.all_gather(value, "dp", axis=0, tiled=True)


def scatter_dp(value):
    return lax.psum_scatter(value, "dp", scatter_dimension=0, tiled=True)


def shards(
    tokens,
    cotangent,
    lengths,
    key_mask,
    attn_gain,
    attn_shift,
    qkv_weight,
    qv_bias,
    proj_weight,
    proj_bias,
    mlp_gain,
    mlp_shift,
    fc_weight,
    fc_bias,
    down_weight,
    down_bias,
):
    _, piece, width = tokens.shape
    dp_count, seq_count = lax.axis_size("dp"), lax.axis_size("seq")
    dp_rank, seq_rank = lax.axis_index("dp"), lax.axis_index("seq")
    own_heads = HEADS // seq_count
    own_width = own_heads * HEAD_DIM
    rows = qkv_weight.shape[0]
    sub = HEAD_DIM // proj_weight.shape[0]
    high = seq_count // sub
    block = down_weight.shape[0]
    rank = jnp.reshape(seq_rank, (1,)).astype(jnp.int32)
    swap = swap_pairs(dp_count, seq_count, sub)
    order = list(range(seq_count - 1, -1, -1))
    if seq_count == 4:
        order = [3, 1, 2, 0]

    in_plane = seq_count == 4 and dp_count == 8
    tokens_own, cot_own = tokens[0], cotangent[0]

    positions = seq_rank * piece + jnp.arange(piece, dtype=jnp.int32)
    own_flags = ((key_mask[0] == 1) & (positions < lengths[0])).astype(BF16)
    length = piece * seq_count
    shared = None
    if in_plane:
        six = jnp.stack([attn_gain, attn_shift, proj_bias, mlp_gain, mlp_shift, down_bias])
        odd = (seq_rank & 1) != 0
        six = jnp.concatenate([jnp.where(odd, 0, six), jnp.where(odd, six, 0)], axis=1)
        small, start = 0, 0
        for item in (six, qv_bias, fc_bias, own_flags):
            item = item.reshape(-1, 128)
            small = small + jnp.pad(item, ((start, 16 - start - item.shape[0]), (0, 0)))
            start += item.shape[0]
        token_all, qkv_full, fc_rows, cot_one, cot_two, down_full, proj_full, vectors, key_bias = opening(
            tokens_own, cot_own, qkv_weight, fc_weight, small, down_weight, proj_weight, dp_count
        )
        fc_full = gather_dp(fc_rows)
    else:
        small = (attn_gain, attn_shift, qv_bias, proj_bias, mlp_gain, mlp_shift, fc_bias, down_bias)
        sizes = [item.shape[0] for item in small]
        packed = jnp.concatenate(small + (own_flags,))
        blocks = gather_blocks(packed)
        flags = jnp.concatenate([item[-piece:] for item in blocks])
        key_bias = jnp.where(flags > 0, 0.0, NEG).astype(F32)[:, None]
        packed = jnp.stack(by_rank([item[:-piece] for item in blocks], seq_rank))
        packed = jnp.stack(by_rank(gather_blocks(packed, "dp"), dp_rank)).astype(F32)
        parts, start = [], 0
        for size in sizes:
            parts.append(packed[:, :, start : start + size])
            start += size
        whole = [part.reshape(1, -1) for part in parts]
        gain_one, shift_one, qv_full, proj_shift, gain_two, shift_two, _, down_shift = whole
        fc_shift = lax.dynamic_index_in_dim(parts[6], seq_rank, axis=1, keepdims=False).reshape(1, -1)
        rank_low, rank_high = seq_rank % sub, seq_rank // sub
        qv_own = qv_full.reshape(2, own_heads, sub, high, HEAD_DIM)
        qv_own = lax.dynamic_index_in_dim(qv_own, rank_low, axis=2, keepdims=False)
        qv_own = lax.dynamic_index_in_dim(qv_own, rank_high, axis=2, keepdims=False).reshape(1, -1)
        qv_own = jnp.pad(qv_own, ((0, 0), (0, width - 2 * own_width)))
        vectors = jnp.concatenate([gain_one, shift_one, jnp.zeros((5, width), F32), qv_own], axis=0)
        qkv_pieces = (
            qkv_weight.reshape(rows, 3, own_heads, sub, high, HEAD_DIM)
            .transpose(4, 3, 0, 1, 2, 5)
            .reshape(seq_count, rows, 3 * own_width)
        )
        fc_pieces = (
            fc_weight.reshape(rows, dp_count, seq_count, block)
            .transpose(2, 0, 1, 3)
            .reshape(seq_count, rows, dp_count * block)
        )
        qkv_full = gather_dp(jnp.concatenate(by_rank(exchange(qkv_pieces, seq_rank), seq_rank), axis=0))
        proj_full = gather_dp(lax.ppermute(proj_weight, BOTH, swap))
        down_full = gather_dp(down_weight)
        fc_full = gather_dp(jnp.concatenate(by_rank(exchange(fc_pieces, seq_rank), seq_rank), axis=0))
        token_blocks = gather_blocks(tokens_own)
        cot_blocks = gather_blocks(after(cot_own, token_blocks[-1]))
        for k in range(seq_count):
            shared = project(k, token_blocks[k], 0, piece, vectors, qkv_full, length, shared)
    if in_plane:
        results = attend_plane(
            tokens_own, cot_own, token_all, qkv_full, cot_one, down_weight, down_full, key_bias, proj_full, vectors
        )
        middle, normed_two, attended, lse, cot_three, down_full = results[:6]
        normed_one, q, keys, values, keys_t, values_t, one_low, two_low = results[6:]
    else:
        normed_one, q, keys, values, keys_t, values_t = shared
        proj_terms, shared = [None] * seq_count, None
        for k in order:
            proj_terms[k], shared = attend(k, rank, q, keys, values_t, key_bias, proj_full, piece, shared)
        attended, lse = shared
        middle, normed_two = rowwise(
            middle_kernel, scatter_blocks(proj_terms), [tokens_own], [proj_shift, gain_two, shift_two], [F32, BF16], 0
        )

    if in_plane:
        cots = (cot_own, cot_one, one_low, cot_two, two_low, cot_three)
        results = feed_plane(normed_two, cots, fc_full, down_full, middle, vectors)
        grad_middle, low_all, sums_two, hidden_sums, down_terms, grad_fc, grad_down = [
            results[i] for i in (0, 1, 2, 3, 8, 10, 14)
        ]
        grad_fc = scatter_dp(grad_fc)
        grads, qv_sums, block_out = retreat_plane(
            low_all, q, keys, values, keys_t, lse, down_terms, middle, key_bias, proj_full, vectors
        )
    else:
        normed_blocks = gather_blocks(normed_two)
        grad_terms, shared = [], None
        for k in range(seq_count):
            term, shared = feed(k, normed_blocks[k], cot_blocks[k], fc_full, fc_shift, down_full, seq_count, shared)
            grad_terms.append(term)
        active, grad_hidden, normed_all, cot_all = shared
        grad_middle, grad_mid_low, *sums_two = rowwise(
            middle_back_kernel, scatter_blocks(grad_terms), [middle, cot_own], [gain_two], [F32, BF16], 4
        )
        down_terms = [
            nn(active[k * piece : (k + 1) * piece], down_full).astype(BF16) for k in range(seq_count)
        ]
        low_blocks = gather_blocks(grad_mid_low)
        grad_down = scatter_dp(tn(active, cot_all).astype(BF16))
        grad_fc = scatter_dp(tn(normed_all, grad_hidden).astype(BF16))
        hidden_sums = jnp.sum(grad_hidden.astype(F32), axis=0)
        block_out = rowwise(out_kernel, scatter_blocks(down_terms), [middle], [down_shift], [BF16], 0)[0]
        sums, shared = None, None
        for k in range(seq_count):
            sums, shared = retreat(
                k, rank, low_blocks[k], proj_full, q, lse, keys, values, keys_t, key_bias, sums, shared,
                k == seq_count - 1,
            )
        grad_q, low_all = shared
        grads = jnp.concatenate([grad_q, sums[0], sums[1]], axis=1)
        qv_sums = jnp.stack([jnp.sum(item.astype(F32), axis=0) for item in (grad_q, sums[1])])
    grad_proj = tn(after(attended, grads), low_all).astype(BF16)
    grad_proj = scatter_dp(after(grad_proj, grad_fc) if in_plane else grad_proj)
    grad_proj = lax.ppermute(grad_proj, BOTH, swap).astype(F32)
    share = attn_gain.shape[0]
    if in_plane:
        tokens_grad, grad_qkv_weight, grad_fc, smalls = closing(
            grads, qkv_full, normed_one, tokens_own, grad_middle, vectors, sums_two, hidden_sums, qv_sums, grad_fc
        )[:4]
        own = lambda row, size: lax.dynamic_slice_in_dim(smalls[row], seq_rank * size, size)
        late = jnp.concatenate([own(0, share), own(1, share), own(6, 2 * share)])
        early = jnp.concatenate([own(row, share) for row in range(2, 6)] + [smalls[7, :block]])
    else:
        back_terms = [None] * seq_count
        for k in order:
            back_terms[k] = back(k, grads, qkv_full, piece)
        tokens_grad, *sums_one = rowwise(
            tokens_back_kernel, scatter_blocks(back_terms), [tokens_own, grad_middle], [gain_one], [F32], 2
        )

        blocks = exchange(grad_fc.reshape(seq_count, rows, dp_count * block), seq_rank)
        if block % 128 == 0:
            fc_places = lambda s: [(0, d, d * seq_count + s) for d in range(dp_count)]
            grad_fc = lay_out(rank, [[item] for item in blocks], fc_weight.shape[1], (fc_places, block))
        else:
            blocks = [item.reshape(rows, dp_count, block) for item in by_rank(blocks, seq_rank)]
            grad_fc = jnp.stack(blocks, axis=2).reshape(fc_weight.shape).astype(F32)
        grad_qkv = scatter_dp(tn(normed_one, grads).astype(BF16))
        blocks = [[item] for item in exchange(grad_qkv.reshape(seq_count, rows, 3 * own_width), seq_rank)]
        qkv_places = lambda s: [
            (0, part * own_heads + head, part * HEADS + (head * sub + s % sub) * high + s // sub)
            for part in range(3)
            for head in range(own_heads)
        ]
        grad_qkv_weight = lay_out(rank, blocks, qkv_weight.shape[1], (qkv_places, HEAD_DIM))

        def spread(vector):
            return vector.reshape(dp_count, seq_count, -1)

        here = (jnp.arange(seq_count) == seq_rank).astype(F32)
        hidden_sums = hidden_sums.reshape(dp_count, 1, -1) * here[None, :, None]
        early = jnp.concatenate([spread(item) for item in sums_two] + [hidden_sums], axis=2)
        early = small_scatter(early, dp_rank, seq_rank)
        here = (jnp.arange(sub) == rank_low)[:, None] & (jnp.arange(high) == rank_high)[None, :]
        qv_sums = qv_sums.reshape(2, own_heads, 1, 1, HEAD_DIM) * here.astype(F32)[None, None, :, :, None]
        late = jnp.concatenate([spread(item) for item in sums_one] + [spread(qv_sums)], axis=2)
        late = small_scatter(late, dp_rank, seq_rank)
    return (
        block_out[None],
        tokens_grad[None],
        late[:share],
        late[share : 2 * share],
        grad_qkv_weight,
        late[2 * share :],
        grad_proj,
        early[2 * share : 3 * share],
        early[:share],
        early[share : 2 * share],
        grad_fc,
        early[4 * share :],
        grad_down.astype(F32),
        early[3 * share : 4 * share],
    )


def solution(mesh):
    in_specs = (
        P("dp", "seq", None),
        P("dp", "seq", None),
        P("dp"),
        P("dp", "seq"),
        P(BOTH),
        P(BOTH),
        P(BOTH, None),
        P(BOTH),
        P(BOTH, None),
        P(BOTH),
        P(BOTH),
        P(BOTH),
        P(BOTH, None),
        P(BOTH),
        P(BOTH, None),
        P(BOTH),
    )
    out_specs = (
        P("dp", "seq", None),
        P("dp", "seq", None),
        P(BOTH),
        P(BOTH),
        P(BOTH, None),
        P(BOTH),
        P(BOTH, None),
        P(BOTH),
        P(BOTH),
        P(BOTH),
        P(BOTH, None),
        P(BOTH),
        P(BOTH, None),
        P(BOTH),
    )
    return jax.shard_map(shards, mesh=mesh, in_specs=in_specs, out_specs=out_specs, check_vma=False)
```

```python
import functools
import math

import jax
import jax.numpy as jnp
from jax import lax
from jax.experimental import pallas as pl
from jax.experimental.pallas import tpu as pltpu
from jax.sharding import PartitionSpec as P

HEADS = 16
HEAD_DIM = 128
EPS = 1e-05
NEG = -1e30
FACTOR = HEAD_DIM ** (-0.5)
LOG2E = math.log2(math.e)
F32 = jnp.float32
BF16 = jnp.bfloat16
BOTH = ("dp", "seq")
MESH = pl.DeviceIdType.MESH


def nn(left, right):
    return lax.dot_general(left, right, (((1,), (0,)), ((), ())), preferred_element_type=F32)


def nt(left, right):
    return lax.dot_general(left, right, (((1,), (1,)), ((), ())), preferred_element_type=F32)


def tn(left, right):
    return lax.dot_general(left, right, (((0,), (0,)), ((), ())), preferred_element_type=F32)


def params(limit_mib=56):
    return pltpu.CompilerParams(dimension_semantics=("arbitrary",), vmem_limit_bytes=limit_mib * 2**20)


def cost(flops, moved, exps=0):
    return pl.CostEstimate(flops=int(flops), bytes_accessed=int(moved), transcendentals=int(exps))


def call_on_block(kernel, grid, inputs, fresh, shared, previous, scratch, estimate, rank=None, limit_mib=62):
    arrays = [item for item, _ in inputs]
    specs = [spec for _, spec in inputs]
    aliases = {}
    lead = 0 if rank is None else 1
    if previous is not None:
        for at, item in enumerate(previous):
            aliases[lead + len(arrays)] = len(fresh) + at
            arrays.append(item)
            specs.append(pl.BlockSpec(memory_space=pl.ANY))
    count = len(inputs)
    skipped = 0 if previous is None else len(previous)

    def body(*refs):
        refs = list(refs)
        kernel(*refs[: lead + count], *refs[lead + count + skipped :])

    out_specs = [spec for _, spec in fresh] + [spec for _, spec in shared]
    out_shape = [shape for shape, _ in fresh] + [shape for shape, _ in shared]
    if rank is None:
        results = pl.pallas_call(
            body, grid=grid, in_specs=specs, out_specs=out_specs, out_shape=out_shape, scratch_shapes=scratch,
            input_output_aliases=aliases, compiler_params=params(limit_mib), cost_estimate=estimate,
        )(*arrays)
    else:
        results = pl.pallas_call(
            body,
            grid_spec=pltpu.PrefetchScalarGridSpec(
                num_scalar_prefetch=1, grid=grid, in_specs=specs, out_specs=out_specs, scratch_shapes=scratch
            ),
            out_shape=out_shape, input_output_aliases=aliases, compiler_params=params(limit_mib), cost_estimate=estimate,
        )(rank, *arrays)
    return results[: len(fresh)], results[len(fresh) :]


def norm_parts(values):
    average = jnp.mean(values, axis=-1, keepdims=True)
    centred = values - average
    scale = lax.rsqrt(jnp.mean(centred * centred, axis=-1, keepdims=True) + EPS)
    return centred * scale, scale


def norm_backward(normed, scale, gain, upstream):
    weighted = upstream * gain
    return scale * (
        weighted
        - jnp.mean(weighted, axis=-1, keepdims=True)
        - normed * jnp.mean(weighted * normed, axis=-1, keepdims=True)
    )


def project_kernel(x, vectors, wq, wk, wv, normed, q, k, v, k_t, v_t):
    columns = wq.shape[1]
    rows = (norm_parts(x[...].astype(F32))[0] * vectors[0:1, :] + vectors[1:2, :]).astype(BF16)
    normed[...] = rows
    q[...] = (nn(rows, wq[...]) + vectors[7:8, :columns]).astype(BF16)
    keys = nn(rows, wk[...])
    k[...] = keys.astype(BF16)
    k_t[...] = keys.T.astype(BF16)
    values = nn(rows, wv[...]) + vectors[7:8, columns : 2 * columns]
    v[...] = values.astype(BF16)
    v_t[...] = values.T.astype(BF16)


def project(at, x, first, rows_here, vectors, weight, count, previous):
    width, columns = x.shape[1], weight.shape[1] // 3
    tile = min(256, rows_here)
    steps = rows_here // tile
    whole = lambda shape: pl.BlockSpec(shape, lambda i: (0, 0))
    rows = lambda n: pl.BlockSpec((tile, n), lambda i: (at * steps + i, 0))
    turned = pl.BlockSpec((columns, tile), lambda i: (0, at * steps + i))
    inputs = [
        (x, pl.BlockSpec((tile, width), lambda i: (first * steps + i, 0))),
        (vectors, whole(vectors.shape)),
        *[(weight, pl.BlockSpec((width, columns), lambda i, part=part: (0, part))) for part in range(3)],
    ]
    shape = lambda *dims: jax.ShapeDtypeStruct(dims, BF16)
    shared = [(shape(count, width), rows(width))] + [(shape(count, columns), rows(columns))] * 3
    shared += [(shape(columns, count), turned)] * 2
    return call_on_block(
        project_kernel, (steps,), inputs, [], shared, previous, [],
        cost(6 * rows_here * width * columns, 4 * rows_here * width + 6 * width * columns + 10 * rows_here * columns),
    )[1]


def rows_of(block, piece):
    return pl.ds(pl.multiple_of(block * piece, piece), piece)


def scores_of(key_ref, bias_ref, query, rel, piece, diagonal):
    rows = rows_of(rel, piece)
    scores = nt(key_ref[rows, :], query) * (FACTOR * LOG2E)
    key_bias = bias_ref[rows, :]
    if not diagonal:
        return scores + key_bias
    key_at = lax.broadcasted_iota(jnp.int32, scores.shape, 0)
    query_at = lax.broadcasted_iota(jnp.int32, scores.shape, 1)
    allowed = ((key_at < query_at) & (key_bias > -1.0)) | (key_at == query_at)
    return jnp.where(allowed, scores, NEG)


def attend_kernel(at, rank_ref, query_ref, key_ref, value_t, bias_ref, proj_ref, part_ref, attended, lse_ref, score_ref, sum_ref):
    piece = query_ref.shape[0]
    rank = rank_ref[0]
    head = pl.program_id(0)
    true = lax.bitwise_xor(at, rank)
    query = query_ref[...]

    def first(block, top):
        scores = scores_of(key_ref, bias_ref, query, lax.bitwise_xor(block, rank), piece, False)
        score_ref[rows_of(block, piece), :] = scores
        return jnp.maximum(top, jnp.max(scores, axis=0, keepdims=True))

    last = scores_of(key_ref, bias_ref, query, at, piece, True)
    top = lax.fori_loop(0, true, first, jnp.max(last, axis=0, keepdims=True))

    def weigh(scores, rel):
        weights = jnp.exp2(scores - top)
        return jnp.sum(weights, axis=0, keepdims=True), nn(value_t[:, rows_of(rel, piece)], weights.astype(BF16))

    def second(block, carry):
        total, out = carry
        more, part = weigh(score_ref[rows_of(block, piece), :], lax.bitwise_xor(block, rank))
        return total + more, out + part

    total, out = lax.fori_loop(0, true, second, weigh(last, at))
    result = (out / total).T.astype(BF16)
    attended[...] = result
    lse_ref[0] = top + jnp.log2(total)
    term = nn(result, proj_ref[...])

    @pl.when(head == 0)
    def _():
        sum_ref[...] = term

    @pl.when(head > 0)
    def _():
        sum_ref[...] += term

    @pl.when(head == pl.num_programs(0) - 1)
    def _():
        part_ref[...] = sum_ref[...].astype(BF16)


def attend(at, rank, q, k, v_t, key_bias, proj, piece, previous):
    length, columns = q.shape
    heads, width = columns // HEAD_DIM, proj.shape[1]
    inputs = [
        (q, pl.BlockSpec((piece, HEAD_DIM), lambda h, r: (at, h))),
        (k, pl.BlockSpec((length, HEAD_DIM), lambda h, r: (0, h))),
        (v_t, pl.BlockSpec((HEAD_DIM, length), lambda h, r: (h, 0))),
        (key_bias, pl.BlockSpec((length, 1), lambda h, r: (0, 0))),
        (proj, pl.BlockSpec((HEAD_DIM, width), lambda h, r: (h, 0))),
    ]
    fresh = [(jax.ShapeDtypeStruct((piece, width), BF16), pl.BlockSpec((piece, width), lambda h, r: (0, 0)))]
    shared = [
        (jax.ShapeDtypeStruct((length, columns), BF16), pl.BlockSpec((piece, HEAD_DIM), lambda h, r: (at, h))),
        (jax.ShapeDtypeStruct((heads, 1, length), F32), pl.BlockSpec((1, 1, piece), lambda h, r: (h, 0, at))),
    ]
    scratch = [pltpu.VMEM((length, piece), F32), pltpu.VMEM((piece, width), F32)]
    (part,), shared = call_on_block(
        functools.partial(attend_kernel, at), (heads,), inputs, fresh, shared, previous, scratch,
        cost(
            2 * length * piece * columns * 1.3 + 2 * piece * columns * width, 6 * length * columns + 2 * width * columns,
            heads * length * piece * 0.6,
        ), rank,
    )
    return part, shared


def feed_kernel(normed, cot, fc, bias, down, part, active_out, hidden_out, normed_out, cot_out, sum_ref):
    step = pl.program_id(0)
    weights = fc[...]
    hidden = nn(normed[...], weights) + bias[...]
    grad_active = nt(cot[...], down[...])
    inner = math.sqrt(2 / math.pi) * (hidden + 0.044715 * (hidden * hidden * hidden))
    bent = jnp.tanh(inner)
    half = 0.5 * (1.0 + bent)
    active_out[...] = (hidden * half).astype(BF16)
    slope = half + (0.5 * hidden) * (1.0 - bent * bent) * (
        math.sqrt(2 / math.pi) * (1.0 + (3 * 0.044715) * (hidden * hidden))
    )
    grad_hidden = (grad_active * slope).astype(BF16)
    hidden_out[...] = grad_hidden
    term = nt(grad_hidden, weights)

    @pl.when(step == 0)
    def _():
        sum_ref[...] = term
        normed_out[...] = normed[...]
        cot_out[...] = cot[...]

    @pl.when(step > 0)
    def _():
        sum_ref[...] += term

    @pl.when(step == pl.num_programs(0) - 1)
    def _():
        part[...] = sum_ref[...].astype(BF16)


def feed(at, normed, cot, fc, bias, down, count, previous):
    piece, width = normed.shape
    inner = fc.shape[1]
    tile = min(512, inner)
    length = piece * count
    rows = pl.BlockSpec((piece, width), lambda j: (0, 0))
    inputs = [
        (normed, rows),
        (cot, rows),
        (fc, pl.BlockSpec((width, tile), lambda j: (0, j))),
        (bias, pl.BlockSpec((1, tile), lambda j: (0, j))),
        (down, pl.BlockSpec((tile, width), lambda j: (j, 0))),
    ]
    shape = lambda n: jax.ShapeDtypeStruct((length, n), BF16)
    columns = pl.BlockSpec((piece, tile), lambda j: (at, j))
    here = pl.BlockSpec((piece, width), lambda j: (at, 0))
    fresh = [(jax.ShapeDtypeStruct((piece, width), BF16), rows)]
    shared = [(shape(inner), columns), (shape(inner), columns), (shape(width), here), (shape(width), here)]
    (part,), shared = call_on_block(
        feed_kernel, (inner // tile,), inputs, fresh, shared, previous, [pltpu.VMEM((piece, width), F32)],
        cost(6 * piece * width * inner, 4 * width * inner + 10 * piece * width + 4 * piece * inner, piece * inner),
    )
    return part, shared


def retreat_kernel(
    at, first_call, last_call, rank_ref, low_ref, proj_ref, query_ref, lse_ref, key_ref, value_ref, key_t, bias_ref, *rest
):
    rest = list(rest)
    key_in, value_in = (None, None) if first_call else (rest.pop(0), rest.pop(0))
    key_out, value_out, query_out, low_out, prob_ref, chance_ref, key_sum, value_sum = rest
    piece = query_ref.shape[0]
    rank = rank_ref[0]
    true = lax.bitwise_xor(at, rank)

    @pl.when(pl.program_id(0) == 0)
    def _():
        low_out[...] = low_ref[...]

    if first_call:
        key_sum[...] = jnp.zeros_like(key_sum)
        value_sum[...] = jnp.zeros_like(value_sum)
    else:
        key_sum[...] = key_in[...]
        value_sum[...] = value_in[...]
    query, lse = query_ref[...], lse_ref[0]
    grad = nt(low_ref[...], proj_ref[...]).astype(BF16)

    def measure(scores, rel):
        rows = rows_of(rel, piece)
        probs = jnp.exp2(scores - lse)
        grad_chances = nt(value_ref[rows, :], grad)
        value_sum[rows, :] += nn(probs.astype(BF16), grad)
        prob_ref[rows, :] = probs
        chance_ref[rows, :] = grad_chances
        return jnp.sum(probs * grad_chances, axis=0, keepdims=True)

    def first(block, weighted):
        rel = lax.bitwise_xor(block, rank)
        return weighted + measure(scores_of(key_ref, bias_ref, query, rel, piece, False), rel)

    last = scores_of(key_ref, bias_ref, query, at, piece, True)
    weighted = lax.fori_loop(0, true, first, measure(last, at))

    def second(block, total):
        rows = rows_of(lax.bitwise_xor(block, rank), piece)
        grad_scores = (prob_ref[rows, :] * (chance_ref[rows, :] - weighted)).astype(BF16)
        key_sum[rows, :] += nn(grad_scores, query)
        return total + nn(key_t[:, rows], grad_scores)

    total = lax.fori_loop(0, true + 1, second, jnp.zeros((HEAD_DIM, piece), F32))
    query_out[...] = (total * FACTOR).T.astype(BF16)
    if last_call:
        key_out[...] = (key_sum[...] * FACTOR).astype(BF16)
        value_out[...] = value_sum[...].astype(BF16)
    else:
        key_out[...] = key_sum[...]
        value_out[...] = value_sum[...]


def retreat(at, rank, low, proj, q, lse, k, v, k_t, key_bias, sums, previous, last_call):
    length, columns = q.shape
    piece, width = low.shape
    heads = columns // HEAD_DIM
    tall = pl.BlockSpec((length, HEAD_DIM), lambda h, r: (0, h))
    part = pl.BlockSpec((piece, HEAD_DIM), lambda h, r: (at, h))
    inputs = [
        (low, pl.BlockSpec((piece, width), lambda h, r: (0, 0))),
        (proj, pl.BlockSpec((HEAD_DIM, width), lambda h, r: (h, 0))),
        (q, part),
        (lse, pl.BlockSpec((1, 1, piece), lambda h, r: (h, 0, at))),
        (k, tall),
        (v, tall),
        (k_t, pl.BlockSpec((HEAD_DIM, length), lambda h, r: (h, 0))),
        (key_bias, pl.BlockSpec((length, 1), lambda h, r: (0, 0))),
    ]
    if sums is not None:
        inputs += [(item, tall) for item in sums]
    kind = BF16 if last_call else F32
    fresh = [(jax.ShapeDtypeStruct((length, columns), kind), tall)] * 2
    shared = [
        (jax.ShapeDtypeStruct((length, columns), BF16), part),
        (jax.ShapeDtypeStruct((length, width), BF16), pl.BlockSpec((piece, width), lambda h, r: (at, 0))),
    ]
    scratch = [pltpu.VMEM((length, piece), F32)] * 2 + [pltpu.VMEM((length, HEAD_DIM), F32)] * 2
    return call_on_block(
        functools.partial(retreat_kernel, at, sums is None, last_call), (heads,), inputs, fresh, shared, previous,
        scratch,
        cost(
            5 * 1.3 * length * piece * columns + 2 * piece * columns * width, 20 * length * columns,
            heads * length * piece * 0.6,
        ), rank,
    )


def back_kernel(grads, weight, out):
    out[...] = nt(grads[...], weight[...]).astype(BF16)


def back(at, grads, weight, piece):
    columns, width = grads.shape[1], weight.shape[0]
    tile = min(512, width)
    return pl.pallas_call(
        back_kernel,
        grid=(width // tile,),
        in_specs=[
            pl.BlockSpec((piece, columns), lambda j: (at, 0)),
            pl.BlockSpec((tile, columns), lambda j: (j, 0)),
        ],
        out_specs=pl.BlockSpec((piece, tile), lambda j: (0, j)),
        out_shape=jax.ShapeDtypeStruct((piece, width), BF16),
        compiler_params=params(),
        cost_estimate=cost(2 * piece * width * columns, 2 * width * columns + 2 * piece * (columns + width)),
    )(grads, weight)


def part_specs(parts, tile, steps, width):
    arrays, specs = [], []
    for part in parts:
        if isinstance(part, tuple):
            middle = steps // 2
            arrays += list(part)
            specs.append(pl.BlockSpec((tile, width), lambda i: (jnp.minimum(i, middle - 1), 0)))
            specs.append(pl.BlockSpec((tile, width), lambda i: (jnp.maximum(i - middle, 0), 0)))
        else:
            arrays.append(part)
            specs.append(pl.BlockSpec((tile, width), lambda i: (i, 0)))
    return arrays, specs


def add_parts(kinds, refs):
    total = None
    upper = pl.program_id(0) < pl.num_programs(0) // 2
    for kind in kinds:
        if kind:
            high, low = refs.pop(0)[...], refs.pop(0)[...]
            term = jnp.where(upper, high.astype(F32), low.astype(F32))
        else:
            term = refs.pop(0)[...].astype(F32)
        total = term if total is None else total + term
    return total


def rowwise(kernel, parts, rows, vectors, outputs, sums):
    count, width = rows[0].shape
    tile = min(128, count // 2)
    steps = count // tile
    arrays, specs = part_specs(parts, tile, steps, width)
    kinds = [isinstance(part, tuple) for part in parts]
    specs += [pl.BlockSpec((tile, width), lambda i: (i, 0))] * len(rows)
    specs += [pl.BlockSpec((1, width), lambda i: (0, 0))] * len(vectors)

    def body(*refs):
        refs = list(refs)
        total = add_parts(kinds, refs)
        tiles = [refs.pop(0)[...] for _ in rows]
        given = [refs.pop(0)[...] for _ in vectors]
        results = kernel(total, tiles, given)
        for result, _ in zip(results, outputs):
            refs.pop(0)[...] = result
        for result in results[len(outputs) :]:
            ref = refs.pop(0)
            column = jnp.sum(result, axis=0, keepdims=True)

            @pl.when(pl.program_id(0) == 0)
            def _():
                ref[...] = column

            @pl.when(pl.program_id(0) > 0)
            def _():
                ref[...] += column

    return pl.pallas_call(
        body,
        grid=(steps,),
        in_specs=specs,
        out_specs=[pl.BlockSpec((tile, width), lambda i: (i, 0))] * len(outputs)
        + [pl.BlockSpec((1, width), lambda i: (0, 0))] * sums,
        out_shape=[jax.ShapeDtypeStruct((count, width), kind) for kind in outputs]
        + [jax.ShapeDtypeStruct((1, width), F32)] * sums,
        compiler_params=params(),
        cost_estimate=cost(20 * count * width, count * width * (2 * len(arrays) + 4 * len(rows) + 4 * len(outputs))),
    )(*arrays, *rows, *vectors)


def middle_kernel(total, rows, vectors):
    (tokens,), (bias, gain, shift_) = rows, vectors
    middle = tokens.astype(F32) + (total + bias)
    return middle, (norm_parts(middle)[0] * gain + shift_).astype(BF16)


def out_kernel(total, rows, vectors):
    return (((rows[0] + (total + vectors[0])).astype(BF16)),)


def middle_back_kernel(total, rows, vectors):
    (middle, cot), (gain,) = rows, vectors
    normed, scale = norm_parts(middle)
    cot = cot.astype(F32)
    grad = cot + norm_backward(normed, scale, gain, total)
    low = grad.astype(BF16)
    return grad, low, total * normed, total, low.astype(F32), cot


def tokens_back_kernel(total, rows, vectors):
    (tokens, grad_middle), (gain,) = rows, vectors
    normed, scale = norm_parts(tokens.astype(F32))
    return grad_middle + norm_backward(normed, scale, gain, total), total * normed, total


def lay_out(rank, blocks, width, places):
    rows = blocks[0][0].shape[0]
    count, each = len(blocks), len(blocks[0])
    unit = places[1]

    def body(rank_ref, *refs):
        out = refs[-1]
        for k in range(count):
            source = lax.bitwise_xor(k, rank_ref[0])
            for array, column, target in places[0](source):
                out[:, pl.ds(pl.multiple_of(target * unit, unit), unit)] = refs[k * each + array][
                    :, column * unit : (column + 1) * unit
                ].astype(F32)

    arrays = [item for block in blocks for item in block]
    return pl.pallas_call(
        body,
        grid_spec=pltpu.PrefetchScalarGridSpec(
            num_scalar_prefetch=1,
            grid=(1,),
            in_specs=[pl.BlockSpec(item.shape, lambda i, r: (0, 0)) for item in arrays],
            out_specs=pl.BlockSpec((rows, width), lambda i, r: (0, 0)),
        ),
        out_shape=jax.ShapeDtypeStruct((rows, width), F32),
        compiler_params=params(),
        cost_estimate=cost(rows * width, 6 * rows * width),
    )(rank, *arrays)


def neighbours():
    rank = lax.axis_index("seq")
    return rank + 1 - 2 * lax.rem(rank, 2), rank + 2 - 4 * lax.rem(lax.div(rank, 2), 2)


def remote(source, target, send, receive, axis, device):
    return pltpu.make_async_remote_copy(
        src_ref=source, dst_ref=target, send_sem=send, recv_sem=receive, device_id={axis: device}, device_id_type=MESH
    )


def greet(axis, device):
    pl.semaphore_signal(pltpu.get_barrier_semaphore(), inc=1, device_id={axis: device}, device_id_type=MESH)


def flip(first, second):
    low = lax.rem(first + second, 2)
    high = lax.rem(lax.div(first, 2) + lax.div(second, 2), 2)
    return 2 * high + low


class LevelScatter:
    def __init__(self, source, mate_in, summed, got, send, receive):
        self.source, self.mate_in, self.summed, self.got = source, mate_in, summed, got
        self.send, self.receive = send, receive
        self.rows = mate_in.shape[0] // 4
        self.place = lax.axis_index("dp")
        self.level, self.core = lax.div(self.place, 2), lax.rem(self.place, 2)
        self.mate = self.place + 1 - 2 * self.core

    def greet(self):
        greet("dp", self.mate)
        count = jnp.int32(1)
        for step in (1, 2):
            up, down = self.level + step <= 3, self.level >= step
            pl.when(up)(lambda step=step: greet("dp", self.place + 2 * step))
            pl.when(down)(lambda step=step: greet("dp", self.place - 2 * step))
            count = count + up.astype(jnp.int32) + down.astype(jnp.int32)
        return count

    def block(self, ref, at):
        return ref.at[pl.ds(at * self.rows, self.rows)]

    def swaps(self):
        return [
            remote(
                self.block(self.source, 2 * at + 1 - self.core), self.block(self.mate_in, at),
                self.send.at[at], self.receive.at[at], "dp", self.mate,
            )
            for at in range(4)
        ]

    def start(self):
        for item in self.swaps():
            item.start()

    def add(self, first, second, out, grid, first_at, second_at, out_at):
        def body(left, right, total):
            total[...] = (left[...].astype(F32) + right[...].astype(F32)).astype(total.dtype)

        spec = lambda at: pl.BlockSpec((self.rows, first.shape[1]), lambda i: (at(i), 0))
        pltpu.emit_pipeline(
            body, grid=(grid,), in_specs=[spec(first_at), spec(second_at)], out_specs=[spec(out_at)]
        )(first, second, out)

    def hop(self, at, slot, index, steps):
        return remote(
            self.block(self.summed, at), self.block(self.got, slot), self.send.at[4 + index], self.receive.at[4 + slot],
            "dp", self.place + 2 * steps,
        )

    def hops(self):
        level = self.level
        return [
            (level == 0, self.hop(3, 3, 0, 1)),
            (level == 3, self.hop(0, 3, 0, -1)),
            (level == 0, self.hop(2, 2, 1, 2)),
            (level == 3, self.hop(1, 2, 1, -2)),
            (level <= 2, self.hop(lax.rem(level + 1, 4), 0, 2, 1)),
            (level >= 1, self.hop(lax.rem(level + 3, 4), 1, 3, -1)),
        ]

    def first_hops(self):
        hops, inner = self.hops(), (self.level == 1) | (self.level == 2)
        return hops[:2] + [(inner, hops[4][1]), (inner, hops[5][1])]

    def later_hops(self):
        hops = self.hops()
        return hops[2:4] + [(self.level == 0, hops[4][1]), (self.level == 3, hops[5][1])]

    def passes(self):
        return [(self.level == 1, self.hop(3, 2, 1, 2)), (self.level == 2, self.hop(0, 2, 1, -2))]

    def combine(self):
        for item in self.swaps():
            item.wait_recv()
        self.add(
            self.source, self.mate_in, self.summed, 4, lambda i: 2 * i + self.core, lambda i: i, lambda i: i
        )

    def spread(self):
        self.combine()
        for condition, copy in self.first_hops():
            pl.when(condition)(lambda copy=copy: copy.start())

    def arrive(self, slot):
        here = self.block(self.got, slot)
        remote(here, here, self.send.at[0], self.receive.at[4 + slot], "dp", self.mate).wait_recv()

    def pass_on(self):
        for level, at in ((1, 3), (2, 0)):

            @pl.when(self.level == level)
            def _(at=at):
                self.arrive(3)
                self.add(self.summed, self.got, self.summed, 1, lambda i: at, lambda i: 3, lambda i: at)

        for condition, copy in self.passes() + self.later_hops():
            pl.when(condition)(lambda copy=copy: copy.start())

    def finish(self, out):
        level = self.level
        pl.when(level >= 1)(lambda: self.arrive(0))
        pl.when(level <= 2)(lambda: self.arrive(1))
        self.arrive(2)
        rows = min(64, self.rows)

        def body(own, mate, below, above, far, total):
            value = own[...].astype(F32) + mate[...].astype(F32) + far[...].astype(F32)
            below_term, above_term = below[...].astype(F32), above[...].astype(F32)
            value = value + jnp.where(level >= 1, below_term, 0.0) + jnp.where(level <= 2, above_term, 0.0)
            total[...] = value.astype(total.dtype)

        steps = self.rows // rows
        spec = lambda at: pl.BlockSpec((rows, out.shape[1]), lambda i: (at * steps + i, 0))
        pltpu.emit_pipeline(
            body,
            grid=(steps,),
            in_specs=[spec(self.place), spec(level), spec(0), spec(1), spec(2)],
            out_specs=[spec(0)],
        )(self.source, self.mate_in, self.got, self.got, self.got, out)

    def close(self):
        for item in self.swaps():
            item.wait_send()
        for condition, copy in self.hops() + self.passes():
            pl.when(condition)(lambda copy=copy: copy.wait_send())


class LateScatter(LevelScatter):
    def __init__(self, summed, got, through, own, send, receive, load):
        self.summed, self.got, self.through, self.own = summed, got, through, own
        self.send, self.receive, self.load = send, receive, load
        self.rows = own.shape[0]
        self.place = lax.axis_index("dp")
        self.level, self.core = lax.div(self.place, 2), lax.rem(self.place, 2)
        self.mate = self.place + 1 - 2 * self.core

    def loads(self):
        passed_on = 3 * lax.rem(self.level, 2)
        return (
            pltpu.make_async_copy(self.block(self.summed, self.level), self.own, self.load.at[0]),
            pltpu.make_async_copy(self.block(self.summed, passed_on), self.through, self.load.at[1]),
        )

    def passes(self):
        target = self.block(self.got, 2)
        send, receive = self.send.at[4 + 1], self.receive.at[4 + 2]
        return [
            (self.level == 1, remote(self.through, target, send, receive, "dp", self.place + 4)),
            (self.level == 2, remote(self.through, target, send, receive, "dp", self.place - 4)),
        ]

    def start(self):
        for condition, copy in self.first_hops():
            pl.when(condition)(lambda copy=copy: copy.start())
        for item in self.loads():
            item.start()

    def part(self, slot):
        return self.got[slot * self.rows : (slot + 1) * self.rows, :].astype(F32)

    def pass_on(self):
        for item in self.loads():
            item.wait()

        @pl.when((self.level == 1) | (self.level == 2))
        def _():
            self.arrive(3)
            self.through[...] = (self.through[...].astype(F32) + self.part(3)).astype(BF16)

        for condition, copy in self.passes() + self.later_hops():
            pl.when(condition)(lambda copy=copy: copy.start())

    def finish(self, out):
        level = self.level
        pl.when(level >= 1)(lambda: self.arrive(0))
        pl.when(level <= 2)(lambda: self.arrive(1))
        self.arrive(2)
        value = self.own[...].astype(F32) + self.part(2)
        value = value + jnp.where(level >= 1, self.part(0), 0.0)
        value = value + jnp.where(level <= 2, self.part(1), 0.0)
        out[...] = value.astype(BF16)

    def close(self):
        for condition, copy in self.hops() + self.passes():
            pl.when(condition)(lambda copy=copy: copy.wait_send())


class NearScatter(LevelScatter):
    def part(self, ref, at):
        return ref[pl.ds(pl.multiple_of(at * self.rows, self.rows), self.rows), :].astype(F32)

    def spread(self):
        for item in self.swaps():
            item.wait_recv()
        for at in range(4):
            total = self.part(self.source, 2 * at + self.core) + self.part(self.mate_in, at)
            self.summed[at * self.rows : (at + 1) * self.rows, :] = total.astype(BF16)
        for condition, copy in self.first_hops():
            pl.when(condition)(lambda copy=copy: copy.start())

    def pass_on(self):
        for level, at in ((1, 3), (2, 0)):

            @pl.when(self.level == level)
            def _(at=at):
                self.arrive(3)
                total = self.part(self.summed, at) + self.part(self.got, 3)
                self.summed[at * self.rows : (at + 1) * self.rows, :] = total.astype(BF16)

        for condition, copy in self.passes() + self.later_hops():
            pl.when(condition)(lambda copy=copy: copy.start())

    def finish(self, out):
        level = self.level
        pl.when(level >= 1)(lambda: self.arrive(0))
        pl.when(level <= 2)(lambda: self.arrive(1))
        self.arrive(2)
        value = self.part(self.source, self.place) + self.part(self.mate_in, level) + self.part(self.got, 2)
        value = value + jnp.where(level >= 1, self.part(self.got, 0), 0.0)
        value = value + jnp.where(level <= 2, self.part(self.got, 1), 0.0)
        out[...] = value.astype(BF16)


class LevelGather:
    def __init__(self, own, full, send, receive, mate_send, mate_receive):
        self.own, self.full, self.send, self.receive = own, full, send, receive
        self.mate_send, self.mate_receive = mate_send, mate_receive
        self.rows = own.shape[0]
        self.place = lax.axis_index("dp")
        self.level, self.core = lax.div(self.place, 2), lax.rem(self.place, 2)
        self.mate = self.place + 1 - 2 * self.core

    greet = LevelScatter.greet

    def shard(self, level):
        return self.full.at[pl.ds((2 * level + self.core) * self.rows, self.rows)]

    def hop(self, index, steps, slot):
        return remote(
            self.own, self.shard(self.level), self.send.at[index], self.receive.at[slot], "dp", self.place + 2 * steps
        )

    def near(self):
        return [(self.level <= 2, self.hop(0, 1, 0)), (self.level >= 1, self.hop(1, -1, 1))]

    def second(self):
        inner = (self.level == 1) | (self.level == 2)
        lower, upper = self.shard(self.level - 1), self.shard(self.level + 1)
        return [
            (inner, remote(lower, lower, self.send.at[2], self.receive.at[2], "dp", self.place + 2)),
            (inner, remote(upper, upper, self.send.at[3], self.receive.at[2], "dp", self.place - 2)),
        ]

    def passes(self):
        first, last = self.shard(0), self.shard(3)
        return [
            (self.level == 2, remote(first, first, self.send.at[4], self.receive.at[3], "dp", self.place + 2)),
            (self.level == 1, remote(last, last, self.send.at[4], self.receive.at[3], "dp", self.place - 2)),
        ]

    def across(self, index, level):
        here = self.own if index == 4 else self.shard(level)
        return remote(here, self.shard(level), self.mate_send.at[index], self.mate_receive.at[index], "dp", self.mate)

    def arrivals(self, slots):
        level = self.level
        two_away = level + 2 - 4 * lax.div(level, 2)
        every = [
            (level >= 1, 0, level - 1),
            (level <= 2, 1, level + 1),
            (level >= 0, 2, two_away),
            ((level == 0) | (level == 3), 3, 3 - level),
        ]
        return [item for item in every if item[1] in slots]

    def start(self, hops):
        for condition, copy in hops:
            pl.when(condition)(lambda copy=copy: copy.start())

    def take(self, slots):
        for condition, slot, level in self.arrivals(slots):

            @pl.when(condition)
            def _(slot=slot, level=level):
                here = self.shard(level)
                remote(here, here, self.send.at[0], self.receive.at[slot], "dp", self.mate).wait_recv()
                self.across(slot, level).start()

    def finish(self, slots, hops):
        for condition, slot, level in self.arrivals(slots):
            pl.when(condition)(lambda slot=slot, level=level: self.across(slot, level).wait())
        for condition, copy in hops:
            pl.when(condition)(lambda copy=copy: copy.wait_send())


def opening_kernel(
    tokens, cot, qkv_weight, fc_weight, small, down, proj,
    token_all, qkv_full, fc_rows, cot_one, cot_two, down_full, proj_full, vectors, key_bias,
    qkv_pieces, fc_pieces, token_buf, qkv_rows, small_rows, small_full, proj_rows, square, local, send, receive, up_send, up_receive, down_send, down_receive, mate_send, mate_receive,
    level_send, level_receive, level_mate_send, level_mate_receive,
):
    piece = tokens.shape[0]
    half = piece // 2
    gather = LevelGather(down, down_full, level_send, level_receive, level_mate_send, level_mate_receive)
    me, place = lax.axis_index("seq"), lax.axis_index("dp")
    one, two = neighbours()
    three = 3 - me
    stages = lax.axis_size("dp") // 2
    level, core = lax.div(place, 2), lax.rem(place, 2)
    mate = place + 1 - 2 * core
    above, below = level < stages - 1, level > 0

    for device in (one, two, three):
        greet("seq", device)
    greet("dp", mate)
    pl.when(above)(lambda: greet("dp", place + 2))
    pl.when(below)(lambda: greet("dp", place - 2))
    swaps = core != lax.rem(me, 2)
    partner = {"dp": mate, "seq": one}

    @pl.when(swaps)
    def _():
        pl.semaphore_signal(pltpu.get_barrier_semaphore(), inc=1, device_id=partner, device_id_type=MESH)

    heads = qkv_pieces.shape[2] // (3 * HEAD_DIM)
    for rank in range(4):
        for part in range(3):
            for head in range(heads):
                source = (part * HEADS + (head * 2 + rank % 2) * 2 + rank // 2) * HEAD_DIM
                target = (part * heads + head) * HEAD_DIM
                qkv_pieces[rank, :, target : target + HEAD_DIM] = qkv_weight[:, source : source + HEAD_DIM]
    count = 4 + above.astype(jnp.int32) + below.astype(jnp.int32) + swaps.astype(jnp.int32)
    pl.semaphore_wait(pltpu.get_barrier_semaphore(), count)

    def block(ref, at, start=0, size=piece):
        return ref.at[pl.ds(at * piece + start, size)]

    def spread(pieces, target, at):
        rows = target.shape[0] // 4
        mine = target.at[pl.ds(me * rows, rows)]
        source = lambda device: pieces if pieces is small else pieces.at[device]
        copies = [
            remote(source(device), mine, send.at[at + i], receive.at[at + i], "seq", device)
            for i, device in enumerate((one, two, three))
        ]
        return copies, source(me), mine

    qkv_copies, qkv_own, qkv_mine = spread(qkv_pieces, qkv_rows, 0)
    small_copies, small_own, small_mine = spread(small, small_rows, 3)
    fc_copies, fc_own, fc_mine = spread(fc_pieces, fc_rows, 6)
    token_one = remote(tokens, block(token_all, 1), send.at[9], receive.at[9], "seq", one)
    token_two = remote(tokens, block(token_all, 2), send.at[10], receive.at[10], "seq", two)
    token_three = (
        remote(block(token_all, 1, 0, half), block(token_all, 3, 0, half), send.at[11], receive.at[11], "seq", two),
        remote(block(token_all, 2, half, half), block(token_all, 3, half, half), send.at[12], receive.at[12], "seq", one),
    )
    first_kept = [pltpu.make_async_copy(qkv_own, qkv_mine, local.at[0]), pltpu.make_async_copy(small_own, small_mine, local.at[1])]
    later_kept = [
        pltpu.make_async_copy(fc_own, fc_mine, local.at[2]),
        pltpu.make_async_copy(token_buf, block(token_all, 0), local.at[3]),
    ]
    token_load = pltpu.make_async_copy(tokens, token_buf, local.at[4])
    cot_copies = (
        remote(cot.at[pl.ds(0, half)], cot_one, send.at[13], receive.at[13], "seq", one),
        remote(cot.at[pl.ds(0, half)], cot_two, send.at[14], receive.at[14], "seq", two),
    )

    proj_copy = pltpu.make_async_remote_copy(
        src_ref=proj, dst_ref=proj_rows, send_sem=send.at[15], recv_sem=receive.at[15], device_id=partner,
        device_id_type=MESH,
    )
    chains = ((qkv_rows, qkv_full), (small_rows, small_full), (proj_rows, proj_full))

    def shard(array, at):
        rows = chains[array][0].shape[0]
        return chains[array][1].at[pl.ds((2 * at + core) * rows, rows)]

    def rising(array, step, device):
        at = level - (step - 1)
        source = chains[array][0] if step == 1 else shard(array, at)
        return remote(source, shard(array, at), up_send.at[array, step - 1], up_receive.at[array, step - 1], "dp", device)

    def falling(array, step, device):
        at = level + (step - 1)
        source = chains[array][0] if step == 1 else shard(array, at)
        return remote(source, shard(array, at), down_send.at[array, step - 1], down_receive.at[array, step - 1], "dp", device)

    def across(array, index, at):
        source = chains[array][0] if index == 0 else shard(array, at)
        return remote(source, shard(array, at), mate_send.at[array, index], mate_receive.at[array, index], "dp", mate)

    rises = lambda step: above & (level >= step - 1)
    falls = lambda step: below & (level <= stages - step)
    from_below = lambda step: level >= step
    from_above = lambda step: level + step <= stages - 1

    def relay(step):
        @pl.when(rises(step))
        def _():
            for array in (1, 0, 2):
                rising(array, step, place + 2).start()

        @pl.when(falls(step))
        def _():
            for array in (1, 0, 2):
                falling(array, step, place - 2).start()

    def take(step):
        @pl.when(from_below(step))
        def _():
            for array in (1, 0, 2):
                got = shard(array, level - step)
                remote(got, got, up_send.at[array, step - 1], up_receive.at[array, step - 1], "dp", mate).wait_recv()
                across(array, step, level - step).start()

        @pl.when(from_above(step))
        def _():
            for array in (1, 0, 2):
                got = shard(array, level + step)
                remote(got, got, down_send.at[array, step - 1], down_receive.at[array, step - 1], "dp", mate).wait_recv()
                across(array, stages - 1 + step, level + step).start()

    for copy in qkv_copies + small_copies + first_kept:
        copy.start()
    pl.when(swaps)(proj_copy.start)

    @pl.when(jnp.logical_not(swaps))
    def _():
        proj_rows[...] = proj[...]

    token_one.start()
    token_two.start()
    gather.start(gather.near())
    gather.across(4, level).start()
    down_kept = pltpu.make_async_copy(down, gather.shard(level), local.at[8])
    down_kept.start()
    token_load.start()
    inner = fc_pieces.shape[2] // 8
    for rank in range(4):
        for d in range(8):
            source = (d * 4 + rank) * inner
            fc_pieces[rank, :, d * inner : (d + 1) * inner] = fc_weight[:, source : source + inner]
    token_load.wait()
    for copy in qkv_copies + small_copies:
        copy.wait_recv()
    pl.when(swaps)(proj_copy.wait_recv)
    for copy in first_kept:
        copy.wait()
    relay(1)
    own_full = [pltpu.make_async_copy(chains[array][0], shard(array, level), local.at[5 + array]) for array in range(3)]
    for array in range(3):
        across(array, 0, level).start()
        own_full[array].start()
    for copy in fc_copies + later_kept:
        copy.start()
    for copy in cot_copies:
        copy.start()
    take(1)
    relay(2)
    take(2)
    relay(3)
    gather.take((0, 1))
    token_one.wait_recv()
    token_two.wait_recv()
    for copy in token_three:
        copy.start()
    take(3)
    for copy in later_kept + own_full:
        copy.wait()
    for copy in fc_copies:
        copy.wait_recv()
    for copy in qkv_copies + small_copies + fc_copies:
        copy.wait_send()
    token_one.wait_send()
    token_two.wait_send()
    for step in range(1, stages):

        @pl.when(rises(step))
        def _(step=step):
            for array in range(3):
                rising(array, step, place + 2).wait_send()

        @pl.when(falls(step))
        def _(step=step):
            for array in range(3):
                falling(array, step, place - 2).wait_send()

        @pl.when(from_below(step))
        def _(step=step):
            for array in range(3):
                across(array, step, level - step).wait()

        @pl.when(from_above(step))
        def _(step=step):
            for array in range(3):
                across(array, stages - 1 + step, level + step).wait()

    for array in range(3):
        across(array, 0, level).wait()
    for copy in token_three:
        copy.wait()
    down_kept.wait()
    pl.when(swaps)(proj_copy.wait_send)
    tile = lambda d, s: small_full[pl.ds(pl.multiple_of((d * 4 + s) * 16, 16), 16), :].astype(F32)
    vectors[...] = jnp.zeros_like(vectors)
    for d in range(8):
        for pair in range(2):
            both = tile(d, 2 * pair) + tile(d, 2 * pair + 1)
            vectors[0:6, (2 * d + pair) * 128 : (2 * d + pair + 1) * 128] = both[0:6]
        own = tile(d, me)
        for i in range(2):
            vectors[6:7, (2 * d + i) * 128 : (2 * d + i + 1) * 128] = own[7 + i : 8 + i]
        bias = tile(d, 2 * lax.rem(me, 2) + lax.div(me, 2))
        vectors[7:8, d * HEAD_DIM : (d + 1) * HEAD_DIM] = bias[6:7]
    square[...] = jnp.zeros_like(square)
    for i in range(4):
        square[4 * i : 4 * i + 4, :] = tile(place, flip(me, i))[9:13]
    turned = square[...].T
    lane = lax.broadcasted_iota(jnp.int32, turned.shape, 1)
    for i in range(16):
        flag = jnp.sum(jnp.where(lane == i, turned, 0.0), axis=1, keepdims=True)
        key_bias[i * 128 : (i + 1) * 128, :] = jnp.where(flag > 0, 0.0, NEG)
    for copy in cot_copies:
        copy.wait()
    gather.finish((0, 1), gather.near())
    gather.across(4, level).wait()


def opening(tokens, cot, qkv_weight, fc_weight, small, down, proj, dp_count):
    piece, width = tokens.shape
    steps = dp_count // 2 - 1
    anywhere = pl.BlockSpec(memory_space=pltpu.HBM)
    shape = lambda rows, columns: jax.ShapeDtypeStruct((rows, columns), BF16)
    dma = pltpu.SemaphoreType.DMA
    inside = pl.BlockSpec(memory_space=pltpu.VMEM)
    own_rows, columns, inner = qkv_weight.shape[0], qkv_weight.shape[1] // 4, fc_weight.shape[1] // 4
    rows, fine = 4 * own_rows, 4 * small.shape[0]
    return pl.pallas_call(
        opening_kernel,
        in_specs=[anywhere] * 2 + [inside] * 5,
        out_specs=[anywhere] * 7 + [inside] * 2,
        out_shape=[
            shape(4 * piece, width),
            shape(rows * dp_count, columns),
            shape(rows, inner),
            shape(piece // 2, width),
            shape(piece // 2, width),
            shape(down.shape[0] * dp_count, width),
            shape(proj.shape[0] * dp_count, width),
            jax.ShapeDtypeStruct((8, width), F32),
            jax.ShapeDtypeStruct((4 * piece, 1), F32),
        ],
        scratch_shapes=[
            pltpu.VMEM((4, own_rows, columns), BF16), pltpu.VMEM((4, own_rows, inner), BF16),
            pltpu.VMEM((piece, width), BF16),
            pltpu.VMEM((rows, columns), BF16), pltpu.VMEM((fine, 128), BF16), pltpu.VMEM((fine * dp_count, 128), BF16),
            pltpu.VMEM(proj.shape, BF16), pltpu.VMEM((128, 128), F32),
            dma((9,)), dma((16,)), dma((16,)), dma((3, steps)), dma((3, steps)), dma((3, steps)), dma((3, steps)),
            dma((3, 2 * steps + 1)), dma((3, 2 * steps + 1)), dma((5,)), dma((4,)), dma((5,)), dma((5,)),
        ],
        compiler_params=pltpu.CompilerParams(collective_id=0, has_side_effects=True, vmem_limit_bytes=62 * 2**20),
        cost_estimate=cost(0, 10 * 4 * piece * width),
    )(tokens, cot, qkv_weight, fc_weight, small, down, proj)


def attend_plane_kernel(
    tokens, cot, token_all, weight, cot_one, down, down_in, key_bias, proj, vectors,
    middle, normed, attended, lse, cot_three, down_full, normed_one, q, k, v, k_t, v_t, one_low, two_low,
    score_ref, joint, terms, passed, joined, arrived, send, receive,
    level_send, level_receive, mate_send, mate_receive,
):
    piece, width = tokens.shape
    half = piece // 2
    length, columns = q.shape
    heads = columns // HEAD_DIM
    rank = lax.axis_index("seq")
    one, two = neighbours()
    gather = LevelGather(down, down_full, level_send, level_receive, mate_send, mate_receive)
    for device in (one, two):
        greet("seq", device)
    pl.semaphore_wait(pltpu.get_barrier_semaphore(), 2 + gather.greet())
    up, lower = pl.ds(0, half), pl.ds(half, half)
    gather.start(gather.second())

    def copy(index, source, target, device):
        return remote(source, target, send.at[index], receive.at[index], "seq", device)

    cot_copies = (copy(0, cot_one, cot_three.at[up], two), copy(1, two_low, cot_three.at[lower], one))
    low_copies = (copy(8, cot.at[lower], one_low, one), copy(9, cot.at[lower], two_low, two))
    across = (copy(2, terms.at[3, up], passed.at[0], one), copy(3, terms.at[3, lower], passed.at[1], two))
    plain_one = copy(4, terms.at[1, up], arrived.at[0, up], one)
    plain_two = copy(5, terms.at[2, lower], arrived.at[1, lower], two)
    joined_one = copy(6, joined.at[0], arrived.at[0, lower], one)
    joined_two = copy(7, joined.at[1], arrived.at[1, up], two)
    for item in low_copies:
        item.start()
    cot_copies[0].start()
    tile = min(256, piece)
    rows = lambda n: pl.BlockSpec((tile, n), lambda i: (i, 0))
    turned = pl.BlockSpec((columns, tile), lambda i: (0, i))
    pltpu.emit_pipeline(
        lambda x, wq, wk, wv, *out: project_kernel(x, vectors, wq, wk, wv, *out),
        grid=(length // tile,),
        in_specs=[rows(width)] + [pl.BlockSpec((width, columns), lambda i, part=part: (0, part)) for part in range(3)],
        out_specs=[rows(width), rows(columns), rows(columns), rows(columns), turned, turned],
    )(token_all, weight, weight, weight, normed_one, q, k, v, k_t, v_t)
    for item in low_copies:
        item.wait_recv()
    cot_copies[1].start()

    def body(query_ref, key_ref, value_t, attended_tile, lse_tile):
        group, head = pl.program_id(0), pl.program_id(1)
        at = 3 - group
        true = flip(at, rank)
        query = query_ref[...]

        def first(block, top):
            scores = scores_of(key_ref, key_bias, query, flip(block, rank), piece, False)
            score_ref[rows_of(block, piece), :] = scores
            return jnp.maximum(top, jnp.max(scores, axis=0, keepdims=True))

        last = scores_of(key_ref, key_bias, query, at, piece, True)
        top = lax.fori_loop(0, true, first, jnp.max(last, axis=0, keepdims=True))

        def weigh(scores, rel):
            weights = jnp.exp2(scores - top)
            return jnp.sum(weights, axis=0, keepdims=True), nn(value_t[:, rows_of(rel, piece)], weights.astype(BF16))

        def second(block, carry):
            total, out = carry
            more, part = weigh(score_ref[rows_of(block, piece), :], flip(block, rank))
            return total + more, out + part

        total, out = lax.fori_loop(0, true, second, weigh(last, at))
        result = (out / total).T.astype(BF16)
        attended_tile[...] = result
        lse_tile[0] = top + jnp.log2(total)
        joint[:, pl.ds(pl.multiple_of(head * HEAD_DIM, HEAD_DIM), HEAD_DIM)] = result

        @pl.when(head == heads - 1)
        def _():
            terms[at] = nn(joint[...], proj[...]).astype(BF16)

        @pl.when((head == heads - 1) & (group == 0))
        def _():
            for item in across:
                item.start()

        @pl.when((head == heads - 1) & (group == 1))
        def _():
            plain_two.start()

        @pl.when((head == 0) & (group == 3))
        def _():
            gather.take((2,))
            gather.start(gather.passes())

        @pl.when((head == heads - 1) & (group == 2))
        def _():
            plain_one.start()
            for item in across:
                item.wait_recv()
            joined[0] = (terms[1, half:].astype(F32) + passed[1].astype(F32)).astype(BF16)
            joined[1] = (terms[2, :half].astype(F32) + passed[0].astype(F32)).astype(BF16)
            joined_one.start()
            joined_two.start()

    pltpu.emit_pipeline(
        body,
        grid=(4, heads),
        in_specs=[
            pl.BlockSpec((piece, HEAD_DIM), lambda g, h: (3 - g, h)),
            pl.BlockSpec((length, HEAD_DIM), lambda g, h: (0, h)),
            pl.BlockSpec((HEAD_DIM, length), lambda g, h: (h, 0)),
        ],
        out_specs=[
            pl.BlockSpec((piece, HEAD_DIM), lambda g, h: (3 - g, h)),
            pl.BlockSpec((1, 1, piece), lambda g, h: (h, 0, 3 - g)),
        ],
    )(q, k, v_t, attended, lse)

    for item in (plain_one, plain_two, joined_one, joined_two):
        item.wait_recv()
    part = min(128, piece)

    def norm_body(token_tile, middle_tile, normed_tile):
        here = pl.ds(pl.multiple_of(pl.program_id(0) * part, part), part)
        total = terms[0, here, :].astype(F32) + arrived[0, here, :].astype(F32) + arrived[1, here, :].astype(F32)
        values = token_tile[...].astype(F32) + (total + vectors[2:3, :])
        middle_tile[...] = values
        normed_tile[...] = (norm_parts(values)[0] * vectors[3:4, :] + vectors[4:5, :]).astype(BF16)

    line = pl.BlockSpec((part, width), lambda i: (i, 0))
    pltpu.emit_pipeline(norm_body, grid=(piece // part,), in_specs=[line], out_specs=[line] * 2)(tokens, middle, normed)
    gather.take((3,))
    gather.finish((2, 3), gather.second() + gather.passes())
    for item in cot_copies:
        item.wait()
    for item in low_copies:
        item.wait_send()
    for item in (*across, plain_one, plain_two, joined_one, joined_two):
        item.wait_send()


def attend_plane(tokens, cot, token_all, weight, cot_one, down, down_in, key_bias, proj, vectors):
    piece, width = tokens.shape
    length, columns = token_all.shape[0], proj.shape[0]
    heads, half = columns // HEAD_DIM, piece // 2
    anywhere = pl.BlockSpec(memory_space=pltpu.HBM)
    inside = pl.BlockSpec(memory_space=pltpu.VMEM)
    shape = lambda *dims: jax.ShapeDtypeStruct(dims, BF16)
    dma = pltpu.SemaphoreType.DMA
    return pl.pallas_call(
        attend_plane_kernel,
        in_specs=[anywhere] * 7 + [inside] * 3,
        out_specs=[anywhere] * 14,
        input_output_aliases={6: 5},
        out_shape=[
            jax.ShapeDtypeStruct((piece, width), F32), shape(piece, width), shape(length, columns),
            jax.ShapeDtypeStruct((heads, 1, length), F32), shape(piece, width), shape(*down_in.shape),
            shape(length, width), *[shape(length, columns)] * 3, *[shape(columns, length)] * 2,
            *[shape(half, width)] * 2,
        ],
        scratch_shapes=[
            pltpu.VMEM((length, piece), F32),
            pltpu.VMEM((piece, columns), BF16),
            pltpu.VMEM((4, piece, width), BF16),
            pltpu.VMEM((2, half, width), BF16),
            pltpu.VMEM((2, half, width), BF16),
            pltpu.VMEM((2, piece, width), BF16),
            dma((10,)), dma((10,)), dma((5,)), dma((4,)), dma((5,)), dma((5,)),
        ],
        compiler_params=pltpu.CompilerParams(collective_id=2, has_side_effects=True, vmem_limit_bytes=62 * 2**20),
        cost_estimate=cost(3 * length * length * columns + 2 * length * columns * width, 10 * length * width, heads * length * length // 2),
    )(tokens, cot, token_all, weight, cot_one, down, down_in, key_bias, proj, vectors)


def sum_rows(ref, at, columns, value, first):
    total = jnp.sum(value, axis=0, keepdims=True)

    @pl.when(first)
    def _():
        ref[at : at + 1, columns] = total

    @pl.when(jnp.logical_not(first))
    def _():
        ref[at : at + 1, columns] += total


def plane_kernel(
    normed, cot_own, one_up, one_low, two_up, two_low, cot_three, fc, down, middle, vectors,
    grad_middle, low_all, sums, hidden_sums, active, hidden_grad, normed_all, cot_all, terms, grad_down, grad_fc,
    mate_in, summed, got, down_share, fc_mate, fc_summed,
    normed_buf, cot_buf, sum_ref, joined, passed, arrived, load, local, send, receive, level_send, level_receive, fc_send, fc_receive,
):
    piece, width = normed.shape
    half = piece // 2
    inner = fc.shape[1]
    length = normed_all.shape[0]
    tile = min(512, inner)
    last = inner // tile - 1
    one, two = neighbours()
    scatter = LevelScatter(grad_down, mate_in, summed, got, level_send, level_receive)
    fc_scatter = LevelScatter(grad_fc, fc_mate, fc_summed, None, fc_send, fc_receive)
    for device in (one, two):
        greet("seq", device)
    pl.semaphore_wait(pltpu.get_barrier_semaphore(), 2 + scatter.greet())

    rows = lambda k, start=0, size=piece: pl.ds(k * piece + start, size)
    first, second = pl.ds(0, half), pl.ds(half, half)

    def copy(index, source, target, device):
        return remote(source, target, send.at[index], receive.at[index], "seq", device)

    normed_first = (copy(0, normed.at[first], normed_buf.at[2], one), copy(1, normed.at[second], normed_buf.at[5], two))
    normed_across = (copy(2, normed_buf.at[2], normed_buf.at[6], two), copy(3, normed_buf.at[5], normed_buf.at[7], one))
    normed_last = (copy(4, normed.at[second], normed_buf.at[3], one), copy(5, normed.at[first], normed_buf.at[4], two))
    across = (copy(6, cot_buf.at[6], passed.at[0], one), copy(7, cot_buf.at[7], passed.at[1], two))
    plain = (copy(8, cot_buf.at[2], arrived.at[0, 0], one), copy(9, cot_buf.at[5], arrived.at[1, 1], two))
    both = (copy(10, joined.at[0], arrived.at[0, 1], one), copy(11, joined.at[1], arrived.at[1, 0], two))
    low_near = (
        copy(12, low_all.at[rows(0)], low_all.at[rows(1)], one),
        copy(13, low_all.at[rows(0)], low_all.at[rows(2)], two),
    )
    low_three = (
        copy(14, low_all.at[rows(1, 0, half)], low_all.at[rows(3, 0, half)], two),
        copy(15, low_all.at[rows(2, half, half)], low_all.at[rows(3, half, half)], one),
    )

    sources = (
        cot_own.at[first], cot_own.at[second], one_up, one_low, two_up, two_low, cot_three.at[first], cot_three.at[second]
    )
    loads = [pltpu.make_async_copy(source, cot_buf.at[i], load.at[i]) for i, source in enumerate(sources)]
    own = [
        pltpu.make_async_copy(normed.at[part], normed_buf.at[i], load.at[8 + i]) for i, part in enumerate((first, second))
    ]
    keep_to = lambda target, i: target.at[pl.ds(i * half, half)]
    keeps = [pltpu.make_async_copy(normed_buf.at[i], keep_to(normed_all, i), local.at[i]) for i in range(8)]
    keeps_cot = [pltpu.make_async_copy(cot_buf.at[i], keep_to(cot_all, i), local.at[8 + i]) for i in range(8)]

    def start(*items):
        for item in items:
            item.start()

    def received(*items):
        for item in items:
            item.wait_recv()

    start(*normed_first, *own, *loads)

    place_of = lambda step: step + 2 * lax.div(step, 3) - 7 * lax.div(step, 6)

    def feed_body(fc_tile, down_tile, active_tile, hidden_tile):
        step, j = pl.program_id(0), pl.program_id(1)
        at = place_of(step)

        @pl.when((step == 0) & (j == 0))
        def _():
            for item in own:
                item.wait()
            start(*keeps[:2])
            for item in loads:
                item.wait()
            start(*keeps_cot)

        @pl.when((step == 2) & (j == 0))
        def _():
            received(*normed_first)
            start(*normed_across, keeps[2], keeps[5])

        @pl.when((step == 4) & (j == 0))
        def _():
            received(*normed_across)
            start(*normed_last, *keeps[6:])

        @pl.when((step == 6) & (j == 0))
        def _():
            received(*normed_last)
            start(*keeps[3:5])

        @pl.when((step == 7) & (j == 0))
        def _():
            start(*plain)

        weights = fc_tile[...]
        columns = pl.ds(pl.multiple_of(j * tile, tile), tile)
        hidden = nn(normed_buf[at], weights) + vectors[6:7, columns]
        grad_active = nt(cot_buf[at], down_tile[...])
        square = hidden * hidden
        bent = jnp.tanh(math.sqrt(2 / math.pi) * (hidden + 0.044715 * (square * hidden)))
        share = 0.5 * (1.0 + bent)
        active_tile[...] = (hidden * share).astype(BF16)
        slope = share + (0.5 * hidden) * (1.0 - bent * bent) * (
            math.sqrt(2 / math.pi) * (1.0 + (3 * 0.044715) * square)
        )
        grad_hidden = (grad_active * slope).astype(BF16)
        hidden_tile[...] = grad_hidden
        sum_rows(hidden_sums, 0, columns, grad_hidden.astype(F32), step == 0)
        term = nt(grad_hidden, weights)

        @pl.when(j == 0)
        def _():
            sum_ref[...] = term

        @pl.when(j > 0)
        def _():
            sum_ref[...] += term

        @pl.when((j == last) & (step == 0))
        def _():
            for item in keeps_cot:
                item.wait()

        @pl.when(j == last)
        def _():
            cot_buf[at] = sum_ref[...].astype(BF16)

        @pl.when((j == last) & (step == 5))
        def _():
            start(*across)

    pltpu.emit_pipeline(
        feed_body,
        grid=(8, inner // tile),
        in_specs=[
            pl.BlockSpec((width, tile), lambda s, j: (0, j)),
            pl.BlockSpec((tile, width), lambda s, j: (j, 0)),
        ],
        out_specs=[pl.BlockSpec((half, tile), lambda s, j: (place_of(s), j))] * 2,
    )(fc, down, active, hidden_grad)

    received(*across)
    joined[0] = (cot_buf[3].astype(F32) + passed[1].astype(F32)).astype(BF16)
    joined[1] = (cot_buf[4].astype(F32) + passed[0].astype(F32)).astype(BF16)
    start(*both)
    for item in keeps:
        item.wait()

    narrow = min(512, width)

    def down_body(active_rows, down_columns, out):
        out[...] = nn(active_rows[...], down_columns[...]).astype(BF16)

    def multiply_down(start):
        pltpu.emit_pipeline(
            down_body,
            grid=(2, width // narrow),
            in_specs=[
                pl.BlockSpec((piece, inner), lambda k, j: (start + k, 0)),
                pl.BlockSpec((inner, narrow), lambda k, j: (0, j)),
            ],
            out_specs=[pl.BlockSpec((piece, narrow), lambda k, j: (start + k, j))],
        )(active, down, terms)

    wide, tall = min(1024, width), min(1024, inner)

    def outer_body(left, right, out):
        out[...] = tn(left[...], right[...]).astype(BF16)

    def outer(left, right, out, shape):
        pltpu.emit_pipeline(
            outer_body,
            grid=(out.shape[0] // shape[0], out.shape[1] // shape[1]),
            in_specs=[
                pl.BlockSpec((length, shape[0]), lambda i, j: (0, i)),
                pl.BlockSpec((length, shape[1]), lambda i, j: (0, j)),
            ],
            out_specs=[pl.BlockSpec(shape, lambda i, j: (i, j))],
        )(left, right, out)

    outer(active, cot_all, grad_down, (tall, wide))
    scatter.start()
    multiply_down(0)
    scatter.spread()
    received(*plain, *both)
    part = min(128, half)
    steps = half // part

    def norm_body(middle_tile, cot_tile, grad_tile, low_tile):
        i = pl.program_id(0)
        at = lax.div(i, steps)
        here = pl.ds(pl.multiple_of(lax.rem(i, steps) * part, part), part)
        upstream = (
            cot_buf[at, here, :].astype(F32) + arrived[0, at, here, :].astype(F32) + arrived[1, at, here, :].astype(F32)
        )
        unit, scale = norm_parts(middle_tile[...])
        cot = cot_tile[...].astype(F32)
        grad = cot + norm_backward(unit, scale, vectors[3:4, :], upstream)
        rounded = grad.astype(BF16)
        grad_tile[...] = grad
        low_tile[...] = rounded
        for at, item in enumerate((upstream * unit, upstream, rounded.astype(F32), cot)):
            sum_rows(sums, at, slice(None), item, i == 0)

    line = pl.BlockSpec((part, width), lambda i: (i, 0))
    pltpu.emit_pipeline(norm_body, grid=(piece // part,), in_specs=[line] * 2, out_specs=[line] * 2)(
        middle, cot_own, grad_middle, low_all
    )
    start(*low_near)
    multiply_down(2)
    scatter.pass_on()
    outer(normed_all, hidden_grad, grad_fc, (wide, tall))
    fc_scatter.start()
    received(*low_near)
    start(*low_three)
    fc_scatter.combine()
    scatter.finish(down_share)
    scatter.close()
    for item in fc_scatter.swaps():
        item.wait_send()
    received(*low_three)
    for item in (*normed_first, *normed_across, *normed_last, *across, *plain, *both, *low_near, *low_three):
        item.wait_send()


def feed_plane(normed, cots, fc, down, middle, vectors):
    piece, width = normed.shape
    inner = fc.shape[1]
    length, half = 4 * piece, piece // 2
    anywhere = pl.BlockSpec(memory_space=pltpu.HBM)
    inside = pl.BlockSpec(memory_space=pltpu.VMEM)
    shape = lambda rows, columns, kind=BF16: jax.ShapeDtypeStruct((rows, columns), kind)
    dma = pltpu.SemaphoreType.DMA
    return pl.pallas_call(
        plane_kernel,
        in_specs=[anywhere] * 10 + [inside],
        out_specs=[anywhere, anywhere, inside, inside] + [anywhere] * 13,
        out_shape=[
            shape(piece, width, F32), shape(length, width), shape(4, width, F32), shape(1, inner, F32),
            shape(length, inner), shape(length, inner), shape(length, width), shape(length, width),
            shape(length, width), shape(inner, width), shape(width, inner),
            shape(inner // 2, width), shape(inner // 2, width), shape(inner // 2, width), shape(inner // 8, width, F32),
            shape(width // 2, inner), shape(width // 2, inner),
        ],
        scratch_shapes=[
            pltpu.VMEM((8, half, width), BF16),
            pltpu.VMEM((8, half, width), BF16),
            pltpu.VMEM((half, width), F32),
            pltpu.VMEM((2, half, width), BF16),
            pltpu.VMEM((2, half, width), BF16),
            pltpu.VMEM((2, 2, half, width), BF16),
            dma((10,)), dma((16,)), dma((16,)), dma((16,)), dma((8,)), dma((8,)), dma((4,)), dma((4,)),
        ],
        compiler_params=pltpu.CompilerParams(collective_id=1, has_side_effects=True, vmem_limit_bytes=60 * 2**20),
        cost_estimate=cost(12 * length * width * inner, 10 * length * width),
    )(normed, *cots, fc, down, middle, vectors)


def retreat_plane_kernel(
    low_all, q, k, v, k_t, lse, terms, middle, fc_summed, attended, key_bias, proj, vectors,
    grads, column_sums, block_out, grad_proj, fc_share,
    prob_ref, chance_ref, grad_ref, key_sum, value_sum, rounded, own, passed, joined, arrived,
    level_got, level_through, level_own, load, local, send, receive, level_send, level_receive, level_load,
):
    piece, width = middle.shape
    half = piece // 2
    length, columns = q.shape
    heads = columns // HEAD_DIM
    rank = lax.axis_index("seq")
    one, two = neighbours()
    scatter = LateScatter(fc_summed, level_got, level_through, level_own, level_send, level_receive, level_load)
    for device in (one, two):
        greet("seq", device)
    pl.semaphore_wait(pltpu.get_barrier_semaphore(), 2 + scatter.greet())
    up, lower = pl.ds(0, half), pl.ds(half, half)
    rows = lambda at, start=0, size=piece: pl.ds(at * piece + start, size)

    def copy(index, source, target, device):
        return remote(source, target, send.at[index], receive.at[index], "seq", device)

    across = (
        copy(0, terms.at[rows(3, 0, half)], passed.at[0], one),
        copy(1, terms.at[rows(3, half, half)], passed.at[1], two),
    )
    plain_one = copy(2, terms.at[rows(1, 0, half)], arrived.at[0, up], one)
    plain_two = copy(3, terms.at[rows(2, half, half)], arrived.at[1, lower], two)
    joined_one = copy(4, joined.at[0], arrived.at[0, lower], one)
    joined_two = copy(5, joined.at[1], arrived.at[1, up], two)
    loads = (
        pltpu.make_async_copy(terms.at[rows(1, half, half)], own.at[0], load.at[0]),
        pltpu.make_async_copy(terms.at[rows(2, 0, half)], own.at[1], load.at[1]),
    )
    for item in (*across, plain_one, plain_two, *loads):
        item.start()
    scatter.start()
    key_sum[...] = jnp.zeros_like(key_sum)
    value_sum[...] = jnp.zeros_like(value_sum)

    def body(low_ref, query_ref, key_ref, value_ref, key_t, lse_ref, query_out):
        at, head = pl.program_id(0), pl.program_id(1)
        true = flip(at, rank)
        here = pl.ds(pl.multiple_of(head * HEAD_DIM, HEAD_DIM), HEAD_DIM)

        @pl.when(head == 0)
        def _():
            grad_ref[...] = nt(low_ref[...], proj[...]).astype(BF16)

        @pl.when((at == 1) & (head == 2))
        def _():
            for item in (*across,):
                item.wait_recv()
            for item in loads:
                item.wait()
            joined[0] = (own[0].astype(F32) + passed[1].astype(F32)).astype(BF16)
            joined[1] = (own[1].astype(F32) + passed[0].astype(F32)).astype(BF16)
            joined_one.start()
            joined_two.start()

        @pl.when((at == 1) & (head == 3))
        def _():
            scatter.pass_on()

        query, grad, base = query_ref[...], grad_ref[:, here], lse_ref[0]

        def measure(scores, rel):
            block = rows_of(rel, piece)
            probs = jnp.exp2(scores - base)
            grad_chances = nt(value_ref[block, :], grad)
            value_sum[block, here] += nn(probs.astype(BF16), grad)
            prob_ref[block, :] = probs
            chance_ref[block, :] = grad_chances
            return jnp.sum(probs * grad_chances, axis=0, keepdims=True)

        def first(block, weighted):
            rel = flip(block, rank)
            return weighted + measure(scores_of(key_ref, key_bias, query, rel, piece, False), rel)

        last = scores_of(key_ref, key_bias, query, at, piece, True)
        weighted = lax.fori_loop(0, true, first, measure(last, at))

        def second(block, total):
            block = rows_of(flip(block, rank), piece)
            grad_scores = (prob_ref[block, :] * (chance_ref[block, :] - weighted)).astype(BF16)
            key_sum[block, here] += nn(grad_scores, query)
            return total + nn(key_t[:, block], grad_scores)

        total = lax.fori_loop(0, true + 1, second, jnp.zeros((HEAD_DIM, piece), F32))
        result = (total * FACTOR).T.astype(BF16)
        query_out[...] = result
        sum_rows(column_sums, 0, here, result.astype(F32), at == 0)

    pltpu.emit_pipeline(
        body,
        grid=(4, heads),
        in_specs=[
            pl.BlockSpec((piece, width), lambda g, h: (g, 0)),
            pl.BlockSpec((piece, HEAD_DIM), lambda g, h: (g, h)),
            pl.BlockSpec((length, HEAD_DIM), lambda g, h: (0, h)),
            pl.BlockSpec((length, HEAD_DIM), lambda g, h: (0, h)),
            pl.BlockSpec((HEAD_DIM, length), lambda g, h: (h, 0)),
            pl.BlockSpec((1, 1, piece), lambda g, h: (h, 0, g)),
        ],
        out_specs=[pl.BlockSpec((piece, HEAD_DIM), lambda g, h: (g, h))],
    )(low_all, q, k, v, k_t, lse, grads)

    rounded[:, :columns] = (key_sum[...] * FACTOR).astype(BF16)
    values = value_sum[...].astype(BF16)
    rounded[:, columns:] = values
    column_sums[1:2, :] = jnp.sum(values.astype(F32), axis=0, keepdims=True)
    keep = pltpu.make_async_copy(rounded, grads.at[:, pl.ds(columns, 2 * columns)], local.at[0])
    keep.start()
    tile = min(512, width)

    def outer_body(left, right, out):
        out[...] = tn(left[...], right[...]).astype(BF16)

    pltpu.emit_pipeline(
        outer_body,
        grid=(width // tile,),
        in_specs=[
            pl.BlockSpec((length, columns), lambda i: (0, 0)),
            pl.BlockSpec((length, tile), lambda i: (0, i)),
        ],
        out_specs=[pl.BlockSpec((columns, tile), lambda i: (0, i))],
    )(attended, low_all, grad_proj)
    for item in (plain_one, plain_two, joined_one, joined_two):
        item.wait_recv()
    part = min(128, piece)

    def out_body(middle_tile, term_tile, out):
        here = pl.ds(pl.multiple_of(pl.program_id(0) * part, part), part)
        total = term_tile[...].astype(F32) + arrived[0, here, :].astype(F32) + arrived[1, here, :].astype(F32)
        out[...] = (middle_tile[...] + (total + vectors[5:6, :])).astype(BF16)

    line = pl.BlockSpec((part, width), lambda i: (i, 0))
    pltpu.emit_pipeline(out_body, grid=(piece // part,), in_specs=[line] * 2, out_specs=[line])(middle, terms, block_out)
    scatter.finish(fc_share)
    scatter.close()
    keep.wait()
    for item in (*across, plain_one, plain_two, joined_one, joined_two):
        item.wait_send()


def retreat_plane(low_all, q, k, v, k_t, lse, terms, middle, fc_summed, attended, key_bias, proj, vectors):
    piece, width = middle.shape
    length, columns = q.shape
    half, inner = piece // 2, fc_summed.shape[1]
    anywhere = pl.BlockSpec(memory_space=pltpu.HBM)
    inside = pl.BlockSpec(memory_space=pltpu.VMEM)
    dma = pltpu.SemaphoreType.DMA
    return pl.pallas_call(
        retreat_plane_kernel,
        in_specs=[anywhere] * 10 + [inside] * 3,
        out_specs=[anywhere, inside, anywhere, anywhere, inside],
        out_shape=[
            jax.ShapeDtypeStruct((length, 3 * columns), BF16),
            jax.ShapeDtypeStruct((2, columns), F32),
            jax.ShapeDtypeStruct((piece, width), BF16),
            jax.ShapeDtypeStruct((columns, width), BF16),
            jax.ShapeDtypeStruct((width // 8, inner), BF16),
        ],
        scratch_shapes=[
            pltpu.VMEM((length, piece), F32),
            pltpu.VMEM((length, piece), F32),
            pltpu.VMEM((piece, columns), BF16),
            pltpu.VMEM((length, columns), F32),
            pltpu.VMEM((length, columns), F32),
            pltpu.VMEM((length, 2 * columns), BF16),
            pltpu.VMEM((2, half, width), BF16),
            pltpu.VMEM((2, half, width), BF16),
            pltpu.VMEM((2, half, width), BF16),
            pltpu.VMEM((2, piece, width), BF16),
            pltpu.VMEM((width // 2, inner), BF16),
            pltpu.VMEM((width // 8, inner), BF16),
            pltpu.VMEM((width // 8, inner), BF16),
            dma((2,)), dma((1,)), dma((6,)), dma((6,)), dma((8,)), dma((8,)), dma((2,)),
        ],
        compiler_params=pltpu.CompilerParams(collective_id=3, has_side_effects=True, vmem_limit_bytes=62 * 2**20),
        cost_estimate=cost(8 * length * length * columns + 2 * length * columns * width, 10 * length * width),
    )(low_all, q, k, v, k_t, lse, terms, middle, fc_summed, attended, key_bias, proj, vectors)


def closing_kernel(
    grads, weight, normed_one, tokens, grad_middle, vectors, sums_two, hidden_sums, qv_sums, fc_share,
    tokens_grad, qkv_out, fc_out, small_out,
    terms, passed, joined, arrived, qkv_in, fc_in, mine, small_in, small_rows, small_got,
    grad_qkv, mate_in, summed, got, qkv_share,
    send, receive, level_send, level_receive, small_send, small_receive, load,
):
    pieces = [[ref.at[i] for ref in (grad_qkv, mate_in, summed, got, qkv_share)] for i in range(2)]
    piece, width = tokens.shape
    half = piece // 2
    columns = grads.shape[1]
    heads = columns // (3 * HEAD_DIM)
    me, place = lax.axis_index("seq"), lax.axis_index("dp")
    one, two = neighbours()
    three = 3 - me
    plane = (one, two, three)
    others = [lax.rem(place + i, 8) for i in range(1, 8)]
    for device in plane:
        greet("seq", device)
    for device in others:
        greet("dp", device)
    pl.semaphore_wait(pltpu.get_barrier_semaphore(), 10)
    scatters = [
        NearScatter(*refs[:4], level_send.at[i], level_receive.at[i]) for i, refs in enumerate(pieces)
    ]
    shares = [refs[4] for refs in pieces]
    up, lower = pl.ds(0, half), pl.ds(half, half)

    def copy(index, source, target, device):
        return remote(source, target, send.at[index], receive.at[index], "seq", device)

    across = (copy(0, terms.at[3, up], passed.at[0], one), copy(1, terms.at[3, lower], passed.at[1], two))
    plain_one = copy(2, terms.at[1, up], arrived.at[0, up], one)
    plain_two = copy(3, terms.at[2, lower], arrived.at[1, lower], two)
    joined_one = copy(4, joined.at[0], arrived.at[0, lower], one)
    joined_two = copy(5, joined.at[1], arrived.at[1, up], two)
    fine = qkv_in.shape[2]
    rows_for = lambda ref, device: ref.at[pl.ds(device * fine, fine)]
    fc_copies = [copy(6 + i, rows_for(fc_share, device), fc_in.at[i], device) for i, device in enumerate(plane)]
    qkv_copies = [
        [copy(15 + 3 * part + i, rows_for(share, device), qkv_in.at[part, i], device) for i, device in enumerate(plane)]
        for part, share in enumerate(shares)
    ]
    small_copies = [copy(9 + i, mine, small_in.at[i], device) for i, device in enumerate(plane)]
    fc_own = pltpu.make_async_copy(rows_for(fc_share, me), fc_in.at[3], load.at[0])
    qkv_own = [
        pltpu.make_async_copy(rows_for(share, me), qkv_in.at[part, 3], load.at[1 + part])
        for part, share in enumerate(shares)
    ]
    row_copies = [
        remote(small_rows.at[device], small_got.at[i], small_send.at[i], small_receive.at[i], "dp", device)
        for i, device in enumerate(others)
    ]

    def back_term(at):
        for start in range(0, width, width // 2):
            columns_here = slice(start, start + width // 2)
            term = nt(grads[at * piece : (at + 1) * piece, :], weight[columns_here, :])
            terms[at, :, columns_here] = term.astype(BF16)

    tile = min(512, width)
    narrow = columns // 2

    def outer(part):
        def body(left):
            here = pl.ds(pl.multiple_of(pl.program_id(0) * tile, tile), tile)
            grad_qkv[part, here, :] = tn(left[...], grads[:, part * narrow : (part + 1) * narrow]).astype(BF16)

        pltpu.emit_pipeline(
            body,
            grid=(width // tile,),
            in_specs=[pl.BlockSpec((normed_one.shape[0], tile), lambda i: (0, i))],
        )(normed_one)

    back_term(3)
    for item in across:
        item.start()
    back_term(1)
    plain_one.start()
    outer(0)
    scatters[0].start()
    back_term(2)
    plain_two.start()
    scatters[0].spread()
    outer(1)
    scatters[1].start()
    for item in across:
        item.wait_recv()
    joined[0] = (terms[1, half:].astype(F32) + passed[1].astype(F32)).astype(BF16)
    joined[1] = (terms[2, :half].astype(F32) + passed[0].astype(F32)).astype(BF16)
    joined_one.start()
    joined_two.start()
    scatters[1].spread()
    scatters[0].pass_on()
    fc_own.start()
    back_term(0)
    mine[...] = jnp.zeros_like(mine)
    mine[2:6, :] = sums_two[...]
    for head in range(heads):
        at = (head * 2 + lax.rem(me, 2)) * 2 + lax.div(me, 2)
        here = pl.ds(pl.multiple_of(at * HEAD_DIM, HEAD_DIM), HEAD_DIM)
        for part in range(2):
            mine[6 + part : 7 + part, here] = qv_sums[part : part + 1, head * HEAD_DIM : (head + 1) * HEAD_DIM]
    scatters[1].pass_on()

    scatters[0].finish(shares[0])
    for item in (plain_one, plain_two, joined_one, joined_two):
        item.wait_recv()
    for item in fc_copies:
        item.start()
    part = min(128, piece)

    def norm_body(token_tile, middle_tile, out):
        i = pl.program_id(0)
        here = pl.ds(pl.multiple_of(i * part, part), part)
        upstream = terms[0, here, :].astype(F32) + arrived[0, here, :].astype(F32) + arrived[1, here, :].astype(F32)
        unit, scale = norm_parts(token_tile[...].astype(F32))
        out[...] = middle_tile[...] + norm_backward(unit, scale, vectors[0:1, :], upstream)
        for at, item in enumerate((upstream * unit, upstream)):
            sum_rows(mine, at, slice(None), item, i == 0)

    line = pl.BlockSpec((part, width), lambda i: (i, 0))
    pltpu.emit_pipeline(norm_body, grid=(piece // part,), in_specs=[line] * 2, out_specs=[line])(
        tokens, grad_middle, tokens_grad
    )
    for item in small_copies:
        item.start()
    scatters[1].finish(shares[1])
    for part in range(2):
        for item in qkv_copies[part]:
            item.start()
        qkv_own[part].start()
    for item in small_copies:
        item.wait_recv()
    mine_total = mine[...] + small_in[0] + small_in[1] + small_in[2]
    small_rows[...] = jnp.zeros_like(small_rows)
    share, wide = width // 8, 2 * width // 8
    for d in range(8):
        small_rows[d, 0:6, 0:share] = mine_total[0:6, d * share : (d + 1) * share]
        row, at = 6 + d // 4, (d % 4) * wide
        small_rows[d, 6:7, :] = mine_total[row : row + 1, at : at + wide]
        inner = hidden_sums.shape[1] // 8
        small_rows[d, 7:8, 0:inner] = hidden_sums[:, d * inner : (d + 1) * inner]
    for item in row_copies:
        item.start()
    sources = (*plane, me)
    fc_own.wait()
    for item in fc_copies:
        item.wait_recv()
    block = fc_in.shape[2] // 8
    for i, source in enumerate(sources):
        for d in range(8):
            target = pl.ds(pl.multiple_of((d * 4 + source) * block, block), block)
            fc_out[:, target] = fc_in[i, :, d * block : (d + 1) * block].astype(F32)
    for part in range(2):
        qkv_own[part].wait()
        for item in qkv_copies[part]:
            item.wait_recv()
    for i, source in enumerate(sources):
        for part in range(3):
            for head in range(heads):
                at = part * HEADS + (head * 2 + lax.rem(source, 2)) * 2 + lax.div(source, 2)
                target = pl.ds(pl.multiple_of(at * HEAD_DIM, HEAD_DIM), HEAD_DIM)
                start = (part * heads + head) * HEAD_DIM
                which, start = start // narrow, start % narrow
                qkv_out[:, target] = qkv_in[which, i, :, start : start + HEAD_DIM].astype(F32)
    for item in row_copies:
        item.wait_recv()
    total = small_rows[place]
    for i in range(7):
        total = total + small_got[i]
    small_out[...] = total
    for item in (*across, plain_one, plain_two, joined_one, joined_two, *fc_copies, *small_copies, *row_copies):
        item.wait_send()
    for part in range(2):
        scatters[part].close()
        for item in qkv_copies[part]:
            item.wait_send()


def closing(grads, weight, normed_one, tokens, grad_middle, vectors, sums_two, hidden_sums, qv_sums, fc_share):
    piece, width = tokens.shape
    columns, half = grads.shape[1], piece // 2
    fine = fc_share.shape[0] // 4
    wide = 2 * width // 8
    anywhere = pl.BlockSpec(memory_space=pltpu.HBM)
    inside = pl.BlockSpec(memory_space=pltpu.VMEM)
    shape = lambda rows, columns, kind=BF16: jax.ShapeDtypeStruct((rows, columns), kind)
    dma = pltpu.SemaphoreType.DMA
    return pl.pallas_call(
        closing_kernel,
        in_specs=[inside, inside, anywhere, anywhere, anywhere, inside, inside, inside, inside, anywhere],
        out_specs=[anywhere, inside, inside, inside],
        out_shape=[
            shape(piece, width, F32), shape(fine, 4 * columns, F32), shape(fine, 4 * fc_share.shape[1], F32),
            shape(8, wide, F32),
        ],
        scratch_shapes=[
            pltpu.VMEM((4, piece, width), BF16),
            pltpu.VMEM((2, half, width), BF16),
            pltpu.VMEM((2, half, width), BF16),
            pltpu.VMEM((2, piece, width), BF16),
            pltpu.VMEM((2, 4, fine, columns // 2), BF16),
            pltpu.VMEM((4, fine, fc_share.shape[1]), BF16),
            pltpu.VMEM((8, width), F32),
            pltpu.VMEM((3, 8, width), F32),
            pltpu.VMEM((8, 8, wide), F32),
            pltpu.VMEM((7, 8, wide), F32),
            *[
                pltpu.VMEM((2, count, columns // 2), BF16)
                for count in (width, width // 2, width // 2, width // 2, width // 8)
            ],
            dma((21,)), dma((21,)), dma((2, 8)), dma((2, 8)), dma((7,)), dma((7,)), dma((3,)),
        ],
        compiler_params=pltpu.CompilerParams(collective_id=4, has_side_effects=True, vmem_limit_bytes=60 * 2**20),
        cost_estimate=cost(16 * piece * width * columns, 10 * piece * width),
    )(grads, weight, normed_one, tokens, grad_middle, vectors, sums_two, hidden_sums, qv_sums, fc_share)


def after(value, *others):
    return lax.optimization_barrier((value, *others))[0]


def shift(value, axis, distance):
    count = lax.axis_size(axis)
    return lax.ppermute(value, axis, [(i, i ^ distance) for i in range(count)])


def gather_blocks(value, axis="seq"):
    return [value] + [shift(value, axis, k) for k in range(1, lax.axis_size(axis))]


def scatter_blocks(blocks, axis="seq"):
    return [blocks[0]] + [shift(blocks[k], axis, k) for k in range(1, lax.axis_size(axis))]


def gather_plane(value):
    if lax.axis_size("seq") != 4:
        return gather_blocks(value)
    half = value.shape[0] // 2
    one, two = shift(value, "seq", 1), shift(value, "seq", 2)
    three = jnp.concatenate([shift(one[:half], "seq", 2), shift(two[half:], "seq", 1)], axis=0)
    return [value, one, two, three]


def scatter_plane(blocks):
    if lax.axis_size("seq") != 4:
        return scatter_blocks(blocks)
    half = blocks[0].shape[0] // 2
    up, low = shift(blocks[3][:half], "seq", 1), shift(blocks[3][half:], "seq", 2)
    one = shift(blocks[1][:half], "seq", 1)
    two = shift(blocks[2][half:], "seq", 2)
    one_low = (blocks[1][half:].astype(F32) + low.astype(F32)).astype(BF16)
    two_up = (blocks[2][:half].astype(F32) + up.astype(F32)).astype(BF16)
    return [blocks[0], (one, shift(one_low, "seq", 1)), (shift(two_up, "seq", 2), two)]


def by_rank(blocks, rank):
    bit = 1
    while bit < len(blocks):
        odd = (rank & bit) != 0
        blocks = [jnp.where(odd, blocks[k ^ bit], blocks[k]) for k in range(len(blocks))]
        bit *= 2
    return blocks


def pick(pieces, at):
    return lax.dynamic_index_in_dim(pieces, at, axis=0, keepdims=False)


def exchange(pieces, rank):
    return scatter_blocks([pick(pieces, rank ^ k) for k in range(pieces.shape[0])])


def small_scatter(pieces, dp_rank, seq_rank):
    total = 0.0
    sent = [lax.dynamic_index_in_dim(pieces, seq_rank ^ k, axis=1, keepdims=False) for k in range(pieces.shape[1])]
    for part in scatter_blocks(sent):
        total = total + part
    sent = [pick(total, dp_rank ^ k) for k in range(pieces.shape[0])]
    total = 0.0
    for part in scatter_blocks(sent, "dp"):
        total = total + part
    return total


def swap_pairs(dp_count, seq_count, sub):
    pairs = []
    for d in range(dp_count):
        for s in range(seq_count):
            source = ((d // sub) * sub + s % sub) * seq_count + (s // sub) * sub + d % sub
            pairs.append((source, d * seq_count + s))
    return pairs


def gather_dp(value):
    return lax.all_gather(value, "dp", axis=0, tiled=True)


def scatter_dp(value):
    return lax.psum_scatter(value, "dp", scatter_dimension=0, tiled=True)


def shards(
    tokens,
    cotangent,
    lengths,
    key_mask,
    attn_gain,
    attn_shift,
    qkv_weight,
    qv_bias,
    proj_weight,
    proj_bias,
    mlp_gain,
    mlp_shift,
    fc_weight,
    fc_bias,
    down_weight,
    down_bias,
):
    _, piece, width = tokens.shape
    dp_count, seq_count = lax.axis_size("dp"), lax.axis_size("seq")
    dp_rank, seq_rank = lax.axis_index("dp"), lax.axis_index("seq")
    own_heads = HEADS // seq_count
    own_width = own_heads * HEAD_DIM
    rows = qkv_weight.shape[0]
    sub = HEAD_DIM // proj_weight.shape[0]
    high = seq_count // sub
    block = down_weight.shape[0]
    rank = jnp.reshape(seq_rank, (1,)).astype(jnp.int32)
    swap = swap_pairs(dp_count, seq_count, sub)
    order = list(range(seq_count - 1, -1, -1))
    if seq_count == 4:
        order = [3, 1, 2, 0]

    in_plane = seq_count == 4 and dp_count == 8
    tokens_own, cot_own = tokens[0], cotangent[0]

    positions = seq_rank * piece + jnp.arange(piece, dtype=jnp.int32)
    own_flags = ((key_mask[0] == 1) & (positions < lengths[0])).astype(BF16)
    length = piece * seq_count
    shared = None
    if in_plane:
        six = jnp.stack([attn_gain, attn_shift, proj_bias, mlp_gain, mlp_shift, down_bias])
        odd = (seq_rank & 1) != 0
        six = jnp.concatenate([jnp.where(odd, 0, six), jnp.where(odd, six, 0)], axis=1)
        small, start = 0, 0
        for item in (six, qv_bias, fc_bias, own_flags):
            item = item.reshape(-1, 128)
            small = small + jnp.pad(item, ((start, 16 - start - item.shape[0]), (0, 0)))
            start += item.shape[0]
        token_all, qkv_full, fc_rows, cot_one, cot_two, down_full, proj_full, vectors, key_bias = opening(
            tokens_own, cot_own, qkv_weight, fc_weight, small, down_weight, proj_weight, dp_count
        )
        fc_full = gather_dp(fc_rows)
    else:
        small = (attn_gain, attn_shift, qv_bias, proj_bias, mlp_gain, mlp_shift, fc_bias, down_bias)
        sizes = [item.shape[0] for item in small]
        packed = jnp.concatenate(small + (own_flags,))
        blocks = gather_blocks(packed)
        flags = jnp.concatenate([item[-piece:] for item in blocks])
        key_bias = jnp.where(flags > 0, 0.0, NEG).astype(F32)[:, None]
        packed = jnp.stack(by_rank([item[:-piece] for item in blocks], seq_rank))
        packed = jnp.stack(by_rank(gather_blocks(packed, "dp"), dp_rank)).astype(F32)
        parts, start = [], 0
        for size in sizes:
            parts.append(packed[:, :, start : start + size])
            start += size
        whole = [part.reshape(1, -1) for part in parts]
        gain_one, shift_one, qv_full, proj_shift, gain_two, shift_two, _, down_shift = whole
        fc_shift = lax.dynamic_index_in_dim(parts[6], seq_rank, axis=1, keepdims=False).reshape(1, -1)
        rank_low, rank_high = seq_rank % sub, seq_rank // sub
        qv_own = qv_full.reshape(2, own_heads, sub, high, HEAD_DIM)
        qv_own = lax.dynamic_index_in_dim(qv_own, rank_low, axis=2, keepdims=False)
        qv_own = lax.dynamic_index_in_dim(qv_own, rank_high, axis=2, keepdims=False).reshape(1, -1)
        qv_own = jnp.pad(qv_own, ((0, 0), (0, width - 2 * own_width)))
        vectors = jnp.concatenate([gain_one, shift_one, jnp.zeros((5, width), F32), qv_own], axis=0)
        qkv_pieces = (
            qkv_weight.reshape(rows, 3, own_heads, sub, high, HEAD_DIM)
            .transpose(4, 3, 0, 1, 2, 5)
            .reshape(seq_count, rows, 3 * own_width)
        )
        fc_pieces = (
            fc_weight.reshape(rows, dp_count, seq_count, block)
            .transpose(2, 0, 1, 3)
            .reshape(seq_count, rows, dp_count * block)
        )
        qkv_full = gather_dp(jnp.concatenate(by_rank(exchange(qkv_pieces, seq_rank), seq_rank), axis=0))
        proj_full = gather_dp(lax.ppermute(proj_weight, BOTH, swap))
        down_full = gather_dp(down_weight)
        fc_full = gather_dp(jnp.concatenate(by_rank(exchange(fc_pieces, seq_rank), seq_rank), axis=0))
        token_blocks = gather_blocks(tokens_own)
        cot_blocks = gather_blocks(after(cot_own, token_blocks[-1]))
        for k in range(seq_count):
            shared = project(k, token_blocks[k], 0, piece, vectors, qkv_full, length, shared)
    if in_plane:
        results = attend_plane(
            tokens_own, cot_own, token_all, qkv_full, cot_one, down_weight, down_full, key_bias, proj_full, vectors
        )
        middle, normed_two, attended, lse, cot_three, down_full = results[:6]
        normed_one, q, keys, values, keys_t, values_t, one_low, two_low = results[6:]
    else:
        normed_one, q, keys, values, keys_t, values_t = shared
        proj_terms, shared = [None] * seq_count, None
        for k in order:
            proj_terms[k], shared = attend(k, rank, q, keys, values_t, key_bias, proj_full, piece, shared)
        attended, lse = shared
        middle, normed_two = rowwise(
            middle_kernel, scatter_blocks(proj_terms), [tokens_own], [proj_shift, gain_two, shift_two], [F32, BF16], 0
        )

    if in_plane:
        cots = (cot_own, cot_one, one_low, cot_two, two_low, cot_three)
        results = feed_plane(normed_two, cots, fc_full, down_full, middle, vectors)
        grad_middle, low_all, sums_two, hidden_sums, down_terms, grad_down, fc_summed = [
            results[i] for i in (0, 1, 2, 3, 8, 14, 16)
        ]
        grads, qv_sums, block_out, grad_proj, grad_fc = retreat_plane(
            low_all, q, keys, values, keys_t, lse, down_terms, middle, fc_summed, attended, key_bias, proj_full, vectors
        )
    else:
        normed_blocks = gather_blocks(normed_two)
        grad_terms, shared = [], None
        for k in range(seq_count):
            term, shared = feed(k, normed_blocks[k], cot_blocks[k], fc_full, fc_shift, down_full, seq_count, shared)
            grad_terms.append(term)
        active, grad_hidden, normed_all, cot_all = shared
        grad_middle, grad_mid_low, *sums_two = rowwise(
            middle_back_kernel, scatter_blocks(grad_terms), [middle, cot_own], [gain_two], [F32, BF16], 4
        )
        down_terms = [
            nn(active[k * piece : (k + 1) * piece], down_full).astype(BF16) for k in range(seq_count)
        ]
        low_blocks = gather_blocks(grad_mid_low)
        grad_down = scatter_dp(tn(active, cot_all).astype(BF16))
        grad_fc = scatter_dp(tn(normed_all, grad_hidden).astype(BF16))
        hidden_sums = jnp.sum(grad_hidden.astype(F32), axis=0)
        block_out = rowwise(out_kernel, scatter_blocks(down_terms), [middle], [down_shift], [BF16], 0)[0]
        sums, shared = None, None
        for k in range(seq_count):
            sums, shared = retreat(
                k, rank, low_blocks[k], proj_full, q, lse, keys, values, keys_t, key_bias, sums, shared,
                k == seq_count - 1,
            )
        grad_q, low_all = shared
        grads = jnp.concatenate([grad_q, sums[0], sums[1]], axis=1)
        qv_sums = jnp.stack([jnp.sum(item.astype(F32), axis=0) for item in (grad_q, sums[1])])
        grad_proj = tn(attended, low_all).astype(BF16)
    grad_proj = lax.ppermute(scatter_dp(grad_proj), BOTH, swap).astype(F32)
    share = attn_gain.shape[0]
    if in_plane:
        tokens_grad, grad_qkv_weight, grad_fc, smalls = closing(
            grads, qkv_full, normed_one, tokens_own, grad_middle, vectors, sums_two, hidden_sums, qv_sums, grad_fc
        )[:4]
        own = lambda row, size: lax.dynamic_slice_in_dim(smalls[row], seq_rank * size, size)
        late = jnp.concatenate([own(0, share), own(1, share), own(6, 2 * share)])
        early = jnp.concatenate([own(row, share) for row in range(2, 6)] + [smalls[7, :block]])
    else:
        back_terms = [None] * seq_count
        for k in order:
            back_terms[k] = back(k, grads, qkv_full, piece)
        tokens_grad, *sums_one = rowwise(
            tokens_back_kernel, scatter_blocks(back_terms), [tokens_own, grad_middle], [gain_one], [F32], 2
        )

        blocks = exchange(grad_fc.reshape(seq_count, rows, dp_count * block), seq_rank)
        if block % 128 == 0:
            fc_places = lambda s: [(0, d, d * seq_count + s) for d in range(dp_count)]
            grad_fc = lay_out(rank, [[item] for item in blocks], fc_weight.shape[1], (fc_places, block))
        else:
            blocks = [item.reshape(rows, dp_count, block) for item in by_rank(blocks, seq_rank)]
            grad_fc = jnp.stack(blocks, axis=2).reshape(fc_weight.shape).astype(F32)
        grad_qkv = scatter_dp(tn(normed_one, grads).astype(BF16))
        blocks = [[item] for item in exchange(grad_qkv.reshape(seq_count, rows, 3 * own_width), seq_rank)]
        qkv_places = lambda s: [
            (0, part * own_heads + head, part * HEADS + (head * sub + s % sub) * high + s // sub)
            for part in range(3)
            for head in range(own_heads)
        ]
        grad_qkv_weight = lay_out(rank, blocks, qkv_weight.shape[1], (qkv_places, HEAD_DIM))

        def spread(vector):
            return vector.reshape(dp_count, seq_count, -1)

        here = (jnp.arange(seq_count) == seq_rank).astype(F32)
        hidden_sums = hidden_sums.reshape(dp_count, 1, -1) * here[None, :, None]
        early = jnp.concatenate([spread(item) for item in sums_two] + [hidden_sums], axis=2)
        early = small_scatter(early, dp_rank, seq_rank)
        here = (jnp.arange(sub) == rank_low)[:, None] & (jnp.arange(high) == rank_high)[None, :]
        qv_sums = qv_sums.reshape(2, own_heads, 1, 1, HEAD_DIM) * here.astype(F32)[None, None, :, :, None]
        late = jnp.concatenate([spread(item) for item in sums_one] + [spread(qv_sums)], axis=2)
        late = small_scatter(late, dp_rank, seq_rank)
    return (
        block_out[None],
        tokens_grad[None],
        late[:share],
        late[share : 2 * share],
        grad_qkv_weight,
        late[2 * share :],
        grad_proj,
        early[2 * share : 3 * share],
        early[:share],
        early[share : 2 * share],
        grad_fc,
        early[4 * share :],
        grad_down.astype(F32),
        early[3 * share : 4 * share],
    )


def solution(mesh):
    in_specs = (
        P("dp", "seq", None),
        P("dp", "seq", None),
        P("dp"),
        P("dp", "seq"),
        P(BOTH),
        P(BOTH),
        P(BOTH, None),
        P(BOTH),
        P(BOTH, None),
        P(BOTH),
        P(BOTH),
        P(BOTH),
        P(BOTH, None),
        P(BOTH),
        P(BOTH, None),
        P(BOTH),
    )
    out_specs = (
        P("dp", "seq", None),
        P("dp", "seq", None),
        P(BOTH),
        P(BOTH),
        P(BOTH, None),
        P(BOTH),
        P(BOTH, None),
        P(BOTH),
        P(BOTH),
        P(BOTH),
        P(BOTH, None),
        P(BOTH),
        P(BOTH, None),
        P(BOTH),
    )
    return jax.shard_map(shards, mesh=mesh, in_specs=in_specs, out_specs=out_specs, check_vma=False)
```

```python
import functools
import math

import jax
import jax.numpy as jnp
from jax import lax
from jax.experimental import pallas as pl
from jax.experimental.pallas import tpu as pltpu
from jax.sharding import PartitionSpec as P

HEADS = 16
HEAD_DIM = 128
EPS = 1e-05
NEG = -1e30
FACTOR = HEAD_DIM ** (-0.5)
LOG2E = math.log2(math.e)
F32 = jnp.float32
BF16 = jnp.bfloat16
BOTH = ("dp", "seq")
MESH = pl.DeviceIdType.MESH


def nn(left, right):
    return lax.dot_general(left, right, (((1,), (0,)), ((), ())), preferred_element_type=F32)


def nt(left, right):
    return lax.dot_general(left, right, (((1,), (1,)), ((), ())), preferred_element_type=F32)


def tn(left, right):
    return lax.dot_general(left, right, (((0,), (0,)), ((), ())), preferred_element_type=F32)


def params(limit_mib=56):
    return pltpu.CompilerParams(dimension_semantics=("arbitrary",), vmem_limit_bytes=limit_mib * 2**20)


def cost(flops, moved, exps=0):
    return pl.CostEstimate(flops=int(flops), bytes_accessed=int(moved), transcendentals=int(exps))


def call_on_block(kernel, grid, inputs, fresh, shared, previous, scratch, estimate, rank=None, limit_mib=62):
    arrays = [item for item, _ in inputs]
    specs = [spec for _, spec in inputs]
    aliases = {}
    lead = 0 if rank is None else 1
    if previous is not None:
        for at, item in enumerate(previous):
            aliases[lead + len(arrays)] = len(fresh) + at
            arrays.append(item)
            specs.append(pl.BlockSpec(memory_space=pl.ANY))
    count = len(inputs)
    skipped = 0 if previous is None else len(previous)

    def body(*refs):
        refs = list(refs)
        kernel(*refs[: lead + count], *refs[lead + count + skipped :])

    out_specs = [spec for _, spec in fresh] + [spec for _, spec in shared]
    out_shape = [shape for shape, _ in fresh] + [shape for shape, _ in shared]
    if rank is None:
        results = pl.pallas_call(
            body, grid=grid, in_specs=specs, out_specs=out_specs, out_shape=out_shape, scratch_shapes=scratch,
            input_output_aliases=aliases, compiler_params=params(limit_mib), cost_estimate=estimate,
        )(*arrays)
    else:
        results = pl.pallas_call(
            body,
            grid_spec=pltpu.PrefetchScalarGridSpec(
                num_scalar_prefetch=1, grid=grid, in_specs=specs, out_specs=out_specs, scratch_shapes=scratch
            ),
            out_shape=out_shape, input_output_aliases=aliases, compiler_params=params(limit_mib), cost_estimate=estimate,
        )(rank, *arrays)
    return results[: len(fresh)], results[len(fresh) :]


def norm_parts(values):
    average = jnp.mean(values, axis=-1, keepdims=True)
    centred = values - average
    scale = lax.rsqrt(jnp.mean(centred * centred, axis=-1, keepdims=True) + EPS)
    return centred * scale, scale


def norm_backward(normed, scale, gain, upstream):
    weighted = upstream * gain
    return scale * (
        weighted
        - jnp.mean(weighted, axis=-1, keepdims=True)
        - normed * jnp.mean(weighted * normed, axis=-1, keepdims=True)
    )


def project_kernel(x, vectors, wq, wk, wv, normed, q, k, v, k_t, v_t):
    columns = wq.shape[1]
    rows = (norm_parts(x[...].astype(F32))[0] * vectors[0:1, :] + vectors[1:2, :]).astype(BF16)
    normed[...] = rows
    q[...] = (nn(rows, wq[...]) + vectors[7:8, :columns]).astype(BF16)
    keys = nn(rows, wk[...])
    k[...] = keys.astype(BF16)
    k_t[...] = keys.T.astype(BF16)
    values = nn(rows, wv[...]) + vectors[7:8, columns : 2 * columns]
    v[...] = values.astype(BF16)
    v_t[...] = values.T.astype(BF16)


def project(at, x, first, rows_here, vectors, weight, count, previous):
    width, columns = x.shape[1], weight.shape[1] // 3
    tile = min(256, rows_here)
    steps = rows_here // tile
    whole = lambda shape: pl.BlockSpec(shape, lambda i: (0, 0))
    rows = lambda n: pl.BlockSpec((tile, n), lambda i: (at * steps + i, 0))
    turned = pl.BlockSpec((columns, tile), lambda i: (0, at * steps + i))
    inputs = [
        (x, pl.BlockSpec((tile, width), lambda i: (first * steps + i, 0))),
        (vectors, whole(vectors.shape)),
        *[(weight, pl.BlockSpec((width, columns), lambda i, part=part: (0, part))) for part in range(3)],
    ]
    shape = lambda *dims: jax.ShapeDtypeStruct(dims, BF16)
    shared = [(shape(count, width), rows(width))] + [(shape(count, columns), rows(columns))] * 3
    shared += [(shape(columns, count), turned)] * 2
    return call_on_block(
        project_kernel, (steps,), inputs, [], shared, previous, [],
        cost(6 * rows_here * width * columns, 4 * rows_here * width + 6 * width * columns + 10 * rows_here * columns),
    )[1]


def rows_of(block, piece):
    return pl.ds(pl.multiple_of(block * piece, piece), piece)


def scores_of(key_ref, bias_ref, query, rel, piece, diagonal):
    rows = rows_of(rel, piece)
    scores = nt(key_ref[rows, :], query) * (FACTOR * LOG2E)
    key_bias = bias_ref[rows, :]
    if not diagonal:
        return scores + key_bias
    key_at = lax.broadcasted_iota(jnp.int32, scores.shape, 0)
    query_at = lax.broadcasted_iota(jnp.int32, scores.shape, 1)
    allowed = ((key_at < query_at) & (key_bias > -1.0)) | (key_at == query_at)
    return jnp.where(allowed, scores, NEG)


def attend_kernel(at, rank_ref, query_ref, key_ref, value_t, bias_ref, proj_ref, part_ref, attended, lse_ref, score_ref, sum_ref):
    piece = query_ref.shape[0]
    rank = rank_ref[0]
    head = pl.program_id(0)
    true = lax.bitwise_xor(at, rank)
    query = query_ref[...]

    def first(block, top):
        scores = scores_of(key_ref, bias_ref, query, lax.bitwise_xor(block, rank), piece, False)
        score_ref[rows_of(block, piece), :] = scores
        return jnp.maximum(top, jnp.max(scores, axis=0, keepdims=True))

    last = scores_of(key_ref, bias_ref, query, at, piece, True)
    top = lax.fori_loop(0, true, first, jnp.max(last, axis=0, keepdims=True))

    def weigh(scores, rel):
        weights = jnp.exp2(scores - top)
        return jnp.sum(weights, axis=0, keepdims=True), nn(value_t[:, rows_of(rel, piece)], weights.astype(BF16))

    def second(block, carry):
        total, out = carry
        more, part = weigh(score_ref[rows_of(block, piece), :], lax.bitwise_xor(block, rank))
        return total + more, out + part

    total, out = lax.fori_loop(0, true, second, weigh(last, at))
    result = (out / total).T.astype(BF16)
    attended[...] = result
    lse_ref[0] = top + jnp.log2(total)
    term = nn(result, proj_ref[...])

    @pl.when(head == 0)
    def _():
        sum_ref[...] = term

    @pl.when(head > 0)
    def _():
        sum_ref[...] += term

    @pl.when(head == pl.num_programs(0) - 1)
    def _():
        part_ref[...] = sum_ref[...].astype(BF16)


def attend(at, rank, q, k, v_t, key_bias, proj, piece, previous):
    length, columns = q.shape
    heads, width = columns // HEAD_DIM, proj.shape[1]
    inputs = [
        (q, pl.BlockSpec((piece, HEAD_DIM), lambda h, r: (at, h))),
        (k, pl.BlockSpec((length, HEAD_DIM), lambda h, r: (0, h))),
        (v_t, pl.BlockSpec((HEAD_DIM, length), lambda h, r: (h, 0))),
        (key_bias, pl.BlockSpec((length, 1), lambda h, r: (0, 0))),
        (proj, pl.BlockSpec((HEAD_DIM, width), lambda h, r: (h, 0))),
    ]
    fresh = [(jax.ShapeDtypeStruct((piece, width), BF16), pl.BlockSpec((piece, width), lambda h, r: (0, 0)))]
    shared = [
        (jax.ShapeDtypeStruct((length, columns), BF16), pl.BlockSpec((piece, HEAD_DIM), lambda h, r: (at, h))),
        (jax.ShapeDtypeStruct((heads, 1, length), F32), pl.BlockSpec((1, 1, piece), lambda h, r: (h, 0, at))),
    ]
    scratch = [pltpu.VMEM((length, piece), F32), pltpu.VMEM((piece, width), F32)]
    (part,), shared = call_on_block(
        functools.partial(attend_kernel, at), (heads,), inputs, fresh, shared, previous, scratch,
        cost(
            2 * length * piece * columns * 1.3 + 2 * piece * columns * width, 6 * length * columns + 2 * width * columns,
            heads * length * piece * 0.6,
        ), rank,
    )
    return part, shared


def feed_kernel(normed, cot, fc, bias, down, part, active_out, hidden_out, normed_out, cot_out, sum_ref):
    step = pl.program_id(0)
    weights = fc[...]
    hidden = nn(normed[...], weights) + bias[...]
    grad_active = nt(cot[...], down[...])
    inner = math.sqrt(2 / math.pi) * (hidden + 0.044715 * (hidden * hidden * hidden))
    bent = jnp.tanh(inner)
    half = 0.5 * (1.0 + bent)
    active_out[...] = (hidden * half).astype(BF16)
    slope = half + (0.5 * hidden) * (1.0 - bent * bent) * (
        math.sqrt(2 / math.pi) * (1.0 + (3 * 0.044715) * (hidden * hidden))
    )
    grad_hidden = (grad_active * slope).astype(BF16)
    hidden_out[...] = grad_hidden
    term = nt(grad_hidden, weights)

    @pl.when(step == 0)
    def _():
        sum_ref[...] = term
        normed_out[...] = normed[...]
        cot_out[...] = cot[...]

    @pl.when(step > 0)
    def _():
        sum_ref[...] += term

    @pl.when(step == pl.num_programs(0) - 1)
    def _():
        part[...] = sum_ref[...].astype(BF16)


def feed(at, normed, cot, fc, bias, down, count, previous):
    piece, width = normed.shape
    inner = fc.shape[1]
    tile = min(512, inner)
    length = piece * count
    rows = pl.BlockSpec((piece, width), lambda j: (0, 0))
    inputs = [
        (normed, rows),
        (cot, rows),
        (fc, pl.BlockSpec((width, tile), lambda j: (0, j))),
        (bias, pl.BlockSpec((1, tile), lambda j: (0, j))),
        (down, pl.BlockSpec((tile, width), lambda j: (j, 0))),
    ]
    shape = lambda n: jax.ShapeDtypeStruct((length, n), BF16)
    columns = pl.BlockSpec((piece, tile), lambda j: (at, j))
    here = pl.BlockSpec((piece, width), lambda j: (at, 0))
    fresh = [(jax.ShapeDtypeStruct((piece, width), BF16), rows)]
    shared = [(shape(inner), columns), (shape(inner), columns), (shape(width), here), (shape(width), here)]
    (part,), shared = call_on_block(
        feed_kernel, (inner // tile,), inputs, fresh, shared, previous, [pltpu.VMEM((piece, width), F32)],
        cost(6 * piece * width * inner, 4 * width * inner + 10 * piece * width + 4 * piece * inner, piece * inner),
    )
    return part, shared


def retreat_kernel(
    at, first_call, last_call, rank_ref, low_ref, proj_ref, query_ref, lse_ref, key_ref, value_ref, key_t, bias_ref, *rest
):
    rest = list(rest)
    key_in, value_in = (None, None) if first_call else (rest.pop(0), rest.pop(0))
    key_out, value_out, query_out, low_out, prob_ref, chance_ref, key_sum, value_sum = rest
    piece = query_ref.shape[0]
    rank = rank_ref[0]
    true = lax.bitwise_xor(at, rank)

    @pl.when(pl.program_id(0) == 0)
    def _():
        low_out[...] = low_ref[...]

    if first_call:
        key_sum[...] = jnp.zeros_like(key_sum)
        value_sum[...] = jnp.zeros_like(value_sum)
    else:
        key_sum[...] = key_in[...]
        value_sum[...] = value_in[...]
    query, lse = query_ref[...], lse_ref[0]
    grad = nt(low_ref[...], proj_ref[...]).astype(BF16)

    def measure(scores, rel):
        rows = rows_of(rel, piece)
        probs = jnp.exp2(scores - lse)
        grad_chances = nt(value_ref[rows, :], grad)
        value_sum[rows, :] += nn(probs.astype(BF16), grad)
        prob_ref[rows, :] = probs
        chance_ref[rows, :] = grad_chances
        return jnp.sum(probs * grad_chances, axis=0, keepdims=True)

    def first(block, weighted):
        rel = lax.bitwise_xor(block, rank)
        return weighted + measure(scores_of(key_ref, bias_ref, query, rel, piece, False), rel)

    last = scores_of(key_ref, bias_ref, query, at, piece, True)
    weighted = lax.fori_loop(0, true, first, measure(last, at))

    def second(block, total):
        rows = rows_of(lax.bitwise_xor(block, rank), piece)
        grad_scores = (prob_ref[rows, :] * (chance_ref[rows, :] - weighted)).astype(BF16)
        key_sum[rows, :] += nn(grad_scores, query)
        return total + nn(key_t[:, rows], grad_scores)

    total = lax.fori_loop(0, true + 1, second, jnp.zeros((HEAD_DIM, piece), F32))
    query_out[...] = (total * FACTOR).T.astype(BF16)
    if last_call:
        key_out[...] = (key_sum[...] * FACTOR).astype(BF16)
        value_out[...] = value_sum[...].astype(BF16)
    else:
        key_out[...] = key_sum[...]
        value_out[...] = value_sum[...]


def retreat(at, rank, low, proj, q, lse, k, v, k_t, key_bias, sums, previous, last_call):
    length, columns = q.shape
    piece, width = low.shape
    heads = columns // HEAD_DIM
    tall = pl.BlockSpec((length, HEAD_DIM), lambda h, r: (0, h))
    part = pl.BlockSpec((piece, HEAD_DIM), lambda h, r: (at, h))
    inputs = [
        (low, pl.BlockSpec((piece, width), lambda h, r: (0, 0))),
        (proj, pl.BlockSpec((HEAD_DIM, width), lambda h, r: (h, 0))),
        (q, part),
        (lse, pl.BlockSpec((1, 1, piece), lambda h, r: (h, 0, at))),
        (k, tall),
        (v, tall),
        (k_t, pl.BlockSpec((HEAD_DIM, length), lambda h, r: (h, 0))),
        (key_bias, pl.BlockSpec((length, 1), lambda h, r: (0, 0))),
    ]
    if sums is not None:
        inputs += [(item, tall) for item in sums]
    kind = BF16 if last_call else F32
    fresh = [(jax.ShapeDtypeStruct((length, columns), kind), tall)] * 2
    shared = [
        (jax.ShapeDtypeStruct((length, columns), BF16), part),
        (jax.ShapeDtypeStruct((length, width), BF16), pl.BlockSpec((piece, width), lambda h, r: (at, 0))),
    ]
    scratch = [pltpu.VMEM((length, piece), F32)] * 2 + [pltpu.VMEM((length, HEAD_DIM), F32)] * 2
    return call_on_block(
        functools.partial(retreat_kernel, at, sums is None, last_call), (heads,), inputs, fresh, shared, previous,
        scratch,
        cost(
            5 * 1.3 * length * piece * columns + 2 * piece * columns * width, 20 * length * columns,
            heads * length * piece * 0.6,
        ), rank,
    )


def back_kernel(grads, weight, out):
    out[...] = nt(grads[...], weight[...]).astype(BF16)


def back(at, grads, weight, piece):
    columns, width = grads.shape[1], weight.shape[0]
    tile = min(512, width)
    return pl.pallas_call(
        back_kernel,
        grid=(width // tile,),
        in_specs=[
            pl.BlockSpec((piece, columns), lambda j: (at, 0)),
            pl.BlockSpec((tile, columns), lambda j: (j, 0)),
        ],
        out_specs=pl.BlockSpec((piece, tile), lambda j: (0, j)),
        out_shape=jax.ShapeDtypeStruct((piece, width), BF16),
        compiler_params=params(),
        cost_estimate=cost(2 * piece * width * columns, 2 * width * columns + 2 * piece * (columns + width)),
    )(grads, weight)


def part_specs(parts, tile, steps, width):
    arrays, specs = [], []
    for part in parts:
        if isinstance(part, tuple):
            middle = steps // 2
            arrays += list(part)
            specs.append(pl.BlockSpec((tile, width), lambda i: (jnp.minimum(i, middle - 1), 0)))
            specs.append(pl.BlockSpec((tile, width), lambda i: (jnp.maximum(i - middle, 0), 0)))
        else:
            arrays.append(part)
            specs.append(pl.BlockSpec((tile, width), lambda i: (i, 0)))
    return arrays, specs


def add_parts(kinds, refs):
    total = None
    upper = pl.program_id(0) < pl.num_programs(0) // 2
    for kind in kinds:
        if kind:
            high, low = refs.pop(0)[...], refs.pop(0)[...]
            term = jnp.where(upper, high.astype(F32), low.astype(F32))
        else:
            term = refs.pop(0)[...].astype(F32)
        total = term if total is None else total + term
    return total


def rowwise(kernel, parts, rows, vectors, outputs, sums):
    count, width = rows[0].shape
    tile = min(128, count // 2)
    steps = count // tile
    arrays, specs = part_specs(parts, tile, steps, width)
    kinds = [isinstance(part, tuple) for part in parts]
    specs += [pl.BlockSpec((tile, width), lambda i: (i, 0))] * len(rows)
    specs += [pl.BlockSpec((1, width), lambda i: (0, 0))] * len(vectors)

    def body(*refs):
        refs = list(refs)
        total = add_parts(kinds, refs)
        tiles = [refs.pop(0)[...] for _ in rows]
        given = [refs.pop(0)[...] for _ in vectors]
        results = kernel(total, tiles, given)
        for result, _ in zip(results, outputs):
            refs.pop(0)[...] = result
        for result in results[len(outputs) :]:
            ref = refs.pop(0)
            column = jnp.sum(result, axis=0, keepdims=True)

            @pl.when(pl.program_id(0) == 0)
            def _():
                ref[...] = column

            @pl.when(pl.program_id(0) > 0)
            def _():
                ref[...] += column

    return pl.pallas_call(
        body,
        grid=(steps,),
        in_specs=specs,
        out_specs=[pl.BlockSpec((tile, width), lambda i: (i, 0))] * len(outputs)
        + [pl.BlockSpec((1, width), lambda i: (0, 0))] * sums,
        out_shape=[jax.ShapeDtypeStruct((count, width), kind) for kind in outputs]
        + [jax.ShapeDtypeStruct((1, width), F32)] * sums,
        compiler_params=params(),
        cost_estimate=cost(20 * count * width, count * width * (2 * len(arrays) + 4 * len(rows) + 4 * len(outputs))),
    )(*arrays, *rows, *vectors)


def middle_kernel(total, rows, vectors):
    (tokens,), (bias, gain, shift_) = rows, vectors
    middle = tokens.astype(F32) + (total + bias)
    return middle, (norm_parts(middle)[0] * gain + shift_).astype(BF16)


def out_kernel(total, rows, vectors):
    return (((rows[0] + (total + vectors[0])).astype(BF16)),)


def middle_back_kernel(total, rows, vectors):
    (middle, cot), (gain,) = rows, vectors
    normed, scale = norm_parts(middle)
    cot = cot.astype(F32)
    grad = cot + norm_backward(normed, scale, gain, total)
    low = grad.astype(BF16)
    return grad, low, total * normed, total, low.astype(F32), cot


def tokens_back_kernel(total, rows, vectors):
    (tokens, grad_middle), (gain,) = rows, vectors
    normed, scale = norm_parts(tokens.astype(F32))
    return grad_middle + norm_backward(normed, scale, gain, total), total * normed, total


def lay_out(rank, blocks, width, places):
    rows = blocks[0][0].shape[0]
    count, each = len(blocks), len(blocks[0])
    unit = places[1]

    def body(rank_ref, *refs):
        out = refs[-1]
        for k in range(count):
            source = lax.bitwise_xor(k, rank_ref[0])
            for array, column, target in places[0](source):
                out[:, pl.ds(pl.multiple_of(target * unit, unit), unit)] = refs[k * each + array][
                    :, column * unit : (column + 1) * unit
                ].astype(F32)

    arrays = [item for block in blocks for item in block]
    return pl.pallas_call(
        body,
        grid_spec=pltpu.PrefetchScalarGridSpec(
            num_scalar_prefetch=1,
            grid=(1,),
            in_specs=[pl.BlockSpec(item.shape, lambda i, r: (0, 0)) for item in arrays],
            out_specs=pl.BlockSpec((rows, width), lambda i, r: (0, 0)),
        ),
        out_shape=jax.ShapeDtypeStruct((rows, width), F32),
        compiler_params=params(),
        cost_estimate=cost(rows * width, 6 * rows * width),
    )(rank, *arrays)


def neighbours():
    rank = lax.axis_index("seq")
    return rank + 1 - 2 * lax.rem(rank, 2), rank + 2 - 4 * lax.rem(lax.div(rank, 2), 2)


def remote(source, target, send, receive, axis, device):
    return pltpu.make_async_remote_copy(
        src_ref=source, dst_ref=target, send_sem=send, recv_sem=receive, device_id={axis: device}, device_id_type=MESH
    )


def greet(axis, device):
    pl.semaphore_signal(pltpu.get_barrier_semaphore(), inc=1, device_id={axis: device}, device_id_type=MESH)


def flip(first, second):
    low = lax.rem(first + second, 2)
    high = lax.rem(lax.div(first, 2) + lax.div(second, 2), 2)
    return 2 * high + low


class LevelScatter:
    def __init__(self, source, mate_in, summed, got, send, receive):
        self.source, self.mate_in, self.summed, self.got = source, mate_in, summed, got
        self.send, self.receive = send, receive
        self.rows = mate_in.shape[0] // 4
        self.place = lax.axis_index("dp")
        self.level, self.core = lax.div(self.place, 2), lax.rem(self.place, 2)
        self.mate = self.place + 1 - 2 * self.core

    def greet(self):
        greet("dp", self.mate)
        count = jnp.int32(1)
        for step in (1, 2):
            up, down = self.level + step <= 3, self.level >= step
            pl.when(up)(lambda step=step: greet("dp", self.place + 2 * step))
            pl.when(down)(lambda step=step: greet("dp", self.place - 2 * step))
            count = count + up.astype(jnp.int32) + down.astype(jnp.int32)
        return count

    def block(self, ref, at):
        return ref.at[pl.ds(at * self.rows, self.rows)]

    def swaps(self):
        return [
            remote(
                self.block(self.source, 2 * at + 1 - self.core), self.block(self.mate_in, at),
                self.send.at[at], self.receive.at[at], "dp", self.mate,
            )
            for at in range(4)
        ]

    def start(self):
        for item in self.swaps():
            item.start()

    def add(self, first, second, out, grid, first_at, second_at, out_at):
        def body(left, right, total):
            total[...] = (left[...].astype(F32) + right[...].astype(F32)).astype(total.dtype)

        spec = lambda at: pl.BlockSpec((self.rows, first.shape[1]), lambda i: (at(i), 0))
        pltpu.emit_pipeline(
            body, grid=(grid,), in_specs=[spec(first_at), spec(second_at)], out_specs=[spec(out_at)]
        )(first, second, out)

    def hop(self, at, slot, index, steps):
        return remote(
            self.block(self.summed, at), self.block(self.got, slot), self.send.at[4 + index], self.receive.at[4 + slot],
            "dp", self.place + 2 * steps,
        )

    def hops(self):
        level = self.level
        return [
            (level == 0, self.hop(3, 3, 0, 1)),
            (level == 3, self.hop(0, 3, 0, -1)),
            (level == 0, self.hop(2, 2, 1, 2)),
            (level == 3, self.hop(1, 2, 1, -2)),
            (level <= 2, self.hop(lax.rem(level + 1, 4), 0, 2, 1)),
            (level >= 1, self.hop(lax.rem(level + 3, 4), 1, 3, -1)),
        ]

    def first_hops(self):
        hops, inner = self.hops(), (self.level == 1) | (self.level == 2)
        return hops[:2] + [(inner, hops[4][1]), (inner, hops[5][1])]

    def later_hops(self):
        hops = self.hops()
        return hops[2:4] + [(self.level == 0, hops[4][1]), (self.level == 3, hops[5][1])]

    def passes(self):
        return [(self.level == 1, self.hop(3, 2, 1, 2)), (self.level == 2, self.hop(0, 2, 1, -2))]

    def combine(self):
        for item in self.swaps():
            item.wait_recv()
        self.add(
            self.source, self.mate_in, self.summed, 4, lambda i: 2 * i + self.core, lambda i: i, lambda i: i
        )

    def spread(self):
        self.combine()
        for condition, copy in self.first_hops():
            pl.when(condition)(lambda copy=copy: copy.start())

    def arrive(self, slot):
        here = self.block(self.got, slot)
        remote(here, here, self.send.at[0], self.receive.at[4 + slot], "dp", self.mate).wait_recv()

    def pass_on(self):
        for level, at in ((1, 3), (2, 0)):

            @pl.when(self.level == level)
            def _(at=at):
                self.arrive(3)
                self.add(self.summed, self.got, self.summed, 1, lambda i: at, lambda i: 3, lambda i: at)

        for condition, copy in self.passes() + self.later_hops():
            pl.when(condition)(lambda copy=copy: copy.start())

    def finish(self, out):
        level = self.level
        pl.when(level >= 1)(lambda: self.arrive(0))
        pl.when(level <= 2)(lambda: self.arrive(1))
        self.arrive(2)
        rows = min(64, self.rows)

        def body(own, mate, below, above, far, total):
            value = own[...].astype(F32) + mate[...].astype(F32) + far[...].astype(F32)
            below_term, above_term = below[...].astype(F32), above[...].astype(F32)
            value = value + jnp.where(level >= 1, below_term, 0.0) + jnp.where(level <= 2, above_term, 0.0)
            total[...] = value.astype(total.dtype)

        steps = self.rows // rows
        spec = lambda at: pl.BlockSpec((rows, out.shape[1]), lambda i: (at * steps + i, 0))
        pltpu.emit_pipeline(
            body,
            grid=(steps,),
            in_specs=[spec(self.place), spec(level), spec(0), spec(1), spec(2)],
            out_specs=[spec(0)],
        )(self.source, self.mate_in, self.got, self.got, self.got, out)

    def close(self):
        for item in self.swaps():
            item.wait_send()
        for condition, copy in self.hops() + self.passes():
            pl.when(condition)(lambda copy=copy: copy.wait_send())


class LateScatter(LevelScatter):
    def __init__(self, summed, got, through, own, send, receive, load):
        self.summed, self.got, self.through, self.own = summed, got, through, own
        self.send, self.receive, self.load = send, receive, load
        self.rows = own.shape[0]
        self.place = lax.axis_index("dp")
        self.level, self.core = lax.div(self.place, 2), lax.rem(self.place, 2)
        self.mate = self.place + 1 - 2 * self.core

    def loads(self):
        passed_on = 3 * lax.rem(self.level, 2)
        return (
            pltpu.make_async_copy(self.block(self.summed, self.level), self.own, self.load.at[0]),
            pltpu.make_async_copy(self.block(self.summed, passed_on), self.through, self.load.at[1]),
        )

    def passes(self):
        target = self.block(self.got, 2)
        send, receive = self.send.at[4 + 1], self.receive.at[4 + 2]
        return [
            (self.level == 1, remote(self.through, target, send, receive, "dp", self.place + 4)),
            (self.level == 2, remote(self.through, target, send, receive, "dp", self.place - 4)),
        ]

    def start(self):
        for condition, copy in self.first_hops():
            pl.when(condition)(lambda copy=copy: copy.start())
        for item in self.loads():
            item.start()

    def part(self, slot):
        return self.got[slot * self.rows : (slot + 1) * self.rows, :].astype(F32)

    def pass_on(self):
        for item in self.loads():
            item.wait()

        @pl.when((self.level == 1) | (self.level == 2))
        def _():
            self.arrive(3)
            self.through[...] = (self.through[...].astype(F32) + self.part(3)).astype(BF16)

        for condition, copy in self.passes() + self.later_hops():
            pl.when(condition)(lambda copy=copy: copy.start())

    def finish(self, out):
        level = self.level
        pl.when(level >= 1)(lambda: self.arrive(0))
        pl.when(level <= 2)(lambda: self.arrive(1))
        self.arrive(2)
        value = self.own[...].astype(F32) + self.part(2)
        value = value + jnp.where(level >= 1, self.part(0), 0.0)
        value = value + jnp.where(level <= 2, self.part(1), 0.0)
        out[...] = value.astype(BF16)

    def close(self):
        for condition, copy in self.hops() + self.passes():
            pl.when(condition)(lambda copy=copy: copy.wait_send())


class NearScatter(LevelScatter):
    def part(self, ref, at):
        return ref[pl.ds(pl.multiple_of(at * self.rows, self.rows), self.rows), :].astype(F32)

    def spread(self):
        for item in self.swaps():
            item.wait_recv()
        for at in range(4):
            total = self.part(self.source, 2 * at + self.core) + self.part(self.mate_in, at)
            self.summed[at * self.rows : (at + 1) * self.rows, :] = total.astype(BF16)
        for condition, copy in self.first_hops():
            pl.when(condition)(lambda copy=copy: copy.start())

    def pass_on(self):
        for level, at in ((1, 3), (2, 0)):

            @pl.when(self.level == level)
            def _(at=at):
                self.arrive(3)
                total = self.part(self.summed, at) + self.part(self.got, 3)
                self.summed[at * self.rows : (at + 1) * self.rows, :] = total.astype(BF16)

        for condition, copy in self.passes() + self.later_hops():
            pl.when(condition)(lambda copy=copy: copy.start())

    def finish(self, out):
        level = self.level
        pl.when(level >= 1)(lambda: self.arrive(0))
        pl.when(level <= 2)(lambda: self.arrive(1))
        self.arrive(2)
        value = self.part(self.source, self.place) + self.part(self.mate_in, level) + self.part(self.got, 2)
        value = value + jnp.where(level >= 1, self.part(self.got, 0), 0.0)
        value = value + jnp.where(level <= 2, self.part(self.got, 1), 0.0)
        out[...] = value.astype(BF16)


class LevelGather:
    def __init__(self, own, full, send, receive, mate_send, mate_receive):
        self.own, self.full, self.send, self.receive = own, full, send, receive
        self.mate_send, self.mate_receive = mate_send, mate_receive
        self.rows = own.shape[0]
        self.place = lax.axis_index("dp")
        self.level, self.core = lax.div(self.place, 2), lax.rem(self.place, 2)
        self.mate = self.place + 1 - 2 * self.core

    greet = LevelScatter.greet

    def shard(self, level):
        return self.full.at[pl.ds((2 * level + self.core) * self.rows, self.rows)]

    def hop(self, index, steps, slot):
        return remote(
            self.own, self.shard(self.level), self.send.at[index], self.receive.at[slot], "dp", self.place + 2 * steps
        )

    def near(self):
        return [(self.level <= 2, self.hop(0, 1, 0)), (self.level >= 1, self.hop(1, -1, 1))]

    def second(self):
        inner = (self.level == 1) | (self.level == 2)
        lower, upper = self.shard(self.level - 1), self.shard(self.level + 1)
        return [
            (inner, remote(lower, lower, self.send.at[2], self.receive.at[2], "dp", self.place + 2)),
            (inner, remote(upper, upper, self.send.at[3], self.receive.at[2], "dp", self.place - 2)),
        ]

    def passes(self):
        first, last = self.shard(0), self.shard(3)
        return [
            (self.level == 2, remote(first, first, self.send.at[4], self.receive.at[3], "dp", self.place + 2)),
            (self.level == 1, remote(last, last, self.send.at[4], self.receive.at[3], "dp", self.place - 2)),
        ]

    def across(self, index, level):
        here = self.own if index == 4 else self.shard(level)
        return remote(here, self.shard(level), self.mate_send.at[index], self.mate_receive.at[index], "dp", self.mate)

    def arrivals(self, slots):
        level = self.level
        two_away = level + 2 - 4 * lax.div(level, 2)
        every = [
            (level >= 1, 0, level - 1),
            (level <= 2, 1, level + 1),
            (level >= 0, 2, two_away),
            ((level == 0) | (level == 3), 3, 3 - level),
        ]
        return [item for item in every if item[1] in slots]

    def start(self, hops):
        for condition, copy in hops:
            pl.when(condition)(lambda copy=copy: copy.start())

    def take(self, slots):
        for condition, slot, level in self.arrivals(slots):

            @pl.when(condition)
            def _(slot=slot, level=level):
                here = self.shard(level)
                remote(here, here, self.send.at[0], self.receive.at[slot], "dp", self.mate).wait_recv()
                self.across(slot, level).start()

    def finish(self, slots, hops):
        for condition, slot, level in self.arrivals(slots):
            pl.when(condition)(lambda slot=slot, level=level: self.across(slot, level).wait())
        for condition, copy in hops:
            pl.when(condition)(lambda copy=copy: copy.wait_send())


def opening_kernel(
    tokens, cot, qkv_weight, fc_weight, small, down, proj,
    token_all, qkv_full, fc_rows, cot_one, cot_two, down_full, proj_full, vectors, key_bias,
    qkv_pieces, fc_pieces, token_buf, qkv_rows, small_rows, small_full, proj_rows, square, local, send, receive, up_send, up_receive, down_send, down_receive, mate_send, mate_receive,
    level_send, level_receive, level_mate_send, level_mate_receive,
):
    piece = tokens.shape[0]
    half = piece // 2
    gather = LevelGather(down, down_full, level_send, level_receive, level_mate_send, level_mate_receive)
    me, place = lax.axis_index("seq"), lax.axis_index("dp")
    one, two = neighbours()
    three = 3 - me
    stages = lax.axis_size("dp") // 2
    level, core = lax.div(place, 2), lax.rem(place, 2)
    mate = place + 1 - 2 * core
    above, below = level < stages - 1, level > 0

    for device in (one, two, three):
        greet("seq", device)
    greet("dp", mate)
    pl.when(above)(lambda: greet("dp", place + 2))
    pl.when(below)(lambda: greet("dp", place - 2))
    swaps = core != lax.rem(me, 2)
    partner = {"dp": mate, "seq": one}

    @pl.when(swaps)
    def _():
        pl.semaphore_signal(pltpu.get_barrier_semaphore(), inc=1, device_id=partner, device_id_type=MESH)

    heads = qkv_pieces.shape[2] // (3 * HEAD_DIM)
    for rank in range(4):
        for part in range(3):
            for head in range(heads):
                source = (part * HEADS + (head * 2 + rank % 2) * 2 + rank // 2) * HEAD_DIM
                target = (part * heads + head) * HEAD_DIM
                qkv_pieces[rank, :, target : target + HEAD_DIM] = qkv_weight[:, source : source + HEAD_DIM]
    count = 4 + above.astype(jnp.int32) + below.astype(jnp.int32) + swaps.astype(jnp.int32)
    pl.semaphore_wait(pltpu.get_barrier_semaphore(), count)

    def block(ref, at, start=0, size=piece):
        return ref.at[pl.ds(at * piece + start, size)]

    def spread(pieces, target, at):
        rows = target.shape[0] // 4
        mine = target.at[pl.ds(me * rows, rows)]
        source = lambda device: pieces if pieces is small else pieces.at[device]
        copies = [
            remote(source(device), mine, send.at[at + i], receive.at[at + i], "seq", device)
            for i, device in enumerate((one, two, three))
        ]
        return copies, source(me), mine

    qkv_copies, qkv_own, qkv_mine = spread(qkv_pieces, qkv_rows, 0)
    small_copies, small_own, small_mine = spread(small, small_rows, 3)
    fc_copies, fc_own, fc_mine = spread(fc_pieces, fc_rows, 6)
    token_one = remote(tokens, block(token_all, 1), send.at[9], receive.at[9], "seq", one)
    token_two = remote(tokens, block(token_all, 2), send.at[10], receive.at[10], "seq", two)
    token_three = (
        remote(block(token_all, 1, 0, half), block(token_all, 3, 0, half), send.at[11], receive.at[11], "seq", two),
        remote(block(token_all, 2, half, half), block(token_all, 3, half, half), send.at[12], receive.at[12], "seq", one),
    )
    first_kept = [pltpu.make_async_copy(qkv_own, qkv_mine, local.at[0]), pltpu.make_async_copy(small_own, small_mine, local.at[1])]
    later_kept = [
        pltpu.make_async_copy(fc_own, fc_mine, local.at[2]),
        pltpu.make_async_copy(token_buf, block(token_all, 0), local.at[3]),
    ]
    token_load = pltpu.make_async_copy(tokens, token_buf, local.at[4])
    cot_copies = (
        remote(cot.at[pl.ds(0, half)], cot_one, send.at[13], receive.at[13], "seq", one),
        remote(cot.at[pl.ds(0, half)], cot_two, send.at[14], receive.at[14], "seq", two),
    )

    proj_copy = pltpu.make_async_remote_copy(
        src_ref=proj, dst_ref=proj_rows, send_sem=send.at[15], recv_sem=receive.at[15], device_id=partner,
        device_id_type=MESH,
    )
    chains = ((qkv_rows, qkv_full), (small_rows, small_full), (proj_rows, proj_full))

    def shard(array, at):
        rows = chains[array][0].shape[0]
        return chains[array][1].at[pl.ds((2 * at + core) * rows, rows)]

    def rising(array, step, device):
        at = level - (step - 1)
        source = chains[array][0] if step == 1 else shard(array, at)
        return remote(source, shard(array, at), up_send.at[array, step - 1], up_receive.at[array, step - 1], "dp", device)

    def falling(array, step, device):
        at = level + (step - 1)
        source = chains[array][0] if step == 1 else shard(array, at)
        return remote(source, shard(array, at), down_send.at[array, step - 1], down_receive.at[array, step - 1], "dp", device)

    def across(array, index, at):
        source = chains[array][0] if index == 0 else shard(array, at)
        return remote(source, shard(array, at), mate_send.at[array, index], mate_receive.at[array, index], "dp", mate)

    rises = lambda step: above & (level >= step - 1)
    falls = lambda step: below & (level <= stages - step)
    from_below = lambda step: level >= step
    from_above = lambda step: level + step <= stages - 1

    def relay(step):
        @pl.when(rises(step))
        def _():
            for array in (1, 0, 2):
                rising(array, step, place + 2).start()

        @pl.when(falls(step))
        def _():
            for array in (1, 0, 2):
                falling(array, step, place - 2).start()

    def take(step):
        @pl.when(from_below(step))
        def _():
            for array in (1, 0, 2):
                got = shard(array, level - step)
                remote(got, got, up_send.at[array, step - 1], up_receive.at[array, step - 1], "dp", mate).wait_recv()
                across(array, step, level - step).start()

        @pl.when(from_above(step))
        def _():
            for array in (1, 0, 2):
                got = shard(array, level + step)
                remote(got, got, down_send.at[array, step - 1], down_receive.at[array, step - 1], "dp", mate).wait_recv()
                across(array, stages - 1 + step, level + step).start()

    for copy in qkv_copies + small_copies + first_kept:
        copy.start()
    pl.when(swaps)(proj_copy.start)

    @pl.when(jnp.logical_not(swaps))
    def _():
        proj_rows[...] = proj[...]

    token_one.start()
    token_two.start()
    gather.start(gather.near())
    gather.across(4, level).start()
    down_kept = pltpu.make_async_copy(down, gather.shard(level), local.at[8])
    down_kept.start()
    token_load.start()
    inner = fc_pieces.shape[2] // 8
    for rank in range(4):
        for d in range(8):
            source = (d * 4 + rank) * inner
            fc_pieces[rank, :, d * inner : (d + 1) * inner] = fc_weight[:, source : source + inner]
    token_load.wait()
    for copy in qkv_copies + small_copies:
        copy.wait_recv()
    pl.when(swaps)(proj_copy.wait_recv)
    for copy in first_kept:
        copy.wait()
    relay(1)
    own_full = [pltpu.make_async_copy(chains[array][0], shard(array, level), local.at[5 + array]) for array in range(3)]
    for array in range(3):
        across(array, 0, level).start()
        own_full[array].start()
    for copy in fc_copies + later_kept:
        copy.start()
    for copy in cot_copies:
        copy.start()
    take(1)
    relay(2)
    take(2)
    relay(3)
    gather.take((0, 1))
    token_one.wait_recv()
    token_two.wait_recv()
    for copy in token_three:
        copy.start()
    take(3)
    for copy in later_kept + own_full:
        copy.wait()
    for copy in fc_copies:
        copy.wait_recv()
    for copy in qkv_copies + small_copies + fc_copies:
        copy.wait_send()
    token_one.wait_send()
    token_two.wait_send()
    for step in range(1, stages):

        @pl.when(rises(step))
        def _(step=step):
            for array in range(3):
                rising(array, step, place + 2).wait_send()

        @pl.when(falls(step))
        def _(step=step):
            for array in range(3):
                falling(array, step, place - 2).wait_send()

        @pl.when(from_below(step))
        def _(step=step):
            for array in range(3):
                across(array, step, level - step).wait()

        @pl.when(from_above(step))
        def _(step=step):
            for array in range(3):
                across(array, stages - 1 + step, level + step).wait()

    for array in range(3):
        across(array, 0, level).wait()
    for copy in token_three:
        copy.wait()
    down_kept.wait()
    pl.when(swaps)(proj_copy.wait_send)
    tile = lambda d, s: small_full[pl.ds(pl.multiple_of((d * 4 + s) * 16, 16), 16), :].astype(F32)
    vectors[...] = jnp.zeros_like(vectors)
    for d in range(8):
        for pair in range(2):
            both = tile(d, 2 * pair) + tile(d, 2 * pair + 1)
            vectors[0:6, (2 * d + pair) * 128 : (2 * d + pair + 1) * 128] = both[0:6]
        own = tile(d, me)
        for i in range(2):
            vectors[6:7, (2 * d + i) * 128 : (2 * d + i + 1) * 128] = own[7 + i : 8 + i]
        bias = tile(d, 2 * lax.rem(me, 2) + lax.div(me, 2))
        vectors[7:8, d * HEAD_DIM : (d + 1) * HEAD_DIM] = bias[6:7]
    square[...] = jnp.zeros_like(square)
    for i in range(4):
        square[4 * i : 4 * i + 4, :] = tile(place, flip(me, i))[9:13]
    turned = square[...].T
    lane = lax.broadcasted_iota(jnp.int32, turned.shape, 1)
    for i in range(16):
        flag = jnp.sum(jnp.where(lane == i, turned, 0.0), axis=1, keepdims=True)
        key_bias[i * 128 : (i + 1) * 128, :] = jnp.where(flag > 0, 0.0, NEG)
    for copy in cot_copies:
        copy.wait()
    gather.finish((0, 1), gather.near())
    gather.across(4, level).wait()


def opening(tokens, cot, qkv_weight, fc_weight, small, down, proj, dp_count):
    piece, width = tokens.shape
    steps = dp_count // 2 - 1
    anywhere = pl.BlockSpec(memory_space=pltpu.HBM)
    shape = lambda rows, columns: jax.ShapeDtypeStruct((rows, columns), BF16)
    dma = pltpu.SemaphoreType.DMA
    inside = pl.BlockSpec(memory_space=pltpu.VMEM)
    own_rows, columns, inner = qkv_weight.shape[0], qkv_weight.shape[1] // 4, fc_weight.shape[1] // 4
    rows, fine = 4 * own_rows, 4 * small.shape[0]
    return pl.pallas_call(
        opening_kernel,
        in_specs=[anywhere] * 2 + [inside] * 5,
        out_specs=[anywhere] * 7 + [inside] * 2,
        out_shape=[
            shape(4 * piece, width),
            shape(rows * dp_count, columns),
            shape(rows, inner),
            shape(piece // 2, width),
            shape(piece // 2, width),
            shape(down.shape[0] * dp_count, width),
            shape(proj.shape[0] * dp_count, width),
            jax.ShapeDtypeStruct((8, width), F32),
            jax.ShapeDtypeStruct((4 * piece, 1), F32),
        ],
        scratch_shapes=[
            pltpu.VMEM((4, own_rows, columns), BF16), pltpu.VMEM((4, own_rows, inner), BF16),
            pltpu.VMEM((piece, width), BF16),
            pltpu.VMEM((rows, columns), BF16), pltpu.VMEM((fine, 128), BF16), pltpu.VMEM((fine * dp_count, 128), BF16),
            pltpu.VMEM(proj.shape, BF16), pltpu.VMEM((128, 128), F32),
            dma((9,)), dma((16,)), dma((16,)), dma((3, steps)), dma((3, steps)), dma((3, steps)), dma((3, steps)),
            dma((3, 2 * steps + 1)), dma((3, 2 * steps + 1)), dma((5,)), dma((4,)), dma((5,)), dma((5,)),
        ],
        compiler_params=pltpu.CompilerParams(collective_id=0, has_side_effects=True, vmem_limit_bytes=62 * 2**20),
        cost_estimate=cost(0, 10 * 4 * piece * width),
    )(tokens, cot, qkv_weight, fc_weight, small, down, proj)


def attend_plane_kernel(
    tokens, cot, token_all, weight, cot_one, down, down_in, key_bias, proj, vectors,
    middle, normed, attended, lse, cot_three, down_full, normed_one, q, k, v, k_t, v_t, one_low, two_low,
    score_ref, joint, terms, passed, joined, arrived, send, receive,
    level_send, level_receive, mate_send, mate_receive,
):
    piece, width = tokens.shape
    half = piece // 2
    length, columns = q.shape
    heads = columns // HEAD_DIM
    rank = lax.axis_index("seq")
    one, two = neighbours()
    gather = LevelGather(down, down_full, level_send, level_receive, mate_send, mate_receive)
    for device in (one, two):
        greet("seq", device)
    pl.semaphore_wait(pltpu.get_barrier_semaphore(), 2 + gather.greet())
    up, lower = pl.ds(0, half), pl.ds(half, half)
    gather.start(gather.second())

    def copy(index, source, target, device):
        return remote(source, target, send.at[index], receive.at[index], "seq", device)

    cot_copies = (copy(0, cot_one, cot_three.at[up], two), copy(1, two_low, cot_three.at[lower], one))
    low_copies = (copy(8, cot.at[lower], one_low, one), copy(9, cot.at[lower], two_low, two))
    across = (copy(2, terms.at[3, up], passed.at[0], one), copy(3, terms.at[3, lower], passed.at[1], two))
    plain_one = copy(4, terms.at[1, up], arrived.at[0, up], one)
    plain_two = copy(5, terms.at[2, lower], arrived.at[1, lower], two)
    joined_one = copy(6, joined.at[0], arrived.at[0, lower], one)
    joined_two = copy(7, joined.at[1], arrived.at[1, up], two)
    for item in low_copies:
        item.start()
    cot_copies[0].start()
    tile = min(256, piece)
    rows = lambda n: pl.BlockSpec((tile, n), lambda i: (i, 0))
    turned = pl.BlockSpec((columns, tile), lambda i: (0, i))
    pltpu.emit_pipeline(
        lambda x, wq, wk, wv, *out: project_kernel(x, vectors, wq, wk, wv, *out),
        grid=(length // tile,),
        in_specs=[rows(width)] + [pl.BlockSpec((width, columns), lambda i, part=part: (0, part)) for part in range(3)],
        out_specs=[rows(width), rows(columns), rows(columns), rows(columns), turned, turned],
    )(token_all, weight, weight, weight, normed_one, q, k, v, k_t, v_t)
    for item in low_copies:
        item.wait_recv()
    cot_copies[1].start()

    def body(query_ref, key_ref, value_t, attended_tile, lse_tile):
        group, head = pl.program_id(0), pl.program_id(1)
        at = 3 - group
        true = flip(at, rank)
        query = query_ref[...]

        def first(block, top):
            scores = scores_of(key_ref, key_bias, query, flip(block, rank), piece, False)
            score_ref[rows_of(block, piece), :] = scores
            return jnp.maximum(top, jnp.max(scores, axis=0, keepdims=True))

        last = scores_of(key_ref, key_bias, query, at, piece, True)
        top = lax.fori_loop(0, true, first, jnp.max(last, axis=0, keepdims=True))

        def weigh(scores, rel):
            weights = jnp.exp2(scores - top)
            return jnp.sum(weights, axis=0, keepdims=True), nn(value_t[:, rows_of(rel, piece)], weights.astype(BF16))

        def second(block, carry):
            total, out = carry
            more, part = weigh(score_ref[rows_of(block, piece), :], flip(block, rank))
            return total + more, out + part

        total, out = lax.fori_loop(0, true, second, weigh(last, at))
        result = (out / total).T.astype(BF16)
        attended_tile[...] = result
        lse_tile[0] = top + jnp.log2(total)
        joint[:, pl.ds(pl.multiple_of(head * HEAD_DIM, HEAD_DIM), HEAD_DIM)] = result

        @pl.when(head == heads - 1)
        def _():
            terms[at] = nn(joint[...], proj[...]).astype(BF16)

        @pl.when((head == heads - 1) & (group == 0))
        def _():
            for item in across:
                item.start()

        @pl.when((head == heads - 1) & (group == 1))
        def _():
            plain_two.start()

        @pl.when((head == 0) & (group == 3))
        def _():
            gather.take((2,))
            gather.start(gather.passes())

        @pl.when((head == heads - 1) & (group == 2))
        def _():
            plain_one.start()
            for item in across:
                item.wait_recv()
            joined[0] = (terms[1, half:].astype(F32) + passed[1].astype(F32)).astype(BF16)
            joined[1] = (terms[2, :half].astype(F32) + passed[0].astype(F32)).astype(BF16)
            joined_one.start()
            joined_two.start()

    pltpu.emit_pipeline(
        body,
        grid=(4, heads),
        in_specs=[
            pl.BlockSpec((piece, HEAD_DIM), lambda g, h: (3 - g, h)),
            pl.BlockSpec((length, HEAD_DIM), lambda g, h: (0, h)),
            pl.BlockSpec((HEAD_DIM, length), lambda g, h: (h, 0)),
        ],
        out_specs=[
            pl.BlockSpec((piece, HEAD_DIM), lambda g, h: (3 - g, h)),
            pl.BlockSpec((1, 1, piece), lambda g, h: (h, 0, 3 - g)),
        ],
    )(q, k, v_t, attended, lse)

    for item in (plain_one, plain_two, joined_one, joined_two):
        item.wait_recv()
    part = min(128, piece)

    def norm_body(token_tile, middle_tile, normed_tile):
        here = pl.ds(pl.multiple_of(pl.program_id(0) * part, part), part)
        total = terms[0, here, :].astype(F32) + arrived[0, here, :].astype(F32) + arrived[1, here, :].astype(F32)
        values = token_tile[...].astype(F32) + (total + vectors[2:3, :])
        middle_tile[...] = values
        normed_tile[...] = (norm_parts(values)[0] * vectors[3:4, :] + vectors[4:5, :]).astype(BF16)

    line = pl.BlockSpec((part, width), lambda i: (i, 0))
    pltpu.emit_pipeline(norm_body, grid=(piece // part,), in_specs=[line], out_specs=[line] * 2)(tokens, middle, normed)
    gather.take((3,))
    gather.finish((2, 3), gather.second() + gather.passes())
    for item in cot_copies:
        item.wait()
    for item in low_copies:
        item.wait_send()
    for item in (*across, plain_one, plain_two, joined_one, joined_two):
        item.wait_send()


def attend_plane(tokens, cot, token_all, weight, cot_one, down, down_in, key_bias, proj, vectors):
    piece, width = tokens.shape
    length, columns = token_all.shape[0], proj.shape[0]
    heads, half = columns // HEAD_DIM, piece // 2
    anywhere = pl.BlockSpec(memory_space=pltpu.HBM)
    inside = pl.BlockSpec(memory_space=pltpu.VMEM)
    shape = lambda *dims: jax.ShapeDtypeStruct(dims, BF16)
    dma = pltpu.SemaphoreType.DMA
    return pl.pallas_call(
        attend_plane_kernel,
        in_specs=[anywhere] * 7 + [inside] * 3,
        out_specs=[anywhere] * 14,
        input_output_aliases={6: 5},
        out_shape=[
            jax.ShapeDtypeStruct((piece, width), F32), shape(piece, width), shape(length, columns),
            jax.ShapeDtypeStruct((heads, 1, length), F32), shape(piece, width), shape(*down_in.shape),
            shape(length, width), *[shape(length, columns)] * 3, *[shape(columns, length)] * 2,
            *[shape(half, width)] * 2,
        ],
        scratch_shapes=[
            pltpu.VMEM((length, piece), F32),
            pltpu.VMEM((piece, columns), BF16),
            pltpu.VMEM((4, piece, width), BF16),
            pltpu.VMEM((2, half, width), BF16),
            pltpu.VMEM((2, half, width), BF16),
            pltpu.VMEM((2, piece, width), BF16),
            dma((10,)), dma((10,)), dma((5,)), dma((4,)), dma((5,)), dma((5,)),
        ],
        compiler_params=pltpu.CompilerParams(collective_id=2, has_side_effects=True, vmem_limit_bytes=62 * 2**20),
        cost_estimate=cost(3 * length * length * columns + 2 * length * columns * width, 10 * length * width, heads * length * length // 2),
    )(tokens, cot, token_all, weight, cot_one, down, down_in, key_bias, proj, vectors)


def sum_rows(ref, at, columns, value, first):
    total = jnp.sum(value, axis=0, keepdims=True)

    @pl.when(first)
    def _():
        ref[at : at + 1, columns] = total

    @pl.when(jnp.logical_not(first))
    def _():
        ref[at : at + 1, columns] += total


def plane_kernel(
    normed, cot_own, one_up, one_low, two_up, two_low, cot_three, fc, down, middle, vectors,
    grad_middle, low_all, sums, hidden_sums, active, hidden_grad, normed_all, cot_all, terms, grad_down, grad_fc,
    mate_in, summed, got, down_share, fc_mate, fc_summed,
    normed_buf, cot_buf, sum_ref, joined, passed, arrived, load, local, send, receive, level_send, level_receive, fc_send, fc_receive,
):
    piece, width = normed.shape
    half = piece // 2
    inner = fc.shape[1]
    length = normed_all.shape[0]
    tile = min(512, inner)
    last = inner // tile - 1
    one, two = neighbours()
    scatter = LevelScatter(grad_down, mate_in, summed, got, level_send, level_receive)
    fc_scatter = LevelScatter(grad_fc, fc_mate, fc_summed, None, fc_send, fc_receive)
    for device in (one, two):
        greet("seq", device)
    pl.semaphore_wait(pltpu.get_barrier_semaphore(), 2 + scatter.greet())

    rows = lambda k, start=0, size=piece: pl.ds(k * piece + start, size)
    first, second = pl.ds(0, half), pl.ds(half, half)

    def copy(index, source, target, device):
        return remote(source, target, send.at[index], receive.at[index], "seq", device)

    normed_first = (copy(0, normed.at[first], normed_buf.at[2], one), copy(1, normed.at[second], normed_buf.at[5], two))
    normed_across = (copy(2, normed_buf.at[2], normed_buf.at[6], two), copy(3, normed_buf.at[5], normed_buf.at[7], one))
    normed_last = (copy(4, normed.at[second], normed_buf.at[3], one), copy(5, normed.at[first], normed_buf.at[4], two))
    across = (copy(6, cot_buf.at[6], passed.at[0], one), copy(7, cot_buf.at[7], passed.at[1], two))
    plain = (copy(8, cot_buf.at[2], arrived.at[0, 0], one), copy(9, cot_buf.at[5], arrived.at[1, 1], two))
    both = (copy(10, joined.at[0], arrived.at[0, 1], one), copy(11, joined.at[1], arrived.at[1, 0], two))
    low_near = (
        copy(12, low_all.at[rows(0)], low_all.at[rows(1)], one),
        copy(13, low_all.at[rows(0)], low_all.at[rows(2)], two),
    )
    low_three = (
        copy(14, low_all.at[rows(1, 0, half)], low_all.at[rows(3, 0, half)], two),
        copy(15, low_all.at[rows(2, half, half)], low_all.at[rows(3, half, half)], one),
    )

    sources = (
        cot_own.at[first], cot_own.at[second], one_up, one_low, two_up, two_low, cot_three.at[first], cot_three.at[second]
    )
    loads = [pltpu.make_async_copy(source, cot_buf.at[i], load.at[i]) for i, source in enumerate(sources)]
    own = [
        pltpu.make_async_copy(normed.at[part], normed_buf.at[i], load.at[8 + i]) for i, part in enumerate((first, second))
    ]
    keep_to = lambda target, i: target.at[pl.ds(i * half, half)]
    keeps = [pltpu.make_async_copy(normed_buf.at[i], keep_to(normed_all, i), local.at[i]) for i in range(8)]
    keeps_cot = [pltpu.make_async_copy(cot_buf.at[i], keep_to(cot_all, i), local.at[8 + i]) for i in range(8)]

    def start(*items):
        for item in items:
            item.start()

    def received(*items):
        for item in items:
            item.wait_recv()

    start(*normed_first, *own, *loads)

    place_of = lambda step: step + 2 * lax.div(step, 3) - 7 * lax.div(step, 6)

    def feed_body(fc_tile, down_tile, active_tile, hidden_tile):
        step, j = pl.program_id(0), pl.program_id(1)
        at = place_of(step)

        @pl.when((step == 0) & (j == 0))
        def _():
            for item in own:
                item.wait()
            start(*keeps[:2])
            for item in loads:
                item.wait()
            start(*keeps_cot)

        @pl.when((step == 2) & (j == 0))
        def _():
            received(*normed_first)
            start(*normed_across, keeps[2], keeps[5])

        @pl.when((step == 4) & (j == 0))
        def _():
            received(*normed_across)
            start(*normed_last, *keeps[6:])

        @pl.when((step == 6) & (j == 0))
        def _():
            received(*normed_last)
            start(*keeps[3:5])

        @pl.when((step == 7) & (j == 0))
        def _():
            start(*plain)

        weights = fc_tile[...]
        columns = pl.ds(pl.multiple_of(j * tile, tile), tile)
        hidden = nn(normed_buf[at], weights) + vectors[6:7, columns]
        grad_active = nt(cot_buf[at], down_tile[...])
        square = hidden * hidden
        bent = jnp.tanh(math.sqrt(2 / math.pi) * (hidden + 0.044715 * (square * hidden)))
        share = 0.5 * (1.0 + bent)
        active_tile[...] = (hidden * share).astype(BF16)
        slope = share + (0.5 * hidden) * (1.0 - bent * bent) * (
            math.sqrt(2 / math.pi) * (1.0 + (3 * 0.044715) * square)
        )
        grad_hidden = (grad_active * slope).astype(BF16)
        hidden_tile[...] = grad_hidden
        sum_rows(hidden_sums, 0, columns, grad_hidden.astype(F32), step == 0)
        term = nt(grad_hidden, weights)

        @pl.when(j == 0)
        def _():
            sum_ref[...] = term

        @pl.when(j > 0)
        def _():
            sum_ref[...] += term

        @pl.when((j == last) & (step == 0))
        def _():
            for item in keeps_cot:
                item.wait()

        @pl.when(j == last)
        def _():
            cot_buf[at] = sum_ref[...].astype(BF16)

        @pl.when((j == last) & (step == 5))
        def _():
            start(*across)

    pltpu.emit_pipeline(
        feed_body,
        grid=(8, inner // tile),
        in_specs=[
            pl.BlockSpec((width, tile), lambda s, j: (0, j)),
            pl.BlockSpec((tile, width), lambda s, j: (j, 0)),
        ],
        out_specs=[pl.BlockSpec((half, tile), lambda s, j: (place_of(s), j))] * 2,
    )(fc, down, active, hidden_grad)

    received(*across)
    joined[0] = (cot_buf[3].astype(F32) + passed[1].astype(F32)).astype(BF16)
    joined[1] = (cot_buf[4].astype(F32) + passed[0].astype(F32)).astype(BF16)
    start(*both)
    for item in keeps:
        item.wait()

    narrow = min(512, width)

    def down_body(active_rows, down_columns, out):
        out[...] = nn(active_rows[...], down_columns[...]).astype(BF16)

    def multiply_down(start):
        pltpu.emit_pipeline(
            down_body,
            grid=(2, width // narrow),
            in_specs=[
                pl.BlockSpec((piece, inner), lambda k, j: (start + k, 0)),
                pl.BlockSpec((inner, narrow), lambda k, j: (0, j)),
            ],
            out_specs=[pl.BlockSpec((piece, narrow), lambda k, j: (start + k, j))],
        )(active, down, terms)

    wide, tall = min(1024, width), min(1024, inner)

    def outer_body(left, right, out):
        out[...] = tn(left[...], right[...]).astype(BF16)

    def outer(left, right, out, shape):
        pltpu.emit_pipeline(
            outer_body,
            grid=(out.shape[0] // shape[0], out.shape[1] // shape[1]),
            in_specs=[
                pl.BlockSpec((length, shape[0]), lambda i, j: (0, i)),
                pl.BlockSpec((length, shape[1]), lambda i, j: (0, j)),
            ],
            out_specs=[pl.BlockSpec(shape, lambda i, j: (i, j))],
        )(left, right, out)

    outer(active, cot_all, grad_down, (tall, wide))
    scatter.start()
    multiply_down(0)
    scatter.spread()
    received(*plain, *both)
    part = min(128, half)
    steps = half // part

    def norm_body(middle_tile, cot_tile, grad_tile, low_tile):
        i = pl.program_id(0)
        at = lax.div(i, steps)
        here = pl.ds(pl.multiple_of(lax.rem(i, steps) * part, part), part)
        upstream = (
            cot_buf[at, here, :].astype(F32) + arrived[0, at, here, :].astype(F32) + arrived[1, at, here, :].astype(F32)
        )
        unit, scale = norm_parts(middle_tile[...])
        cot = cot_tile[...].astype(F32)
        grad = cot + norm_backward(unit, scale, vectors[3:4, :], upstream)
        rounded = grad.astype(BF16)
        grad_tile[...] = grad
        low_tile[...] = rounded
        for at, item in enumerate((upstream * unit, upstream, rounded.astype(F32), cot)):
            sum_rows(sums, at, slice(None), item, i == 0)

    line = pl.BlockSpec((part, width), lambda i: (i, 0))
    pltpu.emit_pipeline(norm_body, grid=(piece // part,), in_specs=[line] * 2, out_specs=[line] * 2)(
        middle, cot_own, grad_middle, low_all
    )
    start(*low_near)
    multiply_down(2)
    scatter.pass_on()
    outer(normed_all, hidden_grad, grad_fc, (wide, tall))
    fc_scatter.start()
    received(*low_near)
    start(*low_three)
    fc_scatter.combine()
    scatter.finish(down_share)
    scatter.close()
    for item in fc_scatter.swaps():
        item.wait_send()
    received(*low_three)
    for item in (*normed_first, *normed_across, *normed_last, *across, *plain, *both, *low_near, *low_three):
        item.wait_send()


def feed_plane(normed, cots, fc, down, middle, vectors):
    piece, width = normed.shape
    inner = fc.shape[1]
    length, half = 4 * piece, piece // 2
    anywhere = pl.BlockSpec(memory_space=pltpu.HBM)
    inside = pl.BlockSpec(memory_space=pltpu.VMEM)
    shape = lambda rows, columns, kind=BF16: jax.ShapeDtypeStruct((rows, columns), kind)
    dma = pltpu.SemaphoreType.DMA
    return pl.pallas_call(
        plane_kernel,
        in_specs=[anywhere] * 10 + [inside],
        out_specs=[anywhere, anywhere, inside, inside] + [anywhere] * 13,
        out_shape=[
            shape(piece, width, F32), shape(length, width), shape(4, width, F32), shape(1, inner, F32),
            shape(length, inner), shape(length, inner), shape(length, width), shape(length, width),
            shape(length, width), shape(inner, width), shape(width, inner),
            shape(inner // 2, width), shape(inner // 2, width), shape(inner // 2, width), shape(inner // 8, width, F32),
            shape(width // 2, inner), shape(width // 2, inner),
        ],
        scratch_shapes=[
            pltpu.VMEM((8, half, width), BF16),
            pltpu.VMEM((8, half, width), BF16),
            pltpu.VMEM((half, width), F32),
            pltpu.VMEM((2, half, width), BF16),
            pltpu.VMEM((2, half, width), BF16),
            pltpu.VMEM((2, 2, half, width), BF16),
            dma((10,)), dma((16,)), dma((16,)), dma((16,)), dma((8,)), dma((8,)), dma((4,)), dma((4,)),
        ],
        compiler_params=pltpu.CompilerParams(collective_id=1, has_side_effects=True, vmem_limit_bytes=60 * 2**20),
        cost_estimate=cost(12 * length * width * inner, 10 * length * width),
    )(normed, *cots, fc, down, middle, vectors)


def retreat_plane_kernel(
    low_all, q, k, v, k_t, lse, terms, middle, fc_summed, attended, key_bias, proj, vectors,
    grads, column_sums, block_out, grad_proj, fc_share,
    prob_ref, chance_ref, grad_ref, key_sum, value_sum, rounded, own, passed, joined, arrived,
    level_got, level_through, level_own, load, local, send, receive, level_send, level_receive, level_load,
):
    piece, width = middle.shape
    half = piece // 2
    length, columns = q.shape
    heads = columns // HEAD_DIM
    rank = lax.axis_index("seq")
    one, two = neighbours()
    scatter = LateScatter(fc_summed, level_got, level_through, level_own, level_send, level_receive, level_load)
    for device in (one, two):
        greet("seq", device)
    pl.semaphore_wait(pltpu.get_barrier_semaphore(), 2 + scatter.greet())
    up, lower = pl.ds(0, half), pl.ds(half, half)
    rows = lambda at, start=0, size=piece: pl.ds(at * piece + start, size)

    def copy(index, source, target, device):
        return remote(source, target, send.at[index], receive.at[index], "seq", device)

    across = (
        copy(0, terms.at[rows(3, 0, half)], passed.at[0], one),
        copy(1, terms.at[rows(3, half, half)], passed.at[1], two),
    )
    plain_one = copy(2, terms.at[rows(1, 0, half)], arrived.at[0, up], one)
    plain_two = copy(3, terms.at[rows(2, half, half)], arrived.at[1, lower], two)
    joined_one = copy(4, joined.at[0], arrived.at[0, lower], one)
    joined_two = copy(5, joined.at[1], arrived.at[1, up], two)
    loads = (
        pltpu.make_async_copy(terms.at[rows(1, half, half)], own.at[0], load.at[0]),
        pltpu.make_async_copy(terms.at[rows(2, 0, half)], own.at[1], load.at[1]),
    )
    for item in (*across, *loads):
        item.start()
    scatter.start()
    key_sum[...] = jnp.zeros_like(key_sum)
    value_sum[...] = jnp.zeros_like(value_sum)

    def body(low_ref, query_ref, key_ref, value_ref, key_t, lse_ref, query_out):
        at, head = pl.program_id(0), pl.program_id(1)
        true = flip(at, rank)
        here = pl.ds(pl.multiple_of(head * HEAD_DIM, HEAD_DIM), HEAD_DIM)

        @pl.when(head == 0)
        def _():
            grad_ref[...] = nt(low_ref[...], proj[...]).astype(BF16)

        @pl.when((at == 1) & (head == 2))
        def _():
            for item in (*across,):
                item.wait_recv()
            for item in loads:
                item.wait()
            joined[0] = (own[0].astype(F32) + passed[1].astype(F32)).astype(BF16)
            joined[1] = (own[1].astype(F32) + passed[0].astype(F32)).astype(BF16)
            for item in (plain_one, plain_two, joined_one, joined_two):
                item.start()

        @pl.when((at == 1) & (head == 3))
        def _():
            scatter.pass_on()

        query, grad, base = query_ref[...], grad_ref[:, here], lse_ref[0]

        def measure(scores, rel):
            block = rows_of(rel, piece)
            probs = jnp.exp2(scores - base)
            grad_chances = nt(value_ref[block, :], grad)
            value_sum[block, here] += nn(probs.astype(BF16), grad)
            prob_ref[block, :] = probs
            chance_ref[block, :] = grad_chances
            return jnp.sum(probs * grad_chances, axis=0, keepdims=True)

        def first(block, weighted):
            rel = flip(block, rank)
            return weighted + measure(scores_of(key_ref, key_bias, query, rel, piece, False), rel)

        last = scores_of(key_ref, key_bias, query, at, piece, True)
        weighted = lax.fori_loop(0, true, first, measure(last, at))

        def second(block, total):
            block = rows_of(flip(block, rank), piece)
            grad_scores = (prob_ref[block, :] * (chance_ref[block, :] - weighted)).astype(BF16)
            key_sum[block, here] += nn(grad_scores, query)
            return total + nn(key_t[:, block], grad_scores)

        total = lax.fori_loop(0, true + 1, second, jnp.zeros((HEAD_DIM, piece), F32))
        result = (total * FACTOR).T.astype(BF16)
        query_out[...] = result
        sum_rows(column_sums, 0, here, result.astype(F32), at == 0)

    pltpu.emit_pipeline(
        body,
        grid=(4, heads),
        in_specs=[
            pl.BlockSpec((piece, width), lambda g, h: (g, 0)),
            pl.BlockSpec((piece, HEAD_DIM), lambda g, h: (g, h)),
            pl.BlockSpec((length, HEAD_DIM), lambda g, h: (0, h)),
            pl.BlockSpec((length, HEAD_DIM), lambda g, h: (0, h)),
            pl.BlockSpec((HEAD_DIM, length), lambda g, h: (h, 0)),
            pl.BlockSpec((1, 1, piece), lambda g, h: (h, 0, g)),
        ],
        out_specs=[pl.BlockSpec((piece, HEAD_DIM), lambda g, h: (g, h))],
    )(low_all, q, k, v, k_t, lse, grads)

    rounded[:, :columns] = (key_sum[...] * FACTOR).astype(BF16)
    values = value_sum[...].astype(BF16)
    rounded[:, columns:] = values
    column_sums[1:2, :] = jnp.sum(values.astype(F32), axis=0, keepdims=True)
    keep = pltpu.make_async_copy(rounded, grads.at[:, pl.ds(columns, 2 * columns)], local.at[0])
    keep.start()
    tile = min(512, width)

    def outer_body(left, right, out):
        out[...] = tn(left[...], right[...]).astype(BF16)

    pltpu.emit_pipeline(
        outer_body,
        grid=(width // tile,),
        in_specs=[
            pl.BlockSpec((length, columns), lambda i: (0, 0)),
            pl.BlockSpec((length, tile), lambda i: (0, i)),
        ],
        out_specs=[pl.BlockSpec((columns, tile), lambda i: (0, i))],
    )(attended, low_all, grad_proj)
    for item in (plain_one, plain_two, joined_one, joined_two):
        item.wait_recv()
    part = min(128, piece)

    def out_body(middle_tile, term_tile, out):
        here = pl.ds(pl.multiple_of(pl.program_id(0) * part, part), part)
        total = term_tile[...].astype(F32) + arrived[0, here, :].astype(F32) + arrived[1, here, :].astype(F32)
        out[...] = (middle_tile[...] + (total + vectors[5:6, :])).astype(BF16)

    line = pl.BlockSpec((part, width), lambda i: (i, 0))
    pltpu.emit_pipeline(out_body, grid=(piece // part,), in_specs=[line] * 2, out_specs=[line])(middle, terms, block_out)
    scatter.finish(fc_share)
    scatter.close()
    keep.wait()
    for item in (*across, plain_one, plain_two, joined_one, joined_two):
        item.wait_send()


def retreat_plane(low_all, q, k, v, k_t, lse, terms, middle, fc_summed, attended, key_bias, proj, vectors):
    piece, width = middle.shape
    length, columns = q.shape
    half, inner = piece // 2, fc_summed.shape[1]
    anywhere = pl.BlockSpec(memory_space=pltpu.HBM)
    inside = pl.BlockSpec(memory_space=pltpu.VMEM)
    dma = pltpu.SemaphoreType.DMA
    return pl.pallas_call(
        retreat_plane_kernel,
        in_specs=[anywhere] * 10 + [inside] * 3,
        out_specs=[anywhere, inside, anywhere, anywhere, inside],
        out_shape=[
            jax.ShapeDtypeStruct((length, 3 * columns), BF16),
            jax.ShapeDtypeStruct((2, columns), F32),
            jax.ShapeDtypeStruct((piece, width), BF16),
            jax.ShapeDtypeStruct((columns, width), BF16),
            jax.ShapeDtypeStruct((width // 8, inner), BF16),
        ],
        scratch_shapes=[
            pltpu.VMEM((length, piece), F32),
            pltpu.VMEM((length, piece), F32),
            pltpu.VMEM((piece, columns), BF16),
            pltpu.VMEM((length, columns), F32),
            pltpu.VMEM((length, columns), F32),
            pltpu.VMEM((length, 2 * columns), BF16),
            pltpu.VMEM((2, half, width), BF16),
            pltpu.VMEM((2, half, width), BF16),
            pltpu.VMEM((2, half, width), BF16),
            pltpu.VMEM((2, piece, width), BF16),
            pltpu.VMEM((width // 2, inner), BF16),
            pltpu.VMEM((width // 8, inner), BF16),
            pltpu.VMEM((width // 8, inner), BF16),
            dma((2,)), dma((1,)), dma((6,)), dma((6,)), dma((8,)), dma((8,)), dma((2,)),
        ],
        compiler_params=pltpu.CompilerParams(collective_id=3, has_side_effects=True, vmem_limit_bytes=62 * 2**20),
        cost_estimate=cost(8 * length * length * columns + 2 * length * columns * width, 10 * length * width),
    )(low_all, q, k, v, k_t, lse, terms, middle, fc_summed, attended, key_bias, proj, vectors)


def closing_kernel(
    grads_in, weight_in, normed_one, tokens, grad_middle, vectors, sums_two, hidden_sums, qv_sums, fc_share,
    tokens_grad, qkv_out, fc_out, small_out,
    terms, passed, joined, arrived, qkv_in, fc_in, mine, small_in, small_rows, small_got,
    grad_qkv, mate_in, summed, got, qkv_share, grads, weight,
    send, receive, level_send, level_receive, small_send, small_receive, load,
):
    pieces = [[ref.at[i] for ref in (grad_qkv, mate_in, summed, got, qkv_share)] for i in range(2)]
    piece, width = tokens.shape
    half = piece // 2
    columns = grads.shape[1]
    farthest, others_in = pl.ds(3 * piece, piece), pl.ds(0, 3 * piece)
    early = (
        pltpu.make_async_copy(weight_in, weight, load.at[3]),
        pltpu.make_async_copy(grads_in.at[farthest], grads.at[farthest], load.at[4]),
    )
    later = pltpu.make_async_copy(grads_in.at[others_in], grads.at[others_in], load.at[5])
    for item in (*early, later):
        item.start()
    heads = columns // (3 * HEAD_DIM)
    me, place = lax.axis_index("seq"), lax.axis_index("dp")
    one, two = neighbours()
    three = 3 - me
    plane = (one, two, three)
    others = [lax.rem(place + i, 8) for i in range(1, 8)]
    for device in plane:
        greet("seq", device)
    for device in others:
        greet("dp", device)
    pl.semaphore_wait(pltpu.get_barrier_semaphore(), 10)
    scatters = [
        NearScatter(*refs[:4], level_send.at[i], level_receive.at[i]) for i, refs in enumerate(pieces)
    ]
    shares = [refs[4] for refs in pieces]
    up, lower = pl.ds(0, half), pl.ds(half, half)

    def copy(index, source, target, device):
        return remote(source, target, send.at[index], receive.at[index], "seq", device)

    across = (copy(0, terms.at[3, up], passed.at[0], one), copy(1, terms.at[3, lower], passed.at[1], two))
    plain_one = copy(2, terms.at[1, up], arrived.at[0, up], one)
    plain_two = copy(3, terms.at[2, lower], arrived.at[1, lower], two)
    joined_one = copy(4, joined.at[0], arrived.at[0, lower], one)
    joined_two = copy(5, joined.at[1], arrived.at[1, up], two)
    fine = qkv_in.shape[2]
    rows_for = lambda ref, device: ref.at[pl.ds(device * fine, fine)]
    fc_copies = [copy(6 + i, rows_for(fc_share, device), fc_in.at[i], device) for i, device in enumerate(plane)]
    qkv_copies = [
        [copy(15 + 3 * part + i, rows_for(share, device), qkv_in.at[part, i], device) for i, device in enumerate(plane)]
        for part, share in enumerate(shares)
    ]
    small_copies = [copy(9 + i, mine, small_in.at[i], device) for i, device in enumerate(plane)]
    fc_own = pltpu.make_async_copy(rows_for(fc_share, me), fc_in.at[3], load.at[0])
    qkv_own = [
        pltpu.make_async_copy(rows_for(share, me), qkv_in.at[part, 3], load.at[1 + part])
        for part, share in enumerate(shares)
    ]
    row_copies = [
        remote(small_rows.at[device], small_got.at[i], small_send.at[i], small_receive.at[i], "dp", device)
        for i, device in enumerate(others)
    ]

    def back_term(at):
        for start in range(0, width, width // 2):
            columns_here = slice(start, start + width // 2)
            term = nt(grads[at * piece : (at + 1) * piece, :], weight[columns_here, :])
            terms[at, :, columns_here] = term.astype(BF16)

    tile = min(512, width)
    narrow = columns // 2

    def outer(part):
        def body(left):
            here = pl.ds(pl.multiple_of(pl.program_id(0) * tile, tile), tile)
            grad_qkv[part, here, :] = tn(left[...], grads[:, part * narrow : (part + 1) * narrow]).astype(BF16)

        pltpu.emit_pipeline(
            body,
            grid=(width // tile,),
            in_specs=[pl.BlockSpec((normed_one.shape[0], tile), lambda i: (0, i))],
        )(normed_one)

    for item in early:
        item.wait()
    back_term(3)
    for item in across:
        item.start()
    later.wait()
    back_term(1)
    plain_one.start()
    outer(0)
    scatters[0].start()
    back_term(2)
    plain_two.start()
    scatters[0].spread()
    outer(1)
    scatters[1].start()
    for item in across:
        item.wait_recv()
    joined[0] = (terms[1, half:].astype(F32) + passed[1].astype(F32)).astype(BF16)
    joined[1] = (terms[2, :half].astype(F32) + passed[0].astype(F32)).astype(BF16)
    joined_one.start()
    joined_two.start()
    scatters[1].spread()
    scatters[0].pass_on()
    fc_own.start()
    back_term(0)
    mine[...] = jnp.zeros_like(mine)
    mine[2:6, :] = sums_two[...]
    for head in range(heads):
        at = (head * 2 + lax.rem(me, 2)) * 2 + lax.div(me, 2)
        here = pl.ds(pl.multiple_of(at * HEAD_DIM, HEAD_DIM), HEAD_DIM)
        for part in range(2):
            mine[6 + part : 7 + part, here] = qv_sums[part : part + 1, head * HEAD_DIM : (head + 1) * HEAD_DIM]
    scatters[1].pass_on()

    scatters[0].finish(shares[0])
    for item in (plain_one, plain_two, joined_one, joined_two):
        item.wait_recv()
    for item in fc_copies:
        item.start()
    part = min(128, piece)

    def norm_body(token_tile, middle_tile, out):
        i = pl.program_id(0)
        here = pl.ds(pl.multiple_of(i * part, part), part)
        upstream = terms[0, here, :].astype(F32) + arrived[0, here, :].astype(F32) + arrived[1, here, :].astype(F32)
        unit, scale = norm_parts(token_tile[...].astype(F32))
        out[...] = middle_tile[...] + norm_backward(unit, scale, vectors[0:1, :], upstream)
        for at, item in enumerate((upstream * unit, upstream)):
            sum_rows(mine, at, slice(None), item, i == 0)

    line = pl.BlockSpec((part, width), lambda i: (i, 0))
    pltpu.emit_pipeline(norm_body, grid=(piece // part,), in_specs=[line] * 2, out_specs=[line])(
        tokens, grad_middle, tokens_grad
    )
    for item in small_copies:
        item.start()
    scatters[1].finish(shares[1])
    for part in range(2):
        for item in qkv_copies[part]:
            item.start()
        qkv_own[part].start()
    for item in small_copies:
        item.wait_recv()
    mine_total = mine[...] + small_in[0] + small_in[1] + small_in[2]
    small_rows[...] = jnp.zeros_like(small_rows)
    share, wide = width // 8, 2 * width // 8
    for d in range(8):
        small_rows[d, 0:6, 0:share] = mine_total[0:6, d * share : (d + 1) * share]
        row, at = 6 + d // 4, (d % 4) * wide
        small_rows[d, 6:7, :] = mine_total[row : row + 1, at : at + wide]
        inner = hidden_sums.shape[1] // 8
        small_rows[d, 7:8, 0:inner] = hidden_sums[:, d * inner : (d + 1) * inner]
    for item in row_copies:
        item.start()
    sources = (*plane, me)
    fc_own.wait()
    for item in fc_copies:
        item.wait_recv()
    block = fc_in.shape[2] // 8
    for i, source in enumerate(sources):
        for d in range(8):
            target = pl.ds(pl.multiple_of((d * 4 + source) * block, block), block)
            fc_out[:, target] = fc_in[i, :, d * block : (d + 1) * block].astype(F32)
    for part in range(2):
        qkv_own[part].wait()
        for item in qkv_copies[part]:
            item.wait_recv()
    for i, source in enumerate(sources):
        for part in range(3):
            for head in range(heads):
                at = part * HEADS + (head * 2 + lax.rem(source, 2)) * 2 + lax.div(source, 2)
                target = pl.ds(pl.multiple_of(at * HEAD_DIM, HEAD_DIM), HEAD_DIM)
                start = (part * heads + head) * HEAD_DIM
                which, start = start // narrow, start % narrow
                qkv_out[:, target] = qkv_in[which, i, :, start : start + HEAD_DIM].astype(F32)
    for item in row_copies:
        item.wait_recv()
    total = small_rows[place]
    for i in range(7):
        total = total + small_got[i]
    small_out[...] = total
    for item in (*across, plain_one, plain_two, joined_one, joined_two, *fc_copies, *small_copies, *row_copies):
        item.wait_send()
    for part in range(2):
        scatters[part].close()
        for item in qkv_copies[part]:
            item.wait_send()


def closing(grads, weight, normed_one, tokens, grad_middle, vectors, sums_two, hidden_sums, qv_sums, fc_share):
    piece, width = tokens.shape
    columns, half = grads.shape[1], piece // 2
    fine = fc_share.shape[0] // 4
    wide = 2 * width // 8
    anywhere = pl.BlockSpec(memory_space=pltpu.HBM)
    inside = pl.BlockSpec(memory_space=pltpu.VMEM)
    shape = lambda rows, columns, kind=BF16: jax.ShapeDtypeStruct((rows, columns), kind)
    dma = pltpu.SemaphoreType.DMA
    return pl.pallas_call(
        closing_kernel,
        in_specs=[anywhere] * 5 + [inside] * 4 + [anywhere],
        out_specs=[anywhere, inside, inside, inside],
        out_shape=[
            shape(piece, width, F32), shape(fine, 4 * columns, F32), shape(fine, 4 * fc_share.shape[1], F32),
            shape(8, wide, F32),
        ],
        scratch_shapes=[
            pltpu.VMEM((4, piece, width), BF16),
            pltpu.VMEM((2, half, width), BF16),
            pltpu.VMEM((2, half, width), BF16),
            pltpu.VMEM((2, piece, width), BF16),
            pltpu.VMEM((2, 4, fine, columns // 2), BF16),
            pltpu.VMEM((4, fine, fc_share.shape[1]), BF16),
            pltpu.VMEM((8, width), F32),
            pltpu.VMEM((3, 8, width), F32),
            pltpu.VMEM((8, 8, wide), F32),
            pltpu.VMEM((7, 8, wide), F32),
            *[
                pltpu.VMEM((2, count, columns // 2), BF16)
                for count in (width, width // 2, width // 2, width // 2, width // 8)
            ],
            pltpu.VMEM(grads.shape, BF16),
            pltpu.VMEM(weight.shape, BF16),
            dma((21,)), dma((21,)), dma((2, 8)), dma((2, 8)), dma((7,)), dma((7,)), dma((6,)),
        ],
        compiler_params=pltpu.CompilerParams(collective_id=4, has_side_effects=True, vmem_limit_bytes=60 * 2**20),
        cost_estimate=cost(16 * piece * width * columns, 10 * piece * width),
    )(grads, weight, normed_one, tokens, grad_middle, vectors, sums_two, hidden_sums, qv_sums, fc_share)


def after(value, *others):
    return lax.optimization_barrier((value, *others))[0]


def shift(value, axis, distance):
    count = lax.axis_size(axis)
    return lax.ppermute(value, axis, [(i, i ^ distance) for i in range(count)])


def gather_blocks(value, axis="seq"):
    return [value] + [shift(value, axis, k) for k in range(1, lax.axis_size(axis))]


def scatter_blocks(blocks, axis="seq"):
    return [blocks[0]] + [shift(blocks[k], axis, k) for k in range(1, lax.axis_size(axis))]


def gather_plane(value):
    if lax.axis_size("seq") != 4:
        return gather_blocks(value)
    half = value.shape[0] // 2
    one, two = shift(value, "seq", 1), shift(value, "seq", 2)
    three = jnp.concatenate([shift(one[:half], "seq", 2), shift(two[half:], "seq", 1)], axis=0)
    return [value, one, two, three]


def scatter_plane(blocks):
    if lax.axis_size("seq") != 4:
        return scatter_blocks(blocks)
    half = blocks[0].shape[0] // 2
    up, low = shift(blocks[3][:half], "seq", 1), shift(blocks[3][half:], "seq", 2)
    one = shift(blocks[1][:half], "seq", 1)
    two = shift(blocks[2][half:], "seq", 2)
    one_low = (blocks[1][half:].astype(F32) + low.astype(F32)).astype(BF16)
    two_up = (blocks[2][:half].astype(F32) + up.astype(F32)).astype(BF16)
    return [blocks[0], (one, shift(one_low, "seq", 1)), (shift(two_up, "seq", 2), two)]


def by_rank(blocks, rank):
    bit = 1
    while bit < len(blocks):
        odd = (rank & bit) != 0
        blocks = [jnp.where(odd, blocks[k ^ bit], blocks[k]) for k in range(len(blocks))]
        bit *= 2
    return blocks


def pick(pieces, at):
    return lax.dynamic_index_in_dim(pieces, at, axis=0, keepdims=False)


def exchange(pieces, rank):
    return scatter_blocks([pick(pieces, rank ^ k) for k in range(pieces.shape[0])])


def small_scatter(pieces, dp_rank, seq_rank):
    total = 0.0
    sent = [lax.dynamic_index_in_dim(pieces, seq_rank ^ k, axis=1, keepdims=False) for k in range(pieces.shape[1])]
    for part in scatter_blocks(sent):
        total = total + part
    sent = [pick(total, dp_rank ^ k) for k in range(pieces.shape[0])]
    total = 0.0
    for part in scatter_blocks(sent, "dp"):
        total = total + part
    return total


def swap_pairs(dp_count, seq_count, sub):
    pairs = []
    for d in range(dp_count):
        for s in range(seq_count):
            source = ((d // sub) * sub + s % sub) * seq_count + (s // sub) * sub + d % sub
            pairs.append((source, d * seq_count + s))
    return pairs


def gather_dp(value):
    return lax.all_gather(value, "dp", axis=0, tiled=True)


def scatter_dp(value):
    return lax.psum_scatter(value, "dp", scatter_dimension=0, tiled=True)


def shards(
    tokens,
    cotangent,
    lengths,
    key_mask,
    attn_gain,
    attn_shift,
    qkv_weight,
    qv_bias,
    proj_weight,
    proj_bias,
    mlp_gain,
    mlp_shift,
    fc_weight,
    fc_bias,
    down_weight,
    down_bias,
):
    _, piece, width = tokens.shape
    dp_count, seq_count = lax.axis_size("dp"), lax.axis_size("seq")
    dp_rank, seq_rank = lax.axis_index("dp"), lax.axis_index("seq")
    own_heads = HEADS // seq_count
    own_width = own_heads * HEAD_DIM
    rows = qkv_weight.shape[0]
    sub = HEAD_DIM // proj_weight.shape[0]
    high = seq_count // sub
    block = down_weight.shape[0]
    rank = jnp.reshape(seq_rank, (1,)).astype(jnp.int32)
    swap = swap_pairs(dp_count, seq_count, sub)
    order = list(range(seq_count - 1, -1, -1))
    if seq_count == 4:
        order = [3, 1, 2, 0]

    in_plane = seq_count == 4 and dp_count == 8
    tokens_own, cot_own = tokens[0], cotangent[0]

    positions = seq_rank * piece + jnp.arange(piece, dtype=jnp.int32)
    own_flags = ((key_mask[0] == 1) & (positions < lengths[0])).astype(BF16)
    length = piece * seq_count
    shared = None
    if in_plane:
        six = jnp.stack([attn_gain, attn_shift, proj_bias, mlp_gain, mlp_shift, down_bias])
        odd = (seq_rank & 1) != 0
        six = jnp.concatenate([jnp.where(odd, 0, six), jnp.where(odd, six, 0)], axis=1)
        small, start = 0, 0
        for item in (six, qv_bias, fc_bias, own_flags):
            item = item.reshape(-1, 128)
            small = small + jnp.pad(item, ((start, 16 - start - item.shape[0]), (0, 0)))
            start += item.shape[0]
        token_all, qkv_full, fc_rows, cot_one, cot_two, down_full, proj_full, vectors, key_bias = opening(
            tokens_own, cot_own, qkv_weight, fc_weight, small, down_weight, proj_weight, dp_count
        )
        fc_full = gather_dp(fc_rows)
    else:
        small = (attn_gain, attn_shift, qv_bias, proj_bias, mlp_gain, mlp_shift, fc_bias, down_bias)
        sizes = [item.shape[0] for item in small]
        packed = jnp.concatenate(small + (own_flags,))
        blocks = gather_blocks(packed)
        flags = jnp.concatenate([item[-piece:] for item in blocks])
        key_bias = jnp.where(flags > 0, 0.0, NEG).astype(F32)[:, None]
        packed = jnp.stack(by_rank([item[:-piece] for item in blocks], seq_rank))
        packed = jnp.stack(by_rank(gather_blocks(packed, "dp"), dp_rank)).astype(F32)
        parts, start = [], 0
        for size in sizes:
            parts.append(packed[:, :, start : start + size])
            start += size
        whole = [part.reshape(1, -1) for part in parts]
        gain_one, shift_one, qv_full, proj_shift, gain_two, shift_two, _, down_shift = whole
        fc_shift = lax.dynamic_index_in_dim(parts[6], seq_rank, axis=1, keepdims=False).reshape(1, -1)
        rank_low, rank_high = seq_rank % sub, seq_rank // sub
        qv_own = qv_full.reshape(2, own_heads, sub, high, HEAD_DIM)
        qv_own = lax.dynamic_index_in_dim(qv_own, rank_low, axis=2, keepdims=False)
        qv_own = lax.dynamic_index_in_dim(qv_own, rank_high, axis=2, keepdims=False).reshape(1, -1)
        qv_own = jnp.pad(qv_own, ((0, 0), (0, width - 2 * own_width)))
        vectors = jnp.concatenate([gain_one, shift_one, jnp.zeros((5, width), F32), qv_own], axis=0)
        qkv_pieces = (
            qkv_weight.reshape(rows, 3, own_heads, sub, high, HEAD_DIM)
            .transpose(4, 3, 0, 1, 2, 5)
            .reshape(seq_count, rows, 3 * own_width)
        )
        fc_pieces = (
            fc_weight.reshape(rows, dp_count, seq_count, block)
            .transpose(2, 0, 1, 3)
            .reshape(seq_count, rows, dp_count * block)
        )
        qkv_full = gather_dp(jnp.concatenate(by_rank(exchange(qkv_pieces, seq_rank), seq_rank), axis=0))
        proj_full = gather_dp(lax.ppermute(proj_weight, BOTH, swap))
        down_full = gather_dp(down_weight)
        fc_full = gather_dp(jnp.concatenate(by_rank(exchange(fc_pieces, seq_rank), seq_rank), axis=0))
        token_blocks = gather_blocks(tokens_own)
        cot_blocks = gather_blocks(after(cot_own, token_blocks[-1]))
        for k in range(seq_count):
            shared = project(k, token_blocks[k], 0, piece, vectors, qkv_full, length, shared)
    if in_plane:
        results = attend_plane(
            tokens_own, cot_own, token_all, qkv_full, cot_one, down_weight, down_full, key_bias, proj_full, vectors
        )
        middle, normed_two, attended, lse, cot_three, down_full = results[:6]
        normed_one, q, keys, values, keys_t, values_t, one_low, two_low = results[6:]
    else:
        normed_one, q, keys, values, keys_t, values_t = shared
        proj_terms, shared = [None] * seq_count, None
        for k in order:
            proj_terms[k], shared = attend(k, rank, q, keys, values_t, key_bias, proj_full, piece, shared)
        attended, lse = shared
        middle, normed_two = rowwise(
            middle_kernel, scatter_blocks(proj_terms), [tokens_own], [proj_shift, gain_two, shift_two], [F32, BF16], 0
        )

    if in_plane:
        cots = (cot_own, cot_one, one_low, cot_two, two_low, cot_three)
        results = feed_plane(normed_two, cots, fc_full, down_full, middle, vectors)
        grad_middle, low_all, sums_two, hidden_sums, down_terms, grad_down, fc_summed = [
            results[i] for i in (0, 1, 2, 3, 8, 14, 16)
        ]
        grads, qv_sums, block_out, grad_proj, grad_fc = retreat_plane(
            low_all, q, keys, values, keys_t, lse, down_terms, middle, fc_summed, attended, key_bias, proj_full, vectors
        )
    else:
        normed_blocks = gather_blocks(normed_two)
        grad_terms, shared = [], None
        for k in range(seq_count):
            term, shared = feed(k, normed_blocks[k], cot_blocks[k], fc_full, fc_shift, down_full, seq_count, shared)
            grad_terms.append(term)
        active, grad_hidden, normed_all, cot_all = shared
        grad_middle, grad_mid_low, *sums_two = rowwise(
            middle_back_kernel, scatter_blocks(grad_terms), [middle, cot_own], [gain_two], [F32, BF16], 4
        )
        down_terms = [
            nn(active[k * piece : (k + 1) * piece], down_full).astype(BF16) for k in range(seq_count)
        ]
        low_blocks = gather_blocks(grad_mid_low)
        grad_down = scatter_dp(tn(active, cot_all).astype(BF16))
        grad_fc = scatter_dp(tn(normed_all, grad_hidden).astype(BF16))
        hidden_sums = jnp.sum(grad_hidden.astype(F32), axis=0)
        block_out = rowwise(out_kernel, scatter_blocks(down_terms), [middle], [down_shift], [BF16], 0)[0]
        sums, shared = None, None
        for k in range(seq_count):
            sums, shared = retreat(
                k, rank, low_blocks[k], proj_full, q, lse, keys, values, keys_t, key_bias, sums, shared,
                k == seq_count - 1,
            )
        grad_q, low_all = shared
        grads = jnp.concatenate([grad_q, sums[0], sums[1]], axis=1)
        qv_sums = jnp.stack([jnp.sum(item.astype(F32), axis=0) for item in (grad_q, sums[1])])
        grad_proj = tn(attended, low_all).astype(BF16)
    grad_proj = lax.ppermute(scatter_dp(grad_proj), BOTH, swap).astype(F32)
    share = attn_gain.shape[0]
    if in_plane:
        tokens_grad, grad_qkv_weight, grad_fc, smalls = closing(
            grads, qkv_full, normed_one, tokens_own, grad_middle, vectors, sums_two, hidden_sums, qv_sums, grad_fc
        )[:4]
        own = lambda row, size: lax.dynamic_slice_in_dim(smalls[row], seq_rank * size, size)
        late = jnp.concatenate([own(0, share), own(1, share), own(6, 2 * share)])
        early = jnp.concatenate([own(row, share) for row in range(2, 6)] + [smalls[7, :block]])
    else:
        back_terms = [None] * seq_count
        for k in order:
            back_terms[k] = back(k, grads, qkv_full, piece)
        tokens_grad, *sums_one = rowwise(
            tokens_back_kernel, scatter_blocks(back_terms), [tokens_own, grad_middle], [gain_one], [F32], 2
        )

        blocks = exchange(grad_fc.reshape(seq_count, rows, dp_count * block), seq_rank)
        if block % 128 == 0:
            fc_places = lambda s: [(0, d, d * seq_count + s) for d in range(dp_count)]
            grad_fc = lay_out(rank, [[item] for item in blocks], fc_weight.shape[1], (fc_places, block))
        else:
            blocks = [item.reshape(rows, dp_count, block) for item in by_rank(blocks, seq_rank)]
            grad_fc = jnp.stack(blocks, axis=2).reshape(fc_weight.shape).astype(F32)
        grad_qkv = scatter_dp(tn(normed_one, grads).astype(BF16))
        blocks = [[item] for item in exchange(grad_qkv.reshape(seq_count, rows, 3 * own_width), seq_rank)]
        qkv_places = lambda s: [
            (0, part * own_heads + head, part * HEADS + (head * sub + s % sub) * high + s // sub)
            for part in range(3)
            for head in range(own_heads)
        ]
        grad_qkv_weight = lay_out(rank, blocks, qkv_weight.shape[1], (qkv_places, HEAD_DIM))

        def spread(vector):
            return vector.reshape(dp_count, seq_count, -1)

        here = (jnp.arange(seq_count) == seq_rank).astype(F32)
        hidden_sums = hidden_sums.reshape(dp_count, 1, -1) * here[None, :, None]
        early = jnp.concatenate([spread(item) for item in sums_two] + [hidden_sums], axis=2)
        early = small_scatter(early, dp_rank, seq_rank)
        here = (jnp.arange(sub) == rank_low)[:, None] & (jnp.arange(high) == rank_high)[None, :]
        qv_sums = qv_sums.reshape(2, own_heads, 1, 1, HEAD_DIM) * here.astype(F32)[None, None, :, :, None]
        late = jnp.concatenate([spread(item) for item in sums_one] + [spread(qv_sums)], axis=2)
        late = small_scatter(late, dp_rank, seq_rank)
    return (
        block_out[None],
        tokens_grad[None],
        late[:share],
        late[share : 2 * share],
        grad_qkv_weight,
        late[2 * share :],
        grad_proj,
        early[2 * share : 3 * share],
        early[:share],
        early[share : 2 * share],
        grad_fc,
        early[4 * share :],
        grad_down.astype(F32),
        early[3 * share : 4 * share],
    )


def solution(mesh):
    in_specs = (
        P("dp", "seq", None),
        P("dp", "seq", None),
        P("dp"),
        P("dp", "seq"),
        P(BOTH),
        P(BOTH),
        P(BOTH, None),
        P(BOTH),
        P(BOTH, None),
        P(BOTH),
        P(BOTH),
        P(BOTH),
        P(BOTH, None),
        P(BOTH),
        P(BOTH, None),
        P(BOTH),
    )
    out_specs = (
        P("dp", "seq", None),
        P("dp", "seq", None),
        P(BOTH),
        P(BOTH),
        P(BOTH, None),
        P(BOTH),
        P(BOTH, None),
        P(BOTH),
        P(BOTH),
        P(BOTH),
        P(BOTH, None),
        P(BOTH),
        P(BOTH, None),
        P(BOTH),
    )
    return jax.shard_map(shards, mesh=mesh, in_specs=in_specs, out_specs=out_specs, check_vma=False)
```

```python
import functools
import math

import jax
import jax.numpy as jnp
from jax import lax
from jax.experimental import pallas as pl
from jax.experimental.pallas import tpu as pltpu
from jax.sharding import PartitionSpec as P

HEADS = 16
HEAD_DIM = 128
EPS = 1e-05
NEG = -1e30
FACTOR = HEAD_DIM ** (-0.5)
LOG2E = math.log2(math.e)
F32 = jnp.float32
BF16 = jnp.bfloat16
BOTH = ("dp", "seq")
MESH = pl.DeviceIdType.MESH


def nn(left, right):
    return lax.dot_general(left, right, (((1,), (0,)), ((), ())), preferred_element_type=F32)


def nt(left, right):
    return lax.dot_general(left, right, (((1,), (1,)), ((), ())), preferred_element_type=F32)


def tn(left, right):
    return lax.dot_general(left, right, (((0,), (0,)), ((), ())), preferred_element_type=F32)


def params(limit_mib=56):
    return pltpu.CompilerParams(dimension_semantics=("arbitrary",), vmem_limit_bytes=limit_mib * 2**20)


def cost(flops, moved, exps=0):
    return pl.CostEstimate(flops=int(flops), bytes_accessed=int(moved), transcendentals=int(exps))


def call_on_block(kernel, grid, inputs, fresh, shared, previous, scratch, estimate, rank=None, limit_mib=62):
    arrays = [item for item, _ in inputs]
    specs = [spec for _, spec in inputs]
    aliases = {}
    lead = 0 if rank is None else 1
    if previous is not None:
        for at, item in enumerate(previous):
            aliases[lead + len(arrays)] = len(fresh) + at
            arrays.append(item)
            specs.append(pl.BlockSpec(memory_space=pl.ANY))
    count = len(inputs)
    skipped = 0 if previous is None else len(previous)

    def body(*refs):
        refs = list(refs)
        kernel(*refs[: lead + count], *refs[lead + count + skipped :])

    out_specs = [spec for _, spec in fresh] + [spec for _, spec in shared]
    out_shape = [shape for shape, _ in fresh] + [shape for shape, _ in shared]
    if rank is None:
        results = pl.pallas_call(
            body, grid=grid, in_specs=specs, out_specs=out_specs, out_shape=out_shape, scratch_shapes=scratch,
            input_output_aliases=aliases, compiler_params=params(limit_mib), cost_estimate=estimate,
        )(*arrays)
    else:
        results = pl.pallas_call(
            body,
            grid_spec=pltpu.PrefetchScalarGridSpec(
                num_scalar_prefetch=1, grid=grid, in_specs=specs, out_specs=out_specs, scratch_shapes=scratch
            ),
            out_shape=out_shape, input_output_aliases=aliases, compiler_params=params(limit_mib), cost_estimate=estimate,
        )(rank, *arrays)
    return results[: len(fresh)], results[len(fresh) :]


def norm_parts(values):
    average = jnp.mean(values, axis=-1, keepdims=True)
    centred = values - average
    scale = lax.rsqrt(jnp.mean(centred * centred, axis=-1, keepdims=True) + EPS)
    return centred * scale, scale


def norm_backward(normed, scale, gain, upstream):
    weighted = upstream * gain
    return scale * (
        weighted
        - jnp.mean(weighted, axis=-1, keepdims=True)
        - normed * jnp.mean(weighted * normed, axis=-1, keepdims=True)
    )


def project_kernel(x, vectors, wq, wk, wv, normed, q, k, v, k_t, v_t):
    columns = wq.shape[1]
    rows = (norm_parts(x[...].astype(F32))[0] * vectors[0:1, :] + vectors[1:2, :]).astype(BF16)
    normed[...] = rows
    q[...] = (nn(rows, wq[...]) + vectors[7:8, :columns]).astype(BF16)
    keys = nn(rows, wk[...])
    k[...] = keys.astype(BF16)
    k_t[...] = keys.T.astype(BF16)
    values = nn(rows, wv[...]) + vectors[7:8, columns : 2 * columns]
    v[...] = values.astype(BF16)
    v_t[...] = values.T.astype(BF16)


def project(at, x, first, rows_here, vectors, weight, count, previous):
    width, columns = x.shape[1], weight.shape[1] // 3
    tile = min(256, rows_here)
    steps = rows_here // tile
    whole = lambda shape: pl.BlockSpec(shape, lambda i: (0, 0))
    rows = lambda n: pl.BlockSpec((tile, n), lambda i: (at * steps + i, 0))
    turned = pl.BlockSpec((columns, tile), lambda i: (0, at * steps + i))
    inputs = [
        (x, pl.BlockSpec((tile, width), lambda i: (first * steps + i, 0))),
        (vectors, whole(vectors.shape)),
        *[(weight, pl.BlockSpec((width, columns), lambda i, part=part: (0, part))) for part in range(3)],
    ]
    shape = lambda *dims: jax.ShapeDtypeStruct(dims, BF16)
    shared = [(shape(count, width), rows(width))] + [(shape(count, columns), rows(columns))] * 3
    shared += [(shape(columns, count), turned)] * 2
    return call_on_block(
        project_kernel, (steps,), inputs, [], shared, previous, [],
        cost(6 * rows_here * width * columns, 4 * rows_here * width + 6 * width * columns + 10 * rows_here * columns),
    )[1]


def rows_of(block, piece):
    return pl.ds(pl.multiple_of(block * piece, piece), piece)


def scores_of(key_ref, bias_ref, query, rel, piece, diagonal):
    rows = rows_of(rel, piece)
    scores = nt(key_ref[rows, :], query) * (FACTOR * LOG2E)
    key_bias = bias_ref[rows, :]
    if not diagonal:
        return scores + key_bias
    key_at = lax.broadcasted_iota(jnp.int32, scores.shape, 0)
    query_at = lax.broadcasted_iota(jnp.int32, scores.shape, 1)
    allowed = ((key_at < query_at) & (key_bias > -1.0)) | (key_at == query_at)
    return jnp.where(allowed, scores, NEG)


def attend_kernel(at, rank_ref, query_ref, key_ref, value_t, bias_ref, proj_ref, part_ref, attended, lse_ref, score_ref, sum_ref):
    piece = query_ref.shape[0]
    rank = rank_ref[0]
    head = pl.program_id(0)
    true = lax.bitwise_xor(at, rank)
    query = query_ref[...]

    def first(block, top):
        scores = scores_of(key_ref, bias_ref, query, lax.bitwise_xor(block, rank), piece, False)
        score_ref[rows_of(block, piece), :] = scores
        return jnp.maximum(top, jnp.max(scores, axis=0, keepdims=True))

    last = scores_of(key_ref, bias_ref, query, at, piece, True)
    top = lax.fori_loop(0, true, first, jnp.max(last, axis=0, keepdims=True))

    def weigh(scores, rel):
        weights = jnp.exp2(scores - top)
        return jnp.sum(weights, axis=0, keepdims=True), nn(value_t[:, rows_of(rel, piece)], weights.astype(BF16))

    def second(block, carry):
        total, out = carry
        more, part = weigh(score_ref[rows_of(block, piece), :], lax.bitwise_xor(block, rank))
        return total + more, out + part

    total, out = lax.fori_loop(0, true, second, weigh(last, at))
    result = (out / total).T.astype(BF16)
    attended[...] = result
    lse_ref[0] = top + jnp.log2(total)
    term = nn(result, proj_ref[...])

    @pl.when(head == 0)
    def _():
        sum_ref[...] = term

    @pl.when(head > 0)
    def _():
        sum_ref[...] += term

    @pl.when(head == pl.num_programs(0) - 1)
    def _():
        part_ref[...] = sum_ref[...].astype(BF16)


def attend(at, rank, q, k, v_t, key_bias, proj, piece, previous):
    length, columns = q.shape
    heads, width = columns // HEAD_DIM, proj.shape[1]
    inputs = [
        (q, pl.BlockSpec((piece, HEAD_DIM), lambda h, r: (at, h))),
        (k, pl.BlockSpec((length, HEAD_DIM), lambda h, r: (0, h))),
        (v_t, pl.BlockSpec((HEAD_DIM, length), lambda h, r: (h, 0))),
        (key_bias, pl.BlockSpec((length, 1), lambda h, r: (0, 0))),
        (proj, pl.BlockSpec((HEAD_DIM, width), lambda h, r: (h, 0))),
    ]
    fresh = [(jax.ShapeDtypeStruct((piece, width), BF16), pl.BlockSpec((piece, width), lambda h, r: (0, 0)))]
    shared = [
        (jax.ShapeDtypeStruct((length, columns), BF16), pl.BlockSpec((piece, HEAD_DIM), lambda h, r: (at, h))),
        (jax.ShapeDtypeStruct((heads, 1, length), F32), pl.BlockSpec((1, 1, piece), lambda h, r: (h, 0, at))),
    ]
    scratch = [pltpu.VMEM((length, piece), F32), pltpu.VMEM((piece, width), F32)]
    (part,), shared = call_on_block(
        functools.partial(attend_kernel, at), (heads,), inputs, fresh, shared, previous, scratch,
        cost(
            2 * length * piece * columns * 1.3 + 2 * piece * columns * width, 6 * length * columns + 2 * width * columns,
            heads * length * piece * 0.6,
        ), rank,
    )
    return part, shared


def feed_kernel(normed, cot, fc, bias, down, part, active_out, hidden_out, normed_out, cot_out, sum_ref):
    step = pl.program_id(0)
    weights = fc[...]
    hidden = nn(normed[...], weights) + bias[...]
    grad_active = nt(cot[...], down[...])
    inner = math.sqrt(2 / math.pi) * (hidden + 0.044715 * (hidden * hidden * hidden))
    bent = jnp.tanh(inner)
    half = 0.5 * (1.0 + bent)
    active_out[...] = (hidden * half).astype(BF16)
    slope = half + (0.5 * hidden) * (1.0 - bent * bent) * (
        math.sqrt(2 / math.pi) * (1.0 + (3 * 0.044715) * (hidden * hidden))
    )
    grad_hidden = (grad_active * slope).astype(BF16)
    hidden_out[...] = grad_hidden
    term = nt(grad_hidden, weights)

    @pl.when(step == 0)
    def _():
        sum_ref[...] = term
        normed_out[...] = normed[...]
        cot_out[...] = cot[...]

    @pl.when(step > 0)
    def _():
        sum_ref[...] += term

    @pl.when(step == pl.num_programs(0) - 1)
    def _():
        part[...] = sum_ref[...].astype(BF16)


def feed(at, normed, cot, fc, bias, down, count, previous):
    piece, width = normed.shape
    inner = fc.shape[1]
    tile = min(512, inner)
    length = piece * count
    rows = pl.BlockSpec((piece, width), lambda j: (0, 0))
    inputs = [
        (normed, rows),
        (cot, rows),
        (fc, pl.BlockSpec((width, tile), lambda j: (0, j))),
        (bias, pl.BlockSpec((1, tile), lambda j: (0, j))),
        (down, pl.BlockSpec((tile, width), lambda j: (j, 0))),
    ]
    shape = lambda n: jax.ShapeDtypeStruct((length, n), BF16)
    columns = pl.BlockSpec((piece, tile), lambda j: (at, j))
    here = pl.BlockSpec((piece, width), lambda j: (at, 0))
    fresh = [(jax.ShapeDtypeStruct((piece, width), BF16), rows)]
    shared = [(shape(inner), columns), (shape(inner), columns), (shape(width), here), (shape(width), here)]
    (part,), shared = call_on_block(
        feed_kernel, (inner // tile,), inputs, fresh, shared, previous, [pltpu.VMEM((piece, width), F32)],
        cost(6 * piece * width * inner, 4 * width * inner + 10 * piece * width + 4 * piece * inner, piece * inner),
    )
    return part, shared


def retreat_kernel(
    at, first_call, last_call, rank_ref, low_ref, proj_ref, query_ref, lse_ref, key_ref, value_ref, key_t, bias_ref, *rest
):
    rest = list(rest)
    key_in, value_in = (None, None) if first_call else (rest.pop(0), rest.pop(0))
    key_out, value_out, query_out, low_out, prob_ref, chance_ref, key_sum, value_sum = rest
    piece = query_ref.shape[0]
    rank = rank_ref[0]
    true = lax.bitwise_xor(at, rank)

    @pl.when(pl.program_id(0) == 0)
    def _():
        low_out[...] = low_ref[...]

    if first_call:
        key_sum[...] = jnp.zeros_like(key_sum)
        value_sum[...] = jnp.zeros_like(value_sum)
    else:
        key_sum[...] = key_in[...]
        value_sum[...] = value_in[...]
    query, lse = query_ref[...], lse_ref[0]
    grad = nt(low_ref[...], proj_ref[...]).astype(BF16)

    def measure(scores, rel):
        rows = rows_of(rel, piece)
        probs = jnp.exp2(scores - lse)
        grad_chances = nt(value_ref[rows, :], grad)
        value_sum[rows, :] += nn(probs.astype(BF16), grad)
        prob_ref[rows, :] = probs
        chance_ref[rows, :] = grad_chances
        return jnp.sum(probs * grad_chances, axis=0, keepdims=True)

    def first(block, weighted):
        rel = lax.bitwise_xor(block, rank)
        return weighted + measure(scores_of(key_ref, bias_ref, query, rel, piece, False), rel)

    last = scores_of(key_ref, bias_ref, query, at, piece, True)
    weighted = lax.fori_loop(0, true, first, measure(last, at))

    def second(block, total):
        rows = rows_of(lax.bitwise_xor(block, rank), piece)
        grad_scores = (prob_ref[rows, :] * (chance_ref[rows, :] - weighted)).astype(BF16)
        key_sum[rows, :] += nn(grad_scores, query)
        return total + nn(key_t[:, rows], grad_scores)

    total = lax.fori_loop(0, true + 1, second, jnp.zeros((HEAD_DIM, piece), F32))
    query_out[...] = (total * FACTOR).T.astype(BF16)
    if last_call:
        key_out[...] = (key_sum[...] * FACTOR).astype(BF16)
        value_out[...] = value_sum[...].astype(BF16)
    else:
        key_out[...] = key_sum[...]
        value_out[...] = value_sum[...]


def retreat(at, rank, low, proj, q, lse, k, v, k_t, key_bias, sums, previous, last_call):
    length, columns = q.shape
    piece, width = low.shape
    heads = columns // HEAD_DIM
    tall = pl.BlockSpec((length, HEAD_DIM), lambda h, r: (0, h))
    part = pl.BlockSpec((piece, HEAD_DIM), lambda h, r: (at, h))
    inputs = [
        (low, pl.BlockSpec((piece, width), lambda h, r: (0, 0))),
        (proj, pl.BlockSpec((HEAD_DIM, width), lambda h, r: (h, 0))),
        (q, part),
        (lse, pl.BlockSpec((1, 1, piece), lambda h, r: (h, 0, at))),
        (k, tall),
        (v, tall),
        (k_t, pl.BlockSpec((HEAD_DIM, length), lambda h, r: (h, 0))),
        (key_bias, pl.BlockSpec((length, 1), lambda h, r: (0, 0))),
    ]
    if sums is not None:
        inputs += [(item, tall) for item in sums]
    kind = BF16 if last_call else F32
    fresh = [(jax.ShapeDtypeStruct((length, columns), kind), tall)] * 2
    shared = [
        (jax.ShapeDtypeStruct((length, columns), BF16), part),
        (jax.ShapeDtypeStruct((length, width), BF16), pl.BlockSpec((piece, width), lambda h, r: (at, 0))),
    ]
    scratch = [pltpu.VMEM((length, piece), F32)] * 2 + [pltpu.VMEM((length, HEAD_DIM), F32)] * 2
    return call_on_block(
        functools.partial(retreat_kernel, at, sums is None, last_call), (heads,), inputs, fresh, shared, previous,
        scratch,
        cost(
            5 * 1.3 * length * piece * columns + 2 * piece * columns * width, 20 * length * columns,
            heads * length * piece * 0.6,
        ), rank,
    )


def back_kernel(grads, weight, out):
    out[...] = nt(grads[...], weight[...]).astype(BF16)


def back(at, grads, weight, piece):
    columns, width = grads.shape[1], weight.shape[0]
    tile = min(512, width)
    return pl.pallas_call(
        back_kernel,
        grid=(width // tile,),
        in_specs=[
            pl.BlockSpec((piece, columns), lambda j: (at, 0)),
            pl.BlockSpec((tile, columns), lambda j: (j, 0)),
        ],
        out_specs=pl.BlockSpec((piece, tile), lambda j: (0, j)),
        out_shape=jax.ShapeDtypeStruct((piece, width), BF16),
        compiler_params=params(),
        cost_estimate=cost(2 * piece * width * columns, 2 * width * columns + 2 * piece * (columns + width)),
    )(grads, weight)


def part_specs(parts, tile, steps, width):
    arrays, specs = [], []
    for part in parts:
        if isinstance(part, tuple):
            middle = steps // 2
            arrays += list(part)
            specs.append(pl.BlockSpec((tile, width), lambda i: (jnp.minimum(i, middle - 1), 0)))
            specs.append(pl.BlockSpec((tile, width), lambda i: (jnp.maximum(i - middle, 0), 0)))
        else:
            arrays.append(part)
            specs.append(pl.BlockSpec((tile, width), lambda i: (i, 0)))
    return arrays, specs


def add_parts(kinds, refs):
    total = None
    upper = pl.program_id(0) < pl.num_programs(0) // 2
    for kind in kinds:
        if kind:
            high, low = refs.pop(0)[...], refs.pop(0)[...]
            term = jnp.where(upper, high.astype(F32), low.astype(F32))
        else:
            term = refs.pop(0)[...].astype(F32)
        total = term if total is None else total + term
    return total


def rowwise(kernel, parts, rows, vectors, outputs, sums):
    count, width = rows[0].shape
    tile = min(128, count // 2)
    steps = count // tile
    arrays, specs = part_specs(parts, tile, steps, width)
    kinds = [isinstance(part, tuple) for part in parts]
    specs += [pl.BlockSpec((tile, width), lambda i: (i, 0))] * len(rows)
    specs += [pl.BlockSpec((1, width), lambda i: (0, 0))] * len(vectors)

    def body(*refs):
        refs = list(refs)
        total = add_parts(kinds, refs)
        tiles = [refs.pop(0)[...] for _ in rows]
        given = [refs.pop(0)[...] for _ in vectors]
        results = kernel(total, tiles, given)
        for result, _ in zip(results, outputs):
            refs.pop(0)[...] = result
        for result in results[len(outputs) :]:
            ref = refs.pop(0)
            column = jnp.sum(result, axis=0, keepdims=True)

            @pl.when(pl.program_id(0) == 0)
            def _():
                ref[...] = column

            @pl.when(pl.program_id(0) > 0)
            def _():
                ref[...] += column

    return pl.pallas_call(
        body,
        grid=(steps,),
        in_specs=specs,
        out_specs=[pl.BlockSpec((tile, width), lambda i: (i, 0))] * len(outputs)
        + [pl.BlockSpec((1, width), lambda i: (0, 0))] * sums,
        out_shape=[jax.ShapeDtypeStruct((count, width), kind) for kind in outputs]
        + [jax.ShapeDtypeStruct((1, width), F32)] * sums,
        compiler_params=params(),
        cost_estimate=cost(20 * count * width, count * width * (2 * len(arrays) + 4 * len(rows) + 4 * len(outputs))),
    )(*arrays, *rows, *vectors)


def middle_kernel(total, rows, vectors):
    (tokens,), (bias, gain, shift_) = rows, vectors
    middle = tokens.astype(F32) + (total + bias)
    return middle, (norm_parts(middle)[0] * gain + shift_).astype(BF16)


def out_kernel(total, rows, vectors):
    return (((rows[0] + (total + vectors[0])).astype(BF16)),)


def middle_back_kernel(total, rows, vectors):
    (middle, cot), (gain,) = rows, vectors
    normed, scale = norm_parts(middle)
    cot = cot.astype(F32)
    grad = cot + norm_backward(normed, scale, gain, total)
    low = grad.astype(BF16)
    return grad, low, total * normed, total, low.astype(F32), cot


def tokens_back_kernel(total, rows, vectors):
    (tokens, grad_middle), (gain,) = rows, vectors
    normed, scale = norm_parts(tokens.astype(F32))
    return grad_middle + norm_backward(normed, scale, gain, total), total * normed, total


def lay_out(rank, blocks, width, places):
    rows = blocks[0][0].shape[0]
    count, each = len(blocks), len(blocks[0])
    unit = places[1]

    def body(rank_ref, *refs):
        out = refs[-1]
        for k in range(count):
            source = lax.bitwise_xor(k, rank_ref[0])
            for array, column, target in places[0](source):
                out[:, pl.ds(pl.multiple_of(target * unit, unit), unit)] = refs[k * each + array][
                    :, column * unit : (column + 1) * unit
                ].astype(F32)

    arrays = [item for block in blocks for item in block]
    return pl.pallas_call(
        body,
        grid_spec=pltpu.PrefetchScalarGridSpec(
            num_scalar_prefetch=1,
            grid=(1,),
            in_specs=[pl.BlockSpec(item.shape, lambda i, r: (0, 0)) for item in arrays],
            out_specs=pl.BlockSpec((rows, width), lambda i, r: (0, 0)),
        ),
        out_shape=jax.ShapeDtypeStruct((rows, width), F32),
        compiler_params=params(),
        cost_estimate=cost(rows * width, 6 * rows * width),
    )(rank, *arrays)


def neighbours():
    rank = lax.axis_index("seq")
    return rank + 1 - 2 * lax.rem(rank, 2), rank + 2 - 4 * lax.rem(lax.div(rank, 2), 2)


def remote(source, target, send, receive, axis, device):
    return pltpu.make_async_remote_copy(
        src_ref=source, dst_ref=target, send_sem=send, recv_sem=receive, device_id={axis: device}, device_id_type=MESH
    )


def greet(axis, device):
    pl.semaphore_signal(pltpu.get_barrier_semaphore(), inc=1, device_id={axis: device}, device_id_type=MESH)


def flip(first, second):
    low = lax.rem(first + second, 2)
    high = lax.rem(lax.div(first, 2) + lax.div(second, 2), 2)
    return 2 * high + low


class LevelScatter:
    def __init__(self, source, mate_in, summed, got, send, receive):
        self.source, self.mate_in, self.summed, self.got = source, mate_in, summed, got
        self.send, self.receive = send, receive
        self.rows = mate_in.shape[0] // 4
        self.place = lax.axis_index("dp")
        self.level, self.core = lax.div(self.place, 2), lax.rem(self.place, 2)
        self.mate = self.place + 1 - 2 * self.core

    def greet(self):
        greet("dp", self.mate)
        count = jnp.int32(1)
        for step in (1, 2):
            up, down = self.level + step <= 3, self.level >= step
            pl.when(up)(lambda step=step: greet("dp", self.place + 2 * step))
            pl.when(down)(lambda step=step: greet("dp", self.place - 2 * step))
            count = count + up.astype(jnp.int32) + down.astype(jnp.int32)
        return count

    def block(self, ref, at):
        return ref.at[pl.ds(at * self.rows, self.rows)]

    def swaps(self):
        return [
            remote(
                self.block(self.source, 2 * at + 1 - self.core), self.block(self.mate_in, at),
                self.send.at[at], self.receive.at[at], "dp", self.mate,
            )
            for at in range(4)
        ]

    def start(self):
        for item in self.swaps():
            item.start()

    def add(self, first, second, out, grid, first_at, second_at, out_at):
        def body(left, right, total):
            total[...] = (left[...].astype(F32) + right[...].astype(F32)).astype(total.dtype)

        spec = lambda at: pl.BlockSpec((self.rows, first.shape[1]), lambda i: (at(i), 0))
        pltpu.emit_pipeline(
            body, grid=(grid,), in_specs=[spec(first_at), spec(second_at)], out_specs=[spec(out_at)]
        )(first, second, out)

    def hop(self, at, slot, index, steps):
        return remote(
            self.block(self.summed, at), self.block(self.got, slot), self.send.at[4 + index], self.receive.at[4 + slot],
            "dp", self.place + 2 * steps,
        )

    def hops(self):
        level = self.level
        return [
            (level == 0, self.hop(3, 3, 0, 1)),
            (level == 3, self.hop(0, 3, 0, -1)),
            (level == 0, self.hop(2, 2, 1, 2)),
            (level == 3, self.hop(1, 2, 1, -2)),
            (level <= 2, self.hop(lax.rem(level + 1, 4), 0, 2, 1)),
            (level >= 1, self.hop(lax.rem(level + 3, 4), 1, 3, -1)),
        ]

    def first_hops(self):
        hops, inner = self.hops(), (self.level == 1) | (self.level == 2)
        return hops[:2] + [(inner, hops[4][1]), (inner, hops[5][1])]

    def later_hops(self):
        hops = self.hops()
        return hops[2:4] + [(self.level == 0, hops[4][1]), (self.level == 3, hops[5][1])]

    def passes(self):
        return [(self.level == 1, self.hop(3, 2, 1, 2)), (self.level == 2, self.hop(0, 2, 1, -2))]

    def combine(self):
        for item in self.swaps():
            item.wait_recv()
        self.add(
            self.source, self.mate_in, self.summed, 4, lambda i: 2 * i + self.core, lambda i: i, lambda i: i
        )

    def spread(self):
        self.combine()
        for condition, copy in self.first_hops():
            pl.when(condition)(lambda copy=copy: copy.start())

    def arrive(self, slot):
        here = self.block(self.got, slot)
        remote(here, here, self.send.at[0], self.receive.at[4 + slot], "dp", self.mate).wait_recv()

    def pass_on(self):
        for level, at in ((1, 3), (2, 0)):

            @pl.when(self.level == level)
            def _(at=at):
                self.arrive(3)
                self.add(self.summed, self.got, self.summed, 1, lambda i: at, lambda i: 3, lambda i: at)

        for condition, copy in self.passes() + self.later_hops():
            pl.when(condition)(lambda copy=copy: copy.start())

    def finish(self, out):
        level = self.level
        pl.when(level >= 1)(lambda: self.arrive(0))
        pl.when(level <= 2)(lambda: self.arrive(1))
        self.arrive(2)
        rows = min(64, self.rows)

        def body(own, mate, below, above, far, total):
            value = own[...].astype(F32) + mate[...].astype(F32) + far[...].astype(F32)
            below_term, above_term = below[...].astype(F32), above[...].astype(F32)
            value = value + jnp.where(level >= 1, below_term, 0.0) + jnp.where(level <= 2, above_term, 0.0)
            total[...] = value.astype(total.dtype)

        steps = self.rows // rows
        spec = lambda at: pl.BlockSpec((rows, out.shape[1]), lambda i: (at * steps + i, 0))
        pltpu.emit_pipeline(
            body,
            grid=(steps,),
            in_specs=[spec(self.place), spec(level), spec(0), spec(1), spec(2)],
            out_specs=[spec(0)],
        )(self.source, self.mate_in, self.got, self.got, self.got, out)

    def close(self):
        for item in self.swaps():
            item.wait_send()
        for condition, copy in self.hops() + self.passes():
            pl.when(condition)(lambda copy=copy: copy.wait_send())


class LateScatter(LevelScatter):
    def __init__(self, summed, got, through, own, send, receive, load):
        self.summed, self.got, self.through, self.own = summed, got, through, own
        self.send, self.receive, self.load = send, receive, load
        self.rows = own.shape[0]
        self.place = lax.axis_index("dp")
        self.level, self.core = lax.div(self.place, 2), lax.rem(self.place, 2)
        self.mate = self.place + 1 - 2 * self.core

    def loads(self):
        passed_on = 3 * lax.rem(self.level, 2)
        return (
            pltpu.make_async_copy(self.block(self.summed, self.level), self.own, self.load.at[0]),
            pltpu.make_async_copy(self.block(self.summed, passed_on), self.through, self.load.at[1]),
        )

    def passes(self):
        target = self.block(self.got, 2)
        send, receive = self.send.at[4 + 1], self.receive.at[4 + 2]
        return [
            (self.level == 1, remote(self.through, target, send, receive, "dp", self.place + 4)),
            (self.level == 2, remote(self.through, target, send, receive, "dp", self.place - 4)),
        ]

    def start(self):
        for condition, copy in self.first_hops():
            pl.when(condition)(lambda copy=copy: copy.start())
        for item in self.loads():
            item.start()

    def part(self, slot):
        return self.got[slot * self.rows : (slot + 1) * self.rows, :].astype(F32)

    def pass_on(self):
        for item in self.loads():
            item.wait()

        @pl.when((self.level == 1) | (self.level == 2))
        def _():
            self.arrive(3)
            self.through[...] = (self.through[...].astype(F32) + self.part(3)).astype(BF16)

        for condition, copy in self.passes() + self.later_hops():
            pl.when(condition)(lambda copy=copy: copy.start())

    def finish(self, out):
        level = self.level
        pl.when(level >= 1)(lambda: self.arrive(0))
        pl.when(level <= 2)(lambda: self.arrive(1))
        self.arrive(2)
        value = self.own[...].astype(F32) + self.part(2)
        value = value + jnp.where(level >= 1, self.part(0), 0.0)
        value = value + jnp.where(level <= 2, self.part(1), 0.0)
        out[...] = value.astype(BF16)

    def close(self):
        for condition, copy in self.hops() + self.passes():
            pl.when(condition)(lambda copy=copy: copy.wait_send())


class NearScatter(LevelScatter):
    def part(self, ref, at):
        return ref[pl.ds(pl.multiple_of(at * self.rows, self.rows), self.rows), :].astype(F32)

    def spread(self):
        for item in self.swaps():
            item.wait_recv()
        for at in range(4):
            total = self.part(self.source, 2 * at + self.core) + self.part(self.mate_in, at)
            self.summed[at * self.rows : (at + 1) * self.rows, :] = total.astype(BF16)
        for condition, copy in self.first_hops():
            pl.when(condition)(lambda copy=copy: copy.start())

    def pass_on(self):
        for level, at in ((1, 3), (2, 0)):

            @pl.when(self.level == level)
            def _(at=at):
                self.arrive(3)
                total = self.part(self.summed, at) + self.part(self.got, 3)
                self.summed[at * self.rows : (at + 1) * self.rows, :] = total.astype(BF16)

        for condition, copy in self.passes() + self.later_hops():
            pl.when(condition)(lambda copy=copy: copy.start())

    def finish(self, out):
        level = self.level
        pl.when(level >= 1)(lambda: self.arrive(0))
        pl.when(level <= 2)(lambda: self.arrive(1))
        self.arrive(2)
        value = self.part(self.source, self.place) + self.part(self.mate_in, level) + self.part(self.got, 2)
        value = value + jnp.where(level >= 1, self.part(self.got, 0), 0.0)
        value = value + jnp.where(level <= 2, self.part(self.got, 1), 0.0)
        out[...] = value.astype(BF16)


class LevelGather:
    def __init__(self, own, full, send, receive, mate_send, mate_receive):
        self.own, self.full, self.send, self.receive = own, full, send, receive
        self.mate_send, self.mate_receive = mate_send, mate_receive
        self.rows = own.shape[0]
        self.place = lax.axis_index("dp")
        self.level, self.core = lax.div(self.place, 2), lax.rem(self.place, 2)
        self.mate = self.place + 1 - 2 * self.core

    greet = LevelScatter.greet

    def shard(self, level):
        return self.full.at[pl.ds((2 * level + self.core) * self.rows, self.rows)]

    def hop(self, index, steps, slot):
        return remote(
            self.own, self.shard(self.level), self.send.at[index], self.receive.at[slot], "dp", self.place + 2 * steps
        )

    def near(self):
        return [(self.level <= 2, self.hop(0, 1, 0)), (self.level >= 1, self.hop(1, -1, 1))]

    def second(self):
        inner = (self.level == 1) | (self.level == 2)
        lower, upper = self.shard(self.level - 1), self.shard(self.level + 1)
        return [
            (inner, remote(lower, lower, self.send.at[2], self.receive.at[2], "dp", self.place + 2)),
            (inner, remote(upper, upper, self.send.at[3], self.receive.at[2], "dp", self.place - 2)),
        ]

    def passes(self):
        first, last = self.shard(0), self.shard(3)
        return [
            (self.level == 2, remote(first, first, self.send.at[4], self.receive.at[3], "dp", self.place + 2)),
            (self.level == 1, remote(last, last, self.send.at[4], self.receive.at[3], "dp", self.place - 2)),
        ]

    def across(self, index, level):
        here = self.own if index == 4 else self.shard(level)
        return remote(here, self.shard(level), self.mate_send.at[index], self.mate_receive.at[index], "dp", self.mate)

    def arrivals(self, slots):
        level = self.level
        two_away = level + 2 - 4 * lax.div(level, 2)
        every = [
            (level >= 1, 0, level - 1),
            (level <= 2, 1, level + 1),
            (level >= 0, 2, two_away),
            ((level == 0) | (level == 3), 3, 3 - level),
        ]
        return [item for item in every if item[1] in slots]

    def start(self, hops):
        for condition, copy in hops:
            pl.when(condition)(lambda copy=copy: copy.start())

    def take(self, slots):
        for condition, slot, level in self.arrivals(slots):

            @pl.when(condition)
            def _(slot=slot, level=level):
                here = self.shard(level)
                remote(here, here, self.send.at[0], self.receive.at[slot], "dp", self.mate).wait_recv()
                self.across(slot, level).start()

    def finish(self, slots, hops):
        for condition, slot, level in self.arrivals(slots):
            pl.when(condition)(lambda slot=slot, level=level: self.across(slot, level).wait())
        for condition, copy in hops:
            pl.when(condition)(lambda copy=copy: copy.wait_send())


def opening_kernel(
    tokens, cot, qkv_in, fc_in, small, down_in, proj_in,
    token_all, qkv_full, fc_rows, cot_one, cot_two, down_full, proj_full, vectors, key_bias,
    qkv_weight, fc_weight, down, proj, entry, qkv_pieces, fc_pieces, token_buf, qkv_rows, small_rows, small_full, proj_rows, square, local, send, receive, up_send, up_receive, down_send, down_receive, mate_send, mate_receive,
    level_send, level_receive, level_mate_send, level_mate_receive,
):
    piece = tokens.shape[0]
    half = piece // 2
    entries = [
        pltpu.make_async_copy(source, target, entry.at[i])
        for i, (source, target) in enumerate(
            ((qkv_in, qkv_weight), (proj_in, proj), (down_in, down), (fc_in, fc_weight))
        )
    ]
    for copy in entries:
        copy.start()
    gather = LevelGather(down, down_full, level_send, level_receive, level_mate_send, level_mate_receive)
    me, place = lax.axis_index("seq"), lax.axis_index("dp")
    one, two = neighbours()
    three = 3 - me
    stages = lax.axis_size("dp") // 2
    level, core = lax.div(place, 2), lax.rem(place, 2)
    mate = place + 1 - 2 * core
    above, below = level < stages - 1, level > 0

    for device in (one, two, three):
        greet("seq", device)
    greet("dp", mate)
    pl.when(above)(lambda: greet("dp", place + 2))
    pl.when(below)(lambda: greet("dp", place - 2))
    swaps = core != lax.rem(me, 2)
    partner = {"dp": mate, "seq": one}

    @pl.when(swaps)
    def _():
        pl.semaphore_signal(pltpu.get_barrier_semaphore(), inc=1, device_id=partner, device_id_type=MESH)

    heads = qkv_pieces.shape[2] // (3 * HEAD_DIM)
    entries[0].wait()
    for rank in range(4):
        for part in range(3):
            for head in range(heads):
                source = (part * HEADS + (head * 2 + rank % 2) * 2 + rank // 2) * HEAD_DIM
                target = (part * heads + head) * HEAD_DIM
                qkv_pieces[rank, :, target : target + HEAD_DIM] = qkv_weight[:, source : source + HEAD_DIM]
    count = 4 + above.astype(jnp.int32) + below.astype(jnp.int32) + swaps.astype(jnp.int32)
    pl.semaphore_wait(pltpu.get_barrier_semaphore(), count)

    def block(ref, at, start=0, size=piece):
        return ref.at[pl.ds(at * piece + start, size)]

    def spread(pieces, target, at):
        rows = target.shape[0] // 4
        mine = target.at[pl.ds(me * rows, rows)]
        source = lambda device: pieces if pieces is small else pieces.at[device]
        copies = [
            remote(source(device), mine, send.at[at + i], receive.at[at + i], "seq", device)
            for i, device in enumerate((one, two, three))
        ]
        return copies, source(me), mine

    qkv_copies, qkv_own, qkv_mine = spread(qkv_pieces, qkv_rows, 0)
    small_copies, small_own, small_mine = spread(small, small_rows, 3)
    fc_copies, fc_own, fc_mine = spread(fc_pieces, fc_rows, 6)
    token_one = remote(tokens, block(token_all, 1), send.at[9], receive.at[9], "seq", one)
    token_two = remote(tokens, block(token_all, 2), send.at[10], receive.at[10], "seq", two)
    token_three = (
        remote(block(token_all, 1, 0, half), block(token_all, 3, 0, half), send.at[11], receive.at[11], "seq", two),
        remote(block(token_all, 2, half, half), block(token_all, 3, half, half), send.at[12], receive.at[12], "seq", one),
    )
    first_kept = [pltpu.make_async_copy(qkv_own, qkv_mine, local.at[0]), pltpu.make_async_copy(small_own, small_mine, local.at[1])]
    later_kept = [
        pltpu.make_async_copy(fc_own, fc_mine, local.at[2]),
        pltpu.make_async_copy(token_buf, block(token_all, 0), local.at[3]),
    ]
    token_load = pltpu.make_async_copy(tokens, token_buf, local.at[4])
    cot_copies = (
        remote(cot.at[pl.ds(0, half)], cot_one, send.at[13], receive.at[13], "seq", one),
        remote(cot.at[pl.ds(0, half)], cot_two, send.at[14], receive.at[14], "seq", two),
    )

    proj_copy = pltpu.make_async_remote_copy(
        src_ref=proj, dst_ref=proj_rows, send_sem=send.at[15], recv_sem=receive.at[15], device_id=partner,
        device_id_type=MESH,
    )
    chains = ((qkv_rows, qkv_full), (small_rows, small_full), (proj_rows, proj_full))

    def shard(array, at):
        rows = chains[array][0].shape[0]
        return chains[array][1].at[pl.ds((2 * at + core) * rows, rows)]

    def rising(array, step, device):
        at = level - (step - 1)
        source = chains[array][0] if step == 1 else shard(array, at)
        return remote(source, shard(array, at), up_send.at[array, step - 1], up_receive.at[array, step - 1], "dp", device)

    def falling(array, step, device):
        at = level + (step - 1)
        source = chains[array][0] if step == 1 else shard(array, at)
        return remote(source, shard(array, at), down_send.at[array, step - 1], down_receive.at[array, step - 1], "dp", device)

    def across(array, index, at):
        source = chains[array][0] if index == 0 else shard(array, at)
        return remote(source, shard(array, at), mate_send.at[array, index], mate_receive.at[array, index], "dp", mate)

    rises = lambda step: above & (level >= step - 1)
    falls = lambda step: below & (level <= stages - step)
    from_below = lambda step: level >= step
    from_above = lambda step: level + step <= stages - 1

    def relay(step):
        @pl.when(rises(step))
        def _():
            for array in (1, 0, 2):
                rising(array, step, place + 2).start()

        @pl.when(falls(step))
        def _():
            for array in (1, 0, 2):
                falling(array, step, place - 2).start()

    def take(step):
        @pl.when(from_below(step))
        def _():
            for array in (1, 0, 2):
                got = shard(array, level - step)
                remote(got, got, up_send.at[array, step - 1], up_receive.at[array, step - 1], "dp", mate).wait_recv()
                across(array, step, level - step).start()

        @pl.when(from_above(step))
        def _():
            for array in (1, 0, 2):
                got = shard(array, level + step)
                remote(got, got, down_send.at[array, step - 1], down_receive.at[array, step - 1], "dp", mate).wait_recv()
                across(array, stages - 1 + step, level + step).start()

    for copy in qkv_copies + small_copies + first_kept:
        copy.start()
    entries[1].wait()
    pl.when(swaps)(proj_copy.start)

    @pl.when(jnp.logical_not(swaps))
    def _():
        proj_rows[...] = proj[...]

    token_one.start()
    token_two.start()
    entries[2].wait()
    gather.start(gather.near())
    gather.across(4, level).start()
    down_kept = pltpu.make_async_copy(down, gather.shard(level), local.at[8])
    down_kept.start()
    token_load.start()
    entries[3].wait()
    inner = fc_pieces.shape[2] // 8
    for rank in range(4):
        for d in range(8):
            source = (d * 4 + rank) * inner
            fc_pieces[rank, :, d * inner : (d + 1) * inner] = fc_weight[:, source : source + inner]
    token_load.wait()
    for copy in qkv_copies + small_copies:
        copy.wait_recv()
    pl.when(swaps)(proj_copy.wait_recv)
    for copy in first_kept:
        copy.wait()
    relay(1)
    own_full = [pltpu.make_async_copy(chains[array][0], shard(array, level), local.at[5 + array]) for array in range(3)]
    for array in range(3):
        across(array, 0, level).start()
        own_full[array].start()
    for copy in fc_copies + later_kept:
        copy.start()
    for copy in cot_copies:
        copy.start()
    take(1)
    relay(2)
    take(2)
    relay(3)
    gather.take((0, 1))
    token_one.wait_recv()
    token_two.wait_recv()
    for copy in token_three:
        copy.start()
    take(3)
    for copy in later_kept + own_full:
        copy.wait()
    for copy in fc_copies:
        copy.wait_recv()
    for copy in qkv_copies + small_copies + fc_copies:
        copy.wait_send()
    token_one.wait_send()
    token_two.wait_send()
    for step in range(1, stages):

        @pl.when(rises(step))
        def _(step=step):
            for array in range(3):
                rising(array, step, place + 2).wait_send()

        @pl.when(falls(step))
        def _(step=step):
            for array in range(3):
                falling(array, step, place - 2).wait_send()

        @pl.when(from_below(step))
        def _(step=step):
            for array in range(3):
                across(array, step, level - step).wait()

        @pl.when(from_above(step))
        def _(step=step):
            for array in range(3):
                across(array, stages - 1 + step, level + step).wait()

    for array in range(3):
        across(array, 0, level).wait()
    for copy in token_three:
        copy.wait()
    down_kept.wait()
    pl.when(swaps)(proj_copy.wait_send)
    tile = lambda d, s: small_full[pl.ds(pl.multiple_of((d * 4 + s) * 16, 16), 16), :].astype(F32)
    vectors[...] = jnp.zeros_like(vectors)
    for d in range(8):
        for pair in range(2):
            both = tile(d, 2 * pair) + tile(d, 2 * pair + 1)
            vectors[0:6, (2 * d + pair) * 128 : (2 * d + pair + 1) * 128] = both[0:6]
        own = tile(d, me)
        for i in range(2):
            vectors[6:7, (2 * d + i) * 128 : (2 * d + i + 1) * 128] = own[7 + i : 8 + i]
        bias = tile(d, 2 * lax.rem(me, 2) + lax.div(me, 2))
        vectors[7:8, d * HEAD_DIM : (d + 1) * HEAD_DIM] = bias[6:7]
    square[...] = jnp.zeros_like(square)
    for i in range(4):
        square[4 * i : 4 * i + 4, :] = tile(place, flip(me, i))[9:13]
    turned = square[...].T
    lane = lax.broadcasted_iota(jnp.int32, turned.shape, 1)
    for i in range(16):
        flag = jnp.sum(jnp.where(lane == i, turned, 0.0), axis=1, keepdims=True)
        key_bias[i * 128 : (i + 1) * 128, :] = jnp.where(flag > 0, 0.0, NEG)
    for copy in cot_copies:
        copy.wait()
    gather.finish((0, 1), gather.near())
    gather.across(4, level).wait()


def opening(tokens, cot, qkv_weight, fc_weight, small, down, proj, dp_count):
    piece, width = tokens.shape
    steps = dp_count // 2 - 1
    anywhere = pl.BlockSpec(memory_space=pltpu.HBM)
    shape = lambda rows, columns: jax.ShapeDtypeStruct((rows, columns), BF16)
    dma = pltpu.SemaphoreType.DMA
    inside = pl.BlockSpec(memory_space=pltpu.VMEM)
    own_rows, columns, inner = qkv_weight.shape[0], qkv_weight.shape[1] // 4, fc_weight.shape[1] // 4
    rows, fine = 4 * own_rows, 4 * small.shape[0]
    return pl.pallas_call(
        opening_kernel,
        in_specs=[anywhere] * 4 + [inside] + [anywhere] * 2,
        out_specs=[anywhere] * 7 + [inside] * 2,
        out_shape=[
            shape(4 * piece, width),
            shape(rows * dp_count, columns),
            shape(rows, inner),
            shape(piece // 2, width),
            shape(piece // 2, width),
            shape(down.shape[0] * dp_count, width),
            shape(proj.shape[0] * dp_count, width),
            jax.ShapeDtypeStruct((8, width), F32),
            jax.ShapeDtypeStruct((4 * piece, 1), F32),
        ],
        scratch_shapes=[
            *[pltpu.VMEM(item.shape, BF16) for item in (qkv_weight, fc_weight, down, proj)], dma((4,)),
            pltpu.VMEM((4, own_rows, columns), BF16), pltpu.VMEM((4, own_rows, inner), BF16),
            pltpu.VMEM((piece, width), BF16),
            pltpu.VMEM((rows, columns), BF16), pltpu.VMEM((fine, 128), BF16), pltpu.VMEM((fine * dp_count, 128), BF16),
            pltpu.VMEM(proj.shape, BF16), pltpu.VMEM((128, 128), F32),
            dma((9,)), dma((16,)), dma((16,)), dma((3, steps)), dma((3, steps)), dma((3, steps)), dma((3, steps)),
            dma((3, 2 * steps + 1)), dma((3, 2 * steps + 1)), dma((5,)), dma((4,)), dma((5,)), dma((5,)),
        ],
        compiler_params=pltpu.CompilerParams(collective_id=0, has_side_effects=True, vmem_limit_bytes=62 * 2**20),
        cost_estimate=cost(0, 10 * 4 * piece * width),
    )(tokens, cot, qkv_weight, fc_weight, small, down, proj)


def attend_plane_kernel(
    tokens, cot, token_all, weight, cot_one, down, down_in, bias_in, proj_in, vectors,
    middle, normed, attended, lse, cot_three, down_full, normed_one, q, k, v, k_t, v_t, one_low, two_low,
    key_bias, proj, entry, score_ref, joint, terms, passed, joined, arrived, send, receive,
    level_send, level_receive, mate_send, mate_receive,
):
    piece, width = tokens.shape
    half = piece // 2
    entries = (
        pltpu.make_async_copy(bias_in, key_bias, entry.at[0]), pltpu.make_async_copy(proj_in, proj, entry.at[1])
    )
    for item in entries:
        item.start()
    length, columns = q.shape
    heads = columns // HEAD_DIM
    rank = lax.axis_index("seq")
    one, two = neighbours()
    gather = LevelGather(down, down_full, level_send, level_receive, mate_send, mate_receive)
    for device in (one, two):
        greet("seq", device)
    pl.semaphore_wait(pltpu.get_barrier_semaphore(), 2 + gather.greet())
    up, lower = pl.ds(0, half), pl.ds(half, half)
    gather.start(gather.second())

    def copy(index, source, target, device):
        return remote(source, target, send.at[index], receive.at[index], "seq", device)

    cot_copies = (copy(0, cot_one, cot_three.at[up], two), copy(1, two_low, cot_three.at[lower], one))
    low_copies = (copy(8, cot.at[lower], one_low, one), copy(9, cot.at[lower], two_low, two))
    across = (copy(2, terms.at[3, up], passed.at[0], one), copy(3, terms.at[3, lower], passed.at[1], two))
    plain_one = copy(4, terms.at[1, up], arrived.at[0, up], one)
    plain_two = copy(5, terms.at[2, lower], arrived.at[1, lower], two)
    joined_one = copy(6, joined.at[0], arrived.at[0, lower], one)
    joined_two = copy(7, joined.at[1], arrived.at[1, up], two)
    for item in low_copies:
        item.start()
    cot_copies[0].start()
    tile = min(256, piece)
    rows = lambda n: pl.BlockSpec((tile, n), lambda i: (i, 0))
    turned = pl.BlockSpec((columns, tile), lambda i: (0, i))
    pltpu.emit_pipeline(
        lambda x, wq, wk, wv, *out: project_kernel(x, vectors, wq, wk, wv, *out),
        grid=(length // tile,),
        in_specs=[rows(width)] + [pl.BlockSpec((width, columns), lambda i, part=part: (0, part)) for part in range(3)],
        out_specs=[rows(width), rows(columns), rows(columns), rows(columns), turned, turned],
    )(token_all, weight, weight, weight, normed_one, q, k, v, k_t, v_t)
    for item in low_copies:
        item.wait_recv()
    cot_copies[1].start()
    for item in entries:
        item.wait()

    def body(query_ref, key_ref, value_t, attended_tile, lse_tile):
        group, head = pl.program_id(0), pl.program_id(1)
        at = 3 - group
        true = flip(at, rank)
        query = query_ref[...]

        def first(block, top):
            scores = scores_of(key_ref, key_bias, query, flip(block, rank), piece, False)
            score_ref[rows_of(block, piece), :] = scores
            return jnp.maximum(top, jnp.max(scores, axis=0, keepdims=True))

        last = scores_of(key_ref, key_bias, query, at, piece, True)
        top = lax.fori_loop(0, true, first, jnp.max(last, axis=0, keepdims=True))

        def weigh(scores, rel):
            weights = jnp.exp2(scores - top)
            return jnp.sum(weights, axis=0, keepdims=True), nn(value_t[:, rows_of(rel, piece)], weights.astype(BF16))

        def second(block, carry):
            total, out = carry
            more, part = weigh(score_ref[rows_of(block, piece), :], flip(block, rank))
            return total + more, out + part

        total, out = lax.fori_loop(0, true, second, weigh(last, at))
        result = (out / total).T.astype(BF16)
        attended_tile[...] = result
        lse_tile[0] = top + jnp.log2(total)
        joint[:, pl.ds(pl.multiple_of(head * HEAD_DIM, HEAD_DIM), HEAD_DIM)] = result

        @pl.when(head == heads - 1)
        def _():
            terms[at] = nn(joint[...], proj[...]).astype(BF16)

        @pl.when((head == heads - 1) & (group == 0))
        def _():
            for item in across:
                item.start()

        @pl.when((head == heads - 1) & (group == 1))
        def _():
            plain_two.start()

        @pl.when((head == 0) & (group == 3))
        def _():
            gather.take((2,))
            gather.start(gather.passes())

        @pl.when((head == heads - 1) & (group == 2))
        def _():
            plain_one.start()
            for item in across:
                item.wait_recv()
            joined[0] = (terms[1, half:].astype(F32) + passed[1].astype(F32)).astype(BF16)
            joined[1] = (terms[2, :half].astype(F32) + passed[0].astype(F32)).astype(BF16)
            joined_one.start()
            joined_two.start()

    pltpu.emit_pipeline(
        body,
        grid=(4, heads),
        in_specs=[
            pl.BlockSpec((piece, HEAD_DIM), lambda g, h: (3 - g, h)),
            pl.BlockSpec((length, HEAD_DIM), lambda g, h: (0, h)),
            pl.BlockSpec((HEAD_DIM, length), lambda g, h: (h, 0)),
        ],
        out_specs=[
            pl.BlockSpec((piece, HEAD_DIM), lambda g, h: (3 - g, h)),
            pl.BlockSpec((1, 1, piece), lambda g, h: (h, 0, 3 - g)),
        ],
    )(q, k, v_t, attended, lse)

    for item in (plain_one, plain_two, joined_one, joined_two):
        item.wait_recv()
    part = min(128, piece)

    def norm_body(token_tile, middle_tile, normed_tile):
        here = pl.ds(pl.multiple_of(pl.program_id(0) * part, part), part)
        total = terms[0, here, :].astype(F32) + arrived[0, here, :].astype(F32) + arrived[1, here, :].astype(F32)
        values = token_tile[...].astype(F32) + (total + vectors[2:3, :])
        middle_tile[...] = values
        normed_tile[...] = (norm_parts(values)[0] * vectors[3:4, :] + vectors[4:5, :]).astype(BF16)

    line = pl.BlockSpec((part, width), lambda i: (i, 0))
    pltpu.emit_pipeline(norm_body, grid=(piece // part,), in_specs=[line], out_specs=[line] * 2)(tokens, middle, normed)
    gather.take((3,))
    gather.finish((2, 3), gather.second() + gather.passes())
    for item in cot_copies:
        item.wait()
    for item in low_copies:
        item.wait_send()
    for item in (*across, plain_one, plain_two, joined_one, joined_two):
        item.wait_send()


def attend_plane(tokens, cot, token_all, weight, cot_one, down, down_in, key_bias, proj, vectors):
    piece, width = tokens.shape
    length, columns = token_all.shape[0], proj.shape[0]
    heads, half = columns // HEAD_DIM, piece // 2
    anywhere = pl.BlockSpec(memory_space=pltpu.HBM)
    inside = pl.BlockSpec(memory_space=pltpu.VMEM)
    shape = lambda *dims: jax.ShapeDtypeStruct(dims, BF16)
    dma = pltpu.SemaphoreType.DMA
    return pl.pallas_call(
        attend_plane_kernel,
        in_specs=[anywhere] * 9 + [inside],
        out_specs=[anywhere] * 14,
        input_output_aliases={6: 5},
        out_shape=[
            jax.ShapeDtypeStruct((piece, width), F32), shape(piece, width), shape(length, columns),
            jax.ShapeDtypeStruct((heads, 1, length), F32), shape(piece, width), shape(*down_in.shape),
            shape(length, width), *[shape(length, columns)] * 3, *[shape(columns, length)] * 2,
            *[shape(half, width)] * 2,
        ],
        scratch_shapes=[
            pltpu.VMEM(key_bias.shape, F32),
            pltpu.VMEM(proj.shape, BF16),
            dma((2,)),
            pltpu.VMEM((length, piece), F32),
            pltpu.VMEM((piece, columns), BF16),
            pltpu.VMEM((4, piece, width), BF16),
            pltpu.VMEM((2, half, width), BF16),
            pltpu.VMEM((2, half, width), BF16),
            pltpu.VMEM((2, piece, width), BF16),
            dma((10,)), dma((10,)), dma((5,)), dma((4,)), dma((5,)), dma((5,)),
        ],
        compiler_params=pltpu.CompilerParams(collective_id=2, has_side_effects=True, vmem_limit_bytes=62 * 2**20),
        cost_estimate=cost(3 * length * length * columns + 2 * length * columns * width, 10 * length * width, heads * length * length // 2),
    )(tokens, cot, token_all, weight, cot_one, down, down_in, key_bias, proj, vectors)


def sum_rows(ref, at, columns, value, first):
    total = jnp.sum(value, axis=0, keepdims=True)

    @pl.when(first)
    def _():
        ref[at : at + 1, columns] = total

    @pl.when(jnp.logical_not(first))
    def _():
        ref[at : at + 1, columns] += total


def plane_kernel(
    normed, cot_own, one_up, one_low, two_up, two_low, cot_three, fc, down, middle, vectors,
    grad_middle, low_all, sums, hidden_sums, active, hidden_grad, normed_all, cot_all, terms, grad_down, grad_fc,
    mate_in, summed, got, down_share, fc_mate, fc_summed,
    normed_buf, cot_buf, sum_ref, joined, passed, arrived, load, local, send, receive, level_send, level_receive, fc_send, fc_receive,
):
    piece, width = normed.shape
    half = piece // 2
    inner = fc.shape[1]
    length = normed_all.shape[0]
    tile = min(512, inner)
    last = inner // tile - 1
    one, two = neighbours()
    scatter = LevelScatter(grad_down, mate_in, summed, got, level_send, level_receive)
    fc_scatter = LevelScatter(grad_fc, fc_mate, fc_summed, None, fc_send, fc_receive)
    for device in (one, two):
        greet("seq", device)
    pl.semaphore_wait(pltpu.get_barrier_semaphore(), 2 + scatter.greet())

    rows = lambda k, start=0, size=piece: pl.ds(k * piece + start, size)
    first, second = pl.ds(0, half), pl.ds(half, half)

    def copy(index, source, target, device):
        return remote(source, target, send.at[index], receive.at[index], "seq", device)

    normed_first = (copy(0, normed.at[first], normed_buf.at[2], one), copy(1, normed.at[second], normed_buf.at[5], two))
    normed_across = (copy(2, normed_buf.at[2], normed_buf.at[6], two), copy(3, normed_buf.at[5], normed_buf.at[7], one))
    normed_last = (copy(4, normed.at[second], normed_buf.at[3], one), copy(5, normed.at[first], normed_buf.at[4], two))
    across = (copy(6, cot_buf.at[6], passed.at[0], one), copy(7, cot_buf.at[7], passed.at[1], two))
    plain = (copy(8, cot_buf.at[2], arrived.at[0, 0], one), copy(9, cot_buf.at[5], arrived.at[1, 1], two))
    both = (copy(10, joined.at[0], arrived.at[0, 1], one), copy(11, joined.at[1], arrived.at[1, 0], two))
    low_near = (
        copy(12, low_all.at[rows(0)], low_all.at[rows(1)], one),
        copy(13, low_all.at[rows(0)], low_all.at[rows(2)], two),
    )
    low_three = (
        copy(14, low_all.at[rows(1, 0, half)], low_all.at[rows(3, 0, half)], two),
        copy(15, low_all.at[rows(2, half, half)], low_all.at[rows(3, half, half)], one),
    )

    sources = (
        cot_own.at[first], cot_own.at[second], one_up, one_low, two_up, two_low, cot_three.at[first], cot_three.at[second]
    )
    loads = [pltpu.make_async_copy(source, cot_buf.at[i], load.at[i]) for i, source in enumerate(sources)]
    own = [
        pltpu.make_async_copy(normed.at[part], normed_buf.at[i], load.at[8 + i]) for i, part in enumerate((first, second))
    ]
    keep_to = lambda target, i: target.at[pl.ds(i * half, half)]
    keeps = [pltpu.make_async_copy(normed_buf.at[i], keep_to(normed_all, i), local.at[i]) for i in range(8)]
    keeps_cot = [pltpu.make_async_copy(cot_buf.at[i], keep_to(cot_all, i), local.at[8 + i]) for i in range(8)]

    def start(*items):
        for item in items:
            item.start()

    def received(*items):
        for item in items:
            item.wait_recv()

    start(*normed_first, *own, *loads)

    place_of = lambda step: step + 2 * lax.div(step, 3) - 7 * lax.div(step, 6)

    def feed_body(fc_tile, down_tile, active_tile, hidden_tile):
        step, j = pl.program_id(0), pl.program_id(1)
        at = place_of(step)

        @pl.when((step == 0) & (j == 0))
        def _():
            for item in own:
                item.wait()
            start(*keeps[:2])
            for item in loads:
                item.wait()
            start(*keeps_cot)

        @pl.when((step == 2) & (j == 0))
        def _():
            received(*normed_first)
            start(*normed_across, keeps[2], keeps[5])

        @pl.when((step == 4) & (j == 0))
        def _():
            received(*normed_across)
            start(*normed_last, *keeps[6:])

        @pl.when((step == 6) & (j == 0))
        def _():
            received(*normed_last)
            start(*keeps[3:5])

        @pl.when((step == 7) & (j == 0))
        def _():
            start(*plain)

        weights = fc_tile[...]
        columns = pl.ds(pl.multiple_of(j * tile, tile), tile)
        hidden = nn(normed_buf[at], weights) + vectors[6:7, columns]
        grad_active = nt(cot_buf[at], down_tile[...])
        square = hidden * hidden
        bent = jnp.tanh(math.sqrt(2 / math.pi) * (hidden + 0.044715 * (square * hidden)))
        share = 0.5 * (1.0 + bent)
        active_tile[...] = (hidden * share).astype(BF16)
        slope = share + (0.5 * hidden) * (1.0 - bent * bent) * (
            math.sqrt(2 / math.pi) * (1.0 + (3 * 0.044715) * square)
        )
        grad_hidden = (grad_active * slope).astype(BF16)
        hidden_tile[...] = grad_hidden
        sum_rows(hidden_sums, 0, columns, grad_hidden.astype(F32), step == 0)
        term = nt(grad_hidden, weights)

        @pl.when(j == 0)
        def _():
            sum_ref[...] = term

        @pl.when(j > 0)
        def _():
            sum_ref[...] += term

        @pl.when((j == last) & (step == 0))
        def _():
            for item in keeps_cot:
                item.wait()

        @pl.when(j == last)
        def _():
            cot_buf[at] = sum_ref[...].astype(BF16)

        @pl.when((j == last) & (step == 5))
        def _():
            start(*across)

    pltpu.emit_pipeline(
        feed_body,
        grid=(8, inner // tile),
        in_specs=[
            pl.BlockSpec((width, tile), lambda s, j: (0, j)),
            pl.BlockSpec((tile, width), lambda s, j: (j, 0)),
        ],
        out_specs=[pl.BlockSpec((half, tile), lambda s, j: (place_of(s), j))] * 2,
    )(fc, down, active, hidden_grad)

    received(*across)
    joined[0] = (cot_buf[3].astype(F32) + passed[1].astype(F32)).astype(BF16)
    joined[1] = (cot_buf[4].astype(F32) + passed[0].astype(F32)).astype(BF16)
    start(*both)
    for item in keeps:
        item.wait()

    narrow = min(512, width)

    def down_body(active_rows, down_columns, out):
        out[...] = nn(active_rows[...], down_columns[...]).astype(BF16)

    def multiply_down(start):
        pltpu.emit_pipeline(
            down_body,
            grid=(2, width // narrow),
            in_specs=[
                pl.BlockSpec((piece, inner), lambda k, j: (start + k, 0)),
                pl.BlockSpec((inner, narrow), lambda k, j: (0, j)),
            ],
            out_specs=[pl.BlockSpec((piece, narrow), lambda k, j: (start + k, j))],
        )(active, down, terms)

    wide, tall = min(1024, width), min(1024, inner)

    def outer_body(left, right, out):
        out[...] = tn(left[...], right[...]).astype(BF16)

    def outer(left, right, out, shape):
        pltpu.emit_pipeline(
            outer_body,
            grid=(out.shape[0] // shape[0], out.shape[1] // shape[1]),
            in_specs=[
                pl.BlockSpec((length, shape[0]), lambda i, j: (0, i)),
                pl.BlockSpec((length, shape[1]), lambda i, j: (0, j)),
            ],
            out_specs=[pl.BlockSpec(shape, lambda i, j: (i, j))],
        )(left, right, out)

    outer(active, cot_all, grad_down, (tall, wide))
    scatter.start()
    multiply_down(0)
    scatter.spread()
    received(*plain, *both)
    part = min(128, half)
    steps = half // part

    def norm_body(middle_tile, cot_tile, grad_tile, low_tile):
        i = pl.program_id(0)
        at = lax.div(i, steps)
        here = pl.ds(pl.multiple_of(lax.rem(i, steps) * part, part), part)
        upstream = (
            cot_buf[at, here, :].astype(F32) + arrived[0, at, here, :].astype(F32) + arrived[1, at, here, :].astype(F32)
        )
        unit, scale = norm_parts(middle_tile[...])
        cot = cot_tile[...].astype(F32)
        grad = cot + norm_backward(unit, scale, vectors[3:4, :], upstream)
        rounded = grad.astype(BF16)
        grad_tile[...] = grad
        low_tile[...] = rounded
        for at, item in enumerate((upstream * unit, upstream, rounded.astype(F32), cot)):
            sum_rows(sums, at, slice(None), item, i == 0)

    line = pl.BlockSpec((part, width), lambda i: (i, 0))
    pltpu.emit_pipeline(norm_body, grid=(piece // part,), in_specs=[line] * 2, out_specs=[line] * 2)(
        middle, cot_own, grad_middle, low_all
    )
    start(*low_near)
    multiply_down(2)
    scatter.pass_on()
    outer(normed_all, hidden_grad, grad_fc, (wide, tall))
    fc_scatter.start()
    received(*low_near)
    start(*low_three)
    fc_scatter.combine()
    scatter.finish(down_share)
    scatter.close()
    for item in fc_scatter.swaps():
        item.wait_send()
    received(*low_three)
    for item in (*normed_first, *normed_across, *normed_last, *across, *plain, *both, *low_near, *low_three):
        item.wait_send()


def feed_plane(normed, cots, fc, down, middle, vectors):
    piece, width = normed.shape
    inner = fc.shape[1]
    length, half = 4 * piece, piece // 2
    anywhere = pl.BlockSpec(memory_space=pltpu.HBM)
    inside = pl.BlockSpec(memory_space=pltpu.VMEM)
    shape = lambda rows, columns, kind=BF16: jax.ShapeDtypeStruct((rows, columns), kind)
    dma = pltpu.SemaphoreType.DMA
    return pl.pallas_call(
        plane_kernel,
        in_specs=[anywhere] * 10 + [inside],
        out_specs=[anywhere, anywhere, inside, inside] + [anywhere] * 13,
        out_shape=[
            shape(piece, width, F32), shape(length, width), shape(4, width, F32), shape(1, inner, F32),
            shape(length, inner), shape(length, inner), shape(length, width), shape(length, width),
            shape(length, width), shape(inner, width), shape(width, inner),
            shape(inner // 2, width), shape(inner // 2, width), shape(inner // 2, width), shape(inner // 8, width, F32),
            shape(width // 2, inner), shape(width // 2, inner),
        ],
        scratch_shapes=[
            pltpu.VMEM((8, half, width), BF16),
            pltpu.VMEM((8, half, width), BF16),
            pltpu.VMEM((half, width), F32),
            pltpu.VMEM((2, half, width), BF16),
            pltpu.VMEM((2, half, width), BF16),
            pltpu.VMEM((2, 2, half, width), BF16),
            dma((10,)), dma((16,)), dma((16,)), dma((16,)), dma((8,)), dma((8,)), dma((4,)), dma((4,)),
        ],
        compiler_params=pltpu.CompilerParams(collective_id=1, has_side_effects=True, vmem_limit_bytes=60 * 2**20),
        cost_estimate=cost(12 * length * width * inner, 10 * length * width),
    )(normed, *cots, fc, down, middle, vectors)


def retreat_plane_kernel(
    low_all, q, k, v, k_t, lse, terms, middle, fc_summed, attended, bias_in, proj_in, vectors,
    grads, column_sums, block_out, grad_proj, fc_share,
    key_bias, proj, entry, prob_ref, chance_ref, grad_ref, key_sum, value_sum, rounded, own, passed, joined, arrived,
    level_got, level_through, level_own, load, local, send, receive, level_send, level_receive, level_load,
):
    piece, width = middle.shape
    half = piece // 2
    entries = (
        pltpu.make_async_copy(bias_in, key_bias, entry.at[0]), pltpu.make_async_copy(proj_in, proj, entry.at[1])
    )
    for item in entries:
        item.start()
    length, columns = q.shape
    heads = columns // HEAD_DIM
    rank = lax.axis_index("seq")
    one, two = neighbours()
    scatter = LateScatter(fc_summed, level_got, level_through, level_own, level_send, level_receive, level_load)
    for device in (one, two):
        greet("seq", device)
    pl.semaphore_wait(pltpu.get_barrier_semaphore(), 2 + scatter.greet())
    up, lower = pl.ds(0, half), pl.ds(half, half)
    rows = lambda at, start=0, size=piece: pl.ds(at * piece + start, size)

    def copy(index, source, target, device):
        return remote(source, target, send.at[index], receive.at[index], "seq", device)

    across = (
        copy(0, terms.at[rows(3, 0, half)], passed.at[0], one),
        copy(1, terms.at[rows(3, half, half)], passed.at[1], two),
    )
    plain_one = copy(2, terms.at[rows(1, 0, half)], arrived.at[0, up], one)
    plain_two = copy(3, terms.at[rows(2, half, half)], arrived.at[1, lower], two)
    joined_one = copy(4, joined.at[0], arrived.at[0, lower], one)
    joined_two = copy(5, joined.at[1], arrived.at[1, up], two)
    loads = (
        pltpu.make_async_copy(terms.at[rows(1, half, half)], own.at[0], load.at[0]),
        pltpu.make_async_copy(terms.at[rows(2, 0, half)], own.at[1], load.at[1]),
    )
    for item in (*across, *loads):
        item.start()
    scatter.start()
    key_sum[...] = jnp.zeros_like(key_sum)
    value_sum[...] = jnp.zeros_like(value_sum)
    for item in entries:
        item.wait()

    def body(low_ref, query_ref, key_ref, value_ref, key_t, lse_ref, query_out):
        at, head = pl.program_id(0), pl.program_id(1)
        true = flip(at, rank)
        here = pl.ds(pl.multiple_of(head * HEAD_DIM, HEAD_DIM), HEAD_DIM)

        @pl.when(head == 0)
        def _():
            grad_ref[...] = nt(low_ref[...], proj[...]).astype(BF16)

        @pl.when((at == 1) & (head == 2))
        def _():
            for item in (*across,):
                item.wait_recv()
            for item in loads:
                item.wait()
            joined[0] = (own[0].astype(F32) + passed[1].astype(F32)).astype(BF16)
            joined[1] = (own[1].astype(F32) + passed[0].astype(F32)).astype(BF16)
            for item in (plain_one, plain_two, joined_one, joined_two):
                item.start()

        @pl.when((at == 1) & (head == 3))
        def _():
            scatter.pass_on()

        query, grad, base = query_ref[...], grad_ref[:, here], lse_ref[0]

        def measure(scores, rel):
            block = rows_of(rel, piece)
            probs = jnp.exp2(scores - base)
            grad_chances = nt(value_ref[block, :], grad)
            value_sum[block, here] += nn(probs.astype(BF16), grad)
            prob_ref[block, :] = probs
            chance_ref[block, :] = grad_chances
            return jnp.sum(probs * grad_chances, axis=0, keepdims=True)

        def first(block, weighted):
            rel = flip(block, rank)
            return weighted + measure(scores_of(key_ref, key_bias, query, rel, piece, False), rel)

        last = scores_of(key_ref, key_bias, query, at, piece, True)
        weighted = lax.fori_loop(0, true, first, measure(last, at))

        def second(block, total):
            block = rows_of(flip(block, rank), piece)
            grad_scores = (prob_ref[block, :] * (chance_ref[block, :] - weighted)).astype(BF16)
            key_sum[block, here] += nn(grad_scores, query)
            return total + nn(key_t[:, block], grad_scores)

        total = lax.fori_loop(0, true + 1, second, jnp.zeros((HEAD_DIM, piece), F32))
        result = (total * FACTOR).T.astype(BF16)
        query_out[...] = result
        sum_rows(column_sums, 0, here, result.astype(F32), at == 0)

    pltpu.emit_pipeline(
        body,
        grid=(4, heads),
        in_specs=[
            pl.BlockSpec((piece, width), lambda g, h: (g, 0)),
            pl.BlockSpec((piece, HEAD_DIM), lambda g, h: (g, h)),
            pl.BlockSpec((length, HEAD_DIM), lambda g, h: (0, h)),
            pl.BlockSpec((length, HEAD_DIM), lambda g, h: (0, h)),
            pl.BlockSpec((HEAD_DIM, length), lambda g, h: (h, 0)),
            pl.BlockSpec((1, 1, piece), lambda g, h: (h, 0, g)),
        ],
        out_specs=[pl.BlockSpec((piece, HEAD_DIM), lambda g, h: (g, h))],
    )(low_all, q, k, v, k_t, lse, grads)

    rounded[:, :columns] = (key_sum[...] * FACTOR).astype(BF16)
    values = value_sum[...].astype(BF16)
    rounded[:, columns:] = values
    column_sums[1:2, :] = jnp.sum(values.astype(F32), axis=0, keepdims=True)
    keep = pltpu.make_async_copy(rounded, grads.at[:, pl.ds(columns, 2 * columns)], local.at[0])
    keep.start()
    tile = min(512, width)

    def outer_body(left, right, out):
        out[...] = tn(left[...], right[...]).astype(BF16)

    pltpu.emit_pipeline(
        outer_body,
        grid=(width // tile,),
        in_specs=[
            pl.BlockSpec((length, columns), lambda i: (0, 0)),
            pl.BlockSpec((length, tile), lambda i: (0, i)),
        ],
        out_specs=[pl.BlockSpec((columns, tile), lambda i: (0, i))],
    )(attended, low_all, grad_proj)
    for item in (plain_one, plain_two, joined_one, joined_two):
        item.wait_recv()
    part = min(128, piece)

    def out_body(middle_tile, term_tile, out):
        here = pl.ds(pl.multiple_of(pl.program_id(0) * part, part), part)
        total = term_tile[...].astype(F32) + arrived[0, here, :].astype(F32) + arrived[1, here, :].astype(F32)
        out[...] = (middle_tile[...] + (total + vectors[5:6, :])).astype(BF16)

    line = pl.BlockSpec((part, width), lambda i: (i, 0))
    pltpu.emit_pipeline(out_body, grid=(piece // part,), in_specs=[line] * 2, out_specs=[line])(middle, terms, block_out)
    scatter.finish(fc_share)
    scatter.close()
    keep.wait()
    for item in (*across, plain_one, plain_two, joined_one, joined_two):
        item.wait_send()


def retreat_plane(low_all, q, k, v, k_t, lse, terms, middle, fc_summed, attended, key_bias, proj, vectors):
    piece, width = middle.shape
    length, columns = q.shape
    half, inner = piece // 2, fc_summed.shape[1]
    anywhere = pl.BlockSpec(memory_space=pltpu.HBM)
    inside = pl.BlockSpec(memory_space=pltpu.VMEM)
    dma = pltpu.SemaphoreType.DMA
    return pl.pallas_call(
        retreat_plane_kernel,
        in_specs=[anywhere] * 12 + [inside],
        out_specs=[anywhere, inside, anywhere, anywhere, inside],
        out_shape=[
            jax.ShapeDtypeStruct((length, 3 * columns), BF16),
            jax.ShapeDtypeStruct((2, columns), F32),
            jax.ShapeDtypeStruct((piece, width), BF16),
            jax.ShapeDtypeStruct((columns, width), BF16),
            jax.ShapeDtypeStruct((width // 8, inner), BF16),
        ],
        scratch_shapes=[
            pltpu.VMEM(key_bias.shape, F32),
            pltpu.VMEM(proj.shape, BF16),
            dma((2,)),
            pltpu.VMEM((length, piece), F32),
            pltpu.VMEM((length, piece), F32),
            pltpu.VMEM((piece, columns), BF16),
            pltpu.VMEM((length, columns), F32),
            pltpu.VMEM((length, columns), F32),
            pltpu.VMEM((length, 2 * columns), BF16),
            pltpu.VMEM((2, half, width), BF16),
            pltpu.VMEM((2, half, width), BF16),
            pltpu.VMEM((2, half, width), BF16),
            pltpu.VMEM((2, piece, width), BF16),
            pltpu.VMEM((width // 2, inner), BF16),
            pltpu.VMEM((width // 8, inner), BF16),
            pltpu.VMEM((width // 8, inner), BF16),
            dma((2,)), dma((1,)), dma((6,)), dma((6,)), dma((8,)), dma((8,)), dma((2,)),
        ],
        compiler_params=pltpu.CompilerParams(collective_id=3, has_side_effects=True, vmem_limit_bytes=62 * 2**20),
        cost_estimate=cost(8 * length * length * columns + 2 * length * columns * width, 10 * length * width),
    )(low_all, q, k, v, k_t, lse, terms, middle, fc_summed, attended, key_bias, proj, vectors)


def closing_kernel(
    grads_in, weight_in, normed_one, tokens, grad_middle, vectors, sums_two, hidden_sums, qv_sums, fc_share,
    tokens_grad, qkv_out, fc_out, small_out,
    terms, passed, joined, arrived, qkv_in, fc_in, mine, small_in, small_rows, small_got,
    grad_qkv, mate_in, summed, got, qkv_share, grads, weight,
    send, receive, level_send, level_receive, small_send, small_receive, load,
):
    pieces = [[ref.at[i] for ref in (grad_qkv, mate_in, summed, got, qkv_share)] for i in range(2)]
    piece, width = tokens.shape
    half = piece // 2
    columns = grads.shape[1]
    farthest, others_in = pl.ds(3 * piece, piece), pl.ds(0, 3 * piece)
    early = (
        pltpu.make_async_copy(weight_in, weight, load.at[3]),
        pltpu.make_async_copy(grads_in.at[farthest], grads.at[farthest], load.at[4]),
    )
    later = pltpu.make_async_copy(grads_in.at[others_in], grads.at[others_in], load.at[5])
    for item in (*early, later):
        item.start()
    heads = columns // (3 * HEAD_DIM)
    me, place = lax.axis_index("seq"), lax.axis_index("dp")
    one, two = neighbours()
    three = 3 - me
    plane = (one, two, three)
    others = [lax.rem(place + i, 8) for i in range(1, 8)]
    for device in plane:
        greet("seq", device)
    for device in others:
        greet("dp", device)
    pl.semaphore_wait(pltpu.get_barrier_semaphore(), 10)
    scatters = [
        NearScatter(*refs[:4], level_send.at[i], level_receive.at[i]) for i, refs in enumerate(pieces)
    ]
    shares = [refs[4] for refs in pieces]
    up, lower = pl.ds(0, half), pl.ds(half, half)

    def copy(index, source, target, device):
        return remote(source, target, send.at[index], receive.at[index], "seq", device)

    across = (copy(0, terms.at[3, up], passed.at[0], one), copy(1, terms.at[3, lower], passed.at[1], two))
    plain_one = copy(2, terms.at[1, up], arrived.at[0, up], one)
    plain_two = copy(3, terms.at[2, lower], arrived.at[1, lower], two)
    joined_one = copy(4, joined.at[0], arrived.at[0, lower], one)
    joined_two = copy(5, joined.at[1], arrived.at[1, up], two)
    fine = qkv_in.shape[2]
    rows_for = lambda ref, device: ref.at[pl.ds(device * fine, fine)]
    fc_copies = [copy(6 + i, rows_for(fc_share, device), fc_in.at[i], device) for i, device in enumerate(plane)]
    qkv_copies = [
        [copy(15 + 3 * part + i, rows_for(share, device), qkv_in.at[part, i], device) for i, device in enumerate(plane)]
        for part, share in enumerate(shares)
    ]
    small_copies = [copy(9 + i, mine, small_in.at[i], device) for i, device in enumerate(plane)]
    fc_own = pltpu.make_async_copy(rows_for(fc_share, me), fc_in.at[3], load.at[0])
    qkv_own = [
        pltpu.make_async_copy(rows_for(share, me), qkv_in.at[part, 3], load.at[1 + part])
        for part, share in enumerate(shares)
    ]
    row_copies = [
        remote(small_rows.at[device], small_got.at[i], small_send.at[i], small_receive.at[i], "dp", device)
        for i, device in enumerate(others)
    ]

    def back_term(at):
        for start in range(0, width, width // 2):
            columns_here = slice(start, start + width // 2)
            term = nt(grads[at * piece : (at + 1) * piece, :], weight[columns_here, :])
            terms[at, :, columns_here] = term.astype(BF16)

    tile = min(512, width)
    narrow = columns // 2

    def outer(part):
        def body(left):
            here = pl.ds(pl.multiple_of(pl.program_id(0) * tile, tile), tile)
            grad_qkv[part, here, :] = tn(left[...], grads[:, part * narrow : (part + 1) * narrow]).astype(BF16)

        pltpu.emit_pipeline(
            body,
            grid=(width // tile,),
            in_specs=[pl.BlockSpec((normed_one.shape[0], tile), lambda i: (0, i))],
        )(normed_one)

    for item in early:
        item.wait()
    back_term(3)
    for item in across:
        item.start()
    later.wait()
    back_term(1)
    plain_one.start()
    outer(0)
    scatters[0].start()
    back_term(2)
    plain_two.start()
    scatters[0].spread()
    outer(1)
    scatters[1].start()
    for item in across:
        item.wait_recv()
    joined[0] = (terms[1, half:].astype(F32) + passed[1].astype(F32)).astype(BF16)
    joined[1] = (terms[2, :half].astype(F32) + passed[0].astype(F32)).astype(BF16)
    joined_one.start()
    joined_two.start()
    scatters[1].spread()
    scatters[0].pass_on()
    fc_own.start()
    back_term(0)
    mine[...] = jnp.zeros_like(mine)
    mine[2:6, :] = sums_two[...]
    for head in range(heads):
        at = (head * 2 + lax.rem(me, 2)) * 2 + lax.div(me, 2)
        here = pl.ds(pl.multiple_of(at * HEAD_DIM, HEAD_DIM), HEAD_DIM)
        for part in range(2):
            mine[6 + part : 7 + part, here] = qv_sums[part : part + 1, head * HEAD_DIM : (head + 1) * HEAD_DIM]
    scatters[1].pass_on()

    scatters[0].finish(shares[0])
    for item in (plain_one, plain_two, joined_one, joined_two):
        item.wait_recv()
    for item in fc_copies:
        item.start()
    part = min(128, piece)

    def norm_body(token_tile, middle_tile, out):
        i = pl.program_id(0)
        here = pl.ds(pl.multiple_of(i * part, part), part)
        upstream = terms[0, here, :].astype(F32) + arrived[0, here, :].astype(F32) + arrived[1, here, :].astype(F32)
        unit, scale = norm_parts(token_tile[...].astype(F32))
        out[...] = middle_tile[...] + norm_backward(unit, scale, vectors[0:1, :], upstream)
        for at, item in enumerate((upstream * unit, upstream)):
            sum_rows(mine, at, slice(None), item, i == 0)

    line = pl.BlockSpec((part, width), lambda i: (i, 0))
    pltpu.emit_pipeline(norm_body, grid=(piece // part,), in_specs=[line] * 2, out_specs=[line])(
        tokens, grad_middle, tokens_grad
    )
    for item in small_copies:
        item.start()
    scatters[1].finish(shares[1])
    for part in range(2):
        for item in qkv_copies[part]:
            item.start()
        qkv_own[part].start()
    for item in small_copies:
        item.wait_recv()
    mine_total = mine[...] + small_in[0] + small_in[1] + small_in[2]
    small_rows[...] = jnp.zeros_like(small_rows)
    share, wide = width // 8, 2 * width // 8
    for d in range(8):
        small_rows[d, 0:6, 0:share] = mine_total[0:6, d * share : (d + 1) * share]
        row, at = 6 + d // 4, (d % 4) * wide
        small_rows[d, 6:7, :] = mine_total[row : row + 1, at : at + wide]
        inner = hidden_sums.shape[1] // 8
        small_rows[d, 7:8, 0:inner] = hidden_sums[:, d * inner : (d + 1) * inner]
    for item in row_copies:
        item.start()
    sources = (*plane, me)
    fc_own.wait()
    for item in fc_copies:
        item.wait_recv()
    block = fc_in.shape[2] // 8
    for i, source in enumerate(sources):
        for d in range(8):
            target = pl.ds(pl.multiple_of((d * 4 + source) * block, block), block)
            fc_out[:, target] = fc_in[i, :, d * block : (d + 1) * block].astype(F32)
    for part in range(2):
        qkv_own[part].wait()
        for item in qkv_copies[part]:
            item.wait_recv()
    for i, source in enumerate(sources):
        for part in range(3):
            for head in range(heads):
                at = part * HEADS + (head * 2 + lax.rem(source, 2)) * 2 + lax.div(source, 2)
                target = pl.ds(pl.multiple_of(at * HEAD_DIM, HEAD_DIM), HEAD_DIM)
                start = (part * heads + head) * HEAD_DIM
                which, start = start // narrow, start % narrow
                qkv_out[:, target] = qkv_in[which, i, :, start : start + HEAD_DIM].astype(F32)
    for item in row_copies:
        item.wait_recv()
    total = small_rows[place]
    for i in range(7):
        total = total + small_got[i]
    small_out[...] = total
    for item in (*across, plain_one, plain_two, joined_one, joined_two, *fc_copies, *small_copies, *row_copies):
        item.wait_send()
    for part in range(2):
        scatters[part].close()
        for item in qkv_copies[part]:
            item.wait_send()


def closing(grads, weight, normed_one, tokens, grad_middle, vectors, sums_two, hidden_sums, qv_sums, fc_share):
    piece, width = tokens.shape
    columns, half = grads.shape[1], piece // 2
    fine = fc_share.shape[0] // 4
    wide = 2 * width // 8
    anywhere = pl.BlockSpec(memory_space=pltpu.HBM)
    inside = pl.BlockSpec(memory_space=pltpu.VMEM)
    shape = lambda rows, columns, kind=BF16: jax.ShapeDtypeStruct((rows, columns), kind)
    dma = pltpu.SemaphoreType.DMA
    return pl.pallas_call(
        closing_kernel,
        in_specs=[anywhere] * 5 + [inside] * 4 + [anywhere],
        out_specs=[anywhere, inside, inside, inside],
        out_shape=[
            shape(piece, width, F32), shape(fine, 4 * columns, F32), shape(fine, 4 * fc_share.shape[1], F32),
            shape(8, wide, F32),
        ],
        scratch_shapes=[
            pltpu.VMEM((4, piece, width), BF16),
            pltpu.VMEM((2, half, width), BF16),
            pltpu.VMEM((2, half, width), BF16),
            pltpu.VMEM((2, piece, width), BF16),
            pltpu.VMEM((2, 4, fine, columns // 2), BF16),
            pltpu.VMEM((4, fine, fc_share.shape[1]), BF16),
            pltpu.VMEM((8, width), F32),
            pltpu.VMEM((3, 8, width), F32),
            pltpu.VMEM((8, 8, wide), F32),
            pltpu.VMEM((7, 8, wide), F32),
            *[
                pltpu.VMEM((2, count, columns // 2), BF16)
                for count in (width, width // 2, width // 2, width // 2, width // 8)
            ],
            pltpu.VMEM(grads.shape, BF16),
            pltpu.VMEM(weight.shape, BF16),
            dma((21,)), dma((21,)), dma((2, 8)), dma((2, 8)), dma((7,)), dma((7,)), dma((6,)),
        ],
        compiler_params=pltpu.CompilerParams(collective_id=4, has_side_effects=True, vmem_limit_bytes=60 * 2**20),
        cost_estimate=cost(16 * piece * width * columns, 10 * piece * width),
    )(grads, weight, normed_one, tokens, grad_middle, vectors, sums_two, hidden_sums, qv_sums, fc_share)


def after(value, *others):
    return lax.optimization_barrier((value, *others))[0]


def shift(value, axis, distance):
    count = lax.axis_size(axis)
    return lax.ppermute(value, axis, [(i, i ^ distance) for i in range(count)])


def gather_blocks(value, axis="seq"):
    return [value] + [shift(value, axis, k) for k in range(1, lax.axis_size(axis))]


def scatter_blocks(blocks, axis="seq"):
    return [blocks[0]] + [shift(blocks[k], axis, k) for k in range(1, lax.axis_size(axis))]


def gather_plane(value):
    if lax.axis_size("seq") != 4:
        return gather_blocks(value)
    half = value.shape[0] // 2
    one, two = shift(value, "seq", 1), shift(value, "seq", 2)
    three = jnp.concatenate([shift(one[:half], "seq", 2), shift(two[half:], "seq", 1)], axis=0)
    return [value, one, two, three]


def scatter_plane(blocks):
    if lax.axis_size("seq") != 4:
        return scatter_blocks(blocks)
    half = blocks[0].shape[0] // 2
    up, low = shift(blocks[3][:half], "seq", 1), shift(blocks[3][half:], "seq", 2)
    one = shift(blocks[1][:half], "seq", 1)
    two = shift(blocks[2][half:], "seq", 2)
    one_low = (blocks[1][half:].astype(F32) + low.astype(F32)).astype(BF16)
    two_up = (blocks[2][:half].astype(F32) + up.astype(F32)).astype(BF16)
    return [blocks[0], (one, shift(one_low, "seq", 1)), (shift(two_up, "seq", 2), two)]


def by_rank(blocks, rank):
    bit = 1
    while bit < len(blocks):
        odd = (rank & bit) != 0
        blocks = [jnp.where(odd, blocks[k ^ bit], blocks[k]) for k in range(len(blocks))]
        bit *= 2
    return blocks


def pick(pieces, at):
    return lax.dynamic_index_in_dim(pieces, at, axis=0, keepdims=False)


def exchange(pieces, rank):
    return scatter_blocks([pick(pieces, rank ^ k) for k in range(pieces.shape[0])])


def small_scatter(pieces, dp_rank, seq_rank):
    total = 0.0
    sent = [lax.dynamic_index_in_dim(pieces, seq_rank ^ k, axis=1, keepdims=False) for k in range(pieces.shape[1])]
    for part in scatter_blocks(sent):
        total = total + part
    sent = [pick(total, dp_rank ^ k) for k in range(pieces.shape[0])]
    total = 0.0
    for part in scatter_blocks(sent, "dp"):
        total = total + part
    return total


def swap_pairs(dp_count, seq_count, sub):
    pairs = []
    for d in range(dp_count):
        for s in range(seq_count):
            source = ((d // sub) * sub + s % sub) * seq_count + (s // sub) * sub + d % sub
            pairs.append((source, d * seq_count + s))
    return pairs


def gather_dp(value):
    return lax.all_gather(value, "dp", axis=0, tiled=True)


def scatter_dp(value):
    return lax.psum_scatter(value, "dp", scatter_dimension=0, tiled=True)


def shards(
    tokens,
    cotangent,
    lengths,
    key_mask,
    attn_gain,
    attn_shift,
    qkv_weight,
    qv_bias,
    proj_weight,
    proj_bias,
    mlp_gain,
    mlp_shift,
    fc_weight,
    fc_bias,
    down_weight,
    down_bias,
):
    _, piece, width = tokens.shape
    dp_count, seq_count = lax.axis_size("dp"), lax.axis_size("seq")
    dp_rank, seq_rank = lax.axis_index("dp"), lax.axis_index("seq")
    own_heads = HEADS // seq_count
    own_width = own_heads * HEAD_DIM
    rows = qkv_weight.shape[0]
    sub = HEAD_DIM // proj_weight.shape[0]
    high = seq_count // sub
    block = down_weight.shape[0]
    rank = jnp.reshape(seq_rank, (1,)).astype(jnp.int32)
    swap = swap_pairs(dp_count, seq_count, sub)
    order = list(range(seq_count - 1, -1, -1))
    if seq_count == 4:
        order = [3, 1, 2, 0]

    in_plane = seq_count == 4 and dp_count == 8
    tokens_own, cot_own = tokens[0], cotangent[0]

    positions = seq_rank * piece + jnp.arange(piece, dtype=jnp.int32)
    own_flags = ((key_mask[0] == 1) & (positions < lengths[0])).astype(BF16)
    length = piece * seq_count
    shared = None
    if in_plane:
        six = jnp.stack([attn_gain, attn_shift, proj_bias, mlp_gain, mlp_shift, down_bias])
        odd = (seq_rank & 1) != 0
        six = jnp.concatenate([jnp.where(odd, 0, six), jnp.where(odd, six, 0)], axis=1)
        small, start = 0, 0
        for item in (six, qv_bias, fc_bias, own_flags):
            item = item.reshape(-1, 128)
            small = small + jnp.pad(item, ((start, 16 - start - item.shape[0]), (0, 0)))
            start += item.shape[0]
        token_all, qkv_full, fc_rows, cot_one, cot_two, down_full, proj_full, vectors, key_bias = opening(
            tokens_own, cot_own, qkv_weight, fc_weight, small, down_weight, proj_weight, dp_count
        )
        fc_full = gather_dp(fc_rows)
    else:
        small = (attn_gain, attn_shift, qv_bias, proj_bias, mlp_gain, mlp_shift, fc_bias, down_bias)
        sizes = [item.shape[0] for item in small]
        packed = jnp.concatenate(small + (own_flags,))
        blocks = gather_blocks(packed)
        flags = jnp.concatenate([item[-piece:] for item in blocks])
        key_bias = jnp.where(flags > 0, 0.0, NEG).astype(F32)[:, None]
        packed = jnp.stack(by_rank([item[:-piece] for item in blocks], seq_rank))
        packed = jnp.stack(by_rank(gather_blocks(packed, "dp"), dp_rank)).astype(F32)
        parts, start = [], 0
        for size in sizes:
            parts.append(packed[:, :, start : start + size])
            start += size
        whole = [part.reshape(1, -1) for part in parts]
        gain_one, shift_one, qv_full, proj_shift, gain_two, shift_two, _, down_shift = whole
        fc_shift = lax.dynamic_index_in_dim(parts[6], seq_rank, axis=1, keepdims=False).reshape(1, -1)
        rank_low, rank_high = seq_rank % sub, seq_rank // sub
        qv_own = qv_full.reshape(2, own_heads, sub, high, HEAD_DIM)
        qv_own = lax.dynamic_index_in_dim(qv_own, rank_low, axis=2, keepdims=False)
        qv_own = lax.dynamic_index_in_dim(qv_own, rank_high, axis=2, keepdims=False).reshape(1, -1)
        qv_own = jnp.pad(qv_own, ((0, 0), (0, width - 2 * own_width)))
        vectors = jnp.concatenate([gain_one, shift_one, jnp.zeros((5, width), F32), qv_own], axis=0)
        qkv_pieces = (
            qkv_weight.reshape(rows, 3, own_heads, sub, high, HEAD_DIM)
            .transpose(4, 3, 0, 1, 2, 5)
            .reshape(seq_count, rows, 3 * own_width)
        )
        fc_pieces = (
            fc_weight.reshape(rows, dp_count, seq_count, block)
            .transpose(2, 0, 1, 3)
            .reshape(seq_count, rows, dp_count * block)
        )
        qkv_full = gather_dp(jnp.concatenate(by_rank(exchange(qkv_pieces, seq_rank), seq_rank), axis=0))
        proj_full = gather_dp(lax.ppermute(proj_weight, BOTH, swap))
        down_full = gather_dp(down_weight)
        fc_full = gather_dp(jnp.concatenate(by_rank(exchange(fc_pieces, seq_rank), seq_rank), axis=0))
        token_blocks = gather_blocks(tokens_own)
        cot_blocks = gather_blocks(after(cot_own, token_blocks[-1]))
        for k in range(seq_count):
            shared = project(k, token_blocks[k], 0, piece, vectors, qkv_full, length, shared)
    if in_plane:
        results = attend_plane(
            tokens_own, cot_own, token_all, qkv_full, cot_one, down_weight, down_full, key_bias, proj_full, vectors
        )
        middle, normed_two, attended, lse, cot_three, down_full = results[:6]
        normed_one, q, keys, values, keys_t, values_t, one_low, two_low = results[6:]
    else:
        normed_one, q, keys, values, keys_t, values_t = shared
        proj_terms, shared = [None] * seq_count, None
        for k in order:
            proj_terms[k], shared = attend(k, rank, q, keys, values_t, key_bias, proj_full, piece, shared)
        attended, lse = shared
        middle, normed_two = rowwise(
            middle_kernel, scatter_blocks(proj_terms), [tokens_own], [proj_shift, gain_two, shift_two], [F32, BF16], 0
        )

    if in_plane:
        cots = (cot_own, cot_one, one_low, cot_two, two_low, cot_three)
        results = feed_plane(normed_two, cots, fc_full, down_full, middle, vectors)
        grad_middle, low_all, sums_two, hidden_sums, down_terms, grad_down, fc_summed = [
            results[i] for i in (0, 1, 2, 3, 8, 14, 16)
        ]
        grads, qv_sums, block_out, grad_proj, grad_fc = retreat_plane(
            low_all, q, keys, values, keys_t, lse, down_terms, middle, fc_summed, attended, key_bias, proj_full, vectors
        )
    else:
        normed_blocks = gather_blocks(normed_two)
        grad_terms, shared = [], None
        for k in range(seq_count):
            term, shared = feed(k, normed_blocks[k], cot_blocks[k], fc_full, fc_shift, down_full, seq_count, shared)
            grad_terms.append(term)
        active, grad_hidden, normed_all, cot_all = shared
        grad_middle, grad_mid_low, *sums_two = rowwise(
            middle_back_kernel, scatter_blocks(grad_terms), [middle, cot_own], [gain_two], [F32, BF16], 4
        )
        down_terms = [
            nn(active[k * piece : (k + 1) * piece], down_full).astype(BF16) for k in range(seq_count)
        ]
        low_blocks = gather_blocks(grad_mid_low)
        grad_down = scatter_dp(tn(active, cot_all).astype(BF16))
        grad_fc = scatter_dp(tn(normed_all, grad_hidden).astype(BF16))
        hidden_sums = jnp.sum(grad_hidden.astype(F32), axis=0)
        block_out = rowwise(out_kernel, scatter_blocks(down_terms), [middle], [down_shift], [BF16], 0)[0]
        sums, shared = None, None
        for k in range(seq_count):
            sums, shared = retreat(
                k, rank, low_blocks[k], proj_full, q, lse, keys, values, keys_t, key_bias, sums, shared,
                k == seq_count - 1,
            )
        grad_q, low_all = shared
        grads = jnp.concatenate([grad_q, sums[0], sums[1]], axis=1)
        qv_sums = jnp.stack([jnp.sum(item.astype(F32), axis=0) for item in (grad_q, sums[1])])
        grad_proj = tn(attended, low_all).astype(BF16)
    grad_proj = lax.ppermute(scatter_dp(grad_proj), BOTH, swap).astype(F32)
    share = attn_gain.shape[0]
    if in_plane:
        tokens_grad, grad_qkv_weight, grad_fc, smalls = closing(
            grads, qkv_full, normed_one, tokens_own, grad_middle, vectors, sums_two, hidden_sums, qv_sums, grad_fc
        )[:4]
        own = lambda row, size: lax.dynamic_slice_in_dim(smalls[row], seq_rank * size, size)
        late = jnp.concatenate([own(0, share), own(1, share), own(6, 2 * share)])
        early = jnp.concatenate([own(row, share) for row in range(2, 6)] + [smalls[7, :block]])
    else:
        back_terms = [None] * seq_count
        for k in order:
            back_terms[k] = back(k, grads, qkv_full, piece)
        tokens_grad, *sums_one = rowwise(
            tokens_back_kernel, scatter_blocks(back_terms), [tokens_own, grad_middle], [gain_one], [F32], 2
        )

        blocks = exchange(grad_fc.reshape(seq_count, rows, dp_count * block), seq_rank)
        if block % 128 == 0:
            fc_places = lambda s: [(0, d, d * seq_count + s) for d in range(dp_count)]
            grad_fc = lay_out(rank, [[item] for item in blocks], fc_weight.shape[1], (fc_places, block))
        else:
            blocks = [item.reshape(rows, dp_count, block) for item in by_rank(blocks, seq_rank)]
            grad_fc = jnp.stack(blocks, axis=2).reshape(fc_weight.shape).astype(F32)
        grad_qkv = scatter_dp(tn(normed_one, grads).astype(BF16))
        blocks = [[item] for item in exchange(grad_qkv.reshape(seq_count, rows, 3 * own_width), seq_rank)]
        qkv_places = lambda s: [
            (0, part * own_heads + head, part * HEADS + (head * sub + s % sub) * high + s // sub)
            for part in range(3)
            for head in range(own_heads)
        ]
        grad_qkv_weight = lay_out(rank, blocks, qkv_weight.shape[1], (qkv_places, HEAD_DIM))

        def spread(vector):
            return vector.reshape(dp_count, seq_count, -1)

        here = (jnp.arange(seq_count) == seq_rank).astype(F32)
        hidden_sums = hidden_sums.reshape(dp_count, 1, -1) * here[None, :, None]
        early = jnp.concatenate([spread(item) for item in sums_two] + [hidden_sums], axis=2)
        early = small_scatter(early, dp_rank, seq_rank)
        here = (jnp.arange(sub) == rank_low)[:, None] & (jnp.arange(high) == rank_high)[None, :]
        qv_sums = qv_sums.reshape(2, own_heads, 1, 1, HEAD_DIM) * here.astype(F32)[None, None, :, :, None]
        late = jnp.concatenate([spread(item) for item in sums_one] + [spread(qv_sums)], axis=2)
        late = small_scatter(late, dp_rank, seq_rank)
    return (
        block_out[None],
        tokens_grad[None],
        late[:share],
        late[share : 2 * share],
        grad_qkv_weight,
        late[2 * share :],
        grad_proj,
        early[2 * share : 3 * share],
        early[:share],
        early[share : 2 * share],
        grad_fc,
        early[4 * share :],
        grad_down.astype(F32),
        early[3 * share : 4 * share],
    )


def solution(mesh):
    in_specs = (
        P("dp", "seq", None),
        P("dp", "seq", None),
        P("dp"),
        P("dp", "seq"),
        P(BOTH),
        P(BOTH),
        P(BOTH, None),
        P(BOTH),
        P(BOTH, None),
        P(BOTH),
        P(BOTH),
        P(BOTH),
        P(BOTH, None),
        P(BOTH),
        P(BOTH, None),
        P(BOTH),
    )
    out_specs = (
        P("dp", "seq", None),
        P("dp", "seq", None),
        P(BOTH),
        P(BOTH),
        P(BOTH, None),
        P(BOTH),
        P(BOTH, None),
        P(BOTH),
        P(BOTH),
        P(BOTH),
        P(BOTH, None),
        P(BOTH),
        P(BOTH, None),
        P(BOTH),
    )
    return jax.shard_map(shards, mesh=mesh, in_specs=in_specs, out_specs=out_specs, check_vma=False)
```

```python
import functools
import math

import jax
import jax.numpy as jnp
from jax import lax
from jax.experimental import pallas as pl
from jax.experimental.pallas import tpu as pltpu
from jax.sharding import PartitionSpec as P

HEADS = 16
HEAD_DIM = 128
EPS = 1e-05
NEG = -1e30
FACTOR = HEAD_DIM ** (-0.5)
LOG2E = math.log2(math.e)
F32 = jnp.float32
BF16 = jnp.bfloat16
BOTH = ("dp", "seq")
MESH = pl.DeviceIdType.MESH


def nn(left, right):
    return lax.dot_general(left, right, (((1,), (0,)), ((), ())), preferred_element_type=F32)


def nt(left, right):
    return lax.dot_general(left, right, (((1,), (1,)), ((), ())), preferred_element_type=F32)


def tn(left, right):
    return lax.dot_general(left, right, (((0,), (0,)), ((), ())), preferred_element_type=F32)


def params(limit_mib=56):
    return pltpu.CompilerParams(dimension_semantics=("arbitrary",), vmem_limit_bytes=limit_mib * 2**20)


def cost(flops, moved, exps=0):
    return pl.CostEstimate(flops=int(flops), bytes_accessed=int(moved), transcendentals=int(exps))


def call_on_block(kernel, grid, inputs, fresh, shared, previous, scratch, estimate, rank=None, limit_mib=62):
    arrays = [item for item, _ in inputs]
    specs = [spec for _, spec in inputs]
    aliases = {}
    lead = 0 if rank is None else 1
    if previous is not None:
        for at, item in enumerate(previous):
            aliases[lead + len(arrays)] = len(fresh) + at
            arrays.append(item)
            specs.append(pl.BlockSpec(memory_space=pl.ANY))
    count = len(inputs)
    skipped = 0 if previous is None else len(previous)

    def body(*refs):
        refs = list(refs)
        kernel(*refs[: lead + count], *refs[lead + count + skipped :])

    out_specs = [spec for _, spec in fresh] + [spec for _, spec in shared]
    out_shape = [shape for shape, _ in fresh] + [shape for shape, _ in shared]
    if rank is None:
        results = pl.pallas_call(
            body, grid=grid, in_specs=specs, out_specs=out_specs, out_shape=out_shape, scratch_shapes=scratch,
            input_output_aliases=aliases, compiler_params=params(limit_mib), cost_estimate=estimate,
        )(*arrays)
    else:
        results = pl.pallas_call(
            body,
            grid_spec=pltpu.PrefetchScalarGridSpec(
                num_scalar_prefetch=1, grid=grid, in_specs=specs, out_specs=out_specs, scratch_shapes=scratch
            ),
            out_shape=out_shape, input_output_aliases=aliases, compiler_params=params(limit_mib), cost_estimate=estimate,
        )(rank, *arrays)
    return results[: len(fresh)], results[len(fresh) :]


def norm_parts(values):
    average = jnp.mean(values, axis=-1, keepdims=True)
    centred = values - average
    scale = lax.rsqrt(jnp.mean(centred * centred, axis=-1, keepdims=True) + EPS)
    return centred * scale, scale


def norm_backward(normed, scale, gain, upstream):
    weighted = upstream * gain
    return scale * (
        weighted
        - jnp.mean(weighted, axis=-1, keepdims=True)
        - normed * jnp.mean(weighted * normed, axis=-1, keepdims=True)
    )


def project_kernel(x, vectors, wq, wk, wv, normed, q, k, v, k_t, v_t):
    columns = wq.shape[1]
    rows = (norm_parts(x[...].astype(F32))[0] * vectors[0:1, :] + vectors[1:2, :]).astype(BF16)
    normed[...] = rows
    q[...] = (nn(rows, wq[...]) + vectors[7:8, :columns]).astype(BF16)
    keys = nn(rows, wk[...])
    k[...] = keys.astype(BF16)
    k_t[...] = keys.T.astype(BF16)
    values = nn(rows, wv[...]) + vectors[7:8, columns : 2 * columns]
    v[...] = values.astype(BF16)
    v_t[...] = values.T.astype(BF16)


def project(at, x, first, rows_here, vectors, weight, count, previous):
    width, columns = x.shape[1], weight.shape[1] // 3
    tile = min(256, rows_here)
    steps = rows_here // tile
    whole = lambda shape: pl.BlockSpec(shape, lambda i: (0, 0))
    rows = lambda n: pl.BlockSpec((tile, n), lambda i: (at * steps + i, 0))
    turned = pl.BlockSpec((columns, tile), lambda i: (0, at * steps + i))
    inputs = [
        (x, pl.BlockSpec((tile, width), lambda i: (first * steps + i, 0))),
        (vectors, whole(vectors.shape)),
        *[(weight, pl.BlockSpec((width, columns), lambda i, part=part: (0, part))) for part in range(3)],
    ]
    shape = lambda *dims: jax.ShapeDtypeStruct(dims, BF16)
    shared = [(shape(count, width), rows(width))] + [(shape(count, columns), rows(columns))] * 3
    shared += [(shape(columns, count), turned)] * 2
    return call_on_block(
        project_kernel, (steps,), inputs, [], shared, previous, [],
        cost(6 * rows_here * width * columns, 4 * rows_here * width + 6 * width * columns + 10 * rows_here * columns),
    )[1]


def rows_of(block, piece):
    return pl.ds(pl.multiple_of(block * piece, piece), piece)


def scores_of(key_ref, bias_ref, query, rel, piece, diagonal):
    rows = rows_of(rel, piece)
    scores = nt(key_ref[rows, :], query) * (FACTOR * LOG2E)
    key_bias = bias_ref[rows, :]
    if not diagonal:
        return scores + key_bias
    key_at = lax.broadcasted_iota(jnp.int32, scores.shape, 0)
    query_at = lax.broadcasted_iota(jnp.int32, scores.shape, 1)
    allowed = ((key_at < query_at) & (key_bias > -1.0)) | (key_at == query_at)
    return jnp.where(allowed, scores, NEG)


def attend_kernel(at, rank_ref, query_ref, key_ref, value_t, bias_ref, proj_ref, part_ref, attended, lse_ref, score_ref, sum_ref):
    piece = query_ref.shape[0]
    rank = rank_ref[0]
    head = pl.program_id(0)
    true = lax.bitwise_xor(at, rank)
    query = query_ref[...]

    def first(block, top):
        scores = scores_of(key_ref, bias_ref, query, lax.bitwise_xor(block, rank), piece, False)
        score_ref[rows_of(block, piece), :] = scores
        return jnp.maximum(top, jnp.max(scores, axis=0, keepdims=True))

    last = scores_of(key_ref, bias_ref, query, at, piece, True)
    top = lax.fori_loop(0, true, first, jnp.max(last, axis=0, keepdims=True))

    def weigh(scores, rel):
        weights = jnp.exp2(scores - top)
        return jnp.sum(weights, axis=0, keepdims=True), nn(value_t[:, rows_of(rel, piece)], weights.astype(BF16))

    def second(block, carry):
        total, out = carry
        more, part = weigh(score_ref[rows_of(block, piece), :], lax.bitwise_xor(block, rank))
        return total + more, out + part

    total, out = lax.fori_loop(0, true, second, weigh(last, at))
    result = (out / total).T.astype(BF16)
    attended[...] = result
    lse_ref[0] = top + jnp.log2(total)
    term = nn(result, proj_ref[...])

    @pl.when(head == 0)
    def _():
        sum_ref[...] = term

    @pl.when(head > 0)
    def _():
        sum_ref[...] += term

    @pl.when(head == pl.num_programs(0) - 1)
    def _():
        part_ref[...] = sum_ref[...].astype(BF16)


def attend(at, rank, q, k, v_t, key_bias, proj, piece, previous):
    length, columns = q.shape
    heads, width = columns // HEAD_DIM, proj.shape[1]
    inputs = [
        (q, pl.BlockSpec((piece, HEAD_DIM), lambda h, r: (at, h))),
        (k, pl.BlockSpec((length, HEAD_DIM), lambda h, r: (0, h))),
        (v_t, pl.BlockSpec((HEAD_DIM, length), lambda h, r: (h, 0))),
        (key_bias, pl.BlockSpec((length, 1), lambda h, r: (0, 0))),
        (proj, pl.BlockSpec((HEAD_DIM, width), lambda h, r: (h, 0))),
    ]
    fresh = [(jax.ShapeDtypeStruct((piece, width), BF16), pl.BlockSpec((piece, width), lambda h, r: (0, 0)))]
    shared = [
        (jax.ShapeDtypeStruct((length, columns), BF16), pl.BlockSpec((piece, HEAD_DIM), lambda h, r: (at, h))),
        (jax.ShapeDtypeStruct((heads, 1, length), F32), pl.BlockSpec((1, 1, piece), lambda h, r: (h, 0, at))),
    ]
    scratch = [pltpu.VMEM((length, piece), F32), pltpu.VMEM((piece, width), F32)]
    (part,), shared = call_on_block(
        functools.partial(attend_kernel, at), (heads,), inputs, fresh, shared, previous, scratch,
        cost(
            2 * length * piece * columns * 1.3 + 2 * piece * columns * width, 6 * length * columns + 2 * width * columns,
            heads * length * piece * 0.6,
        ), rank,
    )
    return part, shared


def feed_kernel(normed, cot, fc, bias, down, part, active_out, hidden_out, normed_out, cot_out, sum_ref):
    step = pl.program_id(0)
    weights = fc[...]
    hidden = nn(normed[...], weights) + bias[...]
    grad_active = nt(cot[...], down[...])
    inner = math.sqrt(2 / math.pi) * (hidden + 0.044715 * (hidden * hidden * hidden))
    bent = jnp.tanh(inner)
    half = 0.5 * (1.0 + bent)
    active_out[...] = (hidden * half).astype(BF16)
    slope = half + (0.5 * hidden) * (1.0 - bent * bent) * (
        math.sqrt(2 / math.pi) * (1.0 + (3 * 0.044715) * (hidden * hidden))
    )
    grad_hidden = (grad_active * slope).astype(BF16)
    hidden_out[...] = grad_hidden
    term = nt(grad_hidden, weights)

    @pl.when(step == 0)
    def _():
        sum_ref[...] = term
        normed_out[...] = normed[...]
        cot_out[...] = cot[...]

    @pl.when(step > 0)
    def _():
        sum_ref[...] += term

    @pl.when(step == pl.num_programs(0) - 1)
    def _():
        part[...] = sum_ref[...].astype(BF16)


def feed(at, normed, cot, fc, bias, down, count, previous):
    piece, width = normed.shape
    inner = fc.shape[1]
    tile = min(512, inner)
    length = piece * count
    rows = pl.BlockSpec((piece, width), lambda j: (0, 0))
    inputs = [
        (normed, rows),
        (cot, rows),
        (fc, pl.BlockSpec((width, tile), lambda j: (0, j))),
        (bias, pl.BlockSpec((1, tile), lambda j: (0, j))),
        (down, pl.BlockSpec((tile, width), lambda j: (j, 0))),
    ]
    shape = lambda n: jax.ShapeDtypeStruct((length, n), BF16)
    columns = pl.BlockSpec((piece, tile), lambda j: (at, j))
    here = pl.BlockSpec((piece, width), lambda j: (at, 0))
    fresh = [(jax.ShapeDtypeStruct((piece, width), BF16), rows)]
    shared = [(shape(inner), columns), (shape(inner), columns), (shape(width), here), (shape(width), here)]
    (part,), shared = call_on_block(
        feed_kernel, (inner // tile,), inputs, fresh, shared, previous, [pltpu.VMEM((piece, width), F32)],
        cost(6 * piece * width * inner, 4 * width * inner + 10 * piece * width + 4 * piece * inner, piece * inner),
    )
    return part, shared


def retreat_kernel(
    at, first_call, last_call, rank_ref, low_ref, proj_ref, query_ref, lse_ref, key_ref, value_ref, key_t, bias_ref, *rest
):
    rest = list(rest)
    key_in, value_in = (None, None) if first_call else (rest.pop(0), rest.pop(0))
    key_out, value_out, query_out, low_out, prob_ref, chance_ref, key_sum, value_sum = rest
    piece = query_ref.shape[0]
    rank = rank_ref[0]
    true = lax.bitwise_xor(at, rank)

    @pl.when(pl.program_id(0) == 0)
    def _():
        low_out[...] = low_ref[...]

    if first_call:
        key_sum[...] = jnp.zeros_like(key_sum)
        value_sum[...] = jnp.zeros_like(value_sum)
    else:
        key_sum[...] = key_in[...]
        value_sum[...] = value_in[...]
    query, lse = query_ref[...], lse_ref[0]
    grad = nt(low_ref[...], proj_ref[...]).astype(BF16)

    def measure(scores, rel):
        rows = rows_of(rel, piece)
        probs = jnp.exp2(scores - lse)
        grad_chances = nt(value_ref[rows, :], grad)
        value_sum[rows, :] += nn(probs.astype(BF16), grad)
        prob_ref[rows, :] = probs
        chance_ref[rows, :] = grad_chances
        return jnp.sum(probs * grad_chances, axis=0, keepdims=True)

    def first(block, weighted):
        rel = lax.bitwise_xor(block, rank)
        return weighted + measure(scores_of(key_ref, bias_ref, query, rel, piece, False), rel)

    last = scores_of(key_ref, bias_ref, query, at, piece, True)
    weighted = lax.fori_loop(0, true, first, measure(last, at))

    def second(block, total):
        rows = rows_of(lax.bitwise_xor(block, rank), piece)
        grad_scores = (prob_ref[rows, :] * (chance_ref[rows, :] - weighted)).astype(BF16)
        key_sum[rows, :] += nn(grad_scores, query)
        return total + nn(key_t[:, rows], grad_scores)

    total = lax.fori_loop(0, true + 1, second, jnp.zeros((HEAD_DIM, piece), F32))
    query_out[...] = (total * FACTOR).T.astype(BF16)
    if last_call:
        key_out[...] = (key_sum[...] * FACTOR).astype(BF16)
        value_out[...] = value_sum[...].astype(BF16)
    else:
        key_out[...] = key_sum[...]
        value_out[...] = value_sum[...]


def retreat(at, rank, low, proj, q, lse, k, v, k_t, key_bias, sums, previous, last_call):
    length, columns = q.shape
    piece, width = low.shape
    heads = columns // HEAD_DIM
    tall = pl.BlockSpec((length, HEAD_DIM), lambda h, r: (0, h))
    part = pl.BlockSpec((piece, HEAD_DIM), lambda h, r: (at, h))
    inputs = [
        (low, pl.BlockSpec((piece, width), lambda h, r: (0, 0))),
        (proj, pl.BlockSpec((HEAD_DIM, width), lambda h, r: (h, 0))),
        (q, part),
        (lse, pl.BlockSpec((1, 1, piece), lambda h, r: (h, 0, at))),
        (k, tall),
        (v, tall),
        (k_t, pl.BlockSpec((HEAD_DIM, length), lambda h, r: (h, 0))),
        (key_bias, pl.BlockSpec((length, 1), lambda h, r: (0, 0))),
    ]
    if sums is not None:
        inputs += [(item, tall) for item in sums]
    kind = BF16 if last_call else F32
    fresh = [(jax.ShapeDtypeStruct((length, columns), kind), tall)] * 2
    shared = [
        (jax.ShapeDtypeStruct((length, columns), BF16), part),
        (jax.ShapeDtypeStruct((length, width), BF16), pl.BlockSpec((piece, width), lambda h, r: (at, 0))),
    ]
    scratch = [pltpu.VMEM((length, piece), F32)] * 2 + [pltpu.VMEM((length, HEAD_DIM), F32)] * 2
    return call_on_block(
        functools.partial(retreat_kernel, at, sums is None, last_call), (heads,), inputs, fresh, shared, previous,
        scratch,
        cost(
            5 * 1.3 * length * piece * columns + 2 * piece * columns * width, 20 * length * columns,
            heads * length * piece * 0.6,
        ), rank,
    )


def back_kernel(grads, weight, out):
    out[...] = nt(grads[...], weight[...]).astype(BF16)


def back(at, grads, weight, piece):
    columns, width = grads.shape[1], weight.shape[0]
    tile = min(512, width)
    return pl.pallas_call(
        back_kernel,
        grid=(width // tile,),
        in_specs=[
            pl.BlockSpec((piece, columns), lambda j: (at, 0)),
            pl.BlockSpec((tile, columns), lambda j: (j, 0)),
        ],
        out_specs=pl.BlockSpec((piece, tile), lambda j: (0, j)),
        out_shape=jax.ShapeDtypeStruct((piece, width), BF16),
        compiler_params=params(),
        cost_estimate=cost(2 * piece * width * columns, 2 * width * columns + 2 * piece * (columns + width)),
    )(grads, weight)


def part_specs(parts, tile, steps, width):
    arrays, specs = [], []
    for part in parts:
        if isinstance(part, tuple):
            middle = steps // 2
            arrays += list(part)
            specs.append(pl.BlockSpec((tile, width), lambda i: (jnp.minimum(i, middle - 1), 0)))
            specs.append(pl.BlockSpec((tile, width), lambda i: (jnp.maximum(i - middle, 0), 0)))
        else:
            arrays.append(part)
            specs.append(pl.BlockSpec((tile, width), lambda i: (i, 0)))
    return arrays, specs


def add_parts(kinds, refs):
    total = None
    upper = pl.program_id(0) < pl.num_programs(0) // 2
    for kind in kinds:
        if kind:
            high, low = refs.pop(0)[...], refs.pop(0)[...]
            term = jnp.where(upper, high.astype(F32), low.astype(F32))
        else:
            term = refs.pop(0)[...].astype(F32)
        total = term if total is None else total + term
    return total


def rowwise(kernel, parts, rows, vectors, outputs, sums):
    count, width = rows[0].shape
    tile = min(128, count // 2)
    steps = count // tile
    arrays, specs = part_specs(parts, tile, steps, width)
    kinds = [isinstance(part, tuple) for part in parts]
    specs += [pl.BlockSpec((tile, width), lambda i: (i, 0))] * len(rows)
    specs += [pl.BlockSpec((1, width), lambda i: (0, 0))] * len(vectors)

    def body(*refs):
        refs = list(refs)
        total = add_parts(kinds, refs)
        tiles = [refs.pop(0)[...] for _ in rows]
        given = [refs.pop(0)[...] for _ in vectors]
        results = kernel(total, tiles, given)
        for result, _ in zip(results, outputs):
            refs.pop(0)[...] = result
        for result in results[len(outputs) :]:
            ref = refs.pop(0)
            column = jnp.sum(result, axis=0, keepdims=True)

            @pl.when(pl.program_id(0) == 0)
            def _():
                ref[...] = column

            @pl.when(pl.program_id(0) > 0)
            def _():
                ref[...] += column

    return pl.pallas_call(
        body,
        grid=(steps,),
        in_specs=specs,
        out_specs=[pl.BlockSpec((tile, width), lambda i: (i, 0))] * len(outputs)
        + [pl.BlockSpec((1, width), lambda i: (0, 0))] * sums,
        out_shape=[jax.ShapeDtypeStruct((count, width), kind) for kind in outputs]
        + [jax.ShapeDtypeStruct((1, width), F32)] * sums,
        compiler_params=params(),
        cost_estimate=cost(20 * count * width, count * width * (2 * len(arrays) + 4 * len(rows) + 4 * len(outputs))),
    )(*arrays, *rows, *vectors)


def middle_kernel(total, rows, vectors):
    (tokens,), (bias, gain, shift_) = rows, vectors
    middle = tokens.astype(F32) + (total + bias)
    return middle, (norm_parts(middle)[0] * gain + shift_).astype(BF16)


def out_kernel(total, rows, vectors):
    return (((rows[0] + (total + vectors[0])).astype(BF16)),)


def middle_back_kernel(total, rows, vectors):
    (middle, cot), (gain,) = rows, vectors
    normed, scale = norm_parts(middle)
    cot = cot.astype(F32)
    grad = cot + norm_backward(normed, scale, gain, total)
    low = grad.astype(BF16)
    return grad, low, total * normed, total, low.astype(F32), cot


def tokens_back_kernel(total, rows, vectors):
    (tokens, grad_middle), (gain,) = rows, vectors
    normed, scale = norm_parts(tokens.astype(F32))
    return grad_middle + norm_backward(normed, scale, gain, total), total * normed, total


def lay_out(rank, blocks, width, places):
    rows = blocks[0][0].shape[0]
    count, each = len(blocks), len(blocks[0])
    unit = places[1]

    def body(rank_ref, *refs):
        out = refs[-1]
        for k in range(count):
            source = lax.bitwise_xor(k, rank_ref[0])
            for array, column, target in places[0](source):
                out[:, pl.ds(pl.multiple_of(target * unit, unit), unit)] = refs[k * each + array][
                    :, column * unit : (column + 1) * unit
                ].astype(F32)

    arrays = [item for block in blocks for item in block]
    return pl.pallas_call(
        body,
        grid_spec=pltpu.PrefetchScalarGridSpec(
            num_scalar_prefetch=1,
            grid=(1,),
            in_specs=[pl.BlockSpec(item.shape, lambda i, r: (0, 0)) for item in arrays],
            out_specs=pl.BlockSpec((rows, width), lambda i, r: (0, 0)),
        ),
        out_shape=jax.ShapeDtypeStruct((rows, width), F32),
        compiler_params=params(),
        cost_estimate=cost(rows * width, 6 * rows * width),
    )(rank, *arrays)


def neighbours():
    rank = lax.axis_index("seq")
    return rank + 1 - 2 * lax.rem(rank, 2), rank + 2 - 4 * lax.rem(lax.div(rank, 2), 2)


def remote(source, target, send, receive, axis, device):
    return pltpu.make_async_remote_copy(
        src_ref=source, dst_ref=target, send_sem=send, recv_sem=receive, device_id={axis: device}, device_id_type=MESH
    )


def greet(axis, device):
    pl.semaphore_signal(pltpu.get_barrier_semaphore(), inc=1, device_id={axis: device}, device_id_type=MESH)


def flip(first, second):
    low = lax.rem(first + second, 2)
    high = lax.rem(lax.div(first, 2) + lax.div(second, 2), 2)
    return 2 * high + low


class LevelScatter:
    def __init__(self, source, mate_in, summed, got, send, receive):
        self.source, self.mate_in, self.summed, self.got = source, mate_in, summed, got
        self.send, self.receive = send, receive
        self.rows = mate_in.shape[0] // 4
        self.place = lax.axis_index("dp")
        self.level, self.core = lax.div(self.place, 2), lax.rem(self.place, 2)
        self.mate = self.place + 1 - 2 * self.core

    def greet(self):
        greet("dp", self.mate)
        count = jnp.int32(1)
        for step in (1, 2):
            up, down = self.level + step <= 3, self.level >= step
            pl.when(up)(lambda step=step: greet("dp", self.place + 2 * step))
            pl.when(down)(lambda step=step: greet("dp", self.place - 2 * step))
            count = count + up.astype(jnp.int32) + down.astype(jnp.int32)
        return count

    def block(self, ref, at):
        return ref.at[pl.ds(at * self.rows, self.rows)]

    def swaps(self):
        return [
            remote(
                self.block(self.source, 2 * at + 1 - self.core), self.block(self.mate_in, at),
                self.send.at[at], self.receive.at[at], "dp", self.mate,
            )
            for at in range(4)
        ]

    def start(self):
        for item in self.swaps():
            item.start()

    def add(self, first, second, out, grid, first_at, second_at, out_at):
        def body(left, right, total):
            total[...] = (left[...].astype(F32) + right[...].astype(F32)).astype(total.dtype)

        spec = lambda at: pl.BlockSpec((self.rows, first.shape[1]), lambda i: (at(i), 0))
        pltpu.emit_pipeline(
            body, grid=(grid,), in_specs=[spec(first_at), spec(second_at)], out_specs=[spec(out_at)]
        )(first, second, out)

    def hop(self, at, slot, index, steps):
        return remote(
            self.block(self.summed, at), self.block(self.got, slot), self.send.at[4 + index], self.receive.at[4 + slot],
            "dp", self.place + 2 * steps,
        )

    def hops(self):
        level = self.level
        return [
            (level == 0, self.hop(3, 3, 0, 1)),
            (level == 3, self.hop(0, 3, 0, -1)),
            (level == 0, self.hop(2, 2, 1, 2)),
            (level == 3, self.hop(1, 2, 1, -2)),
            (level <= 2, self.hop(lax.rem(level + 1, 4), 0, 2, 1)),
            (level >= 1, self.hop(lax.rem(level + 3, 4), 1, 3, -1)),
        ]

    def first_hops(self):
        hops, inner = self.hops(), (self.level == 1) | (self.level == 2)
        return hops[:2] + [(inner, hops[4][1]), (inner, hops[5][1])]

    def later_hops(self):
        hops = self.hops()
        return hops[2:4] + [(self.level == 0, hops[4][1]), (self.level == 3, hops[5][1])]

    def passes(self):
        return [(self.level == 1, self.hop(3, 2, 1, 2)), (self.level == 2, self.hop(0, 2, 1, -2))]

    def combine(self):
        for item in self.swaps():
            item.wait_recv()
        self.add(
            self.source, self.mate_in, self.summed, 4, lambda i: 2 * i + self.core, lambda i: i, lambda i: i
        )

    def spread(self):
        self.combine()
        for condition, copy in self.first_hops():
            pl.when(condition)(lambda copy=copy: copy.start())

    def arrive(self, slot):
        here = self.block(self.got, slot)
        remote(here, here, self.send.at[0], self.receive.at[4 + slot], "dp", self.mate).wait_recv()

    def pass_on(self):
        for level, at in ((1, 3), (2, 0)):

            @pl.when(self.level == level)
            def _(at=at):
                self.arrive(3)
                self.add(self.summed, self.got, self.summed, 1, lambda i: at, lambda i: 3, lambda i: at)

        for condition, copy in self.passes() + self.later_hops():
            pl.when(condition)(lambda copy=copy: copy.start())

    def finish(self, out):
        level = self.level
        pl.when(level >= 1)(lambda: self.arrive(0))
        pl.when(level <= 2)(lambda: self.arrive(1))
        self.arrive(2)
        rows = min(64, self.rows)

        def body(own, mate, below, above, far, total):
            value = own[...].astype(F32) + mate[...].astype(F32) + far[...].astype(F32)
            below_term, above_term = below[...].astype(F32), above[...].astype(F32)
            value = value + jnp.where(level >= 1, below_term, 0.0) + jnp.where(level <= 2, above_term, 0.0)
            total[...] = value.astype(total.dtype)

        steps = self.rows // rows
        spec = lambda at: pl.BlockSpec((rows, out.shape[1]), lambda i: (at * steps + i, 0))
        pltpu.emit_pipeline(
            body,
            grid=(steps,),
            in_specs=[spec(self.place), spec(level), spec(0), spec(1), spec(2)],
            out_specs=[spec(0)],
        )(self.source, self.mate_in, self.got, self.got, self.got, out)

    def close(self):
        for item in self.swaps():
            item.wait_send()
        for condition, copy in self.hops() + self.passes():
            pl.when(condition)(lambda copy=copy: copy.wait_send())


class LateScatter(LevelScatter):
    def __init__(self, summed, got, through, own, send, receive, load):
        self.summed, self.got, self.through, self.own = summed, got, through, own
        self.send, self.receive, self.load = send, receive, load
        self.rows = own.shape[0]
        self.place = lax.axis_index("dp")
        self.level, self.core = lax.div(self.place, 2), lax.rem(self.place, 2)
        self.mate = self.place + 1 - 2 * self.core

    def loads(self):
        passed_on = 3 * lax.rem(self.level, 2)
        return (
            pltpu.make_async_copy(self.block(self.summed, self.level), self.own, self.load.at[0]),
            pltpu.make_async_copy(self.block(self.summed, passed_on), self.through, self.load.at[1]),
        )

    def passes(self):
        target = self.block(self.got, 2)
        send, receive = self.send.at[4 + 1], self.receive.at[4 + 2]
        return [
            (self.level == 1, remote(self.through, target, send, receive, "dp", self.place + 4)),
            (self.level == 2, remote(self.through, target, send, receive, "dp", self.place - 4)),
        ]

    def start(self):
        for condition, copy in self.first_hops():
            pl.when(condition)(lambda copy=copy: copy.start())
        for item in self.loads():
            item.start()

    def part(self, slot):
        return self.got[slot * self.rows : (slot + 1) * self.rows, :].astype(F32)

    def pass_on(self):
        for item in self.loads():
            item.wait()

        @pl.when((self.level == 1) | (self.level == 2))
        def _():
            self.arrive(3)
            self.through[...] = (self.through[...].astype(F32) + self.part(3)).astype(BF16)

        for condition, copy in self.passes() + self.later_hops():
            pl.when(condition)(lambda copy=copy: copy.start())

    def finish(self, out):
        level = self.level
        pl.when(level >= 1)(lambda: self.arrive(0))
        pl.when(level <= 2)(lambda: self.arrive(1))
        self.arrive(2)
        value = self.own[...].astype(F32) + self.part(2)
        value = value + jnp.where(level >= 1, self.part(0), 0.0)
        value = value + jnp.where(level <= 2, self.part(1), 0.0)
        out[...] = value.astype(BF16)

    def close(self):
        for condition, copy in self.hops() + self.passes():
            pl.when(condition)(lambda copy=copy: copy.wait_send())


class NearScatter(LevelScatter):
    def part(self, ref, at):
        return ref[pl.ds(pl.multiple_of(at * self.rows, self.rows), self.rows), :].astype(F32)

    def spread(self):
        for item in self.swaps():
            item.wait_recv()
        for at in range(4):
            total = self.part(self.source, 2 * at + self.core) + self.part(self.mate_in, at)
            self.summed[at * self.rows : (at + 1) * self.rows, :] = total.astype(BF16)
        for condition, copy in self.first_hops():
            pl.when(condition)(lambda copy=copy: copy.start())

    def pass_on(self):
        for level, at in ((1, 3), (2, 0)):

            @pl.when(self.level == level)
            def _(at=at):
                self.arrive(3)
                total = self.part(self.summed, at) + self.part(self.got, 3)
                self.summed[at * self.rows : (at + 1) * self.rows, :] = total.astype(BF16)

        for condition, copy in self.passes() + self.later_hops():
            pl.when(condition)(lambda copy=copy: copy.start())

    def finish(self, out):
        level = self.level
        pl.when(level >= 1)(lambda: self.arrive(0))
        pl.when(level <= 2)(lambda: self.arrive(1))
        self.arrive(2)
        value = self.part(self.source, self.place) + self.part(self.mate_in, level) + self.part(self.got, 2)
        value = value + jnp.where(level >= 1, self.part(self.got, 0), 0.0)
        value = value + jnp.where(level <= 2, self.part(self.got, 1), 0.0)
        out[...] = value.astype(BF16)


class LevelGather:
    def __init__(self, own, full, send, receive, mate_send, mate_receive):
        self.own, self.full, self.send, self.receive = own, full, send, receive
        self.mate_send, self.mate_receive = mate_send, mate_receive
        self.rows = own.shape[0]
        self.place = lax.axis_index("dp")
        self.level, self.core = lax.div(self.place, 2), lax.rem(self.place, 2)
        self.mate = self.place + 1 - 2 * self.core

    greet = LevelScatter.greet

    def shard(self, level):
        return self.full.at[pl.ds((2 * level + self.core) * self.rows, self.rows)]

    def hop(self, index, steps, slot):
        return remote(
            self.own, self.shard(self.level), self.send.at[index], self.receive.at[slot], "dp", self.place + 2 * steps
        )

    def near(self):
        return [(self.level <= 2, self.hop(0, 1, 0)), (self.level >= 1, self.hop(1, -1, 1))]

    def second(self):
        inner = (self.level == 1) | (self.level == 2)
        lower, upper = self.shard(self.level - 1), self.shard(self.level + 1)
        return [
            (inner, remote(lower, lower, self.send.at[2], self.receive.at[2], "dp", self.place + 2)),
            (inner, remote(upper, upper, self.send.at[3], self.receive.at[2], "dp", self.place - 2)),
        ]

    def passes(self):
        first, last = self.shard(0), self.shard(3)
        return [
            (self.level == 2, remote(first, first, self.send.at[4], self.receive.at[3], "dp", self.place + 2)),
            (self.level == 1, remote(last, last, self.send.at[4], self.receive.at[3], "dp", self.place - 2)),
        ]

    def across(self, index, level):
        here = self.own if index == 4 else self.shard(level)
        return remote(here, self.shard(level), self.mate_send.at[index], self.mate_receive.at[index], "dp", self.mate)

    def arrivals(self, slots):
        level = self.level
        two_away = level + 2 - 4 * lax.div(level, 2)
        every = [
            (level >= 1, 0, level - 1),
            (level <= 2, 1, level + 1),
            (level >= 0, 2, two_away),
            ((level == 0) | (level == 3), 3, 3 - level),
        ]
        return [item for item in every if item[1] in slots]

    def start(self, hops):
        for condition, copy in hops:
            pl.when(condition)(lambda copy=copy: copy.start())

    def take(self, slots):
        for condition, slot, level in self.arrivals(slots):

            @pl.when(condition)
            def _(slot=slot, level=level):
                here = self.shard(level)
                remote(here, here, self.send.at[0], self.receive.at[slot], "dp", self.mate).wait_recv()
                self.across(slot, level).start()

    def finish(self, slots, hops):
        for condition, slot, level in self.arrivals(slots):
            pl.when(condition)(lambda slot=slot, level=level: self.across(slot, level).wait())
        for condition, copy in hops:
            pl.when(condition)(lambda copy=copy: copy.wait_send())


def opening_kernel(
    tokens, cot, qkv_in, fc_in, small, down_in, proj_in,
    token_all, qkv_full, fc_rows, cot_one, cot_two, down_full, proj_full, vectors, key_bias,
    qkv_weight, fc_weight, down, proj, entry, qkv_pieces, fc_pieces, token_buf, qkv_rows, small_rows, small_full, proj_rows, square, local, send, receive, up_send, up_receive, down_send, down_receive, mate_send, mate_receive,
    level_send, level_receive, level_mate_send, level_mate_receive,
):
    piece = tokens.shape[0]
    half = piece // 2
    entries = [
        pltpu.make_async_copy(source, target, entry.at[i])
        for i, (source, target) in enumerate(
            ((qkv_in, qkv_weight), (proj_in, proj), (down_in, down), (fc_in, fc_weight))
        )
    ]
    for copy in entries:
        copy.start()
    gather = LevelGather(down, down_full, level_send, level_receive, level_mate_send, level_mate_receive)
    me, place = lax.axis_index("seq"), lax.axis_index("dp")
    one, two = neighbours()
    three = 3 - me
    stages = lax.axis_size("dp") // 2
    level, core = lax.div(place, 2), lax.rem(place, 2)
    mate = place + 1 - 2 * core
    above, below = level < stages - 1, level > 0

    for device in (one, two, three):
        greet("seq", device)
    greet("dp", mate)
    pl.when(above)(lambda: greet("dp", place + 2))
    pl.when(below)(lambda: greet("dp", place - 2))
    swaps = core != lax.rem(me, 2)
    partner = {"dp": mate, "seq": one}

    @pl.when(swaps)
    def _():
        pl.semaphore_signal(pltpu.get_barrier_semaphore(), inc=1, device_id=partner, device_id_type=MESH)

    heads = qkv_pieces.shape[2] // (3 * HEAD_DIM)
    entries[0].wait()
    for rank in range(4):
        for part in range(3):
            for head in range(heads):
                source = (part * HEADS + (head * 2 + rank % 2) * 2 + rank // 2) * HEAD_DIM
                target = (part * heads + head) * HEAD_DIM
                qkv_pieces[rank, :, target : target + HEAD_DIM] = qkv_weight[:, source : source + HEAD_DIM]
    count = 4 + above.astype(jnp.int32) + below.astype(jnp.int32) + swaps.astype(jnp.int32)
    pl.semaphore_wait(pltpu.get_barrier_semaphore(), count)

    def block(ref, at, start=0, size=piece):
        return ref.at[pl.ds(at * piece + start, size)]

    def spread(pieces, target, at):
        rows = target.shape[0] // 4
        mine = target.at[pl.ds(me * rows, rows)]
        source = lambda device: pieces if pieces is small else pieces.at[device]
        copies = [
            remote(source(device), mine, send.at[at + i], receive.at[at + i], "seq", device)
            for i, device in enumerate((one, two, three))
        ]
        return copies, source(me), mine

    qkv_copies, qkv_own, qkv_mine = spread(qkv_pieces, qkv_rows, 0)
    small_copies, small_own, small_mine = spread(small, small_rows, 3)
    fc_copies, fc_own, fc_mine = spread(fc_pieces, fc_rows, 6)
    token_one = remote(tokens, block(token_all, 1), send.at[9], receive.at[9], "seq", one)
    token_two = remote(tokens, block(token_all, 2), send.at[10], receive.at[10], "seq", two)
    token_three = (
        remote(block(token_all, 1, 0, half), block(token_all, 3, 0, half), send.at[11], receive.at[11], "seq", two),
        remote(block(token_all, 2, half, half), block(token_all, 3, half, half), send.at[12], receive.at[12], "seq", one),
    )
    first_kept = [pltpu.make_async_copy(qkv_own, qkv_mine, local.at[0]), pltpu.make_async_copy(small_own, small_mine, local.at[1])]
    later_kept = [
        pltpu.make_async_copy(fc_own, fc_mine, local.at[2]),
        pltpu.make_async_copy(token_buf, block(token_all, 0), local.at[3]),
    ]
    token_load = pltpu.make_async_copy(tokens, token_buf, local.at[4])
    cot_copies = (
        remote(cot.at[pl.ds(0, half)], cot_one, send.at[13], receive.at[13], "seq", one),
        remote(cot.at[pl.ds(0, half)], cot_two, send.at[14], receive.at[14], "seq", two),
    )

    proj_copy = pltpu.make_async_remote_copy(
        src_ref=proj, dst_ref=proj_rows, send_sem=send.at[15], recv_sem=receive.at[15], device_id=partner,
        device_id_type=MESH,
    )
    chains = ((qkv_rows, qkv_full), (small_rows, small_full), (proj_rows, proj_full))

    def shard(array, at):
        rows = chains[array][0].shape[0]
        return chains[array][1].at[pl.ds((2 * at + core) * rows, rows)]

    def rising(array, step, device):
        at = level - (step - 1)
        source = chains[array][0] if step == 1 else shard(array, at)
        return remote(source, shard(array, at), up_send.at[array, step - 1], up_receive.at[array, step - 1], "dp", device)

    def falling(array, step, device):
        at = level + (step - 1)
        source = chains[array][0] if step == 1 else shard(array, at)
        return remote(source, shard(array, at), down_send.at[array, step - 1], down_receive.at[array, step - 1], "dp", device)

    def across(array, index, at):
        source = chains[array][0] if index == 0 else shard(array, at)
        return remote(source, shard(array, at), mate_send.at[array, index], mate_receive.at[array, index], "dp", mate)

    rises = lambda step: above & (level >= step - 1)
    falls = lambda step: below & (level <= stages - step)
    from_below = lambda step: level >= step
    from_above = lambda step: level + step <= stages - 1

    def relay(step):
        @pl.when(rises(step))
        def _():
            for array in (1, 0, 2):
                rising(array, step, place + 2).start()

        @pl.when(falls(step))
        def _():
            for array in (1, 0, 2):
                falling(array, step, place - 2).start()

    def take(step):
        @pl.when(from_below(step))
        def _():
            for array in (1, 0, 2):
                got = shard(array, level - step)
                remote(got, got, up_send.at[array, step - 1], up_receive.at[array, step - 1], "dp", mate).wait_recv()
                across(array, step, level - step).start()

        @pl.when(from_above(step))
        def _():
            for array in (1, 0, 2):
                got = shard(array, level + step)
                remote(got, got, down_send.at[array, step - 1], down_receive.at[array, step - 1], "dp", mate).wait_recv()
                across(array, stages - 1 + step, level + step).start()

    for copy in qkv_copies + small_copies + first_kept:
        copy.start()
    entries[1].wait()
    pl.when(swaps)(proj_copy.start)

    @pl.when(jnp.logical_not(swaps))
    def _():
        proj_rows[...] = proj[...]

    token_one.start()
    token_two.start()
    entries[2].wait()
    gather.start(gather.near())
    gather.across(4, level).start()
    down_kept = pltpu.make_async_copy(down, gather.shard(level), local.at[8])
    down_kept.start()
    token_load.start()
    entries[3].wait()
    inner = fc_pieces.shape[2] // 8
    for rank in range(4):
        for d in range(8):
            source = (d * 4 + rank) * inner
            fc_pieces[rank, :, d * inner : (d + 1) * inner] = fc_weight[:, source : source + inner]
    token_load.wait()
    for copy in qkv_copies + small_copies:
        copy.wait_recv()
    pl.when(swaps)(proj_copy.wait_recv)
    for copy in first_kept:
        copy.wait()
    relay(1)
    own_full = [pltpu.make_async_copy(chains[array][0], shard(array, level), local.at[5 + array]) for array in range(3)]
    for array in range(3):
        across(array, 0, level).start()
        own_full[array].start()
    for copy in fc_copies + later_kept:
        copy.start()
    for copy in cot_copies:
        copy.start()
    take(1)
    relay(2)
    take(2)
    relay(3)
    gather.take((0, 1))
    token_one.wait_recv()
    token_two.wait_recv()
    for copy in token_three:
        copy.start()
    take(3)
    for copy in later_kept + own_full:
        copy.wait()
    for copy in fc_copies:
        copy.wait_recv()
    for copy in qkv_copies + small_copies + fc_copies:
        copy.wait_send()
    token_one.wait_send()
    token_two.wait_send()
    for step in range(1, stages):

        @pl.when(rises(step))
        def _(step=step):
            for array in range(3):
                rising(array, step, place + 2).wait_send()

        @pl.when(falls(step))
        def _(step=step):
            for array in range(3):
                falling(array, step, place - 2).wait_send()

        @pl.when(from_below(step))
        def _(step=step):
            for array in range(3):
                across(array, step, level - step).wait()

        @pl.when(from_above(step))
        def _(step=step):
            for array in range(3):
                across(array, stages - 1 + step, level + step).wait()

    for array in range(3):
        across(array, 0, level).wait()
    for copy in token_three:
        copy.wait()
    down_kept.wait()
    pl.when(swaps)(proj_copy.wait_send)
    tile = lambda d, s: small_full[pl.ds(pl.multiple_of((d * 4 + s) * 16, 16), 16), :].astype(F32)
    vectors[...] = jnp.zeros_like(vectors)
    for d in range(8):
        for pair in range(2):
            both = tile(d, 2 * pair) + tile(d, 2 * pair + 1)
            vectors[0:6, (2 * d + pair) * 128 : (2 * d + pair + 1) * 128] = both[0:6]
        own = tile(d, me)
        for i in range(2):
            vectors[6:7, (2 * d + i) * 128 : (2 * d + i + 1) * 128] = own[7 + i : 8 + i]
        bias = tile(d, 2 * lax.rem(me, 2) + lax.div(me, 2))
        vectors[7:8, d * HEAD_DIM : (d + 1) * HEAD_DIM] = bias[6:7]
    square[...] = jnp.zeros_like(square)
    for i in range(4):
        square[4 * i : 4 * i + 4, :] = tile(place, flip(me, i))[9:13]
    turned = square[...].T
    lane = lax.broadcasted_iota(jnp.int32, turned.shape, 1)
    for i in range(16):
        flag = jnp.sum(jnp.where(lane == i, turned, 0.0), axis=1, keepdims=True)
        key_bias[i * 128 : (i + 1) * 128, :] = jnp.where(flag > 0, 0.0, NEG)
    for copy in cot_copies:
        copy.wait()
    gather.finish((0, 1), gather.near())
    gather.across(4, level).wait()


def opening(tokens, cot, qkv_weight, fc_weight, small, down, proj, dp_count):
    piece, width = tokens.shape
    steps = dp_count // 2 - 1
    anywhere = pl.BlockSpec(memory_space=pltpu.HBM)
    shape = lambda rows, columns: jax.ShapeDtypeStruct((rows, columns), BF16)
    dma = pltpu.SemaphoreType.DMA
    inside = pl.BlockSpec(memory_space=pltpu.VMEM)
    own_rows, columns, inner = qkv_weight.shape[0], qkv_weight.shape[1] // 4, fc_weight.shape[1] // 4
    rows, fine = 4 * own_rows, 4 * small.shape[0]
    return pl.pallas_call(
        opening_kernel,
        in_specs=[anywhere] * 4 + [inside] + [anywhere] * 2,
        out_specs=[anywhere] * 7 + [inside] * 2,
        out_shape=[
            shape(4 * piece, width),
            shape(rows * dp_count, columns),
            shape(rows, inner),
            shape(piece // 2, width),
            shape(piece // 2, width),
            shape(down.shape[0] * dp_count, width),
            shape(proj.shape[0] * dp_count, width),
            jax.ShapeDtypeStruct((8, width), F32),
            jax.ShapeDtypeStruct((4 * piece, 1), F32),
        ],
        scratch_shapes=[
            *[pltpu.VMEM(item.shape, BF16) for item in (qkv_weight, fc_weight, down, proj)], dma((4,)),
            pltpu.VMEM((4, own_rows, columns), BF16), pltpu.VMEM((4, own_rows, inner), BF16),
            pltpu.VMEM((piece, width), BF16),
            pltpu.VMEM((rows, columns), BF16), pltpu.VMEM((fine, 128), BF16), pltpu.VMEM((fine * dp_count, 128), BF16),
            pltpu.VMEM(proj.shape, BF16), pltpu.VMEM((128, 128), F32),
            dma((9,)), dma((16,)), dma((16,)), dma((3, steps)), dma((3, steps)), dma((3, steps)), dma((3, steps)),
            dma((3, 2 * steps + 1)), dma((3, 2 * steps + 1)), dma((5,)), dma((4,)), dma((5,)), dma((5,)),
        ],
        compiler_params=pltpu.CompilerParams(collective_id=0, has_side_effects=True, vmem_limit_bytes=62 * 2**20),
        cost_estimate=cost(0, 10 * 4 * piece * width),
    )(tokens, cot, qkv_weight, fc_weight, small, down, proj)


def attend_plane_kernel(
    tokens, cot, token_all, weight, cot_one, down, down_in, bias_in, proj_in, vectors,
    middle, normed, attended, lse, cot_three, down_full, normed_one, q, k, v, k_t, v_t, one_low, two_low,
    key_bias, proj, entry, score_ref, joint, terms, passed, joined, arrived, send, receive,
    level_send, level_receive, mate_send, mate_receive,
):
    piece, width = tokens.shape
    half = piece // 2
    entries = (
        pltpu.make_async_copy(bias_in, key_bias, entry.at[0]), pltpu.make_async_copy(proj_in, proj, entry.at[1])
    )
    for item in entries:
        item.start()
    length, columns = q.shape
    heads = columns // HEAD_DIM
    rank = lax.axis_index("seq")
    one, two = neighbours()
    gather = LevelGather(down, down_full, level_send, level_receive, mate_send, mate_receive)
    for device in (one, two):
        greet("seq", device)
    pl.semaphore_wait(pltpu.get_barrier_semaphore(), 2 + gather.greet())
    up, lower = pl.ds(0, half), pl.ds(half, half)
    gather.start(gather.second())

    def copy(index, source, target, device):
        return remote(source, target, send.at[index], receive.at[index], "seq", device)

    cot_copies = (copy(0, cot_one, cot_three.at[up], two), copy(1, two_low, cot_three.at[lower], one))
    low_copies = (copy(8, cot.at[lower], one_low, one), copy(9, cot.at[lower], two_low, two))
    across = (copy(2, terms.at[3, up], passed.at[0], one), copy(3, terms.at[3, lower], passed.at[1], two))
    plain_one = copy(4, terms.at[1, up], arrived.at[0, up], one)
    plain_two = copy(5, terms.at[2, lower], arrived.at[1, lower], two)
    joined_one = copy(6, joined.at[0], arrived.at[0, lower], one)
    joined_two = copy(7, joined.at[1], arrived.at[1, up], two)
    for item in low_copies:
        item.start()
    cot_copies[0].start()
    tile = min(256, piece)
    rows = lambda n: pl.BlockSpec((tile, n), lambda i: (i, 0))
    turned = pl.BlockSpec((columns, tile), lambda i: (0, i))
    pltpu.emit_pipeline(
        lambda x, wq, wk, wv, *out: project_kernel(x, vectors, wq, wk, wv, *out),
        grid=(length // tile,),
        in_specs=[rows(width)] + [pl.BlockSpec((width, columns), lambda i, part=part: (0, part)) for part in range(3)],
        out_specs=[rows(width), rows(columns), rows(columns), rows(columns), turned, turned],
    )(token_all, weight, weight, weight, normed_one, q, k, v, k_t, v_t)
    for item in low_copies:
        item.wait_recv()
    cot_copies[1].start()
    for item in entries:
        item.wait()

    def body(query_ref, key_ref, value_t, attended_tile, lse_tile):
        group, head = pl.program_id(0), pl.program_id(1)
        at = 3 - group
        true = flip(at, rank)
        query = query_ref[...]

        def first(block, top):
            scores = scores_of(key_ref, key_bias, query, flip(block, rank), piece, False)
            score_ref[rows_of(block, piece), :] = scores
            return jnp.maximum(top, jnp.max(scores, axis=0, keepdims=True))

        last = scores_of(key_ref, key_bias, query, at, piece, True)
        top = lax.fori_loop(0, true, first, jnp.max(last, axis=0, keepdims=True))

        def weigh(scores, rel):
            weights = jnp.exp2(scores - top)
            return jnp.sum(weights, axis=0, keepdims=True), nn(value_t[:, rows_of(rel, piece)], weights.astype(BF16))

        def second(block, carry):
            total, out = carry
            more, part = weigh(score_ref[rows_of(block, piece), :], flip(block, rank))
            return total + more, out + part

        total, out = lax.fori_loop(0, true, second, weigh(last, at))
        result = (out / total).T.astype(BF16)
        attended_tile[...] = result
        lse_tile[0] = top + jnp.log2(total)
        joint[:, pl.ds(pl.multiple_of(head * HEAD_DIM, HEAD_DIM), HEAD_DIM)] = result

        @pl.when(head == heads - 1)
        def _():
            terms[at] = nn(joint[...], proj[...]).astype(BF16)

        @pl.when((head == heads - 1) & (group == 0))
        def _():
            for item in across:
                item.start()

        @pl.when((head == heads - 1) & (group == 1))
        def _():
            plain_two.start()

        @pl.when((head == 0) & (group == 3))
        def _():
            gather.take((2,))
            gather.start(gather.passes())

        @pl.when((head == heads - 1) & (group == 2))
        def _():
            plain_one.start()
            for item in across:
                item.wait_recv()
            joined[0] = (terms[1, half:].astype(F32) + passed[1].astype(F32)).astype(BF16)
            joined[1] = (terms[2, :half].astype(F32) + passed[0].astype(F32)).astype(BF16)
            joined_one.start()
            joined_two.start()

    pltpu.emit_pipeline(
        body,
        grid=(4, heads),
        in_specs=[
            pl.BlockSpec((piece, HEAD_DIM), lambda g, h: (3 - g, h)),
            pl.BlockSpec((length, HEAD_DIM), lambda g, h: (0, h)),
            pl.BlockSpec((HEAD_DIM, length), lambda g, h: (h, 0)),
        ],
        out_specs=[
            pl.BlockSpec((piece, HEAD_DIM), lambda g, h: (3 - g, h)),
            pl.BlockSpec((1, 1, piece), lambda g, h: (h, 0, 3 - g)),
        ],
    )(q, k, v_t, attended, lse)

    for item in (plain_one, plain_two, joined_one, joined_two):
        item.wait_recv()
    part = min(128, piece)

    def norm_body(token_tile, middle_tile, normed_tile):
        here = pl.ds(pl.multiple_of(pl.program_id(0) * part, part), part)
        total = terms[0, here, :].astype(F32) + arrived[0, here, :].astype(F32) + arrived[1, here, :].astype(F32)
        values = token_tile[...].astype(F32) + (total + vectors[2:3, :])
        middle_tile[...] = values
        normed_tile[...] = (norm_parts(values)[0] * vectors[3:4, :] + vectors[4:5, :]).astype(BF16)

    line = pl.BlockSpec((part, width), lambda i: (i, 0))
    pltpu.emit_pipeline(norm_body, grid=(piece // part,), in_specs=[line], out_specs=[line] * 2)(tokens, middle, normed)
    gather.take((3,))
    gather.finish((2, 3), gather.second() + gather.passes())
    for item in cot_copies:
        item.wait()
    for item in low_copies:
        item.wait_send()
    for item in (*across, plain_one, plain_two, joined_one, joined_two):
        item.wait_send()


def attend_plane(tokens, cot, token_all, weight, cot_one, down, down_in, key_bias, proj, vectors):
    piece, width = tokens.shape
    length, columns = token_all.shape[0], proj.shape[0]
    heads, half = columns // HEAD_DIM, piece // 2
    anywhere = pl.BlockSpec(memory_space=pltpu.HBM)
    inside = pl.BlockSpec(memory_space=pltpu.VMEM)
    shape = lambda *dims: jax.ShapeDtypeStruct(dims, BF16)
    dma = pltpu.SemaphoreType.DMA
    return pl.pallas_call(
        attend_plane_kernel,
        in_specs=[anywhere] * 9 + [inside],
        out_specs=[anywhere] * 14,
        input_output_aliases={6: 5},
        out_shape=[
            jax.ShapeDtypeStruct((piece, width), F32), shape(piece, width), shape(length, columns),
            jax.ShapeDtypeStruct((heads, 1, length), F32), shape(piece, width), shape(*down_in.shape),
            shape(length, width), *[shape(length, columns)] * 3, *[shape(columns, length)] * 2,
            *[shape(half, width)] * 2,
        ],
        scratch_shapes=[
            pltpu.VMEM(key_bias.shape, F32),
            pltpu.VMEM(proj.shape, BF16),
            dma((2,)),
            pltpu.VMEM((length, piece), F32),
            pltpu.VMEM((piece, columns), BF16),
            pltpu.VMEM((4, piece, width), BF16),
            pltpu.VMEM((2, half, width), BF16),
            pltpu.VMEM((2, half, width), BF16),
            pltpu.VMEM((2, piece, width), BF16),
            dma((10,)), dma((10,)), dma((5,)), dma((4,)), dma((5,)), dma((5,)),
        ],
        compiler_params=pltpu.CompilerParams(collective_id=2, has_side_effects=True, vmem_limit_bytes=62 * 2**20),
        cost_estimate=cost(3 * length * length * columns + 2 * length * columns * width, 10 * length * width, heads * length * length // 2),
    )(tokens, cot, token_all, weight, cot_one, down, down_in, key_bias, proj, vectors)


def sum_rows(ref, at, columns, value, first):
    total = jnp.sum(value, axis=0, keepdims=True)

    @pl.when(first)
    def _():
        ref[at : at + 1, columns] = total

    @pl.when(jnp.logical_not(first))
    def _():
        ref[at : at + 1, columns] += total


def plane_kernel(
    normed, cot_own, one_up, one_low, two_up, two_low, cot_three, fc, down, middle, vectors,
    grad_middle, low_all, sums, hidden_sums, active, hidden_grad, normed_all, cot_all, terms, grad_down, grad_fc,
    mate_in, summed, got, down_share, fc_mate, fc_summed,
    normed_buf, cot_buf, sum_ref, joined, passed, arrived, load, local, send, receive, level_send, level_receive, fc_send, fc_receive,
):
    piece, width = normed.shape
    half = piece // 2
    inner = fc.shape[1]
    length = normed_all.shape[0]
    tile = min(512, inner)
    last = inner // tile - 1
    one, two = neighbours()
    scatter = LevelScatter(grad_down, mate_in, summed, got, level_send, level_receive)
    fc_scatter = LevelScatter(grad_fc, fc_mate, fc_summed, None, fc_send, fc_receive)
    for device in (one, two):
        greet("seq", device)
    pl.semaphore_wait(pltpu.get_barrier_semaphore(), 2 + scatter.greet())

    rows = lambda k, start=0, size=piece: pl.ds(k * piece + start, size)
    first, second = pl.ds(0, half), pl.ds(half, half)

    def copy(index, source, target, device):
        return remote(source, target, send.at[index], receive.at[index], "seq", device)

    normed_first = (copy(0, normed.at[first], normed_buf.at[2], one), copy(1, normed.at[second], normed_buf.at[5], two))
    normed_across = (copy(2, normed_buf.at[2], normed_buf.at[6], two), copy(3, normed_buf.at[5], normed_buf.at[7], one))
    normed_last = (copy(4, normed.at[second], normed_buf.at[3], one), copy(5, normed.at[first], normed_buf.at[4], two))
    across = (copy(6, cot_buf.at[6], passed.at[0], one), copy(7, cot_buf.at[7], passed.at[1], two))
    plain = (copy(8, cot_buf.at[2], arrived.at[0, 0], one), copy(9, cot_buf.at[5], arrived.at[1, 1], two))
    both = (copy(10, joined.at[0], arrived.at[0, 1], one), copy(11, joined.at[1], arrived.at[1, 0], two))
    low_near = (
        copy(12, low_all.at[rows(0)], low_all.at[rows(1)], one),
        copy(13, low_all.at[rows(0)], low_all.at[rows(2)], two),
    )
    low_three = (
        copy(14, low_all.at[rows(1, 0, half)], low_all.at[rows(3, 0, half)], two),
        copy(15, low_all.at[rows(2, half, half)], low_all.at[rows(3, half, half)], one),
    )

    sources = (
        cot_own.at[first], cot_own.at[second], one_up, one_low, two_up, two_low, cot_three.at[first], cot_three.at[second]
    )
    loads = [pltpu.make_async_copy(source, cot_buf.at[i], load.at[i]) for i, source in enumerate(sources)]
    own = [
        pltpu.make_async_copy(normed.at[part], normed_buf.at[i], load.at[8 + i]) for i, part in enumerate((first, second))
    ]
    keep_to = lambda target, i: target.at[pl.ds(i * half, half)]
    keeps = [pltpu.make_async_copy(normed_buf.at[i], keep_to(normed_all, i), local.at[i]) for i in range(8)]
    keeps_cot = [pltpu.make_async_copy(cot_buf.at[i], keep_to(cot_all, i), local.at[8 + i]) for i in range(8)]

    def start(*items):
        for item in items:
            item.start()

    def received(*items):
        for item in items:
            item.wait_recv()

    start(*normed_first, *own, *loads)

    place_of = lambda step: step + 2 * lax.div(step, 3) - 7 * lax.div(step, 6)

    def feed_body(fc_tile, down_tile, active_tile, hidden_tile):
        step, j = pl.program_id(0), pl.program_id(1)
        at = place_of(step)

        @pl.when((step == 0) & (j == 0))
        def _():
            for item in own:
                item.wait()
            start(*keeps[:2])
            for item in loads:
                item.wait()
            start(*keeps_cot)

        @pl.when((step == 2) & (j == 0))
        def _():
            received(*normed_first)
            start(*normed_across, keeps[2], keeps[5])

        @pl.when((step == 4) & (j == 0))
        def _():
            received(*normed_across)
            start(*normed_last, *keeps[6:])

        @pl.when((step == 6) & (j == 0))
        def _():
            received(*normed_last)
            start(*keeps[3:5])

        @pl.when((step == 7) & (j == 0))
        def _():
            start(*plain)

        weights = fc_tile[...]
        columns = pl.ds(pl.multiple_of(j * tile, tile), tile)
        hidden = nn(normed_buf[at], weights) + vectors[6:7, columns]
        grad_active = nt(cot_buf[at], down_tile[...])
        square = hidden * hidden
        bent = jnp.tanh(math.sqrt(2 / math.pi) * (hidden + 0.044715 * (square * hidden)))
        share = 0.5 * (1.0 + bent)
        active_tile[...] = (hidden * share).astype(BF16)
        slope = share + (0.5 * hidden) * (1.0 - bent * bent) * (
            math.sqrt(2 / math.pi) * (1.0 + (3 * 0.044715) * square)
        )
        grad_hidden = (grad_active * slope).astype(BF16)
        hidden_tile[...] = grad_hidden
        sum_rows(hidden_sums, 0, columns, grad_hidden.astype(F32), step == 0)
        term = nt(grad_hidden, weights)

        @pl.when(j == 0)
        def _():
            sum_ref[...] = term

        @pl.when(j > 0)
        def _():
            sum_ref[...] += term

        @pl.when((j == last) & (step == 0))
        def _():
            for item in keeps_cot:
                item.wait()

        @pl.when(j == last)
        def _():
            cot_buf[at] = sum_ref[...].astype(BF16)

        @pl.when((j == last) & (step == 5))
        def _():
            start(*across)

    pltpu.emit_pipeline(
        feed_body,
        grid=(8, inner // tile),
        in_specs=[
            pl.BlockSpec((width, tile), lambda s, j: (0, j)),
            pl.BlockSpec((tile, width), lambda s, j: (j, 0)),
        ],
        out_specs=[pl.BlockSpec((half, tile), lambda s, j: (place_of(s), j))] * 2,
    )(fc, down, active, hidden_grad)

    received(*across)
    joined[0] = (cot_buf[3].astype(F32) + passed[1].astype(F32)).astype(BF16)
    joined[1] = (cot_buf[4].astype(F32) + passed[0].astype(F32)).astype(BF16)
    start(*both)
    for item in keeps:
        item.wait()

    narrow = min(512, width)

    def down_body(active_rows, down_columns, out):
        out[...] = nn(active_rows[...], down_columns[...]).astype(BF16)

    def multiply_down(start):
        pltpu.emit_pipeline(
            down_body,
            grid=(2, width // narrow),
            in_specs=[
                pl.BlockSpec((piece, inner), lambda k, j: (start + k, 0)),
                pl.BlockSpec((inner, narrow), lambda k, j: (0, j)),
            ],
            out_specs=[pl.BlockSpec((piece, narrow), lambda k, j: (start + k, j))],
        )(active, down, terms)

    wide, tall = min(1024, width), min(1024, inner)

    def outer_body(left, right, out):
        out[...] = tn(left[...], right[...]).astype(BF16)

    def outer(left, right, out, shape):
        pltpu.emit_pipeline(
            outer_body,
            grid=(out.shape[0] // shape[0], out.shape[1] // shape[1]),
            in_specs=[
                pl.BlockSpec((length, shape[0]), lambda i, j: (0, i)),
                pl.BlockSpec((length, shape[1]), lambda i, j: (0, j)),
            ],
            out_specs=[pl.BlockSpec(shape, lambda i, j: (i, j))],
        )(left, right, out)

    outer(active, cot_all, grad_down, (tall, wide))
    scatter.start()
    multiply_down(0)
    scatter.spread()
    received(*plain, *both)
    part = min(128, half)
    steps = half // part

    def norm_body(middle_tile, cot_tile, grad_tile, low_tile):
        i = pl.program_id(0)
        at = lax.div(i, steps)
        here = pl.ds(pl.multiple_of(lax.rem(i, steps) * part, part), part)
        upstream = (
            cot_buf[at, here, :].astype(F32) + arrived[0, at, here, :].astype(F32) + arrived[1, at, here, :].astype(F32)
        )
        unit, scale = norm_parts(middle_tile[...])
        cot = cot_tile[...].astype(F32)
        grad = cot + norm_backward(unit, scale, vectors[3:4, :], upstream)
        rounded = grad.astype(BF16)
        grad_tile[...] = grad
        low_tile[...] = rounded
        for at, item in enumerate((upstream * unit, upstream, rounded.astype(F32), cot)):
            sum_rows(sums, at, slice(None), item, i == 0)

    line = pl.BlockSpec((part, width), lambda i: (i, 0))
    pltpu.emit_pipeline(norm_body, grid=(piece // part,), in_specs=[line] * 2, out_specs=[line] * 2)(
        middle, cot_own, grad_middle, low_all
    )
    start(*low_near)
    multiply_down(2)
    scatter.pass_on()
    outer(normed_all, hidden_grad, grad_fc, (wide, tall))
    fc_scatter.start()
    received(*low_near)
    start(*low_three)
    fc_scatter.combine()
    scatter.finish(down_share)
    scatter.close()
    for item in fc_scatter.swaps():
        item.wait_send()
    received(*low_three)
    for item in (*normed_first, *normed_across, *normed_last, *across, *plain, *both, *low_near, *low_three):
        item.wait_send()


def feed_plane(normed, cots, fc, down, middle, vectors):
    piece, width = normed.shape
    inner = fc.shape[1]
    length, half = 4 * piece, piece // 2
    anywhere = pl.BlockSpec(memory_space=pltpu.HBM)
    inside = pl.BlockSpec(memory_space=pltpu.VMEM)
    shape = lambda rows, columns, kind=BF16: jax.ShapeDtypeStruct((rows, columns), kind)
    dma = pltpu.SemaphoreType.DMA
    return pl.pallas_call(
        plane_kernel,
        in_specs=[anywhere] * 10 + [inside],
        out_specs=[anywhere, anywhere, inside, inside] + [anywhere] * 13,
        out_shape=[
            shape(piece, width, F32), shape(length, width), shape(4, width, F32), shape(1, inner, F32),
            shape(length, inner), shape(length, inner), shape(length, width), shape(length, width),
            shape(length, width), shape(inner, width), shape(width, inner),
            shape(inner // 2, width), shape(inner // 2, width), shape(inner // 2, width), shape(inner // 8, width, F32),
            shape(width // 2, inner), shape(width // 2, inner),
        ],
        scratch_shapes=[
            pltpu.VMEM((8, half, width), BF16),
            pltpu.VMEM((8, half, width), BF16),
            pltpu.VMEM((half, width), F32),
            pltpu.VMEM((2, half, width), BF16),
            pltpu.VMEM((2, half, width), BF16),
            pltpu.VMEM((2, 2, half, width), BF16),
            dma((10,)), dma((16,)), dma((16,)), dma((16,)), dma((8,)), dma((8,)), dma((4,)), dma((4,)),
        ],
        compiler_params=pltpu.CompilerParams(collective_id=1, has_side_effects=True, vmem_limit_bytes=60 * 2**20),
        cost_estimate=cost(12 * length * width * inner, 10 * length * width),
    )(normed, *cots, fc, down, middle, vectors)


def retreat_plane_kernel(
    low_all, q, k, v, k_t, lse, terms, middle, fc_summed, attended, bias_in, proj_in, vectors,
    grads, column_sums, block_out, grad_proj, fc_share,
    key_bias, proj, entry, prob_ref, chance_ref, grad_ref, key_sum, value_sum, rounded, own, passed, joined, arrived,
    level_got, level_through, level_own, load, local, send, receive, level_send, level_receive, level_load,
):
    piece, width = middle.shape
    half = piece // 2
    entries = (
        pltpu.make_async_copy(bias_in, key_bias, entry.at[0]), pltpu.make_async_copy(proj_in, proj, entry.at[1])
    )
    for item in entries:
        item.start()
    length, columns = q.shape
    heads = columns // HEAD_DIM
    rank = lax.axis_index("seq")
    one, two = neighbours()
    scatter = LateScatter(fc_summed, level_got, level_through, level_own, level_send, level_receive, level_load)
    for device in (one, two):
        greet("seq", device)
    pl.semaphore_wait(pltpu.get_barrier_semaphore(), 2 + scatter.greet())
    up, lower = pl.ds(0, half), pl.ds(half, half)
    rows = lambda at, start=0, size=piece: pl.ds(at * piece + start, size)

    def copy(index, source, target, device):
        return remote(source, target, send.at[index], receive.at[index], "seq", device)

    across = (
        copy(0, terms.at[rows(3, 0, half)], passed.at[0], one),
        copy(1, terms.at[rows(3, half, half)], passed.at[1], two),
    )
    plain_one = copy(2, terms.at[rows(1, 0, half)], arrived.at[0, up], one)
    plain_two = copy(3, terms.at[rows(2, half, half)], arrived.at[1, lower], two)
    joined_one = copy(4, joined.at[0], arrived.at[0, lower], one)
    joined_two = copy(5, joined.at[1], arrived.at[1, up], two)
    loads = (
        pltpu.make_async_copy(terms.at[rows(1, half, half)], own.at[0], load.at[0]),
        pltpu.make_async_copy(terms.at[rows(2, 0, half)], own.at[1], load.at[1]),
    )
    for item in (*across, *loads):
        item.start()
    scatter.start()
    key_sum[...] = jnp.zeros_like(key_sum)
    value_sum[...] = jnp.zeros_like(value_sum)
    for item in entries:
        item.wait()

    def body(low_ref, query_ref, key_ref, value_ref, key_t, lse_ref, query_out):
        at, head = pl.program_id(0), pl.program_id(1)
        true = flip(at, rank)
        here = pl.ds(pl.multiple_of(head * HEAD_DIM, HEAD_DIM), HEAD_DIM)

        @pl.when(head == 0)
        def _():
            grad_ref[...] = nt(low_ref[...], proj[...]).astype(BF16)

        @pl.when((at == 1) & (head == 2))
        def _():
            for item in (*across,):
                item.wait_recv()
            for item in loads:
                item.wait()
            joined[0] = (own[0].astype(F32) + passed[1].astype(F32)).astype(BF16)
            joined[1] = (own[1].astype(F32) + passed[0].astype(F32)).astype(BF16)
            for item in (plain_one, plain_two, joined_one, joined_two):
                item.start()

        @pl.when((at == 1) & (head == 3))
        def _():
            scatter.pass_on()

        query, grad, base = query_ref[...], grad_ref[:, here], lse_ref[0]

        def measure(scores, rel):
            block = rows_of(rel, piece)
            probs = jnp.exp2(scores - base)
            grad_chances = nt(value_ref[block, :], grad)
            value_sum[block, here] += nn(probs.astype(BF16), grad)
            prob_ref[block, :] = probs
            chance_ref[block, :] = grad_chances
            return jnp.sum(probs * grad_chances, axis=0, keepdims=True)

        def first(block, weighted):
            rel = flip(block, rank)
            return weighted + measure(scores_of(key_ref, key_bias, query, rel, piece, False), rel)

        last = scores_of(key_ref, key_bias, query, at, piece, True)
        weighted = lax.fori_loop(0, true, first, measure(last, at))

        def second(block, total):
            block = rows_of(flip(block, rank), piece)
            grad_scores = (prob_ref[block, :] * (chance_ref[block, :] - weighted)).astype(BF16)
            key_sum[block, here] += nn(grad_scores, query)
            return total + nn(key_t[:, block], grad_scores)

        total = lax.fori_loop(0, true + 1, second, jnp.zeros((HEAD_DIM, piece), F32))
        result = (total * FACTOR).T.astype(BF16)
        query_out[...] = result
        sum_rows(column_sums, 0, here, result.astype(F32), at == 0)

    pltpu.emit_pipeline(
        body,
        grid=(4, heads),
        in_specs=[
            pl.BlockSpec((piece, width), lambda g, h: (g, 0)),
            pl.BlockSpec((piece, HEAD_DIM), lambda g, h: (g, h)),
            pl.BlockSpec((length, HEAD_DIM), lambda g, h: (0, h)),
            pl.BlockSpec((length, HEAD_DIM), lambda g, h: (0, h)),
            pl.BlockSpec((HEAD_DIM, length), lambda g, h: (h, 0)),
            pl.BlockSpec((1, 1, piece), lambda g, h: (h, 0, g)),
        ],
        out_specs=[pl.BlockSpec((piece, HEAD_DIM), lambda g, h: (g, h))],
    )(low_all, q, k, v, k_t, lse, grads)

    rounded[:, :columns] = (key_sum[...] * FACTOR).astype(BF16)
    values = value_sum[...].astype(BF16)
    rounded[:, columns:] = values
    column_sums[1:2, :] = jnp.sum(values.astype(F32), axis=0, keepdims=True)
    keep = pltpu.make_async_copy(rounded, grads.at[:, pl.ds(columns, 2 * columns)], local.at[0])
    keep.start()
    tile = min(512, width)

    def outer_body(left, right, out):
        out[...] = tn(left[...], right[...]).astype(BF16)

    pltpu.emit_pipeline(
        outer_body,
        grid=(width // tile,),
        in_specs=[
            pl.BlockSpec((length, columns), lambda i: (0, 0)),
            pl.BlockSpec((length, tile), lambda i: (0, i)),
        ],
        out_specs=[pl.BlockSpec((columns, tile), lambda i: (0, i))],
    )(attended, low_all, grad_proj)
    for item in (plain_one, plain_two, joined_one, joined_two):
        item.wait_recv()
    part = min(128, piece)

    def out_body(middle_tile, term_tile, out):
        here = pl.ds(pl.multiple_of(pl.program_id(0) * part, part), part)
        total = term_tile[...].astype(F32) + arrived[0, here, :].astype(F32) + arrived[1, here, :].astype(F32)
        out[...] = (middle_tile[...] + (total + vectors[5:6, :])).astype(BF16)

    line = pl.BlockSpec((part, width), lambda i: (i, 0))
    pltpu.emit_pipeline(out_body, grid=(piece // part,), in_specs=[line] * 2, out_specs=[line])(middle, terms, block_out)
    scatter.finish(fc_share)
    scatter.close()
    keep.wait()
    for item in (*across, plain_one, plain_two, joined_one, joined_two):
        item.wait_send()


def retreat_plane(low_all, q, k, v, k_t, lse, terms, middle, fc_summed, attended, key_bias, proj, vectors):
    piece, width = middle.shape
    length, columns = q.shape
    half, inner = piece // 2, fc_summed.shape[1]
    anywhere = pl.BlockSpec(memory_space=pltpu.HBM)
    inside = pl.BlockSpec(memory_space=pltpu.VMEM)
    dma = pltpu.SemaphoreType.DMA
    return pl.pallas_call(
        retreat_plane_kernel,
        in_specs=[anywhere] * 12 + [inside],
        out_specs=[anywhere, inside, anywhere, anywhere, inside],
        out_shape=[
            jax.ShapeDtypeStruct((length, 3 * columns), BF16),
            jax.ShapeDtypeStruct((2, columns), F32),
            jax.ShapeDtypeStruct((piece, width), BF16),
            jax.ShapeDtypeStruct((columns, width), BF16),
            jax.ShapeDtypeStruct((width // 8, inner), BF16),
        ],
        scratch_shapes=[
            pltpu.VMEM(key_bias.shape, F32),
            pltpu.VMEM(proj.shape, BF16),
            dma((2,)),
            pltpu.VMEM((length, piece), F32),
            pltpu.VMEM((length, piece), F32),
            pltpu.VMEM((piece, columns), BF16),
            pltpu.VMEM((length, columns), F32),
            pltpu.VMEM((length, columns), F32),
            pltpu.VMEM((length, 2 * columns), BF16),
            pltpu.VMEM((2, half, width), BF16),
            pltpu.VMEM((2, half, width), BF16),
            pltpu.VMEM((2, half, width), BF16),
            pltpu.VMEM((2, piece, width), BF16),
            pltpu.VMEM((width // 2, inner), BF16),
            pltpu.VMEM((width // 8, inner), BF16),
            pltpu.VMEM((width // 8, inner), BF16),
            dma((2,)), dma((1,)), dma((6,)), dma((6,)), dma((8,)), dma((8,)), dma((2,)),
        ],
        compiler_params=pltpu.CompilerParams(collective_id=3, has_side_effects=True, vmem_limit_bytes=62 * 2**20),
        cost_estimate=cost(8 * length * length * columns + 2 * length * columns * width, 10 * length * width),
    )(low_all, q, k, v, k_t, lse, terms, middle, fc_summed, attended, key_bias, proj, vectors)


def closing_kernel(
    grads_in, weight_in, normed_one, tokens, grad_middle, vectors, sums_two, hidden_sums, qv_sums, fc_share,
    tokens_grad, qkv_out, fc_out, small_out,
    terms, passed, joined, arrived, qkv_in, fc_in, mine, small_in, small_rows, small_got,
    grad_qkv, mate_in, summed, got, qkv_share, grads, weight,
    send, receive, level_send, level_receive, small_send, small_receive, load,
):
    pieces = [[ref.at[i] for ref in (grad_qkv, mate_in, summed, got, qkv_share)] for i in range(2)]
    piece, width = tokens.shape
    half = piece // 2
    columns = grads.shape[1]
    farthest, others_in = pl.ds(3 * piece, piece), pl.ds(0, 3 * piece)
    early = (
        pltpu.make_async_copy(weight_in, weight, load.at[3]),
        pltpu.make_async_copy(grads_in.at[farthest], grads.at[farthest], load.at[4]),
    )
    later = pltpu.make_async_copy(grads_in.at[others_in], grads.at[others_in], load.at[5])
    for item in (*early, later):
        item.start()
    heads = columns // (3 * HEAD_DIM)
    me, place = lax.axis_index("seq"), lax.axis_index("dp")
    one, two = neighbours()
    three = 3 - me
    plane = (one, two, three)
    others = [lax.rem(place + i, 8) for i in range(1, 8)]
    for device in plane:
        greet("seq", device)
    for device in others:
        greet("dp", device)
    pl.semaphore_wait(pltpu.get_barrier_semaphore(), 10)
    scatters = [
        NearScatter(*refs[:4], level_send.at[i], level_receive.at[i]) for i, refs in enumerate(pieces)
    ]
    shares = [refs[4] for refs in pieces]
    up, lower = pl.ds(0, half), pl.ds(half, half)

    def copy(index, source, target, device):
        return remote(source, target, send.at[index], receive.at[index], "seq", device)

    across = (copy(0, terms.at[3, up], passed.at[0], one), copy(1, terms.at[3, lower], passed.at[1], two))
    plain_one = copy(2, terms.at[1, up], arrived.at[0, up], one)
    plain_two = copy(3, terms.at[2, lower], arrived.at[1, lower], two)
    joined_one = copy(4, joined.at[0], arrived.at[0, lower], one)
    joined_two = copy(5, joined.at[1], arrived.at[1, up], two)
    fine = qkv_in.shape[2]
    rows_for = lambda ref, device: ref.at[pl.ds(device * fine, fine)]
    fc_copies = [copy(6 + i, rows_for(fc_share, device), fc_in.at[i], device) for i, device in enumerate(plane)]
    qkv_copies = [
        [copy(15 + 3 * part + i, rows_for(share, device), qkv_in.at[part, i], device) for i, device in enumerate(plane)]
        for part, share in enumerate(shares)
    ]
    small_copies = [copy(9 + i, mine, small_in.at[i], device) for i, device in enumerate(plane)]
    fc_own = pltpu.make_async_copy(rows_for(fc_share, me), fc_in.at[3], load.at[0])
    qkv_own = [
        pltpu.make_async_copy(rows_for(share, me), qkv_in.at[part, 3], load.at[1 + part])
        for part, share in enumerate(shares)
    ]
    row_copies = [
        remote(small_rows.at[device], small_got.at[i], small_send.at[i], small_receive.at[i], "dp", device)
        for i, device in enumerate(others)
    ]

    def back_term(at):
        for start in range(0, width, width // 2):
            columns_here = slice(start, start + width // 2)
            term = nt(grads[at * piece : (at + 1) * piece, :], weight[columns_here, :])
            terms[at, :, columns_here] = term.astype(BF16)

    tile = min(512, width)
    narrow = columns // 2

    def outer(part):
        def body(left):
            here = pl.ds(pl.multiple_of(pl.program_id(0) * tile, tile), tile)
            grad_qkv[part, here, :] = tn(left[...], grads[:, part * narrow : (part + 1) * narrow]).astype(BF16)

        pltpu.emit_pipeline(
            body,
            grid=(width // tile,),
            in_specs=[pl.BlockSpec((normed_one.shape[0], tile), lambda i: (0, i))],
        )(normed_one)

    for item in early:
        item.wait()
    back_term(3)
    for item in across:
        item.start()
    later.wait()
    back_term(1)
    plain_one.start()
    outer(0)
    scatters[0].start()
    back_term(2)
    plain_two.start()
    scatters[0].spread()
    outer(1)
    scatters[1].start()
    for item in across:
        item.wait_recv()
    joined[0] = (terms[1, half:].astype(F32) + passed[1].astype(F32)).astype(BF16)
    joined[1] = (terms[2, :half].astype(F32) + passed[0].astype(F32)).astype(BF16)
    joined_one.start()
    joined_two.start()
    scatters[1].spread()
    scatters[0].pass_on()
    fc_own.start()
    back_term(0)
    mine[...] = jnp.zeros_like(mine)
    mine[2:6, :] = sums_two[...]
    for head in range(heads):
        at = (head * 2 + lax.rem(me, 2)) * 2 + lax.div(me, 2)
        here = pl.ds(pl.multiple_of(at * HEAD_DIM, HEAD_DIM), HEAD_DIM)
        for part in range(2):
            mine[6 + part : 7 + part, here] = qv_sums[part : part + 1, head * HEAD_DIM : (head + 1) * HEAD_DIM]
    scatters[1].pass_on()

    scatters[0].finish(shares[0])
    for item in (plain_one, plain_two, joined_one, joined_two):
        item.wait_recv()
    def share_out(part):
        for item in qkv_copies[part]:
            item.start()
        qkv_own[part].start()

    share_out(0)
    for item in fc_copies:
        item.start()
    part = min(128, piece)

    def norm_body(token_tile, middle_tile, out):
        i = pl.program_id(0)
        here = pl.ds(pl.multiple_of(i * part, part), part)
        upstream = terms[0, here, :].astype(F32) + arrived[0, here, :].astype(F32) + arrived[1, here, :].astype(F32)
        unit, scale = norm_parts(token_tile[...].astype(F32))
        out[...] = middle_tile[...] + norm_backward(unit, scale, vectors[0:1, :], upstream)
        for at, item in enumerate((upstream * unit, upstream)):
            sum_rows(mine, at, slice(None), item, i == 0)

    line = pl.BlockSpec((part, width), lambda i: (i, 0))
    pltpu.emit_pipeline(norm_body, grid=(piece // part,), in_specs=[line] * 2, out_specs=[line])(
        tokens, grad_middle, tokens_grad
    )
    for item in small_copies:
        item.start()
    scatters[1].finish(shares[1])
    share_out(1)
    for item in small_copies:
        item.wait_recv()
    mine_total = mine[...] + small_in[0] + small_in[1] + small_in[2]
    small_rows[...] = jnp.zeros_like(small_rows)
    share, wide = width // 8, 2 * width // 8
    for d in range(8):
        small_rows[d, 0:6, 0:share] = mine_total[0:6, d * share : (d + 1) * share]
        row, at = 6 + d // 4, (d % 4) * wide
        small_rows[d, 6:7, :] = mine_total[row : row + 1, at : at + wide]
        inner = hidden_sums.shape[1] // 8
        small_rows[d, 7:8, 0:inner] = hidden_sums[:, d * inner : (d + 1) * inner]
    for item in row_copies:
        item.start()
    sources = (*plane, me)
    fc_own.wait()
    for item in fc_copies:
        item.wait_recv()
    block = fc_in.shape[2] // 8
    for i, source in enumerate(sources):
        for d in range(8):
            target = pl.ds(pl.multiple_of((d * 4 + source) * block, block), block)
            fc_out[:, target] = fc_in[i, :, d * block : (d + 1) * block].astype(F32)
    for part in range(2):
        qkv_own[part].wait()
        for item in qkv_copies[part]:
            item.wait_recv()
    for i, source in enumerate(sources):
        for part in range(3):
            for head in range(heads):
                at = part * HEADS + (head * 2 + lax.rem(source, 2)) * 2 + lax.div(source, 2)
                target = pl.ds(pl.multiple_of(at * HEAD_DIM, HEAD_DIM), HEAD_DIM)
                start = (part * heads + head) * HEAD_DIM
                which, start = start // narrow, start % narrow
                qkv_out[:, target] = qkv_in[which, i, :, start : start + HEAD_DIM].astype(F32)
    for item in row_copies:
        item.wait_recv()
    total = small_rows[place]
    for i in range(7):
        total = total + small_got[i]
    small_out[...] = total
    for item in (*across, plain_one, plain_two, joined_one, joined_two, *fc_copies, *small_copies, *row_copies):
        item.wait_send()
    for part in range(2):
        scatters[part].close()
        for item in qkv_copies[part]:
            item.wait_send()


def closing(grads, weight, normed_one, tokens, grad_middle, vectors, sums_two, hidden_sums, qv_sums, fc_share):
    piece, width = tokens.shape
    columns, half = grads.shape[1], piece // 2
    fine = fc_share.shape[0] // 4
    wide = 2 * width // 8
    anywhere = pl.BlockSpec(memory_space=pltpu.HBM)
    inside = pl.BlockSpec(memory_space=pltpu.VMEM)
    shape = lambda rows, columns, kind=BF16: jax.ShapeDtypeStruct((rows, columns), kind)
    dma = pltpu.SemaphoreType.DMA
    return pl.pallas_call(
        closing_kernel,
        in_specs=[anywhere] * 5 + [inside] * 4 + [anywhere],
        out_specs=[anywhere, inside, inside, inside],
        out_shape=[
            shape(piece, width, F32), shape(fine, 4 * columns, F32), shape(fine, 4 * fc_share.shape[1], F32),
            shape(8, wide, F32),
        ],
        scratch_shapes=[
            pltpu.VMEM((4, piece, width), BF16),
            pltpu.VMEM((2, half, width), BF16),
            pltpu.VMEM((2, half, width), BF16),
            pltpu.VMEM((2, piece, width), BF16),
            pltpu.VMEM((2, 4, fine, columns // 2), BF16),
            pltpu.VMEM((4, fine, fc_share.shape[1]), BF16),
            pltpu.VMEM((8, width), F32),
            pltpu.VMEM((3, 8, width), F32),
            pltpu.VMEM((8, 8, wide), F32),
            pltpu.VMEM((7, 8, wide), F32),
            *[
                pltpu.VMEM((2, count, columns // 2), BF16)
                for count in (width, width // 2, width // 2, width // 2, width // 8)
            ],
            pltpu.VMEM(grads.shape, BF16),
            pltpu.VMEM(weight.shape, BF16),
            dma((21,)), dma((21,)), dma((2, 8)), dma((2, 8)), dma((7,)), dma((7,)), dma((6,)),
        ],
        compiler_params=pltpu.CompilerParams(collective_id=4, has_side_effects=True, vmem_limit_bytes=60 * 2**20),
        cost_estimate=cost(16 * piece * width * columns, 10 * piece * width),
    )(grads, weight, normed_one, tokens, grad_middle, vectors, sums_two, hidden_sums, qv_sums, fc_share)


def after(value, *others):
    return lax.optimization_barrier((value, *others))[0]


def shift(value, axis, distance):
    count = lax.axis_size(axis)
    return lax.ppermute(value, axis, [(i, i ^ distance) for i in range(count)])


def gather_blocks(value, axis="seq"):
    return [value] + [shift(value, axis, k) for k in range(1, lax.axis_size(axis))]


def scatter_blocks(blocks, axis="seq"):
    return [blocks[0]] + [shift(blocks[k], axis, k) for k in range(1, lax.axis_size(axis))]


def gather_plane(value):
    if lax.axis_size("seq") != 4:
        return gather_blocks(value)
    half = value.shape[0] // 2
    one, two = shift(value, "seq", 1), shift(value, "seq", 2)
    three = jnp.concatenate([shift(one[:half], "seq", 2), shift(two[half:], "seq", 1)], axis=0)
    return [value, one, two, three]


def scatter_plane(blocks):
    if lax.axis_size("seq") != 4:
        return scatter_blocks(blocks)
    half = blocks[0].shape[0] // 2
    up, low = shift(blocks[3][:half], "seq", 1), shift(blocks[3][half:], "seq", 2)
    one = shift(blocks[1][:half], "seq", 1)
    two = shift(blocks[2][half:], "seq", 2)
    one_low = (blocks[1][half:].astype(F32) + low.astype(F32)).astype(BF16)
    two_up = (blocks[2][:half].astype(F32) + up.astype(F32)).astype(BF16)
    return [blocks[0], (one, shift(one_low, "seq", 1)), (shift(two_up, "seq", 2), two)]


def by_rank(blocks, rank):
    bit = 1
    while bit < len(blocks):
        odd = (rank & bit) != 0
        blocks = [jnp.where(odd, blocks[k ^ bit], blocks[k]) for k in range(len(blocks))]
        bit *= 2
    return blocks


def pick(pieces, at):
    return lax.dynamic_index_in_dim(pieces, at, axis=0, keepdims=False)


def exchange(pieces, rank):
    return scatter_blocks([pick(pieces, rank ^ k) for k in range(pieces.shape[0])])


def small_scatter(pieces, dp_rank, seq_rank):
    total = 0.0
    sent = [lax.dynamic_index_in_dim(pieces, seq_rank ^ k, axis=1, keepdims=False) for k in range(pieces.shape[1])]
    for part in scatter_blocks(sent):
        total = total + part
    sent = [pick(total, dp_rank ^ k) for k in range(pieces.shape[0])]
    total = 0.0
    for part in scatter_blocks(sent, "dp"):
        total = total + part
    return total


def swap_pairs(dp_count, seq_count, sub):
    pairs = []
    for d in range(dp_count):
        for s in range(seq_count):
            source = ((d // sub) * sub + s % sub) * seq_count + (s // sub) * sub + d % sub
            pairs.append((source, d * seq_count + s))
    return pairs


def gather_dp(value):
    return lax.all_gather(value, "dp", axis=0, tiled=True)


def scatter_dp(value):
    return lax.psum_scatter(value, "dp", scatter_dimension=0, tiled=True)


def shards(
    tokens,
    cotangent,
    lengths,
    key_mask,
    attn_gain,
    attn_shift,
    qkv_weight,
    qv_bias,
    proj_weight,
    proj_bias,
    mlp_gain,
    mlp_shift,
    fc_weight,
    fc_bias,
    down_weight,
    down_bias,
):
    _, piece, width = tokens.shape
    dp_count, seq_count = lax.axis_size("dp"), lax.axis_size("seq")
    dp_rank, seq_rank = lax.axis_index("dp"), lax.axis_index("seq")
    own_heads = HEADS // seq_count
    own_width = own_heads * HEAD_DIM
    rows = qkv_weight.shape[0]
    sub = HEAD_DIM // proj_weight.shape[0]
    high = seq_count // sub
    block = down_weight.shape[0]
    rank = jnp.reshape(seq_rank, (1,)).astype(jnp.int32)
    swap = swap_pairs(dp_count, seq_count, sub)
    order = list(range(seq_count - 1, -1, -1))
    if seq_count == 4:
        order = [3, 1, 2, 0]

    in_plane = seq_count == 4 and dp_count == 8
    tokens_own, cot_own = tokens[0], cotangent[0]

    positions = seq_rank * piece + jnp.arange(piece, dtype=jnp.int32)
    own_flags = ((key_mask[0] == 1) & (positions < lengths[0])).astype(BF16)
    length = piece * seq_count
    shared = None
    if in_plane:
        six = jnp.stack([attn_gain, attn_shift, proj_bias, mlp_gain, mlp_shift, down_bias])
        odd = (seq_rank & 1) != 0
        six = jnp.concatenate([jnp.where(odd, 0, six), jnp.where(odd, six, 0)], axis=1)
        small, start = 0, 0
        for item in (six, qv_bias, fc_bias, own_flags):
            item = item.reshape(-1, 128)
            small = small + jnp.pad(item, ((start, 16 - start - item.shape[0]), (0, 0)))
            start += item.shape[0]
        token_all, qkv_full, fc_rows, cot_one, cot_two, down_full, proj_full, vectors, key_bias = opening(
            tokens_own, cot_own, qkv_weight, fc_weight, small, down_weight, proj_weight, dp_count
        )
        fc_full = gather_dp(fc_rows)
    else:
        small = (attn_gain, attn_shift, qv_bias, proj_bias, mlp_gain, mlp_shift, fc_bias, down_bias)
        sizes = [item.shape[0] for item in small]
        packed = jnp.concatenate(small + (own_flags,))
        blocks = gather_blocks(packed)
        flags = jnp.concatenate([item[-piece:] for item in blocks])
        key_bias = jnp.where(flags > 0, 0.0, NEG).astype(F32)[:, None]
        packed = jnp.stack(by_rank([item[:-piece] for item in blocks], seq_rank))
        packed = jnp.stack(by_rank(gather_blocks(packed, "dp"), dp_rank)).astype(F32)
        parts, start = [], 0
        for size in sizes:
            parts.append(packed[:, :, start : start + size])
            start += size
        whole = [part.reshape(1, -1) for part in parts]
        gain_one, shift_one, qv_full, proj_shift, gain_two, shift_two, _, down_shift = whole
        fc_shift = lax.dynamic_index_in_dim(parts[6], seq_rank, axis=1, keepdims=False).reshape(1, -1)
        rank_low, rank_high = seq_rank % sub, seq_rank // sub
        qv_own = qv_full.reshape(2, own_heads, sub, high, HEAD_DIM)
        qv_own = lax.dynamic_index_in_dim(qv_own, rank_low, axis=2, keepdims=False)
        qv_own = lax.dynamic_index_in_dim(qv_own, rank_high, axis=2, keepdims=False).reshape(1, -1)
        qv_own = jnp.pad(qv_own, ((0, 0), (0, width - 2 * own_width)))
        vectors = jnp.concatenate([gain_one, shift_one, jnp.zeros((5, width), F32), qv_own], axis=0)
        qkv_pieces = (
            qkv_weight.reshape(rows, 3, own_heads, sub, high, HEAD_DIM)
            .transpose(4, 3, 0, 1, 2, 5)
            .reshape(seq_count, rows, 3 * own_width)
        )
        fc_pieces = (
            fc_weight.reshape(rows, dp_count, seq_count, block)
            .transpose(2, 0, 1, 3)
            .reshape(seq_count, rows, dp_count * block)
        )
        qkv_full = gather_dp(jnp.concatenate(by_rank(exchange(qkv_pieces, seq_rank), seq_rank), axis=0))
        proj_full = gather_dp(lax.ppermute(proj_weight, BOTH, swap))
        down_full = gather_dp(down_weight)
        fc_full = gather_dp(jnp.concatenate(by_rank(exchange(fc_pieces, seq_rank), seq_rank), axis=0))
        token_blocks = gather_blocks(tokens_own)
        cot_blocks = gather_blocks(after(cot_own, token_blocks[-1]))
        for k in range(seq_count):
            shared = project(k, token_blocks[k], 0, piece, vectors, qkv_full, length, shared)
    if in_plane:
        results = attend_plane(
            tokens_own, cot_own, token_all, qkv_full, cot_one, down_weight, down_full, key_bias, proj_full, vectors
        )
        middle, normed_two, attended, lse, cot_three, down_full = results[:6]
        normed_one, q, keys, values, keys_t, values_t, one_low, two_low = results[6:]
    else:
        normed_one, q, keys, values, keys_t, values_t = shared
        proj_terms, shared = [None] * seq_count, None
        for k in order:
            proj_terms[k], shared = attend(k, rank, q, keys, values_t, key_bias, proj_full, piece, shared)
        attended, lse = shared
        middle, normed_two = rowwise(
            middle_kernel, scatter_blocks(proj_terms), [tokens_own], [proj_shift, gain_two, shift_two], [F32, BF16], 0
        )

    if in_plane:
        cots = (cot_own, cot_one, one_low, cot_two, two_low, cot_three)
        results = feed_plane(normed_two, cots, fc_full, down_full, middle, vectors)
        grad_middle, low_all, sums_two, hidden_sums, down_terms, grad_down, fc_summed = [
            results[i] for i in (0, 1, 2, 3, 8, 14, 16)
        ]
        grads, qv_sums, block_out, grad_proj, grad_fc = retreat_plane(
            low_all, q, keys, values, keys_t, lse, down_terms, middle, fc_summed, attended, key_bias, proj_full, vectors
        )
    else:
        normed_blocks = gather_blocks(normed_two)
        grad_terms, shared = [], None
        for k in range(seq_count):
            term, shared = feed(k, normed_blocks[k], cot_blocks[k], fc_full, fc_shift, down_full, seq_count, shared)
            grad_terms.append(term)
        active, grad_hidden, normed_all, cot_all = shared
        grad_middle, grad_mid_low, *sums_two = rowwise(
            middle_back_kernel, scatter_blocks(grad_terms), [middle, cot_own], [gain_two], [F32, BF16], 4
        )
        down_terms = [
            nn(active[k * piece : (k + 1) * piece], down_full).astype(BF16) for k in range(seq_count)
        ]
        low_blocks = gather_blocks(grad_mid_low)
        grad_down = scatter_dp(tn(active, cot_all).astype(BF16))
        grad_fc = scatter_dp(tn(normed_all, grad_hidden).astype(BF16))
        hidden_sums = jnp.sum(grad_hidden.astype(F32), axis=0)
        block_out = rowwise(out_kernel, scatter_blocks(down_terms), [middle], [down_shift], [BF16], 0)[0]
        sums, shared = None, None
        for k in range(seq_count):
            sums, shared = retreat(
                k, rank, low_blocks[k], proj_full, q, lse, keys, values, keys_t, key_bias, sums, shared,
                k == seq_count - 1,
            )
        grad_q, low_all = shared
        grads = jnp.concatenate([grad_q, sums[0], sums[1]], axis=1)
        qv_sums = jnp.stack([jnp.sum(item.astype(F32), axis=0) for item in (grad_q, sums[1])])
        grad_proj = tn(attended, low_all).astype(BF16)
    grad_proj = lax.ppermute(scatter_dp(grad_proj), BOTH, swap).astype(F32)
    share = attn_gain.shape[0]
    if in_plane:
        tokens_grad, grad_qkv_weight, grad_fc, smalls = closing(
            grads, qkv_full, normed_one, tokens_own, grad_middle, vectors, sums_two, hidden_sums, qv_sums, grad_fc
        )[:4]
        own = lambda row, size: lax.dynamic_slice_in_dim(smalls[row], seq_rank * size, size)
        late = jnp.concatenate([own(0, share), own(1, share), own(6, 2 * share)])
        early = jnp.concatenate([own(row, share) for row in range(2, 6)] + [smalls[7, :block]])
    else:
        back_terms = [None] * seq_count
        for k in order:
            back_terms[k] = back(k, grads, qkv_full, piece)
        tokens_grad, *sums_one = rowwise(
            tokens_back_kernel, scatter_blocks(back_terms), [tokens_own, grad_middle], [gain_one], [F32], 2
        )

        blocks = exchange(grad_fc.reshape(seq_count, rows, dp_count * block), seq_rank)
        if block % 128 == 0:
            fc_places = lambda s: [(0, d, d * seq_count + s) for d in range(dp_count)]
            grad_fc = lay_out(rank, [[item] for item in blocks], fc_weight.shape[1], (fc_places, block))
        else:
            blocks = [item.reshape(rows, dp_count, block) for item in by_rank(blocks, seq_rank)]
            grad_fc = jnp.stack(blocks, axis=2).reshape(fc_weight.shape).astype(F32)
        grad_qkv = scatter_dp(tn(normed_one, grads).astype(BF16))
        blocks = [[item] for item in exchange(grad_qkv.reshape(seq_count, rows, 3 * own_width), seq_rank)]
        qkv_places = lambda s: [
            (0, part * own_heads + head, part * HEADS + (head * sub + s % sub) * high + s // sub)
            for part in range(3)
            for head in range(own_heads)
        ]
        grad_qkv_weight = lay_out(rank, blocks, qkv_weight.shape[1], (qkv_places, HEAD_DIM))

        def spread(vector):
            return vector.reshape(dp_count, seq_count, -1)

        here = (jnp.arange(seq_count) == seq_rank).astype(F32)
        hidden_sums = hidden_sums.reshape(dp_count, 1, -1) * here[None, :, None]
        early = jnp.concatenate([spread(item) for item in sums_two] + [hidden_sums], axis=2)
        early = small_scatter(early, dp_rank, seq_rank)
        here = (jnp.arange(sub) == rank_low)[:, None] & (jnp.arange(high) == rank_high)[None, :]
        qv_sums = qv_sums.reshape(2, own_heads, 1, 1, HEAD_DIM) * here.astype(F32)[None, None, :, :, None]
        late = jnp.concatenate([spread(item) for item in sums_one] + [spread(qv_sums)], axis=2)
        late = small_scatter(late, dp_rank, seq_rank)
    return (
        block_out[None],
        tokens_grad[None],
        late[:share],
        late[share : 2 * share],
        grad_qkv_weight,
        late[2 * share :],
        grad_proj,
        early[2 * share : 3 * share],
        early[:share],
        early[share : 2 * share],
        grad_fc,
        early[4 * share :],
        grad_down.astype(F32),
        early[3 * share : 4 * share],
    )


def solution(mesh):
    in_specs = (
        P("dp", "seq", None),
        P("dp", "seq", None),
        P("dp"),
        P("dp", "seq"),
        P(BOTH),
        P(BOTH),
        P(BOTH, None),
        P(BOTH),
        P(BOTH, None),
        P(BOTH),
        P(BOTH),
        P(BOTH),
        P(BOTH, None),
        P(BOTH),
        P(BOTH, None),
        P(BOTH),
    )
    out_specs = (
        P("dp", "seq", None),
        P("dp", "seq", None),
        P(BOTH),
        P(BOTH),
        P(BOTH, None),
        P(BOTH),
        P(BOTH, None),
        P(BOTH),
        P(BOTH),
        P(BOTH),
        P(BOTH, None),
        P(BOTH),
        P(BOTH, None),
        P(BOTH),
    )
    return jax.shard_map(shards, mesh=mesh, in_specs=in_specs, out_specs=out_specs, check_vma=False)
```
